32 devices in a mesh: head: 4 (over y, x), blk: 8 (over z, core).
Axes of the slice: x: 2, y: 2, z: 4, core: 2. Of those that a mesh axis runs over, the one named last changes fastest.
Arguments:
- tokens: bfloat16 [4, 1024, 1024], P('head', 'blk'), may hold values from -6 to 6
- doc_start: int32 [4, 1024], P(None, 'blk'), may hold values from 0 to 1023, as said below
- bias_table: float32 [32, 16], replicated, may hold values from -4 to 4
- attn_in: bfloat16 [2, 1024, 3072], P(None, ('head', 'blk')), may hold values from -0.1875 to 0.1875
- attn_out: bfloat16 [2, 1024, 1024], P(None, ('head', 'blk')), may hold values from -0.5 to 0.5
- ff_in: bfloat16 [2, 4096, 1024], P(None, ('head', 'blk')), may hold values from -0.1875 to 0.1875
- ff_out: bfloat16 [2, 4096, 1024], P(None, ('head', 'blk')), may hold values from -0.09375 to 0.09375
- gains: bfloat16 [2, 1024, 2], P(None, ('head', 'blk')), may hold values from 0.5 to 1.5
- cotangent: float32 [4, 1024, 1024], P('head', 'blk'), may hold values from -6 to 6
Outputs:
- output: float32 [4, 1024, 1024], P('head', 'blk')
- grad_tokens: float32 [4, 1024, 1024], P('head', 'blk')
- grad_attn_in: float32 [2, 1024, 3072], P(None, ('head', 'blk'))
- grad_attn_out: float32 [2, 1024, 1024], P(None, ('head', 'blk'))
- grad_ff_in: float32 [2, 4096, 1024], P(None, ('head', 'blk'))
- grad_ff_out: float32 [2, 4096, 1024], P(None, ('head', 'blk'))
- grad_gains: float32 [2, 1024, 2], P(None, ('head', 'blk'))
- grad_bias_table: float32 [32, 16], P('blk', 'head')
The draws below stay inside these ranges and needn't reach their ends.
Inputs may be any that keep to these rules, and one draw needn't show every extreme that they name: doc_start[s, p] is the first position of the document that holds position p of sequence s; documents are runs of consecutive positions. In one sequence, drawn from the seed, a single document fills all 1024 positions; in every other sequence the last position is a document of its own.
All inputs are finite; a program needn't handle non-finite values.
Results may differ from the reference program's by a relative error of at most 0.033.
Values may be sent and summed in bfloat16 or wider, within the bound.
No kernel may reach another device: no remote copies, remote signals or barrier semaphores. Data moves between devices by JAX's collectives and lax.ppermute only.
A program may use at most 768 MiB of HBM per device.

```python
import math
import jax
import jax.numpy as jnp
from jax import lax

D = 1024
HEADS = 16
HDIM = 64
FF = 4096
NBUCK = 32
LAYERS = 2
LEN = 1024
SEQS = 4


def draw_doc_start(key, part):
    key = jax.random.fold_in(key, 7)
    key_coins, key_lengths, key_whole = jax.random.split(key, 3)
    trials = jax.random.randint(key_coins, (SEQS, LEN, 10), 0, 2)
    levels = jnp.sum(jnp.cumprod(trials, axis=2), axis=2).astype(jnp.int32)
    spans = jnp.left_shift(jnp.ones((SEQS, LEN), jnp.int32), 3 + levels)
    lengths = 1 + jax.random.randint(key_lengths, (SEQS, LEN), 0, 8192) % spans
    doc_ends = jnp.cumsum(lengths, axis=1)
    inside = (doc_ends < LEN).astype(jnp.int32)
    row_ids = jnp.broadcast_to(jnp.arange(SEQS, dtype=jnp.int32)[:, None], (SEQS, LEN))
    start_flags = jnp.zeros((SEQS, LEN), jnp.int32).at[row_ids, jnp.minimum(doc_ends, LEN - 1)].max(inside)
    start_flags = start_flags.at[:, 0].set(1).at[:, LEN - 1].set(1)
    places = jnp.arange(LEN, dtype=jnp.int32)[None, :]
    starts = lax.cummax(start_flags * places, axis=1)
    chosen = jax.random.randint(key_whole, (), 0, SEQS)
    starts = jnp.where(jnp.arange(SEQS, dtype=jnp.int32)[:, None] == chosen, 0, starts)
    return starts.astype(jnp.int32)


def block_scale(rng, extent, cuts, least, largest):
    factor_of, own = 1.0, jax.random.fold_in(rng, 6)
    for position, blocks in cuts:
        steps = jnp.exp(jax.random.uniform(jax.random.fold_in(own, position), (blocks,), jnp.float32, least / len(cuts), largest / len(cuts)))
        factor_of = factor_of * jnp.repeat(steps, extent[position] // blocks).reshape([-1 if axis == position else 1 for axis in range(len(extent))])
    return factor_of


def noise(stream_key, extent, width, reach, cuts=(), kind=jnp.bfloat16):
    entries = width * jax.random.normal(stream_key, extent, jnp.float32)
    if cuts:
        entries = entries * block_scale(stream_key, extent, cuts, -0.22, 0.18)
    return jnp.clip(entries, -reach, reach).astype(kind)


def setup_inputs(seed: int = 0) -> dict:
    arg_keys = jax.random.split(jax.random.key(seed), 10)
    tokens = noise(arg_keys[0], (SEQS, LEN, D), 1.0, 6.0, ((0, 4), (1, 8)))
    doc_start = draw_doc_start(jax.random.fold_in(arg_keys[9], 71), 0)
    bias_table = noise(arg_keys[2], (NBUCK, HEADS), 1.0, 4.0, (), jnp.float32)
    attn_in = noise(arg_keys[3], (LAYERS, D, 3 * D), D ** -0.5, 0.1875, ((1, 32),))
    attn_out = noise(arg_keys[4], (LAYERS, D, D), (D // 8) ** -0.5, 0.5, ((1, 32),))
    ff_in = noise(arg_keys[5], (LAYERS, FF, D), D ** -0.5, 0.1875, ((1, 32),))
    ff_out = noise(arg_keys[6], (LAYERS, FF, D), FF ** -0.5, 0.09375, ((1, 32),))
    gains = jnp.clip(1.0 + 0.1 * jax.random.normal(arg_keys[7], (LAYERS, D, 2), jnp.float32), 0.5, 1.5).astype(jnp.bfloat16)
    cotangent = noise(arg_keys[8], (SEQS, LEN, D), 1.0, 6.0, ((0, 4), (1, 8)), jnp.float32)
    return dict(tokens=tokens, doc_start=doc_start, bias_table=bias_table, attn_in=attn_in, attn_out=attn_out, ff_in=ff_in, ff_out=ff_out, gains=gains, cotangent=cotangent)


@jax.custom_vjp
def low(v):
    return lax.optimization_barrier(v.astype(jnp.bfloat16)).astype(jnp.float32)

@jax.custom_vjp
def low_back(v):
    return v

def low_keep(v):
    return (low(v), None)

def low_pass(kept, grad):
    return (grad,)

def back_keep(v):
    return (v, None)

def back_low(kept, grad):
    return (low(grad),)
low.defvjp(low_keep, low_pass)
low_back.defvjp(back_keep, back_low)
bounds = (1, 2, 3, 4, 5, 6, 7, 8, 12, 16, 23, 32, 46, 64, 91)
epsilon = 1e-06
masked = -1e+30
score_scale = 0.125
topmost_value = lax.Precision.HIGHEST

def rms_norm(hidden, gain):
    inverse = lax.rsqrt(lax.optimization_barrier(jnp.mean(hidden * hidden, axis=-1, keepdims=True)) + epsilon)
    return hidden * inverse * gain

def bucket_of(offsets):
    distance = jnp.abs(offsets)
    bucket = jnp.zeros(offsets.shape, jnp.int32)
    for boundary in bounds:
        bucket = bucket + (distance >= boundary).astype(jnp.int32)
    return bucket + 16 * (offsets > 0).astype(jnp.int32)

def attend_block(query_block, leading_row, key_heads, value_heads, query_starts, key_starts, bias_table):
    rows_per_block = query_block.shape[0]
    positions = leading_row + jnp.arange(rows_per_block, dtype=jnp.int32)
    columns = jnp.arange(key_heads.shape[0], dtype=jnp.int32)
    buckets = bucket_of(columns[None, :] - positions[:, None])
    bias_block = jnp.transpose(jnp.take(bias_table, buckets, axis=0), (2, 0, 1))
    raw_scores = jnp.einsum('ihd,jhd->hij', query_block, key_heads, precision=topmost_value) * score_scale + bias_block
    same_doc = query_starts[:, None] == key_starts[None, :]
    scores = jnp.where(same_doc[None], low_back(raw_scores), masked)
    row_peak = lax.optimization_barrier(jnp.max(scores, axis=-1, keepdims=True))
    exp_scores = jnp.exp(scores - row_peak)
    row_total = lax.optimization_barrier(jnp.sum(exp_scores, axis=-1))
    mixed_sum = low_back(jnp.einsum('hij,jhd->ihd', low(exp_scores), value_heads, precision=topmost_value))
    return mixed_sum / jnp.transpose(row_total)[:, :, None]

def attend_sequence(queries, key_heads, value_heads, starts, bias_table):
    length = queries.shape[0]
    rows_per_block = math.gcd(length, 512)
    blocks = length // rows_per_block
    blockwise = jax.checkpoint(attend_block)

    def one_block(element):
        return blockwise(element[0], element[1], key_heads, value_heads, element[2], starts, bias_table)
    firsts = jnp.arange(blocks, dtype=jnp.int32) * rows_per_block
    result = lax.map(one_block, (queries.reshape(blocks, rows_per_block, HEADS, HDIM), firsts, starts.reshape(blocks, rows_per_block)))
    return result.reshape(length, HEADS * HDIM)

def layer(hidden, w_qkv, w_out, input_weight, w_down, gain_pair, bias_table, doc_start):
    normed = low(rms_norm(hidden, gain_pair[:, 0]))
    projected = low(low_back(jnp.dot(normed, w_qkv, precision=topmost_value)))
    queries = projected[:, :, :D].reshape(SEQS, LEN, HEADS, HDIM)
    key_heads = projected[:, :, D:2 * D].reshape(SEQS, LEN, HEADS, HDIM)
    value_heads = projected[:, :, 2 * D:].reshape(SEQS, LEN, HEADS, HDIM)
    attended = lax.map(lambda element: attend_sequence(element[0], element[1], element[2], element[3], bias_table), (queries, key_heads, value_heads, doc_start))
    attended = low(low_back(attended))
    middle = hidden + low_back(jnp.dot(attended, w_out, precision=topmost_value))
    feedforward_normed = low(rms_norm(middle, gain_pair[:, 1]))
    preactivation = low_back(jnp.einsum('jgp,yp->jgy', feedforward_normed, input_weight, precision=topmost_value))
    activated = low(jax.nn.gelu(preactivation, approximate=False))
    return middle + low_back(jnp.dot(activated, w_down, precision=topmost_value))

def reference(tokens, doc_start, bias_table, attn_in, attn_out, ff_in, ff_out, gains, cotangent):

    def forward(hidden, w_qkv, w_out, input_weight, w_down, gain_all, table):
        for layer_id in range(LAYERS):
            hidden = layer(hidden, w_qkv[layer_id], w_out[layer_id], input_weight[layer_id], w_down[layer_id], gain_all[layer_id], table, doc_start)
        return hidden
    primals = (tokens.astype(jnp.float32), attn_in.astype(jnp.float32), attn_out.astype(jnp.float32), ff_in.astype(jnp.float32), ff_out.astype(jnp.float32), gains.astype(jnp.float32), bias_table.astype(jnp.float32))
    output, backward = jax.vjp(forward, *primals)
    gradients = backward(cotangent.astype(jnp.float32))
    return (output, gradients[0], gradients[1], gradients[2], gradients[3], gradients[4], gradients[5], gradients[6])
```

```python
import functools

import jax
import jax.numpy as jnp
import numpy as np
from jax import lax
from jax.experimental import pallas as pl
from jax.experimental.pallas import tpu as pltpu
from jax.sharding import Mesh
from jax.sharding import PartitionSpec as P

bounds = (1, 2, 3, 4, 5, 6, 7, 8, 12, 16, 23, 32, 46, 64, 91)
epsilon = 1e-06
masked = -1e30
score_scale = 0.125
head_dim = 64
tile = 128
everyone = ("head", "z", "core")
bf16 = jnp.bfloat16
f32 = jnp.float32


def contract(lhs, rhs, lhs_dim, rhs_dim):
    return lax.dot_general(
        lhs, rhs, (((lhs_dim,), (rhs_dim,)), ((), ())), preferred_element_type=f32
    )


def near_buckets():
    offsets = np.arange(3 * tile)[None, :] - tile - np.arange(tile)[:, None]
    distance = np.abs(offsets)
    bucket = np.zeros(offsets.shape, np.int32)
    for boundary in bounds:
        bucket += (distance >= boundary).astype(np.int32)
    return bucket + 16 * (offsets > 0).astype(np.int32)


def fill_band(band, table, near, heads_dev, length):
    for head in range(heads_dev):
        band[head, :, : length - tile] = jnp.full((tile, length - tile), table[15, head], f32)
        band[head, :, length - tile : length + 2 * tile] = near[head]
        band[head, :, length + 2 * tile :] = jnp.full(
            (tile, length - 2 * tile), table[31, head], f32
        )


def attention_kernel(heads_dev, length, first, table, near, qkv, doc_row, doc_col, out, stats, band):
    step = pl.program_id(0)
    width = heads_dev * head_dim

    @pl.when(step == 0)
    def _():
        fill_band(band, table, near, heads_dev, length)

    row = pl.multiple_of((first[0] + step) * tile, tile)
    same_doc = doc_col[...] == doc_row[...]
    queries = qkv[pl.ds(row, tile), :width] * bf16(score_scale)
    lanes = lax.broadcasted_iota(jnp.int32, (tile, tile), 1)
    collected = jnp.zeros((tile, tile), f32)
    for head in range(heads_dev):
        own = slice(head * head_dim, (head + 1) * head_dim)
        keys = qkv[:, width + own.start : width + own.stop]
        values = qkv[:, 2 * width + own.start : 2 * width + own.stop]
        scores = contract(queries[:, own], keys, 1, 1)
        scores = scores + band[head, :, pl.ds(pl.multiple_of(length - row, tile), length)]
        scores = jnp.where(same_doc, scores, masked)
        peak = jnp.max(scores, axis=1, keepdims=True)
        weights = jnp.exp(scores - peak)
        total = jnp.sum(weights, axis=1, keepdims=True)
        mixed = contract(weights.astype(bf16), values, 1, 0) / total
        out[:, own] = mixed.astype(bf16)
        collected = jnp.where(lanes == head, peak + jnp.log(total), collected)
    stats[...] = collected


def attention_back_kernel(
    heads_dev, length, split, first, table, near, qkv, doc_row, doc_col, attended, grad_out, stats,
    grad_qkv, grad_near, grad_far, band, grad_band, grad_keys, grad_values,
):
    step = pl.program_id(0)
    width = heads_dev * head_dim

    @pl.when(step == 0)
    def _():
        fill_band(band, table, near, heads_dev, length)
        grad_band[...] = jnp.zeros_like(grad_band)
        grad_keys[...] = jnp.zeros_like(grad_keys)
        grad_values[...] = jnp.zeros_like(grad_values)
        if split > 1:
            grad_qkv[...] = jnp.zeros_like(grad_qkv)

    row = pl.multiple_of((first[0] + step) * tile, tile)
    shift = pl.ds(pl.multiple_of(length - row, tile), length)
    same_doc = doc_col[...] == doc_row[...]
    queries = qkv[pl.ds(row, tile), :width] * bf16(score_scale)
    for head in range(heads_dev):
        own = slice(head * head_dim, (head + 1) * head_dim)
        keys = qkv[:, width + own.start : width + own.stop]
        values = qkv[:, 2 * width + own.start : 2 * width + own.stop]
        upstream = grad_out[:, own]
        scores = contract(queries[:, own], keys, 1, 1) + band[head, :, shift]
        scores = jnp.where(same_doc, scores, masked)
        weights = jnp.exp(scores - stats[:, head : head + 1])
        delta = jnp.sum(
            upstream.astype(f32) * attended[:, own].astype(f32), axis=1, keepdims=True
        )
        grad_scores = weights * (contract(upstream, values, 1, 1) - delta)
        grad_band[head, :, shift] += grad_scores
        grad_low = grad_scores.astype(bf16)
        grad_values[:, own] += contract(weights.astype(bf16), upstream, 0, 0)
        grad_keys[:, own] += contract(grad_low, queries[:, own], 0, 0)
        grad_qkv[pl.ds(row, tile), own] = (
            contract(grad_low, keys, 1, 0) * score_scale
        ).astype(bf16)

    @pl.when(step == pl.num_programs(0) - 1)
    def _():
        grad_qkv[:, width : 2 * width] = grad_keys[...].astype(bf16)
        grad_qkv[:, 2 * width :] = grad_values[...].astype(bf16)
        for head in range(heads_dev):
            grad_near[head] = grad_band[head, :, length - tile : length + 2 * tile]
            grad_far[head, 0] = jnp.full(
                (8, tile), jnp.sum(grad_band[head, :, : length - tile]), f32
            )
            grad_far[head, 1] = jnp.full(
                (8, tile), jnp.sum(grad_band[head, :, length + 2 * tile :]), f32
            )


def whole(shape):
    return pl.BlockSpec(shape, lambda step: (0,) * len(shape))


def attention(qkv, doc_row, doc_col, first, table, near, rows):
    length = qkv.shape[0]
    heads_dev = table.shape[1]
    width = heads_dev * head_dim
    return pl.pallas_call(
        functools.partial(attention_kernel, heads_dev, length),
        grid=(rows // tile,),
        in_specs=[
            pl.BlockSpec(memory_space=pltpu.SMEM),
            pl.BlockSpec(memory_space=pltpu.SMEM),
            whole(near.shape),
            whole(qkv.shape),
            whole(doc_row.shape),
            pl.BlockSpec((tile, 1), lambda step: (step, 0)),
        ],
        out_specs=[
            pl.BlockSpec((tile, width), lambda step: (step, 0)),
            pl.BlockSpec((tile, tile), lambda step: (step, 0)),
        ],
        out_shape=[
            jax.ShapeDtypeStruct((rows, width), bf16),
            jax.ShapeDtypeStruct((rows, tile), f32),
        ],
        scratch_shapes=[pltpu.VMEM((heads_dev, tile, 2 * length), f32)],
        compiler_params=pltpu.CompilerParams(vmem_limit_bytes=40 * 2**20),
        cost_estimate=pl.CostEstimate(
            flops=4 * rows * length * width,
            bytes_accessed=4 * length * width * 2,
            transcendentals=rows * length * heads_dev,
        ),
    )(first, table, near, qkv, doc_row, doc_col)


def attention_back(qkv, doc_row, doc_col, attended, grad_out, stats, first, table, near, split):
    length = qkv.shape[0]
    rows = grad_out.shape[0]
    heads_dev = table.shape[1]
    width = heads_dev * head_dim
    return pl.pallas_call(
        functools.partial(attention_back_kernel, heads_dev, length, split),
        grid=(rows // tile,),
        in_specs=[
            pl.BlockSpec(memory_space=pltpu.SMEM),
            pl.BlockSpec(memory_space=pltpu.SMEM),
            whole(near.shape),
            whole(qkv.shape),
            whole(doc_row.shape),
            pl.BlockSpec((tile, 1), lambda step: (step, 0)),
            pl.BlockSpec((tile, width), lambda step: (step, 0)),
            pl.BlockSpec((tile, width), lambda step: (step, 0)),
            pl.BlockSpec((tile, tile), lambda step: (step, 0)),
        ],
        out_specs=[
            whole((length, 3 * width)),
            whole((heads_dev, tile, 3 * tile)),
            whole((heads_dev, 2, 8, tile)),
        ],
        out_shape=[
            jax.ShapeDtypeStruct((length, 3 * width), bf16),
            jax.ShapeDtypeStruct((heads_dev, tile, 3 * tile), f32),
            jax.ShapeDtypeStruct((heads_dev, 2, 8, tile), f32),
        ],
        scratch_shapes=[
            pltpu.VMEM((heads_dev, tile, 2 * length), f32),
            pltpu.VMEM((heads_dev, tile, 2 * length), f32),
            pltpu.VMEM((length, width), f32),
            pltpu.VMEM((length, width), f32),
        ],
        compiler_params=pltpu.CompilerParams(vmem_limit_bytes=48 * 2**20),
        cost_estimate=pl.CostEstimate(
            flops=10 * rows * length * width,
            bytes_accessed=8 * length * width * 2,
            transcendentals=rows * length * heads_dev,
        ),
    )(first, table, near, qkv, doc_row, doc_col, attended, grad_out, stats)


def inverse_rms(hidden):
    return lax.rsqrt(jnp.mean(hidden * hidden, axis=-1, keepdims=True) + epsilon)


def unit_norm_back(hidden, inverse, grad_unit):
    unit = hidden * inverse
    return inverse * (grad_unit - unit * jnp.mean(grad_unit * unit, axis=-1, keepdims=True))


def gather_rows(block, axes):
    return lax.all_gather(block, axes, axis=0, tiled=True)


def scatter_sum(partial, axes, members):
    blocks = partial.astype(bf16).reshape(members, -1, partial.shape[1])
    return jnp.sum(lax.all_to_all(blocks, axes, 0, 0, tiled=True).astype(f32), axis=0)


def local(tokens, doc_start, bias_table, attn_in, attn_out, ff_in, ff_out, gains, cotangent):
    heads_n, z_n, core_n = (lax.axis_size(axis) for axis in everyone)
    devices = heads_n * z_n * core_n
    at_head, at_z, at_core = (lax.axis_index(axis) for axis in everyone)
    turned = heads_n == z_n
    block_rows, model_width = tokens.shape[1:]
    layer_count, weight_rows = attn_in.shape[:2]
    blocks = z_n * core_n
    length = block_rows * blocks
    heads_all = bias_table.shape[1]

    if turned:
        group, spare = ("head", "core"), ("z",)
        member = at_head * core_n + at_core
        turn = [
            ((h * z_n + z) * core_n + c, (z * z_n + h) * core_n + c)
            for h in range(heads_n)
            for z in range(z_n)
            for c in range(core_n)
        ]
    else:
        group, spare = ("z", "core"), ("head",)
        member = at_z * core_n + at_core
    heads_dev = max(1, heads_all // blocks)
    head_groups = heads_all // heads_dev
    split = blocks // head_groups
    head_group, query_part = member // split, member % split
    query_rows = length // split
    width = heads_dev * head_dim
    first = (query_part * (query_rows // tile)).astype(jnp.int32).reshape(1)

    def relay(array):
        return lax.ppermute(array, everyone, turn) if turned else array

    def for_everyone(by_member):
        shape = by_member.shape[1:]
        if turned:
            spread = jnp.broadcast_to(
                by_member.reshape(heads_n, 1, core_n, *shape), (heads_n, z_n, core_n, *shape)
            )
        else:
            spread = jnp.broadcast_to(by_member[None], (heads_n, blocks, *shape))
        return spread.reshape(devices, *shape)

    def swap(array):
        return lax.all_to_all(array, everyone, 0, 0, tiled=True)

    starts = doc_start.astype(f32)
    if turned:
        starts = jnp.broadcast_to(starts[None, :, None], (heads_n, z_n, core_n, block_rows))
    else:
        starts = jnp.broadcast_to(starts[:, None, None], (heads_n, z_n, core_n, block_rows))
    ff_gains = gains[:, :, 1].astype(f32).reshape(1, -1)
    small = jnp.concatenate(
        [
            starts.reshape(devices, block_rows),
            jnp.broadcast_to(ff_gains, (devices, layer_count * weight_rows)),
        ],
        axis=1,
    )
    small = swap(small)
    doc_row = small[:blocks, :block_rows].reshape(1, length)
    doc_col = lax.dynamic_slice_in_dim(
        doc_row.reshape(length, 1), query_part * query_rows, query_rows, 0
    )
    gain_ff = jnp.transpose(
        small[:, block_rows:].reshape(devices, layer_count, weight_rows), (1, 0, 2)
    ).reshape(layer_count, 1, model_width)

    table = lax.dynamic_slice_in_dim(bias_table, head_group * heads_dev, heads_dev, 1)
    bucket_map = near_buckets()
    near = jnp.zeros((heads_dev, tile, 3 * tile), f32)
    for bucket_id in range(table.shape[0]):
        near = jnp.where(
            (bucket_map == bucket_id)[None], table[bucket_id][:, None, None], near
        )

    gain_attn = gains[:, :, 0].astype(f32)[:, :, None]
    own_in = attn_in.astype(f32)

    def fetch_in(layer_id):
        scaled = (own_in[layer_id] * gain_attn[layer_id]).astype(bf16)
        columns = jnp.transpose(
            scaled.reshape(weight_rows, 3, head_groups, width), (2, 0, 1, 3)
        ).reshape(head_groups, weight_rows, 3 * width)
        columns = jnp.repeat(columns, split, axis=0) if split > 1 else columns
        return swap(for_everyone(columns)).reshape(model_width, 3 * width)

    rows_near = blocks * weight_rows
    near_out = turned and rows_near % (core_n * width) == 0 and rows_near == core_n * width
    out_axes = ("z", "core") if near_out else everyone
    out_row = at_core * width if near_out else head_group * width

    def fetch_out(layer_id):
        return lax.dynamic_slice_in_dim(
            gather_rows(attn_out[layer_id], out_axes), out_row, width, 0
        )

    ff_group, ff_spare = ("head", "core"), "z"
    ff_members = heads_n * core_n

    def fetch_ff(layer_id):
        pair = jnp.concatenate([ff_in[layer_id], ff_out[layer_id]], axis=1)
        pair = gather_rows(pair, ff_spare)
        return pair[:, :model_width], pair[:, model_width:]

    hidden = relay(tokens[0]).astype(f32)
    upstream = relay(cotangent[0])
    weights_in = [fetch_in(layer_id) for layer_id in range(layer_count)]
    weights_out = [fetch_out(layer_id) for layer_id in range(layer_count)]
    weights_ff = [fetch_ff(layer_id) for layer_id in range(layer_count)]

    records = []
    for layer_id in range(layer_count):
        w_in, w_out, (w_up, w_down) = (
            weights_in[layer_id], weights_out[layer_id], weights_ff[layer_id],
        )
        inverse = inverse_rms(hidden)
        units = gather_rows((hidden * inverse).astype(bf16), group)
        qkv = jnp.dot(units, w_in, preferred_element_type=f32).astype(bf16)
        attended, stats = attention(qkv, doc_row, doc_col, first, table, near, query_rows)
        mixed = jnp.dot(attended, w_out, preferred_element_type=f32)
        if split > 1:
            mixed = lax.dynamic_update_slice_in_dim(
                jnp.zeros((length, model_width), f32), mixed, query_part * query_rows, 0
            )
        middle = hidden + scatter_sum(mixed, group, blocks)
        inverse_ff = inverse_rms(middle)
        normed_ff = gather_rows((middle * inverse_ff * gain_ff[layer_id]).astype(bf16), ff_group)
        pre_act = contract(normed_ff, w_up, 1, 1)
        cumulative = 0.5 * (1.0 + lax.erf(pre_act * np.float32(0.5**0.5)))
        activated = (pre_act * cumulative).astype(bf16)
        slope = cumulative + pre_act * jnp.exp(-0.5 * pre_act * pre_act) * np.float32(
            (2 * np.pi) ** -0.5
        )
        ff_result = jnp.dot(activated, w_down, preferred_element_type=f32)
        records.append(
            (hidden, inverse, units, qkv, attended, stats, middle, inverse_ff, normed_ff,
             activated, slope)
        )
        hidden = middle + scatter_sum(ff_result, ff_group, ff_members)
    output = relay(hidden)

    grads_ff, grads_in, grads_out, grads_gain_ff, grads_table = ([None] * layer_count for _ in range(5))
    for layer_id in reversed(range(layer_count)):
        w_in, w_out, (w_up, w_down) = (
            weights_in[layer_id], weights_out[layer_id], weights_ff[layer_id],
        )
        (hidden, inverse, units, qkv, attended, stats, middle, inverse_ff, normed_ff,
         activated, slope) = records[layer_id]
        grad_low = gather_rows(upstream.astype(bf16), ff_group)
        grad_pre = (contract(grad_low, w_down, 1, 1) * slope).astype(bf16)
        grad_normed = scatter_sum(
            jnp.dot(grad_pre, w_up, preferred_element_type=f32), ff_group, ff_members
        )
        grad_pair = jnp.concatenate(
            [contract(grad_pre, normed_ff, 0, 0), contract(activated, grad_low, 0, 0)], axis=1
        ).astype(bf16)
        grads_ff[layer_id] = lax.psum_scatter(
            grad_pair, ff_spare, scatter_dimension=0, tiled=True
        ).astype(f32)
        grads_gain_ff[layer_id] = jnp.sum(grad_normed * middle * inverse_ff, axis=0)
        grad_middle = upstream + unit_norm_back(
            middle, inverse_ff, grad_normed * gain_ff[layer_id]
        )
        branch = gather_rows(grad_middle.astype(bf16), group)
        if split > 1:
            branch = lax.dynamic_slice_in_dim(branch, query_part * query_rows, query_rows, 0)
        grad_attended = contract(branch, w_out, 1, 1).astype(bf16)
        grad_qkv, grad_near, grad_far = attention_back(
            qkv, doc_row, doc_col, attended, grad_attended, stats, first, table, near, split
        )
        grads_table[layer_id] = (grad_near, grad_far[:, :, 0, 0])
        grad_units = scatter_sum(contract(grad_qkv, w_in, 1, 1), group, blocks)
        upstream = grad_middle + unit_norm_back(hidden, inverse, grad_units)
        grad_out = contract(attended, branch, 0, 0).astype(bf16)
        grad_out = lax.dynamic_update_slice_in_dim(
            jnp.zeros((rows_near if near_out else model_width, model_width), bf16), grad_out, out_row, 0
        )
        grads_out[layer_id] = lax.psum_scatter(
            grad_out, out_axes, scatter_dimension=0, tiled=True
        )
        grads_in[layer_id] = contract(units, grad_qkv, 0, 0).astype(bf16)

    bucket_count = table.shape[0]
    near_sum = sum(entry[0] for entry in grads_table)
    far_sum = sum(entry[1] for entry in grads_table)
    grad_table = jnp.stack(
        [
            jnp.sum(jnp.where((bucket_map == bucket_id)[None], near_sum, 0.0), axis=(1, 2))
            for bucket_id in range(bucket_count)
        ]
    )
    grad_table = grad_table.at[15].add(far_sum[:, 0]).at[31].add(far_sum[:, 1])
    grad_table = lax.dynamic_update_slice_in_dim(
        jnp.zeros((bucket_count, heads_all), f32), grad_table, head_group * heads_dev, 1
    )
    grad_table = jnp.transpose(
        grad_table.reshape(blocks, bucket_count // blocks, heads_n, heads_all // heads_n),
        (2, 0, 1, 3),
    ).reshape(devices, -1)
    grad_gain_ff = jnp.transpose(
        jnp.stack(grads_gain_ff).reshape(layer_count, devices, weight_rows), (1, 0, 2)
    ).reshape(devices, -1)
    ends = jnp.sum(swap(jnp.concatenate([grad_gain_ff, grad_table], axis=1)), axis=0)
    grad_gain_ff = ends[: layer_count * weight_rows].reshape(layer_count, weight_rows)
    grad_bias_table = ends[layer_count * weight_rows :].reshape(
        bucket_count // blocks, heads_all // heads_n
    )

    grads_attn_in, grads_gains = [], []
    for layer_id in range(layer_count):
        parts = swap(grads_in[layer_id].reshape(devices, weight_rows, 3 * width)).astype(f32)
        if turned:
            parts = jnp.sum(
                parts.reshape(heads_n, z_n, core_n, weight_rows, 3 * width), axis=1
            )
        else:
            parts = jnp.sum(parts.reshape(heads_n, blocks, weight_rows, 3 * width), axis=0)
        parts = jnp.sum(parts.reshape(head_groups, split, weight_rows, 3, width), axis=1)
        unit_grad = jnp.transpose(parts, (1, 2, 0, 3)).reshape(weight_rows, 3 * model_width)
        grads_attn_in.append(unit_grad * gain_attn[layer_id])
        grads_gains.append(
            jnp.stack(
                [jnp.sum(unit_grad * own_in[layer_id], axis=1), grad_gain_ff[layer_id]], axis=1
            )
        )
    return (
        output[None],
        relay(upstream)[None],
        jnp.stack(grads_attn_in),
        jnp.stack([entry.astype(f32) for entry in grads_out]),
        jnp.stack([entry[:, :model_width] for entry in grads_ff]),
        jnp.stack([entry[:, model_width:] for entry in grads_ff]),
        jnp.stack(grads_gains),
        grad_bias_table,
    )


def solution(mesh):
    sizes = dict(mesh.shape)
    cores = 2
    fine = Mesh(
        mesh.devices.reshape(sizes["head"], sizes["blk"] // cores, cores), everyone
    )
    blk = ("z", "core")
    in_specs = (
        P("head", blk, None),
        P(None, blk),
        P(),
        P(None, everyone, None),
        P(None, everyone, None),
        P(None, everyone, None),
        P(None, everyone, None),
        P(None, everyone, None),
        P("head", blk, None),
    )
    out_specs = (
        P("head", blk, None),
        P("head", blk, None),
        P(None, everyone, None),
        P(None, everyone, None),
        P(None, everyone, None),
        P(None, everyone, None),
        P(None, everyone, None),
        P(blk, "head"),
    )
    return jax.shard_map(local, mesh=fine, in_specs=in_specs, out_specs=out_specs, check_vma=False)
```

```python
import functools

import jax
import jax.numpy as jnp
import numpy as np
from jax import lax
from jax.experimental import pallas as pl
from jax.experimental.pallas import tpu as pltpu
from jax.sharding import Mesh
from jax.sharding import PartitionSpec as P

bounds = (1, 2, 3, 4, 5, 6, 7, 8, 12, 16, 23, 32, 46, 64, 91)
epsilon = 1e-06
masked = -1e30
score_scale = 0.125
head_dim = 64
tile = 128
everyone = ("head", "z", "core")
bf16 = jnp.bfloat16
f32 = jnp.float32


def contract(lhs, rhs, lhs_dim, rhs_dim):
    return lax.dot_general(
        lhs, rhs, (((lhs_dim,), (rhs_dim,)), ((), ())), preferred_element_type=f32
    )


def near_buckets():
    offsets = np.arange(3 * tile)[None, :] - tile - np.arange(tile)[:, None]
    distance = np.abs(offsets)
    bucket = np.zeros(offsets.shape, np.int32)
    for boundary in bounds:
        bucket += (distance >= boundary).astype(np.int32)
    return bucket + 16 * (offsets > 0).astype(np.int32)


def fill_band(band, table, near, heads_dev, length):
    for head in range(heads_dev):
        band[head, :, : length - tile] = jnp.full((tile, length - tile), table[15, head], f32)
        band[head, :, length - tile : length + 2 * tile] = near[head]
        band[head, :, length + 2 * tile :] = jnp.full(
            (tile, length - 2 * tile), table[31, head], f32
        )


def band_starts(place, at, length):
    return [
        pl.multiple_of(length + (place[block] - place[at]) * tile, tile)
        for block in range(length // tile)
    ]


def attention_kernel(
    heads_dev, length, first, place, table, near, qkv, doc_row, doc_col, out, stats, band
):
    step = pl.program_id(0)
    width = heads_dev * head_dim

    @pl.when(step == 0)
    def _():
        fill_band(band, table, near, heads_dev, length)

    row = pl.multiple_of((first[0] + step) * tile, tile)
    starts = band_starts(place, first[0] + step, length)
    same_doc = doc_col[...] == doc_row[...]
    queries = qkv[pl.ds(row, tile), :width] * bf16(score_scale)
    lanes = lax.broadcasted_iota(jnp.int32, (tile, tile), 1)
    collected = jnp.zeros((tile, tile), f32)
    for head in range(heads_dev):
        own = slice(head * head_dim, (head + 1) * head_dim)
        keys = qkv[:, width + own.start : width + own.stop]
        values = qkv[:, 2 * width + own.start : 2 * width + own.stop]
        scores = contract(queries[:, own], keys, 1, 1)
        scores = scores + jnp.concatenate(
            [band[head, :, pl.ds(start, tile)] for start in starts], axis=1
        )
        scores = jnp.where(same_doc, scores, masked)
        peak = jnp.max(scores, axis=1, keepdims=True)
        weights = jnp.exp(scores - peak)
        total = jnp.sum(weights, axis=1, keepdims=True)
        mixed = contract(weights.astype(bf16), values, 1, 0) / total
        out[:, own] = mixed.astype(bf16)
        collected = jnp.where(lanes == head, peak + jnp.log(total), collected)
    stats[...] = collected


def attention_back_kernel(
    heads_dev, length, split, first, place, table, near, qkv, doc_row, doc_col, attended, grad_out, stats,
    grad_qkv, grad_near, grad_far, band, grad_band, grad_keys, grad_values,
):
    step = pl.program_id(0)
    width = heads_dev * head_dim

    @pl.when(step == 0)
    def _():
        fill_band(band, table, near, heads_dev, length)
        grad_band[...] = jnp.zeros_like(grad_band)
        grad_keys[...] = jnp.zeros_like(grad_keys)
        grad_values[...] = jnp.zeros_like(grad_values)
        if split > 1:
            grad_qkv[...] = jnp.zeros_like(grad_qkv)

    row = pl.multiple_of((first[0] + step) * tile, tile)
    starts = band_starts(place, first[0] + step, length)
    same_doc = doc_col[...] == doc_row[...]
    queries = qkv[pl.ds(row, tile), :width] * bf16(score_scale)
    for head in range(heads_dev):
        own = slice(head * head_dim, (head + 1) * head_dim)
        keys = qkv[:, width + own.start : width + own.stop]
        values = qkv[:, 2 * width + own.start : 2 * width + own.stop]
        upstream = grad_out[:, own]
        scores = contract(queries[:, own], keys, 1, 1) + jnp.concatenate(
            [band[head, :, pl.ds(start, tile)] for start in starts], axis=1
        )
        scores = jnp.where(same_doc, scores, masked)
        weights = jnp.exp(scores - stats[:, head : head + 1])
        delta = jnp.sum(
            upstream.astype(f32) * attended[:, own].astype(f32), axis=1, keepdims=True
        )
        grad_scores = weights * (contract(upstream, values, 1, 1) - delta)
        for block, start in enumerate(starts):
            grad_band[head, :, pl.ds(start, tile)] += grad_scores[
                :, block * tile : (block + 1) * tile
            ]
        grad_low = grad_scores.astype(bf16)
        grad_values[:, own] += contract(weights.astype(bf16), upstream, 0, 0)
        grad_keys[:, own] += contract(grad_low, queries[:, own], 0, 0)
        grad_qkv[pl.ds(row, tile), own] = (
            contract(grad_low, keys, 1, 0) * score_scale
        ).astype(bf16)

    @pl.when(step == pl.num_programs(0) - 1)
    def _():
        grad_qkv[:, width : 2 * width] = grad_keys[...].astype(bf16)
        grad_qkv[:, 2 * width :] = grad_values[...].astype(bf16)
        for head in range(heads_dev):
            grad_near[head] = grad_band[head, :, length - tile : length + 2 * tile]
            grad_far[head, 0] = jnp.full(
                (8, tile), jnp.sum(grad_band[head, :, : length - tile]), f32
            )
            grad_far[head, 1] = jnp.full(
                (8, tile), jnp.sum(grad_band[head, :, length + 2 * tile :]), f32
            )


def whole(shape):
    return pl.BlockSpec(shape, lambda step: (0,) * len(shape))


def attention(qkv, doc_row, doc_col, first, place, table, near, rows):
    length = qkv.shape[0]
    heads_dev = table.shape[1]
    width = heads_dev * head_dim
    return pl.pallas_call(
        functools.partial(attention_kernel, heads_dev, length),
        grid=(rows // tile,),
        in_specs=[
            pl.BlockSpec(memory_space=pltpu.SMEM),
            pl.BlockSpec(memory_space=pltpu.SMEM),
            pl.BlockSpec(memory_space=pltpu.SMEM),
            whole(near.shape),
            whole(qkv.shape),
            whole(doc_row.shape),
            pl.BlockSpec((tile, 1), lambda step: (step, 0)),
        ],
        out_specs=[
            pl.BlockSpec((tile, width), lambda step: (step, 0)),
            pl.BlockSpec((tile, tile), lambda step: (step, 0)),
        ],
        out_shape=[
            jax.ShapeDtypeStruct((rows, width), bf16),
            jax.ShapeDtypeStruct((rows, tile), f32),
        ],
        scratch_shapes=[pltpu.VMEM((heads_dev, tile, 2 * length), f32)],
        compiler_params=pltpu.CompilerParams(vmem_limit_bytes=40 * 2**20),
        cost_estimate=pl.CostEstimate(
            flops=4 * rows * length * width,
            bytes_accessed=4 * length * width * 2,
            transcendentals=rows * length * heads_dev,
        ),
    )(first, place, table, near, qkv, doc_row, doc_col)


def attention_back(
    qkv, doc_row, doc_col, attended, grad_out, stats, first, place, table, near, split
):
    length = qkv.shape[0]
    rows = grad_out.shape[0]
    heads_dev = table.shape[1]
    width = heads_dev * head_dim
    return pl.pallas_call(
        functools.partial(attention_back_kernel, heads_dev, length, split),
        grid=(rows // tile,),
        in_specs=[
            pl.BlockSpec(memory_space=pltpu.SMEM),
            pl.BlockSpec(memory_space=pltpu.SMEM),
            pl.BlockSpec(memory_space=pltpu.SMEM),
            whole(near.shape),
            whole(qkv.shape),
            whole(doc_row.shape),
            pl.BlockSpec((tile, 1), lambda step: (step, 0)),
            pl.BlockSpec((tile, width), lambda step: (step, 0)),
            pl.BlockSpec((tile, width), lambda step: (step, 0)),
            pl.BlockSpec((tile, tile), lambda step: (step, 0)),
        ],
        out_specs=[
            whole((length, 3 * width)),
            whole((heads_dev, tile, 3 * tile)),
            whole((heads_dev, 2, 8, tile)),
        ],
        out_shape=[
            jax.ShapeDtypeStruct((length, 3 * width), bf16),
            jax.ShapeDtypeStruct((heads_dev, tile, 3 * tile), f32),
            jax.ShapeDtypeStruct((heads_dev, 2, 8, tile), f32),
        ],
        scratch_shapes=[
            pltpu.VMEM((heads_dev, tile, 2 * length), f32),
            pltpu.VMEM((heads_dev, tile, 2 * length), f32),
            pltpu.VMEM((length, width), f32),
            pltpu.VMEM((length, width), f32),
        ],
        compiler_params=pltpu.CompilerParams(vmem_limit_bytes=48 * 2**20),
        cost_estimate=pl.CostEstimate(
            flops=10 * rows * length * width,
            bytes_accessed=8 * length * width * 2,
            transcendentals=rows * length * heads_dev,
        ),
    )(first, place, table, near, qkv, doc_row, doc_col, attended, grad_out, stats)


def inverse_rms(hidden):
    return lax.rsqrt(jnp.mean(hidden * hidden, axis=-1, keepdims=True) + epsilon)


def unit_norm_back(hidden, inverse, grad_unit):
    unit = hidden * inverse
    return inverse * (grad_unit - unit * jnp.mean(grad_unit * unit, axis=-1, keepdims=True))


def gather_rows(block, axes):
    return lax.all_gather(block, axes, axis=0, tiled=True)


def toggle(array, axis, bits):
    return lax.ppermute(array, axis, [(i, i ^ bits) for i in range(lax.axis_size(axis))])


def plane_gather(block, stream):
    if stream:
        others = [toggle(block, "head", bits) for bits in (1, 2, 3)]
        near_core = [block] + others
        return jnp.concatenate(near_core + [toggle(part, "core", 1) for part in near_core])
    near_core = jnp.concatenate([block] + [toggle(block, "head", bits) for bits in (1, 2, 3)])
    return jnp.concatenate([near_core, toggle(near_core, "core", 1)])


def plane_scatter(partial, stream):
    half = partial.shape[0] // 2
    arrived = toggle(partial[half:].astype(bf16), "core", 1)
    total = (partial[:half] + arrived.astype(f32)).reshape(4, -1, partial.shape[1])
    if stream:
        others = [toggle(total[bits].astype(bf16), "head", bits) for bits in (1, 2, 3)]
        return total[0] + (others[0].astype(f32) + others[1].astype(f32)) + others[2].astype(f32)
    at_head = lax.axis_index("head")
    sent = total.astype(bf16)
    low = at_head % 2 == 1
    high = at_head // 2 == 1
    sent = jnp.where(low, sent.reshape(2, 2, *sent.shape[1:])[:, ::-1].reshape(sent.shape), sent)
    sent = jnp.where(high, sent.reshape(2, 2, *sent.shape[1:])[::-1].reshape(sent.shape), sent)
    return jnp.sum(lax.all_to_all(sent, "head", 0, 0, tiled=True).astype(f32), axis=0)


def scatter_sum(partial, axes, members):
    blocks = partial.astype(bf16).reshape(members, -1, partial.shape[1])
    return jnp.sum(lax.all_to_all(blocks, axes, 0, 0, tiled=True).astype(f32), axis=0)


def local(tokens, doc_start, bias_table, attn_in, attn_out, ff_in, ff_out, gains, cotangent):
    heads_n, z_n, core_n = (lax.axis_size(axis) for axis in everyone)
    devices = heads_n * z_n * core_n
    at_head, at_z, at_core = (lax.axis_index(axis) for axis in everyone)
    turned = heads_n == z_n == 4
    block_rows, model_width = tokens.shape[1:]
    layer_count, weight_rows = attn_in.shape[:2]
    blocks = z_n * core_n
    length = block_rows * blocks
    heads_all = bias_table.shape[1]

    if turned:
        group, spare = ("head", "core"), ("z",)
        member = at_head * core_n + at_core
        turn = [
            ((h * z_n + z) * core_n + c, (z * z_n + h) * core_n + c)
            for h in range(heads_n)
            for z in range(z_n)
            for c in range(core_n)
        ]
    else:
        group, spare = ("z", "core"), ("head",)
        member = at_z * core_n + at_core
    heads_dev = max(1, heads_all // blocks)
    head_groups = heads_all // heads_dev
    split = blocks // head_groups
    head_group, query_part = member // split, member % split
    query_rows = length // split
    width = heads_dev * head_dim
    first = (query_part * (query_rows // tile)).astype(jnp.int32).reshape(1)
    if turned:
        place = jnp.stack(
            [
                (at_head ^ bits) * core_n + (at_core ^ other)
                for other in range(core_n)
                for bits in range(heads_n)
            ]
        ).astype(jnp.int32)
    else:
        place = jnp.arange(blocks, dtype=jnp.int32)

    def gather(block, axes, stream):
        return plane_gather(block, stream) if turned else gather_rows(block, axes)

    def scatter(partial, axes, members, stream):
        return plane_scatter(partial, stream) if turned else scatter_sum(partial, axes, members)

    def relay(array):
        return lax.ppermute(array, everyone, turn) if turned else array

    def for_everyone(by_member):
        shape = by_member.shape[1:]
        if turned:
            spread = jnp.broadcast_to(
                by_member.reshape(heads_n, 1, core_n, *shape), (heads_n, z_n, core_n, *shape)
            )
        else:
            spread = jnp.broadcast_to(by_member[None], (heads_n, blocks, *shape))
        return spread.reshape(devices, *shape)

    def swap(array):
        return lax.all_to_all(array, everyone, 0, 0, tiled=True)

    starts = doc_start.astype(f32)
    if turned:
        starts = jnp.broadcast_to(starts[None, :, None], (heads_n, z_n, core_n, block_rows))
    else:
        starts = jnp.broadcast_to(starts[:, None, None], (heads_n, z_n, core_n, block_rows))
    ff_gains = gains[:, :, 1].astype(f32).reshape(1, -1)
    small = jnp.concatenate(
        [
            starts.reshape(devices, block_rows),
            jnp.broadcast_to(ff_gains, (devices, layer_count * weight_rows)),
        ],
        axis=1,
    )
    small = swap(small)
    doc_row = small[:blocks, :block_rows]
    if turned:
        doc_row = doc_row.reshape(2, 2, core_n, block_rows)
        for axis, bit in ((0, at_head // 2), (1, at_head % 2), (2, at_core)):
            doc_row = jnp.where(bit == 1, jnp.flip(doc_row, axis), doc_row)
        doc_row = jnp.transpose(doc_row, (2, 0, 1, 3))
    doc_row = doc_row.reshape(1, length)
    doc_col = lax.dynamic_slice_in_dim(
        doc_row.reshape(length, 1), query_part * query_rows, query_rows, 0
    )
    gain_ff = jnp.transpose(
        small[:, block_rows:].reshape(devices, layer_count, weight_rows), (1, 0, 2)
    ).reshape(layer_count, 1, model_width)

    table = lax.dynamic_slice_in_dim(bias_table, head_group * heads_dev, heads_dev, 1)
    bucket_map = near_buckets()
    near = jnp.zeros((heads_dev, tile, 3 * tile), f32)
    for bucket_id in range(table.shape[0]):
        near = jnp.where(
            (bucket_map == bucket_id)[None], table[bucket_id][:, None, None], near
        )

    gain_attn = gains[:, :, 0].astype(f32)[:, :, None]
    own_in = attn_in.astype(f32)

    def fetch_in(layer_id):
        scaled = (own_in[layer_id] * gain_attn[layer_id]).astype(bf16)
        columns = jnp.transpose(
            scaled.reshape(weight_rows, 3, head_groups, width), (2, 0, 1, 3)
        ).reshape(head_groups, weight_rows, 3 * width)
        columns = jnp.repeat(columns, split, axis=0) if split > 1 else columns
        return swap(for_everyone(columns)).reshape(model_width, 3 * width)

    rows_near = blocks * weight_rows
    near_out = turned and rows_near % (core_n * width) == 0 and rows_near == core_n * width
    out_axes = ("z", "core") if near_out else everyone
    out_row = at_core * width if near_out else head_group * width

    gathered_out = lax.dynamic_slice_in_dim(
        lax.all_gather(attn_out, out_axes, axis=1, tiled=True), out_row, width, 1
    )

    ff_group, ff_spare = ("head", "core"), "z"
    ff_members = heads_n * core_n

    def fetch_ff(layer_id):
        pair = jnp.concatenate([ff_in[layer_id], ff_out[layer_id]], axis=1)
        pair = gather_rows(pair, ff_spare)
        return pair[:, :model_width], pair[:, model_width:]

    hidden = relay(tokens[0]).astype(f32)
    upstream = relay(cotangent[0].astype(bf16)).astype(f32) if turned else cotangent[0]
    weights_in = [fetch_in(layer_id) for layer_id in range(layer_count)]
    weights_out = [gathered_out[layer_id] for layer_id in range(layer_count)]
    weights_ff = [fetch_ff(layer_id) for layer_id in range(layer_count)]

    records = []
    for layer_id in range(layer_count):
        w_in, w_out, (w_up, w_down) = (
            weights_in[layer_id], weights_out[layer_id], weights_ff[layer_id],
        )
        inverse = inverse_rms(hidden)
        units = gather((hidden * inverse).astype(bf16), group, False)
        qkv = jnp.dot(units, w_in, preferred_element_type=f32).astype(bf16)
        attended, stats = attention(
            qkv, doc_row, doc_col, first, place, table, near, query_rows
        )
        mixed = jnp.dot(attended, w_out, preferred_element_type=f32)
        if split > 1:
            mixed = lax.dynamic_update_slice_in_dim(
                jnp.zeros((length, model_width), f32), mixed, query_part * query_rows, 0
            )
        middle = hidden + scatter(mixed, group, blocks, True)
        inverse_ff = inverse_rms(middle)
        normed_ff = gather(
            (middle * inverse_ff * gain_ff[layer_id]).astype(bf16), ff_group, True
        )
        pre_act = contract(normed_ff, w_up, 1, 1)
        cumulative = 0.5 * (1.0 + lax.erf(pre_act * np.float32(0.5**0.5)))
        activated = (pre_act * cumulative).astype(bf16)
        slope = cumulative + pre_act * jnp.exp(-0.5 * pre_act * pre_act) * np.float32(
            (2 * np.pi) ** -0.5
        )
        ff_result = jnp.dot(activated, w_down, preferred_element_type=f32)
        records.append(
            (hidden, inverse, units, qkv, attended, stats, middle, inverse_ff, normed_ff,
             activated, slope)
        )
        hidden = middle + scatter(ff_result, ff_group, ff_members, False)
    output = relay(hidden.astype(bf16)).astype(f32) if turned else hidden

    grads_ff, grads_in, grads_out, grads_gain_ff, grads_table = ([None] * layer_count for _ in range(5))
    for layer_id in reversed(range(layer_count)):
        w_in, w_out, (w_up, w_down) = (
            weights_in[layer_id], weights_out[layer_id], weights_ff[layer_id],
        )
        (hidden, inverse, units, qkv, attended, stats, middle, inverse_ff, normed_ff,
         activated, slope) = records[layer_id]
        grad_low = gather(upstream.astype(bf16), ff_group, True)
        grad_pre = (contract(grad_low, w_down, 1, 1) * slope).astype(bf16)
        grad_normed = scatter(
            jnp.dot(grad_pre, w_up, preferred_element_type=f32), ff_group, ff_members, False
        )
        grad_pair = jnp.concatenate(
            [contract(grad_pre, normed_ff, 0, 0), contract(activated, grad_low, 0, 0)], axis=1
        ).astype(bf16)
        grads_ff[layer_id] = lax.psum_scatter(
            grad_pair, ff_spare, scatter_dimension=0, tiled=True
        ).astype(f32)
        grads_gain_ff[layer_id] = jnp.sum(grad_normed * middle * inverse_ff, axis=0)
        grad_middle = upstream + unit_norm_back(
            middle, inverse_ff, grad_normed * gain_ff[layer_id]
        )
        branch = gather(grad_middle.astype(bf16), group, False)
        if split > 1:
            branch = lax.dynamic_slice_in_dim(branch, query_part * query_rows, query_rows, 0)
        grad_attended = contract(branch, w_out, 1, 1).astype(bf16)
        grad_qkv, grad_near, grad_far = attention_back(
            qkv, doc_row, doc_col, attended, grad_attended, stats, first, place, table, near, split
        )
        grads_table[layer_id] = (grad_near, grad_far[:, :, 0, 0])
        grad_units = scatter(contract(grad_qkv, w_in, 1, 1), group, blocks, True)
        upstream = grad_middle + unit_norm_back(hidden, inverse, grad_units)
        grad_out = contract(attended, branch, 0, 0).astype(bf16)
        grad_out = lax.dynamic_update_slice_in_dim(
            jnp.zeros((rows_near if near_out else model_width, model_width), bf16), grad_out, out_row, 0
        )
        grads_out[layer_id] = lax.psum_scatter(
            grad_out, out_axes, scatter_dimension=0, tiled=True
        )
        grads_in[layer_id] = contract(units, grad_qkv, 0, 0).astype(bf16)

    bucket_count = table.shape[0]
    near_sum = sum(entry[0] for entry in grads_table)
    far_sum = sum(entry[1] for entry in grads_table)
    grad_table = jnp.stack(
        [
            jnp.sum(jnp.where((bucket_map == bucket_id)[None], near_sum, 0.0), axis=(1, 2))
            for bucket_id in range(bucket_count)
        ]
    )
    grad_table = grad_table.at[15].add(far_sum[:, 0]).at[31].add(far_sum[:, 1])
    grad_table = lax.dynamic_update_slice_in_dim(
        jnp.zeros((bucket_count, heads_all), f32), grad_table, head_group * heads_dev, 1
    )
    grad_table = jnp.transpose(
        grad_table.reshape(blocks, bucket_count // blocks, heads_n, heads_all // heads_n),
        (2, 0, 1, 3),
    ).reshape(devices, -1)
    grad_gain_ff = jnp.transpose(
        jnp.stack(grads_gain_ff).reshape(layer_count, devices, weight_rows), (1, 0, 2)
    ).reshape(devices, -1)
    ends = jnp.sum(swap(jnp.concatenate([grad_gain_ff, grad_table], axis=1)), axis=0)
    grad_gain_ff = ends[: layer_count * weight_rows].reshape(layer_count, weight_rows)
    grad_bias_table = ends[layer_count * weight_rows :].reshape(
        bucket_count // blocks, heads_all // heads_n
    )

    grads_attn_in, grads_gains = [], []
    for layer_id in range(layer_count):
        parts = swap(grads_in[layer_id].reshape(devices, weight_rows, 3 * width)).astype(f32)
        if turned:
            parts = jnp.sum(
                parts.reshape(heads_n, z_n, core_n, weight_rows, 3 * width), axis=1
            )
        else:
            parts = jnp.sum(parts.reshape(heads_n, blocks, weight_rows, 3 * width), axis=0)
        parts = jnp.sum(parts.reshape(head_groups, split, weight_rows, 3, width), axis=1)
        unit_grad = jnp.transpose(parts, (1, 2, 0, 3)).reshape(weight_rows, 3 * model_width)
        grads_attn_in.append(unit_grad * gain_attn[layer_id])
        grads_gains.append(
            jnp.stack(
                [jnp.sum(unit_grad * own_in[layer_id], axis=1), grad_gain_ff[layer_id]], axis=1
            )
        )
    return (
        output[None],
        (relay(upstream.astype(bf16)).astype(f32) if turned else upstream)[None],
        jnp.stack(grads_attn_in),
        jnp.stack([entry.astype(f32) for entry in grads_out]),
        jnp.stack([entry[:, :model_width] for entry in grads_ff]),
        jnp.stack([entry[:, model_width:] for entry in grads_ff]),
        jnp.stack(grads_gains),
        grad_bias_table,
    )


def solution(mesh):
    sizes = dict(mesh.shape)
    cores = 2
    fine = Mesh(
        mesh.devices.reshape(sizes["head"], sizes["blk"] // cores, cores), everyone
    )
    blk = ("z", "core")
    in_specs = (
        P("head", blk, None),
        P(None, blk),
        P(),
        P(None, everyone, None),
        P(None, everyone, None),
        P(None, everyone, None),
        P(None, everyone, None),
        P(None, everyone, None),
        P("head", blk, None),
    )
    out_specs = (
        P("head", blk, None),
        P("head", blk, None),
        P(None, everyone, None),
        P(None, everyone, None),
        P(None, everyone, None),
        P(None, everyone, None),
        P(None, everyone, None),
        P(blk, "head"),
    )
    return jax.shard_map(local, mesh=fine, in_specs=in_specs, out_specs=out_specs, check_vma=False)
```

```python
import functools

import jax
import jax.numpy as jnp
import numpy as np
from jax import lax
from jax.experimental import pallas as pl
from jax.experimental.pallas import tpu as pltpu
from jax.sharding import Mesh
from jax.sharding import PartitionSpec as P

bounds = (1, 2, 3, 4, 5, 6, 7, 8, 12, 16, 23, 32, 46, 64, 91)
epsilon = 1e-06
masked = -1e30
score_scale = 0.125
head_dim = 64
tile = 128
everyone = ("head", "z", "core")
bf16 = jnp.bfloat16
f32 = jnp.float32


def contract(lhs, rhs, lhs_dim, rhs_dim):
    return lax.dot_general(
        lhs, rhs, (((lhs_dim,), (rhs_dim,)), ((), ())), preferred_element_type=f32
    )


def near_buckets():
    offsets = np.arange(3 * tile)[None, :] - tile - np.arange(tile)[:, None]
    distance = np.abs(offsets)
    bucket = np.zeros(offsets.shape, np.int32)
    for boundary in bounds:
        bucket += (distance >= boundary).astype(np.int32)
    return bucket + 16 * (offsets > 0).astype(np.int32)


def fill_band(band, table, near, heads_dev, length):
    for head in range(heads_dev):
        band[head, :, : length - tile] = jnp.full((tile, length - tile), table[15, head], f32)
        band[head, :, length - tile : length + 2 * tile] = near[head]
        band[head, :, length + 2 * tile :] = jnp.full(
            (tile, length - 2 * tile), table[31, head], f32
        )


def band_starts(place, at, length):
    return [
        pl.multiple_of(length + (place[block] - place[at]) * tile, tile)
        for block in range(length // tile)
    ]


def attention_kernel(
    heads_dev, length, first, place, table, near, qkv, doc_row, doc_col, out, stats, band
):
    step = pl.program_id(0)
    width = heads_dev * head_dim

    @pl.when(step == 0)
    def _():
        fill_band(band, table, near, heads_dev, length)

    row = pl.multiple_of((first[0] + step) * tile, tile)
    out_row = pl.multiple_of((place[first[0] + step] - first[0]) * tile, tile)
    starts = band_starts(place, first[0] + step, length)
    same_doc = doc_col[...] == doc_row[...]
    queries = qkv[pl.ds(row, tile), :width] * bf16(score_scale)
    lanes = lax.broadcasted_iota(jnp.int32, (tile, tile), 1)
    collected = jnp.zeros((tile, tile), f32)
    for head in range(heads_dev):
        own = slice(head * head_dim, (head + 1) * head_dim)
        keys = qkv[:, width + own.start : width + own.stop]
        values = qkv[:, 2 * width + own.start : 2 * width + own.stop]
        scores = contract(queries[:, own], keys, 1, 1)
        scores = scores + jnp.concatenate(
            [band[head, :, pl.ds(start, tile)] for start in starts], axis=1
        )
        scores = jnp.where(same_doc, scores, masked)
        peak = jnp.max(scores, axis=1, keepdims=True)
        weights = jnp.exp(scores - peak)
        total = jnp.sum(weights, axis=1, keepdims=True)
        mixed = contract(weights.astype(bf16), values, 1, 0) / total
        out[pl.ds(out_row, tile), own] = mixed.astype(bf16)
        collected = jnp.where(lanes == head, peak + jnp.log(total), collected)
    stats[...] = collected


def attention_back_kernel(
    heads_dev, length, split, first, place, table, near, qkv, doc_row, doc_col, attended, grad_out, stats,
    grad_qkv, grad_near, grad_far, band, grad_band, grad_keys, grad_values,
):
    step = pl.program_id(0)
    width = heads_dev * head_dim

    @pl.when(step == 0)
    def _():
        fill_band(band, table, near, heads_dev, length)
        grad_band[...] = jnp.zeros_like(grad_band)
        grad_keys[...] = jnp.zeros_like(grad_keys)
        grad_values[...] = jnp.zeros_like(grad_values)
        if split > 1:
            grad_qkv[...] = jnp.zeros_like(grad_qkv)

    row = pl.multiple_of((first[0] + step) * tile, tile)
    out_row = pl.multiple_of((place[first[0] + step] - first[0]) * tile, tile)
    starts = band_starts(place, first[0] + step, length)
    same_doc = doc_col[...] == doc_row[...]
    queries = qkv[pl.ds(row, tile), :width] * bf16(score_scale)
    for head in range(heads_dev):
        own = slice(head * head_dim, (head + 1) * head_dim)
        keys = qkv[:, width + own.start : width + own.stop]
        values = qkv[:, 2 * width + own.start : 2 * width + own.stop]
        upstream = grad_out[pl.ds(out_row, tile), own]
        scores = contract(queries[:, own], keys, 1, 1) + jnp.concatenate(
            [band[head, :, pl.ds(start, tile)] for start in starts], axis=1
        )
        scores = jnp.where(same_doc, scores, masked)
        weights = jnp.exp(scores - stats[:, head : head + 1])
        delta = jnp.sum(
            upstream.astype(f32) * attended[pl.ds(out_row, tile), own].astype(f32),
            axis=1,
            keepdims=True,
        )
        grad_scores = weights * (contract(upstream, values, 1, 1) - delta)
        for block, start in enumerate(starts):
            grad_band[head, :, pl.ds(start, tile)] += grad_scores[
                :, block * tile : (block + 1) * tile
            ]
        grad_low = grad_scores.astype(bf16)
        grad_values[:, own] += contract(weights.astype(bf16), upstream, 0, 0)
        grad_keys[:, own] += contract(grad_low, queries[:, own], 0, 0)
        grad_qkv[pl.ds(row, tile), own] = (
            contract(grad_low, keys, 1, 0) * score_scale
        ).astype(bf16)

    @pl.when(step == pl.num_programs(0) - 1)
    def _():
        grad_qkv[:, width : 2 * width] = grad_keys[...].astype(bf16)
        grad_qkv[:, 2 * width :] = grad_values[...].astype(bf16)
        for head in range(heads_dev):
            grad_near[head] = grad_band[head, :, length - tile : length + 2 * tile]
            grad_far[head, 0] = jnp.full(
                (8, tile), jnp.sum(grad_band[head, :, : length - tile]), f32
            )
            grad_far[head, 1] = jnp.full(
                (8, tile), jnp.sum(grad_band[head, :, length + 2 * tile :]), f32
            )


def whole(shape):
    return pl.BlockSpec(shape, lambda step: (0,) * len(shape))


def attention(qkv, doc_row, doc_col, first, place, table, near, rows):
    length = qkv.shape[0]
    heads_dev = table.shape[1]
    width = heads_dev * head_dim
    return pl.pallas_call(
        functools.partial(attention_kernel, heads_dev, length),
        grid=(rows // tile,),
        in_specs=[
            pl.BlockSpec(memory_space=pltpu.SMEM),
            pl.BlockSpec(memory_space=pltpu.SMEM),
            pl.BlockSpec(memory_space=pltpu.SMEM),
            whole(near.shape),
            whole(qkv.shape),
            whole(doc_row.shape),
            pl.BlockSpec((tile, 1), lambda step: (step, 0)),
        ],
        out_specs=[
            whole((rows, width)),
            pl.BlockSpec((tile, tile), lambda step: (step, 0)),
        ],
        out_shape=[
            jax.ShapeDtypeStruct((rows, width), bf16),
            jax.ShapeDtypeStruct((rows, tile), f32),
        ],
        scratch_shapes=[pltpu.VMEM((heads_dev, tile, 2 * length), f32)],
        compiler_params=pltpu.CompilerParams(vmem_limit_bytes=40 * 2**20),
        cost_estimate=pl.CostEstimate(
            flops=4 * rows * length * width,
            bytes_accessed=4 * length * width * 2,
            transcendentals=rows * length * heads_dev,
        ),
    )(first, place, table, near, qkv, doc_row, doc_col)


def attention_back(
    qkv, doc_row, doc_col, attended, grad_out, stats, first, place, table, near, split
):
    length = qkv.shape[0]
    rows = grad_out.shape[0]
    heads_dev = table.shape[1]
    width = heads_dev * head_dim
    return pl.pallas_call(
        functools.partial(attention_back_kernel, heads_dev, length, split),
        grid=(rows // tile,),
        in_specs=[
            pl.BlockSpec(memory_space=pltpu.SMEM),
            pl.BlockSpec(memory_space=pltpu.SMEM),
            pl.BlockSpec(memory_space=pltpu.SMEM),
            whole(near.shape),
            whole(qkv.shape),
            whole(doc_row.shape),
            pl.BlockSpec((tile, 1), lambda step: (step, 0)),
            whole((rows, width)),
            whole((rows, width)),
            pl.BlockSpec((tile, tile), lambda step: (step, 0)),
        ],
        out_specs=[
            whole((length, 3 * width)),
            whole((heads_dev, tile, 3 * tile)),
            whole((heads_dev, 2, 8, tile)),
        ],
        out_shape=[
            jax.ShapeDtypeStruct((length, 3 * width), bf16),
            jax.ShapeDtypeStruct((heads_dev, tile, 3 * tile), f32),
            jax.ShapeDtypeStruct((heads_dev, 2, 8, tile), f32),
        ],
        scratch_shapes=[
            pltpu.VMEM((heads_dev, tile, 2 * length), f32),
            pltpu.VMEM((heads_dev, tile, 2 * length), f32),
            pltpu.VMEM((length, width), f32),
            pltpu.VMEM((length, width), f32),
        ],
        compiler_params=pltpu.CompilerParams(vmem_limit_bytes=48 * 2**20),
        cost_estimate=pl.CostEstimate(
            flops=10 * rows * length * width,
            bytes_accessed=8 * length * width * 2,
            transcendentals=rows * length * heads_dev,
        ),
    )(first, place, table, near, qkv, doc_row, doc_col, attended, grad_out, stats)


def call(kernel, shapes, *operands, smem=0):
    return pl.pallas_call(
        kernel,
        in_specs=[pl.BlockSpec(memory_space=pltpu.SMEM)] * smem
        + [pl.BlockSpec(memory_space=pltpu.VMEM)] * (len(operands) - smem),
        out_specs=[pl.BlockSpec(memory_space=pltpu.VMEM)] * len(shapes),
        out_shape=[jax.ShapeDtypeStruct(shape, kind) for shape, kind in shapes],
        compiler_params=pltpu.CompilerParams(vmem_limit_bytes=32 * 2**20),
    )(*operands)


def share_in_kernel(layers, members, copies, core_n, attn_in, gains, *outs):
    width = attn_in.shape[2] // (3 * members)
    for layer_id in range(layers):
        for member in range(members):
            block = jnp.concatenate(
                [
                    attn_in[layer_id, :, (part * members + member) * width :][:, :width]
                    for part in range(3)
                ],
                axis=1,
            )
            block = (block.astype(f32) * gains[layer_id]).astype(bf16)
            for copy in range(copies):
                target = (member // core_n * copies + copy) * core_n + member % core_n
                outs[layer_id][target] = block


def close_kernel(kept, own, x_part, y_part, xy_part, hidden, units):
    total = (own[...] + x_part[...].astype(f32)) + (
        y_part[...].astype(f32) + xy_part[...].astype(f32)
    )
    total = kept[...] + total
    hidden[...] = total
    units[...] = (total * inverse_rms(total)).astype(bf16)


def out_kernel(pieces, weight, hidden, gain, merged, middle, normed):
    for member in range(pieces.shape[0]):
        merged[:, member * pieces.shape[2] : (member + 1) * pieces.shape[2]] = pieces[member]
    total = hidden[...] + contract(merged[...], weight[...], 1, 0)
    middle[...] = total
    normed[...] = (total * inverse_rms(total) * gain[...]).astype(bf16)


def middle_back_kernel(
    upstream, own, x_part, y_part, xy_part, middle, gain, weight, grad_middle, branch, pieces, grad_gain
):
    grad_normed = (own[...] + x_part[...].astype(f32)) + (
        y_part[...].astype(f32) + xy_part[...].astype(f32)
    )
    inverse = inverse_rms(middle[...])
    grad_gain[...] = jnp.sum(grad_normed * middle[...] * inverse, axis=0, keepdims=True)
    total = upstream[...] + unit_norm_back(middle[...], inverse, grad_normed * gain[...])
    grad_middle[...] = total
    branch[...] = total.astype(bf16)
    spread = contract(branch[...], weight[...], 1, 1).astype(bf16)
    for member in range(pieces.shape[0]):
        pieces[member] = spread[:, member * pieces.shape[2] : (member + 1) * pieces.shape[2]]


def layer_back_kernel(grad_middle, own, x_part, y_part, xy_part, hidden, upstream, low):
    grad_units = (own[...] + x_part[...].astype(f32)) + (
        y_part[...].astype(f32) + xy_part[...].astype(f32)
    )
    total = grad_middle[...] + unit_norm_back(hidden[...], inverse_rms(hidden[...]), grad_units)
    upstream[...] = total
    low[...] = total.astype(bf16)


def inverse_rms(hidden):
    return lax.rsqrt(jnp.mean(hidden * hidden, axis=-1, keepdims=True) + epsilon)


def prepare(bias_table, first_head, heads_dev):
    table = lax.dynamic_slice_in_dim(bias_table, first_head, heads_dev, 1)
    bucket_map = near_buckets()
    near = jnp.zeros((heads_dev, tile, 3 * tile), f32)
    for bucket_id in range(table.shape[0]):
        near = jnp.where((bucket_map == bucket_id)[None], table[bucket_id][:, None, None], near)
    return table, near


def bucket_grads(near_sum, far_sum, bucket_count):
    bucket_map = near_buckets()
    grad_table = jnp.stack(
        [
            jnp.sum(jnp.where((bucket_map == bucket_id)[None], near_sum, 0.0), axis=(1, 2))
            for bucket_id in range(bucket_count)
        ]
    )
    return grad_table.at[15].add(far_sum[:, 0]).at[31].add(far_sum[:, 1])


def gelu_parts(pre_act):
    cumulative = 0.5 * (1.0 + lax.erf(pre_act * np.float32(0.5**0.5)))
    slope = cumulative + pre_act * jnp.exp(-0.5 * pre_act * pre_act) * np.float32(
        (2 * np.pi) ** -0.5
    )
    return (pre_act * cumulative).astype(bf16), slope


def unit_norm_back(hidden, inverse, grad_unit):
    unit = hidden * inverse
    return inverse * (grad_unit - unit * jnp.mean(grad_unit * unit, axis=-1, keepdims=True))


def gather_rows(block, axes):
    return lax.all_gather(block, axes, axis=0, tiled=True)


def toggle(array, axis, bits):
    return lax.ppermute(array, axis, [(i, i ^ bits) for i in range(lax.axis_size(axis))])


def plane_gather(block):
    near_core = jnp.concatenate([block] + [toggle(block, "head", bits) for bits in (1, 2, 3)])
    return jnp.concatenate([near_core, toggle(near_core, "core", 1)])


def plane_scatter(partial):
    half = partial.shape[0] // 2
    arrived = toggle(partial[half:].astype(bf16), "core", 1)
    total = (partial[:half] + arrived.astype(f32)).reshape(4, -1, partial.shape[1])
    return [total[0]] + [toggle(total[bits].astype(bf16), "head", bits) for bits in (1, 2, 3)]


def after(array, other):
    return lax.optimization_barrier((array, other))[0]


def scatter_sum(partial, axes, members):
    blocks = partial.astype(bf16).reshape(members, -1, partial.shape[1])
    return jnp.sum(lax.all_to_all(blocks, axes, 0, 0, tiled=True).astype(f32), axis=0)


def local_general(tokens, doc_start, bias_table, attn_in, attn_out, ff_in, ff_out, gains, cotangent):
    heads_n, z_n, core_n = (lax.axis_size(axis) for axis in everyone)
    devices = heads_n * z_n * core_n
    group, spare = ("z", "core"), "head"
    ff_group, ff_spare, ff_members = ("head", "core"), "z", heads_n * core_n
    blocks = z_n * core_n
    block_rows, model_width = tokens.shape[1:]
    layer_count, weight_rows = attn_in.shape[:2]
    length = block_rows * blocks
    heads_all = bias_table.shape[1]
    member = lax.axis_index("z") * core_n + lax.axis_index("core")
    heads_dev = max(1, heads_all // blocks)
    head_groups = heads_all // heads_dev
    split = blocks // head_groups
    head_group, query_part = member // split, member % split
    query_rows = length // split
    width = heads_dev * head_dim
    first = (query_part * (query_rows // tile)).astype(jnp.int32).reshape(1)
    place = jnp.arange(length // tile, dtype=jnp.int32)
    out_row = head_group * width

    def swap(array):
        return lax.all_to_all(array, everyone, 0, 0, tiled=True)

    starts = jnp.broadcast_to(
        doc_start.astype(f32)[:, None], (heads_n, blocks, block_rows)
    ).reshape(devices, block_rows)
    ff_gains = gains[:, :, 1].astype(f32).reshape(1, -1)
    small = swap(
        jnp.concatenate(
            [starts, jnp.broadcast_to(ff_gains, (devices, layer_count * weight_rows))], axis=1
        )
    )
    doc_row = small[:blocks, :block_rows].reshape(1, length)
    doc_col = lax.dynamic_slice_in_dim(
        doc_row.reshape(length, 1), query_part * query_rows, query_rows, 0
    )
    gain_ff = jnp.transpose(
        small[:, block_rows:].reshape(devices, layer_count, weight_rows), (1, 0, 2)
    ).reshape(layer_count, 1, model_width)
    table, near = prepare(bias_table, head_group * heads_dev, heads_dev)

    gain_attn = gains[:, :, 0].astype(f32)[:, :, None]
    own_in = attn_in.astype(f32)

    def fetch_in(layer_id):
        scaled = (own_in[layer_id] * gain_attn[layer_id]).astype(bf16)
        columns = jnp.transpose(
            scaled.reshape(weight_rows, 3, head_groups, width), (2, 0, 1, 3)
        ).reshape(head_groups, weight_rows, 3 * width)
        columns = jnp.repeat(columns, split, axis=0)
        columns = jnp.broadcast_to(columns[None], (heads_n, *columns.shape))
        return swap(columns.reshape(devices, weight_rows, 3 * width)).reshape(
            model_width, 3 * width
        )

    def fetch_ff(layer_id):
        pair = jnp.concatenate([ff_in[layer_id], ff_out[layer_id]], axis=1)
        pair = gather_rows(pair, ff_spare)
        return pair[:, :model_width], pair[:, model_width:]

    hidden, upstream = tokens[0].astype(f32), cotangent[0]
    weights_in = [fetch_in(layer_id) for layer_id in range(layer_count)]
    weights_out = lax.dynamic_slice_in_dim(
        lax.all_gather(attn_out, everyone, axis=1, tiled=True), out_row, width, 1
    )
    weights_ff = [fetch_ff(layer_id) for layer_id in range(layer_count)]

    records = []
    for layer_id in range(layer_count):
        w_in, w_out, (w_up, w_down) = (
            weights_in[layer_id], weights_out[layer_id], weights_ff[layer_id],
        )
        inverse = inverse_rms(hidden)
        units = gather_rows((hidden * inverse).astype(bf16), group)
        qkv = jnp.dot(units, w_in, preferred_element_type=f32).astype(bf16)
        attended, stats = attention(
            qkv, doc_row, doc_col, first, place, table, near, query_rows
        )
        mixed = jnp.dot(attended, w_out, preferred_element_type=f32)
        if split > 1:
            mixed = lax.dynamic_update_slice_in_dim(
                jnp.zeros((length, model_width), f32), mixed, query_part * query_rows, 0
            )
        middle = hidden + scatter_sum(mixed, group, blocks)
        inverse_ff = inverse_rms(middle)
        normed_ff = gather_rows((middle * inverse_ff * gain_ff[layer_id]).astype(bf16), ff_group)
        activated, slope = gelu_parts(contract(normed_ff, w_up, 1, 1))
        ff_result = jnp.dot(activated, w_down, preferred_element_type=f32)
        records.append(
            (hidden, inverse, units, qkv, attended, stats, middle, inverse_ff, normed_ff,
             activated, slope)
        )
        hidden = middle + scatter_sum(ff_result, ff_group, ff_members)
    output = hidden

    grads_ff, grads_in, grads_out, grads_gain_ff, grads_table = (
        [None] * layer_count for _ in range(5)
    )
    for layer_id in reversed(range(layer_count)):
        w_in, w_out, (w_up, w_down) = (
            weights_in[layer_id], weights_out[layer_id], weights_ff[layer_id],
        )
        (hidden, inverse, units, qkv, attended, stats, middle, inverse_ff, normed_ff,
         activated, slope) = records[layer_id]
        grad_low = gather_rows(upstream.astype(bf16), ff_group)
        grad_pre = (contract(grad_low, w_down, 1, 1) * slope).astype(bf16)
        grad_normed = scatter_sum(
            jnp.dot(grad_pre, w_up, preferred_element_type=f32), ff_group, ff_members
        )
        grad_pair = jnp.concatenate(
            [contract(grad_pre, normed_ff, 0, 0), contract(activated, grad_low, 0, 0)], axis=1
        ).astype(bf16)
        grads_ff[layer_id] = lax.psum_scatter(
            grad_pair, ff_spare, scatter_dimension=0, tiled=True
        ).astype(f32)
        grads_gain_ff[layer_id] = jnp.sum(grad_normed * middle * inverse_ff, axis=0)
        grad_middle = upstream + unit_norm_back(
            middle, inverse_ff, grad_normed * gain_ff[layer_id]
        )
        branch = gather_rows(grad_middle.astype(bf16), group)
        if split > 1:
            branch = lax.dynamic_slice_in_dim(branch, query_part * query_rows, query_rows, 0)
        grad_attended = contract(branch, w_out, 1, 1).astype(bf16)
        grad_qkv, grad_near, grad_far = attention_back(
            qkv, doc_row, doc_col, attended, grad_attended, stats, first, place, table, near, split
        )
        grads_table[layer_id] = (grad_near, grad_far[:, :, 0, 0])
        grad_units = scatter_sum(contract(grad_qkv, w_in, 1, 1), group, blocks)
        upstream = grad_middle + unit_norm_back(hidden, inverse, grad_units)
        grad_out = lax.dynamic_update_slice_in_dim(
            jnp.zeros((model_width, model_width), bf16),
            contract(attended, branch, 0, 0).astype(bf16),
            out_row,
            0,
        )
        grads_out[layer_id] = lax.psum_scatter(
            grad_out, everyone, scatter_dimension=0, tiled=True
        ).astype(f32)
        grads_in[layer_id] = contract(units, grad_qkv, 0, 0).astype(bf16)

    bucket_count = table.shape[0]
    grad_table = bucket_grads(
        sum(entry[0] for entry in grads_table), sum(entry[1] for entry in grads_table), bucket_count
    )
    grad_table = lax.dynamic_update_slice_in_dim(
        jnp.zeros((bucket_count, heads_all), f32), grad_table, head_group * heads_dev, 1
    )
    grad_table = jnp.transpose(
        grad_table.reshape(blocks, bucket_count // blocks, heads_n, heads_all // heads_n),
        (2, 0, 1, 3),
    ).reshape(devices, -1)
    grad_gain_ff = jnp.transpose(
        jnp.stack(grads_gain_ff).reshape(layer_count, devices, weight_rows), (1, 0, 2)
    ).reshape(devices, -1)
    ends = jnp.sum(swap(jnp.concatenate([grad_gain_ff, grad_table], axis=1)), axis=0)
    grad_gain_ff = ends[: layer_count * weight_rows].reshape(layer_count, weight_rows)
    grad_bias_table = ends[layer_count * weight_rows :].reshape(
        bucket_count // blocks, heads_all // heads_n
    )
    grads_attn_in, grads_gains = [], []
    for layer_id in range(layer_count):
        parts = swap(grads_in[layer_id].reshape(devices, weight_rows, 3 * width)).astype(f32)
        parts = jnp.sum(parts.reshape(heads_n, blocks, weight_rows, 3 * width), axis=0)
        parts = jnp.sum(parts.reshape(head_groups, split, weight_rows, 3, width), axis=1)
        unit_grad = jnp.transpose(parts, (1, 2, 0, 3)).reshape(weight_rows, 3 * model_width)
        grads_attn_in.append(unit_grad * gain_attn[layer_id])
        grads_gains.append(
            jnp.stack(
                [jnp.sum(unit_grad * own_in[layer_id], axis=1), grad_gain_ff[layer_id]], axis=1
            )
        )
    return (
        output[None],
        upstream[None],
        jnp.stack(grads_attn_in),
        jnp.stack(grads_out),
        jnp.stack([entry[:, :model_width] for entry in grads_ff]),
        jnp.stack([entry[:, model_width:] for entry in grads_ff]),
        jnp.stack(grads_gains),
        grad_bias_table,
    )


def local_plane(tokens, doc_start, bias_table, attn_in, attn_out, ff_in, ff_out, gains, cotangent):
    heads_n, z_n, core_n = (lax.axis_size(axis) for axis in everyone)
    devices = heads_n * z_n * core_n
    at_head, at_core = lax.axis_index("head"), lax.axis_index("core")
    group = ("head", "core")
    members = heads_n * core_n
    block_rows, model_width = tokens.shape[1:]
    layer_count, weight_rows = attn_in.shape[:2]
    length = block_rows * members
    heads_all = bias_table.shape[1]
    heads_dev = heads_all // members
    width = heads_dev * head_dim
    member = at_head * core_n + at_core
    turn = [
        ((h * z_n + z) * core_n + c, (z * z_n + h) * core_n + c)
        for h in range(heads_n)
        for z in range(z_n)
        for c in range(core_n)
    ]
    first = jnp.zeros((1,), jnp.int32)
    place = jnp.stack(
        [
            (at_head ^ bits) * core_n + (at_core ^ other)
            for other in range(core_n)
            for bits in range(heads_n)
        ]
    ).astype(jnp.int32)

    def relay(array):
        return lax.ppermute(array.astype(bf16), everyone, turn).astype(f32)

    def swap(array):
        return lax.all_to_all(array, everyone, 0, 0, tiled=True)

    gain_attn = gains[:, :, 0].astype(f32)[:, :, None]
    shares = call(
        functools.partial(share_in_kernel, layer_count, members, z_n, core_n),
        [((devices, weight_rows, 3 * width), bf16)] * layer_count,
        attn_in,
        gain_attn,
    )
    hidden = relay(tokens[0])
    weights_in = [swap(shares[0]).reshape(model_width, 3 * width)]

    starts = jnp.broadcast_to(
        doc_start.astype(f32)[None, :, None], (heads_n, z_n, core_n, block_rows)
    )
    ff_gains = gains[:, :, 1].astype(f32).reshape(1, -1)
    small = jnp.concatenate(
        [
            starts.reshape(devices, block_rows),
            jnp.broadcast_to(ff_gains, (devices, layer_count * weight_rows)),
        ],
        axis=1,
    )
    small = swap(small)
    doc_row = small[:members, :block_rows].reshape(2, 2, core_n, block_rows)
    for axis, bit in ((0, at_head // 2), (1, at_head % 2), (2, at_core)):
        doc_row = jnp.where(bit == 1, jnp.flip(doc_row, axis), doc_row)
    doc_row = jnp.transpose(doc_row, (2, 0, 1, 3)).reshape(1, length)
    doc_col = doc_row.reshape(length, 1)
    gain_ff = jnp.transpose(
        small[:, block_rows:].reshape(devices, layer_count, weight_rows), (1, 0, 2)
    ).reshape(layer_count, 1, model_width)
    table, near = prepare(bias_table, member * heads_dev, heads_dev)

    def fetch_ff(layer_id):
        pair = jnp.concatenate([ff_in[layer_id], ff_out[layer_id]], axis=1)
        pair = gather_rows(pair, "z")
        return pair[:, :model_width], pair[:, model_width:]

    weights_out, weights_ff = [], []
    for layer_id in range(layer_count):
        weights_out.append(gather_rows(attn_out[layer_id], everyone))
        weights_ff.append(fetch_ff(layer_id))

    def pieces_to_group(pieces):
        return lax.all_to_all(pieces, group, 0, 0, tiled=True)

    row_shape = (block_rows, model_width)
    records = []
    unit_rows = (hidden * inverse_rms(hidden)).astype(bf16)
    for layer_id in range(layer_count):
        w_in, w_out, (w_up, w_down) = (
            weights_in[layer_id], weights_out[layer_id], weights_ff[layer_id],
        )
        units = plane_gather(unit_rows)
        qkv = jnp.dot(units, w_in, preferred_element_type=f32).astype(bf16)
        if layer_id + 1 < layer_count:
            later = swap(after(shares[layer_id + 1], qkv))
            weights_in.append(later.reshape(model_width, 3 * width))
        attended, stats = attention(qkv, doc_row, doc_col, first, place, table, near, length)
        merged, middle, normed_rows = call(
            out_kernel,
            [(row_shape, bf16), (row_shape, f32), (row_shape, bf16)],
            pieces_to_group(attended.reshape(members, block_rows, width)),
            w_out,
            hidden,
            gain_ff[layer_id],
        )
        normed_ff = plane_gather(normed_rows)
        activated, slope = gelu_parts(contract(normed_ff, w_up, 1, 1))
        parts = plane_scatter(jnp.dot(activated, w_down, preferred_element_type=f32))
        records.append((hidden, units, qkv, attended, stats, merged, middle, normed_ff, activated, slope))
        hidden, unit_rows = call(
            close_kernel, [(row_shape, f32), (row_shape, bf16)], middle, *parts
        )
    output = relay(hidden)

    upstream = relay(after(cotangent[0], records[0][2]))
    low_rows = upstream.astype(bf16)
    grads_ff, grads_in, grads_out, grads_gain_ff, grads_table = (
        [None] * layer_count for _ in range(5)
    )
    for layer_id in reversed(range(layer_count)):
        w_in, w_out, (w_up, w_down) = (
            weights_in[layer_id], weights_out[layer_id], weights_ff[layer_id],
        )
        hidden, units, qkv, attended, stats, merged, middle, normed_ff, activated, slope = records[
            layer_id
        ]
        grad_low = plane_gather(low_rows)
        grad_pre = (contract(grad_low, w_down, 1, 1) * slope).astype(bf16)
        parts = plane_scatter(jnp.dot(grad_pre, w_up, preferred_element_type=f32))
        grad_pair = jnp.concatenate(
            [contract(grad_pre, normed_ff, 0, 0), contract(activated, grad_low, 0, 0)], axis=1
        ).astype(bf16)
        grads_ff[layer_id] = lax.psum_scatter(
            grad_pair, "z", scatter_dimension=0, tiled=True
        ).astype(f32)
        grad_middle, branch, pieces, grads_gain_ff[layer_id] = call(
            middle_back_kernel,
            [
                (row_shape, f32),
                (row_shape, bf16),
                ((members, block_rows, width), bf16),
                ((1, model_width), f32),
            ],
            upstream,
            *parts,
            middle,
            gain_ff[layer_id],
            w_out,
        )
        grad_attended = pieces_to_group(pieces).reshape(length, width)
        grads_out[layer_id] = lax.psum_scatter(
            contract(merged, branch, 0, 0).astype(bf16), everyone, scatter_dimension=0, tiled=True
        ).astype(f32)
        grad_qkv, grad_near, grad_far = attention_back(
            qkv, doc_row, doc_col, attended, grad_attended, stats, first, place, table, near, 1
        )
        grads_table[layer_id] = (grad_near, grad_far[:, :, 0, 0])
        parts = plane_scatter(contract(grad_qkv, w_in, 1, 1))
        upstream, low_rows = call(
            layer_back_kernel, [(row_shape, f32), (row_shape, bf16)], grad_middle, *parts, hidden
        )
        grad_in = contract(units, grad_qkv, 0, 0).astype(bf16)
        grads_in[layer_id] = swap(
            after(grad_in, parts).reshape(devices, weight_rows, 3 * width)
        )

    bucket_count = table.shape[0]
    grad_table = bucket_grads(
        sum(entry[0] for entry in grads_table), sum(entry[1] for entry in grads_table), bucket_count
    )
    grad_table = lax.dynamic_update_slice_in_dim(
        jnp.zeros((bucket_count, heads_all), f32), grad_table, member * heads_dev, 1
    )
    grad_table = jnp.transpose(
        grad_table.reshape(members, bucket_count // members, heads_n, heads_all // heads_n),
        (2, 0, 1, 3),
    ).reshape(devices, -1)
    grad_gain_ff = jnp.transpose(
        jnp.concatenate(grads_gain_ff).reshape(layer_count, devices, weight_rows), (1, 0, 2)
    ).reshape(devices, -1)
    ends = jnp.concatenate([grad_gain_ff, grad_table], axis=1)
    ends = jnp.sum(swap(after(ends, parts)), axis=0)
    grad_gain_ff = ends[: layer_count * weight_rows].reshape(layer_count, weight_rows)
    grad_bias_table = ends[layer_count * weight_rows :].reshape(
        bucket_count // members, heads_all // heads_n
    )
    grads_attn_in, grads_gains = [], []
    for layer_id in range(layer_count):
        parts = grads_in[layer_id].astype(f32).reshape(
            heads_n, z_n, core_n, weight_rows, 3, width
        )
        parts = jnp.sum(parts, axis=1).reshape(members, weight_rows, 3, width)
        unit_grad = jnp.transpose(parts, (1, 2, 0, 3)).reshape(weight_rows, 3 * model_width)
        grads_attn_in.append(unit_grad * gain_attn[layer_id])
        grads_gains.append(
            jnp.stack(
                [
                    jnp.sum(unit_grad * attn_in[layer_id].astype(f32), axis=1),
                    grad_gain_ff[layer_id],
                ],
                axis=1,
            )
        )
    return (
        output[None],
        relay(upstream)[None],
        jnp.stack(grads_attn_in),
        jnp.stack(grads_out),
        jnp.stack([entry[:, :model_width] for entry in grads_ff]),
        jnp.stack([entry[:, model_width:] for entry in grads_ff]),
        jnp.stack(grads_gains),
        grad_bias_table,
    )


def solution(mesh):
    sizes = dict(mesh.shape)
    cores = 2
    fine = Mesh(
        mesh.devices.reshape(sizes["head"], sizes["blk"] // cores, cores), everyone
    )
    blk = ("z", "core")
    in_specs = (
        P("head", blk, None),
        P(None, blk),
        P(),
        P(None, everyone, None),
        P(None, everyone, None),
        P(None, everyone, None),
        P(None, everyone, None),
        P(None, everyone, None),
        P("head", blk, None),
    )
    out_specs = (
        P("head", blk, None),
        P("head", blk, None),
        P(None, everyone, None),
        P(None, everyone, None),
        P(None, everyone, None),
        P(None, everyone, None),
        P(None, everyone, None),
        P(blk, "head"),
    )
    plane = sizes["head"] == 4 and sizes["blk"] == 8
    local = local_plane if plane else local_general
    return jax.shard_map(local, mesh=fine, in_specs=in_specs, out_specs=out_specs, check_vma=False)
```

```python
import functools

import jax
import jax.numpy as jnp
import numpy as np
from jax import lax
from jax.experimental import pallas as pl
from jax.experimental.pallas import tpu as pltpu
from jax.sharding import Mesh
from jax.sharding import PartitionSpec as P

bounds = (1, 2, 3, 4, 5, 6, 7, 8, 12, 16, 23, 32, 46, 64, 91)
epsilon = 1e-06
masked = -1e30
score_scale = 0.125
head_dim = 64
tile = 128
everyone = ("head", "z", "core")
bf16 = jnp.bfloat16
f32 = jnp.float32


def contract(lhs, rhs, lhs_dim, rhs_dim):
    return lax.dot_general(
        lhs, rhs, (((lhs_dim,), (rhs_dim,)), ((), ())), preferred_element_type=f32
    )


def near_buckets(shape):
    offsets = (
        lax.broadcasted_iota(jnp.int32, shape, 1) - tile - lax.broadcasted_iota(jnp.int32, shape, 0)
    )
    distance = jnp.abs(offsets)
    bucket = jnp.where(offsets > 0, 16, 0)
    for boundary in bounds:
        bucket = bucket + jnp.where(distance >= boundary, 1, 0)
    return bucket


def near_kernel(table, near):
    bucket = near_buckets(near.shape[1:])
    for head in range(near.shape[0]):
        values = jnp.zeros(near.shape[1:], f32)
        for bucket_id in range(table.shape[0]):
            values = jnp.where(bucket == bucket_id, table[bucket_id, head], values)
        near[head] = values


def bucket_kernel(layers, *refs):
    nears, fars, out = refs[:layers], refs[layers : 2 * layers], refs[-1]
    bucket = near_buckets(nears[0].shape[1:])
    rows = lax.broadcasted_iota(jnp.int32, out.shape, 0)
    lanes = lax.broadcasted_iota(jnp.int32, out.shape, 1)
    total = jnp.zeros(out.shape, f32)
    for head in range(nears[0].shape[0]):
        strip = sum(near[head] for near in nears)
        for bucket_id in range(out.shape[0]):
            value = jnp.sum(jnp.where(bucket == bucket_id, strip, 0.0), axis=0, keepdims=True)
            value = jnp.sum(value, axis=1, keepdims=True)
            if bucket_id in (15, 31):
                value = value + sum(far[head, bucket_id // 16, :1, :1] for far in fars)
            total = jnp.where((rows == bucket_id) & (lanes == head), value, total)
    out[...] = total


def fill_band(band, table, near, heads_dev, length):
    for head in range(heads_dev):
        band[head, :, : length - tile] = jnp.full((tile, length - tile), table[15, head], f32)
        band[head, :, length - tile : length + 2 * tile] = near[head]
        band[head, :, length + 2 * tile :] = jnp.full(
            (tile, length - 2 * tile), table[31, head], f32
        )


def band_starts(place, at, length):
    return [
        pl.multiple_of(length + (place[block] - place[at]) * tile, tile)
        for block in range(length // tile)
    ]


def attention_kernel(
    heads_dev, length, first, place, table, near, qkv, doc_row, doc_col, out, local, stats, band
):
    step = pl.program_id(0)
    width = heads_dev * head_dim

    @pl.when(step == 0)
    def _():
        fill_band(band, table, near, heads_dev, length)

    row = pl.multiple_of((first[0] + step) * tile, tile)
    out_row = pl.multiple_of((place[first[0] + step] - first[0]) * tile, tile)
    starts = band_starts(place, first[0] + step, length)
    same_doc = doc_col[...] == doc_row[...]
    queries = qkv[pl.ds(row, tile), :width] * bf16(score_scale)
    lanes = lax.broadcasted_iota(jnp.int32, (tile, tile), 1)
    collected = jnp.zeros((tile, tile), f32)
    for head in range(heads_dev):
        own = slice(head * head_dim, (head + 1) * head_dim)
        keys = qkv[:, width + own.start : width + own.stop]
        values = qkv[:, 2 * width + own.start : 2 * width + own.stop]
        scores = contract(queries[:, own], keys, 1, 1)
        scores = scores + jnp.concatenate(
            [band[head, :, pl.ds(start, tile)] for start in starts], axis=1
        )
        scores = jnp.where(same_doc, scores, masked)
        peak = jnp.max(scores, axis=1, keepdims=True)
        weights = jnp.exp(scores - peak)
        total = jnp.sum(weights, axis=1, keepdims=True)
        mixed = contract(weights.astype(bf16), values, 1, 0) / total
        out[pl.ds(out_row, tile), own] = mixed.astype(bf16)
        local[:, own] = mixed.astype(bf16)
        collected = jnp.where(lanes == head, peak + jnp.log(total), collected)
    stats[...] = collected


def attention_back_kernel(
    heads_dev, length, split, first, place, table, near, qkv, doc_row, doc_col, attended, grad_out, stats,
    grad_qkv, grad_near, grad_far, band, grad_band, grad_keys, grad_values,
):
    step = pl.program_id(0)
    width = heads_dev * head_dim

    @pl.when(step == 0)
    def _():
        fill_band(band, table, near, heads_dev, length)
        grad_band[...] = jnp.zeros_like(grad_band)
        grad_keys[...] = jnp.zeros_like(grad_keys)
        grad_values[...] = jnp.zeros_like(grad_values)
        if split > 1:
            grad_qkv[...] = jnp.zeros_like(grad_qkv)

    row = pl.multiple_of((first[0] + step) * tile, tile)
    out_row = pl.multiple_of((place[first[0] + step] - first[0]) * tile, tile)
    starts = band_starts(place, first[0] + step, length)
    same_doc = doc_col[...] == doc_row[...]
    at_step = pl.multiple_of(step * tile, tile)
    queries = qkv[pl.ds(row, tile), :width] * bf16(score_scale)
    for head in range(heads_dev):
        own = slice(head * head_dim, (head + 1) * head_dim)
        keys = qkv[:, width + own.start : width + own.stop]
        values = qkv[:, 2 * width + own.start : 2 * width + own.stop]
        upstream = grad_out[pl.ds(out_row, tile), own]
        scores = contract(queries[:, own], keys, 1, 1) + jnp.concatenate(
            [band[head, :, pl.ds(start, tile)] for start in starts], axis=1
        )
        scores = jnp.where(same_doc, scores, masked)
        weights = jnp.exp(scores - stats[:, head : head + 1])
        delta = jnp.sum(
            upstream.astype(f32) * attended[pl.ds(at_step, tile), own].astype(f32),
            axis=1,
            keepdims=True,
        )
        grad_scores = weights * (contract(upstream, values, 1, 1) - delta)
        for block, start in enumerate(starts):
            grad_band[head, :, pl.ds(start, tile)] += grad_scores[
                :, block * tile : (block + 1) * tile
            ]
        grad_low = grad_scores.astype(bf16)
        grad_values[:, own] += contract(weights.astype(bf16), upstream, 0, 0)
        grad_keys[:, own] += contract(grad_low, queries[:, own], 0, 0)
        grad_qkv[pl.ds(row, tile), own] = (
            contract(grad_low, keys, 1, 0) * score_scale
        ).astype(bf16)

    @pl.when(step == pl.num_programs(0) - 1)
    def _():
        grad_qkv[:, width : 2 * width] = grad_keys[...].astype(bf16)
        grad_qkv[:, 2 * width :] = grad_values[...].astype(bf16)
        for head in range(heads_dev):
            grad_near[head] = grad_band[head, :, length - tile : length + 2 * tile]
            grad_far[head, 0] = jnp.full(
                (8, tile), jnp.sum(grad_band[head, :, : length - tile]), f32
            )
            grad_far[head, 1] = jnp.full(
                (8, tile), jnp.sum(grad_band[head, :, length + 2 * tile :]), f32
            )


def whole(shape):
    return pl.BlockSpec(shape, lambda step: (0,) * len(shape))


def attention(qkv, doc_row, doc_col, first, place, table, near, rows):
    length = qkv.shape[0]
    heads_dev = table.shape[1]
    width = heads_dev * head_dim
    return pl.pallas_call(
        functools.partial(attention_kernel, heads_dev, length),
        grid=(rows // tile,),
        in_specs=[
            pl.BlockSpec(memory_space=pltpu.SMEM),
            pl.BlockSpec(memory_space=pltpu.SMEM),
            pl.BlockSpec(memory_space=pltpu.SMEM),
            whole(near.shape),
            whole(qkv.shape),
            whole(doc_row.shape),
            pl.BlockSpec((tile, 1), lambda step: (step, 0)),
        ],
        out_specs=[
            whole((rows, width)),
            pl.BlockSpec((tile, width), lambda step: (step, 0)),
            pl.BlockSpec((tile, tile), lambda step: (step, 0)),
        ],
        out_shape=[
            jax.ShapeDtypeStruct((rows, width), bf16),
            jax.ShapeDtypeStruct((rows, width), bf16),
            jax.ShapeDtypeStruct((rows, tile), f32),
        ],
        scratch_shapes=[pltpu.VMEM((heads_dev, tile, 2 * length), f32)],
        compiler_params=pltpu.CompilerParams(vmem_limit_bytes=40 * 2**20),
        cost_estimate=pl.CostEstimate(
            flops=4 * rows * length * width,
            bytes_accessed=4 * length * width * 2,
            transcendentals=rows * length * heads_dev,
        ),
    )(first, place, table, near, qkv, doc_row, doc_col)


def attention_back(
    qkv, doc_row, doc_col, attended, grad_out, stats, first, place, table, near, split
):
    length = qkv.shape[0]
    rows = grad_out.shape[0]
    heads_dev = table.shape[1]
    width = heads_dev * head_dim
    return pl.pallas_call(
        functools.partial(attention_back_kernel, heads_dev, length, split),
        grid=(rows // tile,),
        in_specs=[
            pl.BlockSpec(memory_space=pltpu.SMEM),
            pl.BlockSpec(memory_space=pltpu.SMEM),
            pl.BlockSpec(memory_space=pltpu.SMEM),
            whole(near.shape),
            whole(qkv.shape),
            whole(doc_row.shape),
            pl.BlockSpec((tile, 1), lambda step: (step, 0)),
            whole((rows, width)),
            whole((rows, width)),
            pl.BlockSpec((tile, tile), lambda step: (step, 0)),
        ],
        out_specs=[
            whole((length, 3 * width)),
            whole((heads_dev, tile, 3 * tile)),
            whole((heads_dev, 2, 8, tile)),
        ],
        out_shape=[
            jax.ShapeDtypeStruct((length, 3 * width), bf16),
            jax.ShapeDtypeStruct((heads_dev, tile, 3 * tile), f32),
            jax.ShapeDtypeStruct((heads_dev, 2, 8, tile), f32),
        ],
        scratch_shapes=[
            pltpu.VMEM((heads_dev, tile, 2 * length), f32),
            pltpu.VMEM((heads_dev, tile, 2 * length), f32),
            pltpu.VMEM((length, width), f32),
            pltpu.VMEM((length, width), f32),
        ],
        compiler_params=pltpu.CompilerParams(vmem_limit_bytes=48 * 2**20),
        cost_estimate=pl.CostEstimate(
            flops=10 * rows * length * width,
            bytes_accessed=8 * length * width * 2,
            transcendentals=rows * length * heads_dev,
        ),
    )(first, place, table, near, qkv, doc_row, doc_col, attended, grad_out, stats)


def call(kernel, shapes, *operands, smem=0):
    return pl.pallas_call(
        kernel,
        in_specs=[pl.BlockSpec(memory_space=pltpu.SMEM)] * smem
        + [pl.BlockSpec(memory_space=pltpu.VMEM)] * (len(operands) - smem),
        out_specs=[pl.BlockSpec(memory_space=pltpu.VMEM)] * len(shapes),
        out_shape=[jax.ShapeDtypeStruct(shape, kind) for shape, kind in shapes],
        compiler_params=pltpu.CompilerParams(vmem_limit_bytes=32 * 2**20),
    )(*operands)


def share_in_kernel(layers, members, copies, core_n, attn_in, gains, *outs):
    width = attn_in.shape[2] // (3 * members)
    for layer_id in range(layers):
        for member in range(members):
            block = jnp.concatenate(
                [
                    attn_in[layer_id, :, (part * members + member) * width :][:, :width]
                    for part in range(3)
                ],
                axis=1,
            )
            block = (block.astype(f32) * gains[layer_id]).astype(bf16)
            for copy in range(copies):
                target = (member // core_n * copies + copy) * core_n + member % core_n
                outs[layer_id][target] = block


def close_kernel(kept, own, x_part, y_part, xy_part, hidden, units):
    total = (own[...] + x_part[...].astype(f32)) + (
        y_part[...].astype(f32) + xy_part[...].astype(f32)
    )
    total = kept[...] + total
    hidden[...] = total
    units[...] = (total * inverse_rms(total)).astype(bf16)


def out_kernel(pieces, weight, hidden, gain, middle, normed):
    merged = jnp.concatenate([pieces[member] for member in range(pieces.shape[0])], axis=1)
    total = hidden[...] + contract(merged, weight[...], 1, 0)
    middle[...] = total
    normed[...] = (total * inverse_rms(total) * gain[...]).astype(bf16)


def middle_back_kernel(
    upstream, own, x_part, y_part, xy_part, middle, gain, weight, grad_middle, branch, pieces, grad_gain
):
    grad_normed = (own[...] + x_part[...].astype(f32)) + (
        y_part[...].astype(f32) + xy_part[...].astype(f32)
    )
    inverse = inverse_rms(middle[...])
    grad_gain[...] = jnp.sum(grad_normed * middle[...] * inverse, axis=0, keepdims=True)
    total = upstream[...] + unit_norm_back(middle[...], inverse, grad_normed * gain[...])
    grad_middle[...] = total
    branch[...] = total.astype(bf16)
    spread = contract(branch[...], weight[...], 1, 1).astype(bf16)
    for member in range(pieces.shape[0]):
        pieces[member] = spread[:, member * pieces.shape[2] : (member + 1) * pieces.shape[2]]


def layer_back_kernel(grad_middle, own, x_part, y_part, xy_part, hidden, upstream, low):
    grad_units = (own[...] + x_part[...].astype(f32)) + (
        y_part[...].astype(f32) + xy_part[...].astype(f32)
    )
    total = grad_middle[...] + unit_norm_back(hidden[...], inverse_rms(hidden[...]), grad_units)
    upstream[...] = total
    low[...] = total.astype(bf16)


def inverse_rms(hidden):
    return lax.rsqrt(jnp.mean(hidden * hidden, axis=-1, keepdims=True) + epsilon)


def prepare(bias_table, first_head, heads_dev):
    table = lax.dynamic_slice_in_dim(bias_table, first_head, heads_dev, 1)
    (near,) = call(near_kernel, [((heads_dev, tile, 3 * tile), f32)], table, smem=1)
    return table, near


def bucket_grads(grads, bucket_count):
    heads_dev = grads[0][0].shape[0]
    (total,) = call(
        functools.partial(bucket_kernel, len(grads)),
        [((bucket_count, tile), f32)],
        *(entry[0] for entry in grads),
        *(entry[1] for entry in grads),
    )
    return total[:, :heads_dev]


def gelu_parts(pre_act):
    cumulative = 0.5 * (1.0 + lax.erf(pre_act * np.float32(0.5**0.5)))
    slope = cumulative + pre_act * jnp.exp(-0.5 * pre_act * pre_act) * np.float32(
        (2 * np.pi) ** -0.5
    )
    return (pre_act * cumulative).astype(bf16), slope


def unit_norm_back(hidden, inverse, grad_unit):
    unit = hidden * inverse
    return inverse * (grad_unit - unit * jnp.mean(grad_unit * unit, axis=-1, keepdims=True))


def gather_rows(block, axes):
    return lax.all_gather(block, axes, axis=0, tiled=True)


def toggle(array, axis, bits):
    return lax.ppermute(array, axis, [(i, i ^ bits) for i in range(lax.axis_size(axis))])


def plane_gather(block):
    near_core = jnp.concatenate([block] + [toggle(block, "head", bits) for bits in (1, 2, 3)])
    return jnp.concatenate([near_core, toggle(near_core, "core", 1)])


def plane_scatter(partial):
    half = partial.shape[0] // 2
    arrived = toggle(partial[half:].astype(bf16), "core", 1)
    total = (partial[:half] + arrived.astype(f32)).reshape(4, -1, partial.shape[1])
    return [total[0]] + [toggle(total[bits].astype(bf16), "head", bits) for bits in (1, 2, 3)]


def after(array, other):
    return lax.optimization_barrier((array, other))[0]


def scatter_sum(partial, axes, members):
    blocks = partial.astype(bf16).reshape(members, -1, partial.shape[1])
    return jnp.sum(lax.all_to_all(blocks, axes, 0, 0, tiled=True).astype(f32), axis=0)


def local_general(tokens, doc_start, bias_table, attn_in, attn_out, ff_in, ff_out, gains, cotangent):
    heads_n, z_n, core_n = (lax.axis_size(axis) for axis in everyone)
    devices = heads_n * z_n * core_n
    group, spare = ("z", "core"), "head"
    ff_group, ff_spare, ff_members = ("head", "core"), "z", heads_n * core_n
    blocks = z_n * core_n
    block_rows, model_width = tokens.shape[1:]
    layer_count, weight_rows = attn_in.shape[:2]
    length = block_rows * blocks
    heads_all = bias_table.shape[1]
    member = lax.axis_index("z") * core_n + lax.axis_index("core")
    heads_dev = max(1, heads_all // blocks)
    head_groups = heads_all // heads_dev
    split = blocks // head_groups
    head_group, query_part = member // split, member % split
    query_rows = length // split
    width = heads_dev * head_dim
    first = (query_part * (query_rows // tile)).astype(jnp.int32).reshape(1)
    place = jnp.arange(length // tile, dtype=jnp.int32)
    out_row = head_group * width

    def swap(array):
        return lax.all_to_all(array, everyone, 0, 0, tiled=True)

    starts = jnp.broadcast_to(
        doc_start.astype(f32)[:, None], (heads_n, blocks, block_rows)
    ).reshape(devices, block_rows)
    ff_gains = gains[:, :, 1].astype(f32).reshape(1, -1)
    small = swap(
        jnp.concatenate(
            [starts, jnp.broadcast_to(ff_gains, (devices, layer_count * weight_rows))], axis=1
        )
    )
    doc_row = small[:blocks, :block_rows].reshape(1, length)
    doc_col = lax.dynamic_slice_in_dim(
        doc_row.reshape(length, 1), query_part * query_rows, query_rows, 0
    )
    gain_ff = jnp.transpose(
        small[:, block_rows:].reshape(devices, layer_count, weight_rows), (1, 0, 2)
    ).reshape(layer_count, 1, model_width)
    table, near = prepare(bias_table, head_group * heads_dev, heads_dev)

    gain_attn = gains[:, :, 0].astype(f32)[:, :, None]
    own_in = attn_in.astype(f32)

    def fetch_in(layer_id):
        scaled = (own_in[layer_id] * gain_attn[layer_id]).astype(bf16)
        columns = jnp.transpose(
            scaled.reshape(weight_rows, 3, head_groups, width), (2, 0, 1, 3)
        ).reshape(head_groups, weight_rows, 3 * width)
        columns = jnp.repeat(columns, split, axis=0)
        columns = jnp.broadcast_to(columns[None], (heads_n, *columns.shape))
        return swap(columns.reshape(devices, weight_rows, 3 * width)).reshape(
            model_width, 3 * width
        )

    def fetch_ff(layer_id):
        pair = jnp.concatenate([ff_in[layer_id], ff_out[layer_id]], axis=1)
        pair = gather_rows(pair, ff_spare)
        return pair[:, :model_width], pair[:, model_width:]

    hidden, upstream = tokens[0].astype(f32), cotangent[0]
    weights_in = [fetch_in(layer_id) for layer_id in range(layer_count)]
    weights_out = lax.dynamic_slice_in_dim(
        lax.all_gather(attn_out, everyone, axis=1, tiled=True), out_row, width, 1
    )
    weights_ff = [fetch_ff(layer_id) for layer_id in range(layer_count)]

    records = []
    for layer_id in range(layer_count):
        w_in, w_out, (w_up, w_down) = (
            weights_in[layer_id], weights_out[layer_id], weights_ff[layer_id],
        )
        inverse = inverse_rms(hidden)
        units = gather_rows((hidden * inverse).astype(bf16), group)
        qkv = jnp.dot(units, w_in, preferred_element_type=f32).astype(bf16)
        attended, _, stats = attention(
            qkv, doc_row, doc_col, first, place, table, near, query_rows
        )
        mixed = jnp.dot(attended, w_out, preferred_element_type=f32)
        if split > 1:
            mixed = lax.dynamic_update_slice_in_dim(
                jnp.zeros((length, model_width), f32), mixed, query_part * query_rows, 0
            )
        middle = hidden + scatter_sum(mixed, group, blocks)
        inverse_ff = inverse_rms(middle)
        normed_ff = gather_rows((middle * inverse_ff * gain_ff[layer_id]).astype(bf16), ff_group)
        activated, slope = gelu_parts(contract(normed_ff, w_up, 1, 1))
        ff_result = jnp.dot(activated, w_down, preferred_element_type=f32)
        records.append(
            (hidden, inverse, units, qkv, attended, stats, middle, inverse_ff, normed_ff,
             activated, slope)
        )
        hidden = middle + scatter_sum(ff_result, ff_group, ff_members)
    output = hidden

    grads_ff, grads_in, grads_out, grads_gain_ff, grads_table = (
        [None] * layer_count for _ in range(5)
    )
    for layer_id in reversed(range(layer_count)):
        w_in, w_out, (w_up, w_down) = (
            weights_in[layer_id], weights_out[layer_id], weights_ff[layer_id],
        )
        (hidden, inverse, units, qkv, attended, stats, middle, inverse_ff, normed_ff,
         activated, slope) = records[layer_id]
        grad_low = gather_rows(upstream.astype(bf16), ff_group)
        grad_pre = (contract(grad_low, w_down, 1, 1) * slope).astype(bf16)
        grad_normed = scatter_sum(
            jnp.dot(grad_pre, w_up, preferred_element_type=f32), ff_group, ff_members
        )
        grad_pair = jnp.concatenate(
            [contract(grad_pre, normed_ff, 0, 0), contract(activated, grad_low, 0, 0)], axis=1
        ).astype(bf16)
        grads_ff[layer_id] = lax.psum_scatter(
            grad_pair, ff_spare, scatter_dimension=0, tiled=True
        ).astype(f32)
        grads_gain_ff[layer_id] = jnp.sum(grad_normed * middle * inverse_ff, axis=0)
        grad_middle = upstream + unit_norm_back(
            middle, inverse_ff, grad_normed * gain_ff[layer_id]
        )
        branch = gather_rows(grad_middle.astype(bf16), group)
        if split > 1:
            branch = lax.dynamic_slice_in_dim(branch, query_part * query_rows, query_rows, 0)
        grad_attended = contract(branch, w_out, 1, 1).astype(bf16)
        grad_qkv, grad_near, grad_far = attention_back(
            qkv, doc_row, doc_col, attended, grad_attended, stats, first, place, table, near, split
        )
        grads_table[layer_id] = (grad_near, grad_far)
        grad_units = scatter_sum(contract(grad_qkv, w_in, 1, 1), group, blocks)
        upstream = grad_middle + unit_norm_back(hidden, inverse, grad_units)
        grad_out = lax.dynamic_update_slice_in_dim(
            jnp.zeros((model_width, model_width), bf16),
            contract(attended, branch, 0, 0).astype(bf16),
            out_row,
            0,
        )
        grads_out[layer_id] = lax.psum_scatter(
            grad_out, everyone, scatter_dimension=0, tiled=True
        ).astype(f32)
        grads_in[layer_id] = contract(units, grad_qkv, 0, 0).astype(bf16)

    bucket_count = table.shape[0]
    grad_table = bucket_grads(grads_table, bucket_count)
    grad_table = lax.dynamic_update_slice_in_dim(
        jnp.zeros((bucket_count, heads_all), f32), grad_table, head_group * heads_dev, 1
    )
    grad_table = jnp.transpose(
        grad_table.reshape(blocks, bucket_count // blocks, heads_n, heads_all // heads_n),
        (2, 0, 1, 3),
    ).reshape(devices, -1)
    grad_gain_ff = jnp.transpose(
        jnp.stack(grads_gain_ff).reshape(layer_count, devices, weight_rows), (1, 0, 2)
    ).reshape(devices, -1)
    ends = jnp.sum(swap(jnp.concatenate([grad_gain_ff, grad_table], axis=1)), axis=0)
    grad_gain_ff = ends[: layer_count * weight_rows].reshape(layer_count, weight_rows)
    grad_bias_table = ends[layer_count * weight_rows :].reshape(
        bucket_count // blocks, heads_all // heads_n
    )
    grads_attn_in, grads_gains = [], []
    for layer_id in range(layer_count):
        parts = swap(grads_in[layer_id].reshape(devices, weight_rows, 3 * width)).astype(f32)
        parts = jnp.sum(parts.reshape(heads_n, blocks, weight_rows, 3 * width), axis=0)
        parts = jnp.sum(parts.reshape(head_groups, split, weight_rows, 3, width), axis=1)
        unit_grad = jnp.transpose(parts, (1, 2, 0, 3)).reshape(weight_rows, 3 * model_width)
        grads_attn_in.append(unit_grad * gain_attn[layer_id])
        grads_gains.append(
            jnp.stack(
                [jnp.sum(unit_grad * own_in[layer_id], axis=1), grad_gain_ff[layer_id]], axis=1
            )
        )
    return (
        output[None],
        upstream[None],
        jnp.stack(grads_attn_in),
        jnp.stack(grads_out),
        jnp.stack([entry[:, :model_width] for entry in grads_ff]),
        jnp.stack([entry[:, model_width:] for entry in grads_ff]),
        jnp.stack(grads_gains),
        grad_bias_table,
    )


def local_plane(tokens, doc_start, bias_table, attn_in, attn_out, ff_in, ff_out, gains, cotangent):
    heads_n, z_n, core_n = (lax.axis_size(axis) for axis in everyone)
    devices = heads_n * z_n * core_n
    at_head, at_core = lax.axis_index("head"), lax.axis_index("core")
    group = ("head", "core")
    members = heads_n * core_n
    block_rows, model_width = tokens.shape[1:]
    layer_count, weight_rows = attn_in.shape[:2]
    length = block_rows * members
    heads_all = bias_table.shape[1]
    heads_dev = heads_all // members
    width = heads_dev * head_dim
    member = at_head * core_n + at_core
    turn = [
        ((h * z_n + z) * core_n + c, (z * z_n + h) * core_n + c)
        for h in range(heads_n)
        for z in range(z_n)
        for c in range(core_n)
    ]
    first = jnp.zeros((1,), jnp.int32)
    place = jnp.stack(
        [
            (at_head ^ bits) * core_n + (at_core ^ other)
            for other in range(core_n)
            for bits in range(heads_n)
        ]
    ).astype(jnp.int32)

    def relay(array):
        return lax.ppermute(array.astype(bf16), everyone, turn).astype(f32)

    def swap(array):
        return lax.all_to_all(array, everyone, 0, 0, tiled=True)

    gain_attn = gains[:, :, 0].astype(f32)[:, :, None]
    shares = call(
        functools.partial(share_in_kernel, layer_count, members, z_n, core_n),
        [((devices, weight_rows, 3 * width), bf16)] * layer_count,
        attn_in,
        gain_attn,
    )
    hidden = relay(after(tokens[0], shares[0]))
    weights_in = [swap(shares[0]).reshape(model_width, 3 * width)]

    starts = jnp.broadcast_to(
        doc_start.astype(f32)[None, :, None], (heads_n, z_n, core_n, block_rows)
    )
    ff_gains = gains[:, :, 1].astype(f32).reshape(1, -1)
    small = jnp.concatenate(
        [
            starts.reshape(devices, block_rows),
            jnp.broadcast_to(ff_gains, (devices, layer_count * weight_rows)),
        ],
        axis=1,
    )
    small = swap(after(small, hidden))
    doc_row = small[:members, :block_rows].reshape(2, 2, core_n, block_rows)
    for axis, bit in ((0, at_head // 2), (1, at_head % 2), (2, at_core)):
        doc_row = jnp.where(bit == 1, jnp.flip(doc_row, axis), doc_row)
    doc_row = jnp.transpose(doc_row, (2, 0, 1, 3)).reshape(1, length)
    doc_col = doc_row.reshape(length, 1)
    gain_ff = jnp.transpose(
        small[:, block_rows:].reshape(devices, layer_count, weight_rows), (1, 0, 2)
    ).reshape(layer_count, 1, model_width)
    table, near = prepare(bias_table, member * heads_dev, heads_dev)

    def fetch_ff(layer_id):
        pair = jnp.concatenate([ff_in[layer_id], ff_out[layer_id]], axis=1)
        if layer_id == 0:
            pair = after(pair, weights_in[0])
            pair = jnp.concatenate([pair] + [toggle(pair, "z", bits) for bits in range(1, z_n)])
        else:
            pair = gather_rows(pair, "z")
        return pair[:, :model_width], pair[:, model_width:]

    gathered_out = lax.all_gather(attn_out, everyone, axis=1, tiled=True)
    weights_out, weights_ff = [], []
    for layer_id in range(layer_count):
        weights_out.append(gathered_out[layer_id])
        weights_ff.append(fetch_ff(layer_id))

    def pieces_to_group(pieces):
        return lax.all_to_all(pieces, group, 0, 0, tiled=True)

    row_shape = (block_rows, model_width)
    records = []
    unit_rows = after((hidden * inverse_rms(hidden)).astype(bf16), weights_in[0])
    for layer_id in range(layer_count):
        w_in, w_out, (w_up, w_down) = (
            weights_in[layer_id], weights_out[layer_id], weights_ff[layer_id],
        )
        units = plane_gather(unit_rows)
        qkv = jnp.dot(units, w_in, preferred_element_type=f32).astype(bf16)
        if layer_id == 0:
            upstream = lax.ppermute(after(cotangent[0].astype(bf16), qkv), everyone, turn)
        if layer_id + 1 == layer_count:
            grad_low = plane_gather(after(upstream, qkv))
        if layer_id + 1 < layer_count:
            later = swap(after(shares[layer_id + 1], qkv))
            weights_in.append(later.reshape(model_width, 3 * width))
        sent, attended, stats = attention(qkv, doc_row, doc_col, first, place, table, near, length)
        middle, normed_rows = call(
            out_kernel,
            [(row_shape, f32), (row_shape, bf16)],
            pieces_to_group(sent.reshape(members, block_rows, width)),
            w_out,
            hidden,
            gain_ff[layer_id],
        )
        normed_ff = plane_gather(normed_rows)
        activated, slope = gelu_parts(contract(normed_ff, w_up, 1, 1))
        parts = plane_scatter(jnp.dot(activated, w_down, preferred_element_type=f32))
        records.append((hidden, units, qkv, attended, stats, middle, normed_ff, activated, slope))
        hidden, unit_rows = call(
            close_kernel, [(row_shape, f32), (row_shape, bf16)], middle, *parts
        )
    output = lax.ppermute(hidden.astype(bf16), everyone, turn)
    upstream = after(upstream, hidden).astype(f32)
    grads_ff, grads_in, grads_out, grads_gain_ff, grads_table = (
        [None] * layer_count for _ in range(5)
    )
    for layer_id in reversed(range(layer_count)):
        w_in, w_out, (w_up, w_down) = (
            weights_in[layer_id], weights_out[layer_id], weights_ff[layer_id],
        )
        hidden, units, qkv, attended, stats, middle, normed_ff, activated, slope = records[
            layer_id
        ]
        if layer_id + 1 < layer_count:
            grad_low = plane_gather(low_rows)
        grad_pre = (contract(grad_low, w_down, 1, 1) * slope).astype(bf16)
        parts = plane_scatter(jnp.dot(grad_pre, w_up, preferred_element_type=f32))
        grad_pair = jnp.concatenate(
            [contract(grad_pre, normed_ff, 0, 0), contract(activated, grad_low, 0, 0)], axis=1
        ).astype(bf16)
        if layer_id == 0:
            shares = grad_pair.reshape(z_n, -1, 2 * model_width)
            shares = [shares[0]] + [toggle(shares[bits], "z", bits) for bits in range(1, z_n)]
            grads_ff[layer_id] = sum(share.astype(f32) for share in shares)
        else:
            grads_ff[layer_id] = lax.psum_scatter(
                grad_pair, "z", scatter_dimension=0, tiled=True
            ).astype(f32)
        grad_middle, branch, pieces, grads_gain_ff[layer_id] = call(
            middle_back_kernel,
            [
                (row_shape, f32),
                (row_shape, bf16),
                ((members, block_rows, width), bf16),
                ((1, model_width), f32),
            ],
            upstream,
            *parts,
            middle,
            gain_ff[layer_id],
            w_out,
        )
        grad_attended = pieces_to_group(pieces).reshape(length, width)
        branch = plane_gather(after(branch, grad_attended))
        grad_qkv, grad_near, grad_far = attention_back(
            qkv, doc_row, doc_col, attended, grad_attended, stats, first, place, table, near, 1
        )
        grads_table[layer_id] = (grad_near, grad_far)
        parts = plane_scatter(contract(grad_qkv, w_in, 1, 1))
        upstream, low_rows = call(
            layer_back_kernel, [(row_shape, f32), (row_shape, bf16)], grad_middle, *parts, hidden
        )
        grad_out = contract(attended, branch, 0, 0).astype(bf16)
        grad_out = jnp.where(
            jnp.arange(core_n)[:, None, None] == at_core, grad_out[None], bf16(0)
        ).reshape(core_n * width, model_width)
        grads_out[layer_id] = lax.psum_scatter(
            grad_out, ("z", "core"), scatter_dimension=0, tiled=True
        ).astype(f32)
        grad_in = contract(units, grad_qkv, 0, 0).astype(bf16)
        grads_in[layer_id] = swap(
            after(grad_in, upstream).reshape(devices, weight_rows, 3 * width)
        )
        if layer_id + 1 == layer_count:
            output = after(output, grad_qkv).astype(f32)

    bucket_count = table.shape[0]
    grad_table = bucket_grads(grads_table, bucket_count)
    grad_table = lax.dynamic_update_slice_in_dim(
        jnp.zeros((bucket_count, heads_all), f32), grad_table, member * heads_dev, 1
    )
    grad_table = jnp.transpose(
        grad_table.reshape(members, bucket_count // members, heads_n, heads_all // heads_n),
        (2, 0, 1, 3),
    ).reshape(devices, -1)
    grad_gain_ff = jnp.transpose(
        jnp.concatenate(grads_gain_ff).reshape(layer_count, devices, weight_rows), (1, 0, 2)
    ).reshape(devices, -1)
    ends = jnp.concatenate([grad_gain_ff, grad_table], axis=1)
    ends = jnp.sum(swap(ends), axis=0)
    grad_gain_ff = ends[: layer_count * weight_rows].reshape(layer_count, weight_rows)
    grad_bias_table = ends[layer_count * weight_rows :].reshape(
        bucket_count // members, heads_all // heads_n
    )
    grads_attn_in, grads_gains = [], []
    for layer_id in range(layer_count):
        parts = grads_in[layer_id].astype(f32).reshape(
            heads_n, z_n, core_n, weight_rows, 3, width
        )
        parts = jnp.sum(parts, axis=1).reshape(members, weight_rows, 3, width)
        unit_grad = jnp.transpose(parts, (1, 2, 0, 3)).reshape(weight_rows, 3 * model_width)
        grads_attn_in.append(unit_grad * gain_attn[layer_id])
        grads_gains.append(
            jnp.stack(
                [
                    jnp.sum(unit_grad * attn_in[layer_id].astype(f32), axis=1),
                    grad_gain_ff[layer_id],
                ],
                axis=1,
            )
        )
    return (
        output[None],
        relay(upstream)[None],
        jnp.stack(grads_attn_in),
        jnp.stack(grads_out),
        jnp.stack([entry[:, :model_width] for entry in grads_ff]),
        jnp.stack([entry[:, model_width:] for entry in grads_ff]),
        jnp.stack(grads_gains),
        grad_bias_table,
    )


def solution(mesh):
    sizes = dict(mesh.shape)
    cores = 2
    fine = Mesh(
        mesh.devices.reshape(sizes["head"], sizes["blk"] // cores, cores), everyone
    )
    blk = ("z", "core")
    in_specs = (
        P("head", blk, None),
        P(None, blk),
        P(),
        P(None, everyone, None),
        P(None, everyone, None),
        P(None, everyone, None),
        P(None, everyone, None),
        P(None, everyone, None),
        P("head", blk, None),
    )
    out_specs = (
        P("head", blk, None),
        P("head", blk, None),
        P(None, everyone, None),
        P(None, everyone, None),
        P(None, everyone, None),
        P(None, everyone, None),
        P(None, everyone, None),
        P(blk, "head"),
    )
    plane = sizes["head"] == 4 and sizes["blk"] == 8
    local = local_plane if plane else local_general
    return jax.shard_map(local, mesh=fine, in_specs=in_specs, out_specs=out_specs, check_vma=False)
```

```python
import functools

import jax
import jax.numpy as jnp
import numpy as np
from jax import lax
from jax.experimental import pallas as pl
from jax.experimental.pallas import tpu as pltpu
from jax.sharding import Mesh
from jax.sharding import PartitionSpec as P

bounds = (1, 2, 3, 4, 5, 6, 7, 8, 12, 16, 23, 32, 46, 64, 91)
epsilon = 1e-06
masked = -1e30
score_scale = 0.125
head_dim = 64
tile = 128
everyone = ("head", "z", "core")
bf16 = jnp.bfloat16
f32 = jnp.float32


def contract(lhs, rhs, lhs_dim, rhs_dim):
    return lax.dot_general(
        lhs, rhs, (((lhs_dim,), (rhs_dim,)), ((), ())), preferred_element_type=f32
    )


def near_buckets(shape):
    offsets = (
        lax.broadcasted_iota(jnp.int32, shape, 1) - tile - lax.broadcasted_iota(jnp.int32, shape, 0)
    )
    distance = jnp.abs(offsets)
    bucket = jnp.where(offsets > 0, 16, 0)
    for boundary in bounds:
        bucket = bucket + jnp.where(distance >= boundary, 1, 0)
    return bucket


def near_kernel(table, near):
    bucket = near_buckets(near.shape[1:])
    for head in range(near.shape[0]):
        values = jnp.zeros(near.shape[1:], f32)
        for bucket_id in range(table.shape[0]):
            values = jnp.where(bucket == bucket_id, table[bucket_id, head], values)
        near[head] = values


def bucket_kernel(layers, *refs):
    nears, fars, out = refs[:layers], refs[layers : 2 * layers], refs[-1]
    bucket = near_buckets(nears[0].shape[1:])
    rows = lax.broadcasted_iota(jnp.int32, out.shape, 0)
    lanes = lax.broadcasted_iota(jnp.int32, out.shape, 1)
    total = jnp.zeros(out.shape, f32)
    for head in range(nears[0].shape[0]):
        strip = sum(near[head] for near in nears)
        for bucket_id in range(out.shape[0]):
            value = jnp.sum(jnp.where(bucket == bucket_id, strip, 0.0), axis=0, keepdims=True)
            value = jnp.sum(value, axis=1, keepdims=True)
            if bucket_id in (15, 31):
                value = value + sum(far[head, bucket_id // 16, :1, :1] for far in fars)
            total = jnp.where((rows == bucket_id) & (lanes == head), value, total)
    out[...] = total


def fill_band(band, table, near, heads_dev, length):
    for head in range(heads_dev):
        band[head, :, : length - tile] = jnp.full((tile, length - tile), table[15, head], f32)
        band[head, :, length - tile : length + 2 * tile] = near[head]
        band[head, :, length + 2 * tile :] = jnp.full(
            (tile, length - 2 * tile), table[31, head], f32
        )


def band_starts(place, at, length):
    return [
        pl.multiple_of(length + (place[block] - place[at]) * tile, tile)
        for block in range(length // tile)
    ]


def attention_kernel(
    heads_dev, length, first, place, table, near, qkv, doc_row, doc_col, out, local, stats, band
):
    step = pl.program_id(0)
    width = heads_dev * head_dim

    @pl.when(step == 0)
    def _():
        fill_band(band, table, near, heads_dev, length)

    row = pl.multiple_of((first[0] + step) * tile, tile)
    out_row = pl.multiple_of((place[first[0] + step] - first[0]) * tile, tile)
    starts = band_starts(place, first[0] + step, length)
    same_doc = doc_col[...] == doc_row[...]
    queries = qkv[pl.ds(row, tile), :width] * bf16(score_scale)
    lanes = lax.broadcasted_iota(jnp.int32, (tile, tile), 1)
    collected = jnp.zeros((tile, tile), f32)
    for head in range(heads_dev):
        own = slice(head * head_dim, (head + 1) * head_dim)
        keys = qkv[:, width + own.start : width + own.stop]
        values = qkv[:, 2 * width + own.start : 2 * width + own.stop]
        scores = contract(queries[:, own], keys, 1, 1)
        scores = scores + jnp.concatenate(
            [band[head, :, pl.ds(start, tile)] for start in starts], axis=1
        )
        scores = jnp.where(same_doc, scores, masked)
        peak = jnp.max(scores, axis=1, keepdims=True)
        weights = jnp.exp(scores - peak)
        total = jnp.sum(weights, axis=1, keepdims=True)
        mixed = contract(weights.astype(bf16), values, 1, 0) / total
        out[pl.ds(out_row, tile), own] = mixed.astype(bf16)
        local[:, own] = mixed.astype(bf16)
        collected = jnp.where(lanes == head, peak + jnp.log(total), collected)
    stats[...] = collected


def attention_back_kernel(
    heads_dev, length, split, first, place, table, near, qkv, doc_row, doc_col, attended, grad_out, stats,
    grad_qkv, grad_near, grad_far, band, grad_band, grad_keys, grad_values,
):
    step = pl.program_id(0)
    width = heads_dev * head_dim

    @pl.when(step == 0)
    def _():
        fill_band(band, table, near, heads_dev, length)
        grad_band[...] = jnp.zeros_like(grad_band)
        grad_keys[...] = jnp.zeros_like(grad_keys)
        grad_values[...] = jnp.zeros_like(grad_values)
        if split > 1:
            grad_qkv[...] = jnp.zeros_like(grad_qkv)

    row = pl.multiple_of((first[0] + step) * tile, tile)
    out_row = pl.multiple_of((place[first[0] + step] - first[0]) * tile, tile)
    starts = band_starts(place, first[0] + step, length)
    same_doc = doc_col[...] == doc_row[...]
    at_step = pl.multiple_of(step * tile, tile)
    queries = qkv[pl.ds(row, tile), :width] * bf16(score_scale)
    for head in range(heads_dev):
        own = slice(head * head_dim, (head + 1) * head_dim)
        keys = qkv[:, width + own.start : width + own.stop]
        values = qkv[:, 2 * width + own.start : 2 * width + own.stop]
        upstream = grad_out[pl.ds(out_row, tile), own]
        scores = contract(queries[:, own], keys, 1, 1) + jnp.concatenate(
            [band[head, :, pl.ds(start, tile)] for start in starts], axis=1
        )
        scores = jnp.where(same_doc, scores, masked)
        weights = jnp.exp(scores - stats[:, head : head + 1])
        delta = jnp.sum(
            upstream.astype(f32) * attended[pl.ds(at_step, tile), own].astype(f32),
            axis=1,
            keepdims=True,
        )
        grad_scores = weights * (contract(upstream, values, 1, 1) - delta)
        for block, start in enumerate(starts):
            grad_band[head, :, pl.ds(start, tile)] += grad_scores[
                :, block * tile : (block + 1) * tile
            ]
        grad_low = grad_scores.astype(bf16)
        grad_values[:, own] += contract(weights.astype(bf16), upstream, 0, 0)
        grad_keys[:, own] += contract(grad_low, queries[:, own], 0, 0)
        grad_qkv[pl.ds(row, tile), own] = (
            contract(grad_low, keys, 1, 0) * score_scale
        ).astype(bf16)

    @pl.when(step == pl.num_programs(0) - 1)
    def _():
        grad_qkv[:, width : 2 * width] = grad_keys[...].astype(bf16)
        grad_qkv[:, 2 * width :] = grad_values[...].astype(bf16)
        for head in range(heads_dev):
            grad_near[head] = grad_band[head, :, length - tile : length + 2 * tile]
            grad_far[head, 0] = jnp.full(
                (8, tile), jnp.sum(grad_band[head, :, : length - tile]), f32
            )
            grad_far[head, 1] = jnp.full(
                (8, tile), jnp.sum(grad_band[head, :, length + 2 * tile :]), f32
            )


def whole(shape):
    return pl.BlockSpec(shape, lambda step: (0,) * len(shape))


def attention(qkv, doc_row, doc_col, first, place, table, near, rows):
    length = qkv.shape[0]
    heads_dev = table.shape[1]
    width = heads_dev * head_dim
    return pl.pallas_call(
        functools.partial(attention_kernel, heads_dev, length),
        grid=(rows // tile,),
        in_specs=[
            pl.BlockSpec(memory_space=pltpu.SMEM),
            pl.BlockSpec(memory_space=pltpu.SMEM),
            pl.BlockSpec(memory_space=pltpu.SMEM),
            whole(near.shape),
            whole(qkv.shape),
            whole(doc_row.shape),
            pl.BlockSpec((tile, 1), lambda step: (step, 0)),
        ],
        out_specs=[
            whole((rows, width)),
            pl.BlockSpec((tile, width), lambda step: (step, 0)),
            pl.BlockSpec((tile, tile), lambda step: (step, 0)),
        ],
        out_shape=[
            jax.ShapeDtypeStruct((rows, width), bf16),
            jax.ShapeDtypeStruct((rows, width), bf16),
            jax.ShapeDtypeStruct((rows, tile), f32),
        ],
        scratch_shapes=[pltpu.VMEM((heads_dev, tile, 2 * length), f32)],
        compiler_params=pltpu.CompilerParams(vmem_limit_bytes=40 * 2**20),
        cost_estimate=pl.CostEstimate(
            flops=4 * rows * length * width,
            bytes_accessed=4 * length * width * 2,
            transcendentals=rows * length * heads_dev,
        ),
    )(first, place, table, near, qkv, doc_row, doc_col)


def attention_back(
    qkv, doc_row, doc_col, attended, grad_out, stats, first, place, table, near, split
):
    length = qkv.shape[0]
    rows = grad_out.shape[0]
    heads_dev = table.shape[1]
    width = heads_dev * head_dim
    return pl.pallas_call(
        functools.partial(attention_back_kernel, heads_dev, length, split),
        grid=(rows // tile,),
        in_specs=[
            pl.BlockSpec(memory_space=pltpu.SMEM),
            pl.BlockSpec(memory_space=pltpu.SMEM),
            pl.BlockSpec(memory_space=pltpu.SMEM),
            whole(near.shape),
            whole(qkv.shape),
            whole(doc_row.shape),
            pl.BlockSpec((tile, 1), lambda step: (step, 0)),
            whole((rows, width)),
            whole((rows, width)),
            pl.BlockSpec((tile, tile), lambda step: (step, 0)),
        ],
        out_specs=[
            whole((length, 3 * width)),
            whole((heads_dev, tile, 3 * tile)),
            whole((heads_dev, 2, 8, tile)),
        ],
        out_shape=[
            jax.ShapeDtypeStruct((length, 3 * width), bf16),
            jax.ShapeDtypeStruct((heads_dev, tile, 3 * tile), f32),
            jax.ShapeDtypeStruct((heads_dev, 2, 8, tile), f32),
        ],
        scratch_shapes=[
            pltpu.VMEM((heads_dev, tile, 2 * length), f32),
            pltpu.VMEM((heads_dev, tile, 2 * length), f32),
            pltpu.VMEM((length, width), f32),
            pltpu.VMEM((length, width), f32),
        ],
        compiler_params=pltpu.CompilerParams(vmem_limit_bytes=48 * 2**20),
        cost_estimate=pl.CostEstimate(
            flops=10 * rows * length * width,
            bytes_accessed=8 * length * width * 2,
            transcendentals=rows * length * heads_dev,
        ),
    )(first, place, table, near, qkv, doc_row, doc_col, attended, grad_out, stats)


def call(kernel, shapes, *operands, smem=0):
    return pl.pallas_call(
        kernel,
        in_specs=[pl.BlockSpec(memory_space=pltpu.SMEM)] * smem
        + [pl.BlockSpec(memory_space=pltpu.VMEM)] * (len(operands) - smem),
        out_specs=[pl.BlockSpec(memory_space=pltpu.VMEM)] * len(shapes),
        out_shape=[jax.ShapeDtypeStruct(shape, kind) for shape, kind in shapes],
        compiler_params=pltpu.CompilerParams(vmem_limit_bytes=32 * 2**20),
    )(*operands)


def share_in_kernel(layers, members, copies, core_n, attn_in, gains, *outs):
    width = attn_in.shape[2] // (3 * members)
    for layer_id in range(layers):
        for member in range(members):
            block = jnp.concatenate(
                [
                    attn_in[layer_id, :, (part * members + member) * width :][:, :width]
                    for part in range(3)
                ],
                axis=1,
            )
            block = (block.astype(f32) * gains[layer_id]).astype(bf16)
            for copy in range(copies):
                target = (member // core_n * copies + copy) * core_n + member % core_n
                outs[layer_id][target] = block


def plane_attention_kernel(
    length, place, table, strip, near, far, w_in, w_out, doc_row, doc_col,
    qkv, attended, stats, near_part, far_part, band,
):
    step = pl.program_id(0)
    half = length // 2
    heads_dev = table.shape[1]
    width = heads_dev * head_dim

    @pl.when(step == 0)
    def _():
        fill_band(band, table, strip, heads_dev, length)
        qkv[:half] = contract(near[...], w_in[...], 1, 0).astype(bf16)
        qkv[half:] = contract(far[...], w_in[...], 1, 0).astype(bf16)

    row = pl.multiple_of(step * tile, tile)
    starts = band_starts(place, step, length)
    same_doc = doc_col[...] == doc_row[...]
    queries = qkv[pl.ds(row, tile), :width] * bf16(score_scale)
    lanes = lax.broadcasted_iota(jnp.int32, (tile, tile), 1)
    collected = jnp.zeros((tile, tile), f32)
    results = []
    for head in range(heads_dev):
        own = slice(head * head_dim, (head + 1) * head_dim)
        keys = qkv[:, width + own.start : width + own.stop]
        values = qkv[:, 2 * width + own.start : 2 * width + own.stop]
        scores = contract(queries[:, own], keys, 1, 1) + jnp.concatenate(
            [band[head, :, pl.ds(start, tile)] for start in starts], axis=1
        )
        scores = jnp.where(same_doc, scores, masked)
        peak = jnp.max(scores, axis=1, keepdims=True)
        weights = jnp.exp(scores - peak)
        total = jnp.sum(weights, axis=1, keepdims=True)
        results.append((contract(weights.astype(bf16), values, 1, 0) / total).astype(bf16))
        collected = jnp.where(lanes == head, peak + jnp.log(total), collected)
    stats[...] = collected
    merged = jnp.concatenate(results, axis=1)
    attended[...] = merged
    part = contract(merged, w_out[...], 1, 0)

    @pl.when(row < half)
    def _():
        near_part[...] = part

    @pl.when(row >= half)
    def _():
        far_part[...] = part.astype(bf16)


def near_block(steps, columns):
    return pl.BlockSpec((tile, columns), lambda step: (jnp.minimum(step, steps // 2 - 1), 0))


def far_block(steps, columns):
    return pl.BlockSpec((tile, columns), lambda step: (jnp.maximum(step - steps // 2, 0), 0))


def plane_attention(near, far, w_in, w_out, doc_row, doc_col, place, table, strip):
    length, model_width = 2 * near.shape[0], near.shape[1]
    steps = length // tile
    heads_dev = table.shape[1]
    width = heads_dev * head_dim
    return pl.pallas_call(
        functools.partial(plane_attention_kernel, length),
        grid=(steps,),
        in_specs=[
            pl.BlockSpec(memory_space=pltpu.SMEM),
            pl.BlockSpec(memory_space=pltpu.SMEM),
            whole(strip.shape),
            whole(near.shape),
            whole(far.shape),
            whole(w_in.shape),
            whole(w_out.shape),
            whole(doc_row.shape),
            pl.BlockSpec((tile, 1), lambda step: (step, 0)),
        ],
        out_specs=[
            whole((length, 3 * width)),
            pl.BlockSpec((tile, width), lambda step: (step, 0)),
            pl.BlockSpec((tile, tile), lambda step: (step, 0)),
            near_block(steps, model_width),
            far_block(steps, model_width),
        ],
        out_shape=[
            jax.ShapeDtypeStruct((length, 3 * width), bf16),
            jax.ShapeDtypeStruct((length, width), bf16),
            jax.ShapeDtypeStruct((length, tile), f32),
            jax.ShapeDtypeStruct((length // 2, model_width), f32),
            jax.ShapeDtypeStruct((length // 2, model_width), bf16),
        ],
        scratch_shapes=[pltpu.VMEM((heads_dev, tile, 2 * length), f32)],
        compiler_params=pltpu.CompilerParams(vmem_limit_bytes=40 * 2**20),
        cost_estimate=pl.CostEstimate(
            flops=4 * length * length * width + 8 * length * model_width * width,
            bytes_accessed=12 * 2**20,
            transcendentals=length * length * heads_dev,
        ),
    )(place, table, strip, near, far, w_in, w_out, doc_row, doc_col)


def plane_attention_back_kernel(
    length, place, table, strip, qkv, doc_row, doc_col, attended, stats, near, far, w_in, w_out,
    grad_qkv, grad_near, grad_far, grad_out, near_part, far_part,
    band, grad_band, grad_keys, grad_values, out_sum,
):
    step = pl.program_id(0)
    half = length // 2
    heads_dev = table.shape[1]
    width = heads_dev * head_dim

    @pl.when(step == 0)
    def _():
        fill_band(band, table, strip, heads_dev, length)
        grad_band[...] = jnp.zeros_like(grad_band)
        grad_keys[...] = jnp.zeros_like(grad_keys)
        grad_values[...] = jnp.zeros_like(grad_values)
        out_sum[...] = jnp.zeros_like(out_sum)

    row = pl.multiple_of(step * tile, tile)
    starts = band_starts(place, step, length)
    same_doc = doc_col[...] == doc_row[...]
    branch = jnp.where(row < half, near[...], far[...])
    merged = attended[...]
    grad_merged = contract(branch, w_out[...], 1, 1).astype(bf16)
    out_sum[...] += contract(merged, branch, 0, 0)
    products = grad_merged.astype(f32) * merged.astype(f32)
    queries = qkv[pl.ds(row, tile), :width] * bf16(score_scale)
    for head in range(heads_dev):
        own = slice(head * head_dim, (head + 1) * head_dim)
        keys = qkv[:, width + own.start : width + own.stop]
        values = qkv[:, 2 * width + own.start : 2 * width + own.stop]
        upstream = grad_merged[:, own]
        scores = contract(queries[:, own], keys, 1, 1) + jnp.concatenate(
            [band[head, :, pl.ds(start, tile)] for start in starts], axis=1
        )
        scores = jnp.where(same_doc, scores, masked)
        weights = jnp.exp(scores - stats[:, head : head + 1])
        delta = jnp.sum(products[:, own], axis=1, keepdims=True)
        grad_scores = weights * (contract(upstream, values, 1, 1) - delta)
        for block, start in enumerate(starts):
            grad_band[head, :, pl.ds(start, tile)] += grad_scores[
                :, block * tile : (block + 1) * tile
            ]
        grad_low = grad_scores.astype(bf16)
        grad_values[:, own] += contract(weights.astype(bf16), upstream, 0, 0)
        grad_keys[:, own] += contract(grad_low, queries[:, own], 0, 0)
        grad_qkv[pl.ds(row, tile), own] = (
            contract(grad_low, keys, 1, 0) * score_scale
        ).astype(bf16)

    @pl.when(step == pl.num_programs(0) - 1)
    def _():
        grad_qkv[:, width : 2 * width] = grad_keys[...].astype(bf16)
        grad_qkv[:, 2 * width :] = grad_values[...].astype(bf16)
        far_part[...] = contract(grad_qkv[half:], w_in[...], 1, 1).astype(bf16)
        near_part[...] = contract(grad_qkv[:half], w_in[...], 1, 1)
        grad_out[...] = jnp.zeros_like(grad_out)
        at_core = pl.multiple_of(place[length // tile] * width, width)
        grad_out[pl.ds(at_core, width)] = out_sum[...].astype(bf16)
        for head in range(heads_dev):
            grad_near[head] = grad_band[head, :, length - tile : length + 2 * tile]
            grad_far[head, 0] = jnp.full(
                (8, tile), jnp.sum(grad_band[head, :, : length - tile]), f32
            )
            grad_far[head, 1] = jnp.full(
                (8, tile), jnp.sum(grad_band[head, :, length + 2 * tile :]), f32
            )


def plane_attention_back(
    qkv, doc_row, doc_col, attended, stats, near, far, w_in, w_out, place, table, strip
):
    length, model_width = 2 * near.shape[0], near.shape[1]
    steps = length // tile
    heads_dev = table.shape[1]
    width = heads_dev * head_dim
    shapes = [
        ((length, 3 * width), bf16),
        ((heads_dev, tile, 3 * tile), f32),
        ((heads_dev, 2, 8, tile), f32),
        ((2 * width, model_width), bf16),
        ((length // 2, model_width), f32),
        ((length // 2, model_width), bf16),
    ]
    return pl.pallas_call(
        functools.partial(plane_attention_back_kernel, length),
        grid=(steps,),
        in_specs=[
            pl.BlockSpec(memory_space=pltpu.SMEM),
            pl.BlockSpec(memory_space=pltpu.SMEM),
            whole(strip.shape),
            whole(qkv.shape),
            whole(doc_row.shape),
            pl.BlockSpec((tile, 1), lambda step: (step, 0)),
            pl.BlockSpec((tile, width), lambda step: (step, 0)),
            pl.BlockSpec((tile, tile), lambda step: (step, 0)),
            near_block(steps, model_width),
            far_block(steps, model_width),
            whole(w_in.shape),
            whole(w_out.shape),
        ],
        out_specs=[whole(shape) for shape, _ in shapes],
        out_shape=[jax.ShapeDtypeStruct(shape, kind) for shape, kind in shapes],
        scratch_shapes=[
            pltpu.VMEM((heads_dev, tile, 2 * length), f32),
            pltpu.VMEM((heads_dev, tile, 2 * length), f32),
            pltpu.VMEM((length, width), f32),
            pltpu.VMEM((length, width), f32),
            pltpu.VMEM((width, model_width), f32),
        ],
        compiler_params=pltpu.CompilerParams(vmem_limit_bytes=48 * 2**20),
        cost_estimate=pl.CostEstimate(
            flops=10 * length * length * width + 10 * length * model_width * width,
            bytes_accessed=12 * 2**20,
            transcendentals=length * length * heads_dev,
        ),
    )(place, table, strip, qkv, doc_row, doc_col, attended, stats, near, far, w_in, w_out)


def gelu_and_slope(pre_act):
    size = jnp.abs(pre_act)
    gauss = jnp.exp(-0.5 * pre_act * pre_act)
    ratio = 1.0 / (1.0 + np.float32(0.3275911 * 0.5**0.5) * size)
    series = np.float32(1.061405429)
    for factor in (-1.453152027, 1.421413741, -0.284496736, 0.254829592):
        series = series * ratio + np.float32(factor)
    tail = 0.5 * series * ratio * gauss
    cumulative = jnp.where(pre_act < 0, tail, 1.0 - tail)
    slope = cumulative + pre_act * gauss * np.float32((2 * np.pi) ** -0.5)
    return pre_act * cumulative, slope


def ff_kernel(rows, w_up, w_down, activated, slope, part):
    value, gradient = gelu_and_slope(contract(rows[...], w_up[...], 1, 1))
    activated[...] = value.astype(bf16)
    slope[...] = gradient.astype(bf16)
    part[...] = contract(activated[...], w_down[...], 1, 0).astype(part.dtype)


def ff_back_kernel(rows, slope, w_up, w_down, grad_pre, part):
    grad_pre[...] = (contract(rows[...], w_down[...], 1, 1) * slope[...].astype(f32)).astype(bf16)
    part[...] = contract(grad_pre[...], w_up[...], 1, 0).astype(part.dtype)


def by_rows(kernel, step_rows, row_operands, whole_operands, outs):
    rows = row_operands[0].shape[0]
    return pl.pallas_call(
        kernel,
        grid=(rows // step_rows,),
        in_specs=[
            pl.BlockSpec((step_rows, operand.shape[1]), lambda step: (step, 0))
            for operand in row_operands
        ]
        + [whole(operand.shape) for operand in whole_operands],
        out_specs=[pl.BlockSpec((step_rows, columns), lambda step: (step, 0)) for columns, _ in outs],
        out_shape=[jax.ShapeDtypeStruct((rows, columns), kind) for columns, kind in outs],
        compiler_params=pltpu.CompilerParams(vmem_limit_bytes=32 * 2**20),
        cost_estimate=pl.CostEstimate(
            flops=4 * rows * whole_operands[0].shape[0] * whole_operands[0].shape[1],
            bytes_accessed=6 * 2**20,
            transcendentals=0,
        ),
    )(*row_operands, *whole_operands)


def ff_grads_kernel(
    pre_near, pre_far, act_near, act_far, normed_near, normed_far, low_near, low_far, out
):
    columns = normed_near.shape[1]
    out[:, :columns] = (
        contract(pre_near[...], normed_near[...], 0, 0)
        + contract(pre_far[...], normed_far[...], 0, 0)
    ).astype(bf16)
    out[:, columns:] = (
        contract(act_near[...], low_near[...], 0, 0) + contract(act_far[...], low_far[...], 0, 0)
    ).astype(bf16)


def ff_grads(pre, act, normed, low):
    rows, hidden_units = pre[0].shape
    columns = normed[0].shape[1]
    step_units = 256
    return pl.pallas_call(
        ff_grads_kernel,
        grid=(hidden_units // step_units,),
        in_specs=[pl.BlockSpec((rows, step_units), lambda step: (0, step))] * 4
        + [whole((rows, columns))] * 4,
        out_specs=pl.BlockSpec((step_units, 2 * columns), lambda step: (step, 0)),
        out_shape=jax.ShapeDtypeStruct((hidden_units, 2 * columns), bf16),
        compiler_params=pltpu.CompilerParams(vmem_limit_bytes=40 * 2**20),
        cost_estimate=pl.CostEstimate(
            flops=8 * rows * hidden_units * columns, bytes_accessed=8 * 2**20, transcendentals=0
        ),
    )(*pre, *act, *normed, *low)


def in_grads_kernel(near, far, grad_qkv, out):
    half = near.shape[0]
    out[...] = (
        contract(near[...], grad_qkv[:half], 0, 0) + contract(far[...], grad_qkv[half:], 0, 0)
    ).astype(bf16)


def in_grads(near, far, grad_qkv):
    rows, columns = near.shape
    step_columns = 256
    return pl.pallas_call(
        in_grads_kernel,
        grid=(columns // step_columns,),
        in_specs=[pl.BlockSpec((rows, step_columns), lambda step: (0, step))] * 2
        + [whole(grad_qkv.shape)],
        out_specs=pl.BlockSpec((step_columns, grad_qkv.shape[1]), lambda step: (step, 0)),
        out_shape=jax.ShapeDtypeStruct((columns, grad_qkv.shape[1]), bf16),
        compiler_params=pltpu.CompilerParams(vmem_limit_bytes=32 * 2**20),
        cost_estimate=pl.CostEstimate(
            flops=4 * rows * columns * grad_qkv.shape[1],
            bytes_accessed=4 * 2**20,
            transcendentals=0,
        ),
    )(near, far, grad_qkv)


def combine_kernel(near_part, arrived, own, x_part, y_part, xy_part):
    rows = own.shape[0]
    own[...] = near_part[:rows] + arrived[:rows].astype(f32)
    for bits, out in ((1, x_part), (2, y_part), (3, xy_part)):
        block = slice(bits * rows, (bits + 1) * rows)
        out[...] = (near_part[block] + arrived[block].astype(f32)).astype(bf16)


def added(own, x_part, y_part, xy_part):
    return (own[...] + x_part[...].astype(f32)) + (
        y_part[...].astype(f32) + xy_part[...].astype(f32)
    )


def close_kernel(kept, own, x_part, y_part, xy_part, hidden, units):
    total = kept[...] + added(own, x_part, y_part, xy_part)
    hidden[...] = total
    units[...] = (total * inverse_rms(total)).astype(bf16)


def close_gain_kernel(kept, own, x_part, y_part, xy_part, gain, hidden, normed):
    total = kept[...] + added(own, x_part, y_part, xy_part)
    hidden[...] = total
    normed[...] = (total * inverse_rms(total) * gain[...]).astype(bf16)


def last_kernel(kept, own, x_part, y_part, xy_part, hidden):
    hidden[...] = (kept[...] + added(own, x_part, y_part, xy_part)).astype(bf16)


def middle_back_kernel(
    upstream, own, x_part, y_part, xy_part, middle, gain, grad_middle, branch, grad_gain
):
    grad_normed = added(own, x_part, y_part, xy_part)
    inverse = inverse_rms(middle[...])
    grad_gain[...] = jnp.sum(grad_normed * middle[...] * inverse, axis=0, keepdims=True)
    total = upstream[...].astype(f32) + unit_norm_back(
        middle[...], inverse, grad_normed * gain[...]
    )
    grad_middle[...] = total
    branch[...] = total.astype(bf16)


def layer_back_kernel(grad_middle, own, x_part, y_part, xy_part, hidden, upstream, low):
    total = grad_middle[...] + unit_norm_back(
        hidden[...], inverse_rms(hidden[...]), added(own, x_part, y_part, xy_part)
    )
    upstream[...] = total
    low[...] = total.astype(bf16)


def finish_in_kernel(layers, groups, copies, *refs):
    shares, (attn_in, gains), (grad_in, grad_gain) = (
        refs[:layers], refs[layers : layers + 2], refs[layers + 2 :],
    )
    members = groups * 2
    width = attn_in.shape[2] // (3 * members)
    for layer_id in range(layers):
        row_dot = jnp.zeros(grad_gain.shape[1:], f32)
        for member in range(members):
            total = 0.0
            for copy in range(copies):
                source = (member // 2 * copies + copy) * 2 + member % 2
                total = total + shares[layer_id][source].astype(f32)
            for part in range(3):
                columns = slice((part * members + member) * width, (part * members + member + 1) * width)
                block = total[:, part * width : (part + 1) * width]
                grad_in[layer_id, :, columns] = block * gains[layer_id]
                row_dot = row_dot + jnp.sum(
                    block * attn_in[layer_id, :, columns].astype(f32), axis=1, keepdims=True
                )
        grad_gain[layer_id] = row_dot


def finish_ff_kernel(first_layer, counts, *refs):
    grad_up, grad_down = refs[-2:]
    columns = grad_up.shape[2]
    at = 0
    for layer_id, count in enumerate(counts):
        total = refs[at][...].astype(f32)
        for part in refs[at + 1 : at + count]:
            total = total + part[...].astype(f32)
        at += count
        grad_up[layer_id] = total[:, :columns]
        grad_down[layer_id] = total[:, columns:]


def inverse_rms(hidden):
    return lax.rsqrt(jnp.mean(hidden * hidden, axis=-1, keepdims=True) + epsilon)


def prepare(bias_table, first_head, heads_dev):
    table = lax.dynamic_slice_in_dim(bias_table, first_head, heads_dev, 1)
    (near,) = call(near_kernel, [((heads_dev, tile, 3 * tile), f32)], table, smem=1)
    return table, near


def bucket_grads(grads, bucket_count):
    heads_dev = grads[0][0].shape[0]
    (total,) = call(
        functools.partial(bucket_kernel, len(grads)),
        [((bucket_count, tile), f32)],
        *(entry[0] for entry in grads),
        *(entry[1] for entry in grads),
    )
    return total[:, :heads_dev]


def gelu_parts(pre_act):
    cumulative = 0.5 * (1.0 + lax.erf(pre_act * np.float32(0.5**0.5)))
    slope = cumulative + pre_act * jnp.exp(-0.5 * pre_act * pre_act) * np.float32(
        (2 * np.pi) ** -0.5
    )
    return (pre_act * cumulative).astype(bf16), slope


def unit_norm_back(hidden, inverse, grad_unit):
    unit = hidden * inverse
    return inverse * (grad_unit - unit * jnp.mean(grad_unit * unit, axis=-1, keepdims=True))


def gather_rows(block, axes):
    return lax.all_gather(block, axes, axis=0, tiled=True)


def toggle(array, axis, bits):
    return lax.ppermute(array, axis, [(i, i ^ bits) for i in range(lax.axis_size(axis))])


def plane_gather(block, hold=None):
    near = jnp.concatenate([block] + [toggle(block, "head", bits) for bits in (1, 2, 3)])
    near = near if hold is None else after(near, hold)
    return near, toggle(near, "core", 1)


def plane_scatter(near_part, far_part):
    rows, columns = near_part.shape[0] // 4, near_part.shape[1]
    own, *others = call(
        combine_kernel,
        [((rows, columns), f32)] + [((rows, columns), bf16)] * 3,
        near_part,
        toggle(far_part, "core", 1),
    )
    return [own] + [toggle(other, "head", bits) for bits, other in zip((1, 2, 3), others)]


def after(array, other):
    return lax.optimization_barrier((array, other))[0]


def scatter_sum(partial, axes, members):
    blocks = partial.astype(bf16).reshape(members, -1, partial.shape[1])
    return jnp.sum(lax.all_to_all(blocks, axes, 0, 0, tiled=True).astype(f32), axis=0)


def local_general(tokens, doc_start, bias_table, attn_in, attn_out, ff_in, ff_out, gains, cotangent):
    heads_n, z_n, core_n = (lax.axis_size(axis) for axis in everyone)
    devices = heads_n * z_n * core_n
    group, spare = ("z", "core"), "head"
    ff_group, ff_spare, ff_members = ("head", "core"), "z", heads_n * core_n
    blocks = z_n * core_n
    block_rows, model_width = tokens.shape[1:]
    layer_count, weight_rows = attn_in.shape[:2]
    length = block_rows * blocks
    heads_all = bias_table.shape[1]
    member = lax.axis_index("z") * core_n + lax.axis_index("core")
    heads_dev = max(1, heads_all // blocks)
    head_groups = heads_all // heads_dev
    split = blocks // head_groups
    head_group, query_part = member // split, member % split
    query_rows = length // split
    width = heads_dev * head_dim
    first = (query_part * (query_rows // tile)).astype(jnp.int32).reshape(1)
    place = jnp.arange(length // tile, dtype=jnp.int32)
    out_row = head_group * width

    def swap(array):
        return lax.all_to_all(array, everyone, 0, 0, tiled=True)

    starts = jnp.broadcast_to(
        doc_start.astype(f32)[:, None], (heads_n, blocks, block_rows)
    ).reshape(devices, block_rows)
    ff_gains = gains[:, :, 1].astype(f32).reshape(1, -1)
    small = swap(
        jnp.concatenate(
            [starts, jnp.broadcast_to(ff_gains, (devices, layer_count * weight_rows))], axis=1
        )
    )
    doc_row = small[:blocks, :block_rows].reshape(1, length)
    doc_col = lax.dynamic_slice_in_dim(
        doc_row.reshape(length, 1), query_part * query_rows, query_rows, 0
    )
    gain_ff = jnp.transpose(
        small[:, block_rows:].reshape(devices, layer_count, weight_rows), (1, 0, 2)
    ).reshape(layer_count, 1, model_width)
    table, near = prepare(bias_table, head_group * heads_dev, heads_dev)

    gain_attn = gains[:, :, 0].astype(f32)[:, :, None]
    own_in = attn_in.astype(f32)

    def fetch_in(layer_id):
        scaled = (own_in[layer_id] * gain_attn[layer_id]).astype(bf16)
        columns = jnp.transpose(
            scaled.reshape(weight_rows, 3, head_groups, width), (2, 0, 1, 3)
        ).reshape(head_groups, weight_rows, 3 * width)
        columns = jnp.repeat(columns, split, axis=0)
        columns = jnp.broadcast_to(columns[None], (heads_n, *columns.shape))
        return swap(columns.reshape(devices, weight_rows, 3 * width)).reshape(
            model_width, 3 * width
        )

    def fetch_ff(layer_id):
        pair = jnp.concatenate([ff_in[layer_id], ff_out[layer_id]], axis=1)
        pair = gather_rows(pair, ff_spare)
        return pair[:, :model_width], pair[:, model_width:]

    hidden, upstream = tokens[0].astype(f32), cotangent[0]
    weights_in = [fetch_in(layer_id) for layer_id in range(layer_count)]
    weights_out = lax.dynamic_slice_in_dim(
        lax.all_gather(attn_out, everyone, axis=1, tiled=True), out_row, width, 1
    )
    weights_ff = [fetch_ff(layer_id) for layer_id in range(layer_count)]

    records = []
    for layer_id in range(layer_count):
        w_in, w_out, (w_up, w_down) = (
            weights_in[layer_id], weights_out[layer_id], weights_ff[layer_id],
        )
        inverse = inverse_rms(hidden)
        units = gather_rows((hidden * inverse).astype(bf16), group)
        qkv = jnp.dot(units, w_in, preferred_element_type=f32).astype(bf16)
        attended, _, stats = attention(
            qkv, doc_row, doc_col, first, place, table, near, query_rows
        )
        mixed = jnp.dot(attended, w_out, preferred_element_type=f32)
        if split > 1:
            mixed = lax.dynamic_update_slice_in_dim(
                jnp.zeros((length, model_width), f32), mixed, query_part * query_rows, 0
            )
        middle = hidden + scatter_sum(mixed, group, blocks)
        inverse_ff = inverse_rms(middle)
        normed_ff = gather_rows((middle * inverse_ff * gain_ff[layer_id]).astype(bf16), ff_group)
        activated, slope = gelu_parts(contract(normed_ff, w_up, 1, 1))
        ff_result = jnp.dot(activated, w_down, preferred_element_type=f32)
        records.append(
            (hidden, inverse, units, qkv, attended, stats, middle, inverse_ff, normed_ff,
             activated, slope)
        )
        hidden = middle + scatter_sum(ff_result, ff_group, ff_members)
    output = hidden

    grads_ff, grads_in, grads_out, grads_gain_ff, grads_table = (
        [None] * layer_count for _ in range(5)
    )
    for layer_id in reversed(range(layer_count)):
        w_in, w_out, (w_up, w_down) = (
            weights_in[layer_id], weights_out[layer_id], weights_ff[layer_id],
        )
        (hidden, inverse, units, qkv, attended, stats, middle, inverse_ff, normed_ff,
         activated, slope) = records[layer_id]
        grad_low = gather_rows(upstream.astype(bf16), ff_group)
        grad_pre = (contract(grad_low, w_down, 1, 1) * slope).astype(bf16)
        grad_normed = scatter_sum(
            jnp.dot(grad_pre, w_up, preferred_element_type=f32), ff_group, ff_members
        )
        grad_pair = jnp.concatenate(
            [contract(grad_pre, normed_ff, 0, 0), contract(activated, grad_low, 0, 0)], axis=1
        ).astype(bf16)
        grads_ff[layer_id] = lax.psum_scatter(
            grad_pair, ff_spare, scatter_dimension=0, tiled=True
        ).astype(f32)
        grads_gain_ff[layer_id] = jnp.sum(grad_normed * middle * inverse_ff, axis=0)
        grad_middle = upstream + unit_norm_back(
            middle, inverse_ff, grad_normed * gain_ff[layer_id]
        )
        branch = gather_rows(grad_middle.astype(bf16), group)
        if split > 1:
            branch = lax.dynamic_slice_in_dim(branch, query_part * query_rows, query_rows, 0)
        grad_attended = contract(branch, w_out, 1, 1).astype(bf16)
        grad_qkv, grad_near, grad_far = attention_back(
            qkv, doc_row, doc_col, attended, grad_attended, stats, first, place, table, near, split
        )
        grads_table[layer_id] = (grad_near, grad_far)
        grad_units = scatter_sum(contract(grad_qkv, w_in, 1, 1), group, blocks)
        upstream = grad_middle + unit_norm_back(hidden, inverse, grad_units)
        grad_out = lax.dynamic_update_slice_in_dim(
            jnp.zeros((model_width, model_width), bf16),
            contract(attended, branch, 0, 0).astype(bf16),
            out_row,
            0,
        )
        grads_out[layer_id] = lax.psum_scatter(
            grad_out, everyone, scatter_dimension=0, tiled=True
        ).astype(f32)
        grads_in[layer_id] = contract(units, grad_qkv, 0, 0).astype(bf16)

    bucket_count = table.shape[0]
    grad_table = bucket_grads(grads_table, bucket_count)
    grad_table = lax.dynamic_update_slice_in_dim(
        jnp.zeros((bucket_count, heads_all), f32), grad_table, head_group * heads_dev, 1
    )
    grad_table = jnp.transpose(
        grad_table.reshape(blocks, bucket_count // blocks, heads_n, heads_all // heads_n),
        (2, 0, 1, 3),
    ).reshape(devices, -1)
    grad_gain_ff = jnp.transpose(
        jnp.stack(grads_gain_ff).reshape(layer_count, devices, weight_rows), (1, 0, 2)
    ).reshape(devices, -1)
    ends = jnp.sum(swap(jnp.concatenate([grad_gain_ff, grad_table], axis=1)), axis=0)
    grad_gain_ff = ends[: layer_count * weight_rows].reshape(layer_count, weight_rows)
    grad_bias_table = ends[layer_count * weight_rows :].reshape(
        bucket_count // blocks, heads_all // heads_n
    )
    grads_attn_in, grads_gains = [], []
    for layer_id in range(layer_count):
        parts = swap(grads_in[layer_id].reshape(devices, weight_rows, 3 * width)).astype(f32)
        parts = jnp.sum(parts.reshape(heads_n, blocks, weight_rows, 3 * width), axis=0)
        parts = jnp.sum(parts.reshape(head_groups, split, weight_rows, 3, width), axis=1)
        unit_grad = jnp.transpose(parts, (1, 2, 0, 3)).reshape(weight_rows, 3 * model_width)
        grads_attn_in.append(unit_grad * gain_attn[layer_id])
        grads_gains.append(
            jnp.stack(
                [jnp.sum(unit_grad * own_in[layer_id], axis=1), grad_gain_ff[layer_id]], axis=1
            )
        )
    return (
        output[None],
        upstream[None],
        jnp.stack(grads_attn_in),
        jnp.stack(grads_out),
        jnp.stack([entry[:, :model_width] for entry in grads_ff]),
        jnp.stack([entry[:, model_width:] for entry in grads_ff]),
        jnp.stack(grads_gains),
        grad_bias_table,
    )


def local_plane(tokens, doc_start, bias_table, attn_in, attn_out, ff_in, ff_out, gains, cotangent):
    heads_n, z_n, core_n = (lax.axis_size(axis) for axis in everyone)
    devices = heads_n * z_n * core_n
    at_head, at_z, at_core = (lax.axis_index(axis) for axis in everyone)
    members = heads_n * core_n
    block_rows, model_width = tokens.shape[1:]
    layer_count, weight_rows = attn_in.shape[:2]
    length = block_rows * members
    heads_all = bias_table.shape[1]
    heads_dev = heads_all // members
    width = heads_dev * head_dim
    member = at_head * core_n + at_core
    turn = [
        ((h * z_n + z) * core_n + c, (z * z_n + h) * core_n + c)
        for h in range(heads_n)
        for z in range(z_n)
        for c in range(core_n)
    ]
    place = jnp.stack(
        [
            (at_head ^ bits) * core_n + (at_core ^ other)
            for other in range(core_n)
            for bits in range(heads_n)
        ]
        + [at_core]
    ).astype(jnp.int32)

    def relay(array):
        return lax.ppermute(array, everyone, turn)

    def swap(array):
        return lax.all_to_all(array, everyone, 0, 0, tiled=True)

    gain_attn = gains[:, :, 0].astype(f32)[:, :, None]
    shares = call(
        functools.partial(share_in_kernel, layer_count, members, z_n, core_n),
        [((devices, weight_rows, 3 * width), bf16)] * layer_count,
        attn_in,
        gain_attn,
    )
    hidden = relay(after(tokens[0], shares[0])).astype(f32)
    weights_in = [swap(shares[0]).reshape(model_width, 3 * width)]

    starts = jnp.broadcast_to(
        doc_start.astype(f32)[None, :, None], (heads_n, z_n, core_n, block_rows)
    )
    ff_gains = gains[:, :, 1].astype(f32).reshape(1, -1)
    small = jnp.concatenate(
        [
            starts.reshape(devices, block_rows),
            jnp.broadcast_to(ff_gains, (devices, layer_count * weight_rows)),
        ],
        axis=1,
    )
    small = swap(after(small, hidden))
    doc_row = small[:members, :block_rows].reshape(2, 2, core_n, block_rows)
    for axis, bit in ((0, at_head // 2), (1, at_head % 2), (2, at_core)):
        doc_row = jnp.where(bit == 1, jnp.flip(doc_row, axis), doc_row)
    doc_row = jnp.transpose(doc_row, (2, 0, 1, 3)).reshape(1, length)
    doc_col = doc_row.reshape(length, 1)
    gain_ff = jnp.transpose(
        small[:, block_rows:].reshape(devices, layer_count, weight_rows), (1, 0, 2)
    ).reshape(layer_count, 1, model_width)
    table, strip = prepare(bias_table, member * heads_dev, heads_dev)

    held = after(attn_out, weights_in[0])
    quarters = [
        lax.ppermute(
            held,
            ("z", "core"),
            [
                ((2 * c + (a ^ z % 2)) * core_n + (b ^ z // 2), z * core_n + c)
                for z in range(z_n)
                for c in range(core_n)
            ],
        )
        for a in range(2)
        for b in range(2)
    ]
    quarters = jnp.stack(quarters, axis=1).reshape(
        layer_count, 2, 2, weight_rows, model_width
    )
    quarters = jnp.where(at_z % 2 == 1, jnp.flip(quarters, 1), quarters)
    quarters = jnp.where(at_z // 2 == 1, jnp.flip(quarters, 2), quarters)
    weights_out = [quarters[layer_id].reshape(width, model_width) for layer_id in range(layer_count)]

    def fetch_ff(layer_id, hold):
        pair = jnp.concatenate([ff_in[layer_id], ff_out[layer_id]], axis=1)
        pair = gather_rows(after(pair, hold), "z")
        return pair[:, :model_width], pair[:, model_width:]

    weights_ff = [fetch_ff(0, hidden)]

    row_shape = (block_rows, model_width)
    hidden_units = weights_ff[0][0].shape[0]
    records = []
    unit_rows = (hidden * inverse_rms(hidden)).astype(bf16)
    for layer_id in range(layer_count):
        w_in, w_out, (w_up, w_down) = (
            weights_in[layer_id], weights_out[layer_id], weights_ff[layer_id],
        )
        units = plane_gather(unit_rows, w_in)
        qkv, attended, stats, *parts = plane_attention(
            *units, w_in, w_out, doc_row, doc_col, place, table, strip
        )
        parts = plane_scatter(*parts)
        middle, normed_rows = call(
            close_gain_kernel,
            [(row_shape, f32), (row_shape, bf16)],
            hidden,
            *parts,
            gain_ff[layer_id],
        )
        normed = plane_gather(normed_rows)
        if layer_id + 1 < layer_count:
            later = swap(after(shares[layer_id + 1], normed_rows))
            weights_in.append(later.reshape(model_width, 3 * width))
            weights_ff.append(fetch_ff(layer_id + 1, normed_rows))
            upstream = relay(after(cotangent[0].astype(bf16), normed[0]))
        acts, slopes, parts = zip(
            *(
                by_rows(
                    ff_kernel,
                    256,
                    [rows],
                    [w_up, w_down],
                    [(hidden_units, bf16), (hidden_units, bf16), (model_width, kind)],
                )
                for rows, kind in zip(normed, (f32, bf16))
            )
        )
        records.append((hidden, units, qkv, attended, stats, middle, normed, acts, slopes))
        if layer_id + 1 < layer_count:
            hidden, unit_rows = call(
                close_kernel,
                [(row_shape, f32), (row_shape, bf16)],
                middle,
                *plane_scatter(*parts),
            )
    last_parts = parts

    low_rows = upstream
    grads_ff, grads_in, grads_out, grads_gain_ff, grads_table = (
        [None] * layer_count for _ in range(5)
    )
    for layer_id in reversed(range(layer_count)):
        w_in, w_out, (w_up, w_down) = (
            weights_in[layer_id], weights_out[layer_id], weights_ff[layer_id],
        )
        hidden, units, qkv, attended, stats, middle, normed, acts, slopes = records[layer_id]
        low = plane_gather(low_rows)
        pres, parts = zip(
            *(
                by_rows(
                    ff_back_kernel,
                    256,
                    [rows, slope],
                    [w_up, w_down],
                    [(hidden_units, bf16), (model_width, kind)],
                )
                for rows, slope, kind in zip(low, slopes, (f32, bf16))
            )
        )
        parts = plane_scatter(*parts)
        grad_pair = ff_grads(pres, acts, normed, low)
        if layer_id == 0:
            blocks = grad_pair.reshape(z_n, -1, 2 * model_width)
            grads_ff[layer_id] = [
                lax.dynamic_index_in_dim(blocks, at_z, 0, keepdims=False)
            ] + [
                toggle(lax.dynamic_index_in_dim(blocks, at_z ^ bits, 0, keepdims=False), "z", bits)
                for bits in range(1, z_n)
            ]
        else:
            grads_ff[layer_id] = [
                lax.psum_scatter(grad_pair, "z", scatter_dimension=0, tiled=True)
            ]
        grad_middle, branch_rows, grads_gain_ff[layer_id] = call(
            middle_back_kernel,
            [(row_shape, f32), (row_shape, bf16), ((1, model_width), f32)],
            upstream,
            *parts,
            middle,
            gain_ff[layer_id],
        )
        branch = plane_gather(branch_rows)
        grad_qkv, *grads_table[layer_id], grad_out, near_part, far_part = plane_attention_back(
            qkv, doc_row, doc_col, attended, stats, *branch, w_in, w_out, place, table, strip
        )
        if layer_id + 1 == layer_count:
            last_parts = plane_scatter(*after(last_parts, branch[0]))
        parts = plane_scatter(near_part, far_part)
        grads_out[layer_id] = lax.psum_scatter(
            grad_out, ("z", "core"), scatter_dimension=0, tiled=True
        )
        upstream, low_rows = call(
            layer_back_kernel, [(row_shape, f32), (row_shape, bf16)], grad_middle, *parts, hidden
        )
        if layer_id + 1 == layer_count:
            (output,) = call(
                last_kernel, [(row_shape, bf16)], after(middle, low_rows), *last_parts
            )
            output = relay(output)
            hold = low_rows
        else:
            grad_tokens = [
                relay(low_rows[part * tile // 2 : (part + 1) * tile // 2]) for part in range(2)
            ]
            hold = grad_tokens[0]
        grad_in = in_grads(*units, grad_qkv)
        grads_in[layer_id] = swap(
            after(grad_in, hold).reshape(devices, weight_rows, 3 * width)
        )
    output = after(output, low_rows).astype(f32)

    bucket_count = table.shape[0]
    grad_table = bucket_grads(grads_table, bucket_count)
    grad_table = lax.dynamic_update_slice_in_dim(
        jnp.zeros((bucket_count, heads_all), f32), grad_table, member * heads_dev, 1
    )
    grad_table = jnp.transpose(
        grad_table.reshape(members, bucket_count // members, heads_n, heads_all // heads_n),
        (2, 0, 1, 3),
    ).reshape(devices, -1)
    grad_gain_ff = jnp.transpose(
        jnp.concatenate(grads_gain_ff).reshape(layer_count, devices, weight_rows), (1, 0, 2)
    ).reshape(devices, -1)
    ends = jnp.concatenate([grad_gain_ff, grad_table], axis=1)
    ends = jnp.sum(after(swap(ends), grad_tokens[0]), axis=0)
    grad_gain_ff = ends[: layer_count * weight_rows].reshape(layer_count, weight_rows)
    grad_bias_table = ends[layer_count * weight_rows :].reshape(
        bucket_count // members, heads_all // heads_n
    )
    ff_rows = ff_in.shape[1]
    grad_up, grad_down = call(
        functools.partial(finish_ff_kernel, 0, [len(parts) for parts in grads_ff]),
        [((layer_count, ff_rows, model_width), f32)] * 2,
        *after(grads_ff[0] + grads_ff[1], grad_tokens[0]),
    )
    grad_attn_in, grad_gain_attn = call(
        functools.partial(finish_in_kernel, layer_count, heads_n, z_n),
        [(attn_in.shape, f32), ((layer_count, weight_rows, 1), f32)],
        *grads_in,
        attn_in,
        gain_attn,
    )
    return (
        output[None],
        jnp.concatenate(grad_tokens).astype(f32)[None],
        grad_attn_in,
        jnp.stack(grads_out).astype(f32),
        grad_up,
        grad_down,
        jnp.concatenate([grad_gain_attn, grad_gain_ff[:, :, None]], axis=2),
        grad_bias_table,
    )


def solution(mesh):
    sizes = dict(mesh.shape)
    cores = 2
    fine = Mesh(
        mesh.devices.reshape(sizes["head"], sizes["blk"] // cores, cores), everyone
    )
    blk = ("z", "core")
    in_specs = (
        P("head", blk, None),
        P(None, blk),
        P(),
        P(None, everyone, None),
        P(None, everyone, None),
        P(None, everyone, None),
        P(None, everyone, None),
        P(None, everyone, None),
        P("head", blk, None),
    )
    out_specs = (
        P("head", blk, None),
        P("head", blk, None),
        P(None, everyone, None),
        P(None, everyone, None),
        P(None, everyone, None),
        P(None, everyone, None),
        P(None, everyone, None),
        P(blk, "head"),
    )
    plane = sizes["head"] == 4 and sizes["blk"] == 8
    local = local_plane if plane else local_general
    return jax.shard_map(local, mesh=fine, in_specs=in_specs, out_specs=out_specs, check_vma=False)
```

```python
import functools

import jax
import jax.numpy as jnp
import numpy as np
from jax import lax
from jax.experimental import pallas as pl
from jax.experimental.pallas import tpu as pltpu
from jax.sharding import Mesh
from jax.sharding import PartitionSpec as P

bounds = (1, 2, 3, 4, 5, 6, 7, 8, 12, 16, 23, 32, 46, 64, 91)
epsilon = 1e-06
masked = -1e30
score_scale = 0.125
head_dim = 64
tile = 128
everyone = ("head", "z", "core")
bf16 = jnp.bfloat16
f32 = jnp.float32


def contract(lhs, rhs, lhs_dim, rhs_dim):
    return lax.dot_general(
        lhs, rhs, (((lhs_dim,), (rhs_dim,)), ((), ())), preferred_element_type=f32
    )


def near_buckets(shape):
    offsets = (
        lax.broadcasted_iota(jnp.int32, shape, 1) - tile - lax.broadcasted_iota(jnp.int32, shape, 0)
    )
    distance = jnp.abs(offsets)
    bucket = jnp.where(offsets > 0, 16, 0)
    for boundary in bounds:
        bucket = bucket + jnp.where(distance >= boundary, 1, 0)
    return bucket


def near_kernel(table, near):
    bucket = near_buckets(near.shape[1:])
    for head in range(near.shape[0]):
        values = jnp.zeros(near.shape[1:], f32)
        for bucket_id in range(table.shape[0]):
            values = jnp.where(bucket == bucket_id, table[bucket_id, head], values)
        near[head] = values


def bucket_kernel(layers, *refs):
    nears, fars, out = refs[:layers], refs[layers : 2 * layers], refs[-1]
    bucket = near_buckets(nears[0].shape[1:])
    rows = lax.broadcasted_iota(jnp.int32, out.shape, 0)
    lanes = lax.broadcasted_iota(jnp.int32, out.shape, 1)
    total = jnp.zeros(out.shape, f32)
    for head in range(nears[0].shape[0]):
        strip = sum(near[head] for near in nears)
        for bucket_id in range(out.shape[0]):
            value = jnp.sum(jnp.where(bucket == bucket_id, strip, 0.0), axis=0, keepdims=True)
            value = jnp.sum(value, axis=1, keepdims=True)
            if bucket_id in (15, 31):
                value = value + sum(far[head, bucket_id // 16, :1, :1] for far in fars)
            total = jnp.where((rows == bucket_id) & (lanes == head), value, total)
    out[...] = total


def fill_band(band, table, near, heads_dev, length):
    for head in range(heads_dev):
        band[head, :, : length - tile] = jnp.full((tile, length - tile), table[15, head], f32)
        band[head, :, length - tile : length + 2 * tile] = near[head]
        band[head, :, length + 2 * tile :] = jnp.full(
            (tile, length - 2 * tile), table[31, head], f32
        )


def band_starts(place, at, length):
    return [
        pl.multiple_of(length + (place[block] - place[at]) * tile, tile)
        for block in range(length // tile)
    ]


def attention_kernel(
    heads_dev, length, first, place, table, near, qkv, doc_row, doc_col, out, local, stats, band
):
    step = pl.program_id(0)
    width = heads_dev * head_dim

    @pl.when(step == 0)
    def _():
        fill_band(band, table, near, heads_dev, length)

    row = pl.multiple_of((first[0] + step) * tile, tile)
    out_row = pl.multiple_of((place[first[0] + step] - first[0]) * tile, tile)
    starts = band_starts(place, first[0] + step, length)
    same_doc = doc_col[...] == doc_row[...]
    queries = qkv[pl.ds(row, tile), :width] * bf16(score_scale)
    lanes = lax.broadcasted_iota(jnp.int32, (tile, tile), 1)
    collected = jnp.zeros((tile, tile), f32)
    for head in range(heads_dev):
        own = slice(head * head_dim, (head + 1) * head_dim)
        keys = qkv[:, width + own.start : width + own.stop]
        values = qkv[:, 2 * width + own.start : 2 * width + own.stop]
        scores = contract(queries[:, own], keys, 1, 1)
        scores = scores + jnp.concatenate(
            [band[head, :, pl.ds(start, tile)] for start in starts], axis=1
        )
        scores = jnp.where(same_doc, scores, masked)
        peak = jnp.max(scores, axis=1, keepdims=True)
        weights = jnp.exp(scores - peak)
        total = jnp.sum(weights, axis=1, keepdims=True)
        mixed = contract(weights.astype(bf16), values, 1, 0) / total
        out[pl.ds(out_row, tile), own] = mixed.astype(bf16)
        local[:, own] = mixed.astype(bf16)
        collected = jnp.where(lanes == head, peak + jnp.log(total), collected)
    stats[...] = collected


def attention_back_kernel(
    heads_dev, length, split, first, place, table, near, qkv, doc_row, doc_col, attended, grad_out, stats,
    grad_qkv, grad_near, grad_far, band, grad_band, grad_keys, grad_values,
):
    step = pl.program_id(0)
    width = heads_dev * head_dim

    @pl.when(step == 0)
    def _():
        fill_band(band, table, near, heads_dev, length)
        grad_band[...] = jnp.zeros_like(grad_band)
        grad_keys[...] = jnp.zeros_like(grad_keys)
        grad_values[...] = jnp.zeros_like(grad_values)
        if split > 1:
            grad_qkv[...] = jnp.zeros_like(grad_qkv)

    row = pl.multiple_of((first[0] + step) * tile, tile)
    out_row = pl.multiple_of((place[first[0] + step] - first[0]) * tile, tile)
    starts = band_starts(place, first[0] + step, length)
    same_doc = doc_col[...] == doc_row[...]
    at_step = pl.multiple_of(step * tile, tile)
    queries = qkv[pl.ds(row, tile), :width] * bf16(score_scale)
    for head in range(heads_dev):
        own = slice(head * head_dim, (head + 1) * head_dim)
        keys = qkv[:, width + own.start : width + own.stop]
        values = qkv[:, 2 * width + own.start : 2 * width + own.stop]
        upstream = grad_out[pl.ds(out_row, tile), own]
        scores = contract(queries[:, own], keys, 1, 1) + jnp.concatenate(
            [band[head, :, pl.ds(start, tile)] for start in starts], axis=1
        )
        scores = jnp.where(same_doc, scores, masked)
        weights = jnp.exp(scores - stats[:, head : head + 1])
        delta = jnp.sum(
            upstream.astype(f32) * attended[pl.ds(at_step, tile), own].astype(f32),
            axis=1,
            keepdims=True,
        )
        grad_scores = weights * (contract(upstream, values, 1, 1) - delta)
        for block, start in enumerate(starts):
            grad_band[head, :, pl.ds(start, tile)] += grad_scores[
                :, block * tile : (block + 1) * tile
            ]
        grad_low = grad_scores.astype(bf16)
        grad_values[:, own] += contract(weights.astype(bf16), upstream, 0, 0)
        grad_keys[:, own] += contract(grad_low, queries[:, own], 0, 0)
        grad_qkv[pl.ds(row, tile), own] = (
            contract(grad_low, keys, 1, 0) * score_scale
        ).astype(bf16)

    @pl.when(step == pl.num_programs(0) - 1)
    def _():
        grad_qkv[:, width : 2 * width] = grad_keys[...].astype(bf16)
        grad_qkv[:, 2 * width :] = grad_values[...].astype(bf16)
        for head in range(heads_dev):
            grad_near[head] = grad_band[head, :, length - tile : length + 2 * tile]
            grad_far[head, 0] = jnp.full(
                (8, tile), jnp.sum(grad_band[head, :, : length - tile]), f32
            )
            grad_far[head, 1] = jnp.full(
                (8, tile), jnp.sum(grad_band[head, :, length + 2 * tile :]), f32
            )


def whole(shape):
    return pl.BlockSpec(shape, lambda step: (0,) * len(shape))


def attention(qkv, doc_row, doc_col, first, place, table, near, rows):
    length = qkv.shape[0]
    heads_dev = table.shape[1]
    width = heads_dev * head_dim
    return pl.pallas_call(
        functools.partial(attention_kernel, heads_dev, length),
        grid=(rows // tile,),
        in_specs=[
            pl.BlockSpec(memory_space=pltpu.SMEM),
            pl.BlockSpec(memory_space=pltpu.SMEM),
            pl.BlockSpec(memory_space=pltpu.SMEM),
            whole(near.shape),
            whole(qkv.shape),
            whole(doc_row.shape),
            pl.BlockSpec((tile, 1), lambda step: (step, 0)),
        ],
        out_specs=[
            whole((rows, width)),
            pl.BlockSpec((tile, width), lambda step: (step, 0)),
            pl.BlockSpec((tile, tile), lambda step: (step, 0)),
        ],
        out_shape=[
            jax.ShapeDtypeStruct((rows, width), bf16),
            jax.ShapeDtypeStruct((rows, width), bf16),
            jax.ShapeDtypeStruct((rows, tile), f32),
        ],
        scratch_shapes=[pltpu.VMEM((heads_dev, tile, 2 * length), f32)],
        compiler_params=pltpu.CompilerParams(vmem_limit_bytes=40 * 2**20),
        cost_estimate=pl.CostEstimate(
            flops=4 * rows * length * width,
            bytes_accessed=4 * length * width * 2,
            transcendentals=rows * length * heads_dev,
        ),
    )(first, place, table, near, qkv, doc_row, doc_col)


def attention_back(
    qkv, doc_row, doc_col, attended, grad_out, stats, first, place, table, near, split
):
    length = qkv.shape[0]
    rows = grad_out.shape[0]
    heads_dev = table.shape[1]
    width = heads_dev * head_dim
    return pl.pallas_call(
        functools.partial(attention_back_kernel, heads_dev, length, split),
        grid=(rows // tile,),
        in_specs=[
            pl.BlockSpec(memory_space=pltpu.SMEM),
            pl.BlockSpec(memory_space=pltpu.SMEM),
            pl.BlockSpec(memory_space=pltpu.SMEM),
            whole(near.shape),
            whole(qkv.shape),
            whole(doc_row.shape),
            pl.BlockSpec((tile, 1), lambda step: (step, 0)),
            whole((rows, width)),
            whole((rows, width)),
            pl.BlockSpec((tile, tile), lambda step: (step, 0)),
        ],
        out_specs=[
            whole((length, 3 * width)),
            whole((heads_dev, tile, 3 * tile)),
            whole((heads_dev, 2, 8, tile)),
        ],
        out_shape=[
            jax.ShapeDtypeStruct((length, 3 * width), bf16),
            jax.ShapeDtypeStruct((heads_dev, tile, 3 * tile), f32),
            jax.ShapeDtypeStruct((heads_dev, 2, 8, tile), f32),
        ],
        scratch_shapes=[
            pltpu.VMEM((heads_dev, tile, 2 * length), f32),
            pltpu.VMEM((heads_dev, tile, 2 * length), f32),
            pltpu.VMEM((length, width), f32),
            pltpu.VMEM((length, width), f32),
        ],
        compiler_params=pltpu.CompilerParams(vmem_limit_bytes=48 * 2**20),
        cost_estimate=pl.CostEstimate(
            flops=10 * rows * length * width,
            bytes_accessed=8 * length * width * 2,
            transcendentals=rows * length * heads_dev,
        ),
    )(first, place, table, near, qkv, doc_row, doc_col, attended, grad_out, stats)


def call(kernel, shapes, *operands, smem=0):
    return pl.pallas_call(
        kernel,
        in_specs=[pl.BlockSpec(memory_space=pltpu.SMEM)] * smem
        + [pl.BlockSpec(memory_space=pltpu.VMEM)] * (len(operands) - smem),
        out_specs=[pl.BlockSpec(memory_space=pltpu.VMEM)] * len(shapes),
        out_shape=[jax.ShapeDtypeStruct(shape, kind) for shape, kind in shapes],
        compiler_params=pltpu.CompilerParams(vmem_limit_bytes=32 * 2**20),
    )(*operands)


def share_in_kernel(layers, members, copies, core_n, attn_in, gains, *outs):
    width = attn_in.shape[2] // (3 * members)
    for layer_id in range(layers):
        for member in range(members):
            block = jnp.concatenate(
                [
                    attn_in[layer_id, :, (part * members + member) * width :][:, :width]
                    for part in range(3)
                ],
                axis=1,
            )
            block = (block.astype(f32) * gains[layer_id]).astype(bf16)
            for copy in range(copies):
                target = (member // core_n * copies + copy) * core_n + member % core_n
                outs[layer_id][target] = block


def plane_attention_kernel(
    length, place, table, strip, near, far, w_in, w_out, doc_row, doc_col,
    qkv, attended, stats, near_part, far_part, band,
):
    step = pl.program_id(0)
    half = length // 2
    heads_dev = table.shape[1]
    width = heads_dev * head_dim

    @pl.when(step == 0)
    def _():
        fill_band(band, table, strip, heads_dev, length)
        qkv[:half] = contract(near[...], w_in[...], 1, 0).astype(bf16)
        qkv[half:] = contract(far[...], w_in[...], 1, 0).astype(bf16)

    row = pl.multiple_of(step * tile, tile)
    starts = band_starts(place, step, length)
    same_doc = doc_col[...] == doc_row[...]
    queries = qkv[pl.ds(row, tile), :width] * bf16(score_scale)
    lanes = lax.broadcasted_iota(jnp.int32, (tile, tile), 1)
    collected = jnp.zeros((tile, tile), f32)
    results = []
    for head in range(heads_dev):
        own = slice(head * head_dim, (head + 1) * head_dim)
        keys = qkv[:, width + own.start : width + own.stop]
        values = qkv[:, 2 * width + own.start : 2 * width + own.stop]
        scores = contract(queries[:, own], keys, 1, 1) + jnp.concatenate(
            [band[head, :, pl.ds(start, tile)] for start in starts], axis=1
        )
        scores = jnp.where(same_doc, scores, masked)
        peak = jnp.max(scores, axis=1, keepdims=True)
        weights = jnp.exp(scores - peak)
        total = jnp.sum(weights, axis=1, keepdims=True)
        results.append((contract(weights.astype(bf16), values, 1, 0) / total).astype(bf16))
        collected = jnp.where(lanes == head, peak + jnp.log(total), collected)
    stats[...] = collected
    merged = jnp.concatenate(results, axis=1)
    attended[...] = merged
    part = contract(merged, w_out[...], 1, 0)

    @pl.when(row < half)
    def _():
        near_part[...] = part

    @pl.when(row >= half)
    def _():
        far_part[...] = part.astype(bf16)


def near_block(steps, columns):
    return pl.BlockSpec((tile, columns), lambda step: (jnp.minimum(step, steps // 2 - 1), 0))


def far_block(steps, columns):
    return pl.BlockSpec((tile, columns), lambda step: (jnp.maximum(step - steps // 2, 0), 0))


def plane_attention(near, far, w_in, w_out, doc_row, doc_col, place, table, strip):
    length, model_width = 2 * near.shape[0], near.shape[1]
    steps = length // tile
    heads_dev = table.shape[1]
    width = heads_dev * head_dim
    return pl.pallas_call(
        functools.partial(plane_attention_kernel, length),
        grid=(steps,),
        in_specs=[
            pl.BlockSpec(memory_space=pltpu.SMEM),
            pl.BlockSpec(memory_space=pltpu.SMEM),
            whole(strip.shape),
            whole(near.shape),
            whole(far.shape),
            whole(w_in.shape),
            whole(w_out.shape),
            whole(doc_row.shape),
            pl.BlockSpec((tile, 1), lambda step: (step, 0)),
        ],
        out_specs=[
            whole((length, 3 * width)),
            pl.BlockSpec((tile, width), lambda step: (step, 0)),
            pl.BlockSpec((tile, tile), lambda step: (step, 0)),
            near_block(steps, model_width),
            far_block(steps, model_width),
        ],
        out_shape=[
            jax.ShapeDtypeStruct((length, 3 * width), bf16),
            jax.ShapeDtypeStruct((length, width), bf16),
            jax.ShapeDtypeStruct((length, tile), f32),
            jax.ShapeDtypeStruct((length // 2, model_width), f32),
            jax.ShapeDtypeStruct((length // 2, model_width), bf16),
        ],
        scratch_shapes=[pltpu.VMEM((heads_dev, tile, 2 * length), f32)],
        compiler_params=pltpu.CompilerParams(vmem_limit_bytes=40 * 2**20),
        cost_estimate=pl.CostEstimate(
            flops=4 * length * length * width + 8 * length * model_width * width,
            bytes_accessed=12 * 2**20,
            transcendentals=length * length * heads_dev,
        ),
    )(place, table, strip, near, far, w_in, w_out, doc_row, doc_col)


def plane_attention_back_kernel(
    length, place, table, strip, qkv, doc_row, doc_col, attended, stats, near, far, w_in, w_out,
    grad_qkv, grad_near, grad_far, near_part, far_part, *rest
):
    quarters, (band, grad_band, grad_keys, grad_values, out_sum) = rest[:4], rest[4:]
    step = pl.program_id(0)
    half = length // 2
    heads_dev = table.shape[1]
    width = heads_dev * head_dim

    @pl.when(step == 0)
    def _():
        fill_band(band, table, strip, heads_dev, length)
        grad_band[...] = jnp.zeros_like(grad_band)
        grad_keys[...] = jnp.zeros_like(grad_keys)
        grad_values[...] = jnp.zeros_like(grad_values)
        out_sum[...] = jnp.zeros_like(out_sum)

    row = pl.multiple_of(step * tile, tile)
    starts = band_starts(place, step, length)
    same_doc = doc_col[...] == doc_row[...]
    branch = jnp.where(row < half, near[...], far[...])
    merged = attended[...]
    grad_merged = contract(branch, w_out[...], 1, 1).astype(bf16)
    out_sum[...] += contract(merged, branch, 0, 0)
    products = grad_merged.astype(f32) * merged.astype(f32)
    queries = qkv[pl.ds(row, tile), :width] * bf16(score_scale)
    for head in range(heads_dev):
        own = slice(head * head_dim, (head + 1) * head_dim)
        keys = qkv[:, width + own.start : width + own.stop]
        values = qkv[:, 2 * width + own.start : 2 * width + own.stop]
        upstream = grad_merged[:, own]
        scores = contract(queries[:, own], keys, 1, 1) + jnp.concatenate(
            [band[head, :, pl.ds(start, tile)] for start in starts], axis=1
        )
        scores = jnp.where(same_doc, scores, masked)
        weights = jnp.exp(scores - stats[:, head : head + 1])
        delta = jnp.sum(products[:, own], axis=1, keepdims=True)
        grad_scores = weights * (contract(upstream, values, 1, 1) - delta)
        for block, start in enumerate(starts):
            grad_band[head, :, pl.ds(start, tile)] += grad_scores[
                :, block * tile : (block + 1) * tile
            ]
        grad_low = grad_scores.astype(bf16)
        grad_values[:, own] += contract(weights.astype(bf16), upstream, 0, 0)
        grad_keys[:, own] += contract(grad_low, queries[:, own], 0, 0)
        grad_qkv[pl.ds(row, tile), own] = (
            contract(grad_low, keys, 1, 0) * score_scale
        ).astype(bf16)

    @pl.when(step == pl.num_programs(0) - 1)
    def _():
        grad_qkv[:, width : 2 * width] = grad_keys[...].astype(bf16)
        grad_qkv[:, 2 * width :] = grad_values[...].astype(bf16)
        far_part[...] = contract(grad_qkv[half:], w_in[...], 1, 1).astype(bf16)
        near_part[...] = contract(grad_qkv[:half], w_in[...], 1, 1)
        at_z = place[length // tile]
        rows = width // 4
        for index, quarter in enumerate(quarters):
            block = (index // 2 ^ at_z % 2) * 2 + (index % 2 ^ at_z // 2)
            quarter[...] = out_sum[pl.ds(pl.multiple_of(block * rows, rows), rows)].astype(bf16)
        for head in range(heads_dev):
            grad_near[head] = grad_band[head, :, length - tile : length + 2 * tile]
            grad_far[head, 0] = jnp.full(
                (8, tile), jnp.sum(grad_band[head, :, : length - tile]), f32
            )
            grad_far[head, 1] = jnp.full(
                (8, tile), jnp.sum(grad_band[head, :, length + 2 * tile :]), f32
            )


def plane_attention_back(
    qkv, doc_row, doc_col, attended, stats, near, far, w_in, w_out, place, table, strip
):
    length, model_width = 2 * near.shape[0], near.shape[1]
    steps = length // tile
    heads_dev = table.shape[1]
    width = heads_dev * head_dim
    shapes = [
        ((length, 3 * width), bf16),
        ((heads_dev, tile, 3 * tile), f32),
        ((heads_dev, 2, 8, tile), f32),
        ((length // 2, model_width), f32),
        ((length // 2, model_width), bf16),
    ] + [((width // 4, model_width), bf16)] * 4
    return pl.pallas_call(
        functools.partial(plane_attention_back_kernel, length),
        grid=(steps,),
        in_specs=[
            pl.BlockSpec(memory_space=pltpu.SMEM),
            pl.BlockSpec(memory_space=pltpu.SMEM),
            whole(strip.shape),
            whole(qkv.shape),
            whole(doc_row.shape),
            pl.BlockSpec((tile, 1), lambda step: (step, 0)),
            pl.BlockSpec((tile, width), lambda step: (step, 0)),
            pl.BlockSpec((tile, tile), lambda step: (step, 0)),
            near_block(steps, model_width),
            far_block(steps, model_width),
            whole(w_in.shape),
            whole(w_out.shape),
        ],
        out_specs=[whole(shape) for shape, _ in shapes],
        out_shape=[jax.ShapeDtypeStruct(shape, kind) for shape, kind in shapes],
        scratch_shapes=[
            pltpu.VMEM((heads_dev, tile, 2 * length), f32),
            pltpu.VMEM((heads_dev, tile, 2 * length), f32),
            pltpu.VMEM((length, width), f32),
            pltpu.VMEM((length, width), f32),
            pltpu.VMEM((width, model_width), f32),
        ],
        compiler_params=pltpu.CompilerParams(vmem_limit_bytes=48 * 2**20),
        cost_estimate=pl.CostEstimate(
            flops=10 * length * length * width + 10 * length * model_width * width,
            bytes_accessed=12 * 2**20,
            transcendentals=length * length * heads_dev,
        ),
    )(place, table, strip, qkv, doc_row, doc_col, attended, stats, near, far, w_in, w_out)


def gelu_and_slope(pre_act):
    size = jnp.abs(pre_act)
    gauss = jnp.exp(-0.5 * pre_act * pre_act)
    ratio = 1.0 / (1.0 + np.float32(0.3275911 * 0.5**0.5) * size)
    series = np.float32(1.061405429)
    for factor in (-1.453152027, 1.421413741, -0.284496736, 0.254829592):
        series = series * ratio + np.float32(factor)
    tail = 0.5 * series * ratio * gauss
    cumulative = jnp.where(pre_act < 0, tail, 1.0 - tail)
    slope = cumulative + pre_act * gauss * np.float32((2 * np.pi) ** -0.5)
    return pre_act * cumulative, slope


def ff_kernel(rows, pair, activated, slope, part):
    columns = rows.shape[1]
    value, gradient = gelu_and_slope(contract(rows[...], pair[:, :columns], 1, 1))
    activated[...] = value.astype(bf16)
    slope[...] = gradient.astype(bf16)
    part[...] = contract(activated[...], pair[:, columns:], 1, 0).astype(part.dtype)


def ff_back_kernel(rows, slope, pair, grad_pre, part):
    columns = rows.shape[1]
    grad_act = contract(rows[...], pair[:, columns:], 1, 1)
    grad_pre[...] = (grad_act * slope[...].astype(f32)).astype(bf16)
    part[...] = contract(grad_pre[...], pair[:, :columns], 1, 0).astype(part.dtype)


def by_rows(kernel, step_rows, row_operands, whole_operands, outs):
    rows = row_operands[0].shape[0]
    return pl.pallas_call(
        kernel,
        grid=(rows // step_rows,),
        in_specs=[
            pl.BlockSpec((step_rows, operand.shape[1]), lambda step: (step, 0))
            for operand in row_operands
        ]
        + [whole(operand.shape) for operand in whole_operands],
        out_specs=[pl.BlockSpec((step_rows, columns), lambda step: (step, 0)) for columns, _ in outs],
        out_shape=[jax.ShapeDtypeStruct((rows, columns), kind) for columns, kind in outs],
        compiler_params=pltpu.CompilerParams(vmem_limit_bytes=32 * 2**20),
        cost_estimate=pl.CostEstimate(
            flops=4 * rows * whole_operands[0].shape[0] * whole_operands[0].shape[1],
            bytes_accessed=6 * 2**20,
            transcendentals=0,
        ),
    )(*row_operands, *whole_operands)


def ff_grads_kernel(
    pre_near, pre_far, act_near, act_far, normed_near, normed_far, low_near, low_far, *outs
):
    columns = normed_near.shape[1]
    rows = outs[0].shape[0]
    up = (
        contract(pre_near[...], normed_near[...], 0, 0)
        + contract(pre_far[...], normed_far[...], 0, 0)
    ).astype(bf16)
    down = (
        contract(act_near[...], low_near[...], 0, 0) + contract(act_far[...], low_far[...], 0, 0)
    ).astype(bf16)
    for index, out in enumerate(outs):

        @pl.when(pl.program_id(0) == index // 2)
        def _():
            block = slice(index % 2 * rows, (index % 2 + 1) * rows)
            out[:, :columns] = up[block]
            out[:, columns:] = down[block]


def ff_grads(pre, act, normed, low):
    rows, hidden_units = pre[0].shape
    columns = normed[0].shape[1]
    step_units = hidden_units // 2
    shape = (hidden_units // 4, 2 * columns)
    return pl.pallas_call(
        ff_grads_kernel,
        grid=(2,),
        in_specs=[pl.BlockSpec((rows, step_units), lambda step: (0, step))] * 4
        + [whole((rows, columns))] * 4,
        out_specs=[whole(shape)] * 4,
        out_shape=[jax.ShapeDtypeStruct(shape, bf16)] * 4,
        compiler_params=pltpu.CompilerParams(vmem_limit_bytes=40 * 2**20),
        cost_estimate=pl.CostEstimate(
            flops=8 * rows * hidden_units * columns, bytes_accessed=8 * 2**20, transcendentals=0
        ),
    )(*pre, *act, *normed, *low)


def in_grads_kernel(near, far, grad_qkv, out):
    half = near.shape[0]
    out[...] = (
        contract(near[...], grad_qkv[:half], 0, 0) + contract(far[...], grad_qkv[half:], 0, 0)
    ).astype(bf16)


def in_grads(near, far, grad_qkv):
    rows, columns = near.shape
    step_columns = 256
    return pl.pallas_call(
        in_grads_kernel,
        grid=(columns // step_columns,),
        in_specs=[pl.BlockSpec((rows, step_columns), lambda step: (0, step))] * 2
        + [whole(grad_qkv.shape)],
        out_specs=pl.BlockSpec((step_columns, grad_qkv.shape[1]), lambda step: (step, 0)),
        out_shape=jax.ShapeDtypeStruct((columns, grad_qkv.shape[1]), bf16),
        compiler_params=pltpu.CompilerParams(vmem_limit_bytes=32 * 2**20),
        cost_estimate=pl.CostEstimate(
            flops=4 * rows * columns * grad_qkv.shape[1],
            bytes_accessed=4 * 2**20,
            transcendentals=0,
        ),
    )(near, far, grad_qkv)


def combine_kernel(near_part, arrived, own, x_part, y_part, xy_part):
    rows = own.shape[0]
    own[...] = near_part[:rows] + arrived[:rows].astype(f32)
    for bits, out in ((1, x_part), (2, y_part), (3, xy_part)):
        block = slice(bits * rows, (bits + 1) * rows)
        out[...] = (near_part[block] + arrived[block].astype(f32)).astype(bf16)


def added(own, x_part, y_part, xy_part):
    return (own[...] + x_part[...].astype(f32)) + (
        y_part[...].astype(f32) + xy_part[...].astype(f32)
    )


def close_kernel(kept, own, x_part, y_part, xy_part, hidden, units):
    total = kept[...] + added(own, x_part, y_part, xy_part)
    hidden[...] = total
    units[...] = (total * inverse_rms(total)).astype(bf16)


def close_gain_kernel(kept, own, x_part, y_part, xy_part, gain, hidden, normed):
    total = kept[...] + added(own, x_part, y_part, xy_part)
    hidden[...] = total
    normed[...] = (total * inverse_rms(total) * gain[...]).astype(bf16)


def last_kernel(kept, own, x_part, y_part, xy_part, hidden):
    hidden[...] = (kept[...] + added(own, x_part, y_part, xy_part)).astype(bf16)


def middle_back_kernel(
    upstream, own, x_part, y_part, xy_part, middle, gain, grad_middle, branch, grad_gain
):
    grad_normed = added(own, x_part, y_part, xy_part)
    inverse = inverse_rms(middle[...])
    grad_gain[...] = jnp.sum(grad_normed * middle[...] * inverse, axis=0, keepdims=True)
    total = upstream[...].astype(f32) + unit_norm_back(
        middle[...], inverse, grad_normed * gain[...]
    )
    grad_middle[...] = total
    branch[...] = total.astype(bf16)


def layer_back_kernel(grad_middle, own, x_part, y_part, xy_part, hidden, upstream, low):
    total = grad_middle[...] + unit_norm_back(
        hidden[...], inverse_rms(hidden[...]), added(own, x_part, y_part, xy_part)
    )
    upstream[...] = total
    low[...] = total.astype(bf16)


def finish_in_kernel(layers, groups, copies, *refs):
    shares, (attn_in, gains), (grad_in, grad_gain) = (
        refs[:layers], refs[layers : layers + 2], refs[layers + 2 :],
    )
    members = groups * 2
    width = attn_in.shape[2] // (3 * members)
    for layer_id in range(layers):
        row_dot = jnp.zeros(grad_gain.shape[1:], f32)
        for member in range(members):
            total = 0.0
            for copy in range(copies):
                source = (member // 2 * copies + copy) * 2 + member % 2
                total = total + shares[layer_id][source].astype(f32)
            for part in range(3):
                columns = slice((part * members + member) * width, (part * members + member + 1) * width)
                block = total[:, part * width : (part + 1) * width]
                grad_in[layer_id, :, columns] = block * gains[layer_id]
                row_dot = row_dot + jnp.sum(
                    block * attn_in[layer_id, :, columns].astype(f32), axis=1, keepdims=True
                )
        grad_gain[layer_id] = row_dot


def sum_of_four(parts):
    return (parts[0][...].astype(f32) + parts[1][...].astype(f32)) + (
        parts[2][...].astype(f32) + parts[3][...].astype(f32)
    )


def finish_ff_kernel(*refs):
    grad_up, grad_down = refs[-2:]
    columns = grad_up.shape[2]
    for layer_id in range(grad_up.shape[0]):
        total = sum_of_four(refs[4 * layer_id : 4 * layer_id + 4])
        grad_up[layer_id] = total[:, :columns]
        grad_down[layer_id] = total[:, columns:]


def finish_out_kernel(*refs):
    for layer_id in range(refs[-1].shape[0]):
        refs[-1][layer_id] = sum_of_four(refs[4 * layer_id : 4 * layer_id + 4])


def inverse_rms(hidden):
    return lax.rsqrt(jnp.mean(hidden * hidden, axis=-1, keepdims=True) + epsilon)


def prepare(bias_table, first_head, heads_dev):
    table = lax.dynamic_slice_in_dim(bias_table, first_head, heads_dev, 1)
    (near,) = call(near_kernel, [((heads_dev, tile, 3 * tile), f32)], table, smem=1)
    return table, near


def bucket_grads(grads, bucket_count):
    heads_dev = grads[0][0].shape[0]
    (total,) = call(
        functools.partial(bucket_kernel, len(grads)),
        [((bucket_count, tile), f32)],
        *(entry[0] for entry in grads),
        *(entry[1] for entry in grads),
    )
    return total[:, :heads_dev]


def gelu_parts(pre_act):
    cumulative = 0.5 * (1.0 + lax.erf(pre_act * np.float32(0.5**0.5)))
    slope = cumulative + pre_act * jnp.exp(-0.5 * pre_act * pre_act) * np.float32(
        (2 * np.pi) ** -0.5
    )
    return (pre_act * cumulative).astype(bf16), slope


def unit_norm_back(hidden, inverse, grad_unit):
    unit = hidden * inverse
    return inverse * (grad_unit - unit * jnp.mean(grad_unit * unit, axis=-1, keepdims=True))


def gather_rows(block, axes):
    return lax.all_gather(block, axes, axis=0, tiled=True)


def toggle(array, axis, bits):
    return lax.ppermute(array, axis, [(i, i ^ bits) for i in range(lax.axis_size(axis))])


def shift(array, by):
    planes = lax.axis_size("z")
    return lax.ppermute(array, "z", [(i, (i + by) % planes) for i in range(planes)])


def plane_gather(block, *holds):
    near = jnp.concatenate([block] + [toggle(block, "head", bits) for bits in (1, 2, 3)])
    near, *holds = tie(near, *holds)
    return (near, toggle(near, "core", 1), *holds)


def plane_scatter(near_part, far_part):
    rows, columns = near_part.shape[0] // 4, near_part.shape[1]
    own, *others = call(
        combine_kernel,
        [((rows, columns), f32)] + [((rows, columns), bf16)] * 3,
        near_part,
        toggle(far_part, "core", 1),
    )
    return [own] + [toggle(other, "head", bits) for bits, other in zip((1, 2, 3), others)]


def tie(*arrays):
    return lax.optimization_barrier(arrays)


def after(array, other):
    return lax.optimization_barrier((array, other))[0]


def scatter_sum(partial, axes, members):
    blocks = partial.astype(bf16).reshape(members, -1, partial.shape[1])
    return jnp.sum(lax.all_to_all(blocks, axes, 0, 0, tiled=True).astype(f32), axis=0)


def local_general(tokens, doc_start, bias_table, attn_in, attn_out, ff_in, ff_out, gains, cotangent):
    heads_n, z_n, core_n = (lax.axis_size(axis) for axis in everyone)
    devices = heads_n * z_n * core_n
    group, spare = ("z", "core"), "head"
    ff_group, ff_spare, ff_members = ("head", "core"), "z", heads_n * core_n
    blocks = z_n * core_n
    block_rows, model_width = tokens.shape[1:]
    layer_count, weight_rows = attn_in.shape[:2]
    length = block_rows * blocks
    heads_all = bias_table.shape[1]
    member = lax.axis_index("z") * core_n + lax.axis_index("core")
    heads_dev = max(1, heads_all // blocks)
    head_groups = heads_all // heads_dev
    split = blocks // head_groups
    head_group, query_part = member // split, member % split
    query_rows = length // split
    width = heads_dev * head_dim
    first = (query_part * (query_rows // tile)).astype(jnp.int32).reshape(1)
    place = jnp.arange(length // tile, dtype=jnp.int32)
    out_row = head_group * width

    def swap(array):
        return lax.all_to_all(array, everyone, 0, 0, tiled=True)

    starts = jnp.broadcast_to(
        doc_start.astype(f32)[:, None], (heads_n, blocks, block_rows)
    ).reshape(devices, block_rows)
    ff_gains = gains[:, :, 1].astype(f32).reshape(1, -1)
    small = swap(
        jnp.concatenate(
            [starts, jnp.broadcast_to(ff_gains, (devices, layer_count * weight_rows))], axis=1
        )
    )
    doc_row = small[:blocks, :block_rows].reshape(1, length)
    doc_col = lax.dynamic_slice_in_dim(
        doc_row.reshape(length, 1), query_part * query_rows, query_rows, 0
    )
    gain_ff = jnp.transpose(
        small[:, block_rows:].reshape(devices, layer_count, weight_rows), (1, 0, 2)
    ).reshape(layer_count, 1, model_width)
    table, near = prepare(bias_table, head_group * heads_dev, heads_dev)

    gain_attn = gains[:, :, 0].astype(f32)[:, :, None]
    own_in = attn_in.astype(f32)

    def fetch_in(layer_id):
        scaled = (own_in[layer_id] * gain_attn[layer_id]).astype(bf16)
        columns = jnp.transpose(
            scaled.reshape(weight_rows, 3, head_groups, width), (2, 0, 1, 3)
        ).reshape(head_groups, weight_rows, 3 * width)
        columns = jnp.repeat(columns, split, axis=0)
        columns = jnp.broadcast_to(columns[None], (heads_n, *columns.shape))
        return swap(columns.reshape(devices, weight_rows, 3 * width)).reshape(
            model_width, 3 * width
        )

    def fetch_ff(layer_id):
        pair = jnp.concatenate([ff_in[layer_id], ff_out[layer_id]], axis=1)
        pair = gather_rows(pair, ff_spare)
        return pair[:, :model_width], pair[:, model_width:]

    hidden, upstream = tokens[0].astype(f32), cotangent[0]
    weights_in = [fetch_in(layer_id) for layer_id in range(layer_count)]
    weights_out = lax.dynamic_slice_in_dim(
        lax.all_gather(attn_out, everyone, axis=1, tiled=True), out_row, width, 1
    )
    weights_ff = [fetch_ff(layer_id) for layer_id in range(layer_count)]

    records = []
    for layer_id in range(layer_count):
        w_in, w_out, (w_up, w_down) = (
            weights_in[layer_id], weights_out[layer_id], weights_ff[layer_id],
        )
        inverse = inverse_rms(hidden)
        units = gather_rows((hidden * inverse).astype(bf16), group)
        qkv = jnp.dot(units, w_in, preferred_element_type=f32).astype(bf16)
        attended, _, stats = attention(
            qkv, doc_row, doc_col, first, place, table, near, query_rows
        )
        mixed = jnp.dot(attended, w_out, preferred_element_type=f32)
        if split > 1:
            mixed = lax.dynamic_update_slice_in_dim(
                jnp.zeros((length, model_width), f32), mixed, query_part * query_rows, 0
            )
        middle = hidden + scatter_sum(mixed, group, blocks)
        inverse_ff = inverse_rms(middle)
        normed_ff = gather_rows((middle * inverse_ff * gain_ff[layer_id]).astype(bf16), ff_group)
        activated, slope = gelu_parts(contract(normed_ff, w_up, 1, 1))
        ff_result = jnp.dot(activated, w_down, preferred_element_type=f32)
        records.append(
            (hidden, inverse, units, qkv, attended, stats, middle, inverse_ff, normed_ff,
             activated, slope)
        )
        hidden = middle + scatter_sum(ff_result, ff_group, ff_members)
    output = hidden

    grads_ff, grads_in, grads_out, grads_gain_ff, grads_table = (
        [None] * layer_count for _ in range(5)
    )
    for layer_id in reversed(range(layer_count)):
        w_in, w_out, (w_up, w_down) = (
            weights_in[layer_id], weights_out[layer_id], weights_ff[layer_id],
        )
        (hidden, inverse, units, qkv, attended, stats, middle, inverse_ff, normed_ff,
         activated, slope) = records[layer_id]
        grad_low = gather_rows(upstream.astype(bf16), ff_group)
        grad_pre = (contract(grad_low, w_down, 1, 1) * slope).astype(bf16)
        grad_normed = scatter_sum(
            jnp.dot(grad_pre, w_up, preferred_element_type=f32), ff_group, ff_members
        )
        grad_pair = jnp.concatenate(
            [contract(grad_pre, normed_ff, 0, 0), contract(activated, grad_low, 0, 0)], axis=1
        ).astype(bf16)
        grads_ff[layer_id] = lax.psum_scatter(
            grad_pair, ff_spare, scatter_dimension=0, tiled=True
        ).astype(f32)
        grads_gain_ff[layer_id] = jnp.sum(grad_normed * middle * inverse_ff, axis=0)
        grad_middle = upstream + unit_norm_back(
            middle, inverse_ff, grad_normed * gain_ff[layer_id]
        )
        branch = gather_rows(grad_middle.astype(bf16), group)
        if split > 1:
            branch = lax.dynamic_slice_in_dim(branch, query_part * query_rows, query_rows, 0)
        grad_attended = contract(branch, w_out, 1, 1).astype(bf16)
        grad_qkv, grad_near, grad_far = attention_back(
            qkv, doc_row, doc_col, attended, grad_attended, stats, first, place, table, near, split
        )
        grads_table[layer_id] = (grad_near, grad_far)
        grad_units = scatter_sum(contract(grad_qkv, w_in, 1, 1), group, blocks)
        upstream = grad_middle + unit_norm_back(hidden, inverse, grad_units)
        grad_out = lax.dynamic_update_slice_in_dim(
            jnp.zeros((model_width, model_width), bf16),
            contract(attended, branch, 0, 0).astype(bf16),
            out_row,
            0,
        )
        grads_out[layer_id] = lax.psum_scatter(
            grad_out, everyone, scatter_dimension=0, tiled=True
        ).astype(f32)
        grads_in[layer_id] = contract(units, grad_qkv, 0, 0).astype(bf16)

    bucket_count = table.shape[0]
    grad_table = bucket_grads(grads_table, bucket_count)
    grad_table = lax.dynamic_update_slice_in_dim(
        jnp.zeros((bucket_count, heads_all), f32), grad_table, head_group * heads_dev, 1
    )
    grad_table = jnp.transpose(
        grad_table.reshape(blocks, bucket_count // blocks, heads_n, heads_all // heads_n),
        (2, 0, 1, 3),
    ).reshape(devices, -1)
    grad_gain_ff = jnp.transpose(
        jnp.stack(grads_gain_ff).reshape(layer_count, devices, weight_rows), (1, 0, 2)
    ).reshape(devices, -1)
    ends = jnp.sum(swap(jnp.concatenate([grad_gain_ff, grad_table], axis=1)), axis=0)
    grad_gain_ff = ends[: layer_count * weight_rows].reshape(layer_count, weight_rows)
    grad_bias_table = ends[layer_count * weight_rows :].reshape(
        bucket_count // blocks, heads_all // heads_n
    )
    grads_attn_in, grads_gains = [], []
    for layer_id in range(layer_count):
        parts = swap(grads_in[layer_id].reshape(devices, weight_rows, 3 * width)).astype(f32)
        parts = jnp.sum(parts.reshape(heads_n, blocks, weight_rows, 3 * width), axis=0)
        parts = jnp.sum(parts.reshape(head_groups, split, weight_rows, 3, width), axis=1)
        unit_grad = jnp.transpose(parts, (1, 2, 0, 3)).reshape(weight_rows, 3 * model_width)
        grads_attn_in.append(unit_grad * gain_attn[layer_id])
        grads_gains.append(
            jnp.stack(
                [jnp.sum(unit_grad * own_in[layer_id], axis=1), grad_gain_ff[layer_id]], axis=1
            )
        )
    return (
        output[None],
        upstream[None],
        jnp.stack(grads_attn_in),
        jnp.stack(grads_out),
        jnp.stack([entry[:, :model_width] for entry in grads_ff]),
        jnp.stack([entry[:, model_width:] for entry in grads_ff]),
        jnp.stack(grads_gains),
        grad_bias_table,
    )


def local_plane(tokens, doc_start, bias_table, attn_in, attn_out, ff_in, ff_out, gains, cotangent):
    heads_n, z_n, core_n = (lax.axis_size(axis) for axis in everyone)
    devices = heads_n * z_n * core_n
    at_head, at_z, at_core = (lax.axis_index(axis) for axis in everyone)
    members = heads_n * core_n
    block_rows, model_width = tokens.shape[1:]
    layer_count, weight_rows = attn_in.shape[:2]
    length = block_rows * members
    heads_all = bias_table.shape[1]
    heads_dev = heads_all // members
    width = heads_dev * head_dim
    member = at_head * core_n + at_core
    turn = [
        ((h * z_n + z) * core_n + c, (z * z_n + h) * core_n + c)
        for h in range(heads_n)
        for z in range(z_n)
        for c in range(core_n)
    ]
    place = jnp.stack(
        [
            (at_head ^ bits) * core_n + (at_core ^ other)
            for other in range(core_n)
            for bits in range(heads_n)
        ]
        + [at_z]
    ).astype(jnp.int32)

    def relay(array):
        return lax.ppermute(array, everyone, turn)

    def swap(array):
        return lax.all_to_all(array, everyone, 0, 0, tiled=True)

    gain_attn = gains[:, :, 0].astype(f32)[:, :, None]
    shares = call(
        functools.partial(share_in_kernel, layer_count, members, z_n, core_n),
        [((devices, weight_rows, 3 * width), bf16)] * layer_count,
        attn_in,
        gain_attn,
    )
    quarter_turns = [
        [
            (z * core_n + c, (2 * c + (a ^ z % 2)) * core_n + (b ^ z // 2))
            for z in range(z_n)
            for c in range(core_n)
        ]
        for a in range(2)
        for b in range(2)
    ]

    def fetch_out(layer_id, hold):
        held = after(attn_out[layer_id], hold)
        return [
            lax.ppermute(held, ("z", "core"), [(holder, user) for user, holder in turns])
            for turns in quarter_turns
        ]

    def place_out(quarters):
        rows = jnp.stack(quarters).reshape(2, 2, weight_rows, model_width)
        rows = jnp.where(at_z % 2 == 1, jnp.flip(rows, 0), rows)
        rows = jnp.where(at_z // 2 == 1, jnp.flip(rows, 1), rows)
        return rows.reshape(width, model_width)

    hidden, w_in, quarters = tie(
        relay(after(tokens[0], shares[0])), swap(shares[0]), fetch_out(0, shares[0])
    )
    hidden = hidden.astype(f32)
    weights_in = [w_in.reshape(model_width, 3 * width)]
    weights_out = [place_out(quarters)]

    starts = jnp.broadcast_to(
        doc_start.astype(f32)[None, :, None], (heads_n, z_n, core_n, block_rows)
    )
    ff_gains = gains[:, :, 1].astype(f32).reshape(1, -1)
    small = jnp.concatenate(
        [
            starts.reshape(devices, block_rows),
            jnp.broadcast_to(ff_gains, (devices, layer_count * weight_rows)),
        ],
        axis=1,
    )
    small = swap(after(small, hidden))
    doc_row = small[:members, :block_rows].reshape(2, 2, core_n, block_rows)
    for axis, bit in ((0, at_head // 2), (1, at_head % 2), (2, at_core)):
        doc_row = jnp.where(bit == 1, jnp.flip(doc_row, axis), doc_row)
    doc_row = jnp.transpose(doc_row, (2, 0, 1, 3)).reshape(1, length)
    doc_col = doc_row.reshape(length, 1)
    gain_ff = jnp.transpose(
        small[:, block_rows:].reshape(devices, layer_count, weight_rows), (1, 0, 2)
    ).reshape(layer_count, 1, model_width)
    table, strip = prepare(bias_table, member * heads_dev, heads_dev)

    ff_pairs = [
        jnp.concatenate([ff_in[layer_id], ff_out[layer_id]], axis=1) for layer_id in range(layer_count)
    ]

    def ff_halves(layer_id, hold):
        return [shift(after(array[layer_id], hold), 2) for array in (ff_in, ff_out)]

    def ff_pair(layer_id, lower, upper, halves):
        return jnp.concatenate([ff_pairs[layer_id], lower, upper, jnp.concatenate(halves, axis=1)])

    def ff_both(kernel, row_operands, pair, columns):
        return zip(
            *(
                by_rows(
                    kernel,
                    256,
                    operands,
                    [pair],
                    [(pair.shape[0], bf16)] * columns + [(model_width, kind)],
                )
                for operands, kind in zip(zip(*row_operands), (f32, bf16))
            )
        )

    row_shape = (block_rows, model_width)
    records = []
    unit_rows = (hidden * inverse_rms(hidden)).astype(bf16)

    near, far, lower = plane_gather(unit_rows, shift(after(ff_pairs[0], hidden), 1))
    units = (near, far)
    qkv, attended, stats, *parts = plane_attention(
        *units, weights_in[0], weights_out[0], doc_row, doc_col, place, table, strip
    )
    parts, upstream = tie(parts, relay(after(cotangent[0].astype(bf16), far)))
    halves = ff_halves(0, parts[0])
    parts, upper, half = tie(
        plane_scatter(*parts), shift(after(ff_pairs[0], parts[0]), -1), halves[0]
    )
    middle, normed_rows = call(
        close_gain_kernel, [(row_shape, f32), (row_shape, bf16)], hidden, *parts, gain_ff[0]
    )
    near, far, other_half = plane_gather(normed_rows, halves[1])
    normed = (near, far)
    pair = ff_pair(0, lower, upper, [half, other_half])
    weights_ff = [pair]
    acts, slopes, parts = ff_both(ff_kernel, [normed], pair, 2)
    records.append((hidden, units, qkv, attended, stats, middle, normed, acts, slopes))
    parts, lower, w_in = tie(
        plane_scatter(*parts),
        shift(after(ff_pairs[1], parts[0]), 1),
        swap(after(shares[1], parts[0])),
    )
    weights_in.append(w_in.reshape(model_width, 3 * width))
    hidden, unit_rows = call(close_kernel, [(row_shape, f32), (row_shape, bf16)], middle, *parts)

    near, far, upper, quarters = plane_gather(
        unit_rows, shift(after(ff_pairs[1], unit_rows), -1), fetch_out(1, unit_rows)
    )
    units = (near, far)
    weights_out.append(place_out(quarters))
    qkv, attended, stats, *parts = plane_attention(
        *units, weights_in[1], weights_out[1], doc_row, doc_col, place, table, strip
    )
    low = plane_gather(after(upstream, far))
    parts, near_low, halves = tie(parts, low[0], ff_halves(1, far))
    low = (near_low, low[1])
    middle, normed_rows = call(
        close_gain_kernel,
        [(row_shape, f32), (row_shape, bf16)],
        hidden,
        *plane_scatter(*parts),
        gain_ff[1],
    )
    normed = plane_gather(normed_rows)
    pair = ff_pair(1, lower, upper, halves)
    weights_ff.append(pair)
    acts, slopes, last_parts = ff_both(ff_kernel, [normed], pair, 2)
    records.append((hidden, units, qkv, attended, stats, middle, normed, acts, slopes))

    grads_ff, grads_in, grads_out, grads_gain_ff, grads_table = (
        [None] * layer_count for _ in range(5)
    )
    for layer_id in reversed(range(layer_count)):
        last = layer_id + 1 == layer_count
        w_in, w_out, pair = weights_in[layer_id], weights_out[layer_id], weights_ff[layer_id]
        hidden, units, qkv, attended, stats, middle, normed, acts, slopes = records[layer_id]
        if not last:
            near, far, grads_in[1] = plane_gather(low_rows, swap(after(grad_in, low_rows)))
            low = (near, far)
        pres, parts = ff_both(ff_back_kernel, [low, slopes], pair, 1)
        parts, planes = tie(plane_scatter(*parts), ff_grads(pres, acts, normed, low))
        if last:
            last_parts = plane_scatter(*after(last_parts, parts))
        grad_middle, branch_rows, grads_gain_ff[layer_id] = call(
            middle_back_kernel,
            [(row_shape, f32), (row_shape, bf16), ((1, model_width), f32)],
            upstream,
            *parts,
            middle,
            gain_ff[layer_id],
        )
        *branch, lower, upper = plane_gather(
            branch_rows,
            shift(after(planes[1], branch_rows), -1),
            shift(after(planes[2], branch_rows), 1),
        )
        grad_qkv, grad_near, grad_far, near_part, far_part, *quarters = plane_attention_back(
            qkv, doc_row, doc_col, attended, stats, *branch, w_in, w_out, place, table, strip
        )
        opposite = shift(after(planes[3], branch[1] if last else near_part), 2)
        if last:
            near_part, far_part, last_parts, opposite = tie(
                near_part, far_part, last_parts, opposite
            )
        else:
            near_part, far_part, output = tie(near_part, far_part, output)
        parts, grad_in, grads_table[layer_id], quarters, opposite = tie(
            plane_scatter(near_part, far_part),
            in_grads(*units, grad_qkv),
            bucket_grads([(grad_near, grad_far)], table.shape[0]),
            [
                lax.ppermute(quarter, ("z", "core"), turns)
                for quarter, turns in zip(quarters, quarter_turns)
            ],
            opposite,
        )
        grad_in = grad_in.reshape(devices, weight_rows, 3 * width)
        grads_out[layer_id] = quarters
        grads_ff[layer_id] = [planes[0], lower, upper, opposite]
        if last:
            (output,) = call(last_kernel, [(row_shape, bf16)], middle, *last_parts)
            parts, output = tie(parts, output)
        upstream, low_rows = call(
            layer_back_kernel, [(row_shape, f32), (row_shape, bf16)], grad_middle, *parts, hidden
        )
        if last:
            output = relay(after(output, low_rows))
    grad_tokens = [relay(low_rows[part * tile // 2 : (part + 1) * tile // 2]) for part in range(2)]
    grads_in[0] = swap(after(grad_in, grad_tokens[0]))

    bucket_count = table.shape[0]
    grad_table = sum(grads_table)
    grad_table = lax.dynamic_update_slice_in_dim(
        jnp.zeros((bucket_count, heads_all), f32), grad_table, member * heads_dev, 1
    )
    grad_table = jnp.transpose(
        grad_table.reshape(members, bucket_count // members, heads_n, heads_all // heads_n),
        (2, 0, 1, 3),
    ).reshape(devices, -1)
    grad_gain_ff = jnp.transpose(
        jnp.concatenate(grads_gain_ff).reshape(layer_count, devices, weight_rows), (1, 0, 2)
    ).reshape(devices, -1)
    ends = jnp.concatenate([grad_gain_ff, grad_table], axis=1)
    ends = jnp.sum(after(swap(ends), grad_tokens[0]), axis=0)
    grad_gain_ff = ends[: layer_count * weight_rows].reshape(layer_count, weight_rows)
    grad_bias_table = ends[layer_count * weight_rows :].reshape(
        bucket_count // members, heads_all // heads_n
    )
    ff_rows = ff_in.shape[1]
    grad_up, grad_down = call(
        finish_ff_kernel,
        [((layer_count, ff_rows, model_width), f32)] * 2,
        *after(grads_ff[0] + grads_ff[1], grad_tokens[0]),
    )
    (grad_attn_out,) = call(
        finish_out_kernel,
        [(attn_out.shape, f32)],
        *after(grads_out[0] + grads_out[1], grad_tokens[0]),
    )
    grad_attn_in, grad_gain_attn = call(
        functools.partial(finish_in_kernel, layer_count, heads_n, z_n),
        [(attn_in.shape, f32), ((layer_count, weight_rows, 1), f32)],
        *grads_in,
        attn_in,
        gain_attn,
    )
    return (
        output.astype(f32)[None],
        jnp.concatenate(grad_tokens).astype(f32)[None],
        grad_attn_in,
        grad_attn_out,
        grad_up,
        grad_down,
        jnp.concatenate([grad_gain_attn, grad_gain_ff[:, :, None]], axis=2),
        grad_bias_table,
    )


def solution(mesh):
    sizes = dict(mesh.shape)
    cores = 2
    fine = Mesh(
        mesh.devices.reshape(sizes["head"], sizes["blk"] // cores, cores), everyone
    )
    blk = ("z", "core")
    in_specs = (
        P("head", blk, None),
        P(None, blk),
        P(),
        P(None, everyone, None),
        P(None, everyone, None),
        P(None, everyone, None),
        P(None, everyone, None),
        P(None, everyone, None),
        P("head", blk, None),
    )
    out_specs = (
        P("head", blk, None),
        P("head", blk, None),
        P(None, everyone, None),
        P(None, everyone, None),
        P(None, everyone, None),
        P(None, everyone, None),
        P(None, everyone, None),
        P(blk, "head"),
    )
    plane = sizes["head"] == 4 and sizes["blk"] == 8
    local = local_plane if plane else local_general
    return jax.shard_map(local, mesh=fine, in_specs=in_specs, out_specs=out_specs, check_vma=False)
```

```python
import functools

import jax
import jax.numpy as jnp
import numpy as np
from jax import lax
from jax.experimental import pallas as pl
from jax.experimental.pallas import tpu as pltpu
from jax.sharding import Mesh
from jax.sharding import PartitionSpec as P

bounds = (1, 2, 3, 4, 5, 6, 7, 8, 12, 16, 23, 32, 46, 64, 91)
epsilon = 1e-06
masked = -1e30
score_scale = 0.125
head_dim = 64
tile = 128
everyone = ("head", "z", "core")
bf16 = jnp.bfloat16
f32 = jnp.float32


def contract(lhs, rhs, lhs_dim, rhs_dim):
    return lax.dot_general(
        lhs, rhs, (((lhs_dim,), (rhs_dim,)), ((), ())), preferred_element_type=f32
    )


def near_buckets(shape):
    offsets = (
        lax.broadcasted_iota(jnp.int32, shape, 1) - tile - lax.broadcasted_iota(jnp.int32, shape, 0)
    )
    distance = jnp.abs(offsets)
    bucket = jnp.where(offsets > 0, 16, 0)
    for boundary in bounds:
        bucket = bucket + jnp.where(distance >= boundary, 1, 0)
    return bucket


def near_kernel(table, near):
    bucket = near_buckets(near.shape[1:])
    for head in range(near.shape[0]):
        values = jnp.zeros(near.shape[1:], f32)
        for bucket_id in range(table.shape[0]):
            values = jnp.where(bucket == bucket_id, table[bucket_id, head], values)
        near[head] = values


def bucket_kernel(layers, *refs):
    nears, fars, out = refs[:layers], refs[layers : 2 * layers], refs[-1]
    bucket = near_buckets(nears[0].shape[1:])
    rows = lax.broadcasted_iota(jnp.int32, out.shape, 0)
    lanes = lax.broadcasted_iota(jnp.int32, out.shape, 1)
    total = jnp.zeros(out.shape, f32)
    for head in range(nears[0].shape[0]):
        strip = sum(near[head] for near in nears)
        for bucket_id in range(out.shape[0]):
            value = jnp.sum(jnp.where(bucket == bucket_id, strip, 0.0), axis=0, keepdims=True)
            value = jnp.sum(value, axis=1, keepdims=True)
            if bucket_id in (15, 31):
                value = value + sum(far[head, bucket_id // 16, :1, :1] for far in fars)
            total = jnp.where((rows == bucket_id) & (lanes == head), value, total)
    out[...] = total


def fill_band(band, table, near, heads_dev, length):
    for head in range(heads_dev):
        band[head, :, : length - tile] = jnp.full((tile, length - tile), table[15, head], f32)
        band[head, :, length - tile : length + 2 * tile] = near[head]
        band[head, :, length + 2 * tile :] = jnp.full(
            (tile, length - 2 * tile), table[31, head], f32
        )


def band_starts(place, at, length):
    return [
        pl.multiple_of(length + (place[block] - place[at]) * tile, tile)
        for block in range(length // tile)
    ]


def attention_kernel(
    heads_dev, length, first, place, table, near, qkv, doc_row, doc_col, out, local, stats, band
):
    step = pl.program_id(0)
    width = heads_dev * head_dim

    @pl.when(step == 0)
    def _():
        fill_band(band, table, near, heads_dev, length)

    row = pl.multiple_of((first[0] + step) * tile, tile)
    out_row = pl.multiple_of((place[first[0] + step] - first[0]) * tile, tile)
    starts = band_starts(place, first[0] + step, length)
    same_doc = doc_col[...] == doc_row[...]
    queries = qkv[pl.ds(row, tile), :width] * bf16(score_scale)
    lanes = lax.broadcasted_iota(jnp.int32, (tile, tile), 1)
    collected = jnp.zeros((tile, tile), f32)
    for head in range(heads_dev):
        own = slice(head * head_dim, (head + 1) * head_dim)
        keys = qkv[:, width + own.start : width + own.stop]
        values = qkv[:, 2 * width + own.start : 2 * width + own.stop]
        scores = contract(queries[:, own], keys, 1, 1)
        scores = scores + jnp.concatenate(
            [band[head, :, pl.ds(start, tile)] for start in starts], axis=1
        )
        scores = jnp.where(same_doc, scores, masked)
        peak = jnp.max(scores, axis=1, keepdims=True)
        weights = jnp.exp(scores - peak)
        total = jnp.sum(weights, axis=1, keepdims=True)
        mixed = contract(weights.astype(bf16), values, 1, 0) / total
        out[pl.ds(out_row, tile), own] = mixed.astype(bf16)
        local[:, own] = mixed.astype(bf16)
        collected = jnp.where(lanes == head, peak + jnp.log(total), collected)
    stats[...] = collected


def attention_back_kernel(
    heads_dev, length, split, first, place, table, near, qkv, doc_row, doc_col, attended, grad_out, stats,
    grad_qkv, grad_near, grad_far, band, grad_band, grad_keys, grad_values,
):
    step = pl.program_id(0)
    width = heads_dev * head_dim

    @pl.when(step == 0)
    def _():
        fill_band(band, table, near, heads_dev, length)
        grad_band[...] = jnp.zeros_like(grad_band)
        grad_keys[...] = jnp.zeros_like(grad_keys)
        grad_values[...] = jnp.zeros_like(grad_values)
        if split > 1:
            grad_qkv[...] = jnp.zeros_like(grad_qkv)

    row = pl.multiple_of((first[0] + step) * tile, tile)
    out_row = pl.multiple_of((place[first[0] + step] - first[0]) * tile, tile)
    starts = band_starts(place, first[0] + step, length)
    same_doc = doc_col[...] == doc_row[...]
    at_step = pl.multiple_of(step * tile, tile)
    queries = qkv[pl.ds(row, tile), :width] * bf16(score_scale)
    for head in range(heads_dev):
        own = slice(head * head_dim, (head + 1) * head_dim)
        keys = qkv[:, width + own.start : width + own.stop]
        values = qkv[:, 2 * width + own.start : 2 * width + own.stop]
        upstream = grad_out[pl.ds(out_row, tile), own]
        scores = contract(queries[:, own], keys, 1, 1) + jnp.concatenate(
            [band[head, :, pl.ds(start, tile)] for start in starts], axis=1
        )
        scores = jnp.where(same_doc, scores, masked)
        weights = jnp.exp(scores - stats[:, head : head + 1])
        delta = jnp.sum(
            upstream.astype(f32) * attended[pl.ds(at_step, tile), own].astype(f32),
            axis=1,
            keepdims=True,
        )
        grad_scores = weights * (contract(upstream, values, 1, 1) - delta)
        for block, start in enumerate(starts):
            grad_band[head, :, pl.ds(start, tile)] += grad_scores[
                :, block * tile : (block + 1) * tile
            ]
        grad_low = grad_scores.astype(bf16)
        grad_values[:, own] += contract(weights.astype(bf16), upstream, 0, 0)
        grad_keys[:, own] += contract(grad_low, queries[:, own], 0, 0)
        grad_qkv[pl.ds(row, tile), own] = (
            contract(grad_low, keys, 1, 0) * score_scale
        ).astype(bf16)

    @pl.when(step == pl.num_programs(0) - 1)
    def _():
        grad_qkv[:, width : 2 * width] = grad_keys[...].astype(bf16)
        grad_qkv[:, 2 * width :] = grad_values[...].astype(bf16)
        for head in range(heads_dev):
            grad_near[head] = grad_band[head, :, length - tile : length + 2 * tile]
            grad_far[head, 0] = jnp.full(
                (8, tile), jnp.sum(grad_band[head, :, : length - tile]), f32
            )
            grad_far[head, 1] = jnp.full(
                (8, tile), jnp.sum(grad_band[head, :, length + 2 * tile :]), f32
            )


def whole(shape):
    return pl.BlockSpec(shape, lambda step: (0,) * len(shape))


def attention(qkv, doc_row, doc_col, first, place, table, near, rows):
    length = qkv.shape[0]
    heads_dev = table.shape[1]
    width = heads_dev * head_dim
    return pl.pallas_call(
        functools.partial(attention_kernel, heads_dev, length),
        grid=(rows // tile,),
        in_specs=[
            pl.BlockSpec(memory_space=pltpu.SMEM),
            pl.BlockSpec(memory_space=pltpu.SMEM),
            pl.BlockSpec(memory_space=pltpu.SMEM),
            whole(near.shape),
            whole(qkv.shape),
            whole(doc_row.shape),
            pl.BlockSpec((tile, 1), lambda step: (step, 0)),
        ],
        out_specs=[
            whole((rows, width)),
            pl.BlockSpec((tile, width), lambda step: (step, 0)),
            pl.BlockSpec((tile, tile), lambda step: (step, 0)),
        ],
        out_shape=[
            jax.ShapeDtypeStruct((rows, width), bf16),
            jax.ShapeDtypeStruct((rows, width), bf16),
            jax.ShapeDtypeStruct((rows, tile), f32),
        ],
        scratch_shapes=[pltpu.VMEM((heads_dev, tile, 2 * length), f32)],
        compiler_params=pltpu.CompilerParams(vmem_limit_bytes=40 * 2**20),
        cost_estimate=pl.CostEstimate(
            flops=4 * rows * length * width,
            bytes_accessed=4 * length * width * 2,
            transcendentals=rows * length * heads_dev,
        ),
    )(first, place, table, near, qkv, doc_row, doc_col)


def attention_back(
    qkv, doc_row, doc_col, attended, grad_out, stats, first, place, table, near, split
):
    length = qkv.shape[0]
    rows = grad_out.shape[0]
    heads_dev = table.shape[1]
    width = heads_dev * head_dim
    return pl.pallas_call(
        functools.partial(attention_back_kernel, heads_dev, length, split),
        grid=(rows // tile,),
        in_specs=[
            pl.BlockSpec(memory_space=pltpu.SMEM),
            pl.BlockSpec(memory_space=pltpu.SMEM),
            pl.BlockSpec(memory_space=pltpu.SMEM),
            whole(near.shape),
            whole(qkv.shape),
            whole(doc_row.shape),
            pl.BlockSpec((tile, 1), lambda step: (step, 0)),
            whole((rows, width)),
            whole((rows, width)),
            pl.BlockSpec((tile, tile), lambda step: (step, 0)),
        ],
        out_specs=[
            whole((length, 3 * width)),
            whole((heads_dev, tile, 3 * tile)),
            whole((heads_dev, 2, 8, tile)),
        ],
        out_shape=[
            jax.ShapeDtypeStruct((length, 3 * width), bf16),
            jax.ShapeDtypeStruct((heads_dev, tile, 3 * tile), f32),
            jax.ShapeDtypeStruct((heads_dev, 2, 8, tile), f32),
        ],
        scratch_shapes=[
            pltpu.VMEM((heads_dev, tile, 2 * length), f32),
            pltpu.VMEM((heads_dev, tile, 2 * length), f32),
            pltpu.VMEM((length, width), f32),
            pltpu.VMEM((length, width), f32),
        ],
        compiler_params=pltpu.CompilerParams(vmem_limit_bytes=48 * 2**20),
        cost_estimate=pl.CostEstimate(
            flops=10 * rows * length * width,
            bytes_accessed=8 * length * width * 2,
            transcendentals=rows * length * heads_dev,
        ),
    )(first, place, table, near, qkv, doc_row, doc_col, attended, grad_out, stats)


def call(kernel, shapes, *operands, smem=0):
    return pl.pallas_call(
        kernel,
        in_specs=[pl.BlockSpec(memory_space=pltpu.SMEM)] * smem
        + [pl.BlockSpec(memory_space=pltpu.VMEM)] * (len(operands) - smem),
        out_specs=[pl.BlockSpec(memory_space=pltpu.VMEM)] * len(shapes),
        out_shape=[jax.ShapeDtypeStruct(shape, kind) for shape, kind in shapes],
        compiler_params=pltpu.CompilerParams(vmem_limit_bytes=32 * 2**20),
    )(*operands)


def share_in_kernel(copies, core_n, place, attn_in, gains, first, near, far):
    members = first.shape[0] // copies
    rows, width = attn_in.shape[1], attn_in.shape[2] // (3 * members)

    def columns(layer_id, member):
        block = jnp.concatenate(
            [
                attn_in[
                    layer_id, :, pl.ds(pl.multiple_of((part * members + member) * width, width), width)
                ]
                for part in range(3)
            ],
            axis=1,
        )
        return (block.astype(f32) * gains[layer_id]).astype(bf16)

    for member in range(members):
        block = columns(0, member)
        for copy in range(copies):
            first[(member // core_n * copies + copy) * core_n + member % core_n] = block
    half = members // 2
    for index in range(members):
        out = near if index < half else far
        out[index % half * rows : (index % half + 1) * rows] = columns(1, place[index])


def row_of(chip, plane, core, rows, planes=4):
    return pl.multiple_of(((chip * planes + plane) * 2 + core) * rows, rows)


def assemble_in_kernel(place, own, lower, upper, opposite, out):
    at_z, at_core, at_head = place[8], place[0] % 2, place[0] // 2
    rows = own.shape[0] // 8
    for part, offset in ((own, 0), (lower, 3), (upper, 1), (opposite, 2)):
        plane = (at_z + offset) % 4
        for index in range(8):
            row = row_of(at_head ^ (index // 2), plane, at_core ^ (index % 2), rows)
            out[pl.ds(row, rows)] = part[index * rows : (index + 1) * rows]


def plane_attention_kernel(
    length, place, table, strip, near, far, w_in, *refs
):
    quarters, (doc_row, doc_col, w_out, qkv, attended, stats, near_part, far_part, band) = (
        refs[:4], refs[4:],
    )
    step = pl.program_id(0)
    half = length // 2
    heads_dev = table.shape[1]
    width = heads_dev * head_dim

    @pl.when(step == 0)
    def _():
        fill_band(band, table, strip, heads_dev, length)
        at_z = place[length // tile]
        rows = width // 4
        for index, quarter in enumerate(quarters):
            block = (index // 2 ^ at_z % 2) * 2 + (index % 2 ^ at_z // 2)
            w_out[pl.ds(pl.multiple_of(block * rows, rows), rows)] = quarter[...]
        qkv[:half] = contract(near[...], w_in[...], 1, 0).astype(bf16)
        qkv[half:] = contract(far[...], w_in[...], 1, 0).astype(bf16)

    row = pl.multiple_of(step * tile, tile)
    starts = band_starts(place, step, length)
    same_doc = doc_col[...] == doc_row[...]
    queries = qkv[pl.ds(row, tile), :width] * bf16(score_scale)
    lanes = lax.broadcasted_iota(jnp.int32, (tile, tile), 1)
    collected = jnp.zeros((tile, tile), f32)
    results = []
    for head in range(heads_dev):
        own = slice(head * head_dim, (head + 1) * head_dim)
        keys = qkv[:, width + own.start : width + own.stop]
        values = qkv[:, 2 * width + own.start : 2 * width + own.stop]
        scores = contract(queries[:, own], keys, 1, 1) + jnp.concatenate(
            [band[head, :, pl.ds(start, tile)] for start in starts], axis=1
        )
        scores = jnp.where(same_doc, scores, masked)
        peak = jnp.max(scores, axis=1, keepdims=True)
        weights = jnp.exp(scores - peak)
        total = jnp.sum(weights, axis=1, keepdims=True)
        results.append((contract(weights.astype(bf16), values, 1, 0) / total).astype(bf16))
        collected = jnp.where(lanes == head, peak + jnp.log(total), collected)
    stats[...] = collected
    merged = jnp.concatenate(results, axis=1)
    attended[...] = merged
    part = contract(merged, w_out[...], 1, 0)

    @pl.when(row < half)
    def _():
        near_part[...] = part

    @pl.when(row >= half)
    def _():
        far_part[...] = part.astype(bf16)


def near_block(steps, columns):
    return pl.BlockSpec((tile, columns), lambda step: (jnp.minimum(step, steps // 2 - 1), 0))


def far_block(steps, columns):
    return pl.BlockSpec((tile, columns), lambda step: (jnp.maximum(step - steps // 2, 0), 0))


def plane_attention(near, far, w_in, quarters, doc_row, doc_col, place, table, strip):
    length, model_width = 2 * near.shape[0], near.shape[1]
    steps = length // tile
    heads_dev = table.shape[1]
    width = heads_dev * head_dim
    return pl.pallas_call(
        functools.partial(plane_attention_kernel, length),
        grid=(steps,),
        in_specs=[
            pl.BlockSpec(memory_space=pltpu.SMEM),
            pl.BlockSpec(memory_space=pltpu.SMEM),
            whole(strip.shape),
            whole(near.shape),
            whole(far.shape),
            whole(w_in.shape),
            *[whole(quarter.shape) for quarter in quarters],
            whole(doc_row.shape),
            pl.BlockSpec((tile, 1), lambda step: (step, 0)),
        ],
        out_specs=[
            whole((width, model_width)),
            whole((length, 3 * width)),
            pl.BlockSpec((tile, width), lambda step: (step, 0)),
            pl.BlockSpec((tile, tile), lambda step: (step, 0)),
            near_block(steps, model_width),
            far_block(steps, model_width),
        ],
        out_shape=[
            jax.ShapeDtypeStruct((width, model_width), bf16),
            jax.ShapeDtypeStruct((length, 3 * width), bf16),
            jax.ShapeDtypeStruct((length, width), bf16),
            jax.ShapeDtypeStruct((length, tile), f32),
            jax.ShapeDtypeStruct((length // 2, model_width), f32),
            jax.ShapeDtypeStruct((length // 2, model_width), bf16),
        ],
        scratch_shapes=[pltpu.VMEM((heads_dev, tile, 2 * length), f32)],
        compiler_params=pltpu.CompilerParams(vmem_limit_bytes=40 * 2**20),
        cost_estimate=pl.CostEstimate(
            flops=4 * length * length * width + 8 * length * model_width * width,
            bytes_accessed=12 * 2**20,
            transcendentals=length * length * heads_dev,
        ),
    )(place, table, strip, near, far, w_in, *quarters, doc_row, doc_col)


def plane_attention_back_kernel(
    length, place, table, strip, qkv, doc_row, doc_col, attended, stats, near, far, w_in, w_out,
    grad_qkv, grad_near, grad_far, near_part, far_part, *rest
):
    quarters, (band, grad_band, grad_keys, grad_values, out_sum) = rest[:4], rest[4:]
    step = pl.program_id(0)
    half = length // 2
    heads_dev = table.shape[1]
    width = heads_dev * head_dim

    @pl.when(step == 0)
    def _():
        fill_band(band, table, strip, heads_dev, length)
        grad_band[...] = jnp.zeros_like(grad_band)
        grad_keys[...] = jnp.zeros_like(grad_keys)
        grad_values[...] = jnp.zeros_like(grad_values)
        out_sum[...] = jnp.zeros_like(out_sum)

    row = pl.multiple_of(step * tile, tile)
    starts = band_starts(place, step, length)
    same_doc = doc_col[...] == doc_row[...]
    branch = jnp.where(row < half, near[...], far[...])
    merged = attended[...]
    grad_merged = contract(branch, w_out[...], 1, 1).astype(bf16)
    out_sum[...] += contract(merged, branch, 0, 0)
    products = grad_merged.astype(f32) * merged.astype(f32)
    queries = qkv[pl.ds(row, tile), :width] * bf16(score_scale)
    for head in range(heads_dev):
        own = slice(head * head_dim, (head + 1) * head_dim)
        keys = qkv[:, width + own.start : width + own.stop]
        values = qkv[:, 2 * width + own.start : 2 * width + own.stop]
        upstream = grad_merged[:, own]
        scores = contract(queries[:, own], keys, 1, 1) + jnp.concatenate(
            [band[head, :, pl.ds(start, tile)] for start in starts], axis=1
        )
        scores = jnp.where(same_doc, scores, masked)
        weights = jnp.exp(scores - stats[:, head : head + 1])
        delta = jnp.sum(products[:, own], axis=1, keepdims=True)
        grad_scores = weights * (contract(upstream, values, 1, 1) - delta)
        for block, start in enumerate(starts):
            grad_band[head, :, pl.ds(start, tile)] += grad_scores[
                :, block * tile : (block + 1) * tile
            ]
        grad_low = grad_scores.astype(bf16)
        grad_values[:, own] += contract(weights.astype(bf16), upstream, 0, 0)
        grad_keys[:, own] += contract(grad_low, queries[:, own], 0, 0)
        grad_qkv[pl.ds(row, tile), own] = (
            contract(grad_low, keys, 1, 0) * score_scale
        ).astype(bf16)

    @pl.when(step == pl.num_programs(0) - 1)
    def _():
        grad_qkv[:, width : 2 * width] = grad_keys[...].astype(bf16)
        grad_qkv[:, 2 * width :] = grad_values[...].astype(bf16)
        far_part[...] = contract(grad_qkv[half:], w_in[...], 1, 1).astype(bf16)
        near_part[...] = contract(grad_qkv[:half], w_in[...], 1, 1)
        at_z = place[length // tile]
        rows = width // 4
        for index, quarter in enumerate(quarters):
            block = (index // 2 ^ at_z % 2) * 2 + (index % 2 ^ at_z // 2)
            quarter[...] = out_sum[pl.ds(pl.multiple_of(block * rows, rows), rows)].astype(bf16)
        for head in range(heads_dev):
            grad_near[head] = grad_band[head, :, length - tile : length + 2 * tile]
            grad_far[head, 0] = jnp.full(
                (8, tile), jnp.sum(grad_band[head, :, : length - tile]), f32
            )
            grad_far[head, 1] = jnp.full(
                (8, tile), jnp.sum(grad_band[head, :, length + 2 * tile :]), f32
            )


def plane_attention_back(
    qkv, doc_row, doc_col, attended, stats, near, far, w_in, w_out, place, table, strip
):
    length, model_width = 2 * near.shape[0], near.shape[1]
    steps = length // tile
    heads_dev = table.shape[1]
    width = heads_dev * head_dim
    shapes = [
        ((length, 3 * width), bf16),
        ((heads_dev, tile, 3 * tile), f32),
        ((heads_dev, 2, 8, tile), f32),
        ((length // 2, model_width), f32),
        ((length // 2, model_width), bf16),
    ] + [((width // 4, model_width), bf16)] * 4
    return pl.pallas_call(
        functools.partial(plane_attention_back_kernel, length),
        grid=(steps,),
        in_specs=[
            pl.BlockSpec(memory_space=pltpu.SMEM),
            pl.BlockSpec(memory_space=pltpu.SMEM),
            whole(strip.shape),
            whole(qkv.shape),
            whole(doc_row.shape),
            pl.BlockSpec((tile, 1), lambda step: (step, 0)),
            pl.BlockSpec((tile, width), lambda step: (step, 0)),
            pl.BlockSpec((tile, tile), lambda step: (step, 0)),
            near_block(steps, model_width),
            far_block(steps, model_width),
            whole(w_in.shape),
            whole(w_out.shape),
        ],
        out_specs=[whole(shape) for shape, _ in shapes],
        out_shape=[jax.ShapeDtypeStruct(shape, kind) for shape, kind in shapes],
        scratch_shapes=[
            pltpu.VMEM((heads_dev, tile, 2 * length), f32),
            pltpu.VMEM((heads_dev, tile, 2 * length), f32),
            pltpu.VMEM((length, width), f32),
            pltpu.VMEM((length, width), f32),
            pltpu.VMEM((width, model_width), f32),
        ],
        compiler_params=pltpu.CompilerParams(vmem_limit_bytes=48 * 2**20),
        cost_estimate=pl.CostEstimate(
            flops=10 * length * length * width + 10 * length * model_width * width,
            bytes_accessed=12 * 2**20,
            transcendentals=length * length * heads_dev,
        ),
    )(place, table, strip, qkv, doc_row, doc_col, attended, stats, near, far, w_in, w_out)


def gelu_and_slope(pre_act):
    size = jnp.abs(pre_act)
    gauss = jnp.exp(-0.5 * pre_act * pre_act)
    ratio = 1.0 / (1.0 + np.float32(0.3275911 * 0.5**0.5) * size)
    series = np.float32(1.061405429)
    for factor in (-1.453152027, 1.421413741, -0.284496736, 0.254829592):
        series = series * ratio + np.float32(factor)
    tail = 0.5 * series * ratio * gauss
    cumulative = jnp.where(pre_act < 0, tail, 1.0 - tail)
    slope = cumulative + pre_act * gauss * np.float32((2 * np.pi) ** -0.5)
    return pre_act * cumulative, slope


def ff_kernel(rows, pair, activated, slope, part):
    columns = rows.shape[1]
    value, gradient = gelu_and_slope(contract(rows[...], pair[:, :columns], 1, 1))
    activated[...] = value.astype(bf16)
    slope[...] = gradient.astype(bf16)
    part[...] = contract(activated[...], pair[:, columns:], 1, 0).astype(part.dtype)


def ff_first_kernel(rows, *refs):
    parts, (activated, slope, part, pair) = refs[:8], refs[8:]
    columns = rows.shape[1]

    @pl.when(pl.program_id(0) == 0)
    def _():
        units = parts[0].shape[0]
        for index, ref in enumerate(parts):
            block = pl.ds(index % 4 * units, units)
            pair[block, index // 4 * columns : (index // 4 + 1) * columns] = ref[...]

    ff_kernel(rows, pair, activated, slope, part)


def ff_back_kernel(rows, slope, pair, grad_pre, part):
    columns = rows.shape[1]
    grad_act = contract(rows[...], pair[:, columns:], 1, 1)
    grad_pre[...] = (grad_act * slope[...].astype(f32)).astype(bf16)
    part[...] = contract(grad_pre[...], pair[:, :columns], 1, 0).astype(part.dtype)


def by_rows(kernel, step_rows, row_operands, whole_operands, outs, whole_outs=()):
    rows = row_operands[0].shape[0]
    return pl.pallas_call(
        kernel,
        grid=(rows // step_rows,),
        in_specs=[
            pl.BlockSpec((step_rows, operand.shape[1]), lambda step: (step, 0))
            for operand in row_operands
        ]
        + [whole(operand.shape) for operand in whole_operands],
        out_specs=[pl.BlockSpec((step_rows, columns), lambda step: (step, 0)) for columns, _ in outs]
        + [whole(shape) for shape in whole_outs],
        out_shape=[jax.ShapeDtypeStruct((rows, columns), kind) for columns, kind in outs]
        + [jax.ShapeDtypeStruct(shape, bf16) for shape in whole_outs],
        compiler_params=pltpu.CompilerParams(vmem_limit_bytes=32 * 2**20),
        cost_estimate=pl.CostEstimate(
            flops=4 * rows * outs[0][0] * row_operands[0].shape[1],
            bytes_accessed=6 * 2**20,
            transcendentals=0,
        ),
    )(*row_operands, *whole_operands)


def ff_grads_kernel(
    pre_near, pre_far, act_near, act_far, normed_near, normed_far, low_near, low_far, *outs
):
    columns = normed_near.shape[1]
    rows = outs[0].shape[0]
    up = (
        contract(pre_near[...], normed_near[...], 0, 0)
        + contract(pre_far[...], normed_far[...], 0, 0)
    ).astype(bf16)
    down = (
        contract(act_near[...], low_near[...], 0, 0) + contract(act_far[...], low_far[...], 0, 0)
    ).astype(bf16)
    for index, out in enumerate(outs):

        @pl.when(pl.program_id(0) == index // 2)
        def _():
            block = slice(index % 2 * rows, (index % 2 + 1) * rows)
            out[:, :columns] = up[block]
            out[:, columns:] = down[block]


def ff_grads(pre, act, normed, low):
    rows, hidden_units = pre[0].shape
    columns = normed[0].shape[1]
    step_units = hidden_units // 2
    shape = (hidden_units // 4, 2 * columns)
    return pl.pallas_call(
        ff_grads_kernel,
        grid=(2,),
        in_specs=[pl.BlockSpec((rows, step_units), lambda step: (0, step))] * 4
        + [whole((rows, columns))] * 4,
        out_specs=[whole(shape)] * 4,
        out_shape=[jax.ShapeDtypeStruct(shape, bf16)] * 4,
        compiler_params=pltpu.CompilerParams(vmem_limit_bytes=40 * 2**20),
        cost_estimate=pl.CostEstimate(
            flops=8 * rows * hidden_units * columns, bytes_accessed=8 * 2**20, transcendentals=0
        ),
    )(*pre, *act, *normed, *low)


def in_grads_kernel(place, near, far, grad_qkv, own, lower, upper, opposite, total):
    half = near.shape[0]
    total[...] = (
        contract(near[...], grad_qkv[:half], 0, 0) + contract(far[...], grad_qkv[half:], 0, 0)
    ).astype(bf16)
    rows = own.shape[0] // 8
    for out, offset in ((own, 0), (lower, 3), (upper, 1), (opposite, 2)):
        plane = (place[8] + offset) % 4
        for index in range(8):
            owner = place[index]
            row = row_of(owner // 2, plane, owner % 2, rows)
            out[index * rows : (index + 1) * rows] = total[pl.ds(row, rows)]


def in_grads(place, near, far, grad_qkv):
    columns = grad_qkv.shape[1]
    shape = (near.shape[1] // 4, columns)
    return pl.pallas_call(
        in_grads_kernel,
        in_specs=[pl.BlockSpec(memory_space=pltpu.SMEM)]
        + [pl.BlockSpec(memory_space=pltpu.VMEM)] * 3,
        out_specs=[pl.BlockSpec(memory_space=pltpu.VMEM)] * 4,
        out_shape=[jax.ShapeDtypeStruct(shape, bf16)] * 4,
        scratch_shapes=[pltpu.VMEM((near.shape[1], columns), bf16)],
        compiler_params=pltpu.CompilerParams(vmem_limit_bytes=32 * 2**20),
        cost_estimate=pl.CostEstimate(
            flops=4 * near.shape[0] * near.shape[1] * columns,
            bytes_accessed=4 * 2**20,
            transcendentals=0,
        ),
    )(place, near, far, grad_qkv)


def add_in_kernel(own, lower, upper, opposite, near, far):
    total = sum_of_four([own, lower, upper, opposite]).astype(bf16)
    half = near.shape[0]
    near[...] = total[:half]
    far[...] = total[half:]


def combine_kernel(near_part, arrived, own, x_part, y_part, xy_part):
    rows = own.shape[0]
    own[...] = near_part[:rows] + arrived[:rows].astype(f32)
    for bits, out in ((1, x_part), (2, y_part), (3, xy_part)):
        block = slice(bits * rows, (bits + 1) * rows)
        out[...] = (near_part[block] + arrived[block].astype(f32)).astype(bf16)


def added(own, x_part, y_part, xy_part):
    return (own[...] + x_part[...].astype(f32)) + (
        y_part[...].astype(f32) + xy_part[...].astype(f32)
    )


def close_kernel(kept, own, x_part, y_part, xy_part, hidden, units):
    total = kept[...] + added(own, x_part, y_part, xy_part)
    hidden[...] = total
    units[...] = (total * inverse_rms(total)).astype(bf16)


def close_gain_kernel(kept, own, x_part, y_part, xy_part, gain, hidden, normed):
    total = kept[...] + added(own, x_part, y_part, xy_part)
    hidden[...] = total
    normed[...] = (total * inverse_rms(total) * gain[...]).astype(bf16)


def last_kernel(kept, own, x_part, y_part, xy_part, hidden):
    hidden[...] = (kept[...] + added(own, x_part, y_part, xy_part)).astype(bf16)


def middle_back_kernel(
    upstream, own, x_part, y_part, xy_part, middle, gain, grad_middle, branch, grad_gain
):
    grad_normed = added(own, x_part, y_part, xy_part)
    inverse = inverse_rms(middle[...])
    grad_gain[...] = jnp.sum(grad_normed * middle[...] * inverse, axis=0, keepdims=True)
    total = upstream[...].astype(f32) + unit_norm_back(
        middle[...], inverse, grad_normed * gain[...]
    )
    grad_middle[...] = total
    branch[...] = total.astype(bf16)


def layer_back_kernel(grad_middle, own, x_part, y_part, xy_part, hidden, upstream, low):
    total = grad_middle[...] + unit_norm_back(
        hidden[...], inverse_rms(hidden[...]), added(own, x_part, y_part, xy_part)
    )
    upstream[...] = total
    low[...] = total.astype(bf16)


def finish_in_kernel(layers, place, *refs):
    shares, (attn_in, gains, grad_in, grad_gain) = refs[: 4 * layers], refs[4 * layers :]
    width = shares[0].shape[1] // 6
    members = attn_in.shape[2] // (3 * width)
    for layer_id in range(layers):
        row_dot = jnp.zeros(grad_gain.shape[1:], f32)
        for index in range(members):
            share = shares[4 * layer_id + index % 4]
            member = place[index]
            for part in range(3):
                at = (index // 4 * 3 + part) * width
                block = share[:, at : at + width].astype(f32)
                columns = pl.ds(pl.multiple_of((part * members + member) * width, width), width)
                grad_in[layer_id, :, columns] = block * gains[layer_id]
                row_dot = row_dot + jnp.sum(
                    block * attn_in[layer_id, :, columns].astype(f32), axis=1, keepdims=True
                )
        grad_gain[layer_id] = row_dot


def sum_of_four(parts):
    return (parts[0][...].astype(f32) + parts[1][...].astype(f32)) + (
        parts[2][...].astype(f32) + parts[3][...].astype(f32)
    )


def finish_ff_kernel(*refs):
    grad_up, grad_down = refs[-2:]
    columns = grad_up.shape[2]
    for layer_id in range(grad_up.shape[0]):
        total = sum_of_four(refs[4 * layer_id : 4 * layer_id + 4])
        grad_up[layer_id] = total[:, :columns]
        grad_down[layer_id] = total[:, columns:]


def finish_out_kernel(*refs):
    for layer_id in range(refs[-1].shape[0]):
        refs[-1][layer_id] = sum_of_four(refs[4 * layer_id : 4 * layer_id + 4])


def inverse_rms(hidden):
    return lax.rsqrt(jnp.mean(hidden * hidden, axis=-1, keepdims=True) + epsilon)


def prepare(bias_table, first_head, heads_dev):
    table = lax.dynamic_slice_in_dim(bias_table, first_head, heads_dev, 1)
    (near,) = call(near_kernel, [((heads_dev, tile, 3 * tile), f32)], table, smem=1)
    return table, near


def bucket_grads(grads, bucket_count):
    heads_dev = grads[0][0].shape[0]
    (total,) = call(
        functools.partial(bucket_kernel, len(grads)),
        [((bucket_count, tile), f32)],
        *(entry[0] for entry in grads),
        *(entry[1] for entry in grads),
    )
    return total[:, :heads_dev]


def gelu_parts(pre_act):
    cumulative = 0.5 * (1.0 + lax.erf(pre_act * np.float32(0.5**0.5)))
    slope = cumulative + pre_act * jnp.exp(-0.5 * pre_act * pre_act) * np.float32(
        (2 * np.pi) ** -0.5
    )
    return (pre_act * cumulative).astype(bf16), slope


def unit_norm_back(hidden, inverse, grad_unit):
    unit = hidden * inverse
    return inverse * (grad_unit - unit * jnp.mean(grad_unit * unit, axis=-1, keepdims=True))


def gather_rows(block, axes):
    return lax.all_gather(block, axes, axis=0, tiled=True)


def toggle(array, axis, bits):
    return lax.ppermute(array, axis, [(i, i ^ bits) for i in range(lax.axis_size(axis))])


def shift(array, by):
    planes = lax.axis_size("z")
    return lax.ppermute(array, "z", [(i, (i + by) % planes) for i in range(planes)])


def plane_gather(block, *holds):
    near = jnp.concatenate([block] + [toggle(block, "head", bits) for bits in (1, 2, 3)])
    near, *holds = tie(near, *holds)
    return (near, toggle(near, "core", 1), *holds)


def plane_scatter(near_part, far_part):
    rows, columns = near_part.shape[0] // 4, near_part.shape[1]
    own, *others = call(
        combine_kernel,
        [((rows, columns), f32)] + [((rows, columns), bf16)] * 3,
        near_part,
        toggle(far_part, "core", 1),
    )
    return [own] + [toggle(other, "head", bits) for bits, other in zip((1, 2, 3), others)]


def tie(*arrays):
    return lax.optimization_barrier(arrays)


def after(array, other):
    return lax.optimization_barrier((array, other))[0]


def scatter_sum(partial, axes, members):
    blocks = partial.astype(bf16).reshape(members, -1, partial.shape[1])
    return jnp.sum(lax.all_to_all(blocks, axes, 0, 0, tiled=True).astype(f32), axis=0)


def local_general(tokens, doc_start, bias_table, attn_in, attn_out, ff_in, ff_out, gains, cotangent):
    heads_n, z_n, core_n = (lax.axis_size(axis) for axis in everyone)
    devices = heads_n * z_n * core_n
    group, spare = ("z", "core"), "head"
    ff_group, ff_spare, ff_members = ("head", "core"), "z", heads_n * core_n
    blocks = z_n * core_n
    block_rows, model_width = tokens.shape[1:]
    layer_count, weight_rows = attn_in.shape[:2]
    length = block_rows * blocks
    heads_all = bias_table.shape[1]
    member = lax.axis_index("z") * core_n + lax.axis_index("core")
    heads_dev = max(1, heads_all // blocks)
    head_groups = heads_all // heads_dev
    split = blocks // head_groups
    head_group, query_part = member // split, member % split
    query_rows = length // split
    width = heads_dev * head_dim
    first = (query_part * (query_rows // tile)).astype(jnp.int32).reshape(1)
    place = jnp.arange(length // tile, dtype=jnp.int32)
    out_row = head_group * width

    def swap(array):
        return lax.all_to_all(array, everyone, 0, 0, tiled=True)

    starts = jnp.broadcast_to(
        doc_start.astype(f32)[:, None], (heads_n, blocks, block_rows)
    ).reshape(devices, block_rows)
    ff_gains = gains[:, :, 1].astype(f32).reshape(1, -1)
    small = swap(
        jnp.concatenate(
            [starts, jnp.broadcast_to(ff_gains, (devices, layer_count * weight_rows))], axis=1
        )
    )
    doc_row = small[:blocks, :block_rows].reshape(1, length)
    doc_col = lax.dynamic_slice_in_dim(
        doc_row.reshape(length, 1), query_part * query_rows, query_rows, 0
    )
    gain_ff = jnp.transpose(
        small[:, block_rows:].reshape(devices, layer_count, weight_rows), (1, 0, 2)
    ).reshape(layer_count, 1, model_width)
    table, near = prepare(bias_table, head_group * heads_dev, heads_dev)

    gain_attn = gains[:, :, 0].astype(f32)[:, :, None]
    own_in = attn_in.astype(f32)

    def fetch_in(layer_id):
        scaled = (own_in[layer_id] * gain_attn[layer_id]).astype(bf16)
        columns = jnp.transpose(
            scaled.reshape(weight_rows, 3, head_groups, width), (2, 0, 1, 3)
        ).reshape(head_groups, weight_rows, 3 * width)
        columns = jnp.repeat(columns, split, axis=0)
        columns = jnp.broadcast_to(columns[None], (heads_n, *columns.shape))
        return swap(columns.reshape(devices, weight_rows, 3 * width)).reshape(
            model_width, 3 * width
        )

    def fetch_ff(layer_id):
        pair = jnp.concatenate([ff_in[layer_id], ff_out[layer_id]], axis=1)
        pair = gather_rows(pair, ff_spare)
        return pair[:, :model_width], pair[:, model_width:]

    hidden, upstream = tokens[0].astype(f32), cotangent[0]
    weights_in = [fetch_in(layer_id) for layer_id in range(layer_count)]
    weights_out = lax.dynamic_slice_in_dim(
        lax.all_gather(attn_out, everyone, axis=1, tiled=True), out_row, width, 1
    )
    weights_ff = [fetch_ff(layer_id) for layer_id in range(layer_count)]

    records = []
    for layer_id in range(layer_count):
        w_in, w_out, (w_up, w_down) = (
            weights_in[layer_id], weights_out[layer_id], weights_ff[layer_id],
        )
        inverse = inverse_rms(hidden)
        units = gather_rows((hidden * inverse).astype(bf16), group)
        qkv = jnp.dot(units, w_in, preferred_element_type=f32).astype(bf16)
        attended, _, stats = attention(
            qkv, doc_row, doc_col, first, place, table, near, query_rows
        )
        mixed = jnp.dot(attended, w_out, preferred_element_type=f32)
        if split > 1:
            mixed = lax.dynamic_update_slice_in_dim(
                jnp.zeros((length, model_width), f32), mixed, query_part * query_rows, 0
            )
        middle = hidden + scatter_sum(mixed, group, blocks)
        inverse_ff = inverse_rms(middle)
        normed_ff = gather_rows((middle * inverse_ff * gain_ff[layer_id]).astype(bf16), ff_group)
        activated, slope = gelu_parts(contract(normed_ff, w_up, 1, 1))
        ff_result = jnp.dot(activated, w_down, preferred_element_type=f32)
        records.append(
            (hidden, inverse, units, qkv, attended, stats, middle, inverse_ff, normed_ff,
             activated, slope)
        )
        hidden = middle + scatter_sum(ff_result, ff_group, ff_members)
    output = hidden

    grads_ff, grads_in, grads_out, grads_gain_ff, grads_table = (
        [None] * layer_count for _ in range(5)
    )
    for layer_id in reversed(range(layer_count)):
        w_in, w_out, (w_up, w_down) = (
            weights_in[layer_id], weights_out[layer_id], weights_ff[layer_id],
        )
        (hidden, inverse, units, qkv, attended, stats, middle, inverse_ff, normed_ff,
         activated, slope) = records[layer_id]
        grad_low = gather_rows(upstream.astype(bf16), ff_group)
        grad_pre = (contract(grad_low, w_down, 1, 1) * slope).astype(bf16)
        grad_normed = scatter_sum(
            jnp.dot(grad_pre, w_up, preferred_element_type=f32), ff_group, ff_members
        )
        grad_pair = jnp.concatenate(
            [contract(grad_pre, normed_ff, 0, 0), contract(activated, grad_low, 0, 0)], axis=1
        ).astype(bf16)
        grads_ff[layer_id] = lax.psum_scatter(
            grad_pair, ff_spare, scatter_dimension=0, tiled=True
        ).astype(f32)
        grads_gain_ff[layer_id] = jnp.sum(grad_normed * middle * inverse_ff, axis=0)
        grad_middle = upstream + unit_norm_back(
            middle, inverse_ff, grad_normed * gain_ff[layer_id]
        )
        branch = gather_rows(grad_middle.astype(bf16), group)
        if split > 1:
            branch = lax.dynamic_slice_in_dim(branch, query_part * query_rows, query_rows, 0)
        grad_attended = contract(branch, w_out, 1, 1).astype(bf16)
        grad_qkv, grad_near, grad_far = attention_back(
            qkv, doc_row, doc_col, attended, grad_attended, stats, first, place, table, near, split
        )
        grads_table[layer_id] = (grad_near, grad_far)
        grad_units = scatter_sum(contract(grad_qkv, w_in, 1, 1), group, blocks)
        upstream = grad_middle + unit_norm_back(hidden, inverse, grad_units)
        grad_out = lax.dynamic_update_slice_in_dim(
            jnp.zeros((model_width, model_width), bf16),
            contract(attended, branch, 0, 0).astype(bf16),
            out_row,
            0,
        )
        grads_out[layer_id] = lax.psum_scatter(
            grad_out, everyone, scatter_dimension=0, tiled=True
        ).astype(f32)
        grads_in[layer_id] = contract(units, grad_qkv, 0, 0).astype(bf16)

    bucket_count = table.shape[0]
    grad_table = bucket_grads(grads_table, bucket_count)
    grad_table = lax.dynamic_update_slice_in_dim(
        jnp.zeros((bucket_count, heads_all), f32), grad_table, head_group * heads_dev, 1
    )
    grad_table = jnp.transpose(
        grad_table.reshape(blocks, bucket_count // blocks, heads_n, heads_all // heads_n),
        (2, 0, 1, 3),
    ).reshape(devices, -1)
    grad_gain_ff = jnp.transpose(
        jnp.stack(grads_gain_ff).reshape(layer_count, devices, weight_rows), (1, 0, 2)
    ).reshape(devices, -1)
    ends = jnp.sum(swap(jnp.concatenate([grad_gain_ff, grad_table], axis=1)), axis=0)
    grad_gain_ff = ends[: layer_count * weight_rows].reshape(layer_count, weight_rows)
    grad_bias_table = ends[layer_count * weight_rows :].reshape(
        bucket_count // blocks, heads_all // heads_n
    )
    grads_attn_in, grads_gains = [], []
    for layer_id in range(layer_count):
        parts = swap(grads_in[layer_id].reshape(devices, weight_rows, 3 * width)).astype(f32)
        parts = jnp.sum(parts.reshape(heads_n, blocks, weight_rows, 3 * width), axis=0)
        parts = jnp.sum(parts.reshape(head_groups, split, weight_rows, 3, width), axis=1)
        unit_grad = jnp.transpose(parts, (1, 2, 0, 3)).reshape(weight_rows, 3 * model_width)
        grads_attn_in.append(unit_grad * gain_attn[layer_id])
        grads_gains.append(
            jnp.stack(
                [jnp.sum(unit_grad * own_in[layer_id], axis=1), grad_gain_ff[layer_id]], axis=1
            )
        )
    return (
        output[None],
        upstream[None],
        jnp.stack(grads_attn_in),
        jnp.stack(grads_out),
        jnp.stack([entry[:, :model_width] for entry in grads_ff]),
        jnp.stack([entry[:, model_width:] for entry in grads_ff]),
        jnp.stack(grads_gains),
        grad_bias_table,
    )


def local_plane(tokens, doc_start, bias_table, attn_in, attn_out, ff_in, ff_out, gains, cotangent):
    heads_n, z_n, core_n = (lax.axis_size(axis) for axis in everyone)
    devices = heads_n * z_n * core_n
    at_head, at_z, at_core = (lax.axis_index(axis) for axis in everyone)
    members = heads_n * core_n
    block_rows, model_width = tokens.shape[1:]
    layer_count, weight_rows = attn_in.shape[:2]
    length = block_rows * members
    heads_all = bias_table.shape[1]
    heads_dev = heads_all // members
    width = heads_dev * head_dim
    member = at_head * core_n + at_core
    turn = [
        ((h * z_n + z) * core_n + c, (z * z_n + h) * core_n + c)
        for h in range(heads_n)
        for z in range(z_n)
        for c in range(core_n)
    ]
    place = jnp.stack(
        [
            (at_head ^ bits) * core_n + (at_core ^ other)
            for other in range(core_n)
            for bits in range(heads_n)
        ]
        + [at_z]
    ).astype(jnp.int32)

    def relay(array):
        return lax.ppermute(array, everyone, turn)

    def swap(array):
        return lax.all_to_all(array, everyone, 0, 0, tiled=True)

    row_shape = (block_rows, model_width)
    share_shape = (members // 2 * weight_rows, 3 * width)
    gain_attn = gains[:, :, 0].astype(f32)[:, :, None]
    first_share, near_share, far_share = call(
        functools.partial(share_in_kernel, z_n, core_n),
        [((devices, weight_rows, 3 * width), bf16)] + [(share_shape, bf16)] * 2,
        place,
        attn_in,
        gain_attn,
        smem=1,
    )

    quarter_turns = [
        [
            (z * core_n + c, (2 * c + (a ^ z % 2)) * core_n + (b ^ z // 2))
            for z in range(z_n)
            for c in range(core_n)
        ]
        for a in range(2)
        for b in range(2)
    ]

    def fetch_out(layer_id, hold):
        held = after(attn_out[layer_id], hold)
        return [
            lax.ppermute(held, ("z", "core"), [(holder, user) for user, holder in turns])
            for turns in quarter_turns
        ]

    starts = jnp.broadcast_to(
        doc_start.astype(f32)[None, :, None], (heads_n, z_n, core_n, block_rows)
    )
    ff_gains = gains[:, :, 1].astype(f32).reshape(1, -1)
    small = jnp.concatenate(
        [
            starts.reshape(devices, block_rows),
            jnp.broadcast_to(ff_gains, (devices, layer_count * weight_rows)),
        ],
        axis=1,
    )
    table, strip = prepare(bias_table, member * heads_dev, heads_dev)
    hidden, small, strip = tie(relay(tokens[0]), swap(small), strip)
    hidden = hidden.astype(f32)
    doc_row = small[:members, :block_rows].reshape(2, 2, core_n, block_rows)
    for axis, bit in ((0, at_head // 2), (1, at_head % 2), (2, at_core)):
        doc_row = jnp.where(bit == 1, jnp.flip(doc_row, axis), doc_row)
    doc_row = jnp.transpose(doc_row, (2, 0, 1, 3)).reshape(1, length)
    doc_col = doc_row.reshape(length, 1)
    gain_ff = jnp.transpose(
        small[:, block_rows:].reshape(devices, layer_count, weight_rows), (1, 0, 2)
    ).reshape(layer_count, 1, model_width)

    def round_planes(array, by, hold):
        return shift(after(array, hold), by)

    def fetch_ff(layer_id, by, hold):
        return [round_planes(array[layer_id], by, hold) for array in (ff_in, ff_out)]

    def ff_first(rows, layer_id, lower, upper, opposite, kind):
        parts = [
            part
            for side, array in enumerate((ff_in, ff_out))
            for part in (array[layer_id], lower[side], upper[side], opposite[side])
        ]
        units = 4 * ff_in.shape[1]
        return by_rows(
            ff_first_kernel,
            256,
            [rows],
            parts,
            [(units, bf16), (units, bf16), (model_width, kind)],
            [(units, 2 * model_width)],
        )

    def ff_forward(normed, layer_id, *weights):
        *near, pair = ff_first(normed[0], layer_id, *weights, f32)
        units = pair.shape[0]
        far = by_rows(
            ff_kernel,
            256,
            [normed[1]],
            [pair],
            [(units, bf16), (units, bf16), (model_width, bf16)],
        )
        return pair, *zip(near, far)

    def ff_backward(low, slopes, pair):
        return zip(
            *(
                by_rows(
                    ff_back_kernel,
                    256,
                    [rows, slope],
                    [pair],
                    [(pair.shape[0], bf16), (model_width, kind)],
                )
                for rows, slope, kind in zip(low, slopes, (f32, bf16))
            )
        )

    def share_chips(near, arrived, axis):
        rows = near.shape[0] // 4
        blocks = [
            jnp.concatenate(
                [near[bits * rows : (bits + 1) * rows], arrived[bits * rows : (bits + 1) * rows]],
                axis=axis,
            )
            for bits in range(4)
        ]
        return [blocks[0]] + [toggle(blocks[bits], "head", bits) for bits in (1, 2, 3)]

    units_shape = [(row_shape, f32), (row_shape, bf16)]
    unit_rows = (hidden * inverse_rms(hidden)).astype(bf16)

    near, far, w_in, quarters, doc_row, doc_col, gain_ff, far_share = plane_gather(
        unit_rows,
        swap(after(first_share, hidden)),
        fetch_out(0, hidden),
        doc_row,
        doc_col,
        gain_ff,
        toggle(after(far_share, hidden), "core", 1),
    )
    units = (near, far)
    w_in = w_in.reshape(model_width, 3 * width)
    w_out, qkv, attended, stats, *parts = plane_attention(
        *units, w_in, quarters, doc_row, doc_col, place, table, strip
    )
    parts, lower, upper, share = tie(
        parts,
        fetch_ff(0, 1, near),
        fetch_ff(0, -1, near),
        share_chips(after(near_share, near), far_share, 0),
    )
    opposite = fetch_ff(0, 2, parts[0])
    parts, opposite_in = tie(plane_scatter(*parts), opposite[0])
    middle, normed_rows = call(close_gain_kernel, units_shape, hidden, *parts, gain_ff[0])
    near, far, opposite_out = plane_gather(normed_rows, opposite[1])
    normed = (near, far)
    pair, acts, slopes, parts = ff_forward(normed, 0, lower, upper, [opposite_in, opposite_out])
    records = [
        (hidden, units, w_in, w_out, pair, qkv, attended, stats, middle, normed, acts, slopes)
    ]
    parts, upstream = tie(parts, relay(after(cotangent[0].astype(bf16), near)))
    share = jnp.concatenate(share)
    parts, lower_in, *shares = tie(
        plane_scatter(*parts),
        round_planes(ff_in[1], 1, parts[0]),
        round_planes(share, 1, parts[0]),
        round_planes(share, -1, parts[0]),
    )
    hidden, unit_rows = call(close_kernel, units_shape, middle, *parts)

    near, far, opposite, quarters = plane_gather(
        unit_rows, round_planes(share, 2, unit_rows), fetch_out(1, unit_rows)
    )
    units = (near, far)
    (w_in,) = call(
        assemble_in_kernel,
        [((model_width, 3 * width), bf16)],
        place,
        share,
        *shares,
        opposite,
        smem=1,
    )
    w_out, qkv, attended, stats, *parts = plane_attention(
        *units, w_in, quarters, doc_row, doc_col, place, table, strip
    )
    low = plane_gather(after(upstream, far))
    parts, near_low, lower_out, upper = tie(
        parts, low[0], round_planes(ff_out[1], 1, far), fetch_ff(1, -1, far)
    )
    low = (near_low, low[1])
    opposite = fetch_ff(1, 2, parts[0])
    parts, opposite_in = tie(plane_scatter(*parts), opposite[0])
    middle, normed_rows = call(close_gain_kernel, units_shape, hidden, *parts, gain_ff[1])
    near, far, opposite_out = plane_gather(normed_rows, opposite[1])
    normed = (near, far)
    pair, acts, slopes, last_parts = ff_forward(
        normed, 1, [lower_in, lower_out], upper, [opposite_in, opposite_out]
    )
    records.append(
        (hidden, units, w_in, w_out, pair, qkv, attended, stats, middle, normed, acts, slopes)
    )

    def back_to_middle(parts, upstream, middle, gain):
        return call(
            middle_back_kernel, units_shape + [((1, model_width), f32)], upstream, *parts, middle, gain
        )

    def attention_grads(record, branch):
        _, _, w_in, w_out, _, qkv, attended, stats, *_ = record
        grad_qkv, grad_near, grad_far, near_part, far_part, *quarters = plane_attention_back(
            qkv, doc_row, doc_col, attended, stats, *branch, w_in, w_out, place, table, strip
        )
        return grad_qkv, (grad_near, grad_far), (near_part, far_part), quarters

    def owners_quarters(quarters):
        return [
            lax.ppermute(quarter, ("z", "core"), turns)
            for quarter, turns in zip(quarters, quarter_turns)
        ]

    def table_grads(near_and_far):
        return bucket_grads([near_and_far], table.shape[0])

    def add_in(own, lower, upper, opposite):
        return call(add_in_kernel, [(share_shape, bf16)] * 2, own, lower, upper, opposite)

    record = records[1]
    hidden, units, _, _, pair, *_, middle, normed, acts, slopes = record
    pres, parts = ff_backward(low, slopes, pair)
    planes = ff_grads(pres, acts, normed, low)
    parts, ff_lower = tie(plane_scatter(*parts), shift(planes[1], -1))
    last_parts = plane_scatter(*after(last_parts, parts))
    grad_middle, branch_rows, gain_1 = back_to_middle(parts, upstream, middle, gain_ff[1])
    *branch, ff_upper = plane_gather(branch_rows, round_planes(planes[2], 1, branch_rows))
    grad_qkv, strips_1, parts, quarters = attention_grads(record, branch)
    parts, last_parts, ff_opposite = tie(
        parts, last_parts, round_planes(planes[3], 2, branch[1])
    )
    grads_ff = [planes[0], ff_lower, ff_upper, ff_opposite]
    grad_in = in_grads(place, *units, grad_qkv)
    parts, in_lower, in_upper, quarters_1, output, table_1 = tie(
        plane_scatter(*parts),
        shift(grad_in[1], -1),
        shift(grad_in[2], 1),
        owners_quarters(quarters),
        call(last_kernel, [(row_shape, bf16)], middle, *last_parts)[0],
        table_grads(strips_1),
    )
    upstream, low_rows = call(layer_back_kernel, units_shape, grad_middle, *parts, hidden)

    record = records[0]
    hidden, units, _, _, pair, *_, middle, normed, acts, slopes = record
    *low, in_opposite = plane_gather(low_rows, round_planes(grad_in[3], 2, low_rows))
    pres, parts = ff_backward(low, slopes, pair)
    parts, output = tie(parts, relay(after(output, low[0])))
    planes = ff_grads(pres, acts, normed, low)
    near_in, far_in = add_in(grad_in[0], in_lower, in_upper, in_opposite)
    parts, ff_lower, far_in = tie(
        plane_scatter(*parts), shift(planes[1], -1), toggle(after(far_in, parts[0]), "core", 1)
    )
    grad_middle, branch_rows, gain_0 = back_to_middle(parts, upstream, middle, gain_ff[0])
    *branch, ff_upper, shares_1 = plane_gather(
        branch_rows,
        round_planes(planes[2], 1, branch_rows),
        share_chips(after(near_in, branch_rows), far_in, 1),
    )
    grad_qkv, strips_0, parts, quarters = attention_grads(record, branch)
    parts, ff_opposite = tie(parts, round_planes(planes[3], 2, branch[1]))
    grads_ff = [planes[0], ff_lower, ff_upper, ff_opposite] + grads_ff
    grad_in = in_grads(place, *units, grad_qkv)
    parts, in_opposite, in_lower, table_0 = tie(
        plane_scatter(*parts),
        shift(grad_in[3], 2),
        shift(grad_in[1], -1),
        table_grads(strips_0),
    )
    upstream, low_rows = call(layer_back_kernel, units_shape, grad_middle, *parts, hidden)
    grad_tokens = relay(low_rows)
    in_upper = round_planes(grad_in[2], 1, low_rows)
    quarters_0 = owners_quarters(after(quarters, low_rows))
    near_in, far_in = add_in(grad_in[0], in_lower, in_upper, in_opposite)
    shares_0 = share_chips(near_in, toggle(far_in, "core", 1), 1)

    bucket_count = table.shape[0]
    grad_table = table_0 + table_1
    grad_table = lax.dynamic_update_slice_in_dim(
        jnp.zeros((bucket_count, heads_all), f32), grad_table, member * heads_dev, 1
    )
    grad_table = jnp.transpose(
        grad_table.reshape(members, bucket_count // members, heads_n, heads_all // heads_n),
        (2, 0, 1, 3),
    ).reshape(devices, -1)
    grad_gain_ff = jnp.transpose(
        jnp.concatenate([gain_0, gain_1]).reshape(layer_count, devices, weight_rows), (1, 0, 2)
    ).reshape(devices, -1)
    ends = jnp.concatenate([grad_gain_ff, grad_table], axis=1)
    ends = jnp.sum(swap(after(ends, low_rows)), axis=0)
    grad_gain_ff = ends[: layer_count * weight_rows].reshape(layer_count, weight_rows)
    grad_bias_table = ends[layer_count * weight_rows :].reshape(
        bucket_count // members, heads_all // heads_n
    )
    grad_up, grad_down = call(finish_ff_kernel, [(ff_in.shape, f32)] * 2, *after(grads_ff, low_rows))
    (grad_attn_out,) = call(finish_out_kernel, [(attn_out.shape, f32)], *quarters_0, *quarters_1)
    grad_attn_in, grad_gain_attn = call(
        functools.partial(finish_in_kernel, layer_count),
        [(attn_in.shape, f32), ((layer_count, weight_rows, 1), f32)],
        place,
        *shares_0,
        *shares_1,
        attn_in,
        gain_attn,
        smem=1,
    )
    return (
        output.astype(f32)[None],
        grad_tokens.astype(f32)[None],
        grad_attn_in,
        grad_attn_out,
        grad_up,
        grad_down,
        jnp.concatenate([grad_gain_attn, grad_gain_ff[:, :, None]], axis=2),
        grad_bias_table,
    )


def solution(mesh):
    sizes = dict(mesh.shape)
    cores = 2
    fine = Mesh(
        mesh.devices.reshape(sizes["head"], sizes["blk"] // cores, cores), everyone
    )
    blk = ("z", "core")
    in_specs = (
        P("head", blk, None),
        P(None, blk),
        P(),
        P(None, everyone, None),
        P(None, everyone, None),
        P(None, everyone, None),
        P(None, everyone, None),
        P(None, everyone, None),
        P("head", blk, None),
    )
    out_specs = (
        P("head", blk, None),
        P("head", blk, None),
        P(None, everyone, None),
        P(None, everyone, None),
        P(None, everyone, None),
        P(None, everyone, None),
        P(None, everyone, None),
        P(blk, "head"),
    )
    plane = sizes["head"] == 4 and sizes["blk"] == 8
    local = local_plane if plane else local_general
    return jax.shard_map(local, mesh=fine, in_specs=in_specs, out_specs=out_specs, check_vma=False)
```

```python
import functools

import jax
import jax.numpy as jnp
import numpy as np
from jax import lax
from jax.experimental import pallas as pl
from jax.experimental.pallas import tpu as pltpu
from jax.sharding import Mesh
from jax.sharding import PartitionSpec as P

bounds = (1, 2, 3, 4, 5, 6, 7, 8, 12, 16, 23, 32, 46, 64, 91)
epsilon = 1e-06
masked = -1e30
score_scale = 0.125
head_dim = 64
tile = 128
everyone = ("head", "z", "core")
bf16 = jnp.bfloat16
f32 = jnp.float32


def contract(lhs, rhs, lhs_dim, rhs_dim):
    return lax.dot_general(
        lhs, rhs, (((lhs_dim,), (rhs_dim,)), ((), ())), preferred_element_type=f32
    )


def near_buckets(shape):
    offsets = (
        lax.broadcasted_iota(jnp.int32, shape, 1) - tile - lax.broadcasted_iota(jnp.int32, shape, 0)
    )
    distance = jnp.abs(offsets)
    bucket = jnp.where(offsets > 0, 16, 0)
    for boundary in bounds:
        bucket = bucket + jnp.where(distance >= boundary, 1, 0)
    return bucket


def near_kernel(table, near):
    bucket = near_buckets(near.shape[1:])
    for head in range(near.shape[0]):
        values = jnp.zeros(near.shape[1:], f32)
        for bucket_id in range(table.shape[0]):
            values = jnp.where(bucket == bucket_id, table[bucket_id, head], values)
        near[head] = values


def bucket_kernel(first_lane, near, far, out):
    bucket = near_buckets(near.shape[1:])
    rows = lax.broadcasted_iota(jnp.int32, out.shape, 0)
    lanes = lax.broadcasted_iota(jnp.int32, out.shape, 1)
    total = jnp.zeros(out.shape, f32)
    for head in range(near.shape[0]):
        strip = near[head]
        for bucket_id in range(out.shape[0]):
            value = jnp.sum(jnp.where(bucket == bucket_id, strip, 0.0), axis=0, keepdims=True)
            value = jnp.sum(value, axis=1, keepdims=True)
            if bucket_id in (15, 31):
                value = value + far[head, bucket_id // 16, :1, :1]
            total = jnp.where((rows == bucket_id) & (lanes == head + first_lane[0]), value, total)
    out[...] = total


def fill_band(band, table, near, heads_dev, length):
    for head in range(heads_dev):
        band[head, :, : length - tile] = jnp.full((tile, length - tile), table[15, head], f32)
        band[head, :, length - tile : length + 2 * tile] = near[head]
        band[head, :, length + 2 * tile :] = jnp.full(
            (tile, length - 2 * tile), table[31, head], f32
        )


def band_starts(place, at, length):
    return [
        pl.multiple_of(length + (place[block] - place[at]) * tile, tile)
        for block in range(length // tile)
    ]


def attention_kernel(
    heads_dev, length, first, place, table, near, qkv, doc_row, doc_col, out, local, stats, band
):
    step = pl.program_id(0)
    width = heads_dev * head_dim

    @pl.when(step == 0)
    def _():
        fill_band(band, table, near, heads_dev, length)

    row = pl.multiple_of((first[0] + step) * tile, tile)
    out_row = pl.multiple_of((place[first[0] + step] - first[0]) * tile, tile)
    starts = band_starts(place, first[0] + step, length)
    same_doc = doc_col[...] == doc_row[...]
    queries = qkv[pl.ds(row, tile), :width] * bf16(score_scale)
    lanes = lax.broadcasted_iota(jnp.int32, (tile, tile), 1)
    collected = jnp.zeros((tile, tile), f32)
    for head in range(heads_dev):
        own = slice(head * head_dim, (head + 1) * head_dim)
        keys = qkv[:, width + own.start : width + own.stop]
        values = qkv[:, 2 * width + own.start : 2 * width + own.stop]
        scores = contract(queries[:, own], keys, 1, 1)
        scores = scores + jnp.concatenate(
            [band[head, :, pl.ds(start, tile)] for start in starts], axis=1
        )
        scores = jnp.where(same_doc, scores, masked)
        peak = jnp.max(scores, axis=1, keepdims=True)
        weights = jnp.exp(scores - peak)
        total = jnp.sum(weights, axis=1, keepdims=True)
        mixed = contract(weights.astype(bf16), values, 1, 0) / total
        out[pl.ds(out_row, tile), own] = mixed.astype(bf16)
        local[:, own] = mixed.astype(bf16)
        collected = jnp.where(lanes == head, peak + jnp.log(total), collected)
    stats[...] = collected


def attention_back_kernel(
    heads_dev, length, split, first, place, table, near, qkv, doc_row, doc_col, attended, grad_out, stats,
    grad_qkv, grad_near, grad_far, band, grad_band, grad_keys, grad_values,
):
    step = pl.program_id(0)
    width = heads_dev * head_dim

    @pl.when(step == 0)
    def _():
        fill_band(band, table, near, heads_dev, length)
        grad_band[...] = jnp.zeros_like(grad_band)
        grad_keys[...] = jnp.zeros_like(grad_keys)
        grad_values[...] = jnp.zeros_like(grad_values)
        if split > 1:
            grad_qkv[...] = jnp.zeros_like(grad_qkv)

    row = pl.multiple_of((first[0] + step) * tile, tile)
    out_row = pl.multiple_of((place[first[0] + step] - first[0]) * tile, tile)
    starts = band_starts(place, first[0] + step, length)
    same_doc = doc_col[...] == doc_row[...]
    at_step = pl.multiple_of(step * tile, tile)
    queries = qkv[pl.ds(row, tile), :width] * bf16(score_scale)
    for head in range(heads_dev):
        own = slice(head * head_dim, (head + 1) * head_dim)
        keys = qkv[:, width + own.start : width + own.stop]
        values = qkv[:, 2 * width + own.start : 2 * width + own.stop]
        upstream = grad_out[pl.ds(out_row, tile), own]
        scores = contract(queries[:, own], keys, 1, 1) + jnp.concatenate(
            [band[head, :, pl.ds(start, tile)] for start in starts], axis=1
        )
        scores = jnp.where(same_doc, scores, masked)
        weights = jnp.exp(scores - stats[:, head : head + 1])
        delta = jnp.sum(
            upstream.astype(f32) * attended[pl.ds(at_step, tile), own].astype(f32),
            axis=1,
            keepdims=True,
        )
        grad_scores = weights * (contract(upstream, values, 1, 1) - delta)
        for block, start in enumerate(starts):
            grad_band[head, :, pl.ds(start, tile)] += grad_scores[
                :, block * tile : (block + 1) * tile
            ]
        grad_low = grad_scores.astype(bf16)
        grad_values[:, own] += contract(weights.astype(bf16), upstream, 0, 0)
        grad_keys[:, own] += contract(grad_low, queries[:, own], 0, 0)
        grad_qkv[pl.ds(row, tile), own] = (
            contract(grad_low, keys, 1, 0) * score_scale
        ).astype(bf16)

    @pl.when(step == pl.num_programs(0) - 1)
    def _():
        grad_qkv[:, width : 2 * width] = grad_keys[...].astype(bf16)
        grad_qkv[:, 2 * width :] = grad_values[...].astype(bf16)
        for head in range(heads_dev):
            grad_near[head] = grad_band[head, :, length - tile : length + 2 * tile]
            grad_far[head, 0] = jnp.full(
                (8, tile), jnp.sum(grad_band[head, :, : length - tile]), f32
            )
            grad_far[head, 1] = jnp.full(
                (8, tile), jnp.sum(grad_band[head, :, length + 2 * tile :]), f32
            )


def whole(shape):
    return pl.BlockSpec(shape, lambda step: (0,) * len(shape))


def attention(qkv, doc_row, doc_col, first, place, table, near, rows):
    length = qkv.shape[0]
    heads_dev = table.shape[1]
    width = heads_dev * head_dim
    return pl.pallas_call(
        functools.partial(attention_kernel, heads_dev, length),
        grid=(rows // tile,),
        in_specs=[
            pl.BlockSpec(memory_space=pltpu.SMEM),
            pl.BlockSpec(memory_space=pltpu.SMEM),
            pl.BlockSpec(memory_space=pltpu.SMEM),
            whole(near.shape),
            whole(qkv.shape),
            whole(doc_row.shape),
            pl.BlockSpec((tile, 1), lambda step: (step, 0)),
        ],
        out_specs=[
            whole((rows, width)),
            pl.BlockSpec((tile, width), lambda step: (step, 0)),
            pl.BlockSpec((tile, tile), lambda step: (step, 0)),
        ],
        out_shape=[
            jax.ShapeDtypeStruct((rows, width), bf16),
            jax.ShapeDtypeStruct((rows, width), bf16),
            jax.ShapeDtypeStruct((rows, tile), f32),
        ],
        scratch_shapes=[pltpu.VMEM((heads_dev, tile, 2 * length), f32)],
        compiler_params=pltpu.CompilerParams(vmem_limit_bytes=40 * 2**20),
        cost_estimate=pl.CostEstimate(
            flops=4 * rows * length * width,
            bytes_accessed=4 * length * width * 2,
            transcendentals=rows * length * heads_dev,
        ),
    )(first, place, table, near, qkv, doc_row, doc_col)


def attention_back(
    qkv, doc_row, doc_col, attended, grad_out, stats, first, place, table, near, split
):
    length = qkv.shape[0]
    rows = grad_out.shape[0]
    heads_dev = table.shape[1]
    width = heads_dev * head_dim
    return pl.pallas_call(
        functools.partial(attention_back_kernel, heads_dev, length, split),
        grid=(rows // tile,),
        in_specs=[
            pl.BlockSpec(memory_space=pltpu.SMEM),
            pl.BlockSpec(memory_space=pltpu.SMEM),
            pl.BlockSpec(memory_space=pltpu.SMEM),
            whole(near.shape),
            whole(qkv.shape),
            whole(doc_row.shape),
            pl.BlockSpec((tile, 1), lambda step: (step, 0)),
            whole((rows, width)),
            whole((rows, width)),
            pl.BlockSpec((tile, tile), lambda step: (step, 0)),
        ],
        out_specs=[
            whole((length, 3 * width)),
            whole((heads_dev, tile, 3 * tile)),
            whole((heads_dev, 2, 8, tile)),
        ],
        out_shape=[
            jax.ShapeDtypeStruct((length, 3 * width), bf16),
            jax.ShapeDtypeStruct((heads_dev, tile, 3 * tile), f32),
            jax.ShapeDtypeStruct((heads_dev, 2, 8, tile), f32),
        ],
        scratch_shapes=[
            pltpu.VMEM((heads_dev, tile, 2 * length), f32),
            pltpu.VMEM((heads_dev, tile, 2 * length), f32),
            pltpu.VMEM((length, width), f32),
            pltpu.VMEM((length, width), f32),
        ],
        compiler_params=pltpu.CompilerParams(vmem_limit_bytes=48 * 2**20),
        cost_estimate=pl.CostEstimate(
            flops=10 * rows * length * width,
            bytes_accessed=8 * length * width * 2,
            transcendentals=rows * length * heads_dev,
        ),
    )(first, place, table, near, qkv, doc_row, doc_col, attended, grad_out, stats)


def call(kernel, shapes, *operands, smem=0):
    return pl.pallas_call(
        kernel,
        in_specs=[pl.BlockSpec(memory_space=pltpu.SMEM)] * smem
        + [pl.BlockSpec(memory_space=pltpu.VMEM)] * (len(operands) - smem),
        out_specs=[pl.BlockSpec(memory_space=pltpu.VMEM)] * len(shapes),
        out_shape=[jax.ShapeDtypeStruct(shape, kind) for shape, kind in shapes],
        compiler_params=pltpu.CompilerParams(vmem_limit_bytes=16 * 2**20),
    )(*operands)


def share_in_kernel(copies, core_n, place, attn_in, gains, first, near, far):
    members = first.shape[0] // copies
    rows, width = attn_in.shape[1], attn_in.shape[2] // (3 * members)

    def columns(layer_id, member):
        block = jnp.concatenate(
            [
                attn_in[
                    layer_id, :, pl.ds(pl.multiple_of((part * members + member) * width, width), width)
                ]
                for part in range(3)
            ],
            axis=1,
        )
        return (block.astype(f32) * gains[layer_id]).astype(bf16)

    for member in range(members):
        block = columns(0, member)
        for copy in range(copies):
            first[(member // core_n * copies + copy) * core_n + member % core_n] = block
    half = members // 2
    for index in range(members):
        out = near if index < half else far
        out[index % half * rows : (index % half + 1) * rows] = columns(1, place[index])


def row_of(chip, plane, core, rows, planes=4):
    return pl.multiple_of(((chip * planes + plane) * 2 + core) * rows, rows)


def assemble_in_kernel(place, own, lower, upper, opposite, out):
    at_z, at_core, at_head = place[8], place[0] % 2, place[0] // 2
    rows = own.shape[0] // 8
    for part, offset in ((own, 0), (lower, 3), (upper, 1), (opposite, 2)):
        plane = (at_z + offset) % 4
        for index in range(8):
            row = row_of(at_head ^ (index // 2), plane, at_core ^ (index % 2), rows)
            out[pl.ds(row, rows)] = part[index * rows : (index + 1) * rows]


def plane_attention_kernel(
    length, place, table, strip, near, far, w_in, *refs
):
    quarters, (doc_row, doc_col, w_out, qkv, attended, stats, near_part, far_part, band) = (
        refs[:4], refs[4:],
    )
    step = pl.program_id(0)
    half = length // 2
    heads_dev = table.shape[1]
    width = heads_dev * head_dim

    @pl.when(step == 0)
    def _():
        fill_band(band, table, strip, heads_dev, length)
        at_z = place[length // tile]
        rows = width // 4
        for index, quarter in enumerate(quarters):
            block = (index // 2 ^ at_z % 2) * 2 + (index % 2 ^ at_z // 2)
            w_out[pl.ds(pl.multiple_of(block * rows, rows), rows)] = quarter[...]
        qkv[:half] = contract(near[...], w_in[...], 1, 0).astype(bf16)
        qkv[half:] = contract(far[...], w_in[...], 1, 0).astype(bf16)

    row = pl.multiple_of(step * tile, tile)
    starts = band_starts(place, step, length)
    same_doc = doc_col[...] == doc_row[...]
    queries = qkv[pl.ds(row, tile), :width] * bf16(score_scale)
    lanes = lax.broadcasted_iota(jnp.int32, (tile, tile), 1)
    collected = jnp.zeros((tile, tile), f32)
    results = []
    for head in range(heads_dev):
        own = slice(head * head_dim, (head + 1) * head_dim)
        keys = qkv[:, width + own.start : width + own.stop]
        values = qkv[:, 2 * width + own.start : 2 * width + own.stop]
        scores = contract(queries[:, own], keys, 1, 1) + jnp.concatenate(
            [band[head, :, pl.ds(start, tile)] for start in starts], axis=1
        )
        scores = jnp.where(same_doc, scores, masked)
        peak = jnp.max(scores, axis=1, keepdims=True)
        weights = jnp.exp(scores - peak)
        total = jnp.sum(weights, axis=1, keepdims=True)
        results.append((contract(weights.astype(bf16), values, 1, 0) / total).astype(bf16))
        collected = jnp.where(lanes == head, peak + jnp.log(total), collected)
    stats[...] = collected
    merged = jnp.concatenate(results, axis=1)
    attended[...] = merged
    part = contract(merged, w_out[...], 1, 0)

    @pl.when(row < half)
    def _():
        near_part[...] = part

    @pl.when(row >= half)
    def _():
        far_part[...] = part.astype(bf16)


def near_block(steps, columns):
    return pl.BlockSpec((tile, columns), lambda step: (jnp.minimum(step, steps // 2 - 1), 0))


def far_block(steps, columns):
    return pl.BlockSpec((tile, columns), lambda step: (jnp.maximum(step - steps // 2, 0), 0))


def plane_attention(near, far, w_in, quarters, doc_row, doc_col, place, table, strip):
    length, model_width = 2 * near.shape[0], near.shape[1]
    steps = length // tile
    heads_dev = table.shape[1]
    width = heads_dev * head_dim
    return pl.pallas_call(
        functools.partial(plane_attention_kernel, length),
        grid=(steps,),
        in_specs=[
            pl.BlockSpec(memory_space=pltpu.SMEM),
            pl.BlockSpec(memory_space=pltpu.SMEM),
            whole(strip.shape),
            whole(near.shape),
            whole(far.shape),
            whole(w_in.shape),
            *[whole(quarter.shape) for quarter in quarters],
            whole(doc_row.shape),
            pl.BlockSpec((tile, 1), lambda step: (step, 0)),
        ],
        out_specs=[
            whole((width, model_width)),
            whole((length, 3 * width)),
            pl.BlockSpec((tile, width), lambda step: (step, 0)),
            pl.BlockSpec((tile, tile), lambda step: (step, 0)),
            near_block(steps, model_width),
            far_block(steps, model_width),
        ],
        out_shape=[
            jax.ShapeDtypeStruct((width, model_width), bf16),
            jax.ShapeDtypeStruct((length, 3 * width), bf16),
            jax.ShapeDtypeStruct((length, width), bf16),
            jax.ShapeDtypeStruct((length, tile), f32),
            jax.ShapeDtypeStruct((length // 2, model_width), f32),
            jax.ShapeDtypeStruct((length // 2, model_width), bf16),
        ],
        scratch_shapes=[pltpu.VMEM((heads_dev, tile, 2 * length), f32)],
        compiler_params=pltpu.CompilerParams(vmem_limit_bytes=24 * 2**20),
        cost_estimate=pl.CostEstimate(
            flops=4 * length * length * width + 8 * length * model_width * width,
            bytes_accessed=12 * 2**20,
            transcendentals=length * length * heads_dev,
        ),
    )(place, table, strip, near, far, w_in, *quarters, doc_row, doc_col)


def plane_attention_back_kernel(
    length, place, table, strip, qkv, doc_row, doc_col, attended, stats, near, far, w_in, w_out,
    grad_qkv, grad_near, grad_far, near_part, far_part, *rest
):
    quarters, (band, grad_band, grad_keys, grad_values, out_sum) = rest[:4], rest[4:]
    step = pl.program_id(0)
    half = length // 2
    heads_dev = table.shape[1]
    width = heads_dev * head_dim

    @pl.when(step == 0)
    def _():
        fill_band(band, table, strip, heads_dev, length)
        grad_band[...] = jnp.zeros_like(grad_band)
        grad_keys[...] = jnp.zeros_like(grad_keys)
        grad_values[...] = jnp.zeros_like(grad_values)
        out_sum[...] = jnp.zeros_like(out_sum)

    row = pl.multiple_of(step * tile, tile)
    starts = band_starts(place, step, length)
    same_doc = doc_col[...] == doc_row[...]
    branch = jnp.where(row < half, near[...], far[...])
    merged = attended[...]
    grad_merged = contract(branch, w_out[...], 1, 1).astype(bf16)
    out_sum[...] += contract(merged, branch, 0, 0)
    products = grad_merged.astype(f32) * merged.astype(f32)
    queries = qkv[pl.ds(row, tile), :width] * bf16(score_scale)
    for head in range(heads_dev):
        own = slice(head * head_dim, (head + 1) * head_dim)
        keys = qkv[:, width + own.start : width + own.stop]
        values = qkv[:, 2 * width + own.start : 2 * width + own.stop]
        upstream = grad_merged[:, own]
        scores = contract(queries[:, own], keys, 1, 1) + jnp.concatenate(
            [band[head, :, pl.ds(start, tile)] for start in starts], axis=1
        )
        scores = jnp.where(same_doc, scores, masked)
        weights = jnp.exp(scores - stats[:, head : head + 1])
        delta = jnp.sum(products[:, own], axis=1, keepdims=True)
        grad_scores = weights * (contract(upstream, values, 1, 1) - delta)
        for block, start in enumerate(starts):
            grad_band[head, :, pl.ds(start, tile)] += grad_scores[
                :, block * tile : (block + 1) * tile
            ]
        grad_low = grad_scores.astype(bf16)
        grad_values[:, own] += contract(weights.astype(bf16), upstream, 0, 0)
        grad_keys[:, own] += contract(grad_low, queries[:, own], 0, 0)
        grad_qkv[pl.ds(row, tile), own] = (
            contract(grad_low, keys, 1, 0) * score_scale
        ).astype(bf16)

    @pl.when(step == pl.num_programs(0) - 1)
    def _():
        grad_qkv[:, width : 2 * width] = grad_keys[...].astype(bf16)
        grad_qkv[:, 2 * width :] = grad_values[...].astype(bf16)
        far_part[...] = contract(grad_qkv[half:], w_in[...], 1, 1).astype(bf16)
        near_part[...] = contract(grad_qkv[:half], w_in[...], 1, 1)
        at_z = place[length // tile]
        rows = width // 4
        for index, quarter in enumerate(quarters):
            block = (index // 2 ^ at_z % 2) * 2 + (index % 2 ^ at_z // 2)
            quarter[...] = out_sum[pl.ds(pl.multiple_of(block * rows, rows), rows)].astype(bf16)
        for head in range(heads_dev):
            grad_near[head] = grad_band[head, :, length - tile : length + 2 * tile]
            grad_far[head, 0] = jnp.full(
                (8, tile), jnp.sum(grad_band[head, :, : length - tile]), f32
            )
            grad_far[head, 1] = jnp.full(
                (8, tile), jnp.sum(grad_band[head, :, length + 2 * tile :]), f32
            )


def plane_attention_back(
    qkv, doc_row, doc_col, attended, stats, near, far, w_in, w_out, place, table, strip
):
    length, model_width = 2 * near.shape[0], near.shape[1]
    steps = length // tile
    heads_dev = table.shape[1]
    width = heads_dev * head_dim
    shapes = [
        ((length, 3 * width), bf16),
        ((heads_dev, tile, 3 * tile), f32),
        ((heads_dev, 2, 8, tile), f32),
        ((length // 2, model_width), f32),
        ((length // 2, model_width), bf16),
    ] + [((width // 4, model_width), bf16)] * 4
    return pl.pallas_call(
        functools.partial(plane_attention_back_kernel, length),
        grid=(steps,),
        in_specs=[
            pl.BlockSpec(memory_space=pltpu.SMEM),
            pl.BlockSpec(memory_space=pltpu.SMEM),
            whole(strip.shape),
            whole(qkv.shape),
            whole(doc_row.shape),
            pl.BlockSpec((tile, 1), lambda step: (step, 0)),
            pl.BlockSpec((tile, width), lambda step: (step, 0)),
            pl.BlockSpec((tile, tile), lambda step: (step, 0)),
            near_block(steps, model_width),
            far_block(steps, model_width),
            whole(w_in.shape),
            whole(w_out.shape),
        ],
        out_specs=[whole(shape) for shape, _ in shapes],
        out_shape=[jax.ShapeDtypeStruct(shape, kind) for shape, kind in shapes],
        scratch_shapes=[
            pltpu.VMEM((heads_dev, tile, 2 * length), f32),
            pltpu.VMEM((heads_dev, tile, 2 * length), f32),
            pltpu.VMEM((length, width), f32),
            pltpu.VMEM((length, width), f32),
            pltpu.VMEM((width, model_width), f32),
        ],
        compiler_params=pltpu.CompilerParams(vmem_limit_bytes=28 * 2**20),
        cost_estimate=pl.CostEstimate(
            flops=10 * length * length * width + 10 * length * model_width * width,
            bytes_accessed=12 * 2**20,
            transcendentals=length * length * heads_dev,
        ),
    )(place, table, strip, qkv, doc_row, doc_col, attended, stats, near, far, w_in, w_out)


def gelu_and_slope(pre_act):
    size = jnp.abs(pre_act)
    gauss = jnp.exp(-0.5 * pre_act * pre_act)
    ratio = 1.0 / (1.0 + np.float32(0.3275911 * 0.5**0.5) * size)
    series = np.float32(1.061405429)
    for factor in (-1.453152027, 1.421413741, -0.284496736, 0.254829592):
        series = series * ratio + np.float32(factor)
    tail = 0.5 * series * ratio * gauss
    cumulative = jnp.where(pre_act < 0, tail, 1.0 - tail)
    slope = cumulative + pre_act * gauss * np.float32((2 * np.pi) ** -0.5)
    return pre_act * cumulative, slope


def ff_kernel(rows, pair, activated, slope, part):
    columns = rows.shape[1]
    value, gradient = gelu_and_slope(contract(rows[...], pair[:, :columns], 1, 1))
    activated[...] = value.astype(bf16)
    slope[...] = gradient.astype(bf16)
    part[...] = contract(activated[...], pair[:, columns:], 1, 0).astype(part.dtype)


def ff_first_kernel(rows, *refs):
    parts, (activated, slope, part, pair) = refs[:8], refs[8:]
    columns = rows.shape[1]

    @pl.when(pl.program_id(0) == 0)
    def _():
        units = parts[0].shape[0]
        for index, ref in enumerate(parts):
            block = pl.ds(index % 4 * units, units)
            pair[block, index // 4 * columns : (index // 4 + 1) * columns] = ref[...]

    ff_kernel(rows, pair, activated, slope, part)


def ff_back_kernel(rows, slope, pair, grad_pre, part):
    columns = rows.shape[1]
    grad_act = contract(rows[...], pair[:, columns:], 1, 1)
    grad_pre[...] = (grad_act * slope[...].astype(f32)).astype(bf16)
    part[...] = contract(grad_pre[...], pair[:, :columns], 1, 0).astype(part.dtype)


def by_rows(kernel, step_rows, row_operands, whole_operands, outs, whole_outs=()):
    rows = row_operands[0].shape[0]
    return pl.pallas_call(
        kernel,
        grid=(rows // step_rows,),
        in_specs=[
            pl.BlockSpec((step_rows, operand.shape[1]), lambda step: (step, 0))
            for operand in row_operands
        ]
        + [whole(operand.shape) for operand in whole_operands],
        out_specs=[pl.BlockSpec((step_rows, columns), lambda step: (step, 0)) for columns, _ in outs]
        + [whole(shape) for shape in whole_outs],
        out_shape=[jax.ShapeDtypeStruct((rows, columns), kind) for columns, kind in outs]
        + [jax.ShapeDtypeStruct(shape, bf16) for shape in whole_outs],
        compiler_params=pltpu.CompilerParams(vmem_limit_bytes=20 * 2**20),
        cost_estimate=pl.CostEstimate(
            flops=4 * rows * outs[0][0] * row_operands[0].shape[1],
            bytes_accessed=6 * 2**20,
            transcendentals=0,
        ),
    )(*row_operands, *whole_operands)


def ff_grads_kernel(
    pre_near, pre_far, act_near, act_far, normed_near, normed_far, low_near, low_far, *outs
):
    columns = normed_near.shape[1]
    rows = outs[0].shape[0]
    up = (
        contract(pre_near[...], normed_near[...], 0, 0)
        + contract(pre_far[...], normed_far[...], 0, 0)
    ).astype(bf16)
    down = (
        contract(act_near[...], low_near[...], 0, 0) + contract(act_far[...], low_far[...], 0, 0)
    ).astype(bf16)
    for index, out in enumerate(outs):

        @pl.when(pl.program_id(0) == index // 2)
        def _():
            block = slice(index % 2 * rows, (index % 2 + 1) * rows)
            out[:, :columns] = up[block]
            out[:, columns:] = down[block]


def ff_grads(pre, act, normed, low):
    rows, hidden_units = pre[0].shape
    columns = normed[0].shape[1]
    step_units = hidden_units // 2
    shape = (hidden_units // 4, 2 * columns)
    return pl.pallas_call(
        ff_grads_kernel,
        grid=(2,),
        in_specs=[pl.BlockSpec((rows, step_units), lambda step: (0, step))] * 4
        + [whole((rows, columns))] * 4,
        out_specs=[whole(shape)] * 4,
        out_shape=[jax.ShapeDtypeStruct(shape, bf16)] * 4,
        compiler_params=pltpu.CompilerParams(vmem_limit_bytes=28 * 2**20),
        cost_estimate=pl.CostEstimate(
            flops=8 * rows * hidden_units * columns, bytes_accessed=8 * 2**20, transcendentals=0
        ),
    )(*pre, *act, *normed, *low)


def in_grads_kernel(place, near, far, grad_qkv, own, lower, upper, opposite, total):
    half = near.shape[0]
    total[...] = (
        contract(near[...], grad_qkv[:half], 0, 0) + contract(far[...], grad_qkv[half:], 0, 0)
    ).astype(bf16)
    rows = own.shape[0] // 8
    for out, offset in ((own, 0), (lower, 3), (upper, 1), (opposite, 2)):
        plane = (place[8] + offset) % 4
        for index in range(8):
            owner = place[index]
            row = row_of(owner // 2, plane, owner % 2, rows)
            out[index * rows : (index + 1) * rows] = total[pl.ds(row, rows)]


def in_grads(place, near, far, grad_qkv):
    columns = grad_qkv.shape[1]
    shape = (near.shape[1] // 4, columns)
    return pl.pallas_call(
        in_grads_kernel,
        in_specs=[pl.BlockSpec(memory_space=pltpu.SMEM)]
        + [pl.BlockSpec(memory_space=pltpu.VMEM)] * 3,
        out_specs=[pl.BlockSpec(memory_space=pltpu.VMEM)] * 4,
        out_shape=[jax.ShapeDtypeStruct(shape, bf16)] * 4,
        scratch_shapes=[pltpu.VMEM((near.shape[1], columns), bf16)],
        compiler_params=pltpu.CompilerParams(vmem_limit_bytes=16 * 2**20),
        cost_estimate=pl.CostEstimate(
            flops=4 * near.shape[0] * near.shape[1] * columns,
            bytes_accessed=4 * 2**20,
            transcendentals=0,
        ),
    )(place, near, far, grad_qkv)


def add_in_kernel(own, lower, upper, opposite, near, far):
    total = sum_of_four([own, lower, upper, opposite]).astype(bf16)
    half = near.shape[0]
    near[...] = total[:half]
    far[...] = total[half:]


def combine_kernel(near_part, arrived, own, x_part, y_part, xy_part):
    rows = own.shape[0]
    own[...] = near_part[:rows] + arrived[:rows].astype(f32)
    for bits, out in ((1, x_part), (2, y_part), (3, xy_part)):
        block = slice(bits * rows, (bits + 1) * rows)
        out[...] = (near_part[block] + arrived[block].astype(f32)).astype(bf16)


def added(own, x_part, y_part, xy_part):
    return (own[...] + x_part[...].astype(f32)) + (
        y_part[...].astype(f32) + xy_part[...].astype(f32)
    )


def close_kernel(kept, own, x_part, y_part, xy_part, hidden, units):
    total = kept[...] + added(own, x_part, y_part, xy_part)
    hidden[...] = total
    units[...] = (total * inverse_rms(total)).astype(bf16)


def close_gain_kernel(kept, own, x_part, y_part, xy_part, gain, hidden, normed):
    total = kept[...] + added(own, x_part, y_part, xy_part)
    hidden[...] = total
    normed[...] = (total * inverse_rms(total) * gain[...]).astype(bf16)


def last_kernel(kept, own, x_part, y_part, xy_part, hidden):
    hidden[...] = (kept[...] + added(own, x_part, y_part, xy_part)).astype(bf16)


def middle_back_kernel(
    upstream, own, x_part, y_part, xy_part, middle, gain, grad_middle, branch, grad_gain
):
    grad_normed = added(own, x_part, y_part, xy_part)
    inverse = inverse_rms(middle[...])
    grad_gain[...] = jnp.sum(grad_normed * middle[...] * inverse, axis=0, keepdims=True)
    total = upstream[...].astype(f32) + unit_norm_back(
        middle[...], inverse, grad_normed * gain[...]
    )
    grad_middle[...] = total
    branch[...] = total.astype(bf16)


def layer_back_kernel(grad_middle, own, x_part, y_part, xy_part, hidden, upstream, low):
    total = grad_middle[...] + unit_norm_back(
        hidden[...], inverse_rms(hidden[...]), added(own, x_part, y_part, xy_part)
    )
    upstream[...] = total
    low[...] = total.astype(bf16)


def pair_kernel(axis, near, arrived, *outs):
    rows = near.shape[0] // len(outs)
    for index, out in enumerate(outs):
        block = slice(index * rows, (index + 1) * rows)
        if axis == 0:
            out[:rows] = near[block]
            out[rows:] = arrived[block]
        else:
            columns = near.shape[1]
            out[:, :columns] = near[block]
            out[:, columns:] = arrived[block]


def join_kernel(*refs):
    out, rows = refs[-1], refs[0].shape[0]
    for index, ref in enumerate(refs[:-1]):
        out[index * rows : (index + 1) * rows] = ref[...]


def unit_kernel(tokens, hidden, units):
    total = tokens[...].astype(f32)
    hidden[...] = total
    units[...] = (total * inverse_rms(total)).astype(bf16)


def ends_kernel(planes, place, gain_0, gain_1, table_0, table_1, out):
    devices = out.shape[0]
    blocks = planes * 2
    buckets = table_0.shape[0] // blocks
    at_head = place[0] // 2
    out[...] = jnp.zeros_like(out)
    total = table_0[...] + table_1[...]
    features = gain_0.shape[1] // devices
    for device in range(devices):
        chunk = slice(device * features // tile * tile, device * features // tile * tile + tile)
        out[device, 0:1] = gain_0[:, chunk]
        out[device, 1:2] = gain_1[:, chunk]
    for block in range(blocks):
        out[at_head * blocks + block, 2 : 2 + buckets] = total[
            block * buckets : (block + 1) * buckets
        ]


def finish_in_kernel(layers, place, *refs):
    shares, (attn_in, gains, ends, grad_in, grad_gain, grad_table) = (
        refs[: 4 * layers], refs[4 * layers :],
    )
    rows = attn_in.shape[1]
    summed = ends[0]
    for source in range(1, ends.shape[0]):
        summed = summed + ends[source]
    grad_table[...] = summed[2 : 2 + grad_table.shape[0]]
    first = ((place[0] // 2 * 4 + place[8]) * 2 + place[0] % 2) * rows % tile
    own = first + lax.broadcasted_iota(jnp.int32, (rows, tile), 0) == lax.broadcasted_iota(
        jnp.int32, (rows, tile), 1
    )
    width = shares[0].shape[1] // 6
    members = attn_in.shape[2] // (3 * width)
    for layer_id in range(layers):
        row_dot = jnp.zeros((rows, 1), f32)
        for index in range(members):
            share = shares[4 * layer_id + index % 4]
            member = place[index]
            for part in range(3):
                at = (index // 4 * 3 + part) * width
                block = share[:, at : at + width].astype(f32)
                columns = pl.ds(pl.multiple_of((part * members + member) * width, width), width)
                grad_in[layer_id, :, columns] = block * gains[layer_id]
                row_dot = row_dot + jnp.sum(
                    block * attn_in[layer_id, :, columns].astype(f32), axis=1, keepdims=True
                )
        ff_gain = jnp.sum(
            jnp.where(own, summed[layer_id : layer_id + 1], 0.0), axis=1, keepdims=True
        )
        grad_gain[layer_id] = jnp.concatenate([row_dot, ff_gain], axis=1)


def sum_of_four(parts):
    return (parts[0][...].astype(f32) + parts[1][...].astype(f32)) + (
        parts[2][...].astype(f32) + parts[3][...].astype(f32)
    )


def finish_ff_kernel(*refs):
    grad_up, grad_down = refs[-2:]
    columns = grad_up.shape[2]
    for layer_id in range(grad_up.shape[0]):
        total = sum_of_four(refs[4 * layer_id : 4 * layer_id + 4])
        grad_up[layer_id] = total[:, :columns]
        grad_down[layer_id] = total[:, columns:]


def finish_out_kernel(*refs):
    for layer_id in range(refs[-1].shape[0]):
        refs[-1][layer_id] = sum_of_four(refs[4 * layer_id : 4 * layer_id + 4])


def inverse_rms(hidden):
    return lax.rsqrt(jnp.mean(hidden * hidden, axis=-1, keepdims=True) + epsilon)


def prepare(bias_table, first_head, heads_dev):
    table = lax.dynamic_slice_in_dim(bias_table, first_head, heads_dev, 1)
    (near,) = call(near_kernel, [((heads_dev, tile, 3 * tile), f32)], table, smem=1)
    return table, near


def bucket_grads(first_lane, grads, bucket_count):
    (total,) = call(bucket_kernel, [((bucket_count, tile), f32)], first_lane, *grads, smem=1)
    return total


def gelu_parts(pre_act):
    cumulative = 0.5 * (1.0 + lax.erf(pre_act * np.float32(0.5**0.5)))
    slope = cumulative + pre_act * jnp.exp(-0.5 * pre_act * pre_act) * np.float32(
        (2 * np.pi) ** -0.5
    )
    return (pre_act * cumulative).astype(bf16), slope


def unit_norm_back(hidden, inverse, grad_unit):
    unit = hidden * inverse
    return inverse * (grad_unit - unit * jnp.mean(grad_unit * unit, axis=-1, keepdims=True))


def gather_rows(block, axes):
    return lax.all_gather(block, axes, axis=0, tiled=True)


def toggle(array, axis, bits):
    return lax.ppermute(array, axis, [(i, i ^ bits) for i in range(lax.axis_size(axis))])


def shift(array, by):
    planes = lax.axis_size("z")
    return lax.ppermute(array, "z", [(i, (i + by) % planes) for i in range(planes)])


def plane_gather(block, *holds):
    near = jnp.concatenate([block] + [toggle(block, "head", bits) for bits in (1, 2, 3)])
    near, *holds = tie(near, *holds)
    return (near, toggle(near, "core", 1), *holds)


def plane_scatter(near_part, far_part, *holds):
    rows, columns = near_part.shape[0] // 4, near_part.shape[1]
    arrived, *holds = tie(toggle(far_part, "core", 1), *holds)
    own, *others = call(
        combine_kernel,
        [((rows, columns), f32)] + [((rows, columns), bf16)] * 3,
        near_part,
        arrived,
    )
    shares = [own] + [toggle(other, "head", bits) for bits, other in zip((1, 2, 3), others)]
    return (shares, own, *holds)


def tie(*arrays):
    return lax.optimization_barrier(arrays)


def after(array, other):
    return lax.optimization_barrier((array, other))[0]


def scatter_sum(partial, axes, members):
    blocks = partial.astype(bf16).reshape(members, -1, partial.shape[1])
    return jnp.sum(lax.all_to_all(blocks, axes, 0, 0, tiled=True).astype(f32), axis=0)


def local_general(tokens, doc_start, bias_table, attn_in, attn_out, ff_in, ff_out, gains, cotangent):
    heads_n, z_n, core_n = (lax.axis_size(axis) for axis in everyone)
    devices = heads_n * z_n * core_n
    group, spare = ("z", "core"), "head"
    ff_group, ff_spare, ff_members = ("head", "core"), "z", heads_n * core_n
    blocks = z_n * core_n
    block_rows, model_width = tokens.shape[1:]
    layer_count, weight_rows = attn_in.shape[:2]
    length = block_rows * blocks
    heads_all = bias_table.shape[1]
    member = lax.axis_index("z") * core_n + lax.axis_index("core")
    heads_dev = max(1, heads_all // blocks)
    head_groups = heads_all // heads_dev
    split = blocks // head_groups
    head_group, query_part = member // split, member % split
    query_rows = length // split
    width = heads_dev * head_dim
    first = (query_part * (query_rows // tile)).astype(jnp.int32).reshape(1)
    place = jnp.arange(length // tile, dtype=jnp.int32)
    out_row = head_group * width

    def swap(array):
        return lax.all_to_all(array, everyone, 0, 0, tiled=True)

    starts = jnp.broadcast_to(
        doc_start.astype(f32)[:, None], (heads_n, blocks, block_rows)
    ).reshape(devices, block_rows)
    ff_gains = gains[:, :, 1].astype(f32).reshape(1, -1)
    small = swap(
        jnp.concatenate(
            [starts, jnp.broadcast_to(ff_gains, (devices, layer_count * weight_rows))], axis=1
        )
    )
    doc_row = small[:blocks, :block_rows].reshape(1, length)
    doc_col = lax.dynamic_slice_in_dim(
        doc_row.reshape(length, 1), query_part * query_rows, query_rows, 0
    )
    gain_ff = jnp.transpose(
        small[:, block_rows:].reshape(devices, layer_count, weight_rows), (1, 0, 2)
    ).reshape(layer_count, 1, model_width)
    table, near = prepare(bias_table, head_group * heads_dev, heads_dev)

    gain_attn = gains[:, :, 0].astype(f32)[:, :, None]
    own_in = attn_in.astype(f32)

    def fetch_in(layer_id):
        scaled = (own_in[layer_id] * gain_attn[layer_id]).astype(bf16)
        columns = jnp.transpose(
            scaled.reshape(weight_rows, 3, head_groups, width), (2, 0, 1, 3)
        ).reshape(head_groups, weight_rows, 3 * width)
        columns = jnp.repeat(columns, split, axis=0)
        columns = jnp.broadcast_to(columns[None], (heads_n, *columns.shape))
        return swap(columns.reshape(devices, weight_rows, 3 * width)).reshape(
            model_width, 3 * width
        )

    def fetch_ff(layer_id):
        pair = jnp.concatenate([ff_in[layer_id], ff_out[layer_id]], axis=1)
        pair = gather_rows(pair, ff_spare)
        return pair[:, :model_width], pair[:, model_width:]

    hidden, upstream = tokens[0].astype(f32), cotangent[0]
    weights_in = [fetch_in(layer_id) for layer_id in range(layer_count)]
    weights_out = lax.dynamic_slice_in_dim(
        lax.all_gather(attn_out, everyone, axis=1, tiled=True), out_row, width, 1
    )
    weights_ff = [fetch_ff(layer_id) for layer_id in range(layer_count)]

    records = []
    for layer_id in range(layer_count):
        w_in, w_out, (w_up, w_down) = (
            weights_in[layer_id], weights_out[layer_id], weights_ff[layer_id],
        )
        inverse = inverse_rms(hidden)
        units = gather_rows((hidden * inverse).astype(bf16), group)
        qkv = jnp.dot(units, w_in, preferred_element_type=f32).astype(bf16)
        attended, _, stats = attention(
            qkv, doc_row, doc_col, first, place, table, near, query_rows
        )
        mixed = jnp.dot(attended, w_out, preferred_element_type=f32)
        if split > 1:
            mixed = lax.dynamic_update_slice_in_dim(
                jnp.zeros((length, model_width), f32), mixed, query_part * query_rows, 0
            )
        middle = hidden + scatter_sum(mixed, group, blocks)
        inverse_ff = inverse_rms(middle)
        normed_ff = gather_rows((middle * inverse_ff * gain_ff[layer_id]).astype(bf16), ff_group)
        activated, slope = gelu_parts(contract(normed_ff, w_up, 1, 1))
        ff_result = jnp.dot(activated, w_down, preferred_element_type=f32)
        records.append(
            (hidden, inverse, units, qkv, attended, stats, middle, inverse_ff, normed_ff,
             activated, slope)
        )
        hidden = middle + scatter_sum(ff_result, ff_group, ff_members)
    output = hidden

    grads_ff, grads_in, grads_out, grads_gain_ff, grads_table = (
        [None] * layer_count for _ in range(5)
    )
    for layer_id in reversed(range(layer_count)):
        w_in, w_out, (w_up, w_down) = (
            weights_in[layer_id], weights_out[layer_id], weights_ff[layer_id],
        )
        (hidden, inverse, units, qkv, attended, stats, middle, inverse_ff, normed_ff,
         activated, slope) = records[layer_id]
        grad_low = gather_rows(upstream.astype(bf16), ff_group)
        grad_pre = (contract(grad_low, w_down, 1, 1) * slope).astype(bf16)
        grad_normed = scatter_sum(
            jnp.dot(grad_pre, w_up, preferred_element_type=f32), ff_group, ff_members
        )
        grad_pair = jnp.concatenate(
            [contract(grad_pre, normed_ff, 0, 0), contract(activated, grad_low, 0, 0)], axis=1
        ).astype(bf16)
        grads_ff[layer_id] = lax.psum_scatter(
            grad_pair, ff_spare, scatter_dimension=0, tiled=True
        ).astype(f32)
        grads_gain_ff[layer_id] = jnp.sum(grad_normed * middle * inverse_ff, axis=0)
        grad_middle = upstream + unit_norm_back(
            middle, inverse_ff, grad_normed * gain_ff[layer_id]
        )
        branch = gather_rows(grad_middle.astype(bf16), group)
        if split > 1:
            branch = lax.dynamic_slice_in_dim(branch, query_part * query_rows, query_rows, 0)
        grad_attended = contract(branch, w_out, 1, 1).astype(bf16)
        grad_qkv, grad_near, grad_far = attention_back(
            qkv, doc_row, doc_col, attended, grad_attended, stats, first, place, table, near, split
        )
        grads_table[layer_id] = (grad_near, grad_far)
        grad_units = scatter_sum(contract(grad_qkv, w_in, 1, 1), group, blocks)
        upstream = grad_middle + unit_norm_back(hidden, inverse, grad_units)
        grad_out = lax.dynamic_update_slice_in_dim(
            jnp.zeros((model_width, model_width), bf16),
            contract(attended, branch, 0, 0).astype(bf16),
            out_row,
            0,
        )
        grads_out[layer_id] = lax.psum_scatter(
            grad_out, everyone, scatter_dimension=0, tiled=True
        ).astype(f32)
        grads_in[layer_id] = contract(units, grad_qkv, 0, 0).astype(bf16)

    bucket_count = table.shape[0]
    grad_table = sum(
        bucket_grads(jnp.zeros((1,), jnp.int32), entry, bucket_count) for entry in grads_table
    )[:, :heads_dev]
    grad_table = lax.dynamic_update_slice_in_dim(
        jnp.zeros((bucket_count, heads_all), f32), grad_table, head_group * heads_dev, 1
    )
    grad_table = jnp.transpose(
        grad_table.reshape(blocks, bucket_count // blocks, heads_n, heads_all // heads_n),
        (2, 0, 1, 3),
    ).reshape(devices, -1)
    grad_gain_ff = jnp.transpose(
        jnp.stack(grads_gain_ff).reshape(layer_count, devices, weight_rows), (1, 0, 2)
    ).reshape(devices, -1)
    ends = jnp.sum(swap(jnp.concatenate([grad_gain_ff, grad_table], axis=1)), axis=0)
    grad_gain_ff = ends[: layer_count * weight_rows].reshape(layer_count, weight_rows)
    grad_bias_table = ends[layer_count * weight_rows :].reshape(
        bucket_count // blocks, heads_all // heads_n
    )
    grads_attn_in, grads_gains = [], []
    for layer_id in range(layer_count):
        parts = swap(grads_in[layer_id].reshape(devices, weight_rows, 3 * width)).astype(f32)
        parts = jnp.sum(parts.reshape(heads_n, blocks, weight_rows, 3 * width), axis=0)
        parts = jnp.sum(parts.reshape(head_groups, split, weight_rows, 3, width), axis=1)
        unit_grad = jnp.transpose(parts, (1, 2, 0, 3)).reshape(weight_rows, 3 * model_width)
        grads_attn_in.append(unit_grad * gain_attn[layer_id])
        grads_gains.append(
            jnp.stack(
                [jnp.sum(unit_grad * own_in[layer_id], axis=1), grad_gain_ff[layer_id]], axis=1
            )
        )
    return (
        output[None],
        upstream[None],
        jnp.stack(grads_attn_in),
        jnp.stack(grads_out),
        jnp.stack([entry[:, :model_width] for entry in grads_ff]),
        jnp.stack([entry[:, model_width:] for entry in grads_ff]),
        jnp.stack(grads_gains),
        grad_bias_table,
    )


def local_plane(tokens, doc_start, bias_table, attn_in, attn_out, ff_in, ff_out, gains, cotangent):
    heads_n, z_n, core_n = (lax.axis_size(axis) for axis in everyone)
    devices = heads_n * z_n * core_n
    at_head, at_z, at_core = (lax.axis_index(axis) for axis in everyone)
    members = heads_n * core_n
    block_rows, model_width = tokens.shape[1:]
    layer_count, weight_rows = attn_in.shape[:2]
    length = block_rows * members
    heads_all = bias_table.shape[1]
    heads_dev = heads_all // members
    width = heads_dev * head_dim
    member = at_head * core_n + at_core
    turn = [
        ((h * z_n + z) * core_n + c, (z * z_n + h) * core_n + c)
        for h in range(heads_n)
        for z in range(z_n)
        for c in range(core_n)
    ]
    place = jnp.stack(
        [
            (at_head ^ bits) * core_n + (at_core ^ other)
            for other in range(core_n)
            for bits in range(heads_n)
        ]
        + [at_z]
    ).astype(jnp.int32)

    def relay(array):
        return lax.ppermute(array, everyone, turn)

    def swap(array):
        return lax.all_to_all(array, everyone, 0, 0, tiled=True)

    row_shape = (block_rows, model_width)
    share_shape = (members // 2 * weight_rows, 3 * width)
    gain_attn = gains[:, :, 0].astype(f32)[:, :, None]
    first_share, near_share, far_share = call(
        functools.partial(share_in_kernel, z_n, core_n),
        [((devices, weight_rows, 3 * width), bf16)] + [(share_shape, bf16)] * 2,
        place,
        attn_in,
        gain_attn,
        smem=1,
    )

    quarter_turns = [
        [
            (z * core_n + c, (2 * c + (a ^ z % 2)) * core_n + (b ^ z // 2))
            for z in range(z_n)
            for c in range(core_n)
        ]
        for a in range(2)
        for b in range(2)
    ]

    def fetch_out(layer_id, hold):
        held = after(attn_out[layer_id], hold)
        return [
            lax.ppermute(held, ("z", "core"), [(holder, user) for user, holder in turns])
            for turns in quarter_turns
        ]

    starts = jnp.broadcast_to(
        doc_start.astype(f32)[None, :, None], (heads_n, z_n, core_n, block_rows)
    )
    ff_gains = gains[:, :, 1].astype(f32).reshape(1, -1)
    small = jnp.concatenate(
        [
            starts.reshape(devices, block_rows),
            jnp.broadcast_to(ff_gains, (devices, layer_count * weight_rows)),
        ],
        axis=1,
    )
    table, strip = prepare(bias_table, member * heads_dev, heads_dev)
    hidden, small, strip = tie(relay(tokens[0]), swap(small), strip)
    doc_row = small[:members, :block_rows].reshape(2, 2, core_n, block_rows)
    for axis, bit in ((0, at_head // 2), (1, at_head % 2), (2, at_core)):
        doc_row = jnp.where(bit == 1, jnp.flip(doc_row, axis), doc_row)
    doc_row = jnp.transpose(doc_row, (2, 0, 1, 3)).reshape(1, length)
    doc_col = doc_row.reshape(length, 1)
    gain_ff = jnp.transpose(
        small[:, block_rows:].reshape(devices, layer_count, weight_rows), (1, 0, 2)
    ).reshape(layer_count, 1, model_width)

    def round_planes(array, by, hold):
        return shift(after(array, hold), by)

    def fetch_ff(layer_id, by, hold):
        return [round_planes(array[layer_id], by, hold) for array in (ff_in, ff_out)]

    def ff_first(rows, layer_id, lower, upper, opposite, kind):
        parts = [
            part
            for side, array in enumerate((ff_in, ff_out))
            for part in (array[layer_id], lower[side], upper[side], opposite[side])
        ]
        units = 4 * ff_in.shape[1]
        return by_rows(
            ff_first_kernel,
            256,
            [rows],
            parts,
            [(units, bf16), (units, bf16), (model_width, kind)],
            [(units, 2 * model_width)],
        )

    def ff_forward(normed, layer_id, *weights):
        *near, pair = ff_first(normed[0], layer_id, *weights, f32)
        units = pair.shape[0]
        far = by_rows(
            ff_kernel,
            256,
            [normed[1]],
            [pair],
            [(units, bf16), (units, bf16), (model_width, bf16)],
        )
        return pair, *zip(near, far)

    def ff_backward(low, slopes, pair):
        return zip(
            *(
                by_rows(
                    ff_back_kernel,
                    256,
                    [rows, slope],
                    [pair],
                    [(pair.shape[0], bf16), (model_width, kind)],
                )
                for rows, slope, kind in zip(low, slopes, (f32, bf16))
            )
        )

    def pair_chips(near, arrived, axis):
        rows, columns = near.shape[0] // 4, near.shape[1]
        shape = (2 * rows, columns) if axis == 0 else (rows, 2 * columns)
        return call(functools.partial(pair_kernel, axis), [(shape, bf16)] * 4, near, arrived)

    def share_chips(blocks):
        return [blocks[0]] + [toggle(blocks[bits], "head", bits) for bits in (1, 2, 3)]

    units_shape = [(row_shape, f32), (row_shape, bf16)]
    hidden, unit_rows = call(unit_kernel, units_shape, hidden)

    near, far, w_in, quarters, doc_row, doc_col, gain_ff = plane_gather(
        unit_rows,
        swap(first_share),
        fetch_out(0, hidden),
        doc_row,
        doc_col,
        gain_ff,
    )
    units = (near, far)
    w_in = w_in.reshape(model_width, 3 * width)
    w_out, qkv, attended, stats, *parts = plane_attention(
        *units, w_in, quarters, doc_row, doc_col, place, table, strip
    )
    parts, own, lower, upstream, far_share = plane_scatter(
        *parts,
        fetch_ff(0, 1, near),
        relay(after(cotangent[0].astype(bf16), near)),
        toggle(after(far_share, near), "core", 1),
    )
    parts, upper, shares = tie(
        parts, fetch_ff(0, -1, own), pair_chips(near_share, after(far_share, own), 0)
    )
    middle, normed_rows = call(close_gain_kernel, units_shape, hidden, *parts, gain_ff[0])
    near, far, opposite, shares = plane_gather(
        normed_rows, fetch_ff(0, 2, normed_rows), share_chips(after(shares, normed_rows))
    )
    normed = (near, far)
    pair, acts, slopes, parts = ff_forward(normed, 0, lower, upper, opposite)
    records = [
        (hidden, units, w_in, w_out, pair, qkv, attended, stats, middle, normed, acts, slopes)
    ]
    (share,) = call(join_kernel, [((weight_rows * members, 3 * width), bf16)], *shares)
    parts, own, lower_in = plane_scatter(*parts, round_planes(ff_in[1], 1, near))
    parts, *shares = tie(
        parts, round_planes(share, 1, own), round_planes(share, -1, own)
    )
    hidden, unit_rows = call(close_kernel, units_shape, middle, *parts)

    near, far, opposite, quarters = plane_gather(
        unit_rows, round_planes(share, 2, unit_rows), fetch_out(1, unit_rows)
    )
    units = (near, far)
    (w_in,) = call(
        assemble_in_kernel,
        [((model_width, 3 * width), bf16)],
        place,
        share,
        *shares,
        opposite,
        smem=1,
    )
    w_out, qkv, attended, stats, *parts = plane_attention(
        *units, w_in, quarters, doc_row, doc_col, place, table, strip
    )
    low = plane_gather(after(upstream, far))
    parts, own, near_low, lower_out, upper = plane_scatter(
        *parts, low[0], round_planes(ff_out[1], 1, far), fetch_ff(1, -1, far)
    )
    low = (near_low, low[1])
    parts, opposite_in = tie(parts, round_planes(ff_in[1], 2, own))
    middle, normed_rows = call(close_gain_kernel, units_shape, hidden, *parts, gain_ff[1])
    near, far, opposite_out = plane_gather(normed_rows, round_planes(ff_out[1], 2, normed_rows))
    normed = (near, far)
    pair, acts, slopes, last_parts = ff_forward(
        normed, 1, [lower_in, lower_out], upper, [opposite_in, opposite_out]
    )
    records.append(
        (hidden, units, w_in, w_out, pair, qkv, attended, stats, middle, normed, acts, slopes)
    )

    def back_to_middle(parts, upstream, middle, gain):
        return call(
            middle_back_kernel, units_shape + [((1, model_width), f32)], upstream, *parts, middle, gain
        )

    def attention_grads(record, branch):
        _, _, w_in, w_out, _, qkv, attended, stats, *_ = record
        grad_qkv, grad_near, grad_far, near_part, far_part, *quarters = plane_attention_back(
            qkv, doc_row, doc_col, attended, stats, *branch, w_in, w_out, place, table, strip
        )
        return grad_qkv, (grad_near, grad_far), (near_part, far_part), quarters

    def owners_quarters(quarters):
        return [
            lax.ppermute(quarter, ("z", "core"), turns)
            for quarter, turns in zip(quarters, quarter_turns)
        ]

    def table_grads(near_and_far):
        return bucket_grads(at_core.reshape(1) * heads_dev, near_and_far, table.shape[0])

    def add_in(own, lower, upper, opposite):
        return call(add_in_kernel, [(share_shape, bf16)] * 2, own, lower, upper, opposite)

    record = records[1]
    hidden, units, _, _, pair, *_, middle, normed, acts, slopes = record
    pres, parts = ff_backward(low, slopes, pair)
    parts, own = plane_scatter(*parts)
    planes = ff_grads(after(pres, own), acts, normed, low)
    parts, ff_lower = tie(parts, shift(planes[1], -1))
    last_parts, _ = plane_scatter(*after(last_parts, parts))
    grad_middle, branch_rows, gain_1 = back_to_middle(parts, upstream, middle, gain_ff[1])
    *branch, ff_upper = plane_gather(branch_rows, round_planes(planes[2], 1, branch_rows))
    grad_qkv, strips_1, parts, quarters = attention_grads(record, branch)
    parts, own, last_parts, ff_opposite = plane_scatter(
        *parts, last_parts, round_planes(planes[3], 2, branch[1])
    )
    grads_ff = [planes[0], ff_lower, ff_upper, ff_opposite]
    grad_in = in_grads(place, *units, after(grad_qkv, own))
    parts, in_lower, in_upper, quarters_1, output, table_1 = tie(
        parts,
        shift(grad_in[1], -1),
        shift(grad_in[2], 1),
        owners_quarters(after(quarters, own)),
        call(last_kernel, [(row_shape, bf16)], middle, *after(last_parts, own))[0],
        table_grads(after(strips_1, own)),
    )
    upstream, low_rows = call(layer_back_kernel, units_shape, grad_middle, *parts, hidden)

    record = records[0]
    hidden, units, _, _, pair, *_, middle, normed, acts, slopes = record
    *low, in_opposite = plane_gather(low_rows, round_planes(grad_in[3], 2, low_rows))
    near_in, far_in = add_in(grad_in[0], in_lower, in_upper, in_opposite)
    pres, parts = ff_backward(low, slopes, pair)
    parts, own, far_in = plane_scatter(*parts, toggle(far_in, "core", 1))
    planes = ff_grads(after(pres, own), acts, normed, low)
    parts, ff_lower, shares_1 = tie(
        parts, shift(planes[1], -1), pair_chips(near_in, after(far_in, own), 1)
    )
    grad_middle, branch_rows, gain_0 = back_to_middle(parts, upstream, middle, gain_ff[0])
    *branch, ff_upper, shares_1 = plane_gather(
        branch_rows,
        round_planes(planes[2], 1, branch_rows),
        share_chips(after(shares_1, branch_rows)),
    )
    grad_qkv, strips_0, parts, quarters = attention_grads(record, branch)
    parts, own, output, ff_opposite = plane_scatter(
        *parts, relay(after(output, branch[1])), round_planes(planes[3], 2, branch[1])
    )
    grads_ff = [planes[0], ff_lower, ff_upper, ff_opposite] + grads_ff
    grad_in = in_grads(place, *units, after(grad_qkv, own))
    parts, in_opposite, in_lower, in_upper, table_0, output, (grad_up, grad_down) = tie(
        parts,
        shift(grad_in[3], 2),
        shift(grad_in[1], -1),
        shift(grad_in[2], 1),
        table_grads(after(strips_0, own)),
        after(output, own).astype(f32),
        call(finish_ff_kernel, [(ff_in.shape, f32)] * 2, *after(grads_ff, own)),
    )
    upstream, low_rows = call(layer_back_kernel, units_shape, grad_middle, *parts, hidden)
    grad_tokens = relay(low_rows)
    quarters_0 = owners_quarters(after(quarters, low_rows))
    near_in, far_in = add_in(*after([grad_in[0], in_lower, in_upper, in_opposite], low_rows))
    shares_0 = share_chips(pair_chips(near_in, toggle(far_in, "core", 1), 1))
    (ends,) = call(
        functools.partial(ends_kernel, z_n),
        [((devices, 8, tile), f32)],
        place,
        *after([gain_0, gain_1, table_0, table_1], low_rows),
        smem=1,
    )
    (grad_attn_out,) = call(finish_out_kernel, [(attn_out.shape, f32)], *quarters_0, *quarters_1)
    own_buckets = table.shape[0] // (z_n * core_n)
    grad_attn_in, grad_gains, grad_table = call(
        functools.partial(finish_in_kernel, layer_count),
        [(attn_in.shape, f32), (gains.shape, f32), ((own_buckets, tile), f32)],
        place,
        *shares_0,
        *shares_1,
        attn_in,
        gain_attn,
        swap(ends),
        smem=1,
    )
    return (
        output[None],
        grad_tokens.astype(f32)[None],
        grad_attn_in,
        grad_attn_out,
        grad_up,
        grad_down,
        grad_gains,
        grad_table[:, : heads_all // heads_n],
    )


def solution(mesh):
    sizes = dict(mesh.shape)
    cores = 2
    fine = Mesh(
        mesh.devices.reshape(sizes["head"], sizes["blk"] // cores, cores), everyone
    )
    blk = ("z", "core")
    in_specs = (
        P("head", blk, None),
        P(None, blk),
        P(),
        P(None, everyone, None),
        P(None, everyone, None),
        P(None, everyone, None),
        P(None, everyone, None),
        P(None, everyone, None),
        P("head", blk, None),
    )
    out_specs = (
        P("head", blk, None),
        P("head", blk, None),
        P(None, everyone, None),
        P(None, everyone, None),
        P(None, everyone, None),
        P(None, everyone, None),
        P(None, everyone, None),
        P(blk, "head"),
    )
    plane = sizes["head"] == 4 and sizes["blk"] == 8
    local = local_plane if plane else local_general
    return jax.shard_map(local, mesh=fine, in_specs=in_specs, out_specs=out_specs, check_vma=False)
```

```python
import functools

import jax
import jax.numpy as jnp
import numpy as np
from jax import lax
from jax.experimental import pallas as pl
from jax.experimental.pallas import tpu as pltpu
from jax.sharding import Mesh
from jax.sharding import PartitionSpec as P

bounds = (1, 2, 3, 4, 5, 6, 7, 8, 12, 16, 23, 32, 46, 64, 91)
epsilon = 1e-06
masked = -1e30
score_scale = 0.125
head_dim = 64
tile = 128
everyone = ("head", "z", "core")
bf16 = jnp.bfloat16
f32 = jnp.float32


def contract(lhs, rhs, lhs_dim, rhs_dim):
    return lax.dot_general(
        lhs, rhs, (((lhs_dim,), (rhs_dim,)), ((), ())), preferred_element_type=f32
    )


def near_buckets(shape):
    offsets = (
        lax.broadcasted_iota(jnp.int32, shape, 1) - tile - lax.broadcasted_iota(jnp.int32, shape, 0)
    )
    distance = jnp.abs(offsets)
    bucket = jnp.where(offsets > 0, 16, 0)
    for boundary in bounds:
        bucket = bucket + jnp.where(distance >= boundary, 1, 0)
    return bucket


def near_kernel(table, near):
    bucket = near_buckets(near.shape[1:])
    for head in range(near.shape[0]):
        values = jnp.zeros(near.shape[1:], f32)
        for bucket_id in range(table.shape[0]):
            values = jnp.where(bucket == bucket_id, table[bucket_id, head], values)
        near[head] = values


def bucket_kernel(first_lane, near, far, out):
    bucket = near_buckets(near.shape[1:])
    rows = lax.broadcasted_iota(jnp.int32, out.shape, 0)
    lanes = lax.broadcasted_iota(jnp.int32, out.shape, 1)
    total = jnp.zeros(out.shape, f32)
    for head in range(near.shape[0]):
        strip = near[head]
        for bucket_id in range(out.shape[0]):
            value = jnp.sum(jnp.where(bucket == bucket_id, strip, 0.0), axis=0, keepdims=True)
            value = jnp.sum(value, axis=1, keepdims=True)
            if bucket_id in (15, 31):
                value = value + far[head, bucket_id // 16, :1, :1]
            total = jnp.where((rows == bucket_id) & (lanes == head + first_lane[0]), value, total)
    out[...] = total


def fill_band(band, table, near, heads_dev, length):
    for head in range(heads_dev):
        band[head, :, : length - tile] = jnp.full((tile, length - tile), table[15, head], f32)
        band[head, :, length - tile : length + 2 * tile] = near[head]
        band[head, :, length + 2 * tile :] = jnp.full(
            (tile, length - 2 * tile), table[31, head], f32
        )


def band_starts(place, at, length, skip=0):
    return [
        pl.multiple_of(length + (place[skip + block] - place[skip + at]) * tile, tile)
        for block in range(length // tile)
    ]


def attention_kernel(
    heads_dev, length, first, place, table, near, qkv, doc_row, doc_col, out, local, stats, band
):
    step = pl.program_id(0)
    width = heads_dev * head_dim

    @pl.when(step == 0)
    def _():
        fill_band(band, table, near, heads_dev, length)

    row = pl.multiple_of((first[0] + step) * tile, tile)
    out_row = pl.multiple_of((place[first[0] + step] - first[0]) * tile, tile)
    starts = band_starts(place, first[0] + step, length)
    same_doc = doc_col[...] == doc_row[...]
    queries = qkv[pl.ds(row, tile), :width] * bf16(score_scale)
    lanes = lax.broadcasted_iota(jnp.int32, (tile, tile), 1)
    collected = jnp.zeros((tile, tile), f32)
    for head in range(heads_dev):
        own = slice(head * head_dim, (head + 1) * head_dim)
        keys = qkv[:, width + own.start : width + own.stop]
        values = qkv[:, 2 * width + own.start : 2 * width + own.stop]
        scores = contract(queries[:, own], keys, 1, 1)
        scores = scores + jnp.concatenate(
            [band[head, :, pl.ds(start, tile)] for start in starts], axis=1
        )
        scores = jnp.where(same_doc, scores, masked)
        peak = jnp.max(scores, axis=1, keepdims=True)
        weights = jnp.exp(scores - peak)
        total = jnp.sum(weights, axis=1, keepdims=True)
        mixed = contract(weights.astype(bf16), values, 1, 0) / total
        out[pl.ds(out_row, tile), own] = mixed.astype(bf16)
        local[:, own] = mixed.astype(bf16)
        collected = jnp.where(lanes == head, peak + jnp.log(total), collected)
    stats[...] = collected


def attention_back_kernel(
    heads_dev, length, split, first, place, table, near, qkv, doc_row, doc_col, attended, grad_out, stats,
    grad_qkv, grad_near, grad_far, band, grad_band, grad_keys, grad_values,
):
    step = pl.program_id(0)
    width = heads_dev * head_dim

    @pl.when(step == 0)
    def _():
        fill_band(band, table, near, heads_dev, length)
        grad_band[...] = jnp.zeros_like(grad_band)
        grad_keys[...] = jnp.zeros_like(grad_keys)
        grad_values[...] = jnp.zeros_like(grad_values)
        if split > 1:
            grad_qkv[...] = jnp.zeros_like(grad_qkv)

    row = pl.multiple_of((first[0] + step) * tile, tile)
    out_row = pl.multiple_of((place[first[0] + step] - first[0]) * tile, tile)
    starts = band_starts(place, first[0] + step, length)
    same_doc = doc_col[...] == doc_row[...]
    at_step = pl.multiple_of(step * tile, tile)
    queries = qkv[pl.ds(row, tile), :width] * bf16(score_scale)
    for head in range(heads_dev):
        own = slice(head * head_dim, (head + 1) * head_dim)
        keys = qkv[:, width + own.start : width + own.stop]
        values = qkv[:, 2 * width + own.start : 2 * width + own.stop]
        upstream = grad_out[pl.ds(out_row, tile), own]
        scores = contract(queries[:, own], keys, 1, 1) + jnp.concatenate(
            [band[head, :, pl.ds(start, tile)] for start in starts], axis=1
        )
        scores = jnp.where(same_doc, scores, masked)
        weights = jnp.exp(scores - stats[:, head : head + 1])
        delta = jnp.sum(
            upstream.astype(f32) * attended[pl.ds(at_step, tile), own].astype(f32),
            axis=1,
            keepdims=True,
        )
        grad_scores = weights * (contract(upstream, values, 1, 1) - delta)
        for block, start in enumerate(starts):
            grad_band[head, :, pl.ds(start, tile)] += grad_scores[
                :, block * tile : (block + 1) * tile
            ]
        grad_low = grad_scores.astype(bf16)
        grad_values[:, own] += contract(weights.astype(bf16), upstream, 0, 0)
        grad_keys[:, own] += contract(grad_low, queries[:, own], 0, 0)
        grad_qkv[pl.ds(row, tile), own] = (
            contract(grad_low, keys, 1, 0) * score_scale
        ).astype(bf16)

    @pl.when(step == pl.num_programs(0) - 1)
    def _():
        grad_qkv[:, width : 2 * width] = grad_keys[...].astype(bf16)
        grad_qkv[:, 2 * width :] = grad_values[...].astype(bf16)
        for head in range(heads_dev):
            grad_near[head] = grad_band[head, :, length - tile : length + 2 * tile]
            grad_far[head, 0] = jnp.full(
                (8, tile), jnp.sum(grad_band[head, :, : length - tile]), f32
            )
            grad_far[head, 1] = jnp.full(
                (8, tile), jnp.sum(grad_band[head, :, length + 2 * tile :]), f32
            )


def whole(shape):
    return pl.BlockSpec(shape, lambda step: (0,) * len(shape))


def attention(qkv, doc_row, doc_col, first, place, table, near, rows):
    length = qkv.shape[0]
    heads_dev = table.shape[1]
    width = heads_dev * head_dim
    return pl.pallas_call(
        functools.partial(attention_kernel, heads_dev, length),
        grid=(rows // tile,),
        in_specs=[
            pl.BlockSpec(memory_space=pltpu.SMEM),
            pl.BlockSpec(memory_space=pltpu.SMEM),
            pl.BlockSpec(memory_space=pltpu.SMEM),
            whole(near.shape),
            whole(qkv.shape),
            whole(doc_row.shape),
            pl.BlockSpec((tile, 1), lambda step: (step, 0)),
        ],
        out_specs=[
            whole((rows, width)),
            pl.BlockSpec((tile, width), lambda step: (step, 0)),
            pl.BlockSpec((tile, tile), lambda step: (step, 0)),
        ],
        out_shape=[
            jax.ShapeDtypeStruct((rows, width), bf16),
            jax.ShapeDtypeStruct((rows, width), bf16),
            jax.ShapeDtypeStruct((rows, tile), f32),
        ],
        scratch_shapes=[pltpu.VMEM((heads_dev, tile, 2 * length), f32)],
        compiler_params=pltpu.CompilerParams(vmem_limit_bytes=40 * 2**20),
        cost_estimate=pl.CostEstimate(
            flops=4 * rows * length * width,
            bytes_accessed=4 * length * width * 2,
            transcendentals=rows * length * heads_dev,
        ),
    )(first, place, table, near, qkv, doc_row, doc_col)


def attention_back(
    qkv, doc_row, doc_col, attended, grad_out, stats, first, place, table, near, split
):
    length = qkv.shape[0]
    rows = grad_out.shape[0]
    heads_dev = table.shape[1]
    width = heads_dev * head_dim
    return pl.pallas_call(
        functools.partial(attention_back_kernel, heads_dev, length, split),
        grid=(rows // tile,),
        in_specs=[
            pl.BlockSpec(memory_space=pltpu.SMEM),
            pl.BlockSpec(memory_space=pltpu.SMEM),
            pl.BlockSpec(memory_space=pltpu.SMEM),
            whole(near.shape),
            whole(qkv.shape),
            whole(doc_row.shape),
            pl.BlockSpec((tile, 1), lambda step: (step, 0)),
            whole((rows, width)),
            whole((rows, width)),
            pl.BlockSpec((tile, tile), lambda step: (step, 0)),
        ],
        out_specs=[
            whole((length, 3 * width)),
            whole((heads_dev, tile, 3 * tile)),
            whole((heads_dev, 2, 8, tile)),
        ],
        out_shape=[
            jax.ShapeDtypeStruct((length, 3 * width), bf16),
            jax.ShapeDtypeStruct((heads_dev, tile, 3 * tile), f32),
            jax.ShapeDtypeStruct((heads_dev, 2, 8, tile), f32),
        ],
        scratch_shapes=[
            pltpu.VMEM((heads_dev, tile, 2 * length), f32),
            pltpu.VMEM((heads_dev, tile, 2 * length), f32),
            pltpu.VMEM((length, width), f32),
            pltpu.VMEM((length, width), f32),
        ],
        compiler_params=pltpu.CompilerParams(vmem_limit_bytes=48 * 2**20),
        cost_estimate=pl.CostEstimate(
            flops=10 * rows * length * width,
            bytes_accessed=8 * length * width * 2,
            transcendentals=rows * length * heads_dev,
        ),
    )(first, place, table, near, qkv, doc_row, doc_col, attended, grad_out, stats)


def call(kernel, shapes, *operands, smem=0):
    return pl.pallas_call(
        kernel,
        in_specs=[pl.BlockSpec(memory_space=pltpu.SMEM)] * smem
        + [pl.BlockSpec(memory_space=pltpu.VMEM)] * (len(operands) - smem),
        out_specs=[pl.BlockSpec(memory_space=pltpu.VMEM)] * len(shapes),
        out_shape=[jax.ShapeDtypeStruct(shape, kind) for shape, kind in shapes],
        compiler_params=pltpu.CompilerParams(vmem_limit_bytes=16 * 2**20),
    )(*operands)


def share_in_kernel(place, attn_in, gains, *outs):
    rows, members = attn_in.shape[1], 2 * outs[0].shape[0] // attn_in.shape[1]
    width = attn_in.shape[2] // (3 * members)
    half = members // 2
    for layer_id in range(attn_in.shape[0]):
        for index in range(members):
            member = place[index]
            block = jnp.concatenate(
                [
                    attn_in[
                        layer_id,
                        :,
                        pl.ds(pl.multiple_of((part * members + member) * width, width), width),
                    ]
                    for part in range(3)
                ],
                axis=1,
            )
            outs[2 * layer_id + index // half][index % half * rows : (index % half + 1) * rows] = (
                block.astype(f32) * gains[layer_id]
            ).astype(bf16)


def row_of(chip, plane, core, rows, planes=4):
    return pl.multiple_of(((chip * planes + plane) * 2 + core) * rows, rows)


def assemble_in_kernel(place, own, lower, upper, opposite, out):
    at_z, at_core, at_head = place[8], place[0] % 2, place[0] // 2
    rows = own.shape[0] // 8
    for part, offset in ((own, 0), (lower, 3), (upper, 1), (opposite, 2)):
        plane = (at_z + offset) % 4
        for index in range(8):
            row = row_of(at_head ^ (index // 2), plane, at_core ^ (index % 2), rows)
            out[pl.ds(row, rows)] = part[index * rows : (index + 1) * rows]


def plane_attention_kernel(
    length, place, table, strip, near, far, w_in, *refs
):
    quarters, (doc_row, doc_col, w_out, qkv, attended, stats, near_part, far_part, band) = (
        refs[:4], refs[4:],
    )
    step = pl.program_id(0)
    half = length // 2
    heads_dev = table.shape[1]
    width = heads_dev * head_dim

    @pl.when(step == 0)
    def _():
        fill_band(band, table, strip, heads_dev, length)
        at_z = place[length // tile]
        rows = width // 4
        for index, quarter in enumerate(quarters):
            block = (index // 2 ^ at_z % 2) * 2 + (index % 2 ^ at_z // 2)
            w_out[pl.ds(pl.multiple_of(block * rows, rows), rows)] = quarter[...]
        qkv[:half] = contract(near[...], w_in[...], 1, 0).astype(bf16)
        qkv[half:] = contract(far[...], w_in[...], 1, 0).astype(bf16)

    row = pl.multiple_of(step * tile, tile)
    starts = band_starts(place, step, length, length // tile + 1)
    same_doc = doc_col[...] == doc_row[...]
    queries = qkv[pl.ds(row, tile), :width] * bf16(score_scale)
    lanes = lax.broadcasted_iota(jnp.int32, (tile, tile), 1)
    collected = jnp.zeros((tile, tile), f32)
    results = []
    for head in range(heads_dev):
        own = slice(head * head_dim, (head + 1) * head_dim)
        keys = qkv[:, width + own.start : width + own.stop]
        values = qkv[:, 2 * width + own.start : 2 * width + own.stop]
        scores = contract(queries[:, own], keys, 1, 1) + jnp.concatenate(
            [band[head, :, pl.ds(start, tile)] for start in starts], axis=1
        )
        scores = jnp.where(same_doc, scores, masked)
        peak = jnp.max(scores, axis=1, keepdims=True)
        weights = jnp.exp(scores - peak)
        total = jnp.sum(weights, axis=1, keepdims=True)
        results.append((contract(weights.astype(bf16), values, 1, 0) / total).astype(bf16))
        collected = jnp.where(lanes == head, peak + jnp.log(total), collected)
    stats[...] = collected
    merged = jnp.concatenate(results, axis=1)
    attended[...] = merged
    part = contract(merged, w_out[...], 1, 0)

    @pl.when(row < half)
    def _():
        near_part[...] = part

    @pl.when(row >= half)
    def _():
        far_part[...] = part.astype(bf16)


def near_block(steps, columns):
    return pl.BlockSpec((tile, columns), lambda step: (jnp.minimum(step, steps // 2 - 1), 0))


def far_block(steps, columns):
    return pl.BlockSpec((tile, columns), lambda step: (jnp.maximum(step - steps // 2, 0), 0))


def plane_attention(near, far, w_in, quarters, doc_row, doc_col, place, table, strip):
    length, model_width = 2 * near.shape[0], near.shape[1]
    steps = length // tile
    heads_dev = table.shape[1]
    width = heads_dev * head_dim
    return pl.pallas_call(
        functools.partial(plane_attention_kernel, length),
        grid=(steps,),
        in_specs=[
            pl.BlockSpec(memory_space=pltpu.SMEM),
            pl.BlockSpec(memory_space=pltpu.SMEM),
            whole(strip.shape),
            whole(near.shape),
            whole(far.shape),
            whole(w_in.shape),
            *[whole(quarter.shape) for quarter in quarters],
            whole(doc_row.shape),
            pl.BlockSpec((tile, 1), lambda step: (step, 0)),
        ],
        out_specs=[
            whole((width, model_width)),
            whole((length, 3 * width)),
            pl.BlockSpec((tile, width), lambda step: (step, 0)),
            pl.BlockSpec((tile, tile), lambda step: (step, 0)),
            near_block(steps, model_width),
            far_block(steps, model_width),
        ],
        out_shape=[
            jax.ShapeDtypeStruct((width, model_width), bf16),
            jax.ShapeDtypeStruct((length, 3 * width), bf16),
            jax.ShapeDtypeStruct((length, width), bf16),
            jax.ShapeDtypeStruct((length, tile), f32),
            jax.ShapeDtypeStruct((length // 2, model_width), f32),
            jax.ShapeDtypeStruct((length // 2, model_width), bf16),
        ],
        scratch_shapes=[pltpu.VMEM((heads_dev, tile, 2 * length), f32)],
        compiler_params=pltpu.CompilerParams(vmem_limit_bytes=24 * 2**20),
        cost_estimate=pl.CostEstimate(
            flops=4 * length * length * width + 8 * length * model_width * width,
            bytes_accessed=12 * 2**20,
            transcendentals=length * length * heads_dev,
        ),
    )(place, table, strip, near, far, w_in, *quarters, doc_row, doc_col)


def plane_attention_back_kernel(
    length, place, table, strip, qkv, doc_row, doc_col, attended, stats, near, far, w_in, w_out,
    grad_qkv, grad_near, grad_far, near_part, far_part, *rest
):
    quarters, (band, grad_band, grad_keys, grad_values, out_sum) = rest[:4], rest[4:]
    step = pl.program_id(0)
    half = length // 2
    heads_dev = table.shape[1]
    width = heads_dev * head_dim

    @pl.when(step == 0)
    def _():
        fill_band(band, table, strip, heads_dev, length)
        grad_band[...] = jnp.zeros_like(grad_band)
        grad_keys[...] = jnp.zeros_like(grad_keys)
        grad_values[...] = jnp.zeros_like(grad_values)
        out_sum[...] = jnp.zeros_like(out_sum)

    row = pl.multiple_of(step * tile, tile)
    starts = band_starts(place, step, length, length // tile + 1)
    same_doc = doc_col[...] == doc_row[...]
    branch = jnp.where(row < half, near[...], far[...])
    merged = attended[...]
    grad_merged = contract(branch, w_out[...], 1, 1).astype(bf16)
    out_sum[...] += contract(merged, branch, 0, 0)
    products = grad_merged.astype(f32) * merged.astype(f32)
    queries = qkv[pl.ds(row, tile), :width] * bf16(score_scale)
    for head in range(heads_dev):
        own = slice(head * head_dim, (head + 1) * head_dim)
        keys = qkv[:, width + own.start : width + own.stop]
        values = qkv[:, 2 * width + own.start : 2 * width + own.stop]
        upstream = grad_merged[:, own]
        scores = contract(queries[:, own], keys, 1, 1) + jnp.concatenate(
            [band[head, :, pl.ds(start, tile)] for start in starts], axis=1
        )
        scores = jnp.where(same_doc, scores, masked)
        weights = jnp.exp(scores - stats[:, head : head + 1])
        delta = jnp.sum(products[:, own], axis=1, keepdims=True)
        grad_scores = weights * (contract(upstream, values, 1, 1) - delta)
        for block, start in enumerate(starts):
            grad_band[head, :, pl.ds(start, tile)] += grad_scores[
                :, block * tile : (block + 1) * tile
            ]
        grad_low = grad_scores.astype(bf16)
        grad_values[:, own] += contract(weights.astype(bf16), upstream, 0, 0)
        grad_keys[:, own] += contract(grad_low, queries[:, own], 0, 0)
        grad_qkv[pl.ds(row, tile), own] = (
            contract(grad_low, keys, 1, 0) * score_scale
        ).astype(bf16)

    @pl.when(step == pl.num_programs(0) - 1)
    def _():
        grad_qkv[:, width : 2 * width] = grad_keys[...].astype(bf16)
        grad_qkv[:, 2 * width :] = grad_values[...].astype(bf16)
        far_part[...] = contract(grad_qkv[half:], w_in[...], 1, 1).astype(bf16)
        near_part[...] = contract(grad_qkv[:half], w_in[...], 1, 1)
        at_z = place[length // tile]
        rows = width // 4
        for index, quarter in enumerate(quarters):
            block = (index // 2 ^ at_z % 2) * 2 + (index % 2 ^ at_z // 2)
            quarter[...] = out_sum[pl.ds(pl.multiple_of(block * rows, rows), rows)].astype(bf16)
        for head in range(heads_dev):
            grad_near[head] = grad_band[head, :, length - tile : length + 2 * tile]
            grad_far[head, 0] = jnp.full(
                (8, tile), jnp.sum(grad_band[head, :, : length - tile]), f32
            )
            grad_far[head, 1] = jnp.full(
                (8, tile), jnp.sum(grad_band[head, :, length + 2 * tile :]), f32
            )


def plane_attention_back(
    qkv, doc_row, doc_col, attended, stats, near, far, w_in, w_out, place, table, strip
):
    length, model_width = 2 * near.shape[0], near.shape[1]
    steps = length // tile
    heads_dev = table.shape[1]
    width = heads_dev * head_dim
    shapes = [
        ((length, 3 * width), bf16),
        ((heads_dev, tile, 3 * tile), f32),
        ((heads_dev, 2, 8, tile), f32),
        ((length // 2, model_width), f32),
        ((length // 2, model_width), bf16),
    ] + [((width // 4, model_width), bf16)] * 4
    return pl.pallas_call(
        functools.partial(plane_attention_back_kernel, length),
        grid=(steps,),
        in_specs=[
            pl.BlockSpec(memory_space=pltpu.SMEM),
            pl.BlockSpec(memory_space=pltpu.SMEM),
            whole(strip.shape),
            whole(qkv.shape),
            whole(doc_row.shape),
            pl.BlockSpec((tile, 1), lambda step: (step, 0)),
            pl.BlockSpec((tile, width), lambda step: (step, 0)),
            pl.BlockSpec((tile, tile), lambda step: (step, 0)),
            near_block(steps, model_width),
            far_block(steps, model_width),
            whole(w_in.shape),
            whole(w_out.shape),
        ],
        out_specs=[whole(shape) for shape, _ in shapes],
        out_shape=[jax.ShapeDtypeStruct(shape, kind) for shape, kind in shapes],
        scratch_shapes=[
            pltpu.VMEM((heads_dev, tile, 2 * length), f32),
            pltpu.VMEM((heads_dev, tile, 2 * length), f32),
            pltpu.VMEM((length, width), f32),
            pltpu.VMEM((length, width), f32),
            pltpu.VMEM((width, model_width), f32),
        ],
        compiler_params=pltpu.CompilerParams(vmem_limit_bytes=28 * 2**20),
        cost_estimate=pl.CostEstimate(
            flops=10 * length * length * width + 10 * length * model_width * width,
            bytes_accessed=12 * 2**20,
            transcendentals=length * length * heads_dev,
        ),
    )(place, table, strip, qkv, doc_row, doc_col, attended, stats, near, far, w_in, w_out)


def gelu_and_slope(pre_act):
    size = jnp.abs(pre_act)
    gauss = jnp.exp(-0.5 * pre_act * pre_act)
    ratio = 1.0 / (1.0 + np.float32(0.3275911 * 0.5**0.5) * size)
    series = np.float32(1.061405429)
    for factor in (-1.453152027, 1.421413741, -0.284496736, 0.254829592):
        series = series * ratio + np.float32(factor)
    tail = 0.5 * series * ratio * gauss
    cumulative = jnp.where(pre_act < 0, tail, 1.0 - tail)
    slope = cumulative + pre_act * gauss * np.float32((2 * np.pi) ** -0.5)
    return pre_act * cumulative, slope


def ff_kernel(rows, pair, activated, slope, part):
    columns = rows.shape[1]
    value, gradient = gelu_and_slope(contract(rows[...], pair[:, :columns], 1, 1))
    activated[...] = value.astype(bf16)
    slope[...] = gradient.astype(bf16)
    part[...] = contract(activated[...], pair[:, columns:], 1, 0).astype(part.dtype)


def ff_first_kernel(rows, *refs):
    parts, (activated, slope, part, pair) = refs[:8], refs[8:]
    columns = rows.shape[1]

    @pl.when(pl.program_id(0) == 0)
    def _():
        units = parts[0].shape[0]
        for index, ref in enumerate(parts):
            block = pl.ds(index % 4 * units, units)
            pair[block, index // 4 * columns : (index // 4 + 1) * columns] = ref[...]

    ff_kernel(rows, pair, activated, slope, part)


def ff_back_kernel(rows, slope, pair, grad_pre, part):
    columns = rows.shape[1]
    grad_act = contract(rows[...], pair[:, columns:], 1, 1)
    grad_pre[...] = (grad_act * slope[...].astype(f32)).astype(bf16)
    part[...] = contract(grad_pre[...], pair[:, :columns], 1, 0).astype(part.dtype)


def by_rows(kernel, step_rows, row_operands, whole_operands, outs, whole_outs=()):
    rows = row_operands[0].shape[0]
    return pl.pallas_call(
        kernel,
        grid=(rows // step_rows,),
        in_specs=[
            pl.BlockSpec((step_rows, operand.shape[1]), lambda step: (step, 0))
            for operand in row_operands
        ]
        + [whole(operand.shape) for operand in whole_operands],
        out_specs=[pl.BlockSpec((step_rows, columns), lambda step: (step, 0)) for columns, _ in outs]
        + [whole(shape) for shape in whole_outs],
        out_shape=[jax.ShapeDtypeStruct((rows, columns), kind) for columns, kind in outs]
        + [jax.ShapeDtypeStruct(shape, bf16) for shape in whole_outs],
        compiler_params=pltpu.CompilerParams(vmem_limit_bytes=20 * 2**20),
        cost_estimate=pl.CostEstimate(
            flops=4 * rows * outs[0][0] * row_operands[0].shape[1],
            bytes_accessed=6 * 2**20,
            transcendentals=0,
        ),
    )(*row_operands, *whole_operands)


def ff_grads_kernel(
    pre_near, pre_far, act_near, act_far, normed_near, normed_far, low_near, low_far, *outs
):
    columns = normed_near.shape[1]
    rows = outs[0].shape[0]
    up = (
        contract(pre_near[...], normed_near[...], 0, 0)
        + contract(pre_far[...], normed_far[...], 0, 0)
    ).astype(bf16)
    down = (
        contract(act_near[...], low_near[...], 0, 0) + contract(act_far[...], low_far[...], 0, 0)
    ).astype(bf16)

    @pl.when(pl.program_id(0) == 0)
    def _():
        for index in range(2):
            block = slice(index * rows, (index + 1) * rows)
            outs[index][:, :columns] = up[block]
            outs[index][:, columns:] = down[block]

    @pl.when(pl.program_id(0) == 1)
    def _():
        outs[2][:, :columns] = up[:rows]
        outs[2][:, columns:] = down[:rows]
        outs[3][...] = up[rows:]
        outs[4][...] = down[rows:]


def ff_grads(pre, act, normed, low):
    rows, hidden_units = pre[0].shape
    columns = normed[0].shape[1]
    step_units = hidden_units // 2
    shapes = [(hidden_units // 4, 2 * columns)] * 3 + [(hidden_units // 4, columns)] * 2
    return pl.pallas_call(
        ff_grads_kernel,
        grid=(2,),
        in_specs=[pl.BlockSpec((rows, step_units), lambda step: (0, step))] * 4
        + [whole((rows, columns))] * 4,
        out_specs=[whole(shape) for shape in shapes],
        out_shape=[jax.ShapeDtypeStruct(shape, bf16) for shape in shapes],
        compiler_params=pltpu.CompilerParams(vmem_limit_bytes=28 * 2**20),
        cost_estimate=pl.CostEstimate(
            flops=8 * rows * hidden_units * columns, bytes_accessed=8 * 2**20, transcendentals=0
        ),
    )(*pre, *act, *normed, *low)


def in_grads_kernel(place, near, far, grad_qkv, own, lower, upper, opposite, total):
    half = near.shape[0]
    total[...] = (
        contract(near[...], grad_qkv[:half], 0, 0) + contract(far[...], grad_qkv[half:], 0, 0)
    ).astype(bf16)
    rows = own.shape[0] // 8
    for out, offset in ((own, 0), (lower, 3), (upper, 1), (opposite, 2)):
        plane = (place[8] + offset) % 4
        for index in range(8):
            owner = place[index]
            row = row_of(owner // 2, plane, owner % 2, rows)
            out[index * rows : (index + 1) * rows] = total[pl.ds(row, rows)]


def in_grads(place, near, far, grad_qkv):
    columns = grad_qkv.shape[1]
    shape = (near.shape[1] // 4, columns)
    return pl.pallas_call(
        in_grads_kernel,
        in_specs=[pl.BlockSpec(memory_space=pltpu.SMEM)]
        + [pl.BlockSpec(memory_space=pltpu.VMEM)] * 3,
        out_specs=[pl.BlockSpec(memory_space=pltpu.VMEM)] * 4,
        out_shape=[jax.ShapeDtypeStruct(shape, bf16)] * 4,
        scratch_shapes=[pltpu.VMEM((near.shape[1], columns), bf16)],
        compiler_params=pltpu.CompilerParams(vmem_limit_bytes=16 * 2**20),
        cost_estimate=pl.CostEstimate(
            flops=4 * near.shape[0] * near.shape[1] * columns,
            bytes_accessed=4 * 2**20,
            transcendentals=0,
        ),
    )(place, near, far, grad_qkv)


def add_in_kernel(own, lower, upper, opposite, near, far):
    total = sum_of_four([own, lower, upper, opposite]).astype(bf16)
    half = near.shape[0]
    near[...] = total[:half]
    far[...] = total[half:]


def combine_kernel(near_part, arrived, own, x_part, y_part, xy_part):
    rows = own.shape[0]
    own[...] = near_part[:rows] + arrived[:rows].astype(f32)
    for bits, out in ((1, x_part), (2, y_part), (3, xy_part)):
        block = slice(bits * rows, (bits + 1) * rows)
        out[...] = (near_part[block] + arrived[block].astype(f32)).astype(bf16)


def added(own, x_part, y_part, xy_part):
    return (own[...] + x_part[...].astype(f32)) + (
        y_part[...].astype(f32) + xy_part[...].astype(f32)
    )


def close_kernel(kept, own, x_part, y_part, xy_part, hidden, units):
    total = kept[...] + added(own, x_part, y_part, xy_part)
    hidden[...] = total
    units[...] = (total * inverse_rms(total)).astype(bf16)


def close_gain_kernel(kept, own, x_part, y_part, xy_part, gain, hidden, normed):
    total = kept[...] + added(own, x_part, y_part, xy_part)
    hidden[...] = total
    normed[...] = (total * inverse_rms(total) * gain[...]).astype(bf16)


def last_kernel(kept, own, x_part, y_part, xy_part, hidden):
    hidden[...] = (kept[...] + added(own, x_part, y_part, xy_part)).astype(bf16)


def middle_back_kernel(
    upstream, own, x_part, y_part, xy_part, middle, gain, grad_middle, branch, grad_gain
):
    grad_normed = added(own, x_part, y_part, xy_part)
    inverse = inverse_rms(middle[...])
    grad_gain[...] = jnp.sum(grad_normed * middle[...] * inverse, axis=0, keepdims=True)
    total = upstream[...].astype(f32) + unit_norm_back(
        middle[...], inverse, grad_normed * gain[...]
    )
    grad_middle[...] = total
    branch[...] = total.astype(bf16)


def layer_back_kernel(grad_middle, own, x_part, y_part, xy_part, hidden, upstream, low):
    total = grad_middle[...] + unit_norm_back(
        hidden[...], inverse_rms(hidden[...]), added(own, x_part, y_part, xy_part)
    )
    upstream[...] = total
    low[...] = total.astype(bf16)


def pair_kernel(axis, near, arrived, *outs):
    rows = near.shape[0] // len(outs)
    for index, out in enumerate(outs):
        block = slice(index * rows, (index + 1) * rows)
        if axis == 0:
            out[:rows] = near[block]
            out[rows:] = arrived[block]
        else:
            columns = near.shape[1]
            out[:, :columns] = near[block]
            out[:, columns:] = arrived[block]


def join_kernel(*refs):
    out, rows = refs[-1], refs[0].shape[0]
    for index, ref in enumerate(refs[:-1]):
        out[index * rows : (index + 1) * rows] = ref[...]


def unit_kernel(tokens, hidden, units):
    total = tokens[...].astype(f32)
    hidden[...] = total
    units[...] = (total * inverse_rms(total)).astype(bf16)


def ends_kernel(planes, place, gain_0, gain_1, table_0, table_1, out):
    devices = out.shape[0]
    blocks = planes * 2
    buckets = table_0.shape[0] // blocks
    at_head = place[0] // 2
    out[...] = jnp.zeros_like(out)
    total = table_0[...] + table_1[...]
    features = gain_0.shape[1] // devices
    for device in range(devices):
        chunk = slice(device * features // tile * tile, device * features // tile * tile + tile)
        out[device, 0:1] = gain_0[:, chunk]
        out[device, 1:2] = gain_1[:, chunk]
    for block in range(blocks):
        out[at_head * blocks + block, 2 : 2 + buckets] = total[
            block * buckets : (block + 1) * buckets
        ]


def finish_in_kernel(layers, place, *refs):
    shares, (attn_in, gains, ends, grad_in, grad_gain, grad_table) = (
        refs[: 4 * layers], refs[4 * layers :],
    )
    rows = attn_in.shape[1]
    summed = ends[0]
    for source in range(1, ends.shape[0]):
        summed = summed + ends[source]
    grad_table[...] = summed[2 : 2 + grad_table.shape[0]]
    first = ((place[0] // 2 * 4 + place[8]) * 2 + place[0] % 2) * rows % tile
    own = first + lax.broadcasted_iota(jnp.int32, (rows, tile), 0) == lax.broadcasted_iota(
        jnp.int32, (rows, tile), 1
    )
    width = shares[0].shape[1] // 6
    members = attn_in.shape[2] // (3 * width)
    for layer_id in range(layers):
        row_dot = jnp.zeros((rows, 1), f32)
        for index in range(members):
            share = shares[4 * layer_id + index % 4]
            member = place[index]
            for part in range(3):
                at = (index // 4 * 3 + part) * width
                block = share[:, at : at + width].astype(f32)
                columns = pl.ds(pl.multiple_of((part * members + member) * width, width), width)
                grad_in[layer_id, :, columns] = block * gains[layer_id]
                row_dot = row_dot + jnp.sum(
                    block * attn_in[layer_id, :, columns].astype(f32), axis=1, keepdims=True
                )
        ff_gain = jnp.sum(
            jnp.where(own, summed[layer_id : layer_id + 1], 0.0), axis=1, keepdims=True
        )
        grad_gain[layer_id] = jnp.concatenate([row_dot, ff_gain], axis=1)


def sum_of_four(parts):
    return (parts[0][...].astype(f32) + parts[1][...].astype(f32)) + (
        parts[2][...].astype(f32) + parts[3][...].astype(f32)
    )


def finish_ff_kernel(*refs):
    grads = refs[-2:]
    columns = grads[0].shape[2]
    for layer_id in range(grads[0].shape[0]):
        parts = refs[5 * layer_id : 5 * layer_id + 5]
        for side, out in enumerate(grads):
            halves = [part.at[:, side * columns : (side + 1) * columns] for part in parts[:3]]
            out[layer_id] = sum_of_four(halves + [parts[3 + side]])


def finish_out_kernel(*refs):
    for layer_id in range(refs[-1].shape[0]):
        refs[-1][layer_id] = sum_of_four(refs[4 * layer_id : 4 * layer_id + 4])


def inverse_rms(hidden):
    return lax.rsqrt(jnp.mean(hidden * hidden, axis=-1, keepdims=True) + epsilon)


def prepare(bias_table, first_head, heads_dev):
    table = lax.dynamic_slice_in_dim(bias_table, first_head, heads_dev, 1)
    (near,) = call(near_kernel, [((heads_dev, tile, 3 * tile), f32)], table, smem=1)
    return table, near


def bucket_grads(first_lane, grads, bucket_count):
    (total,) = call(bucket_kernel, [((bucket_count, tile), f32)], first_lane, *grads, smem=1)
    return total


def gelu_parts(pre_act):
    cumulative = 0.5 * (1.0 + lax.erf(pre_act * np.float32(0.5**0.5)))
    slope = cumulative + pre_act * jnp.exp(-0.5 * pre_act * pre_act) * np.float32(
        (2 * np.pi) ** -0.5
    )
    return (pre_act * cumulative).astype(bf16), slope


def unit_norm_back(hidden, inverse, grad_unit):
    unit = hidden * inverse
    return inverse * (grad_unit - unit * jnp.mean(grad_unit * unit, axis=-1, keepdims=True))


def gather_rows(block, axes):
    return lax.all_gather(block, axes, axis=0, tiled=True)


def toggle(array, axis, bits):
    return lax.ppermute(array, axis, [(i, i ^ bits) for i in range(lax.axis_size(axis))])


def shift(array, by):
    planes = lax.axis_size("z")
    return lax.ppermute(array, "z", [(i, (i + by) % planes) for i in range(planes)])


def plane_gather(block, *holds):
    near = jnp.concatenate([block] + [toggle(block, "head", bits) for bits in (1, 2, 3)])
    near, *holds = tie(near, *holds)
    return (near, toggle(near, "core", 1), *holds)


def plane_scatter(near_part, far_part):
    rows, columns = near_part.shape[0] // 4, near_part.shape[1]
    own, *others = call(
        combine_kernel,
        [((rows, columns), f32)] + [((rows, columns), bf16)] * 3,
        near_part,
        toggle(far_part, "core", 1),
    )
    shares = [own] + [toggle(other, "head", bits) for bits, other in zip((1, 2, 3), others)]
    return shares, own


def tie(*arrays):
    return lax.optimization_barrier(arrays)


def after(array, other):
    return lax.optimization_barrier((array, other))[0]


def scatter_sum(partial, axes, members):
    blocks = partial.astype(bf16).reshape(members, -1, partial.shape[1])
    return jnp.sum(lax.all_to_all(blocks, axes, 0, 0, tiled=True).astype(f32), axis=0)


def local_general(tokens, doc_start, bias_table, attn_in, attn_out, ff_in, ff_out, gains, cotangent):
    heads_n, z_n, core_n = (lax.axis_size(axis) for axis in everyone)
    devices = heads_n * z_n * core_n
    group, spare = ("z", "core"), "head"
    ff_group, ff_spare, ff_members = ("head", "core"), "z", heads_n * core_n
    blocks = z_n * core_n
    block_rows, model_width = tokens.shape[1:]
    layer_count, weight_rows = attn_in.shape[:2]
    length = block_rows * blocks
    heads_all = bias_table.shape[1]
    member = lax.axis_index("z") * core_n + lax.axis_index("core")
    heads_dev = max(1, heads_all // blocks)
    head_groups = heads_all // heads_dev
    split = blocks // head_groups
    head_group, query_part = member // split, member % split
    query_rows = length // split
    width = heads_dev * head_dim
    first = (query_part * (query_rows // tile)).astype(jnp.int32).reshape(1)
    place = jnp.arange(length // tile, dtype=jnp.int32)
    out_row = head_group * width

    def swap(array):
        return lax.all_to_all(array, everyone, 0, 0, tiled=True)

    starts = jnp.broadcast_to(
        doc_start.astype(f32)[:, None], (heads_n, blocks, block_rows)
    ).reshape(devices, block_rows)
    ff_gains = gains[:, :, 1].astype(f32).reshape(1, -1)
    small = swap(
        jnp.concatenate(
            [starts, jnp.broadcast_to(ff_gains, (devices, layer_count * weight_rows))], axis=1
        )
    )
    doc_row = small[:blocks, :block_rows].reshape(1, length)
    doc_col = lax.dynamic_slice_in_dim(
        doc_row.reshape(length, 1), query_part * query_rows, query_rows, 0
    )
    gain_ff = jnp.transpose(
        small[:, block_rows:].reshape(devices, layer_count, weight_rows), (1, 0, 2)
    ).reshape(layer_count, 1, model_width)
    table, near = prepare(bias_table, head_group * heads_dev, heads_dev)

    gain_attn = gains[:, :, 0].astype(f32)[:, :, None]
    own_in = attn_in.astype(f32)

    def fetch_in(layer_id):
        scaled = (own_in[layer_id] * gain_attn[layer_id]).astype(bf16)
        columns = jnp.transpose(
            scaled.reshape(weight_rows, 3, head_groups, width), (2, 0, 1, 3)
        ).reshape(head_groups, weight_rows, 3 * width)
        columns = jnp.repeat(columns, split, axis=0)
        columns = jnp.broadcast_to(columns[None], (heads_n, *columns.shape))
        return swap(columns.reshape(devices, weight_rows, 3 * width)).reshape(
            model_width, 3 * width
        )

    def fetch_ff(layer_id):
        pair = jnp.concatenate([ff_in[layer_id], ff_out[layer_id]], axis=1)
        pair = gather_rows(pair, ff_spare)
        return pair[:, :model_width], pair[:, model_width:]

    hidden, upstream = tokens[0].astype(f32), cotangent[0]
    weights_in = [fetch_in(layer_id) for layer_id in range(layer_count)]
    weights_out = lax.dynamic_slice_in_dim(
        lax.all_gather(attn_out, everyone, axis=1, tiled=True), out_row, width, 1
    )
    weights_ff = [fetch_ff(layer_id) for layer_id in range(layer_count)]

    records = []
    for layer_id in range(layer_count):
        w_in, w_out, (w_up, w_down) = (
            weights_in[layer_id], weights_out[layer_id], weights_ff[layer_id],
        )
        inverse = inverse_rms(hidden)
        units = gather_rows((hidden * inverse).astype(bf16), group)
        qkv = jnp.dot(units, w_in, preferred_element_type=f32).astype(bf16)
        attended, _, stats = attention(
            qkv, doc_row, doc_col, first, place, table, near, query_rows
        )
        mixed = jnp.dot(attended, w_out, preferred_element_type=f32)
        if split > 1:
            mixed = lax.dynamic_update_slice_in_dim(
                jnp.zeros((length, model_width), f32), mixed, query_part * query_rows, 0
            )
        middle = hidden + scatter_sum(mixed, group, blocks)
        inverse_ff = inverse_rms(middle)
        normed_ff = gather_rows((middle * inverse_ff * gain_ff[layer_id]).astype(bf16), ff_group)
        activated, slope = gelu_parts(contract(normed_ff, w_up, 1, 1))
        ff_result = jnp.dot(activated, w_down, preferred_element_type=f32)
        records.append(
            (hidden, inverse, units, qkv, attended, stats, middle, inverse_ff, normed_ff,
             activated, slope)
        )
        hidden = middle + scatter_sum(ff_result, ff_group, ff_members)
    output = hidden

    grads_ff, grads_in, grads_out, grads_gain_ff, grads_table = (
        [None] * layer_count for _ in range(5)
    )
    for layer_id in reversed(range(layer_count)):
        w_in, w_out, (w_up, w_down) = (
            weights_in[layer_id], weights_out[layer_id], weights_ff[layer_id],
        )
        (hidden, inverse, units, qkv, attended, stats, middle, inverse_ff, normed_ff,
         activated, slope) = records[layer_id]
        grad_low = gather_rows(upstream.astype(bf16), ff_group)
        grad_pre = (contract(grad_low, w_down, 1, 1) * slope).astype(bf16)
        grad_normed = scatter_sum(
            jnp.dot(grad_pre, w_up, preferred_element_type=f32), ff_group, ff_members
        )
        grad_pair = jnp.concatenate(
            [contract(grad_pre, normed_ff, 0, 0), contract(activated, grad_low, 0, 0)], axis=1
        ).astype(bf16)
        grads_ff[layer_id] = lax.psum_scatter(
            grad_pair, ff_spare, scatter_dimension=0, tiled=True
        ).astype(f32)
        grads_gain_ff[layer_id] = jnp.sum(grad_normed * middle * inverse_ff, axis=0)
        grad_middle = upstream + unit_norm_back(
            middle, inverse_ff, grad_normed * gain_ff[layer_id]
        )
        branch = gather_rows(grad_middle.astype(bf16), group)
        if split > 1:
            branch = lax.dynamic_slice_in_dim(branch, query_part * query_rows, query_rows, 0)
        grad_attended = contract(branch, w_out, 1, 1).astype(bf16)
        grad_qkv, grad_near, grad_far = attention_back(
            qkv, doc_row, doc_col, attended, grad_attended, stats, first, place, table, near, split
        )
        grads_table[layer_id] = (grad_near, grad_far)
        grad_units = scatter_sum(contract(grad_qkv, w_in, 1, 1), group, blocks)
        upstream = grad_middle + unit_norm_back(hidden, inverse, grad_units)
        grad_out = lax.dynamic_update_slice_in_dim(
            jnp.zeros((model_width, model_width), bf16),
            contract(attended, branch, 0, 0).astype(bf16),
            out_row,
            0,
        )
        grads_out[layer_id] = lax.psum_scatter(
            grad_out, everyone, scatter_dimension=0, tiled=True
        ).astype(f32)
        grads_in[layer_id] = contract(units, grad_qkv, 0, 0).astype(bf16)

    bucket_count = table.shape[0]
    grad_table = sum(
        bucket_grads(jnp.zeros((1,), jnp.int32), entry, bucket_count) for entry in grads_table
    )[:, :heads_dev]
    grad_table = lax.dynamic_update_slice_in_dim(
        jnp.zeros((bucket_count, heads_all), f32), grad_table, head_group * heads_dev, 1
    )
    grad_table = jnp.transpose(
        grad_table.reshape(blocks, bucket_count // blocks, heads_n, heads_all // heads_n),
        (2, 0, 1, 3),
    ).reshape(devices, -1)
    grad_gain_ff = jnp.transpose(
        jnp.stack(grads_gain_ff).reshape(layer_count, devices, weight_rows), (1, 0, 2)
    ).reshape(devices, -1)
    ends = jnp.sum(swap(jnp.concatenate([grad_gain_ff, grad_table], axis=1)), axis=0)
    grad_gain_ff = ends[: layer_count * weight_rows].reshape(layer_count, weight_rows)
    grad_bias_table = ends[layer_count * weight_rows :].reshape(
        bucket_count // blocks, heads_all // heads_n
    )
    grads_attn_in, grads_gains = [], []
    for layer_id in range(layer_count):
        parts = swap(grads_in[layer_id].reshape(devices, weight_rows, 3 * width)).astype(f32)
        parts = jnp.sum(parts.reshape(heads_n, blocks, weight_rows, 3 * width), axis=0)
        parts = jnp.sum(parts.reshape(head_groups, split, weight_rows, 3, width), axis=1)
        unit_grad = jnp.transpose(parts, (1, 2, 0, 3)).reshape(weight_rows, 3 * model_width)
        grads_attn_in.append(unit_grad * gain_attn[layer_id])
        grads_gains.append(
            jnp.stack(
                [jnp.sum(unit_grad * own_in[layer_id], axis=1), grad_gain_ff[layer_id]], axis=1
            )
        )
    return (
        output[None],
        upstream[None],
        jnp.stack(grads_attn_in),
        jnp.stack(grads_out),
        jnp.stack([entry[:, :model_width] for entry in grads_ff]),
        jnp.stack([entry[:, model_width:] for entry in grads_ff]),
        jnp.stack(grads_gains),
        grad_bias_table,
    )


def local_plane(tokens, doc_start, bias_table, attn_in, attn_out, ff_in, ff_out, gains, cotangent):
    heads_n, z_n, core_n = (lax.axis_size(axis) for axis in everyone)
    devices = heads_n * z_n * core_n
    at_head, at_z, at_core = (lax.axis_index(axis) for axis in everyone)
    members = heads_n * core_n
    block_rows, model_width = tokens.shape[1:]
    layer_count, weight_rows = attn_in.shape[:2]
    length = block_rows * members
    heads_all = bias_table.shape[1]
    heads_dev = heads_all // members
    width = heads_dev * head_dim
    member = at_head * core_n + at_core
    turn = [
        ((h * z_n + z) * core_n + c, ((h ^ z) * z_n + h) * core_n + c)
        for h in range(heads_n)
        for z in range(z_n)
        for c in range(core_n)
    ]
    turn_back = [(target, source) for source, target in turn]
    place = jnp.stack(
        [
            (at_head ^ bits) * core_n + (at_core ^ other)
            for other in range(core_n)
            for bits in range(heads_n)
        ]
        + [at_z]
        + [
            (at_head ^ bits ^ at_z) * core_n + (at_core ^ other)
            for other in range(core_n)
            for bits in range(heads_n)
        ]
    ).astype(jnp.int32)

    def relay(array):
        return lax.ppermute(array, everyone, turn)

    def relay_back(array):
        return lax.ppermute(array, everyone, turn_back)

    def swap(array):
        return lax.all_to_all(array, everyone, 0, 0, tiled=True)

    row_shape = (block_rows, model_width)
    share_shape = (members // 2 * weight_rows, 3 * width)
    gain_attn = gains[:, :, 0].astype(f32)[:, :, None]
    shares_in = call(
        share_in_kernel, [(share_shape, bf16)] * 2 * layer_count, place, attn_in, gain_attn, smem=1
    )

    quarter_turns = [
        [
            (z * core_n + c, (2 * c + (a ^ z % 2)) * core_n + (b ^ z // 2))
            for z in range(z_n)
            for c in range(core_n)
        ]
        for a in range(2)
        for b in range(2)
    ]

    def fetch_out(layer_id, hold):
        held = after(attn_out[layer_id], hold)
        return [
            lax.ppermute(held, ("z", "core"), [(holder, user) for user, holder in turns])
            for turns in quarter_turns
        ]

    starts = jnp.broadcast_to(
        doc_start.astype(f32)[None, :, None], (heads_n, z_n, core_n, block_rows)
    )
    ff_gains = gains[:, :, 1].astype(f32).reshape(1, -1)
    small = jnp.concatenate(
        [
            starts.reshape(devices, block_rows),
            jnp.broadcast_to(ff_gains, (devices, layer_count * weight_rows)),
        ],
        axis=1,
    )
    table, strip = prepare(bias_table, member * heads_dev, heads_dev)
    hidden, small, strip = tie(relay(tokens[0]), swap(small), strip)
    doc_row = small[:members, :block_rows].reshape(2, 2, core_n, block_rows)
    at_block = at_head ^ at_z
    for axis, bit in ((0, at_block // 2), (1, at_block % 2), (2, at_core)):
        doc_row = jnp.where(bit == 1, jnp.flip(doc_row, axis), doc_row)
    doc_row = jnp.transpose(doc_row, (2, 0, 1, 3)).reshape(1, length)
    doc_col = doc_row.reshape(length, 1)
    gain_ff = jnp.transpose(
        small[:, block_rows:].reshape(devices, layer_count, weight_rows), (1, 0, 2)
    ).reshape(layer_count, 1, model_width)

    def round_planes(array, by, hold):
        return shift(after(array, hold), by)

    def fetch_ff(layer_id, by, hold):
        return [round_planes(array[layer_id], by, hold) for array in (ff_in, ff_out)]

    def ff_first(rows, layer_id, lower, upper, opposite, kind):
        parts = [
            part
            for side, array in enumerate((ff_in, ff_out))
            for part in (array[layer_id], lower[side], upper[side], opposite[side])
        ]
        units = 4 * ff_in.shape[1]
        return by_rows(
            ff_first_kernel,
            256,
            [rows],
            parts,
            [(units, bf16), (units, bf16), (model_width, kind)],
            [(units, 2 * model_width)],
        )

    def ff_forward(normed, layer_id, *weights):
        *near, pair = ff_first(normed[0], layer_id, *weights, f32)
        units = pair.shape[0]
        far = by_rows(
            ff_kernel,
            256,
            [normed[1]],
            [pair],
            [(units, bf16), (units, bf16), (model_width, bf16)],
        )
        return pair, *zip(near, far)

    def ff_backward(low, slopes, pair):
        return zip(
            *(
                by_rows(
                    ff_back_kernel,
                    256,
                    [rows, slope],
                    [pair],
                    [(pair.shape[0], bf16), (model_width, kind)],
                )
                for rows, slope, kind in zip(low, slopes, (f32, bf16))
            )
        )

    def pair_chips(near, arrived, axis):
        rows, columns = near.shape[0] // 4, near.shape[1]
        shape = (2 * rows, columns) if axis == 0 else (rows, 2 * columns)
        return call(functools.partial(pair_kernel, axis), [(shape, bf16)] * 4, near, arrived)

    def share_chips(blocks):
        return [blocks[0]] + [toggle(blocks[bits], "head", bits) for bits in (1, 2, 3)]

    units_shape = [(row_shape, f32), (row_shape, bf16)]
    def fetch_plane(layer_id, hold):
        near, far = after(tuple(shares_in[2 * layer_id : 2 * layer_id + 2]), hold)
        return share_chips(pair_chips(near, toggle(far, "core", 1), 0))

    def join(shares):
        return call(join_kernel, [((weight_rows * members, 3 * width), bf16)], *shares)[0]

    def assemble_in(share, lower, upper, opposite):
        return call(
            assemble_in_kernel,
            [((model_width, 3 * width), bf16)],
            place,
            share,
            lower,
            upper,
            opposite,
            smem=1,
        )[0]

    hidden, shares = tie(hidden, fetch_plane(0, shares_in[0]))
    hidden, unit_rows = call(unit_kernel, units_shape, hidden)
    share = join(shares)
    near, far, lower, upper, opposite, quarters, doc_row, doc_col, gain_ff = plane_gather(
        unit_rows,
        shift(share, 1),
        shift(share, -1),
        shift(share, 2),
        fetch_out(0, hidden),
        doc_row,
        doc_col,
        gain_ff,
    )
    units = (near, far)
    w_in = assemble_in(share, lower, upper, opposite)
    w_out, qkv, attended, stats, *parts = plane_attention(
        *units, w_in, quarters, doc_row, doc_col, place, table, strip
    )
    parts, upstream = tie(parts, relay(after(cotangent[0].astype(bf16), near)))
    parts, own = plane_scatter(*parts)
    parts, lower, upper, shares = tie(
        parts, fetch_ff(0, 1, own), fetch_ff(0, -1, own), fetch_plane(1, own)
    )
    middle, normed_rows = call(close_gain_kernel, units_shape, hidden, *parts, gain_ff[0])
    near, far, opposite = plane_gather(normed_rows, fetch_ff(0, 2, normed_rows))
    normed = (near, far)
    pair, acts, slopes, parts = ff_forward(normed, 0, lower, upper, opposite)
    records = [
        (hidden, units, w_in, w_out, pair, qkv, attended, stats, middle, normed, acts, slopes)
    ]
    share = join(after(shares, near))
    parts, own = plane_scatter(*parts)
    parts, *shares = tie(
        parts,
        round_planes(share, 1, own),
        round_planes(share, -1, own),
        round_planes(share, 2, own),
    )
    hidden, unit_rows = call(close_kernel, units_shape, middle, *parts)

    near, far, lower, quarters = plane_gather(
        unit_rows, fetch_ff(1, 1, unit_rows), fetch_out(1, unit_rows)
    )
    units = (near, far)
    w_in = assemble_in(share, *shares)
    w_out, qkv, attended, stats, *parts = plane_attention(
        *units, w_in, quarters, doc_row, doc_col, place, table, strip
    )
    low = plane_gather(after(upstream, far))
    parts, near_low, upper = tie(parts, low[0], fetch_ff(1, -1, far))
    low = (near_low, low[1])
    parts, own = plane_scatter(*parts)
    parts, opposite_in = tie(parts, round_planes(ff_in[1], 2, own))
    middle, normed_rows = call(close_gain_kernel, units_shape, hidden, *parts, gain_ff[1])
    near, far, opposite_out = plane_gather(normed_rows, round_planes(ff_out[1], 2, normed_rows))
    normed = (near, far)
    pair, acts, slopes, last_parts = ff_forward(
        normed, 1, lower, upper, [opposite_in, opposite_out]
    )
    records.append(
        (hidden, units, w_in, w_out, pair, qkv, attended, stats, middle, normed, acts, slopes)
    )

    def back_to_middle(parts, upstream, middle, gain):
        return call(
            middle_back_kernel, units_shape + [((1, model_width), f32)], upstream, *parts, middle, gain
        )

    def attention_grads(record, branch):
        _, _, w_in, w_out, _, qkv, attended, stats, *_ = record
        grad_qkv, grad_near, grad_far, near_part, far_part, *quarters = plane_attention_back(
            qkv, doc_row, doc_col, attended, stats, *branch, w_in, w_out, place, table, strip
        )
        return grad_qkv, (grad_near, grad_far), (near_part, far_part), quarters

    def owners_quarters(quarters):
        return [
            lax.ppermute(quarter, ("z", "core"), turns)
            for quarter, turns in zip(quarters, quarter_turns)
        ]

    def table_grads(near_and_far):
        return bucket_grads(at_core.reshape(1) * heads_dev, near_and_far, table.shape[0])

    def add_in(own, lower, upper, opposite):
        return call(add_in_kernel, [(share_shape, bf16)] * 2, own, lower, upper, opposite)

    record = records[1]
    hidden, units, _, _, pair, *_, middle, normed, acts, slopes = record
    pres, parts = ff_backward(low, slopes, pair)
    parts, own = plane_scatter(*parts)
    planes = ff_grads(after(pres, own), acts, normed, low)
    parts, ff_lower = tie(parts, shift(planes[1], -1))
    last_parts, _ = plane_scatter(*after(last_parts, parts))
    grad_middle, branch_rows, gain_1 = back_to_middle(parts, upstream, middle, gain_ff[1])
    *branch, ff_upper = plane_gather(branch_rows, round_planes(planes[2], 1, branch_rows))
    grad_qkv, strips_1, parts, quarters = attention_grads(record, branch)
    parts, last_parts, opposite_up = tie(
        parts, last_parts, round_planes(planes[3], 2, branch[1])
    )
    parts, own = plane_scatter(*parts)
    grad_in = in_grads(place, *units, after(grad_qkv, own))
    parts, opposite_down, in_opposite, output, table_1 = tie(
        parts,
        round_planes(planes[4], 2, own),
        shift(grad_in[3], 2),
        call(last_kernel, [(row_shape, bf16)], middle, *after(last_parts, own))[0],
        table_grads(after(strips_1, own)),
    )
    grads_ff = [planes[0], ff_lower, ff_upper, opposite_up, opposite_down]
    upstream, low_rows = call(layer_back_kernel, units_shape, grad_middle, *parts, hidden)

    record = records[0]
    hidden, units, _, _, pair, *_, middle, normed, acts, slopes = record
    *low, in_lower, in_upper, quarters_1 = plane_gather(
        low_rows,
        round_planes(grad_in[1], -1, low_rows),
        round_planes(grad_in[2], 1, low_rows),
        owners_quarters(after(quarters, low_rows)),
    )
    pres, parts = ff_backward(low, slopes, pair)
    parts, own = plane_scatter(*parts)
    near_in, far_in = add_in(*after([grad_in[0], in_lower, in_upper, in_opposite], own))
    planes = ff_grads(after(pres, own), acts, normed, low)
    parts, ff_lower, far_in = tie(parts, shift(planes[1], -1), toggle(far_in, "core", 1))
    grad_middle, branch_rows, gain_0 = back_to_middle(parts, upstream, middle, gain_ff[0])
    *branch, ff_upper, opposite_up, shares_1 = plane_gather(
        branch_rows,
        round_planes(planes[2], 1, branch_rows),
        round_planes(planes[3], 2, branch_rows),
        share_chips(pair_chips(near_in, after(far_in, branch_rows), 1)),
    )
    grad_qkv, strips_0, parts, quarters = attention_grads(record, branch)
    parts, output = tie(parts, relay_back(after(output, branch[1])))
    parts, own = plane_scatter(*parts)
    grad_in = in_grads(place, *units, after(grad_qkv, own))
    parts, opposite_down, in_opposite, table_0, output = tie(
        parts,
        round_planes(planes[4], 2, own),
        shift(grad_in[3], 2),
        table_grads(after(strips_0, own)),
        after(output, own).astype(f32),
    )
    grads_ff = [planes[0], ff_lower, ff_upper, opposite_up, opposite_down] + grads_ff
    upstream, low_rows = call(layer_back_kernel, units_shape, grad_middle, *parts, hidden)
    grad_tokens = relay_back(low_rows)
    in_lower = round_planes(grad_in[1], -1, low_rows)
    in_upper = round_planes(grad_in[2], 1, low_rows)
    grad_up, grad_down = call(finish_ff_kernel, [(ff_in.shape, f32)] * 2, *after(grads_ff, low_rows))
    quarters_0 = owners_quarters(after(quarters, low_rows))
    near_in, far_in = add_in(grad_in[0], in_lower, in_upper, in_opposite)
    shares_0 = share_chips(pair_chips(near_in, toggle(far_in, "core", 1), 1))
    (ends,) = call(
        functools.partial(ends_kernel, z_n),
        [((devices, 8, tile), f32)],
        place,
        *after([gain_0, gain_1, table_0, table_1], low_rows),
        smem=1,
    )
    (grad_attn_out,) = call(finish_out_kernel, [(attn_out.shape, f32)], *quarters_0, *quarters_1)
    own_buckets = table.shape[0] // (z_n * core_n)
    grad_attn_in, grad_gains, grad_table = call(
        functools.partial(finish_in_kernel, layer_count),
        [(attn_in.shape, f32), (gains.shape, f32), ((own_buckets, tile), f32)],
        place,
        *shares_0,
        *shares_1,
        attn_in,
        gain_attn,
        swap(ends),
        smem=1,
    )
    return (
        output[None],
        grad_tokens.astype(f32)[None],
        grad_attn_in,
        grad_attn_out,
        grad_up,
        grad_down,
        grad_gains,
        grad_table[:, : heads_all // heads_n],
    )


def solution(mesh):
    sizes = dict(mesh.shape)
    cores = 2
    fine = Mesh(
        mesh.devices.reshape(sizes["head"], sizes["blk"] // cores, cores), everyone
    )
    blk = ("z", "core")
    in_specs = (
        P("head", blk, None),
        P(None, blk),
        P(),
        P(None, everyone, None),
        P(None, everyone, None),
        P(None, everyone, None),
        P(None, everyone, None),
        P(None, everyone, None),
        P("head", blk, None),
    )
    out_specs = (
        P("head", blk, None),
        P("head", blk, None),
        P(None, everyone, None),
        P(None, everyone, None),
        P(None, everyone, None),
        P(None, everyone, None),
        P(None, everyone, None),
        P(blk, "head"),
    )
    plane = sizes["head"] == 4 and sizes["blk"] == 8
    local = local_plane if plane else local_general
    return jax.shard_map(local, mesh=fine, in_specs=in_specs, out_specs=out_specs, check_vma=False)
```

```python
import functools

import jax
import jax.numpy as jnp
import numpy as np
from jax import lax
from jax.experimental import pallas as pl
from jax.experimental.pallas import tpu as pltpu
from jax.sharding import Mesh
from jax.sharding import PartitionSpec as P

bounds = (1, 2, 3, 4, 5, 6, 7, 8, 12, 16, 23, 32, 46, 64, 91)
epsilon = 1e-06
masked = -1e30
score_scale = 0.125
head_dim = 64
tile = 128
everyone = ("head", "z", "core")
bf16 = jnp.bfloat16
f32 = jnp.float32


def contract(lhs, rhs, lhs_dim, rhs_dim):
    return lax.dot_general(
        lhs, rhs, (((lhs_dim,), (rhs_dim,)), ((), ())), preferred_element_type=f32
    )


def near_buckets(shape):
    offsets = (
        lax.broadcasted_iota(jnp.int32, shape, 1) - tile - lax.broadcasted_iota(jnp.int32, shape, 0)
    )
    distance = jnp.abs(offsets)
    bucket = jnp.where(offsets > 0, 16, 0)
    for boundary in bounds:
        bucket = bucket + jnp.where(distance >= boundary, 1, 0)
    return bucket


def near_kernel(table, near):
    bucket = near_buckets(near.shape[1:])
    for head in range(near.shape[0]):
        values = jnp.zeros(near.shape[1:], f32)
        for bucket_id in range(table.shape[0]):
            values = jnp.where(bucket == bucket_id, table[bucket_id, head], values)
        near[head] = values


def bucket_kernel(first_lane, near, far, out):
    bucket = near_buckets(near.shape[1:])
    rows = lax.broadcasted_iota(jnp.int32, out.shape, 0)
    lanes = lax.broadcasted_iota(jnp.int32, out.shape, 1)
    total = jnp.zeros(out.shape, f32)
    for head in range(near.shape[0]):
        strip = near[head]
        for bucket_id in range(out.shape[0]):
            value = jnp.sum(jnp.where(bucket == bucket_id, strip, 0.0), axis=0, keepdims=True)
            value = jnp.sum(value, axis=1, keepdims=True)
            if bucket_id in (15, 31):
                value = value + far[head, bucket_id // 16, :1, :1]
            total = jnp.where((rows == bucket_id) & (lanes == head + first_lane[0]), value, total)
    out[...] = total


def fill_band(band, table, near, heads_dev, length):
    for head in range(heads_dev):
        band[head, :, : length - tile] = jnp.full((tile, length - tile), table[15, head], f32)
        band[head, :, length - tile : length + 2 * tile] = near[head]
        band[head, :, length + 2 * tile :] = jnp.full(
            (tile, length - 2 * tile), table[31, head], f32
        )


def band_starts(place, at, length, skip=0):
    return [
        pl.multiple_of(length + (place[skip + block] - place[skip + at]) * tile, tile)
        for block in range(length // tile)
    ]


def attention_kernel(
    heads_dev, length, first, place, table, near, qkv, doc_row, doc_col, out, local, stats, band
):
    step = pl.program_id(0)
    width = heads_dev * head_dim

    @pl.when(step == 0)
    def _():
        fill_band(band, table, near, heads_dev, length)

    row = pl.multiple_of((first[0] + step) * tile, tile)
    out_row = pl.multiple_of((place[first[0] + step] - first[0]) * tile, tile)
    starts = band_starts(place, first[0] + step, length)
    same_doc = doc_col[...] == doc_row[...]
    queries = qkv[pl.ds(row, tile), :width] * bf16(score_scale)
    lanes = lax.broadcasted_iota(jnp.int32, (tile, tile), 1)
    collected = jnp.zeros((tile, tile), f32)
    for head in range(heads_dev):
        own = slice(head * head_dim, (head + 1) * head_dim)
        keys = qkv[:, width + own.start : width + own.stop]
        values = qkv[:, 2 * width + own.start : 2 * width + own.stop]
        scores = contract(queries[:, own], keys, 1, 1)
        scores = scores + jnp.concatenate(
            [band[head, :, pl.ds(start, tile)] for start in starts], axis=1
        )
        scores = jnp.where(same_doc, scores, masked)
        peak = jnp.max(scores, axis=1, keepdims=True)
        weights = jnp.exp(scores - peak)
        total = jnp.sum(weights, axis=1, keepdims=True)
        mixed = contract(weights.astype(bf16), values, 1, 0) / total
        out[pl.ds(out_row, tile), own] = mixed.astype(bf16)
        local[:, own] = mixed.astype(bf16)
        collected = jnp.where(lanes == head, peak + jnp.log(total), collected)
    stats[...] = collected


def attention_back_kernel(
    heads_dev, length, split, first, place, table, near, qkv, doc_row, doc_col, attended, grad_out, stats,
    grad_qkv, grad_near, grad_far, band, grad_band, grad_keys, grad_values,
):
    step = pl.program_id(0)
    width = heads_dev * head_dim

    @pl.when(step == 0)
    def _():
        fill_band(band, table, near, heads_dev, length)
        grad_band[...] = jnp.zeros_like(grad_band)
        grad_keys[...] = jnp.zeros_like(grad_keys)
        grad_values[...] = jnp.zeros_like(grad_values)
        if split > 1:
            grad_qkv[...] = jnp.zeros_like(grad_qkv)

    row = pl.multiple_of((first[0] + step) * tile, tile)
    out_row = pl.multiple_of((place[first[0] + step] - first[0]) * tile, tile)
    starts = band_starts(place, first[0] + step, length)
    same_doc = doc_col[...] == doc_row[...]
    at_step = pl.multiple_of(step * tile, tile)
    queries = qkv[pl.ds(row, tile), :width] * bf16(score_scale)
    for head in range(heads_dev):
        own = slice(head * head_dim, (head + 1) * head_dim)
        keys = qkv[:, width + own.start : width + own.stop]
        values = qkv[:, 2 * width + own.start : 2 * width + own.stop]
        upstream = grad_out[pl.ds(out_row, tile), own]
        scores = contract(queries[:, own], keys, 1, 1) + jnp.concatenate(
            [band[head, :, pl.ds(start, tile)] for start in starts], axis=1
        )
        scores = jnp.where(same_doc, scores, masked)
        weights = jnp.exp(scores - stats[:, head : head + 1])
        delta = jnp.sum(
            upstream.astype(f32) * attended[pl.ds(at_step, tile), own].astype(f32),
            axis=1,
            keepdims=True,
        )
        grad_scores = weights * (contract(upstream, values, 1, 1) - delta)
        for block, start in enumerate(starts):
            grad_band[head, :, pl.ds(start, tile)] += grad_scores[
                :, block * tile : (block + 1) * tile
            ]
        grad_low = grad_scores.astype(bf16)
        grad_values[:, own] += contract(weights.astype(bf16), upstream, 0, 0)
        grad_keys[:, own] += contract(grad_low, queries[:, own], 0, 0)
        grad_qkv[pl.ds(row, tile), own] = (
            contract(grad_low, keys, 1, 0) * score_scale
        ).astype(bf16)

    @pl.when(step == pl.num_programs(0) - 1)
    def _():
        grad_qkv[:, width : 2 * width] = grad_keys[...].astype(bf16)
        grad_qkv[:, 2 * width :] = grad_values[...].astype(bf16)
        for head in range(heads_dev):
            grad_near[head] = grad_band[head, :, length - tile : length + 2 * tile]
            grad_far[head, 0] = jnp.full(
                (8, tile), jnp.sum(grad_band[head, :, : length - tile]), f32
            )
            grad_far[head, 1] = jnp.full(
                (8, tile), jnp.sum(grad_band[head, :, length + 2 * tile :]), f32
            )


def whole(shape):
    return pl.BlockSpec(shape, lambda step: (0,) * len(shape))


def attention(qkv, doc_row, doc_col, first, place, table, near, rows):
    length = qkv.shape[0]
    heads_dev = table.shape[1]
    width = heads_dev * head_dim
    return pl.pallas_call(
        functools.partial(attention_kernel, heads_dev, length),
        grid=(rows // tile,),
        in_specs=[
            pl.BlockSpec(memory_space=pltpu.SMEM),
            pl.BlockSpec(memory_space=pltpu.SMEM),
            pl.BlockSpec(memory_space=pltpu.SMEM),
            whole(near.shape),
            whole(qkv.shape),
            whole(doc_row.shape),
            pl.BlockSpec((tile, 1), lambda step: (step, 0)),
        ],
        out_specs=[
            whole((rows, width)),
            pl.BlockSpec((tile, width), lambda step: (step, 0)),
            pl.BlockSpec((tile, tile), lambda step: (step, 0)),
        ],
        out_shape=[
            jax.ShapeDtypeStruct((rows, width), bf16),
            jax.ShapeDtypeStruct((rows, width), bf16),
            jax.ShapeDtypeStruct((rows, tile), f32),
        ],
        scratch_shapes=[pltpu.VMEM((heads_dev, tile, 2 * length), f32)],
        compiler_params=pltpu.CompilerParams(vmem_limit_bytes=60 * 2**20),
        cost_estimate=pl.CostEstimate(
            flops=4 * rows * length * width,
            bytes_accessed=4 * length * width * 2,
            transcendentals=rows * length * heads_dev,
        ),
    )(first, place, table, near, qkv, doc_row, doc_col)


def attention_back(
    qkv, doc_row, doc_col, attended, grad_out, stats, first, place, table, near, split
):
    length = qkv.shape[0]
    rows = grad_out.shape[0]
    heads_dev = table.shape[1]
    width = heads_dev * head_dim
    return pl.pallas_call(
        functools.partial(attention_back_kernel, heads_dev, length, split),
        grid=(rows // tile,),
        in_specs=[
            pl.BlockSpec(memory_space=pltpu.SMEM),
            pl.BlockSpec(memory_space=pltpu.SMEM),
            pl.BlockSpec(memory_space=pltpu.SMEM),
            whole(near.shape),
            whole(qkv.shape),
            whole(doc_row.shape),
            pl.BlockSpec((tile, 1), lambda step: (step, 0)),
            whole((rows, width)),
            whole((rows, width)),
            pl.BlockSpec((tile, tile), lambda step: (step, 0)),
        ],
        out_specs=[
            whole((length, 3 * width)),
            whole((heads_dev, tile, 3 * tile)),
            whole((heads_dev, 2, 8, tile)),
        ],
        out_shape=[
            jax.ShapeDtypeStruct((length, 3 * width), bf16),
            jax.ShapeDtypeStruct((heads_dev, tile, 3 * tile), f32),
            jax.ShapeDtypeStruct((heads_dev, 2, 8, tile), f32),
        ],
        scratch_shapes=[
            pltpu.VMEM((heads_dev, tile, 2 * length), f32),
            pltpu.VMEM((heads_dev, tile, 2 * length), f32),
            pltpu.VMEM((length, width), f32),
            pltpu.VMEM((length, width), f32),
        ],
        compiler_params=pltpu.CompilerParams(vmem_limit_bytes=60 * 2**20),
        cost_estimate=pl.CostEstimate(
            flops=10 * rows * length * width,
            bytes_accessed=8 * length * width * 2,
            transcendentals=rows * length * heads_dev,
        ),
    )(first, place, table, near, qkv, doc_row, doc_col, attended, grad_out, stats)


def call(kernel, shapes, *operands, smem=0):
    return pl.pallas_call(
        kernel,
        in_specs=[pl.BlockSpec(memory_space=pltpu.SMEM)] * smem
        + [pl.BlockSpec(memory_space=pltpu.VMEM)] * (len(operands) - smem),
        out_specs=[pl.BlockSpec(memory_space=pltpu.VMEM)] * len(shapes),
        out_shape=[jax.ShapeDtypeStruct(shape, kind) for shape, kind in shapes],
        compiler_params=pltpu.CompilerParams(vmem_limit_bytes=60 * 2**20),
    )(*operands)


def share_in_kernel(place, attn_in, gains, *outs):
    rows, members = attn_in.shape[1], 2 * outs[0].shape[0] // attn_in.shape[1]
    width = attn_in.shape[2] // (3 * members)
    half = members // 2
    for layer_id in range(attn_in.shape[0]):
        for index in range(members):
            member = place[index]
            block = jnp.concatenate(
                [
                    attn_in[
                        layer_id,
                        :,
                        pl.ds(pl.multiple_of((part * members + member) * width, width), width),
                    ]
                    for part in range(3)
                ],
                axis=1,
            )
            outs[2 * layer_id + index // half][index % half * rows : (index % half + 1) * rows] = (
                block.astype(f32) * gains[layer_id]
            ).astype(bf16)


def row_of(chip, plane, core, rows, planes=4):
    return pl.multiple_of(((chip * planes + plane) * 2 + core) * rows, rows)


def assemble_in_kernel(place, own, lower, upper, opposite, out):
    at_z, at_core, at_head = place[8], place[0] % 2, place[0] // 2
    rows = own.shape[0] // 8
    for part, offset in ((own, 0), (lower, 3), (upper, 1), (opposite, 2)):
        plane = (at_z + offset) % 4
        for index in range(8):
            row = row_of(at_head ^ (index // 2), plane, at_core ^ (index % 2), rows)
            out[pl.ds(row, rows)] = part[index * rows : (index + 1) * rows]


def plane_attention_kernel(
    length, place, table, strip, near, far, w_in, *refs
):
    quarters, (doc_row, doc_col, w_out, qkv, attended, stats, near_part, far_part, band) = (
        refs[:4], refs[4:],
    )
    step = pl.program_id(0)
    half = length // 2
    heads_dev = table.shape[1]
    width = heads_dev * head_dim

    @pl.when(step == 0)
    def _():
        fill_band(band, table, strip, heads_dev, length)
        at_z = place[length // tile]
        rows = width // 4
        for index, quarter in enumerate(quarters):
            block = (index // 2 ^ at_z % 2) * 2 + (index % 2 ^ at_z // 2)
            w_out[pl.ds(pl.multiple_of(block * rows, rows), rows)] = quarter[...]
        qkv[:half] = contract(near[...], w_in[...], 1, 0).astype(bf16)
        qkv[half:] = contract(far[...], w_in[...], 1, 0).astype(bf16)

    row = pl.multiple_of(step * tile, tile)
    starts = band_starts(place, step, length, length // tile + 1)
    same_doc = doc_col[...] == doc_row[...]
    queries = qkv[pl.ds(row, tile), :width] * bf16(score_scale)
    lanes = lax.broadcasted_iota(jnp.int32, (tile, tile), 1)
    collected = jnp.zeros((tile, tile), f32)
    results = []
    for head in range(heads_dev):
        own = slice(head * head_dim, (head + 1) * head_dim)
        keys = qkv[:, width + own.start : width + own.stop]
        values = qkv[:, 2 * width + own.start : 2 * width + own.stop]
        scores = contract(queries[:, own], keys, 1, 1) + jnp.concatenate(
            [band[head, :, pl.ds(start, tile)] for start in starts], axis=1
        )
        scores = jnp.where(same_doc, scores, masked)
        peak = jnp.max(scores, axis=1, keepdims=True)
        weights = jnp.exp(scores - peak)
        total = jnp.sum(weights, axis=1, keepdims=True)
        results.append((contract(weights.astype(bf16), values, 1, 0) / total).astype(bf16))
        collected = jnp.where(lanes == head, peak + jnp.log(total), collected)
    stats[...] = collected
    merged = jnp.concatenate(results, axis=1)
    attended[...] = merged
    part = contract(merged, w_out[...], 1, 0)

    @pl.when(row < half)
    def _():
        near_part[...] = part

    @pl.when(row >= half)
    def _():
        far_part[...] = part.astype(bf16)


def near_block(steps, columns):
    return pl.BlockSpec((tile, columns), lambda step: (jnp.minimum(step, steps // 2 - 1), 0))


def far_block(steps, columns):
    return pl.BlockSpec((tile, columns), lambda step: (jnp.maximum(step - steps // 2, 0), 0))


def plane_attention(near, far, w_in, quarters, doc_row, doc_col, place, table, strip):
    length, model_width = 2 * near.shape[0], near.shape[1]
    steps = length // tile
    heads_dev = table.shape[1]
    width = heads_dev * head_dim
    return pl.pallas_call(
        functools.partial(plane_attention_kernel, length),
        grid=(steps,),
        in_specs=[
            pl.BlockSpec(memory_space=pltpu.SMEM),
            pl.BlockSpec(memory_space=pltpu.SMEM),
            whole(strip.shape),
            whole(near.shape),
            whole(far.shape),
            whole(w_in.shape),
            *[whole(quarter.shape) for quarter in quarters],
            whole(doc_row.shape),
            pl.BlockSpec((tile, 1), lambda step: (step, 0)),
        ],
        out_specs=[
            whole((width, model_width)),
            whole((length, 3 * width)),
            pl.BlockSpec((tile, width), lambda step: (step, 0)),
            pl.BlockSpec((tile, tile), lambda step: (step, 0)),
            near_block(steps, model_width),
            far_block(steps, model_width),
        ],
        out_shape=[
            jax.ShapeDtypeStruct((width, model_width), bf16),
            jax.ShapeDtypeStruct((length, 3 * width), bf16),
            jax.ShapeDtypeStruct((length, width), bf16),
            jax.ShapeDtypeStruct((length, tile), f32),
            jax.ShapeDtypeStruct((length // 2, model_width), f32),
            jax.ShapeDtypeStruct((length // 2, model_width), bf16),
        ],
        scratch_shapes=[pltpu.VMEM((heads_dev, tile, 2 * length), f32)],
        compiler_params=pltpu.CompilerParams(vmem_limit_bytes=60 * 2**20),
        cost_estimate=pl.CostEstimate(
            flops=4 * length * length * width + 8 * length * model_width * width,
            bytes_accessed=12 * 2**20,
            transcendentals=length * length * heads_dev,
        ),
    )(place, table, strip, near, far, w_in, *quarters, doc_row, doc_col)


def plane_attention_back_kernel(
    length, place, table, strip, qkv, doc_row, doc_col, attended, stats, near, far, w_in, w_out,
    grad_qkv, grad_near, grad_far, near_part, far_part, *rest
):
    quarters, (band, grad_band, grad_keys, grad_values, out_sum) = rest[:4], rest[4:]
    step = pl.program_id(0)
    half = length // 2
    heads_dev = table.shape[1]
    width = heads_dev * head_dim

    @pl.when(step == 0)
    def _():
        fill_band(band, table, strip, heads_dev, length)
        grad_band[...] = jnp.zeros_like(grad_band)
        grad_keys[...] = jnp.zeros_like(grad_keys)
        grad_values[...] = jnp.zeros_like(grad_values)
        out_sum[...] = jnp.zeros_like(out_sum)

    row = pl.multiple_of(step * tile, tile)
    starts = band_starts(place, step, length, length // tile + 1)
    same_doc = doc_col[...] == doc_row[...]
    branch = jnp.where(row < half, near[...], far[...])
    merged = attended[...]
    grad_merged = contract(branch, w_out[...], 1, 1).astype(bf16)
    out_sum[...] += contract(merged, branch, 0, 0)
    products = grad_merged.astype(f32) * merged.astype(f32)
    queries = qkv[pl.ds(row, tile), :width] * bf16(score_scale)
    for head in range(heads_dev):
        own = slice(head * head_dim, (head + 1) * head_dim)
        keys = qkv[:, width + own.start : width + own.stop]
        values = qkv[:, 2 * width + own.start : 2 * width + own.stop]
        upstream = grad_merged[:, own]
        scores = contract(queries[:, own], keys, 1, 1) + jnp.concatenate(
            [band[head, :, pl.ds(start, tile)] for start in starts], axis=1
        )
        scores = jnp.where(same_doc, scores, masked)
        weights = jnp.exp(scores - stats[:, head : head + 1])
        delta = jnp.sum(products[:, own], axis=1, keepdims=True)
        grad_scores = weights * (contract(upstream, values, 1, 1) - delta)
        for block, start in enumerate(starts):
            grad_band[head, :, pl.ds(start, tile)] += grad_scores[
                :, block * tile : (block + 1) * tile
            ]
        grad_low = grad_scores.astype(bf16)
        grad_values[:, own] += contract(weights.astype(bf16), upstream, 0, 0)
        grad_keys[:, own] += contract(grad_low, queries[:, own], 0, 0)
        grad_qkv[pl.ds(row, tile), own] = (
            contract(grad_low, keys, 1, 0) * score_scale
        ).astype(bf16)

    @pl.when(step == pl.num_programs(0) - 1)
    def _():
        grad_qkv[:, width : 2 * width] = grad_keys[...].astype(bf16)
        grad_qkv[:, 2 * width :] = grad_values[...].astype(bf16)
        far_part[...] = contract(grad_qkv[half:], w_in[...], 1, 1).astype(bf16)
        near_part[...] = contract(grad_qkv[:half], w_in[...], 1, 1)
        at_z = place[length // tile]
        rows = width // 4
        for index, quarter in enumerate(quarters):
            block = (index // 2 ^ at_z % 2) * 2 + (index % 2 ^ at_z // 2)
            quarter[...] = out_sum[pl.ds(pl.multiple_of(block * rows, rows), rows)].astype(bf16)
        for head in range(heads_dev):
            grad_near[head] = grad_band[head, :, length - tile : length + 2 * tile]
            grad_far[head, 0] = jnp.full(
                (8, tile), jnp.sum(grad_band[head, :, : length - tile]), f32
            )
            grad_far[head, 1] = jnp.full(
                (8, tile), jnp.sum(grad_band[head, :, length + 2 * tile :]), f32
            )


def plane_attention_back(
    qkv, doc_row, doc_col, attended, stats, near, far, w_in, w_out, place, table, strip
):
    length, model_width = 2 * near.shape[0], near.shape[1]
    steps = length // tile
    heads_dev = table.shape[1]
    width = heads_dev * head_dim
    shapes = [
        ((length, 3 * width), bf16),
        ((heads_dev, tile, 3 * tile), f32),
        ((heads_dev, 2, 8, tile), f32),
        ((length // 2, model_width), f32),
        ((length // 2, model_width), bf16),
    ] + [((width // 4, model_width), bf16)] * 4
    return pl.pallas_call(
        functools.partial(plane_attention_back_kernel, length),
        grid=(steps,),
        in_specs=[
            pl.BlockSpec(memory_space=pltpu.SMEM),
            pl.BlockSpec(memory_space=pltpu.SMEM),
            whole(strip.shape),
            whole(qkv.shape),
            whole(doc_row.shape),
            pl.BlockSpec((tile, 1), lambda step: (step, 0)),
            pl.BlockSpec((tile, width), lambda step: (step, 0)),
            pl.BlockSpec((tile, tile), lambda step: (step, 0)),
            near_block(steps, model_width),
            far_block(steps, model_width),
            whole(w_in.shape),
            whole(w_out.shape),
        ],
        out_specs=[whole(shape) for shape, _ in shapes],
        out_shape=[jax.ShapeDtypeStruct(shape, kind) for shape, kind in shapes],
        scratch_shapes=[
            pltpu.VMEM((heads_dev, tile, 2 * length), f32),
            pltpu.VMEM((heads_dev, tile, 2 * length), f32),
            pltpu.VMEM((length, width), f32),
            pltpu.VMEM((length, width), f32),
            pltpu.VMEM((width, model_width), f32),
        ],
        compiler_params=pltpu.CompilerParams(vmem_limit_bytes=60 * 2**20),
        cost_estimate=pl.CostEstimate(
            flops=10 * length * length * width + 10 * length * model_width * width,
            bytes_accessed=12 * 2**20,
            transcendentals=length * length * heads_dev,
        ),
    )(place, table, strip, qkv, doc_row, doc_col, attended, stats, near, far, w_in, w_out)


def gelu_and_slope(pre_act):
    size = jnp.abs(pre_act)
    gauss = jnp.exp(-0.5 * pre_act * pre_act)
    ratio = 1.0 / (1.0 + np.float32(0.3275911 * 0.5**0.5) * size)
    series = np.float32(1.061405429)
    for factor in (-1.453152027, 1.421413741, -0.284496736, 0.254829592):
        series = series * ratio + np.float32(factor)
    tail = 0.5 * series * ratio * gauss
    cumulative = jnp.where(pre_act < 0, tail, 1.0 - tail)
    slope = cumulative + pre_act * gauss * np.float32((2 * np.pi) ** -0.5)
    return pre_act * cumulative, slope


def ff_kernel(rows, pair, activated, slope, part):
    columns = rows.shape[1]
    value, gradient = gelu_and_slope(contract(rows[...], pair[:, :columns], 1, 1))
    activated[...] = value.astype(bf16)
    slope[...] = gradient.astype(bf16)
    part[...] = contract(activated[...], pair[:, columns:], 1, 0).astype(part.dtype)


def ff_first_kernel(rows, *refs):
    parts, (activated, slope, part, pair) = refs[:8], refs[8:]
    columns = rows.shape[1]

    @pl.when(pl.program_id(0) == 0)
    def _():
        units = parts[0].shape[0]
        for index, ref in enumerate(parts):
            block = pl.ds(index % 4 * units, units)
            pair[block, index // 4 * columns : (index // 4 + 1) * columns] = ref[...]

    ff_kernel(rows, pair, activated, slope, part)


def ff_back_kernel(rows, slope, pair, grad_pre, part):
    columns = rows.shape[1]
    grad_act = contract(rows[...], pair[:, columns:], 1, 1)
    grad_pre[...] = (grad_act * slope[...].astype(f32)).astype(bf16)
    part[...] = contract(grad_pre[...], pair[:, :columns], 1, 0).astype(part.dtype)


def by_rows(kernel, step_rows, row_operands, whole_operands, outs, whole_outs=()):
    rows = row_operands[0].shape[0]
    return pl.pallas_call(
        kernel,
        grid=(rows // step_rows,),
        in_specs=[
            pl.BlockSpec((step_rows, operand.shape[1]), lambda step: (step, 0))
            for operand in row_operands
        ]
        + [whole(operand.shape) for operand in whole_operands],
        out_specs=[pl.BlockSpec((step_rows, columns), lambda step: (step, 0)) for columns, _ in outs]
        + [whole(shape) for shape in whole_outs],
        out_shape=[jax.ShapeDtypeStruct((rows, columns), kind) for columns, kind in outs]
        + [jax.ShapeDtypeStruct(shape, bf16) for shape in whole_outs],
        compiler_params=pltpu.CompilerParams(vmem_limit_bytes=60 * 2**20),
        cost_estimate=pl.CostEstimate(
            flops=4 * rows * outs[0][0] * row_operands[0].shape[1],
            bytes_accessed=6 * 2**20,
            transcendentals=0,
        ),
    )(*row_operands, *whole_operands)


def ff_grads_kernel(
    pre_near, pre_far, act_near, act_far, normed_near, normed_far, low_near, low_far, *outs
):
    columns = normed_near.shape[1]
    rows = outs[0].shape[0]
    up = (
        contract(pre_near[...], normed_near[...], 0, 0)
        + contract(pre_far[...], normed_far[...], 0, 0)
    ).astype(bf16)
    down = (
        contract(act_near[...], low_near[...], 0, 0) + contract(act_far[...], low_far[...], 0, 0)
    ).astype(bf16)

    @pl.when(pl.program_id(0) == 0)
    def _():
        for index in range(2):
            block = slice(index * rows, (index + 1) * rows)
            outs[index][:, :columns] = up[block]
            outs[index][:, columns:] = down[block]

    @pl.when(pl.program_id(0) == 1)
    def _():
        outs[2][:, :columns] = up[:rows]
        outs[2][:, columns:] = down[:rows]
        outs[3][...] = up[rows:]
        outs[4][...] = down[rows:]


def ff_grads(pre, act, normed, low):
    rows, hidden_units = pre[0].shape
    columns = normed[0].shape[1]
    step_units = hidden_units // 2
    shapes = [(hidden_units // 4, 2 * columns)] * 3 + [(hidden_units // 4, columns)] * 2
    return pl.pallas_call(
        ff_grads_kernel,
        grid=(2,),
        in_specs=[pl.BlockSpec((rows, step_units), lambda step: (0, step))] * 4
        + [whole((rows, columns))] * 4,
        out_specs=[whole(shape) for shape in shapes],
        out_shape=[jax.ShapeDtypeStruct(shape, bf16) for shape in shapes],
        compiler_params=pltpu.CompilerParams(vmem_limit_bytes=60 * 2**20),
        cost_estimate=pl.CostEstimate(
            flops=8 * rows * hidden_units * columns, bytes_accessed=8 * 2**20, transcendentals=0
        ),
    )(*pre, *act, *normed, *low)


def in_grads_kernel(place, near, far, grad_qkv, own, lower, upper, opposite, total):
    half = near.shape[0]
    total[...] = (
        contract(near[...], grad_qkv[:half], 0, 0) + contract(far[...], grad_qkv[half:], 0, 0)
    ).astype(bf16)
    rows = own.shape[0] // 8
    for out, offset in ((own, 0), (lower, 3), (upper, 1), (opposite, 2)):
        plane = (place[8] + offset) % 4
        for index in range(8):
            owner = place[index]
            row = row_of(owner // 2, plane, owner % 2, rows)
            out[index * rows : (index + 1) * rows] = total[pl.ds(row, rows)]


def in_grads(place, near, far, grad_qkv):
    columns = grad_qkv.shape[1]
    shape = (near.shape[1] // 4, columns)
    return pl.pallas_call(
        in_grads_kernel,
        in_specs=[pl.BlockSpec(memory_space=pltpu.SMEM)]
        + [pl.BlockSpec(memory_space=pltpu.VMEM)] * 3,
        out_specs=[pl.BlockSpec(memory_space=pltpu.VMEM)] * 4,
        out_shape=[jax.ShapeDtypeStruct(shape, bf16)] * 4,
        scratch_shapes=[pltpu.VMEM((near.shape[1], columns), bf16)],
        compiler_params=pltpu.CompilerParams(vmem_limit_bytes=60 * 2**20),
        cost_estimate=pl.CostEstimate(
            flops=4 * near.shape[0] * near.shape[1] * columns,
            bytes_accessed=4 * 2**20,
            transcendentals=0,
        ),
    )(place, near, far, grad_qkv)


def add_in_kernel(own, lower, upper, opposite, near, far):
    total = sum_of_four([own, lower, upper, opposite]).astype(bf16)
    half = near.shape[0]
    near[...] = total[:half]
    far[...] = total[half:]


def combine_kernel(near_part, arrived, own, x_part, y_part, xy_part):
    rows = own.shape[0]
    own[...] = near_part[:rows] + arrived[:rows].astype(f32)
    for bits, out in ((1, x_part), (2, y_part), (3, xy_part)):
        block = slice(bits * rows, (bits + 1) * rows)
        out[...] = (near_part[block] + arrived[block].astype(f32)).astype(bf16)


def added(own, x_part, y_part, xy_part):
    return (own[...] + x_part[...].astype(f32)) + (
        y_part[...].astype(f32) + xy_part[...].astype(f32)
    )


def close_kernel(kept, own, x_part, y_part, xy_part, hidden, units):
    total = kept[...] + added(own, x_part, y_part, xy_part)
    hidden[...] = total
    units[...] = (total * inverse_rms(total)).astype(bf16)


def close_gain_kernel(kept, own, x_part, y_part, xy_part, gain, hidden, normed):
    total = kept[...] + added(own, x_part, y_part, xy_part)
    hidden[...] = total
    normed[...] = (total * inverse_rms(total) * gain[...]).astype(bf16)


def last_kernel(kept, own, x_part, y_part, xy_part, hidden):
    hidden[...] = (kept[...] + added(own, x_part, y_part, xy_part)).astype(bf16)


def middle_back_kernel(
    upstream, own, x_part, y_part, xy_part, middle, gain, grad_middle, branch, grad_gain
):
    grad_normed = added(own, x_part, y_part, xy_part)
    inverse = inverse_rms(middle[...])
    grad_gain[...] = jnp.sum(grad_normed * middle[...] * inverse, axis=0, keepdims=True)
    total = upstream[...].astype(f32) + unit_norm_back(
        middle[...], inverse, grad_normed * gain[...]
    )
    grad_middle[...] = total
    branch[...] = total.astype(bf16)


def layer_back_kernel(grad_middle, own, x_part, y_part, xy_part, hidden, upstream, low):
    total = grad_middle[...] + unit_norm_back(
        hidden[...], inverse_rms(hidden[...]), added(own, x_part, y_part, xy_part)
    )
    upstream[...] = total
    low[...] = total.astype(bf16)


def pair_kernel(axis, near, arrived, *outs):
    rows = near.shape[0] // len(outs)
    for index, out in enumerate(outs):
        block = slice(index * rows, (index + 1) * rows)
        if axis == 0:
            out[:rows] = near[block]
            out[rows:] = arrived[block]
        else:
            columns = near.shape[1]
            out[:, :columns] = near[block]
            out[:, columns:] = arrived[block]


def join_kernel(*refs):
    out, rows = refs[-1], refs[0].shape[0]
    for index, ref in enumerate(refs[:-1]):
        out[index * rows : (index + 1) * rows] = ref[...]


def unit_kernel(tokens, hidden, units):
    total = tokens[...].astype(f32)
    hidden[...] = total
    units[...] = (total * inverse_rms(total)).astype(bf16)


def ends_kernel(planes, place, gain_0, gain_1, table_0, table_1, out):
    devices = out.shape[0]
    blocks = planes * 2
    buckets = table_0.shape[0] // blocks
    at_head = place[0] // 2
    out[...] = jnp.zeros_like(out)
    total = table_0[...] + table_1[...]
    features = gain_0.shape[1] // devices
    for device in range(devices):
        chunk = slice(device * features // tile * tile, device * features // tile * tile + tile)
        out[device, 0:1] = gain_0[:, chunk]
        out[device, 1:2] = gain_1[:, chunk]
    for block in range(blocks):
        out[at_head * blocks + block, 2 : 2 + buckets] = total[
            block * buckets : (block + 1) * buckets
        ]


def finish_in_kernel(layers, place, *refs):
    shares, (attn_in, gains, ends, grad_in, grad_gain, grad_table) = (
        refs[: 4 * layers], refs[4 * layers :],
    )
    rows = attn_in.shape[1]
    summed = ends[0]
    for source in range(1, ends.shape[0]):
        summed = summed + ends[source]
    grad_table[...] = summed[2 : 2 + grad_table.shape[0]]
    first = ((place[0] // 2 * 4 + place[8]) * 2 + place[0] % 2) * rows % tile
    own = first + lax.broadcasted_iota(jnp.int32, (rows, tile), 0) == lax.broadcasted_iota(
        jnp.int32, (rows, tile), 1
    )
    width = shares[0].shape[1] // 6
    members = attn_in.shape[2] // (3 * width)
    for layer_id in range(layers):
        row_dot = jnp.zeros((rows, 1), f32)
        for index in range(members):
            share = shares[4 * layer_id + index % 4]
            member = place[index]
            for part in range(3):
                at = (index // 4 * 3 + part) * width
                block = share[:, at : at + width].astype(f32)
                columns = pl.ds(pl.multiple_of((part * members + member) * width, width), width)
                grad_in[layer_id, :, columns] = block * gains[layer_id]
                row_dot = row_dot + jnp.sum(
                    block * attn_in[layer_id, :, columns].astype(f32), axis=1, keepdims=True
                )
        ff_gain = jnp.sum(
            jnp.where(own, summed[layer_id : layer_id + 1], 0.0), axis=1, keepdims=True
        )
        grad_gain[layer_id] = jnp.concatenate([row_dot, ff_gain], axis=1)


def sum_of_four(parts):
    return (parts[0][...].astype(f32) + parts[1][...].astype(f32)) + (
        parts[2][...].astype(f32) + parts[3][...].astype(f32)
    )


def finish_ff_kernel(*refs):
    grads = refs[-2:]
    columns = grads[0].shape[2]
    for layer_id in range(grads[0].shape[0]):
        parts = refs[5 * layer_id : 5 * layer_id + 5]
        for side, out in enumerate(grads):
            halves = [part.at[:, side * columns : (side + 1) * columns] for part in parts[:3]]
            out[layer_id] = sum_of_four(halves + [parts[3 + side]])


def finish_out_kernel(*refs):
    for layer_id in range(refs[-1].shape[0]):
        refs[-1][layer_id] = sum_of_four(refs[4 * layer_id : 4 * layer_id + 4])


def inverse_rms(hidden):
    return lax.rsqrt(jnp.mean(hidden * hidden, axis=-1, keepdims=True) + epsilon)


def prepare(bias_table, first_head, heads_dev):
    table = lax.dynamic_slice_in_dim(bias_table, first_head, heads_dev, 1)
    (near,) = call(near_kernel, [((heads_dev, tile, 3 * tile), f32)], table, smem=1)
    return table, near


def bucket_grads(first_lane, grads, bucket_count):
    (total,) = call(bucket_kernel, [((bucket_count, tile), f32)], first_lane, *grads, smem=1)
    return total


def gelu_parts(pre_act):
    cumulative = 0.5 * (1.0 + lax.erf(pre_act * np.float32(0.5**0.5)))
    slope = cumulative + pre_act * jnp.exp(-0.5 * pre_act * pre_act) * np.float32(
        (2 * np.pi) ** -0.5
    )
    return (pre_act * cumulative).astype(bf16), slope


def unit_norm_back(hidden, inverse, grad_unit):
    unit = hidden * inverse
    return inverse * (grad_unit - unit * jnp.mean(grad_unit * unit, axis=-1, keepdims=True))


def gather_rows(block, axes):
    return lax.all_gather(block, axes, axis=0, tiled=True)


def toggle(array, axis, bits):
    return lax.ppermute(array, axis, [(i, i ^ bits) for i in range(lax.axis_size(axis))])


def shift(array, by):
    planes = lax.axis_size("z")
    return lax.ppermute(array, "z", [(i, (i + by) % planes) for i in range(planes)])


def plane_gather(block, *holds):
    near = jnp.concatenate([block] + [toggle(block, "head", bits) for bits in (1, 2, 3)])
    near, *holds = tie(near, *holds)
    return (near, toggle(near, "core", 1), *holds)


def plane_scatter(near_part, far_part):
    rows, columns = near_part.shape[0] // 4, near_part.shape[1]
    own, *others = call(
        combine_kernel,
        [((rows, columns), f32)] + [((rows, columns), bf16)] * 3,
        near_part,
        toggle(far_part, "core", 1),
    )
    shares = [own] + [toggle(other, "head", bits) for bits, other in zip((1, 2, 3), others)]
    return shares, own


def tie(*arrays):
    return lax.optimization_barrier(arrays)


def after(array, other):
    return lax.optimization_barrier((array, other))[0]


def scatter_sum(partial, axes, members):
    blocks = partial.astype(bf16).reshape(members, -1, partial.shape[1])
    return jnp.sum(lax.all_to_all(blocks, axes, 0, 0, tiled=True).astype(f32), axis=0)


def local_general(tokens, doc_start, bias_table, attn_in, attn_out, ff_in, ff_out, gains, cotangent):
    heads_n, z_n, core_n = (lax.axis_size(axis) for axis in everyone)
    devices = heads_n * z_n * core_n
    group, spare = ("z", "core"), "head"
    ff_group, ff_spare, ff_members = ("head", "core"), "z", heads_n * core_n
    blocks = z_n * core_n
    block_rows, model_width = tokens.shape[1:]
    layer_count, weight_rows = attn_in.shape[:2]
    length = block_rows * blocks
    heads_all = bias_table.shape[1]
    member = lax.axis_index("z") * core_n + lax.axis_index("core")
    heads_dev = max(1, heads_all // blocks)
    head_groups = heads_all // heads_dev
    split = blocks // head_groups
    head_group, query_part = member // split, member % split
    query_rows = length // split
    width = heads_dev * head_dim
    first = (query_part * (query_rows // tile)).astype(jnp.int32).reshape(1)
    place = jnp.arange(length // tile, dtype=jnp.int32)
    out_row = head_group * width

    def swap(array):
        return lax.all_to_all(array, everyone, 0, 0, tiled=True)

    starts = jnp.broadcast_to(
        doc_start.astype(f32)[:, None], (heads_n, blocks, block_rows)
    ).reshape(devices, block_rows)
    ff_gains = gains[:, :, 1].astype(f32).reshape(1, -1)
    small = swap(
        jnp.concatenate(
            [starts, jnp.broadcast_to(ff_gains, (devices, layer_count * weight_rows))], axis=1
        )
    )
    doc_row = small[:blocks, :block_rows].reshape(1, length)
    doc_col = lax.dynamic_slice_in_dim(
        doc_row.reshape(length, 1), query_part * query_rows, query_rows, 0
    )
    gain_ff = jnp.transpose(
        small[:, block_rows:].reshape(devices, layer_count, weight_rows), (1, 0, 2)
    ).reshape(layer_count, 1, model_width)
    table, near = prepare(bias_table, head_group * heads_dev, heads_dev)

    gain_attn = gains[:, :, 0].astype(f32)[:, :, None]
    own_in = attn_in.astype(f32)

    def fetch_in(layer_id):
        scaled = (own_in[layer_id] * gain_attn[layer_id]).astype(bf16)
        columns = jnp.transpose(
            scaled.reshape(weight_rows, 3, head_groups, width), (2, 0, 1, 3)
        ).reshape(head_groups, weight_rows, 3 * width)
        columns = jnp.repeat(columns, split, axis=0)
        columns = jnp.broadcast_to(columns[None], (heads_n, *columns.shape))
        return swap(columns.reshape(devices, weight_rows, 3 * width)).reshape(
            model_width, 3 * width
        )

    def fetch_ff(layer_id):
        pair = jnp.concatenate([ff_in[layer_id], ff_out[layer_id]], axis=1)
        pair = gather_rows(pair, ff_spare)
        return pair[:, :model_width], pair[:, model_width:]

    hidden, upstream = tokens[0].astype(f32), cotangent[0]
    weights_in = [fetch_in(layer_id) for layer_id in range(layer_count)]
    weights_out = lax.dynamic_slice_in_dim(
        lax.all_gather(attn_out, everyone, axis=1, tiled=True), out_row, width, 1
    )
    weights_ff = [fetch_ff(layer_id) for layer_id in range(layer_count)]

    records = []
    for layer_id in range(layer_count):
        w_in, w_out, (w_up, w_down) = (
            weights_in[layer_id], weights_out[layer_id], weights_ff[layer_id],
        )
        inverse = inverse_rms(hidden)
        units = gather_rows((hidden * inverse).astype(bf16), group)
        qkv = jnp.dot(units, w_in, preferred_element_type=f32).astype(bf16)
        attended, _, stats = attention(
            qkv, doc_row, doc_col, first, place, table, near, query_rows
        )
        mixed = jnp.dot(attended, w_out, preferred_element_type=f32)
        if split > 1:
            mixed = lax.dynamic_update_slice_in_dim(
                jnp.zeros((length, model_width), f32), mixed, query_part * query_rows, 0
            )
        middle = hidden + scatter_sum(mixed, group, blocks)
        inverse_ff = inverse_rms(middle)
        normed_ff = gather_rows((middle * inverse_ff * gain_ff[layer_id]).astype(bf16), ff_group)
        activated, slope = gelu_parts(contract(normed_ff, w_up, 1, 1))
        ff_result = jnp.dot(activated, w_down, preferred_element_type=f32)
        records.append(
            (hidden, inverse, units, qkv, attended, stats, middle, inverse_ff, normed_ff,
             activated, slope)
        )
        hidden = middle + scatter_sum(ff_result, ff_group, ff_members)
    output = hidden

    grads_ff, grads_in, grads_out, grads_gain_ff, grads_table = (
        [None] * layer_count for _ in range(5)
    )
    for layer_id in reversed(range(layer_count)):
        w_in, w_out, (w_up, w_down) = (
            weights_in[layer_id], weights_out[layer_id], weights_ff[layer_id],
        )
        (hidden, inverse, units, qkv, attended, stats, middle, inverse_ff, normed_ff,
         activated, slope) = records[layer_id]
        grad_low = gather_rows(upstream.astype(bf16), ff_group)
        grad_pre = (contract(grad_low, w_down, 1, 1) * slope).astype(bf16)
        grad_normed = scatter_sum(
            jnp.dot(grad_pre, w_up, preferred_element_type=f32), ff_group, ff_members
        )
        grad_pair = jnp.concatenate(
            [contract(grad_pre, normed_ff, 0, 0), contract(activated, grad_low, 0, 0)], axis=1
        ).astype(bf16)
        grads_ff[layer_id] = lax.psum_scatter(
            grad_pair, ff_spare, scatter_dimension=0, tiled=True
        ).astype(f32)
        grads_gain_ff[layer_id] = jnp.sum(grad_normed * middle * inverse_ff, axis=0)
        grad_middle = upstream + unit_norm_back(
            middle, inverse_ff, grad_normed * gain_ff[layer_id]
        )
        branch = gather_rows(grad_middle.astype(bf16), group)
        if split > 1:
            branch = lax.dynamic_slice_in_dim(branch, query_part * query_rows, query_rows, 0)
        grad_attended = contract(branch, w_out, 1, 1).astype(bf16)
        grad_qkv, grad_near, grad_far = attention_back(
            qkv, doc_row, doc_col, attended, grad_attended, stats, first, place, table, near, split
        )
        grads_table[layer_id] = (grad_near, grad_far)
        grad_units = scatter_sum(contract(grad_qkv, w_in, 1, 1), group, blocks)
        upstream = grad_middle + unit_norm_back(hidden, inverse, grad_units)
        grad_out = lax.dynamic_update_slice_in_dim(
            jnp.zeros((model_width, model_width), bf16),
            contract(attended, branch, 0, 0).astype(bf16),
            out_row,
            0,
        )
        grads_out[layer_id] = lax.psum_scatter(
            grad_out, everyone, scatter_dimension=0, tiled=True
        ).astype(f32)
        grads_in[layer_id] = contract(units, grad_qkv, 0, 0).astype(bf16)

    bucket_count = table.shape[0]
    grad_table = sum(
        bucket_grads(jnp.zeros((1,), jnp.int32), entry, bucket_count) for entry in grads_table
    )[:, :heads_dev]
    grad_table = lax.dynamic_update_slice_in_dim(
        jnp.zeros((bucket_count, heads_all), f32), grad_table, head_group * heads_dev, 1
    )
    grad_table = jnp.transpose(
        grad_table.reshape(blocks, bucket_count // blocks, heads_n, heads_all // heads_n),
        (2, 0, 1, 3),
    ).reshape(devices, -1)
    grad_gain_ff = jnp.transpose(
        jnp.stack(grads_gain_ff).reshape(layer_count, devices, weight_rows), (1, 0, 2)
    ).reshape(devices, -1)
    ends = jnp.sum(swap(jnp.concatenate([grad_gain_ff, grad_table], axis=1)), axis=0)
    grad_gain_ff = ends[: layer_count * weight_rows].reshape(layer_count, weight_rows)
    grad_bias_table = ends[layer_count * weight_rows :].reshape(
        bucket_count // blocks, heads_all // heads_n
    )
    grads_attn_in, grads_gains = [], []
    for layer_id in range(layer_count):
        parts = swap(grads_in[layer_id].reshape(devices, weight_rows, 3 * width)).astype(f32)
        parts = jnp.sum(parts.reshape(heads_n, blocks, weight_rows, 3 * width), axis=0)
        parts = jnp.sum(parts.reshape(head_groups, split, weight_rows, 3, width), axis=1)
        unit_grad = jnp.transpose(parts, (1, 2, 0, 3)).reshape(weight_rows, 3 * model_width)
        grads_attn_in.append(unit_grad * gain_attn[layer_id])
        grads_gains.append(
            jnp.stack(
                [jnp.sum(unit_grad * own_in[layer_id], axis=1), grad_gain_ff[layer_id]], axis=1
            )
        )
    return (
        output[None],
        upstream[None],
        jnp.stack(grads_attn_in),
        jnp.stack(grads_out),
        jnp.stack([entry[:, :model_width] for entry in grads_ff]),
        jnp.stack([entry[:, model_width:] for entry in grads_ff]),
        jnp.stack(grads_gains),
        grad_bias_table,
    )


def local_plane(tokens, doc_start, bias_table, attn_in, attn_out, ff_in, ff_out, gains, cotangent):
    heads_n, z_n, core_n = (lax.axis_size(axis) for axis in everyone)
    devices = heads_n * z_n * core_n
    at_head, at_z, at_core = (lax.axis_index(axis) for axis in everyone)
    members = heads_n * core_n
    block_rows, model_width = tokens.shape[1:]
    layer_count, weight_rows = attn_in.shape[:2]
    length = block_rows * members
    heads_all = bias_table.shape[1]
    heads_dev = heads_all // members
    width = heads_dev * head_dim
    member = at_head * core_n + at_core
    turn = [
        ((h * z_n + z) * core_n + c, ((h ^ z) * z_n + h) * core_n + c)
        for h in range(heads_n)
        for z in range(z_n)
        for c in range(core_n)
    ]
    turn_back = [(target, source) for source, target in turn]
    place = jnp.stack(
        [
            (at_head ^ bits) * core_n + (at_core ^ other)
            for other in range(core_n)
            for bits in range(heads_n)
        ]
        + [at_z]
        + [
            (at_head ^ bits ^ at_z) * core_n + (at_core ^ other)
            for other in range(core_n)
            for bits in range(heads_n)
        ]
    ).astype(jnp.int32)

    def relay(array):
        return lax.ppermute(array, everyone, turn)

    def relay_back(array):
        return lax.ppermute(array, everyone, turn_back)

    def swap(array):
        return lax.all_to_all(array, everyone, 0, 0, tiled=True)

    row_shape = (block_rows, model_width)
    share_shape = (members // 2 * weight_rows, 3 * width)
    gain_attn = gains[:, :, 0].astype(f32)[:, :, None]
    shares_in = call(
        share_in_kernel, [(share_shape, bf16)] * 2 * layer_count, place, attn_in, gain_attn, smem=1
    )

    quarter_turns = [
        [
            (z * core_n + c, (2 * c + (a ^ z % 2)) * core_n + (b ^ z // 2))
            for z in range(z_n)
            for c in range(core_n)
        ]
        for a in range(2)
        for b in range(2)
    ]

    def fetch_out(layer_id, hold):
        held = after(attn_out[layer_id], hold)
        return [
            lax.ppermute(held, ("z", "core"), [(holder, user) for user, holder in turns])
            for turns in quarter_turns
        ]

    starts = jnp.broadcast_to(
        doc_start.astype(f32)[None, :, None], (heads_n, z_n, core_n, block_rows)
    )
    ff_gains = gains[:, :, 1].astype(f32).reshape(1, -1)
    small = jnp.concatenate(
        [
            starts.reshape(devices, block_rows),
            jnp.broadcast_to(ff_gains, (devices, layer_count * weight_rows)),
        ],
        axis=1,
    )
    table, strip = prepare(bias_table, member * heads_dev, heads_dev)
    hidden, small, strip = tie(relay(tokens[0]), swap(small), strip)
    doc_row = small[:members, :block_rows].reshape(2, 2, core_n, block_rows)
    at_block = at_head ^ at_z
    for axis, bit in ((0, at_block // 2), (1, at_block % 2), (2, at_core)):
        doc_row = jnp.where(bit == 1, jnp.flip(doc_row, axis), doc_row)
    doc_row = jnp.transpose(doc_row, (2, 0, 1, 3)).reshape(1, length)
    doc_col = doc_row.reshape(length, 1)
    gain_ff = jnp.transpose(
        small[:, block_rows:].reshape(devices, layer_count, weight_rows), (1, 0, 2)
    ).reshape(layer_count, 1, model_width)

    def round_planes(array, by, hold):
        return shift(after(array, hold), by)

    def fetch_ff(layer_id, by, hold):
        return [round_planes(array[layer_id], by, hold) for array in (ff_in, ff_out)]

    def ff_first(rows, layer_id, lower, upper, opposite, kind):
        parts = [
            part
            for side, array in enumerate((ff_in, ff_out))
            for part in (array[layer_id], lower[side], upper[side], opposite[side])
        ]
        units = 4 * ff_in.shape[1]
        return by_rows(
            ff_first_kernel,
            256,
            [rows],
            parts,
            [(units, bf16), (units, bf16), (model_width, kind)],
            [(units, 2 * model_width)],
        )

    def ff_forward(normed, layer_id, *weights):
        *near, pair = ff_first(normed[0], layer_id, *weights, f32)
        units = pair.shape[0]
        far = by_rows(
            ff_kernel,
            256,
            [normed[1]],
            [pair],
            [(units, bf16), (units, bf16), (model_width, bf16)],
        )
        return pair, *zip(near, far)

    def ff_backward(low, slopes, pair):
        return zip(
            *(
                by_rows(
                    ff_back_kernel,
                    256,
                    [rows, slope],
                    [pair],
                    [(pair.shape[0], bf16), (model_width, kind)],
                )
                for rows, slope, kind in zip(low, slopes, (f32, bf16))
            )
        )

    def pair_chips(near, arrived, axis):
        rows, columns = near.shape[0] // 4, near.shape[1]
        shape = (2 * rows, columns) if axis == 0 else (rows, 2 * columns)
        return call(functools.partial(pair_kernel, axis), [(shape, bf16)] * 4, near, arrived)

    def share_chips(blocks):
        return [blocks[0]] + [toggle(blocks[bits], "head", bits) for bits in (1, 2, 3)]

    units_shape = [(row_shape, f32), (row_shape, bf16)]
    def fetch_plane(layer_id, hold):
        near, far = after(tuple(shares_in[2 * layer_id : 2 * layer_id + 2]), hold)
        return share_chips(pair_chips(near, toggle(far, "core", 1), 0))

    def join(shares):
        return call(join_kernel, [((weight_rows * members, 3 * width), bf16)], *shares)[0]

    def assemble_in(share, lower, upper, opposite):
        return call(
            assemble_in_kernel,
            [((model_width, 3 * width), bf16)],
            place,
            share,
            lower,
            upper,
            opposite,
            smem=1,
        )[0]

    hidden, shares = tie(hidden, fetch_plane(0, shares_in[0]))
    hidden, unit_rows = call(unit_kernel, units_shape, hidden)
    share = join(shares)
    near, far, lower, upper, opposite, quarters, doc_row, doc_col, gain_ff = plane_gather(
        unit_rows,
        shift(share, 1),
        shift(share, -1),
        shift(share, 2),
        fetch_out(0, hidden),
        doc_row,
        doc_col,
        gain_ff,
    )
    units = (near, far)
    w_in = assemble_in(share, lower, upper, opposite)
    w_out, qkv, attended, stats, *parts = plane_attention(
        *units, w_in, quarters, doc_row, doc_col, place, table, strip
    )
    parts, upstream = tie(parts, relay(after(cotangent[0].astype(bf16), near)))
    parts, own = plane_scatter(*parts)
    parts, lower, upper, shares = tie(
        parts, fetch_ff(0, 1, own), fetch_ff(0, -1, own), fetch_plane(1, own)
    )
    middle, normed_rows = call(close_gain_kernel, units_shape, hidden, *parts, gain_ff[0])
    near, far, opposite = plane_gather(normed_rows, fetch_ff(0, 2, normed_rows))
    normed = (near, far)
    pair, acts, slopes, parts = ff_forward(normed, 0, lower, upper, opposite)
    records = [
        (hidden, units, w_in, w_out, pair, qkv, attended, stats, middle, normed, acts, slopes)
    ]
    share = join(after(shares, near))
    parts, own = plane_scatter(*parts)
    parts, *shares = tie(
        parts,
        round_planes(share, 1, own),
        round_planes(share, -1, own),
        round_planes(share, 2, own),
    )
    hidden, unit_rows = call(close_kernel, units_shape, middle, *parts)

    near, far, lower, quarters = plane_gather(
        unit_rows, fetch_ff(1, 1, unit_rows), fetch_out(1, unit_rows)
    )
    units = (near, far)
    w_in = assemble_in(share, *shares)
    w_out, qkv, attended, stats, *parts = plane_attention(
        *units, w_in, quarters, doc_row, doc_col, place, table, strip
    )
    low = plane_gather(after(upstream, far))
    parts, near_low, upper = tie(parts, low[0], fetch_ff(1, -1, far))
    low = (near_low, low[1])
    parts, own = plane_scatter(*parts)
    parts, opposite_in = tie(parts, round_planes(ff_in[1], 2, own))
    middle, normed_rows = call(close_gain_kernel, units_shape, hidden, *parts, gain_ff[1])
    near, far, opposite_out = plane_gather(normed_rows, round_planes(ff_out[1], 2, normed_rows))
    normed = (near, far)
    pair, acts, slopes, last_parts = ff_forward(
        normed, 1, lower, upper, [opposite_in, opposite_out]
    )
    records.append(
        (hidden, units, w_in, w_out, pair, qkv, attended, stats, middle, normed, acts, slopes)
    )

    def back_to_middle(parts, upstream, middle, gain):
        return call(
            middle_back_kernel, units_shape + [((1, model_width), f32)], upstream, *parts, middle, gain
        )

    def attention_grads(record, branch):
        _, _, w_in, w_out, _, qkv, attended, stats, *_ = record
        grad_qkv, grad_near, grad_far, near_part, far_part, *quarters = plane_attention_back(
            qkv, doc_row, doc_col, attended, stats, *branch, w_in, w_out, place, table, strip
        )
        return grad_qkv, (grad_near, grad_far), (near_part, far_part), quarters

    def owners_quarters(quarters):
        return [
            lax.ppermute(quarter, ("z", "core"), turns)
            for quarter, turns in zip(quarters, quarter_turns)
        ]

    def table_grads(near_and_far):
        return bucket_grads(at_core.reshape(1) * heads_dev, near_and_far, table.shape[0])

    def add_in(own, lower, upper, opposite):
        return call(add_in_kernel, [(share_shape, bf16)] * 2, own, lower, upper, opposite)

    record = records[1]
    hidden, units, _, _, pair, *_, middle, normed, acts, slopes = record
    pres, parts = ff_backward(low, slopes, pair)
    parts, own = plane_scatter(*parts)
    planes = ff_grads(after(pres, own), acts, normed, low)
    parts, ff_lower = tie(parts, shift(planes[1], -1))
    last_parts, _ = plane_scatter(*after(last_parts, parts))
    grad_middle, branch_rows, gain_1 = back_to_middle(parts, upstream, middle, gain_ff[1])
    *branch, ff_upper = plane_gather(branch_rows, round_planes(planes[2], 1, branch_rows))
    grad_qkv, strips_1, parts, quarters = attention_grads(record, branch)
    parts, last_parts, opposite_up = tie(
        parts, last_parts, round_planes(planes[3], 2, branch[1])
    )
    parts, own = plane_scatter(*parts)
    grad_in = in_grads(place, *units, after(grad_qkv, own))
    parts, opposite_down, in_opposite, output, table_1 = tie(
        parts,
        round_planes(planes[4], 2, own),
        shift(grad_in[3], 2),
        call(last_kernel, [(row_shape, bf16)], middle, *after(last_parts, own))[0],
        table_grads(after(strips_1, own)),
    )
    grads_ff = [planes[0], ff_lower, ff_upper, opposite_up, opposite_down]
    upstream, low_rows = call(layer_back_kernel, units_shape, grad_middle, *parts, hidden)

    record = records[0]
    hidden, units, _, _, pair, *_, middle, normed, acts, slopes = record
    *low, in_lower, in_upper, quarters_1 = plane_gather(
        low_rows,
        round_planes(grad_in[1], -1, low_rows),
        round_planes(grad_in[2], 1, low_rows),
        owners_quarters(after(quarters, low_rows)),
    )
    pres, parts = ff_backward(low, slopes, pair)
    parts, own = plane_scatter(*parts)
    near_in, far_in = add_in(*after([grad_in[0], in_lower, in_upper, in_opposite], own))
    planes = ff_grads(after(pres, own), acts, normed, low)
    parts, ff_lower, far_in = tie(parts, shift(planes[1], -1), toggle(far_in, "core", 1))
    grad_middle, branch_rows, gain_0 = back_to_middle(parts, upstream, middle, gain_ff[0])
    *branch, ff_upper, opposite_up, shares_1 = plane_gather(
        branch_rows,
        round_planes(planes[2], 1, branch_rows),
        round_planes(planes[3], 2, branch_rows),
        share_chips(pair_chips(near_in, after(far_in, branch_rows), 1)),
    )
    grad_qkv, strips_0, parts, quarters = attention_grads(record, branch)
    parts, output = tie(parts, relay_back(after(output, branch[1])))
    parts, own = plane_scatter(*parts)
    grad_in = in_grads(place, *units, after(grad_qkv, own))
    parts, opposite_down, in_opposite, table_0, output = tie(
        parts,
        round_planes(planes[4], 2, own),
        shift(grad_in[3], 2),
        table_grads(after(strips_0, own)),
        after(output, own).astype(f32),
    )
    grads_ff = [planes[0], ff_lower, ff_upper, opposite_up, opposite_down] + grads_ff
    upstream, low_rows = call(layer_back_kernel, units_shape, grad_middle, *parts, hidden)
    grad_tokens = relay_back(low_rows)
    in_lower = round_planes(grad_in[1], -1, low_rows)
    in_upper = round_planes(grad_in[2], 1, low_rows)
    grad_up, grad_down = call(finish_ff_kernel, [(ff_in.shape, f32)] * 2, *after(grads_ff, low_rows))
    quarters_0 = owners_quarters(after(quarters, low_rows))
    near_in, far_in = add_in(grad_in[0], in_lower, in_upper, in_opposite)
    shares_0 = share_chips(pair_chips(near_in, toggle(far_in, "core", 1), 1))
    (ends,) = call(
        functools.partial(ends_kernel, z_n),
        [((devices, 8, tile), f32)],
        place,
        *after([gain_0, gain_1, table_0, table_1], low_rows),
        smem=1,
    )
    (grad_attn_out,) = call(finish_out_kernel, [(attn_out.shape, f32)], *quarters_0, *quarters_1)
    own_buckets = table.shape[0] // (z_n * core_n)
    grad_attn_in, grad_gains, grad_table = call(
        functools.partial(finish_in_kernel, layer_count),
        [(attn_in.shape, f32), (gains.shape, f32), ((own_buckets, tile), f32)],
        place,
        *shares_0,
        *shares_1,
        attn_in,
        gain_attn,
        swap(ends),
        smem=1,
    )
    return (
        output[None],
        grad_tokens.astype(f32)[None],
        grad_attn_in,
        grad_attn_out,
        grad_up,
        grad_down,
        grad_gains,
        grad_table[:, : heads_all // heads_n],
    )


def solution(mesh):
    sizes = dict(mesh.shape)
    cores = 2
    fine = Mesh(
        mesh.devices.reshape(sizes["head"], sizes["blk"] // cores, cores), everyone
    )
    blk = ("z", "core")
    in_specs = (
        P("head", blk, None),
        P(None, blk),
        P(),
        P(None, everyone, None),
        P(None, everyone, None),
        P(None, everyone, None),
        P(None, everyone, None),
        P(None, everyone, None),
        P("head", blk, None),
    )
    out_specs = (
        P("head", blk, None),
        P("head", blk, None),
        P(None, everyone, None),
        P(None, everyone, None),
        P(None, everyone, None),
        P(None, everyone, None),
        P(None, everyone, None),
        P(blk, "head"),
    )
    plane = sizes["head"] == 4 and sizes["blk"] == 8
    local = local_plane if plane else local_general
    return jax.shard_map(local, mesh=fine, in_specs=in_specs, out_specs=out_specs, check_vma=False)
```

```python
import functools

import jax
import jax.numpy as jnp
import numpy as np
from jax import lax
from jax.experimental import pallas as pl
from jax.experimental.pallas import tpu as pltpu
from jax.sharding import Mesh
from jax.sharding import PartitionSpec as P

bounds = (1, 2, 3, 4, 5, 6, 7, 8, 12, 16, 23, 32, 46, 64, 91)
epsilon = 1e-06
masked = -1e30
score_scale = 0.125
head_dim = 64
tile = 128
everyone = ("head", "z", "core")
bf16 = jnp.bfloat16
f32 = jnp.float32


def contract(lhs, rhs, lhs_dim, rhs_dim):
    return lax.dot_general(
        lhs, rhs, (((lhs_dim,), (rhs_dim,)), ((), ())), preferred_element_type=f32
    )


def near_buckets(shape):
    offsets = (
        lax.broadcasted_iota(jnp.int32, shape, 1) - tile - lax.broadcasted_iota(jnp.int32, shape, 0)
    )
    distance = jnp.abs(offsets)
    bucket = jnp.where(offsets > 0, 16, 0)
    for boundary in bounds:
        bucket = bucket + jnp.where(distance >= boundary, 1, 0)
    return bucket


def near_kernel(table, near):
    bucket = near_buckets(near.shape[1:])
    for head in range(near.shape[0]):
        values = jnp.zeros(near.shape[1:], f32)
        for bucket_id in range(table.shape[0]):
            values = jnp.where(bucket == bucket_id, table[bucket_id, head], values)
        near[head] = values


def bucket_kernel(first_lane, near, far, out):
    bucket = near_buckets(near.shape[1:])
    rows = lax.broadcasted_iota(jnp.int32, out.shape, 0)
    lanes = lax.broadcasted_iota(jnp.int32, out.shape, 1)
    total = jnp.zeros(out.shape, f32)
    for head in range(near.shape[0]):
        strip = near[head]
        for bucket_id in range(out.shape[0]):
            value = jnp.sum(jnp.where(bucket == bucket_id, strip, 0.0), axis=0, keepdims=True)
            value = jnp.sum(value, axis=1, keepdims=True)
            if bucket_id in (15, 31):
                value = value + far[head, bucket_id // 16, :1, :1]
            total = jnp.where((rows == bucket_id) & (lanes == head + first_lane[0]), value, total)
    out[...] = total


def fill_band(band, table, near, heads_dev, length):
    for head in range(heads_dev):
        band[head, :, : length - tile] = jnp.full((tile, length - tile), table[15, head], f32)
        band[head, :, length - tile : length + 2 * tile] = near[head]
        band[head, :, length + 2 * tile :] = jnp.full(
            (tile, length - 2 * tile), table[31, head], f32
        )


def band_starts(place, at, length, skip=0):
    return [
        pl.multiple_of(length + (place[skip + block] - place[skip + at]) * tile, tile)
        for block in range(length // tile)
    ]


def attention_kernel(
    heads_dev, length, first, place, table, near, qkv, doc_row, doc_col, out, local, stats, band
):
    step = pl.program_id(0)
    width = heads_dev * head_dim

    @pl.when(step == 0)
    def _():
        fill_band(band, table, near, heads_dev, length)

    row = pl.multiple_of((first[0] + step) * tile, tile)
    out_row = pl.multiple_of((place[first[0] + step] - first[0]) * tile, tile)
    starts = band_starts(place, first[0] + step, length)
    same_doc = doc_col[...] == doc_row[...]
    queries = qkv[pl.ds(row, tile), :width] * bf16(score_scale)
    lanes = lax.broadcasted_iota(jnp.int32, (tile, tile), 1)
    collected = jnp.zeros((tile, tile), f32)
    for head in range(heads_dev):
        own = slice(head * head_dim, (head + 1) * head_dim)
        keys = qkv[:, width + own.start : width + own.stop]
        values = qkv[:, 2 * width + own.start : 2 * width + own.stop]
        scores = contract(queries[:, own], keys, 1, 1)
        scores = scores + jnp.concatenate(
            [band[head, :, pl.ds(start, tile)] for start in starts], axis=1
        )
        scores = jnp.where(same_doc, scores, masked)
        peak = jnp.max(scores, axis=1, keepdims=True)
        weights = jnp.exp(scores - peak)
        total = jnp.sum(weights, axis=1, keepdims=True)
        mixed = contract(weights.astype(bf16), values, 1, 0) / total
        out[pl.ds(out_row, tile), own] = mixed.astype(bf16)
        local[:, own] = mixed.astype(bf16)
        collected = jnp.where(lanes == head, peak + jnp.log(total), collected)
    stats[...] = collected


def attention_back_kernel(
    heads_dev, length, split, first, place, table, near, qkv, doc_row, doc_col, attended, grad_out, stats,
    grad_qkv, grad_near, grad_far, band, grad_band, grad_keys, grad_values,
):
    step = pl.program_id(0)
    width = heads_dev * head_dim

    @pl.when(step == 0)
    def _():
        fill_band(band, table, near, heads_dev, length)
        grad_band[...] = jnp.zeros_like(grad_band)
        grad_keys[...] = jnp.zeros_like(grad_keys)
        grad_values[...] = jnp.zeros_like(grad_values)
        if split > 1:
            grad_qkv[...] = jnp.zeros_like(grad_qkv)

    row = pl.multiple_of((first[0] + step) * tile, tile)
    out_row = pl.multiple_of((place[first[0] + step] - first[0]) * tile, tile)
    starts = band_starts(place, first[0] + step, length)
    same_doc = doc_col[...] == doc_row[...]
    at_step = pl.multiple_of(step * tile, tile)
    queries = qkv[pl.ds(row, tile), :width] * bf16(score_scale)
    for head in range(heads_dev):
        own = slice(head * head_dim, (head + 1) * head_dim)
        keys = qkv[:, width + own.start : width + own.stop]
        values = qkv[:, 2 * width + own.start : 2 * width + own.stop]
        upstream = grad_out[pl.ds(out_row, tile), own]
        scores = contract(queries[:, own], keys, 1, 1) + jnp.concatenate(
            [band[head, :, pl.ds(start, tile)] for start in starts], axis=1
        )
        scores = jnp.where(same_doc, scores, masked)
        weights = jnp.exp(scores - stats[:, head : head + 1])
        delta = jnp.sum(
            upstream.astype(f32) * attended[pl.ds(at_step, tile), own].astype(f32),
            axis=1,
            keepdims=True,
        )
        grad_scores = weights * (contract(upstream, values, 1, 1) - delta)
        for block, start in enumerate(starts):
            grad_band[head, :, pl.ds(start, tile)] += grad_scores[
                :, block * tile : (block + 1) * tile
            ]
        grad_low = grad_scores.astype(bf16)
        grad_values[:, own] += contract(weights.astype(bf16), upstream, 0, 0)
        grad_keys[:, own] += contract(grad_low, queries[:, own], 0, 0)
        grad_qkv[pl.ds(row, tile), own] = (
            contract(grad_low, keys, 1, 0) * score_scale
        ).astype(bf16)

    @pl.when(step == pl.num_programs(0) - 1)
    def _():
        grad_qkv[:, width : 2 * width] = grad_keys[...].astype(bf16)
        grad_qkv[:, 2 * width :] = grad_values[...].astype(bf16)
        for head in range(heads_dev):
            grad_near[head] = grad_band[head, :, length - tile : length + 2 * tile]
            grad_far[head, 0] = jnp.full(
                (8, tile), jnp.sum(grad_band[head, :, : length - tile]), f32
            )
            grad_far[head, 1] = jnp.full(
                (8, tile), jnp.sum(grad_band[head, :, length + 2 * tile :]), f32
            )


def whole(shape):
    return pl.BlockSpec(shape, lambda step: (0,) * len(shape), pipeline_mode=pl.Buffered(1))


def attention(qkv, doc_row, doc_col, first, place, table, near, rows):
    length = qkv.shape[0]
    heads_dev = table.shape[1]
    width = heads_dev * head_dim
    return pl.pallas_call(
        functools.partial(attention_kernel, heads_dev, length),
        grid=(rows // tile,),
        in_specs=[
            pl.BlockSpec(memory_space=pltpu.SMEM),
            pl.BlockSpec(memory_space=pltpu.SMEM),
            pl.BlockSpec(memory_space=pltpu.SMEM),
            whole(near.shape),
            whole(qkv.shape),
            whole(doc_row.shape),
            pl.BlockSpec((tile, 1), lambda step: (step, 0)),
        ],
        out_specs=[
            whole((rows, width)),
            pl.BlockSpec((tile, width), lambda step: (step, 0)),
            pl.BlockSpec((tile, tile), lambda step: (step, 0)),
        ],
        out_shape=[
            jax.ShapeDtypeStruct((rows, width), bf16),
            jax.ShapeDtypeStruct((rows, width), bf16),
            jax.ShapeDtypeStruct((rows, tile), f32),
        ],
        scratch_shapes=[pltpu.VMEM((heads_dev, tile, 2 * length), f32)],
        compiler_params=pltpu.CompilerParams(vmem_limit_bytes=40 * 2**20),
        cost_estimate=pl.CostEstimate(
            flops=4 * rows * length * width,
            bytes_accessed=4 * length * width * 2,
            transcendentals=rows * length * heads_dev,
        ),
    )(first, place, table, near, qkv, doc_row, doc_col)


def attention_back(
    qkv, doc_row, doc_col, attended, grad_out, stats, first, place, table, near, split
):
    length = qkv.shape[0]
    rows = grad_out.shape[0]
    heads_dev = table.shape[1]
    width = heads_dev * head_dim
    return pl.pallas_call(
        functools.partial(attention_back_kernel, heads_dev, length, split),
        grid=(rows // tile,),
        in_specs=[
            pl.BlockSpec(memory_space=pltpu.SMEM),
            pl.BlockSpec(memory_space=pltpu.SMEM),
            pl.BlockSpec(memory_space=pltpu.SMEM),
            whole(near.shape),
            whole(qkv.shape),
            whole(doc_row.shape),
            pl.BlockSpec((tile, 1), lambda step: (step, 0)),
            whole((rows, width)),
            whole((rows, width)),
            pl.BlockSpec((tile, tile), lambda step: (step, 0)),
        ],
        out_specs=[
            whole((length, 3 * width)),
            whole((heads_dev, tile, 3 * tile)),
            whole((heads_dev, 2, 8, tile)),
        ],
        out_shape=[
            jax.ShapeDtypeStruct((length, 3 * width), bf16),
            jax.ShapeDtypeStruct((heads_dev, tile, 3 * tile), f32),
            jax.ShapeDtypeStruct((heads_dev, 2, 8, tile), f32),
        ],
        scratch_shapes=[
            pltpu.VMEM((heads_dev, tile, 2 * length), f32),
            pltpu.VMEM((heads_dev, tile, 2 * length), f32),
            pltpu.VMEM((length, width), f32),
            pltpu.VMEM((length, width), f32),
        ],
        compiler_params=pltpu.CompilerParams(vmem_limit_bytes=48 * 2**20),
        cost_estimate=pl.CostEstimate(
            flops=10 * rows * length * width,
            bytes_accessed=8 * length * width * 2,
            transcendentals=rows * length * heads_dev,
        ),
    )(first, place, table, near, qkv, doc_row, doc_col, attended, grad_out, stats)


def call(kernel, shapes, *operands, smem=0):
    return pl.pallas_call(
        kernel,
        in_specs=[pl.BlockSpec(memory_space=pltpu.SMEM)] * smem
        + [pl.BlockSpec(memory_space=pltpu.VMEM)] * (len(operands) - smem),
        out_specs=[pl.BlockSpec(memory_space=pltpu.VMEM)] * len(shapes),
        out_shape=[jax.ShapeDtypeStruct(shape, kind) for shape, kind in shapes],
        compiler_params=pltpu.CompilerParams(vmem_limit_bytes=10 * 2**20),
    )(*operands)


def share_in_kernel(place, attn_in, gains, near, far):
    layers, rows = attn_in.shape[:2]
    half = near.shape[0] // (layers * rows)
    width = near.shape[1] // 3
    for index in range(2 * half):
        member = place[index]
        for layer_id in range(layers):
            block = jnp.concatenate(
                [
                    attn_in[
                        layer_id,
                        :,
                        pl.ds(pl.multiple_of((part * 2 * half + member) * width, width), width),
                    ]
                    for part in range(3)
                ],
                axis=1,
            )
            at = (index % half * layers + layer_id) * rows
            out = near if index < half else far
            out[at : at + rows] = (block.astype(f32) * gains[layer_id]).astype(bf16)


def join_kernel(*refs):
    shares, outs = refs[:4], refs[4:]
    rows = outs[0].shape[0] // 8
    for chip, share in enumerate(shares):
        for core in range(2):
            for layer_id, out in enumerate(outs):
                source = (core * len(outs) + layer_id) * rows
                target = (chip * 2 + core) * rows
                out[target : target + rows] = share[source : source + rows]


def row_of(chip, plane, core, rows, planes=4):
    return pl.multiple_of(((chip * planes + plane) * 2 + core) * rows, rows)


def assemble_in_kernel(place, own, lower, upper, opposite, out):
    at_z, at_core, at_head = place[8], place[0] % 2, place[0] // 2
    rows = own.shape[0] // 8
    for part, offset in ((own, 0), (lower, 3), (upper, 1), (opposite, 2)):
        plane = (at_z + offset) % 4
        for index in range(8):
            row = row_of(at_head ^ (index // 2), plane, at_core ^ (index % 2), rows)
            out[pl.ds(row, rows)] = part[index * rows : (index + 1) * rows]


def plane_attention_kernel(
    length, place, table, strip, near, far, w_in, *refs
):
    quarters, (doc_row, doc_col, w_out, qkv, attended, stats, near_part, far_part, band) = (
        refs[:4], refs[4:],
    )
    step = pl.program_id(0)
    half = length // 2
    heads_dev = table.shape[1]
    width = heads_dev * head_dim

    @pl.when(step == 0)
    def _():
        fill_band(band, table, strip, heads_dev, length)
        at_z = place[length // tile]
        rows = width // 4
        for index, quarter in enumerate(quarters):
            block = (index // 2 ^ at_z % 2) * 2 + (index % 2 ^ at_z // 2)
            w_out[pl.ds(pl.multiple_of(block * rows, rows), rows)] = quarter[...]
        qkv[:half] = contract(near[...], w_in[...], 1, 0).astype(bf16)
        qkv[half:] = contract(far[...], w_in[...], 1, 0).astype(bf16)

    row = pl.multiple_of(step * tile, tile)
    starts = band_starts(place, step, length, length // tile + 1)
    same_doc = doc_col[...] == doc_row[...]
    queries = qkv[pl.ds(row, tile), :width] * bf16(score_scale)
    lanes = lax.broadcasted_iota(jnp.int32, (tile, tile), 1)
    collected = jnp.zeros((tile, tile), f32)
    results = []
    for head in range(heads_dev):
        own = slice(head * head_dim, (head + 1) * head_dim)
        keys = qkv[:, width + own.start : width + own.stop]
        values = qkv[:, 2 * width + own.start : 2 * width + own.stop]
        scores = contract(queries[:, own], keys, 1, 1) + jnp.concatenate(
            [band[head, :, pl.ds(start, tile)] for start in starts], axis=1
        )
        scores = jnp.where(same_doc, scores, masked)
        peak = jnp.max(scores, axis=1, keepdims=True)
        weights = jnp.exp(scores - peak)
        total = jnp.sum(weights, axis=1, keepdims=True)
        results.append((contract(weights.astype(bf16), values, 1, 0) / total).astype(bf16))
        collected = jnp.where(lanes == head, peak + jnp.log(total), collected)
    stats[...] = collected
    merged = jnp.concatenate(results, axis=1)
    attended[...] = merged
    part = contract(merged, w_out[...], 1, 0)

    @pl.when(row < half)
    def _():
        near_part[...] = part

    @pl.when(row >= half)
    def _():
        far_part[...] = part.astype(bf16)


def near_block(steps, columns):
    return pl.BlockSpec((tile, columns), lambda step: (jnp.minimum(step, steps // 2 - 1), 0))


def far_block(steps, columns):
    return pl.BlockSpec((tile, columns), lambda step: (jnp.maximum(step - steps // 2, 0), 0))


def plane_attention(near, far, w_in, quarters, doc_row, doc_col, place, table, strip):
    length, model_width = 2 * near.shape[0], near.shape[1]
    steps = length // tile
    heads_dev = table.shape[1]
    width = heads_dev * head_dim
    return pl.pallas_call(
        functools.partial(plane_attention_kernel, length),
        grid=(steps,),
        in_specs=[
            pl.BlockSpec(memory_space=pltpu.SMEM),
            pl.BlockSpec(memory_space=pltpu.SMEM),
            whole(strip.shape),
            whole(near.shape),
            whole(far.shape),
            whole(w_in.shape),
            *[whole(quarter.shape) for quarter in quarters],
            whole(doc_row.shape),
            pl.BlockSpec((tile, 1), lambda step: (step, 0)),
        ],
        out_specs=[
            whole((width, model_width)),
            whole((length, 3 * width)),
            pl.BlockSpec((tile, width), lambda step: (step, 0)),
            pl.BlockSpec((tile, tile), lambda step: (step, 0)),
            near_block(steps, model_width),
            far_block(steps, model_width),
        ],
        out_shape=[
            jax.ShapeDtypeStruct((width, model_width), bf16),
            jax.ShapeDtypeStruct((length, 3 * width), bf16),
            jax.ShapeDtypeStruct((length, width), bf16),
            jax.ShapeDtypeStruct((length, tile), f32),
            jax.ShapeDtypeStruct((length // 2, model_width), f32),
            jax.ShapeDtypeStruct((length // 2, model_width), bf16),
        ],
        scratch_shapes=[pltpu.VMEM((heads_dev, tile, 2 * length), f32)],
        compiler_params=pltpu.CompilerParams(vmem_limit_bytes=14 * 2**20),
        cost_estimate=pl.CostEstimate(
            flops=4 * length * length * width + 8 * length * model_width * width,
            bytes_accessed=12 * 2**20,
            transcendentals=length * length * heads_dev,
        ),
    )(place, table, strip, near, far, w_in, *quarters, doc_row, doc_col)


def plane_attention_back_kernel(
    length, place, table, strip, qkv, doc_row, doc_col, attended, stats, near, far, w_in, w_out,
    grad_qkv, grad_near, grad_far, near_part, far_part, *rest
):
    quarters, (band, grad_band, grad_keys, grad_values, out_sum) = rest[:4], rest[4:]
    step = pl.program_id(0)
    half = length // 2
    heads_dev = table.shape[1]
    width = heads_dev * head_dim

    @pl.when(step == 0)
    def _():
        fill_band(band, table, strip, heads_dev, length)
        grad_band[...] = jnp.zeros_like(grad_band)
        grad_keys[...] = jnp.zeros_like(grad_keys)
        grad_values[...] = jnp.zeros_like(grad_values)
        out_sum[...] = jnp.zeros_like(out_sum)

    row = pl.multiple_of(step * tile, tile)
    starts = band_starts(place, step, length, length // tile + 1)
    same_doc = doc_col[...] == doc_row[...]
    branch = jnp.where(row < half, near[...], far[...])
    merged = attended[...]
    grad_merged = contract(branch, w_out[...], 1, 1).astype(bf16)
    out_sum[...] += contract(merged, branch, 0, 0)
    products = grad_merged.astype(f32) * merged.astype(f32)
    queries = qkv[pl.ds(row, tile), :width] * bf16(score_scale)
    for head in range(heads_dev):
        own = slice(head * head_dim, (head + 1) * head_dim)
        keys = qkv[:, width + own.start : width + own.stop]
        values = qkv[:, 2 * width + own.start : 2 * width + own.stop]
        upstream = grad_merged[:, own]
        scores = contract(queries[:, own], keys, 1, 1) + jnp.concatenate(
            [band[head, :, pl.ds(start, tile)] for start in starts], axis=1
        )
        scores = jnp.where(same_doc, scores, masked)
        weights = jnp.exp(scores - stats[:, head : head + 1])
        delta = jnp.sum(products[:, own], axis=1, keepdims=True)
        grad_scores = weights * (contract(upstream, values, 1, 1) - delta)
        for block, start in enumerate(starts):
            grad_band[head, :, pl.ds(start, tile)] += grad_scores[
                :, block * tile : (block + 1) * tile
            ]
        grad_low = grad_scores.astype(bf16)
        grad_values[:, own] += contract(weights.astype(bf16), upstream, 0, 0)
        grad_keys[:, own] += contract(grad_low, queries[:, own], 0, 0)
        grad_qkv[pl.ds(row, tile), own] = (
            contract(grad_low, keys, 1, 0) * score_scale
        ).astype(bf16)

    @pl.when(step == pl.num_programs(0) - 1)
    def _():
        grad_qkv[:, width : 2 * width] = grad_keys[...].astype(bf16)
        grad_qkv[:, 2 * width :] = grad_values[...].astype(bf16)
        far_part[...] = contract(grad_qkv[half:], w_in[...], 1, 1).astype(bf16)
        near_part[...] = contract(grad_qkv[:half], w_in[...], 1, 1)
        at_z = place[length // tile]
        rows = width // 4
        for index, quarter in enumerate(quarters):
            block = (index // 2 ^ at_z % 2) * 2 + (index % 2 ^ at_z // 2)
            quarter[...] = out_sum[pl.ds(pl.multiple_of(block * rows, rows), rows)].astype(bf16)
        for head in range(heads_dev):
            grad_near[head] = grad_band[head, :, length - tile : length + 2 * tile]
            grad_far[head, 0] = jnp.full(
                (8, tile), jnp.sum(grad_band[head, :, : length - tile]), f32
            )
            grad_far[head, 1] = jnp.full(
                (8, tile), jnp.sum(grad_band[head, :, length + 2 * tile :]), f32
            )


def plane_attention_back(
    qkv, doc_row, doc_col, attended, stats, near, far, w_in, w_out, place, table, strip
):
    length, model_width = 2 * near.shape[0], near.shape[1]
    steps = length // tile
    heads_dev = table.shape[1]
    width = heads_dev * head_dim
    shapes = [
        ((length, 3 * width), bf16),
        ((heads_dev, tile, 3 * tile), f32),
        ((heads_dev, 2, 8, tile), f32),
        ((length // 2, model_width), f32),
        ((length // 2, model_width), bf16),
    ] + [((width // 4, model_width), bf16)] * 4
    return pl.pallas_call(
        functools.partial(plane_attention_back_kernel, length),
        grid=(steps,),
        in_specs=[
            pl.BlockSpec(memory_space=pltpu.SMEM),
            pl.BlockSpec(memory_space=pltpu.SMEM),
            whole(strip.shape),
            whole(qkv.shape),
            whole(doc_row.shape),
            pl.BlockSpec((tile, 1), lambda step: (step, 0)),
            pl.BlockSpec((tile, width), lambda step: (step, 0)),
            pl.BlockSpec((tile, tile), lambda step: (step, 0)),
            near_block(steps, model_width),
            far_block(steps, model_width),
            whole(w_in.shape),
            whole(w_out.shape),
        ],
        out_specs=[whole(shape) for shape, _ in shapes],
        out_shape=[jax.ShapeDtypeStruct(shape, kind) for shape, kind in shapes],
        scratch_shapes=[
            pltpu.VMEM((heads_dev, tile, 2 * length), f32),
            pltpu.VMEM((heads_dev, tile, 2 * length), f32),
            pltpu.VMEM((length, width), f32),
            pltpu.VMEM((length, width), f32),
            pltpu.VMEM((width, model_width), f32),
        ],
        compiler_params=pltpu.CompilerParams(vmem_limit_bytes=20 * 2**20),
        cost_estimate=pl.CostEstimate(
            flops=10 * length * length * width + 10 * length * model_width * width,
            bytes_accessed=12 * 2**20,
            transcendentals=length * length * heads_dev,
        ),
    )(place, table, strip, qkv, doc_row, doc_col, attended, stats, near, far, w_in, w_out)


def gelu_and_slope(pre_act):
    size = jnp.abs(pre_act)
    gauss = jnp.exp(-0.5 * pre_act * pre_act)
    ratio = 1.0 / (1.0 + np.float32(0.3275911 * 0.5**0.5) * size)
    series = np.float32(1.061405429)
    for factor in (-1.453152027, 1.421413741, -0.284496736, 0.254829592):
        series = series * ratio + np.float32(factor)
    tail = 0.5 * series * ratio * gauss
    cumulative = jnp.where(pre_act < 0, tail, 1.0 - tail)
    slope = cumulative + pre_act * gauss * np.float32((2 * np.pi) ** -0.5)
    return pre_act * cumulative, slope


def ff_kernel(rows, pair, activated, slope, part):
    columns = rows.shape[1]
    value, gradient = gelu_and_slope(contract(rows[...], pair[:, :columns], 1, 1))
    activated[...] = value.astype(bf16)
    slope[...] = gradient.astype(bf16)
    part[...] = contract(activated[...], pair[:, columns:], 1, 0).astype(part.dtype)


def ff_back_kernel(rows, slope, pair, grad_pre, part):
    columns = rows.shape[1]
    grad_act = contract(rows[...], pair[:, columns:], 1, 1)
    grad_pre[...] = (grad_act * slope[...].astype(f32)).astype(bf16)
    part[...] = contract(grad_pre[...], pair[:, :columns], 1, 0).astype(part.dtype)


def by_rows(kernel, step_rows, row_operands, whole_operands, outs, whole_outs=()):
    rows = row_operands[0].shape[0]
    return pl.pallas_call(
        kernel,
        grid=(rows // step_rows,),
        in_specs=[
            pl.BlockSpec((step_rows, operand.shape[1]), lambda step: (step, 0))
            for operand in row_operands
        ]
        + [whole(operand.shape) for operand in whole_operands],
        out_specs=[pl.BlockSpec((step_rows, columns), lambda step: (step, 0)) for columns, _ in outs]
        + [whole(shape) for shape in whole_outs],
        out_shape=[jax.ShapeDtypeStruct((rows, columns), kind) for columns, kind in outs]
        + [jax.ShapeDtypeStruct(shape, bf16) for shape in whole_outs],
        compiler_params=pltpu.CompilerParams(vmem_limit_bytes=10 * 2**20),
        cost_estimate=pl.CostEstimate(
            flops=4 * rows * outs[0][0] * row_operands[0].shape[1],
            bytes_accessed=6 * 2**20,
            transcendentals=0,
        ),
    )(*row_operands, *whole_operands)


def ff_grads_kernel(
    place, pre_near, pre_far, act_near, act_far, normed_near, normed_far, low_near, low_far, *outs
):
    columns = normed_near.shape[1]
    units = outs[0].shape[0]
    step = pl.program_id(0)
    offset = jnp.where(step == 1, 3, jnp.where(step == 2, 1, jnp.where(step == 3, 2, 0)))
    plane = pl.ds(pl.multiple_of((place[8] + offset) % 4 * units, units), units)
    up = (
        contract(pre_near[:, plane], normed_near[...], 0, 0)
        + contract(pre_far[:, plane], normed_far[...], 0, 0)
    ).astype(bf16)
    down = (
        contract(act_near[:, plane], low_near[...], 0, 0)
        + contract(act_far[:, plane], low_far[...], 0, 0)
    ).astype(bf16)
    for index in range(3):

        @pl.when(step == index)
        def _():
            outs[index][:, :columns] = up
            outs[index][:, columns:] = down

    @pl.when(step == 3)
    def _():
        outs[3][...] = up
        outs[4][...] = down


def ff_grads(place, pre, act, normed, low):
    rows, hidden_units = pre[0].shape
    columns = normed[0].shape[1]
    shapes = [(hidden_units // 4, 2 * columns)] * 3 + [(hidden_units // 4, columns)] * 2
    return pl.pallas_call(
        ff_grads_kernel,
        grid=(4,),
        in_specs=[pl.BlockSpec(memory_space=pltpu.SMEM)]
        + [whole((rows, hidden_units))] * 4
        + [whole((rows, columns))] * 4,
        out_specs=[whole(shape) for shape in shapes],
        out_shape=[jax.ShapeDtypeStruct(shape, bf16) for shape in shapes],
        compiler_params=pltpu.CompilerParams(vmem_limit_bytes=14 * 2**20),
        cost_estimate=pl.CostEstimate(
            flops=8 * rows * hidden_units * columns, bytes_accessed=8 * 2**20, transcendentals=0
        ),
    )(place, *pre, *act, *normed, *low)


def in_grads_kernel(place, near, far, grad_qkv, *refs):
    ends, outs, (total, extra) = refs[:-6], refs[-6:-2], refs[-2:]
    half = near.shape[0]
    columns = grad_qkv.shape[1]
    total[:, :columns] = (
        contract(near[...], grad_qkv[:half], 0, 0) + contract(far[...], grad_qkv[half:], 0, 0)
    ).astype(bf16)
    rows = outs[0].shape[0] // 8
    if ends:
        gain_0, gain_1, table_0, table_1 = ends
        lines = lax.broadcasted_iota(jnp.int32, (tile, gain_0.shape[1]), 0)
        gains = jnp.where(lines == 0, gain_0[...], jnp.where(lines == 1, gain_1[...], 0.0))
        extra[...] = jnp.transpose(gains)
        table = table_0[...] + table_1[...]
        buckets = table.shape[0] // 8
        blank = jnp.zeros((8 - buckets, tile), f32)
        for block in range(8):
            row = pl.multiple_of((place[0] // 2 * 8 + block) * rows, rows)
            extra[pl.ds(row, 8)] += jnp.concatenate(
                [table[block * buckets : (block + 1) * buckets], blank]
            )
        total[:, columns:] = extra[...].astype(bf16)
    for out, offset in zip(outs, (0, 3, 1, 2)):
        plane = (place[8] + offset) % 4
        for index in range(8):
            owner = place[index]
            row = row_of(owner // 2, plane, owner % 2, rows)
            out[index * rows : (index + 1) * rows] = total[pl.ds(row, rows)]


def in_grads(place, near, far, grad_qkv, *ends):
    columns = grad_qkv.shape[1] + (tile if ends else 0)
    shape = (near.shape[1] // 4, columns)
    return pl.pallas_call(
        in_grads_kernel,
        in_specs=[pl.BlockSpec(memory_space=pltpu.SMEM)]
        + [pl.BlockSpec(memory_space=pltpu.VMEM)] * (3 + len(ends)),
        out_specs=[pl.BlockSpec(memory_space=pltpu.VMEM)] * 4,
        out_shape=[jax.ShapeDtypeStruct(shape, bf16)] * 4,
        scratch_shapes=[
            pltpu.VMEM((near.shape[1], columns), bf16),
            pltpu.VMEM((near.shape[1], tile), f32),
        ],
        compiler_params=pltpu.CompilerParams(vmem_limit_bytes=12 * 2**20),
        cost_estimate=pl.CostEstimate(
            flops=4 * near.shape[0] * near.shape[1] * columns,
            bytes_accessed=4 * 2**20,
            transcendentals=0,
        ),
    )(place, near, far, grad_qkv, *ends)


def add_in_kernel(own, lower, upper, opposite, near, far):
    total = sum_of_four([own, lower, upper, opposite]).astype(bf16)
    half = near.shape[0]
    near[...] = total[:half]
    far[...] = total[half:]


def combine_kernel(near_part, arrived, own, x_part, y_part, xy_part):
    rows = own.shape[0]
    own[...] = near_part[:rows] + arrived[:rows].astype(f32)
    for bits, out in ((1, x_part), (2, y_part), (3, xy_part)):
        block = slice(bits * rows, (bits + 1) * rows)
        out[...] = (near_part[block] + arrived[block].astype(f32)).astype(bf16)


def added(own, x_part, y_part, xy_part):
    return (own[...] + x_part[...].astype(f32)) + (
        y_part[...].astype(f32) + xy_part[...].astype(f32)
    )


def close_kernel(kept, own, x_part, y_part, xy_part, hidden, units):
    total = kept[...] + added(own, x_part, y_part, xy_part)
    hidden[...] = total
    units[...] = (total * inverse_rms(total)).astype(bf16)


def close_gain_kernel(kept, own, x_part, y_part, xy_part, gain, hidden, normed):
    total = kept[...] + added(own, x_part, y_part, xy_part)
    hidden[...] = total
    normed[...] = (total * inverse_rms(total) * gain[...]).astype(bf16)


def last_kernel(kept, own, x_part, y_part, xy_part, hidden):
    hidden[...] = (kept[...] + added(own, x_part, y_part, xy_part)).astype(bf16)


def middle_back_kernel(
    upstream, own, x_part, y_part, xy_part, middle, gain, grad_middle, branch, grad_gain
):
    grad_normed = added(own, x_part, y_part, xy_part)
    inverse = inverse_rms(middle[...])
    grad_gain[...] = jnp.sum(grad_normed * middle[...] * inverse, axis=0, keepdims=True)
    total = upstream[...].astype(f32) + unit_norm_back(
        middle[...], inverse, grad_normed * gain[...]
    )
    grad_middle[...] = total
    branch[...] = total.astype(bf16)


def layer_back_kernel(grad_middle, own, x_part, y_part, xy_part, hidden, upstream, low):
    total = grad_middle[...] + unit_norm_back(
        hidden[...], inverse_rms(hidden[...]), added(own, x_part, y_part, xy_part)
    )
    upstream[...] = total
    low[...] = total.astype(bf16)


def pair_kernel(axis, near, arrived, *outs):
    rows = near.shape[0] // len(outs)
    for index, out in enumerate(outs):
        block = slice(index * rows, (index + 1) * rows)
        if axis == 0:
            out[:rows] = near[block]
            out[rows:] = arrived[block]
        else:
            columns = near.shape[1]
            out[:, :columns] = near[block]
            out[:, columns:] = arrived[block]


def unit_kernel(tokens, hidden, units):
    total = tokens[...].astype(f32)
    hidden[...] = total
    units[...] = (total * inverse_rms(total)).astype(bf16)


def finish_in_kernel(layers, place, *refs):
    shares, (attn_in, gains, grad_in, grad_gain, ends) = refs[: 4 * layers], refs[4 * layers :]
    rows = attn_in.shape[1]
    width = shares[-1].shape[1] // 6
    members = attn_in.shape[2] // (3 * width)
    for layer_id in range(layers):
        row_dot = jnp.zeros((rows, 1), f32)
        for index in range(members):
            share = shares[4 * layer_id + index % 4]
            first = index // 4 * (share.shape[1] // 2)
            member = place[index]
            for part in range(3):
                block = share[:, first + part * width : first + (part + 1) * width].astype(f32)
                columns = pl.ds(pl.multiple_of((part * members + member) * width, width), width)
                grad_in[layer_id, :, columns] = block * gains[layer_id]
                row_dot = row_dot + jnp.sum(
                    block * attn_in[layer_id, :, columns].astype(f32), axis=1, keepdims=True
                )
            if layer_id == 0:
                block = share[:, first + 3 * width : first + 4 * width].astype(f32)
                ends[...] = block if index == 0 else ends[...] + block
        grad_gain[layer_id] = jnp.concatenate(
            [row_dot, ends[:, layer_id : layer_id + 1]], axis=1
        )


def sum_of_four(parts):
    return (parts[0][...].astype(f32) + parts[1][...].astype(f32)) + (
        parts[2][...].astype(f32) + parts[3][...].astype(f32)
    )


def finish_ff_kernel(*refs):
    grads = refs[-2:]
    columns = grads[0].shape[2]
    for layer_id in range(grads[0].shape[0]):
        parts = refs[5 * layer_id : 5 * layer_id + 5]
        for side, out in enumerate(grads):
            halves = [part.at[:, side * columns : (side + 1) * columns] for part in parts[:3]]
            out[layer_id] = sum_of_four(halves + [parts[3 + side]])


def finish_out_kernel(*refs):
    for layer_id in range(refs[-1].shape[0]):
        refs[-1][layer_id] = sum_of_four(refs[4 * layer_id : 4 * layer_id + 4])


def inverse_rms(hidden):
    return lax.rsqrt(jnp.mean(hidden * hidden, axis=-1, keepdims=True) + epsilon)


def prepare(bias_table, first_head, heads_dev):
    table = lax.dynamic_slice_in_dim(bias_table, first_head, heads_dev, 1)
    (near,) = call(near_kernel, [((heads_dev, tile, 3 * tile), f32)], table, smem=1)
    return table, near


def bucket_grads(first_lane, grads, bucket_count):
    (total,) = call(bucket_kernel, [((bucket_count, tile), f32)], first_lane, *grads, smem=1)
    return total


def gelu_parts(pre_act):
    cumulative = 0.5 * (1.0 + lax.erf(pre_act * np.float32(0.5**0.5)))
    slope = cumulative + pre_act * jnp.exp(-0.5 * pre_act * pre_act) * np.float32(
        (2 * np.pi) ** -0.5
    )
    return (pre_act * cumulative).astype(bf16), slope


def unit_norm_back(hidden, inverse, grad_unit):
    unit = hidden * inverse
    return inverse * (grad_unit - unit * jnp.mean(grad_unit * unit, axis=-1, keepdims=True))


def gather_rows(block, axes):
    return lax.all_gather(block, axes, axis=0, tiled=True)


def toggle(array, axis, bits):
    return lax.ppermute(array, axis, [(i, i ^ bits) for i in range(lax.axis_size(axis))])


def shift(array, by):
    planes = lax.axis_size("z")
    return lax.ppermute(array, "z", [(i, (i + by) % planes) for i in range(planes)])


def plane_gather(block, *holds):
    near = jnp.concatenate([block] + [toggle(block, "head", bits) for bits in (1, 2, 3)])
    near, *holds = tie(near, *holds)
    return (near, toggle(near, "core", 1), *holds)


def plane_scatter(near_part, far_part):
    rows, columns = near_part.shape[0] // 4, near_part.shape[1]
    own, *others = call(
        combine_kernel,
        [((rows, columns), f32)] + [((rows, columns), bf16)] * 3,
        near_part,
        toggle(far_part, "core", 1),
    )
    shares = [own] + [toggle(other, "head", bits) for bits, other in zip((1, 2, 3), others)]
    return shares, own


def tie(*arrays):
    return lax.optimization_barrier(arrays)


def after(array, other):
    return lax.optimization_barrier((array, other))[0]


def scatter_sum(partial, axes, members):
    blocks = partial.astype(bf16).reshape(members, -1, partial.shape[1])
    return jnp.sum(lax.all_to_all(blocks, axes, 0, 0, tiled=True).astype(f32), axis=0)


def local_general(tokens, doc_start, bias_table, attn_in, attn_out, ff_in, ff_out, gains, cotangent):
    heads_n, z_n, core_n = (lax.axis_size(axis) for axis in everyone)
    devices = heads_n * z_n * core_n
    group, spare = ("z", "core"), "head"
    ff_group, ff_spare, ff_members = ("head", "core"), "z", heads_n * core_n
    blocks = z_n * core_n
    block_rows, model_width = tokens.shape[1:]
    layer_count, weight_rows = attn_in.shape[:2]
    length = block_rows * blocks
    heads_all = bias_table.shape[1]
    member = lax.axis_index("z") * core_n + lax.axis_index("core")
    heads_dev = max(1, heads_all // blocks)
    head_groups = heads_all // heads_dev
    split = blocks // head_groups
    head_group, query_part = member // split, member % split
    query_rows = length // split
    width = heads_dev * head_dim
    first = (query_part * (query_rows // tile)).astype(jnp.int32).reshape(1)
    place = jnp.arange(length // tile, dtype=jnp.int32)
    out_row = head_group * width

    def swap(array):
        return lax.all_to_all(array, everyone, 0, 0, tiled=True)

    starts = jnp.broadcast_to(
        doc_start.astype(f32)[:, None], (heads_n, blocks, block_rows)
    ).reshape(devices, block_rows)
    ff_gains = gains[:, :, 1].astype(f32).reshape(1, -1)
    small = swap(
        jnp.concatenate(
            [starts, jnp.broadcast_to(ff_gains, (devices, layer_count * weight_rows))], axis=1
        )
    )
    doc_row = small[:blocks, :block_rows].reshape(1, length)
    doc_col = lax.dynamic_slice_in_dim(
        doc_row.reshape(length, 1), query_part * query_rows, query_rows, 0
    )
    gain_ff = jnp.transpose(
        small[:, block_rows:].reshape(devices, layer_count, weight_rows), (1, 0, 2)
    ).reshape(layer_count, 1, model_width)
    table, near = prepare(bias_table, head_group * heads_dev, heads_dev)

    gain_attn = gains[:, :, 0].astype(f32)[:, :, None]
    own_in = attn_in.astype(f32)

    def fetch_in(layer_id):
        scaled = (own_in[layer_id] * gain_attn[layer_id]).astype(bf16)
        columns = jnp.transpose(
            scaled.reshape(weight_rows, 3, head_groups, width), (2, 0, 1, 3)
        ).reshape(head_groups, weight_rows, 3 * width)
        columns = jnp.repeat(columns, split, axis=0)
        columns = jnp.broadcast_to(columns[None], (heads_n, *columns.shape))
        return swap(columns.reshape(devices, weight_rows, 3 * width)).reshape(
            model_width, 3 * width
        )

    def fetch_ff(layer_id):
        pair = jnp.concatenate([ff_in[layer_id], ff_out[layer_id]], axis=1)
        pair = gather_rows(pair, ff_spare)
        return pair[:, :model_width], pair[:, model_width:]

    hidden, upstream = tokens[0].astype(f32), cotangent[0]
    weights_in = [fetch_in(layer_id) for layer_id in range(layer_count)]
    weights_out = lax.dynamic_slice_in_dim(
        lax.all_gather(attn_out, everyone, axis=1, tiled=True), out_row, width, 1
    )
    weights_ff = [fetch_ff(layer_id) for layer_id in range(layer_count)]

    records = []
    for layer_id in range(layer_count):
        w_in, w_out, (w_up, w_down) = (
            weights_in[layer_id], weights_out[layer_id], weights_ff[layer_id],
        )
        inverse = inverse_rms(hidden)
        units = gather_rows((hidden * inverse).astype(bf16), group)
        qkv = jnp.dot(units, w_in, preferred_element_type=f32).astype(bf16)
        attended, _, stats = attention(
            qkv, doc_row, doc_col, first, place, table, near, query_rows
        )
        mixed = jnp.dot(attended, w_out, preferred_element_type=f32)
        if split > 1:
            mixed = lax.dynamic_update_slice_in_dim(
                jnp.zeros((length, model_width), f32), mixed, query_part * query_rows, 0
            )
        middle = hidden + scatter_sum(mixed, group, blocks)
        inverse_ff = inverse_rms(middle)
        normed_ff = gather_rows((middle * inverse_ff * gain_ff[layer_id]).astype(bf16), ff_group)
        activated, slope = gelu_parts(contract(normed_ff, w_up, 1, 1))
        ff_result = jnp.dot(activated, w_down, preferred_element_type=f32)
        records.append(
            (hidden, inverse, units, qkv, attended, stats, middle, inverse_ff, normed_ff,
             activated, slope)
        )
        hidden = middle + scatter_sum(ff_result, ff_group, ff_members)
    output = hidden

    grads_ff, grads_in, grads_out, grads_gain_ff, grads_table = (
        [None] * layer_count for _ in range(5)
    )
    for layer_id in reversed(range(layer_count)):
        w_in, w_out, (w_up, w_down) = (
            weights_in[layer_id], weights_out[layer_id], weights_ff[layer_id],
        )
        (hidden, inverse, units, qkv, attended, stats, middle, inverse_ff, normed_ff,
         activated, slope) = records[layer_id]
        grad_low = gather_rows(upstream.astype(bf16), ff_group)
        grad_pre = (contract(grad_low, w_down, 1, 1) * slope).astype(bf16)
        grad_normed = scatter_sum(
            jnp.dot(grad_pre, w_up, preferred_element_type=f32), ff_group, ff_members
        )
        grad_pair = jnp.concatenate(
            [contract(grad_pre, normed_ff, 0, 0), contract(activated, grad_low, 0, 0)], axis=1
        ).astype(bf16)
        grads_ff[layer_id] = lax.psum_scatter(
            grad_pair, ff_spare, scatter_dimension=0, tiled=True
        ).astype(f32)
        grads_gain_ff[layer_id] = jnp.sum(grad_normed * middle * inverse_ff, axis=0)
        grad_middle = upstream + unit_norm_back(
            middle, inverse_ff, grad_normed * gain_ff[layer_id]
        )
        branch = gather_rows(grad_middle.astype(bf16), group)
        if split > 1:
            branch = lax.dynamic_slice_in_dim(branch, query_part * query_rows, query_rows, 0)
        grad_attended = contract(branch, w_out, 1, 1).astype(bf16)
        grad_qkv, grad_near, grad_far = attention_back(
            qkv, doc_row, doc_col, attended, grad_attended, stats, first, place, table, near, split
        )
        grads_table[layer_id] = (grad_near, grad_far)
        grad_units = scatter_sum(contract(grad_qkv, w_in, 1, 1), group, blocks)
        upstream = grad_middle + unit_norm_back(hidden, inverse, grad_units)
        grad_out = lax.dynamic_update_slice_in_dim(
            jnp.zeros((model_width, model_width), bf16),
            contract(attended, branch, 0, 0).astype(bf16),
            out_row,
            0,
        )
        grads_out[layer_id] = lax.psum_scatter(
            grad_out, everyone, scatter_dimension=0, tiled=True
        ).astype(f32)
        grads_in[layer_id] = contract(units, grad_qkv, 0, 0).astype(bf16)

    bucket_count = table.shape[0]
    grad_table = sum(
        bucket_grads(jnp.zeros((1,), jnp.int32), entry, bucket_count) for entry in grads_table
    )[:, :heads_dev]
    grad_table = lax.dynamic_update_slice_in_dim(
        jnp.zeros((bucket_count, heads_all), f32), grad_table, head_group * heads_dev, 1
    )
    grad_table = jnp.transpose(
        grad_table.reshape(blocks, bucket_count // blocks, heads_n, heads_all // heads_n),
        (2, 0, 1, 3),
    ).reshape(devices, -1)
    grad_gain_ff = jnp.transpose(
        jnp.stack(grads_gain_ff).reshape(layer_count, devices, weight_rows), (1, 0, 2)
    ).reshape(devices, -1)
    ends = jnp.sum(swap(jnp.concatenate([grad_gain_ff, grad_table], axis=1)), axis=0)
    grad_gain_ff = ends[: layer_count * weight_rows].reshape(layer_count, weight_rows)
    grad_bias_table = ends[layer_count * weight_rows :].reshape(
        bucket_count // blocks, heads_all // heads_n
    )
    grads_attn_in, grads_gains = [], []
    for layer_id in range(layer_count):
        parts = swap(grads_in[layer_id].reshape(devices, weight_rows, 3 * width)).astype(f32)
        parts = jnp.sum(parts.reshape(heads_n, blocks, weight_rows, 3 * width), axis=0)
        parts = jnp.sum(parts.reshape(head_groups, split, weight_rows, 3, width), axis=1)
        unit_grad = jnp.transpose(parts, (1, 2, 0, 3)).reshape(weight_rows, 3 * model_width)
        grads_attn_in.append(unit_grad * gain_attn[layer_id])
        grads_gains.append(
            jnp.stack(
                [jnp.sum(unit_grad * own_in[layer_id], axis=1), grad_gain_ff[layer_id]], axis=1
            )
        )
    return (
        output[None],
        upstream[None],
        jnp.stack(grads_attn_in),
        jnp.stack(grads_out),
        jnp.stack([entry[:, :model_width] for entry in grads_ff]),
        jnp.stack([entry[:, model_width:] for entry in grads_ff]),
        jnp.stack(grads_gains),
        grad_bias_table,
    )


def local_plane(tokens, doc_start, bias_table, attn_in, attn_out, ff_in, ff_out, gains, cotangent):
    heads_n, z_n, core_n = (lax.axis_size(axis) for axis in everyone)
    devices = heads_n * z_n * core_n
    at_head, at_z, at_core = (lax.axis_index(axis) for axis in everyone)
    members = heads_n * core_n
    block_rows, model_width = tokens.shape[1:]
    layer_count, weight_rows = attn_in.shape[:2]
    length = block_rows * members
    heads_all = bias_table.shape[1]
    heads_dev = heads_all // members
    width = heads_dev * head_dim
    member = at_head * core_n + at_core
    turn = [
        ((h * z_n + z) * core_n + c, ((h ^ z) * z_n + h) * core_n + c)
        for h in range(heads_n)
        for z in range(z_n)
        for c in range(core_n)
    ]
    turn_back = [(target, source) for source, target in turn]
    place = jnp.stack(
        [
            (at_head ^ bits) * core_n + (at_core ^ other)
            for other in range(core_n)
            for bits in range(heads_n)
        ]
        + [at_z]
        + [
            (at_head ^ bits ^ at_z) * core_n + (at_core ^ other)
            for other in range(core_n)
            for bits in range(heads_n)
        ]
    ).astype(jnp.int32)

    def relay(array):
        return lax.ppermute(array, everyone, turn)

    def relay_back(array):
        return lax.ppermute(array, everyone, turn_back)

    def swap(array):
        return lax.all_to_all(array, everyone, 0, 0, tiled=True)

    row_shape = (block_rows, model_width)
    gain_attn = gains[:, :, 0].astype(f32)[:, :, None]
    near_share, far_share = call(
        share_in_kernel,
        [((members // 2 * layer_count * weight_rows, 3 * width), bf16)] * 2,
        place,
        attn_in,
        gain_attn,
        smem=1,
    )

    quarter_turns = [
        [
            (z * core_n + c, (2 * c + (a ^ z % 2)) * core_n + (b ^ z // 2))
            for z in range(z_n)
            for c in range(core_n)
        ]
        for a in range(2)
        for b in range(2)
    ]

    def fetch_out(layer_id, hold):
        held = after(attn_out[layer_id], hold)
        return [
            lax.ppermute(held, ("z", "core"), [(holder, user) for user, holder in turns])
            for turns in quarter_turns
        ]

    starts = jnp.broadcast_to(
        doc_start.astype(f32)[None, :, None], (heads_n, z_n, core_n, block_rows)
    )
    ff_gains = gains[:, :, 1].astype(f32).reshape(1, -1)
    small = jnp.concatenate(
        [
            starts.reshape(devices, block_rows),
            jnp.broadcast_to(ff_gains, (devices, layer_count * weight_rows)),
        ],
        axis=1,
    )
    table, strip = prepare(bias_table, member * heads_dev, heads_dev)
    hidden, strip = tie(relay(tokens[0]), strip)
    small = swap(after(small, hidden))
    doc_row = small[:members, :block_rows].reshape(2, 2, core_n, block_rows)
    at_block = at_head ^ at_z
    for axis, bit in ((0, at_block // 2), (1, at_block % 2), (2, at_core)):
        doc_row = jnp.where(bit == 1, jnp.flip(doc_row, axis), doc_row)
    doc_row = jnp.transpose(doc_row, (2, 0, 1, 3)).reshape(1, length)
    doc_col = doc_row.reshape(length, 1)
    gain_ff = jnp.transpose(
        small[:, block_rows:].reshape(devices, layer_count, weight_rows), (1, 0, 2)
    ).reshape(layer_count, 1, model_width)

    def round_planes(array, by, hold):
        return shift(after(array, hold), by)

    def fetch_ff(layer_id, hold):
        pair = jnp.concatenate([ff_in[layer_id], ff_out[layer_id]], axis=1)
        return gather_rows(after(pair, hold), "z")

    def ff_both(kernel, row_operands, pair, columns):
        return zip(
            *(
                by_rows(
                    kernel,
                    256,
                    operands,
                    [pair],
                    [(pair.shape[0], bf16)] * columns + [(model_width, kind)],
                )
                for operands, kind in zip(zip(*row_operands), (f32, bf16))
            )
        )

    def ff_forward(normed, pair):
        return ff_both(ff_kernel, [normed], pair, 2)

    def ff_backward(low, slopes, pair):
        return ff_both(ff_back_kernel, [low, slopes], pair, 1)

    def pair_chips(near, arrived, axis):
        rows, columns = near.shape[0] // 4, near.shape[1]
        shape = (2 * rows, columns) if axis == 0 else (rows, 2 * columns)
        return call(functools.partial(pair_kernel, axis), [(shape, bf16)] * 4, near, arrived)

    def share_chips(blocks):
        return [blocks[0]] + [toggle(blocks[bits], "head", bits) for bits in (1, 2, 3)]

    units_shape = [(row_shape, f32), (row_shape, bf16)]
    def assemble_in(share, lower, upper, opposite):
        return call(
            assemble_in_kernel,
            [((model_width, 3 * width), bf16)],
            place,
            share,
            lower,
            upper,
            opposite,
            smem=1,
        )[0]

    hidden, shares, quarters = tie(
        hidden,
        share_chips(pair_chips(near_share, toggle(far_share, "core", 1), 0)),
        fetch_out(0, near_share),
    )
    hidden, unit_rows = call(unit_kernel, units_shape, hidden)
    pairs = [fetch_ff(0, hidden)]
    share, later_share = call(
        join_kernel, [((members * weight_rows, 3 * width), bf16)] * layer_count, *shares
    )
    near, far, lower, upper, opposite, doc_row, doc_col, gain_ff = plane_gather(
        unit_rows,
        shift(share, 1),
        shift(share, -1),
        shift(share, 2),
        doc_row,
        doc_col,
        gain_ff,
    )
    units = (near, far)
    w_in = assemble_in(share, lower, upper, opposite)
    w_out, qkv, attended, stats, *parts = plane_attention(
        *units, w_in, quarters, doc_row, doc_col, place, table, strip
    )
    parts, upstream = tie(parts, relay(after(cotangent[0].astype(bf16), near)))
    parts, _ = plane_scatter(*parts)
    middle, normed_rows = call(close_gain_kernel, units_shape, hidden, *parts, gain_ff[0])
    pairs.append(fetch_ff(1, normed_rows))
    normed = plane_gather(normed_rows)
    acts, slopes, parts = ff_forward(normed, pairs[0])
    records = [
        (hidden, units, w_in, w_out, pairs[0], qkv, attended, stats, middle, normed, acts, slopes)
    ]
    parts, own = plane_scatter(*parts)
    parts, lower, upper = tie(
        parts, round_planes(later_share, 1, own), round_planes(later_share, -1, own)
    )
    hidden, unit_rows = call(close_kernel, units_shape, middle, *parts)

    near, far, opposite, quarters = plane_gather(
        unit_rows, round_planes(later_share, 2, unit_rows), fetch_out(1, unit_rows)
    )
    units = (near, far)
    w_in = assemble_in(later_share, lower, upper, opposite)
    w_out, qkv, attended, stats, *parts = plane_attention(
        *units, w_in, quarters, doc_row, doc_col, place, table, strip
    )
    low = plane_gather(after(upstream, far))
    parts, near_low = tie(parts, low[0])
    low = (near_low, low[1])
    parts, _ = plane_scatter(*parts)
    middle, normed_rows = call(close_gain_kernel, units_shape, hidden, *parts, gain_ff[1])
    normed = plane_gather(normed_rows)
    acts, slopes, last_parts = ff_forward(normed, pairs[1])
    records.append(
        (hidden, units, w_in, w_out, pairs[1], qkv, attended, stats, middle, normed, acts, slopes)
    )

    def back_to_middle(parts, upstream, middle, gain):
        return call(
            middle_back_kernel, units_shape + [((1, model_width), f32)], upstream, *parts, middle, gain
        )

    def attention_grads(record, branch):
        _, _, w_in, w_out, _, qkv, attended, stats, *_ = record
        grad_qkv, grad_near, grad_far, near_part, far_part, *quarters = plane_attention_back(
            qkv, doc_row, doc_col, attended, stats, *branch, w_in, w_out, place, table, strip
        )
        return grad_qkv, (grad_near, grad_far), (near_part, far_part), quarters

    def owners_quarters(quarters):
        return [
            lax.ppermute(quarter, ("z", "core"), turns)
            for quarter, turns in zip(quarters, quarter_turns)
        ]

    def table_grads(near_and_far):
        return bucket_grads(at_core.reshape(1) * heads_dev + 8, near_and_far, table.shape[0])

    def add_in(own, lower, upper, opposite):
        shape = (own.shape[0] // 2, own.shape[1])
        return call(add_in_kernel, [(shape, bf16)] * 2, own, lower, upper, opposite)

    record = records[1]
    hidden, units, _, _, pair, *_, middle, normed, acts, slopes = record
    pres, parts = ff_backward(low, slopes, pair)
    parts, own = plane_scatter(*parts)
    planes = ff_grads(place, after(pres, own), acts, normed, low)
    parts, ff_lower = tie(parts, shift(planes[1], -1))
    last_parts, _ = plane_scatter(*after(last_parts, parts))
    grad_middle, branch_rows, gain_1 = back_to_middle(parts, upstream, middle, gain_ff[1])
    *branch, ff_upper = plane_gather(branch_rows, round_planes(planes[2], 1, branch_rows))
    grad_qkv, strips_1, parts, quarters_1 = attention_grads(record, branch)
    parts, last_parts, opposite_up = tie(
        parts, last_parts, round_planes(planes[3], 2, branch[1])
    )
    parts, own = plane_scatter(*parts)
    grad_in = in_grads(place, *units, after(grad_qkv, own))
    parts, opposite_down, in_opposite, output, table_1 = tie(
        parts,
        round_planes(planes[4], 2, own),
        shift(grad_in[3], 2),
        call(last_kernel, [(row_shape, bf16)], middle, *after(last_parts, own))[0],
        table_grads(after(strips_1, own)),
    )
    grads_ff = [planes[0], ff_lower, ff_upper, opposite_up, opposite_down]
    upstream, low_rows = call(layer_back_kernel, units_shape, grad_middle, *parts, hidden)

    record = records[0]
    hidden, units, _, _, pair, *_, middle, normed, acts, slopes = record
    *low, in_lower, in_upper = plane_gather(
        low_rows,
        round_planes(grad_in[1], -1, low_rows),
        round_planes(grad_in[2], 1, low_rows),
    )
    pres, parts = ff_backward(low, slopes, pair)
    parts, own = plane_scatter(*parts)
    near_in, far_in = add_in(*after([grad_in[0], in_lower, in_upper, in_opposite], own))
    planes = ff_grads(place, after(pres, own), acts, normed, low)
    parts, ff_lower, far_in = tie(parts, shift(planes[1], -1), toggle(far_in, "core", 1))
    grad_middle, branch_rows, gain_0 = back_to_middle(parts, upstream, middle, gain_ff[0])
    *branch, ff_upper, shares_1 = plane_gather(
        branch_rows,
        round_planes(planes[2], 1, branch_rows),
        pair_chips(near_in, after(far_in, branch_rows), 1),
    )
    grad_qkv, strips_0, parts, quarters_0 = attention_grads(record, branch)
    parts, output, quarters_1, shares_1 = tie(
        parts,
        relay_back(after(output, branch[1])),
        owners_quarters(after(quarters_1, branch[1])),
        share_chips(after(shares_1, branch[1])),
    )
    parts, own = plane_scatter(*parts)
    table_0 = table_grads(after(strips_0, own))
    grad_in = in_grads(
        place, *units, after(grad_qkv, own), gain_0, gain_1, table_0, table_1
    )
    parts, opposite_up, in_opposite, output = tie(
        parts,
        round_planes(planes[3], 2, own),
        shift(grad_in[3], 2),
        after(output, own).astype(f32),
    )
    upstream, low_rows = call(layer_back_kernel, units_shape, grad_middle, *parts, hidden)
    grad_tokens = relay_back(low_rows)
    in_lower = round_planes(grad_in[1], -1, low_rows)
    in_upper = round_planes(grad_in[2], 1, low_rows)
    opposite_down = round_planes(planes[4], 2, low_rows)
    grads_ff = [planes[0], ff_lower, ff_upper, opposite_up, opposite_down] + grads_ff
    grad_up, grad_down = call(finish_ff_kernel, [(ff_in.shape, f32)] * 2, *after(grads_ff, low_rows))
    quarters_0 = owners_quarters(after(quarters_0, low_rows))
    near_in, far_in = add_in(grad_in[0], in_lower, in_upper, in_opposite)
    shares_0 = share_chips(pair_chips(near_in, toggle(far_in, "core", 1), 1))
    (grad_attn_out,) = call(finish_out_kernel, [(attn_out.shape, f32)], *quarters_0, *quarters_1)
    own_buckets = table.shape[0] // (z_n * core_n)
    grad_attn_in, grad_gains, ends = call(
        functools.partial(finish_in_kernel, layer_count),
        [(attn_in.shape, f32), (gains.shape, f32), ((weight_rows, tile), f32)],
        place,
        *shares_0,
        *shares_1,
        attn_in,
        gain_attn,
        smem=1,
    )
    return (
        output[None],
        grad_tokens.astype(f32)[None],
        grad_attn_in,
        grad_attn_out,
        grad_up,
        grad_down,
        grad_gains,
        ends[:own_buckets, 8 : 8 + heads_all // heads_n],
    )


def solution(mesh):
    sizes = dict(mesh.shape)
    cores = 2
    fine = Mesh(
        mesh.devices.reshape(sizes["head"], sizes["blk"] // cores, cores), everyone
    )
    blk = ("z", "core")
    in_specs = (
        P("head", blk, None),
        P(None, blk),
        P(),
        P(None, everyone, None),
        P(None, everyone, None),
        P(None, everyone, None),
        P(None, everyone, None),
        P(None, everyone, None),
        P("head", blk, None),
    )
    out_specs = (
        P("head", blk, None),
        P("head", blk, None),
        P(None, everyone, None),
        P(None, everyone, None),
        P(None, everyone, None),
        P(None, everyone, None),
        P(None, everyone, None),
        P(blk, "head"),
    )
    plane = sizes["head"] == 4 and sizes["blk"] == 8
    local = local_plane if plane else local_general
    return jax.shard_map(local, mesh=fine, in_specs=in_specs, out_specs=out_specs, check_vma=False)
```

```python
import functools

import jax
import jax.numpy as jnp
import numpy as np
from jax import lax
from jax.experimental import pallas as pl
from jax.experimental.pallas import tpu as pltpu
from jax.sharding import Mesh
from jax.sharding import PartitionSpec as P

bounds = (1, 2, 3, 4, 5, 6, 7, 8, 12, 16, 23, 32, 46, 64, 91)
epsilon = 1e-06
masked = -1e30
score_scale = 0.125
head_dim = 64
tile = 128
everyone = ("head", "z", "core")
bf16 = jnp.bfloat16
f32 = jnp.float32


def contract(lhs, rhs, lhs_dim, rhs_dim):
    return lax.dot_general(
        lhs, rhs, (((lhs_dim,), (rhs_dim,)), ((), ())), preferred_element_type=f32
    )


def near_buckets(shape):
    offsets = (
        lax.broadcasted_iota(jnp.int32, shape, 1) - tile - lax.broadcasted_iota(jnp.int32, shape, 0)
    )
    distance = jnp.abs(offsets)
    bucket = jnp.where(offsets > 0, 16, 0)
    for boundary in bounds:
        bucket = bucket + jnp.where(distance >= boundary, 1, 0)
    return bucket


def near_kernel(table, near):
    bucket = near_buckets(near.shape[1:])
    for head in range(near.shape[0]):
        values = jnp.zeros(near.shape[1:], f32)
        for bucket_id in range(table.shape[0]):
            values = jnp.where(bucket == bucket_id, table[bucket_id, head], values)
        near[head] = values


def bucket_kernel(first_lane, near, far, out):
    bucket = near_buckets(near.shape[1:])
    rows = lax.broadcasted_iota(jnp.int32, out.shape, 0)
    lanes = lax.broadcasted_iota(jnp.int32, out.shape, 1)
    total = jnp.zeros(out.shape, f32)
    for head in range(near.shape[0]):
        strip = near[head]
        for bucket_id in range(out.shape[0]):
            value = jnp.sum(jnp.where(bucket == bucket_id, strip, 0.0), axis=0, keepdims=True)
            value = jnp.sum(value, axis=1, keepdims=True)
            if bucket_id in (15, 31):
                value = value + far[head, bucket_id // 16, :1, :1]
            total = jnp.where((rows == bucket_id) & (lanes == head + first_lane[0]), value, total)
    out[...] = total


def fill_band(band, table, near, heads_dev, length):
    for head in range(heads_dev):
        band[head, :, : length - tile] = jnp.full((tile, length - tile), table[15, head], f32)
        band[head, :, length - tile : length + 2 * tile] = near[head]
        band[head, :, length + 2 * tile :] = jnp.full(
            (tile, length - 2 * tile), table[31, head], f32
        )


def band_starts(place, at, length, skip=0):
    return [
        pl.multiple_of(length + (place[skip + block] - place[skip + at]) * tile, tile)
        for block in range(length // tile)
    ]


def attention_kernel(
    heads_dev, length, first, place, table, near, qkv, doc_row, doc_col, out, local, stats, band
):
    step = pl.program_id(0)
    width = heads_dev * head_dim

    @pl.when(step == 0)
    def _():
        fill_band(band, table, near, heads_dev, length)

    row = pl.multiple_of((first[0] + step) * tile, tile)
    out_row = pl.multiple_of((place[first[0] + step] - first[0]) * tile, tile)
    starts = band_starts(place, first[0] + step, length)
    same_doc = doc_col[...] == doc_row[...]
    queries = qkv[pl.ds(row, tile), :width] * bf16(score_scale)
    lanes = lax.broadcasted_iota(jnp.int32, (tile, tile), 1)
    collected = jnp.zeros((tile, tile), f32)
    for head in range(heads_dev):
        own = slice(head * head_dim, (head + 1) * head_dim)
        keys = qkv[:, width + own.start : width + own.stop]
        values = qkv[:, 2 * width + own.start : 2 * width + own.stop]
        scores = contract(queries[:, own], keys, 1, 1)
        scores = scores + jnp.concatenate(
            [band[head, :, pl.ds(start, tile)] for start in starts], axis=1
        )
        scores = jnp.where(same_doc, scores, masked)
        peak = jnp.max(scores, axis=1, keepdims=True)
        weights = jnp.exp(scores - peak)
        total = jnp.sum(weights, axis=1, keepdims=True)
        mixed = contract(weights.astype(bf16), values, 1, 0) / total
        out[pl.ds(out_row, tile), own] = mixed.astype(bf16)
        local[:, own] = mixed.astype(bf16)
        collected = jnp.where(lanes == head, peak + jnp.log(total), collected)
    stats[...] = collected


def attention_back_kernel(
    heads_dev, length, split, first, place, table, near, qkv, doc_row, doc_col, attended, grad_out, stats,
    grad_qkv, grad_near, grad_far, band, grad_band, grad_keys, grad_values,
):
    step = pl.program_id(0)
    width = heads_dev * head_dim

    @pl.when(step == 0)
    def _():
        fill_band(band, table, near, heads_dev, length)
        grad_band[...] = jnp.zeros_like(grad_band)
        grad_keys[...] = jnp.zeros_like(grad_keys)
        grad_values[...] = jnp.zeros_like(grad_values)
        if split > 1:
            grad_qkv[...] = jnp.zeros_like(grad_qkv)

    row = pl.multiple_of((first[0] + step) * tile, tile)
    out_row = pl.multiple_of((place[first[0] + step] - first[0]) * tile, tile)
    starts = band_starts(place, first[0] + step, length)
    same_doc = doc_col[...] == doc_row[...]
    at_step = pl.multiple_of(step * tile, tile)
    queries = qkv[pl.ds(row, tile), :width] * bf16(score_scale)
    for head in range(heads_dev):
        own = slice(head * head_dim, (head + 1) * head_dim)
        keys = qkv[:, width + own.start : width + own.stop]
        values = qkv[:, 2 * width + own.start : 2 * width + own.stop]
        upstream = grad_out[pl.ds(out_row, tile), own]
        scores = contract(queries[:, own], keys, 1, 1) + jnp.concatenate(
            [band[head, :, pl.ds(start, tile)] for start in starts], axis=1
        )
        scores = jnp.where(same_doc, scores, masked)
        weights = jnp.exp(scores - stats[:, head : head + 1])
        delta = jnp.sum(
            upstream.astype(f32) * attended[pl.ds(at_step, tile), own].astype(f32),
            axis=1,
            keepdims=True,
        )
        grad_scores = weights * (contract(upstream, values, 1, 1) - delta)
        for block, start in enumerate(starts):
            grad_band[head, :, pl.ds(start, tile)] += grad_scores[
                :, block * tile : (block + 1) * tile
            ]
        grad_low = grad_scores.astype(bf16)
        grad_values[:, own] += contract(weights.astype(bf16), upstream, 0, 0)
        grad_keys[:, own] += contract(grad_low, queries[:, own], 0, 0)
        grad_qkv[pl.ds(row, tile), own] = (
            contract(grad_low, keys, 1, 0) * score_scale
        ).astype(bf16)

    @pl.when(step == pl.num_programs(0) - 1)
    def _():
        grad_qkv[:, width : 2 * width] = grad_keys[...].astype(bf16)
        grad_qkv[:, 2 * width :] = grad_values[...].astype(bf16)
        for head in range(heads_dev):
            grad_near[head] = grad_band[head, :, length - tile : length + 2 * tile]
            grad_far[head, 0] = jnp.full(
                (8, tile), jnp.sum(grad_band[head, :, : length - tile]), f32
            )
            grad_far[head, 1] = jnp.full(
                (8, tile), jnp.sum(grad_band[head, :, length + 2 * tile :]), f32
            )


def whole(shape):
    return pl.BlockSpec(shape, lambda step: (0,) * len(shape), pipeline_mode=pl.Buffered(1))


def attention(qkv, doc_row, doc_col, first, place, table, near, rows):
    length = qkv.shape[0]
    heads_dev = table.shape[1]
    width = heads_dev * head_dim
    return pl.pallas_call(
        functools.partial(attention_kernel, heads_dev, length),
        grid=(rows // tile,),
        in_specs=[
            pl.BlockSpec(memory_space=pltpu.SMEM),
            pl.BlockSpec(memory_space=pltpu.SMEM),
            pl.BlockSpec(memory_space=pltpu.SMEM),
            whole(near.shape),
            whole(qkv.shape),
            whole(doc_row.shape),
            pl.BlockSpec((tile, 1), lambda step: (step, 0)),
        ],
        out_specs=[
            whole((rows, width)),
            pl.BlockSpec((tile, width), lambda step: (step, 0)),
            pl.BlockSpec((tile, tile), lambda step: (step, 0)),
        ],
        out_shape=[
            jax.ShapeDtypeStruct((rows, width), bf16),
            jax.ShapeDtypeStruct((rows, width), bf16),
            jax.ShapeDtypeStruct((rows, tile), f32),
        ],
        scratch_shapes=[pltpu.VMEM((heads_dev, tile, 2 * length), f32)],
        compiler_params=pltpu.CompilerParams(vmem_limit_bytes=40 * 2**20),
        cost_estimate=pl.CostEstimate(
            flops=4 * rows * length * width,
            bytes_accessed=4 * length * width * 2,
            transcendentals=rows * length * heads_dev,
        ),
    )(first, place, table, near, qkv, doc_row, doc_col)


def attention_back(
    qkv, doc_row, doc_col, attended, grad_out, stats, first, place, table, near, split
):
    length = qkv.shape[0]
    rows = grad_out.shape[0]
    heads_dev = table.shape[1]
    width = heads_dev * head_dim
    return pl.pallas_call(
        functools.partial(attention_back_kernel, heads_dev, length, split),
        grid=(rows // tile,),
        in_specs=[
            pl.BlockSpec(memory_space=pltpu.SMEM),
            pl.BlockSpec(memory_space=pltpu.SMEM),
            pl.BlockSpec(memory_space=pltpu.SMEM),
            whole(near.shape),
            whole(qkv.shape),
            whole(doc_row.shape),
            pl.BlockSpec((tile, 1), lambda step: (step, 0)),
            whole((rows, width)),
            whole((rows, width)),
            pl.BlockSpec((tile, tile), lambda step: (step, 0)),
        ],
        out_specs=[
            whole((length, 3 * width)),
            whole((heads_dev, tile, 3 * tile)),
            whole((heads_dev, 2, 8, tile)),
        ],
        out_shape=[
            jax.ShapeDtypeStruct((length, 3 * width), bf16),
            jax.ShapeDtypeStruct((heads_dev, tile, 3 * tile), f32),
            jax.ShapeDtypeStruct((heads_dev, 2, 8, tile), f32),
        ],
        scratch_shapes=[
            pltpu.VMEM((heads_dev, tile, 2 * length), f32),
            pltpu.VMEM((heads_dev, tile, 2 * length), f32),
            pltpu.VMEM((length, width), f32),
            pltpu.VMEM((length, width), f32),
        ],
        compiler_params=pltpu.CompilerParams(vmem_limit_bytes=48 * 2**20),
        cost_estimate=pl.CostEstimate(
            flops=10 * rows * length * width,
            bytes_accessed=8 * length * width * 2,
            transcendentals=rows * length * heads_dev,
        ),
    )(first, place, table, near, qkv, doc_row, doc_col, attended, grad_out, stats)


def call(kernel, shapes, *operands, smem=0):
    return pl.pallas_call(
        kernel,
        in_specs=[pl.BlockSpec(memory_space=pltpu.SMEM)] * smem
        + [pl.BlockSpec(memory_space=pltpu.VMEM)] * (len(operands) - smem),
        out_specs=[pl.BlockSpec(memory_space=pltpu.VMEM)] * len(shapes),
        out_shape=[jax.ShapeDtypeStruct(shape, kind) for shape, kind in shapes],
        compiler_params=pltpu.CompilerParams(vmem_limit_bytes=10 * 2**20),
    )(*operands)


def share_in_kernel(place, attn_in, gains, near, far):
    layers, rows = attn_in.shape[:2]
    half = near.shape[0] // (layers * rows)
    width = near.shape[1] // 3
    for index in range(2 * half):
        member = place[index]
        for layer_id in range(layers):
            block = jnp.concatenate(
                [
                    attn_in[
                        layer_id,
                        :,
                        pl.ds(pl.multiple_of((part * 2 * half + member) * width, width), width),
                    ]
                    for part in range(3)
                ],
                axis=1,
            )
            at = (index % half * layers + layer_id) * rows
            out = near if index < half else far
            out[at : at + rows] = (block.astype(f32) * gains[layer_id]).astype(bf16)


def join_kernel(*refs):
    shares, outs = refs[:4], refs[4:]
    rows = outs[0].shape[0] // 8
    for chip, share in enumerate(shares):
        for core in range(2):
            for layer_id, out in enumerate(outs):
                source = (core * len(outs) + layer_id) * rows
                target = (chip * 2 + core) * rows
                out[target : target + rows] = share[source : source + rows]


def row_of(chip, plane, core, rows, planes=4):
    return pl.multiple_of(((chip * planes + plane) * 2 + core) * rows, rows)


def assemble_in_kernel(place, own, lower, upper, opposite, out):
    at_z, at_core, at_head = place[8], place[0] % 2, place[0] // 2
    rows = own.shape[0] // 8
    for part, offset in ((own, 0), (lower, 3), (upper, 1), (opposite, 2)):
        plane = (at_z + offset) % 4
        for index in range(8):
            row = row_of(at_head ^ (index // 2), plane, at_core ^ (index % 2), rows)
            out[pl.ds(row, rows)] = part[index * rows : (index + 1) * rows]


def plane_attention_kernel(
    length, place, table, strip, near, far, w_in, *refs
):
    halves, (doc_row, doc_col, w_out, qkv, attended, stats, near_part, far_part, band) = (
        refs[:2], refs[2:],
    )
    step = pl.program_id(0)
    half = length // 2
    heads_dev = table.shape[1]
    width = heads_dev * head_dim

    @pl.when(step == 0)
    def _():
        fill_band(band, table, strip, heads_dev, length)
        swapped = place[length // tile] % 2 == 1
        rows = width // 2
        w_out[:rows] = jnp.where(swapped, halves[1][...], halves[0][...])
        w_out[rows:] = jnp.where(swapped, halves[0][...], halves[1][...])
        qkv[:half] = contract(near[...], w_in[...], 1, 0).astype(bf16)
        qkv[half:] = contract(far[...], w_in[...], 1, 0).astype(bf16)

    row = pl.multiple_of(step * tile, tile)
    starts = band_starts(place, step, length, length // tile + 1)
    same_doc = doc_col[...] == doc_row[...]
    queries = qkv[pl.ds(row, tile), :width] * bf16(score_scale)
    lanes = lax.broadcasted_iota(jnp.int32, (tile, tile), 1)
    collected = jnp.zeros((tile, tile), f32)
    results = []
    for head in range(heads_dev):
        own = slice(head * head_dim, (head + 1) * head_dim)
        keys = qkv[:, width + own.start : width + own.stop]
        values = qkv[:, 2 * width + own.start : 2 * width + own.stop]
        scores = contract(queries[:, own], keys, 1, 1) + jnp.concatenate(
            [band[head, :, pl.ds(start, tile)] for start in starts], axis=1
        )
        scores = jnp.where(same_doc, scores, masked)
        peak = jnp.max(scores, axis=1, keepdims=True)
        weights = jnp.exp(scores - peak)
        total = jnp.sum(weights, axis=1, keepdims=True)
        results.append((contract(weights.astype(bf16), values, 1, 0) / total).astype(bf16))
        collected = jnp.where(lanes == head, peak + jnp.log(total), collected)
    stats[...] = collected
    merged = jnp.concatenate(results, axis=1)
    attended[...] = merged
    part = contract(merged, w_out[...], 1, 0)

    @pl.when(row < half)
    def _():
        near_part[...] = part

    @pl.when(row >= half)
    def _():
        far_part[...] = part.astype(bf16)


def near_block(steps, columns):
    return pl.BlockSpec((tile, columns), lambda step: (jnp.minimum(step, steps // 2 - 1), 0))


def far_block(steps, columns):
    return pl.BlockSpec((tile, columns), lambda step: (jnp.maximum(step - steps // 2, 0), 0))


def plane_attention(near, far, w_in, halves, doc_row, doc_col, place, table, strip):
    length, model_width = 2 * near.shape[0], near.shape[1]
    steps = length // tile
    heads_dev = table.shape[1]
    width = heads_dev * head_dim
    return pl.pallas_call(
        functools.partial(plane_attention_kernel, length),
        grid=(steps,),
        in_specs=[
            pl.BlockSpec(memory_space=pltpu.SMEM),
            pl.BlockSpec(memory_space=pltpu.SMEM),
            whole(strip.shape),
            whole(near.shape),
            whole(far.shape),
            whole(w_in.shape),
            *[whole(half.shape) for half in halves],
            whole(doc_row.shape),
            pl.BlockSpec((tile, 1), lambda step: (step, 0)),
        ],
        out_specs=[
            whole((width, model_width)),
            whole((length, 3 * width)),
            pl.BlockSpec((tile, width), lambda step: (step, 0)),
            pl.BlockSpec((tile, tile), lambda step: (step, 0)),
            near_block(steps, model_width),
            far_block(steps, model_width),
        ],
        out_shape=[
            jax.ShapeDtypeStruct((width, model_width), bf16),
            jax.ShapeDtypeStruct((length, 3 * width), bf16),
            jax.ShapeDtypeStruct((length, width), bf16),
            jax.ShapeDtypeStruct((length, tile), f32),
            jax.ShapeDtypeStruct((length // 2, model_width), f32),
            jax.ShapeDtypeStruct((length // 2, model_width), bf16),
        ],
        scratch_shapes=[pltpu.VMEM((heads_dev, tile, 2 * length), f32)],
        compiler_params=pltpu.CompilerParams(vmem_limit_bytes=14 * 2**20),
        cost_estimate=pl.CostEstimate(
            flops=4 * length * length * width + 8 * length * model_width * width,
            bytes_accessed=12 * 2**20,
            transcendentals=length * length * heads_dev,
        ),
    )(place, table, strip, near, far, w_in, *halves, doc_row, doc_col)


def plane_attention_back_kernel(
    length, place, table, strip, qkv, doc_row, doc_col, attended, stats, near, far, w_in, w_out,
    grad_qkv, grad_near, grad_far, near_part, far_part, *rest
):
    halves, (band, grad_band, grad_keys, grad_values, out_sum) = rest[:2], rest[2:]
    step = pl.program_id(0)
    half = length // 2
    heads_dev = table.shape[1]
    width = heads_dev * head_dim

    @pl.when(step == 0)
    def _():
        fill_band(band, table, strip, heads_dev, length)
        grad_band[...] = jnp.zeros_like(grad_band)
        grad_keys[...] = jnp.zeros_like(grad_keys)
        grad_values[...] = jnp.zeros_like(grad_values)
        out_sum[...] = jnp.zeros_like(out_sum)

    row = pl.multiple_of(step * tile, tile)
    starts = band_starts(place, step, length, length // tile + 1)
    same_doc = doc_col[...] == doc_row[...]
    branch = jnp.where(row < half, near[...], far[...])
    merged = attended[...]
    grad_merged = contract(branch, w_out[...], 1, 1).astype(bf16)
    out_sum[...] += contract(merged, branch, 0, 0)
    products = grad_merged.astype(f32) * merged.astype(f32)
    queries = qkv[pl.ds(row, tile), :width] * bf16(score_scale)
    for head in range(heads_dev):
        own = slice(head * head_dim, (head + 1) * head_dim)
        keys = qkv[:, width + own.start : width + own.stop]
        values = qkv[:, 2 * width + own.start : 2 * width + own.stop]
        upstream = grad_merged[:, own]
        scores = contract(queries[:, own], keys, 1, 1) + jnp.concatenate(
            [band[head, :, pl.ds(start, tile)] for start in starts], axis=1
        )
        scores = jnp.where(same_doc, scores, masked)
        weights = jnp.exp(scores - stats[:, head : head + 1])
        delta = jnp.sum(products[:, own], axis=1, keepdims=True)
        grad_scores = weights * (contract(upstream, values, 1, 1) - delta)
        for block, start in enumerate(starts):
            grad_band[head, :, pl.ds(start, tile)] += grad_scores[
                :, block * tile : (block + 1) * tile
            ]
        grad_low = grad_scores.astype(bf16)
        grad_values[:, own] += contract(weights.astype(bf16), upstream, 0, 0)
        grad_keys[:, own] += contract(grad_low, queries[:, own], 0, 0)
        grad_qkv[pl.ds(row, tile), own] = (
            contract(grad_low, keys, 1, 0) * score_scale
        ).astype(bf16)

    @pl.when(step == pl.num_programs(0) - 1)
    def _():
        grad_qkv[:, width : 2 * width] = grad_keys[...].astype(bf16)
        grad_qkv[:, 2 * width :] = grad_values[...].astype(bf16)
        far_part[...] = contract(grad_qkv[half:], w_in[...], 1, 1).astype(bf16)
        near_part[...] = contract(grad_qkv[:half], w_in[...], 1, 1)
        rows = width // 2
        for index, part in enumerate(halves):
            block = index ^ place[length // tile] % 2
            part[...] = out_sum[pl.ds(pl.multiple_of(block * rows, rows), rows)].astype(bf16)
        for head in range(heads_dev):
            grad_near[head] = grad_band[head, :, length - tile : length + 2 * tile]
            grad_far[head, 0] = jnp.full(
                (8, tile), jnp.sum(grad_band[head, :, : length - tile]), f32
            )
            grad_far[head, 1] = jnp.full(
                (8, tile), jnp.sum(grad_band[head, :, length + 2 * tile :]), f32
            )


def plane_attention_back(
    qkv, doc_row, doc_col, attended, stats, near, far, w_in, w_out, place, table, strip
):
    length, model_width = 2 * near.shape[0], near.shape[1]
    steps = length // tile
    heads_dev = table.shape[1]
    width = heads_dev * head_dim
    shapes = [
        ((length, 3 * width), bf16),
        ((heads_dev, tile, 3 * tile), f32),
        ((heads_dev, 2, 8, tile), f32),
        ((length // 2, model_width), f32),
        ((length // 2, model_width), bf16),
    ] + [((width // 2, model_width), bf16)] * 2
    return pl.pallas_call(
        functools.partial(plane_attention_back_kernel, length),
        grid=(steps,),
        in_specs=[
            pl.BlockSpec(memory_space=pltpu.SMEM),
            pl.BlockSpec(memory_space=pltpu.SMEM),
            whole(strip.shape),
            whole(qkv.shape),
            whole(doc_row.shape),
            pl.BlockSpec((tile, 1), lambda step: (step, 0)),
            pl.BlockSpec((tile, width), lambda step: (step, 0)),
            pl.BlockSpec((tile, tile), lambda step: (step, 0)),
            near_block(steps, model_width),
            far_block(steps, model_width),
            whole(w_in.shape),
            whole(w_out.shape),
        ],
        out_specs=[whole(shape) for shape, _ in shapes],
        out_shape=[jax.ShapeDtypeStruct(shape, kind) for shape, kind in shapes],
        scratch_shapes=[
            pltpu.VMEM((heads_dev, tile, 2 * length), f32),
            pltpu.VMEM((heads_dev, tile, 2 * length), f32),
            pltpu.VMEM((length, width), f32),
            pltpu.VMEM((length, width), f32),
            pltpu.VMEM((width, model_width), f32),
        ],
        compiler_params=pltpu.CompilerParams(vmem_limit_bytes=20 * 2**20),
        cost_estimate=pl.CostEstimate(
            flops=10 * length * length * width + 10 * length * model_width * width,
            bytes_accessed=12 * 2**20,
            transcendentals=length * length * heads_dev,
        ),
    )(place, table, strip, qkv, doc_row, doc_col, attended, stats, near, far, w_in, w_out)


def gelu_and_slope(pre_act):
    size = jnp.abs(pre_act)
    gauss = jnp.exp(-0.5 * pre_act * pre_act)
    ratio = 1.0 / (1.0 + np.float32(0.3275911 * 0.5**0.5) * size)
    series = np.float32(1.061405429)
    for factor in (-1.453152027, 1.421413741, -0.284496736, 0.254829592):
        series = series * ratio + np.float32(factor)
    tail = 0.5 * series * ratio * gauss
    cumulative = jnp.where(pre_act < 0, tail, 1.0 - tail)
    slope = cumulative + pre_act * gauss * np.float32((2 * np.pi) ** -0.5)
    return pre_act * cumulative, slope


def ff_kernel(rows, pair, activated, slope, part):
    columns = rows.shape[1]
    value, gradient = gelu_and_slope(contract(rows[...], pair[:, :columns], 1, 1))
    activated[...] = value.astype(bf16)
    slope[...] = gradient.astype(bf16)
    part[...] = contract(activated[...], pair[:, columns:], 1, 0).astype(part.dtype)


def ff_first_kernel(rows, *refs):
    parts, (activated, slope, part, pair) = refs[:4], refs[4:]

    @pl.when(pl.program_id(0) == 0)
    def _():
        units = parts[0].shape[0]
        for index, ref in enumerate(parts):
            pair[index * units : (index + 1) * units] = ref[...]

    ff_kernel(rows, pair, activated, slope, part)


def ff_back_kernel(rows, slope, pair, grad_pre, part):
    columns = rows.shape[1]
    grad_act = contract(rows[...], pair[:, columns:], 1, 1)
    grad_pre[...] = (grad_act * slope[...].astype(f32)).astype(bf16)
    part[...] = contract(grad_pre[...], pair[:, :columns], 1, 0).astype(part.dtype)


def by_rows(kernel, step_rows, row_operands, whole_operands, outs, whole_outs=()):
    rows = row_operands[0].shape[0]
    return pl.pallas_call(
        kernel,
        grid=(rows // step_rows,),
        in_specs=[
            pl.BlockSpec((step_rows, operand.shape[1]), lambda step: (step, 0))
            for operand in row_operands
        ]
        + [whole(operand.shape) for operand in whole_operands],
        out_specs=[pl.BlockSpec((step_rows, columns), lambda step: (step, 0)) for columns, _ in outs]
        + [whole(shape) for shape in whole_outs],
        out_shape=[jax.ShapeDtypeStruct((rows, columns), kind) for columns, kind in outs]
        + [jax.ShapeDtypeStruct(shape, bf16) for shape in whole_outs],
        compiler_params=pltpu.CompilerParams(vmem_limit_bytes=10 * 2**20),
        cost_estimate=pl.CostEstimate(
            flops=4 * rows * outs[0][0] * row_operands[0].shape[1],
            bytes_accessed=6 * 2**20,
            transcendentals=0,
        ),
    )(*row_operands, *whole_operands)


def ff_grads_kernel(
    pre_near, pre_far, act_near, act_far, normed_near, normed_far, low_near, low_far, *outs
):
    columns = normed_near.shape[1]
    units = outs[0].shape[0]
    up = (
        contract(pre_near[...], normed_near[...], 0, 0)
        + contract(pre_far[...], normed_far[...], 0, 0)
    ).astype(bf16)
    down = (
        contract(act_near[...], low_near[...], 0, 0) + contract(act_far[...], low_far[...], 0, 0)
    ).astype(bf16)

    @pl.when(pl.program_id(0) == 0)
    def _():
        for index in range(2):
            block = slice(index * units, (index + 1) * units)
            outs[index][:, :columns] = up[block]
            outs[index][:, columns:] = down[block]

    @pl.when(pl.program_id(0) == 1)
    def _():
        outs[2][:, :columns] = up[:units]
        outs[2][:, columns:] = down[:units]
        outs[3][...] = up[units:]
        outs[4][...] = down[units:]


def ff_grads(pre, act, normed, low):
    rows, hidden_units = pre[0].shape
    columns = normed[0].shape[1]
    shapes = [(hidden_units // 4, 2 * columns)] * 3 + [(hidden_units // 4, columns)] * 2
    return pl.pallas_call(
        ff_grads_kernel,
        grid=(2,),
        in_specs=[pl.BlockSpec((rows, hidden_units // 2), lambda step: (0, step))] * 4
        + [whole((rows, columns))] * 4,
        out_specs=[whole(shape) for shape in shapes],
        out_shape=[jax.ShapeDtypeStruct(shape, bf16) for shape in shapes],
        compiler_params=pltpu.CompilerParams(vmem_limit_bytes=14 * 2**20),
        cost_estimate=pl.CostEstimate(
            flops=8 * rows * hidden_units * columns, bytes_accessed=8 * 2**20, transcendentals=0
        ),
    )(*pre, *act, *normed, *low)


def in_grads_kernel(place, near, far, grad_qkv, *refs):
    ends, outs, (total, extra) = refs[:-6], refs[-6:-2], refs[-2:]
    half = near.shape[0]
    columns = grad_qkv.shape[1]
    total[:, :columns] = (
        contract(near[...], grad_qkv[:half], 0, 0) + contract(far[...], grad_qkv[half:], 0, 0)
    ).astype(bf16)
    rows = outs[0].shape[0] // 8
    if ends:
        gain_0, gain_1, table_0, table_1 = ends
        lines = lax.broadcasted_iota(jnp.int32, (tile, gain_0.shape[1]), 0)
        gains = jnp.where(lines == 0, gain_0[...], jnp.where(lines == 1, gain_1[...], 0.0))
        extra[...] = jnp.transpose(gains)
        table = table_0[...] + table_1[...]
        buckets = table.shape[0] // 8
        blank = jnp.zeros((8 - buckets, tile), f32)
        for block in range(8):
            row = pl.multiple_of((place[0] // 2 * 8 + block) * rows, rows)
            extra[pl.ds(row, 8)] += jnp.concatenate(
                [table[block * buckets : (block + 1) * buckets], blank]
            )
        total[:, columns:] = extra[...].astype(bf16)
    for out, offset in zip(outs, (0, 3, 1, 2)):
        plane = (place[8] + offset) % 4
        for index in range(8):
            owner = place[index]
            row = row_of(owner // 2, plane, owner % 2, rows)
            out[index * rows : (index + 1) * rows] = total[pl.ds(row, rows)]


def in_grads(place, near, far, grad_qkv, *ends):
    columns = grad_qkv.shape[1] + (tile if ends else 0)
    shape = (near.shape[1] // 4, columns)
    return pl.pallas_call(
        in_grads_kernel,
        in_specs=[pl.BlockSpec(memory_space=pltpu.SMEM)]
        + [pl.BlockSpec(memory_space=pltpu.VMEM)] * (3 + len(ends)),
        out_specs=[pl.BlockSpec(memory_space=pltpu.VMEM)] * 4,
        out_shape=[jax.ShapeDtypeStruct(shape, bf16)] * 4,
        scratch_shapes=[
            pltpu.VMEM((near.shape[1], columns), bf16),
            pltpu.VMEM((near.shape[1], tile), f32),
        ],
        compiler_params=pltpu.CompilerParams(vmem_limit_bytes=12 * 2**20),
        cost_estimate=pl.CostEstimate(
            flops=4 * near.shape[0] * near.shape[1] * columns,
            bytes_accessed=4 * 2**20,
            transcendentals=0,
        ),
    )(place, near, far, grad_qkv, *ends)


def add_in_kernel(own, lower, upper, opposite, near, far):
    total = sum_of_four([own, lower, upper, opposite]).astype(bf16)
    half = near.shape[0]
    near[...] = total[:half]
    far[...] = total[half:]


def combine_kernel(near_part, arrived, own, x_part, y_part, xy_part):
    rows = own.shape[0]
    own[...] = near_part[:rows] + arrived[:rows].astype(f32)
    for bits, out in ((1, x_part), (2, y_part), (3, xy_part)):
        block = slice(bits * rows, (bits + 1) * rows)
        out[...] = (near_part[block] + arrived[block].astype(f32)).astype(bf16)


def added(own, x_part, y_part, xy_part):
    return (own[...] + x_part[...].astype(f32)) + (
        y_part[...].astype(f32) + xy_part[...].astype(f32)
    )


def close_kernel(kept, own, x_part, y_part, xy_part, hidden, units):
    total = kept[...] + added(own, x_part, y_part, xy_part)
    hidden[...] = total
    units[...] = (total * inverse_rms(total)).astype(bf16)


def close_gain_kernel(kept, own, x_part, y_part, xy_part, gain, hidden, normed):
    total = kept[...] + added(own, x_part, y_part, xy_part)
    hidden[...] = total
    normed[...] = (total * inverse_rms(total) * gain[...]).astype(bf16)


def last_kernel(kept, own, x_part, y_part, xy_part, hidden):
    hidden[...] = (kept[...] + added(own, x_part, y_part, xy_part)).astype(bf16)


def middle_back_kernel(
    upstream, own, x_part, y_part, xy_part, middle, gain, grad_middle, branch, grad_gain
):
    grad_normed = added(own, x_part, y_part, xy_part)
    inverse = inverse_rms(middle[...])
    grad_gain[...] = jnp.sum(grad_normed * middle[...] * inverse, axis=0, keepdims=True)
    total = upstream[...].astype(f32) + unit_norm_back(
        middle[...], inverse, grad_normed * gain[...]
    )
    grad_middle[...] = total
    branch[...] = total.astype(bf16)


def layer_back_kernel(grad_middle, own, x_part, y_part, xy_part, hidden, upstream, low):
    total = grad_middle[...] + unit_norm_back(
        hidden[...], inverse_rms(hidden[...]), added(own, x_part, y_part, xy_part)
    )
    upstream[...] = total
    low[...] = total.astype(bf16)


def pair_kernel(axis, near, arrived, *outs):
    rows = near.shape[0] // len(outs)
    for index, out in enumerate(outs):
        block = slice(index * rows, (index + 1) * rows)
        if axis == 0:
            out[:rows] = near[block]
            out[rows:] = arrived[block]
        else:
            columns = near.shape[1]
            out[:, :columns] = near[block]
            out[:, columns:] = arrived[block]


def unit_kernel(tokens, hidden, units):
    total = tokens[...].astype(f32)
    hidden[...] = total
    units[...] = (total * inverse_rms(total)).astype(bf16)


def finish_in_kernel(layers, place, *refs):
    shares, (attn_in, gains, grad_in, grad_gain, ends) = refs[:4], refs[4:]
    rows = attn_in.shape[1]
    width = shares[0].shape[1] // 14
    members = attn_in.shape[2] // (3 * width)
    for layer_id in range(layers):
        row_dot = jnp.zeros((rows, 1), f32)
        for index in range(members):
            share = shares[index % 4]
            first = (index // 4 * 7 + layer_id * 4) * width
            member = place[index]
            for part in range(3):
                block = share[:, first + part * width : first + (part + 1) * width].astype(f32)
                columns = pl.ds(pl.multiple_of((part * members + member) * width, width), width)
                grad_in[layer_id, :, columns] = block * gains[layer_id]
                row_dot = row_dot + jnp.sum(
                    block * attn_in[layer_id, :, columns].astype(f32), axis=1, keepdims=True
                )
            if layer_id == 0:
                block = share[:, first + 3 * width : first + 4 * width].astype(f32)
                ends[...] = block if index == 0 else ends[...] + block
        grad_gain[layer_id] = jnp.concatenate(
            [row_dot, ends[:, layer_id : layer_id + 1]], axis=1
        )


def sum_of_four(parts):
    return (parts[0][...].astype(f32) + parts[1][...].astype(f32)) + (
        parts[2][...].astype(f32) + parts[3][...].astype(f32)
    )


def finish_ff_kernel(*refs):
    grads = refs[-2:]
    columns = grads[0].shape[2]
    for layer_id in range(grads[0].shape[0]):
        parts = refs[5 * layer_id : 5 * layer_id + 5]
        for side, out in enumerate(grads):
            halves = [part.at[:, side * columns : (side + 1) * columns] for part in parts[:3]]
            out[layer_id] = sum_of_four(halves + [parts[3 + side]])


def add_out_kernel(place, *refs):
    parts, (own, other) = refs[:-2], refs[-2:]
    for layer_id in range(own.shape[0]):
        total = parts[2 * layer_id][...].astype(f32) + parts[2 * layer_id + 1][...].astype(f32)
        rows = total.shape[0] // 2
        second = place[0] % 2 == 1
        own[layer_id] = jnp.where(second, total[rows:], total[:rows])
        other[layer_id] = jnp.where(second, total[:rows], total[rows:]).astype(bf16)


def finish_out_kernel(own, arrived, out):
    out[...] = own[...] + arrived[...].astype(f32)


def inverse_rms(hidden):
    return lax.rsqrt(jnp.mean(hidden * hidden, axis=-1, keepdims=True) + epsilon)


def prepare(bias_table, first_head, heads_dev):
    table = lax.dynamic_slice_in_dim(bias_table, first_head, heads_dev, 1)
    (near,) = call(near_kernel, [((heads_dev, tile, 3 * tile), f32)], table, smem=1)
    return table, near


def bucket_grads(first_lane, grads, bucket_count):
    (total,) = call(bucket_kernel, [((bucket_count, tile), f32)], first_lane, *grads, smem=1)
    return total


def gelu_parts(pre_act):
    cumulative = 0.5 * (1.0 + lax.erf(pre_act * np.float32(0.5**0.5)))
    slope = cumulative + pre_act * jnp.exp(-0.5 * pre_act * pre_act) * np.float32(
        (2 * np.pi) ** -0.5
    )
    return (pre_act * cumulative).astype(bf16), slope


def unit_norm_back(hidden, inverse, grad_unit):
    unit = hidden * inverse
    return inverse * (grad_unit - unit * jnp.mean(grad_unit * unit, axis=-1, keepdims=True))


def gather_rows(block, axes):
    return lax.all_gather(block, axes, axis=0, tiled=True)


def toggle(array, axis, bits):
    return lax.ppermute(array, axis, [(i, i ^ bits) for i in range(lax.axis_size(axis))])


def shift(array, by):
    planes = lax.axis_size("z")
    return lax.ppermute(array, "z", [(i, (i + by) % planes) for i in range(planes)])


def plane_gather(block, *holds):
    near = jnp.concatenate([block] + [toggle(block, "head", bits) for bits in (1, 2, 3)])
    near, *holds = tie(near, *holds)
    return (near, toggle(near, "core", 1), *holds)


def plane_scatter(near_part, far_part):
    rows, columns = near_part.shape[0] // 4, near_part.shape[1]
    own, *others = call(
        combine_kernel,
        [((rows, columns), f32)] + [((rows, columns), bf16)] * 3,
        near_part,
        toggle(far_part, "core", 1),
    )
    shares = [own] + [toggle(other, "head", bits) for bits, other in zip((1, 2, 3), others)]
    return shares, own


def tie(*arrays):
    return lax.optimization_barrier(arrays)


def after(array, other):
    return lax.optimization_barrier((array, other))[0]


def scatter_sum(partial, axes, members):
    blocks = partial.astype(bf16).reshape(members, -1, partial.shape[1])
    return jnp.sum(lax.all_to_all(blocks, axes, 0, 0, tiled=True).astype(f32), axis=0)


def local_general(tokens, doc_start, bias_table, attn_in, attn_out, ff_in, ff_out, gains, cotangent):
    heads_n, z_n, core_n = (lax.axis_size(axis) for axis in everyone)
    devices = heads_n * z_n * core_n
    group, spare = ("z", "core"), "head"
    ff_group, ff_spare, ff_members = ("head", "core"), "z", heads_n * core_n
    blocks = z_n * core_n
    block_rows, model_width = tokens.shape[1:]
    layer_count, weight_rows = attn_in.shape[:2]
    length = block_rows * blocks
    heads_all = bias_table.shape[1]
    member = lax.axis_index("z") * core_n + lax.axis_index("core")
    heads_dev = max(1, heads_all // blocks)
    head_groups = heads_all // heads_dev
    split = blocks // head_groups
    head_group, query_part = member // split, member % split
    query_rows = length // split
    width = heads_dev * head_dim
    first = (query_part * (query_rows // tile)).astype(jnp.int32).reshape(1)
    place = jnp.arange(length // tile, dtype=jnp.int32)
    out_row = head_group * width

    def swap(array):
        return lax.all_to_all(array, everyone, 0, 0, tiled=True)

    starts = jnp.broadcast_to(
        doc_start.astype(f32)[:, None], (heads_n, blocks, block_rows)
    ).reshape(devices, block_rows)
    ff_gains = gains[:, :, 1].astype(f32).reshape(1, -1)
    small = swap(
        jnp.concatenate(
            [starts, jnp.broadcast_to(ff_gains, (devices, layer_count * weight_rows))], axis=1
        )
    )
    doc_row = small[:blocks, :block_rows].reshape(1, length)
    doc_col = lax.dynamic_slice_in_dim(
        doc_row.reshape(length, 1), query_part * query_rows, query_rows, 0
    )
    gain_ff = jnp.transpose(
        small[:, block_rows:].reshape(devices, layer_count, weight_rows), (1, 0, 2)
    ).reshape(layer_count, 1, model_width)
    table, near = prepare(bias_table, head_group * heads_dev, heads_dev)

    gain_attn = gains[:, :, 0].astype(f32)[:, :, None]
    own_in = attn_in.astype(f32)

    def fetch_in(layer_id):
        scaled = (own_in[layer_id] * gain_attn[layer_id]).astype(bf16)
        columns = jnp.transpose(
            scaled.reshape(weight_rows, 3, head_groups, width), (2, 0, 1, 3)
        ).reshape(head_groups, weight_rows, 3 * width)
        columns = jnp.repeat(columns, split, axis=0)
        columns = jnp.broadcast_to(columns[None], (heads_n, *columns.shape))
        return swap(columns.reshape(devices, weight_rows, 3 * width)).reshape(
            model_width, 3 * width
        )

    def fetch_ff(layer_id):
        pair = jnp.concatenate([ff_in[layer_id], ff_out[layer_id]], axis=1)
        pair = gather_rows(pair, ff_spare)
        return pair[:, :model_width], pair[:, model_width:]

    hidden, upstream = tokens[0].astype(f32), cotangent[0]
    weights_in = [fetch_in(layer_id) for layer_id in range(layer_count)]
    weights_out = lax.dynamic_slice_in_dim(
        lax.all_gather(attn_out, everyone, axis=1, tiled=True), out_row, width, 1
    )
    weights_ff = [fetch_ff(layer_id) for layer_id in range(layer_count)]

    records = []
    for layer_id in range(layer_count):
        w_in, w_out, (w_up, w_down) = (
            weights_in[layer_id], weights_out[layer_id], weights_ff[layer_id],
        )
        inverse = inverse_rms(hidden)
        units = gather_rows((hidden * inverse).astype(bf16), group)
        qkv = jnp.dot(units, w_in, preferred_element_type=f32).astype(bf16)
        attended, _, stats = attention(
            qkv, doc_row, doc_col, first, place, table, near, query_rows
        )
        mixed = jnp.dot(attended, w_out, preferred_element_type=f32)
        if split > 1:
            mixed = lax.dynamic_update_slice_in_dim(
                jnp.zeros((length, model_width), f32), mixed, query_part * query_rows, 0
            )
        middle = hidden + scatter_sum(mixed, group, blocks)
        inverse_ff = inverse_rms(middle)
        normed_ff = gather_rows((middle * inverse_ff * gain_ff[layer_id]).astype(bf16), ff_group)
        activated, slope = gelu_parts(contract(normed_ff, w_up, 1, 1))
        ff_result = jnp.dot(activated, w_down, preferred_element_type=f32)
        records.append(
            (hidden, inverse, units, qkv, attended, stats, middle, inverse_ff, normed_ff,
             activated, slope)
        )
        hidden = middle + scatter_sum(ff_result, ff_group, ff_members)
    output = hidden

    grads_ff, grads_in, grads_out, grads_gain_ff, grads_table = (
        [None] * layer_count for _ in range(5)
    )
    for layer_id in reversed(range(layer_count)):
        w_in, w_out, (w_up, w_down) = (
            weights_in[layer_id], weights_out[layer_id], weights_ff[layer_id],
        )
        (hidden, inverse, units, qkv, attended, stats, middle, inverse_ff, normed_ff,
         activated, slope) = records[layer_id]
        grad_low = gather_rows(upstream.astype(bf16), ff_group)
        grad_pre = (contract(grad_low, w_down, 1, 1) * slope).astype(bf16)
        grad_normed = scatter_sum(
            jnp.dot(grad_pre, w_up, preferred_element_type=f32), ff_group, ff_members
        )
        grad_pair = jnp.concatenate(
            [contract(grad_pre, normed_ff, 0, 0), contract(activated, grad_low, 0, 0)], axis=1
        ).astype(bf16)
        grads_ff[layer_id] = lax.psum_scatter(
            grad_pair, ff_spare, scatter_dimension=0, tiled=True
        ).astype(f32)
        grads_gain_ff[layer_id] = jnp.sum(grad_normed * middle * inverse_ff, axis=0)
        grad_middle = upstream + unit_norm_back(
            middle, inverse_ff, grad_normed * gain_ff[layer_id]
        )
        branch = gather_rows(grad_middle.astype(bf16), group)
        if split > 1:
            branch = lax.dynamic_slice_in_dim(branch, query_part * query_rows, query_rows, 0)
        grad_attended = contract(branch, w_out, 1, 1).astype(bf16)
        grad_qkv, grad_near, grad_far = attention_back(
            qkv, doc_row, doc_col, attended, grad_attended, stats, first, place, table, near, split
        )
        grads_table[layer_id] = (grad_near, grad_far)
        grad_units = scatter_sum(contract(grad_qkv, w_in, 1, 1), group, blocks)
        upstream = grad_middle + unit_norm_back(hidden, inverse, grad_units)
        grad_out = lax.dynamic_update_slice_in_dim(
            jnp.zeros((model_width, model_width), bf16),
            contract(attended, branch, 0, 0).astype(bf16),
            out_row,
            0,
        )
        grads_out[layer_id] = lax.psum_scatter(
            grad_out, everyone, scatter_dimension=0, tiled=True
        ).astype(f32)
        grads_in[layer_id] = contract(units, grad_qkv, 0, 0).astype(bf16)

    bucket_count = table.shape[0]
    grad_table = sum(
        bucket_grads(jnp.zeros((1,), jnp.int32), entry, bucket_count) for entry in grads_table
    )[:, :heads_dev]
    grad_table = lax.dynamic_update_slice_in_dim(
        jnp.zeros((bucket_count, heads_all), f32), grad_table, head_group * heads_dev, 1
    )
    grad_table = jnp.transpose(
        grad_table.reshape(blocks, bucket_count // blocks, heads_n, heads_all // heads_n),
        (2, 0, 1, 3),
    ).reshape(devices, -1)
    grad_gain_ff = jnp.transpose(
        jnp.stack(grads_gain_ff).reshape(layer_count, devices, weight_rows), (1, 0, 2)
    ).reshape(devices, -1)
    ends = jnp.sum(swap(jnp.concatenate([grad_gain_ff, grad_table], axis=1)), axis=0)
    grad_gain_ff = ends[: layer_count * weight_rows].reshape(layer_count, weight_rows)
    grad_bias_table = ends[layer_count * weight_rows :].reshape(
        bucket_count // blocks, heads_all // heads_n
    )
    grads_attn_in, grads_gains = [], []
    for layer_id in range(layer_count):
        parts = swap(grads_in[layer_id].reshape(devices, weight_rows, 3 * width)).astype(f32)
        parts = jnp.sum(parts.reshape(heads_n, blocks, weight_rows, 3 * width), axis=0)
        parts = jnp.sum(parts.reshape(head_groups, split, weight_rows, 3, width), axis=1)
        unit_grad = jnp.transpose(parts, (1, 2, 0, 3)).reshape(weight_rows, 3 * model_width)
        grads_attn_in.append(unit_grad * gain_attn[layer_id])
        grads_gains.append(
            jnp.stack(
                [jnp.sum(unit_grad * own_in[layer_id], axis=1), grad_gain_ff[layer_id]], axis=1
            )
        )
    return (
        output[None],
        upstream[None],
        jnp.stack(grads_attn_in),
        jnp.stack(grads_out),
        jnp.stack([entry[:, :model_width] for entry in grads_ff]),
        jnp.stack([entry[:, model_width:] for entry in grads_ff]),
        jnp.stack(grads_gains),
        grad_bias_table,
    )


def local_plane(tokens, doc_start, bias_table, attn_in, attn_out, ff_in, ff_out, gains, cotangent):
    heads_n, z_n, core_n = (lax.axis_size(axis) for axis in everyone)
    devices = heads_n * z_n * core_n
    at_head, at_z, at_core = (lax.axis_index(axis) for axis in everyone)
    members = heads_n * core_n
    block_rows, model_width = tokens.shape[1:]
    layer_count, weight_rows = attn_in.shape[:2]
    length = block_rows * members
    heads_all = bias_table.shape[1]
    heads_dev = heads_all // members
    width = heads_dev * head_dim
    member = at_head * core_n + at_core
    turn = [
        ((h * z_n + z) * core_n + c, ((h ^ z) * z_n + h) * core_n + c)
        for h in range(heads_n)
        for z in range(z_n)
        for c in range(core_n)
    ]
    turn_back = [(target, source) for source, target in turn]
    place = jnp.stack(
        [
            (at_head ^ bits) * core_n + (at_core ^ other)
            for other in range(core_n)
            for bits in range(heads_n)
        ]
        + [at_z]
        + [
            (at_head ^ bits ^ at_z) * core_n + (at_core ^ other)
            for other in range(core_n)
            for bits in range(heads_n)
        ]
    ).astype(jnp.int32)

    def relay(array):
        return lax.ppermute(array, everyone, turn)

    def relay_back(array):
        return lax.ppermute(array, everyone, turn_back)

    def swap(array):
        return lax.all_to_all(array, everyone, 0, 0, tiled=True)

    row_shape = (block_rows, model_width)
    gain_attn = gains[:, :, 0].astype(f32)[:, :, None]
    near_share, far_share = call(
        share_in_kernel,
        [((members // 2 * layer_count * weight_rows, 3 * width), bf16)] * 2,
        place,
        attn_in,
        gain_attn,
        smem=1,
    )

    half_turns = [
        [
            (z * core_n + c, (2 * c + (a ^ z % 2)) * core_n + z // 2)
            for z in range(z_n)
            for c in range(core_n)
        ]
        for a in range(2)
    ]

    def fetch_out(layer_id, hold):
        own = attn_out[layer_id]
        other = toggle(own, "core", 1)
        head = jnp.where(
            at_core == 0, jnp.concatenate([own, other]), jnp.concatenate([other, own])
        )
        head = after(head, hold)
        return [
            lax.ppermute(head, ("z", "core"), [(holder, user) for user, holder in turns])
            for turns in half_turns
        ]

    def owners_halves(halves):
        return [
            lax.ppermute(half, ("z", "core"), turns) for half, turns in zip(halves, half_turns)
        ]

    def pair_chips(near, arrived, axis):
        rows, columns = near.shape[0] // 4, near.shape[1]
        shape = (2 * rows, columns) if axis == 0 else (rows, 2 * columns)
        return call(functools.partial(pair_kernel, axis), [(shape, bf16)] * 4, near, arrived)

    def share_chips(blocks):
        return [blocks[0]] + [toggle(blocks[bits], "head", bits) for bits in (1, 2, 3)]

    units_shape = [(row_shape, f32), (row_shape, bf16)]

    starts = jnp.broadcast_to(
        doc_start.astype(f32)[None, :, None], (heads_n, z_n, core_n, block_rows)
    )
    ff_gains = gains[:, :, 1].astype(f32).reshape(1, -1)
    small = jnp.concatenate(
        [
            starts.reshape(devices, block_rows),
            jnp.broadcast_to(ff_gains, (devices, layer_count * weight_rows)),
        ],
        axis=1,
    )
    table, strip = prepare(bias_table, member * heads_dev, heads_dev)
    hidden, strip = tie(relay(tokens[0]), strip)
    hidden, shares, cotangent_low = tie(
        hidden,
        share_chips(pair_chips(near_share, toggle(far_share, "core", 1), 0)),
        cotangent[0].astype(bf16),
    )
    hidden, unit_rows = call(unit_kernel, units_shape, hidden)
    first_rows = [toggle(unit_rows, "head", bits) for bits in (1, 2, 3)]
    small = swap(after(small, first_rows[0]))
    doc_row = small[:members, :block_rows].reshape(2, 2, core_n, block_rows)
    at_block = at_head ^ at_z
    for axis, bit in ((0, at_block // 2), (1, at_block % 2), (2, at_core)):
        doc_row = jnp.where(bit == 1, jnp.flip(doc_row, axis), doc_row)
    doc_row = jnp.transpose(doc_row, (2, 0, 1, 3)).reshape(1, length)
    doc_col = doc_row.reshape(length, 1)
    gain_ff = jnp.transpose(
        small[:, block_rows:].reshape(devices, layer_count, weight_rows), (1, 0, 2)
    ).reshape(layer_count, 1, model_width)

    def round_planes(array, by, hold):
        return shift(after(array, hold), by)

    ff_pairs = [
        jnp.concatenate([ff_in[layer_id], ff_out[layer_id]], axis=1) for layer_id in range(layer_count)
    ]

    def ff_both(kernel, row_operands, pair, columns):
        return zip(
            *(
                by_rows(
                    kernel,
                    256,
                    operands,
                    [pair],
                    [(pair.shape[0], bf16)] * columns + [(model_width, kind)],
                )
                for operands, kind in zip(zip(*row_operands), (f32, bf16))
            )
        )

    def ff_forward(normed, *parts):
        units = parts[0].shape[0] * len(parts)
        outs = [(units, bf16), (units, bf16)]
        *near, pair = by_rows(
            ff_first_kernel,
            256,
            [normed[0]],
            parts,
            outs + [(model_width, f32)],
            [(units, 2 * model_width)],
        )
        far = by_rows(ff_kernel, 256, [normed[1]], [pair], outs + [(model_width, bf16)])
        return pair, *zip(near, far)

    def ff_backward(low, slopes, pair):
        return ff_both(ff_back_kernel, [low, slopes], pair, 1)

    def assemble_in(share, lower, upper, opposite):
        return call(
            assemble_in_kernel,
            [((model_width, 3 * width), bf16)],
            place,
            share,
            lower,
            upper,
            opposite,
            smem=1,
        )[0]

    share, later_share = call(
        join_kernel, [((members * weight_rows, 3 * width), bf16)] * layer_count, *shares
    )
    near, lower, upper, opposite, halves, doc_row, doc_col, gain_ff, *ff_pairs = tie(
        jnp.concatenate([unit_rows, *first_rows]),
        shift(share, 1),
        shift(share, -1),
        shift(share, 2),
        fetch_out(0, hidden),
        doc_row,
        doc_col,
        gain_ff,
        *ff_pairs,
    )
    units = (near, toggle(near, "core", 1))
    w_in = assemble_in(share, lower, upper, opposite)
    w_out, qkv, attended, stats, *parts = plane_attention(
        *units, w_in, halves, doc_row, doc_col, place, table, strip
    )
    parts, lower, upstream = tie(
        parts, round_planes(ff_pairs[0], 1, near), relay(after(cotangent_low, near))
    )
    parts, own = plane_scatter(*parts)
    parts, upper = tie(parts, round_planes(ff_pairs[0], -1, own))
    middle, normed_rows = call(close_gain_kernel, units_shape, hidden, *parts, gain_ff[0])
    *normed, opposite = plane_gather(normed_rows, round_planes(ff_pairs[0], 2, normed_rows))
    pair, acts, slopes, parts = ff_forward(normed, ff_pairs[0], lower, upper, opposite)
    records = [
        (hidden, units, w_in, w_out, pair, qkv, attended, stats, middle, normed, acts, slopes)
    ]
    parts, own = plane_scatter(*parts)
    parts, lower, upper = tie(
        parts, round_planes(later_share, 1, own), round_planes(later_share, -1, own)
    )
    hidden, unit_rows = call(close_kernel, units_shape, middle, *parts)

    near, far, opposite, halves = plane_gather(
        unit_rows, round_planes(later_share, 2, unit_rows), fetch_out(1, unit_rows)
    )
    units = (near, far)
    w_in = assemble_in(later_share, lower, upper, opposite)
    w_out, qkv, attended, stats, *parts = plane_attention(
        *units, w_in, halves, doc_row, doc_col, place, table, strip
    )
    low = plane_gather(after(upstream, far))
    parts, near_low, lower = tie(parts, low[0], round_planes(ff_pairs[1], 1, far))
    low = (near_low, low[1])
    parts, own = plane_scatter(*parts)
    parts, upper = tie(parts, round_planes(ff_pairs[1], -1, own))
    middle, normed_rows = call(close_gain_kernel, units_shape, hidden, *parts, gain_ff[1])
    *normed, opposite = plane_gather(normed_rows, round_planes(ff_pairs[1], 2, normed_rows))
    pair, acts, slopes, last_parts = ff_forward(normed, ff_pairs[1], lower, upper, opposite)
    records.append(
        (hidden, units, w_in, w_out, pair, qkv, attended, stats, middle, normed, acts, slopes)
    )

    def back_to_middle(parts, upstream, middle, gain):
        return call(
            middle_back_kernel, units_shape + [((1, model_width), f32)], upstream, *parts, middle, gain
        )

    def attention_grads(record, branch):
        _, _, w_in, w_out, _, qkv, attended, stats, *_ = record
        grad_qkv, grad_near, grad_far, near_part, far_part, *halves = plane_attention_back(
            qkv, doc_row, doc_col, attended, stats, *branch, w_in, w_out, place, table, strip
        )
        return grad_qkv, (grad_near, grad_far), (near_part, far_part), halves

    def table_grads(near_and_far):
        return bucket_grads(at_core.reshape(1) * heads_dev + 8, near_and_far, table.shape[0])

    def add_in(own, lower, upper, opposite):
        shape = (own.shape[0] // 2, own.shape[1])
        return call(add_in_kernel, [(shape, bf16)] * 2, own, lower, upper, opposite)

    record = records[1]
    hidden, units, _, _, pair, *_, middle, normed, acts, slopes = record
    pres, parts = ff_backward(low, slopes, pair)
    parts, own = plane_scatter(*parts)
    planes = ff_grads(after(pres, own), acts, normed, low)
    parts, ff_lower = tie(parts, shift(planes[1], -1))
    last_parts, _ = plane_scatter(*after(last_parts, parts))
    grad_middle, branch_rows, gain_1 = back_to_middle(parts, upstream, middle, gain_ff[1])
    *branch, ff_upper = plane_gather(branch_rows, round_planes(planes[2], 1, branch_rows))
    grad_qkv, strips_1, parts, halves_1 = attention_grads(record, branch)
    parts, last_parts, opposite_up = tie(
        parts, last_parts, round_planes(planes[3], 2, branch[1])
    )
    parts, own = plane_scatter(*parts)
    grad_in = in_grads(place, *units, after(grad_qkv, own))
    parts, opposite_down, in_opposite, output, table_1 = tie(
        parts,
        round_planes(planes[4], 2, own),
        shift(grad_in[3], 2),
        call(last_kernel, [(row_shape, bf16)], middle, *after(last_parts, own))[0],
        table_grads(after(strips_1, own)),
    )
    grads_ff = [planes[0], ff_lower, ff_upper, opposite_up, opposite_down]
    upstream, low_rows = call(layer_back_kernel, units_shape, grad_middle, *parts, hidden)

    record = records[0]
    hidden, units, _, _, pair, *_, middle, normed, acts, slopes = record
    *low, in_lower, in_upper = plane_gather(
        low_rows,
        round_planes(grad_in[1], -1, low_rows),
        round_planes(grad_in[2], 1, low_rows),
    )
    pres, parts = ff_backward(low, slopes, pair)
    parts, own = plane_scatter(*parts)
    planes = ff_grads(after(pres, own), acts, normed, low)
    parts, ff_lower, adds_1 = tie(
        parts,
        shift(planes[1], -1),
        add_in(*after([grad_in[0], in_lower, in_upper, in_opposite], own)),
    )
    grad_middle, branch_rows, gain_0 = back_to_middle(parts, upstream, middle, gain_ff[0])
    *branch, ff_upper, halves_1 = plane_gather(
        branch_rows,
        round_planes(planes[2], 1, branch_rows),
        owners_halves(after(halves_1, branch_rows)),
    )
    grad_qkv, strips_0, parts, halves_0 = attention_grads(record, branch)
    parts, output, opposite_up = tie(
        parts,
        relay_back(after(output, branch[1])),
        round_planes(planes[3], 2, branch[1]),
    )
    parts, own = plane_scatter(*parts)
    table_0 = table_grads(after(strips_0, own))
    grad_in = in_grads(
        place, *units, after(grad_qkv, own), gain_0, gain_1, table_0, table_1
    )
    parts, opposite_down, in_opposite, output = tie(
        parts,
        round_planes(planes[4], 2, own),
        shift(grad_in[3], 2),
        after(output, own).astype(f32),
    )
    upstream, low_rows = call(layer_back_kernel, units_shape, grad_middle, *parts, hidden)
    in_lower = round_planes(grad_in[1], -1, low_rows)
    in_upper = round_planes(grad_in[2], 1, low_rows)
    grad_tokens = relay_back(low_rows)
    halves_0 = owners_halves(after(halves_0, low_rows))
    grads_ff = [planes[0], ff_lower, ff_upper, opposite_up, opposite_down] + grads_ff
    grad_up, grad_down = call(finish_ff_kernel, [(ff_in.shape, f32)] * 2, *after(grads_ff, low_rows))
    own_out, other_out = call(
        add_out_kernel, [(attn_out.shape, f32), (attn_out.shape, bf16)], place, *halves_0, *halves_1, smem=1
    )
    (grad_attn_out,) = call(
        finish_out_kernel, [(attn_out.shape, f32)], own_out, toggle(other_out, "core", 1)
    )
    adds_0 = add_in(grad_in[0], in_lower, in_upper, in_opposite)
    near_in, far_in = (jnp.concatenate(pair, axis=1) for pair in zip(adds_0, adds_1))
    shares_in = share_chips(pair_chips(near_in, toggle(far_in, "core", 1), 1))
    own_buckets = table.shape[0] // (z_n * core_n)
    grad_attn_in, grad_gains, ends = call(
        functools.partial(finish_in_kernel, layer_count),
        [(attn_in.shape, f32), (gains.shape, f32), ((weight_rows, tile), f32)],
        place,
        *shares_in,
        attn_in,
        gain_attn,
        smem=1,
    )
    return (
        output[None],
        grad_tokens.astype(f32)[None],
        grad_attn_in,
        grad_attn_out,
        grad_up,
        grad_down,
        grad_gains,
        ends[:own_buckets, 8 : 8 + heads_all // heads_n],
    )


def solution(mesh):
    sizes = dict(mesh.shape)
    cores = 2
    fine = Mesh(
        mesh.devices.reshape(sizes["head"], sizes["blk"] // cores, cores), everyone
    )
    blk = ("z", "core")
    in_specs = (
        P("head", blk, None),
        P(None, blk),
        P(),
        P(None, everyone, None),
        P(None, everyone, None),
        P(None, everyone, None),
        P(None, everyone, None),
        P(None, everyone, None),
        P("head", blk, None),
    )
    out_specs = (
        P("head", blk, None),
        P("head", blk, None),
        P(None, everyone, None),
        P(None, everyone, None),
        P(None, everyone, None),
        P(None, everyone, None),
        P(None, everyone, None),
        P(blk, "head"),
    )
    plane = sizes["head"] == 4 and sizes["blk"] == 8
    local = local_plane if plane else local_general
    return jax.shard_map(local, mesh=fine, in_specs=in_specs, out_specs=out_specs, check_vma=False)
```

```python
import functools

import jax
import jax.numpy as jnp
import numpy as np
from jax import lax
from jax.experimental import pallas as pl
from jax.experimental.pallas import tpu as pltpu
from jax.sharding import Mesh
from jax.sharding import PartitionSpec as P

bounds = (1, 2, 3, 4, 5, 6, 7, 8, 12, 16, 23, 32, 46, 64, 91)
epsilon = 1e-06
masked = -1e30
score_scale = 0.125
head_dim = 64
tile = 128
everyone = ("head", "z", "core")
bf16 = jnp.bfloat16
f32 = jnp.float32


def contract(lhs, rhs, lhs_dim, rhs_dim):
    return lax.dot_general(
        lhs, rhs, (((lhs_dim,), (rhs_dim,)), ((), ())), preferred_element_type=f32
    )


def near_buckets(shape):
    offsets = (
        lax.broadcasted_iota(jnp.int32, shape, 1) - tile - lax.broadcasted_iota(jnp.int32, shape, 0)
    )
    distance = jnp.abs(offsets)
    bucket = jnp.where(offsets > 0, 16, 0)
    for boundary in bounds:
        bucket = bucket + jnp.where(distance >= boundary, 1, 0)
    return bucket


def near_kernel(table, near):
    bucket = near_buckets(near.shape[1:])
    for head in range(near.shape[0]):
        values = jnp.zeros(near.shape[1:], f32)
        for bucket_id in range(table.shape[0]):
            values = jnp.where(bucket == bucket_id, table[bucket_id, head], values)
        near[head] = values


def bucket_kernel(first_lane, near, far, out):
    bucket = near_buckets(near.shape[1:])
    rows = lax.broadcasted_iota(jnp.int32, out.shape, 0)
    lanes = lax.broadcasted_iota(jnp.int32, out.shape, 1)
    total = jnp.zeros(out.shape, f32)
    for head in range(near.shape[0]):
        strip = near[head]
        for bucket_id in range(out.shape[0]):
            value = jnp.sum(jnp.where(bucket == bucket_id, strip, 0.0), axis=0, keepdims=True)
            value = jnp.sum(value, axis=1, keepdims=True)
            if bucket_id in (15, 31):
                value = value + far[head, bucket_id // 16, :1, :1]
            total = jnp.where((rows == bucket_id) & (lanes == head + first_lane[0]), value, total)
    out[...] = total


def fill_band(band, table, near, heads_dev, length):
    for head in range(heads_dev):
        band[head, :, : length - tile] = jnp.full((tile, length - tile), table[15, head], f32)
        band[head, :, length - tile : length + 2 * tile] = near[head]
        band[head, :, length + 2 * tile :] = jnp.full(
            (tile, length - 2 * tile), table[31, head], f32
        )


def band_starts(place, at, length, skip=0):
    return [
        pl.multiple_of(length + (place[skip + block] - place[skip + at]) * tile, tile)
        for block in range(length // tile)
    ]


def attention_kernel(
    heads_dev, length, first, place, table, near, qkv, doc_row, doc_col, out, local, stats, band
):
    step = pl.program_id(0)
    width = heads_dev * head_dim

    @pl.when(step == 0)
    def _():
        fill_band(band, table, near, heads_dev, length)

    row = pl.multiple_of((first[0] + step) * tile, tile)
    out_row = pl.multiple_of((place[first[0] + step] - first[0]) * tile, tile)
    starts = band_starts(place, first[0] + step, length)
    same_doc = doc_col[...] == doc_row[...]
    queries = qkv[pl.ds(row, tile), :width] * bf16(score_scale)
    lanes = lax.broadcasted_iota(jnp.int32, (tile, tile), 1)
    collected = jnp.zeros((tile, tile), f32)
    for head in range(heads_dev):
        own = slice(head * head_dim, (head + 1) * head_dim)
        keys = qkv[:, width + own.start : width + own.stop]
        values = qkv[:, 2 * width + own.start : 2 * width + own.stop]
        scores = contract(queries[:, own], keys, 1, 1)
        scores = scores + jnp.concatenate(
            [band[head, :, pl.ds(start, tile)] for start in starts], axis=1
        )
        scores = jnp.where(same_doc, scores, masked)
        peak = jnp.max(scores, axis=1, keepdims=True)
        weights = jnp.exp(scores - peak)
        total = jnp.sum(weights, axis=1, keepdims=True)
        mixed = contract(weights.astype(bf16), values, 1, 0) / total
        out[pl.ds(out_row, tile), own] = mixed.astype(bf16)
        local[:, own] = mixed.astype(bf16)
        collected = jnp.where(lanes == head, peak + jnp.log(total), collected)
    stats[...] = collected


def attention_back_kernel(
    heads_dev, length, split, first, place, table, near, qkv, doc_row, doc_col, attended, grad_out, stats,
    grad_qkv, grad_near, grad_far, band, grad_band, grad_keys, grad_values,
):
    step = pl.program_id(0)
    width = heads_dev * head_dim

    @pl.when(step == 0)
    def _():
        fill_band(band, table, near, heads_dev, length)
        grad_band[...] = jnp.zeros_like(grad_band)
        grad_keys[...] = jnp.zeros_like(grad_keys)
        grad_values[...] = jnp.zeros_like(grad_values)
        if split > 1:
            grad_qkv[...] = jnp.zeros_like(grad_qkv)

    row = pl.multiple_of((first[0] + step) * tile, tile)
    out_row = pl.multiple_of((place[first[0] + step] - first[0]) * tile, tile)
    starts = band_starts(place, first[0] + step, length)
    same_doc = doc_col[...] == doc_row[...]
    at_step = pl.multiple_of(step * tile, tile)
    queries = qkv[pl.ds(row, tile), :width] * bf16(score_scale)
    for head in range(heads_dev):
        own = slice(head * head_dim, (head + 1) * head_dim)
        keys = qkv[:, width + own.start : width + own.stop]
        values = qkv[:, 2 * width + own.start : 2 * width + own.stop]
        upstream = grad_out[pl.ds(out_row, tile), own]
        scores = contract(queries[:, own], keys, 1, 1) + jnp.concatenate(
            [band[head, :, pl.ds(start, tile)] for start in starts], axis=1
        )
        scores = jnp.where(same_doc, scores, masked)
        weights = jnp.exp(scores - stats[:, head : head + 1])
        delta = jnp.sum(
            upstream.astype(f32) * attended[pl.ds(at_step, tile), own].astype(f32),
            axis=1,
            keepdims=True,
        )
        grad_scores = weights * (contract(upstream, values, 1, 1) - delta)
        for block, start in enumerate(starts):
            grad_band[head, :, pl.ds(start, tile)] += grad_scores[
                :, block * tile : (block + 1) * tile
            ]
        grad_low = grad_scores.astype(bf16)
        grad_values[:, own] += contract(weights.astype(bf16), upstream, 0, 0)
        grad_keys[:, own] += contract(grad_low, queries[:, own], 0, 0)
        grad_qkv[pl.ds(row, tile), own] = (
            contract(grad_low, keys, 1, 0) * score_scale
        ).astype(bf16)

    @pl.when(step == pl.num_programs(0) - 1)
    def _():
        grad_qkv[:, width : 2 * width] = grad_keys[...].astype(bf16)
        grad_qkv[:, 2 * width :] = grad_values[...].astype(bf16)
        for head in range(heads_dev):
            grad_near[head] = grad_band[head, :, length - tile : length + 2 * tile]
            grad_far[head, 0] = jnp.full(
                (8, tile), jnp.sum(grad_band[head, :, : length - tile]), f32
            )
            grad_far[head, 1] = jnp.full(
                (8, tile), jnp.sum(grad_band[head, :, length + 2 * tile :]), f32
            )


def whole(shape):
    return pl.BlockSpec(shape, lambda step: (0,) * len(shape), pipeline_mode=pl.Buffered(1))


def attention(qkv, doc_row, doc_col, first, place, table, near, rows):
    length = qkv.shape[0]
    heads_dev = table.shape[1]
    width = heads_dev * head_dim
    return pl.pallas_call(
        functools.partial(attention_kernel, heads_dev, length),
        grid=(rows // tile,),
        in_specs=[
            pl.BlockSpec(memory_space=pltpu.SMEM),
            pl.BlockSpec(memory_space=pltpu.SMEM),
            pl.BlockSpec(memory_space=pltpu.SMEM),
            whole(near.shape),
            whole(qkv.shape),
            whole(doc_row.shape),
            pl.BlockSpec((tile, 1), lambda step: (step, 0)),
        ],
        out_specs=[
            whole((rows, width)),
            pl.BlockSpec((tile, width), lambda step: (step, 0)),
            pl.BlockSpec((tile, tile), lambda step: (step, 0)),
        ],
        out_shape=[
            jax.ShapeDtypeStruct((rows, width), bf16),
            jax.ShapeDtypeStruct((rows, width), bf16),
            jax.ShapeDtypeStruct((rows, tile), f32),
        ],
        scratch_shapes=[pltpu.VMEM((heads_dev, tile, 2 * length), f32)],
        compiler_params=pltpu.CompilerParams(vmem_limit_bytes=40 * 2**20),
        cost_estimate=pl.CostEstimate(
            flops=4 * rows * length * width,
            bytes_accessed=4 * length * width * 2,
            transcendentals=rows * length * heads_dev,
        ),
    )(first, place, table, near, qkv, doc_row, doc_col)


def attention_back(
    qkv, doc_row, doc_col, attended, grad_out, stats, first, place, table, near, split
):
    length = qkv.shape[0]
    rows = grad_out.shape[0]
    heads_dev = table.shape[1]
    width = heads_dev * head_dim
    return pl.pallas_call(
        functools.partial(attention_back_kernel, heads_dev, length, split),
        grid=(rows // tile,),
        in_specs=[
            pl.BlockSpec(memory_space=pltpu.SMEM),
            pl.BlockSpec(memory_space=pltpu.SMEM),
            pl.BlockSpec(memory_space=pltpu.SMEM),
            whole(near.shape),
            whole(qkv.shape),
            whole(doc_row.shape),
            pl.BlockSpec((tile, 1), lambda step: (step, 0)),
            whole((rows, width)),
            whole((rows, width)),
            pl.BlockSpec((tile, tile), lambda step: (step, 0)),
        ],
        out_specs=[
            whole((length, 3 * width)),
            whole((heads_dev, tile, 3 * tile)),
            whole((heads_dev, 2, 8, tile)),
        ],
        out_shape=[
            jax.ShapeDtypeStruct((length, 3 * width), bf16),
            jax.ShapeDtypeStruct((heads_dev, tile, 3 * tile), f32),
            jax.ShapeDtypeStruct((heads_dev, 2, 8, tile), f32),
        ],
        scratch_shapes=[
            pltpu.VMEM((heads_dev, tile, 2 * length), f32),
            pltpu.VMEM((heads_dev, tile, 2 * length), f32),
            pltpu.VMEM((length, width), f32),
            pltpu.VMEM((length, width), f32),
        ],
        compiler_params=pltpu.CompilerParams(vmem_limit_bytes=48 * 2**20),
        cost_estimate=pl.CostEstimate(
            flops=10 * rows * length * width,
            bytes_accessed=8 * length * width * 2,
            transcendentals=rows * length * heads_dev,
        ),
    )(first, place, table, near, qkv, doc_row, doc_col, attended, grad_out, stats)


def call(kernel, shapes, *operands, smem=0):
    return pl.pallas_call(
        kernel,
        in_specs=[pl.BlockSpec(memory_space=pltpu.SMEM)] * smem
        + [pl.BlockSpec(memory_space=pltpu.VMEM)] * (len(operands) - smem),
        out_specs=[pl.BlockSpec(memory_space=pltpu.VMEM)] * len(shapes),
        out_shape=[jax.ShapeDtypeStruct(shape, kind) for shape, kind in shapes],
        compiler_params=pltpu.CompilerParams(vmem_limit_bytes=10 * 2**20),
    )(*operands)


def share_in_kernel(place, attn_in, gains, near, far):
    layers, rows = attn_in.shape[:2]
    half = near.shape[0] // (layers * rows)
    width = near.shape[1] // 3
    for index in range(2 * half):
        member = place[index]
        for layer_id in range(layers):
            block = jnp.concatenate(
                [
                    attn_in[
                        layer_id,
                        :,
                        pl.ds(pl.multiple_of((part * 2 * half + member) * width, width), width),
                    ]
                    for part in range(3)
                ],
                axis=1,
            )
            at = (index % half * layers + layer_id) * rows
            out = near if index < half else far
            out[at : at + rows] = (block.astype(f32) * gains[layer_id]).astype(bf16)


def join_kernel(*refs):
    shares, outs = refs[:4], refs[4:]
    rows = outs[0].shape[0] // 8
    for chip, share in enumerate(shares):
        for core in range(2):
            for layer_id, out in enumerate(outs):
                source = (core * len(outs) + layer_id) * rows
                target = (chip * 2 + core) * rows
                out[target : target + rows] = share[source : source + rows]


def row_of(chip, plane, core, rows, planes=4):
    return pl.multiple_of(((chip * planes + plane) * 2 + core) * rows, rows)


def assemble_in_kernel(place, own, lower, upper, opposite, out):
    at_z, at_core, at_head = place[8], place[0] % 2, place[0] // 2
    rows = own.shape[0] // 8
    for part, offset in ((own, 0), (lower, 3), (upper, 1), (opposite, 2)):
        plane = (at_z + offset) % 4
        for index in range(8):
            row = row_of(at_head ^ (index // 2), plane, at_core ^ (index % 2), rows)
            out[pl.ds(row, rows)] = part[index * rows : (index + 1) * rows]


def plane_attention_kernel(
    length, place, table, strip, near, far, w_in, *refs
):
    halves, (doc_row, doc_col, w_out, qkv, attended, stats, near_part, far_part, band) = (
        refs[:2], refs[2:],
    )
    step = pl.program_id(0)
    half = length // 2
    heads_dev = table.shape[1]
    width = heads_dev * head_dim

    @pl.when(step == 0)
    def _():
        fill_band(band, table, strip, heads_dev, length)
        swapped = place[length // tile] % 2 == 1
        rows = width // 2
        w_out[:rows] = jnp.where(swapped, halves[1][...], halves[0][...])
        w_out[rows:] = jnp.where(swapped, halves[0][...], halves[1][...])
        qkv[:half] = contract(near[...], w_in[...], 1, 0).astype(bf16)
        qkv[half:] = contract(far[...], w_in[...], 1, 0).astype(bf16)

    row = pl.multiple_of(step * half, half)
    queries = qkv[pl.ds(row, half), :width] * bf16(score_scale)
    lanes = lax.broadcasted_iota(jnp.int32, (tile, tile), 1)
    blocks = half // tile
    collected = [jnp.zeros((tile, tile), f32)] * blocks
    results = []
    for head in range(heads_dev):
        own = slice(head * head_dim, (head + 1) * head_dim)
        keys = qkv[:, width + own.start : width + own.stop]
        values = qkv[:, 2 * width + own.start : 2 * width + own.stop]
        raw_scores = contract(queries[:, own], keys, 1, 1)
        weights, totals = [], []
        for block in range(blocks):
            lines = slice(block * tile, (block + 1) * tile)
            starts = band_starts(place, step * blocks + block, length, length // tile + 1)
            scores = raw_scores[lines] + jnp.concatenate(
                [band[head, :, pl.ds(start, tile)] for start in starts], axis=1
            )
            scores = jnp.where(doc_col[lines] == doc_row[...], scores, masked)
            peak = jnp.max(scores, axis=1, keepdims=True)
            exp_scores = jnp.exp(scores - peak)
            total = jnp.sum(exp_scores, axis=1, keepdims=True)
            weights.append(exp_scores.astype(bf16))
            totals.append(total)
            collected[block] = jnp.where(lanes == head, peak + jnp.log(total), collected[block])
        mixed = contract(jnp.concatenate(weights), values, 1, 0) / jnp.concatenate(totals)
        results.append(mixed.astype(bf16))
    stats[...] = jnp.concatenate(collected)
    merged = jnp.concatenate(results, axis=1)
    attended[...] = merged
    part = contract(merged, w_out[...], 1, 0)

    @pl.when(step == 0)
    def _():
        near_part[...] = part

    @pl.when(step == 1)
    def _():
        far_part[...] = part.astype(bf16)


def plane_attention(near, far, w_in, halves, doc_row, doc_col, place, table, strip):
    length, model_width = 2 * near.shape[0], near.shape[1]
    half = length // 2
    heads_dev = table.shape[1]
    width = heads_dev * head_dim
    return pl.pallas_call(
        functools.partial(plane_attention_kernel, length),
        grid=(2,),
        in_specs=[
            pl.BlockSpec(memory_space=pltpu.SMEM),
            pl.BlockSpec(memory_space=pltpu.SMEM),
            whole(strip.shape),
            whole(near.shape),
            whole(far.shape),
            whole(w_in.shape),
            *[whole(half.shape) for half in halves],
            whole(doc_row.shape),
            pl.BlockSpec((half, 1), lambda step: (step, 0)),
        ],
        out_specs=[
            whole((width, model_width)),
            whole((length, 3 * width)),
            pl.BlockSpec((half, width), lambda step: (step, 0)),
            pl.BlockSpec((half, tile), lambda step: (step, 0)),
            whole((half, model_width)),
            whole((half, model_width)),
        ],
        out_shape=[
            jax.ShapeDtypeStruct((width, model_width), bf16),
            jax.ShapeDtypeStruct((length, 3 * width), bf16),
            jax.ShapeDtypeStruct((length, width), bf16),
            jax.ShapeDtypeStruct((length, tile), f32),
            jax.ShapeDtypeStruct((length // 2, model_width), f32),
            jax.ShapeDtypeStruct((length // 2, model_width), bf16),
        ],
        scratch_shapes=[pltpu.VMEM((heads_dev, tile, 2 * length), f32)],
        compiler_params=pltpu.CompilerParams(vmem_limit_bytes=24 * 2**20),
        cost_estimate=pl.CostEstimate(
            flops=4 * length * length * width + 8 * length * model_width * width,
            bytes_accessed=12 * 2**20,
            transcendentals=length * length * heads_dev,
        ),
    )(place, table, strip, near, far, w_in, *halves, doc_row, doc_col)


def plane_attention_back_kernel(
    length, place, table, strip, qkv, doc_row, doc_col, attended, stats, near, far, w_in, w_out,
    grad_qkv, grad_near, grad_far, near_part, far_part, *rest
):
    halves, (band, grad_band, grad_keys, grad_values, out_sum) = rest[:2], rest[2:]
    step = pl.program_id(0)
    half = length // 2
    heads_dev = table.shape[1]
    width = heads_dev * head_dim

    @pl.when(step == 0)
    def _():
        fill_band(band, table, strip, heads_dev, length)
        grad_band[...] = jnp.zeros_like(grad_band)
        grad_keys[...] = jnp.zeros_like(grad_keys)
        grad_values[...] = jnp.zeros_like(grad_values)
        out_sum[...] = jnp.zeros_like(out_sum)

    row = pl.multiple_of(step * half, half)
    branch = jnp.where(step == 0, near[...], far[...])
    merged = attended[...]
    grad_merged = contract(branch, w_out[...], 1, 1).astype(bf16)
    out_sum[...] += contract(merged, branch, 0, 0)
    products = grad_merged.astype(f32) * merged.astype(f32)
    queries = qkv[pl.ds(row, half), :width] * bf16(score_scale)
    blocks = half // tile
    for head in range(heads_dev):
        own = slice(head * head_dim, (head + 1) * head_dim)
        keys = qkv[:, width + own.start : width + own.stop]
        values = qkv[:, 2 * width + own.start : 2 * width + own.stop]
        upstream = grad_merged[:, own]
        raw_scores = contract(queries[:, own], keys, 1, 1)
        grad_weights = contract(upstream, values, 1, 1)
        delta = jnp.sum(products[:, own], axis=1, keepdims=True)
        weights_low, grads_low = [], []
        for block in range(blocks):
            lines = slice(block * tile, (block + 1) * tile)
            starts = band_starts(place, step * blocks + block, length, length // tile + 1)
            scores = raw_scores[lines] + jnp.concatenate(
                [band[head, :, pl.ds(start, tile)] for start in starts], axis=1
            )
            scores = jnp.where(doc_col[lines] == doc_row[...], scores, masked)
            weights = jnp.exp(scores - stats[lines, head : head + 1])
            grad_scores = weights * (grad_weights[lines] - delta[lines])
            for index, start in enumerate(starts):
                grad_band[head, :, pl.ds(start, tile)] += grad_scores[
                    :, index * tile : (index + 1) * tile
                ]
            weights_low.append(weights.astype(bf16))
            grads_low.append(grad_scores.astype(bf16))
        weights_low, grads_low = jnp.concatenate(weights_low), jnp.concatenate(grads_low)
        grad_values[:, own] += contract(weights_low, upstream, 0, 0)
        grad_keys[:, own] += contract(grads_low, queries[:, own], 0, 0)
        grad_qkv[pl.ds(row, half), own] = (
            contract(grads_low, keys, 1, 0) * score_scale
        ).astype(bf16)

    @pl.when(step == pl.num_programs(0) - 1)
    def _():
        grad_qkv[:, width : 2 * width] = grad_keys[...].astype(bf16)
        grad_qkv[:, 2 * width :] = grad_values[...].astype(bf16)
        far_part[...] = contract(grad_qkv[half:], w_in[...], 1, 1).astype(bf16)
        near_part[...] = contract(grad_qkv[:half], w_in[...], 1, 1)
        rows = width // 2
        for index, part in enumerate(halves):
            block = index ^ place[length // tile] % 2
            part[...] = out_sum[pl.ds(pl.multiple_of(block * rows, rows), rows)].astype(bf16)
        for head in range(heads_dev):
            grad_near[head] = grad_band[head, :, length - tile : length + 2 * tile]
            grad_far[head, 0] = jnp.full(
                (8, tile), jnp.sum(grad_band[head, :, : length - tile]), f32
            )
            grad_far[head, 1] = jnp.full(
                (8, tile), jnp.sum(grad_band[head, :, length + 2 * tile :]), f32
            )


def plane_attention_back(
    qkv, doc_row, doc_col, attended, stats, near, far, w_in, w_out, place, table, strip
):
    length, model_width = 2 * near.shape[0], near.shape[1]
    half = length // 2
    heads_dev = table.shape[1]
    width = heads_dev * head_dim
    shapes = [
        ((length, 3 * width), bf16),
        ((heads_dev, tile, 3 * tile), f32),
        ((heads_dev, 2, 8, tile), f32),
        ((length // 2, model_width), f32),
        ((length // 2, model_width), bf16),
    ] + [((width // 2, model_width), bf16)] * 2
    return pl.pallas_call(
        functools.partial(plane_attention_back_kernel, length),
        grid=(2,),
        in_specs=[
            pl.BlockSpec(memory_space=pltpu.SMEM),
            pl.BlockSpec(memory_space=pltpu.SMEM),
            whole(strip.shape),
            whole(qkv.shape),
            whole(doc_row.shape),
            pl.BlockSpec((half, 1), lambda step: (step, 0)),
            pl.BlockSpec((half, width), lambda step: (step, 0)),
            pl.BlockSpec((half, tile), lambda step: (step, 0)),
            whole((half, model_width)),
            whole((half, model_width)),
            whole(w_in.shape),
            whole(w_out.shape),
        ],
        out_specs=[whole(shape) for shape, _ in shapes],
        out_shape=[jax.ShapeDtypeStruct(shape, kind) for shape, kind in shapes],
        scratch_shapes=[
            pltpu.VMEM((heads_dev, tile, 2 * length), f32),
            pltpu.VMEM((heads_dev, tile, 2 * length), f32),
            pltpu.VMEM((length, width), f32),
            pltpu.VMEM((length, width), f32),
            pltpu.VMEM((width, model_width), f32),
        ],
        compiler_params=pltpu.CompilerParams(vmem_limit_bytes=32 * 2**20),
        cost_estimate=pl.CostEstimate(
            flops=10 * length * length * width + 10 * length * model_width * width,
            bytes_accessed=12 * 2**20,
            transcendentals=length * length * heads_dev,
        ),
    )(place, table, strip, qkv, doc_row, doc_col, attended, stats, near, far, w_in, w_out)


def gelu_and_slope(pre_act):
    size = jnp.abs(pre_act)
    gauss = jnp.exp(-0.5 * pre_act * pre_act)
    ratio = 1.0 / (1.0 + np.float32(0.3275911 * 0.5**0.5) * size)
    series = np.float32(1.061405429)
    for factor in (-1.453152027, 1.421413741, -0.284496736, 0.254829592):
        series = series * ratio + np.float32(factor)
    tail = 0.5 * series * ratio * gauss
    cumulative = jnp.where(pre_act < 0, tail, 1.0 - tail)
    slope = cumulative + pre_act * gauss * np.float32((2 * np.pi) ** -0.5)
    return pre_act * cumulative, slope


def ff_kernel(rows, pair, activated, slope, part):
    columns = rows.shape[1]
    value, gradient = gelu_and_slope(contract(rows[...], pair[:, :columns], 1, 1))
    activated[...] = value.astype(bf16)
    slope[...] = gradient.astype(bf16)
    part[...] = contract(activated[...], pair[:, columns:], 1, 0).astype(part.dtype)


def ff_first_kernel(rows, *refs):
    parts, (activated, slope, part, pair) = refs[:5], refs[5:]

    @pl.when(pl.program_id(0) == 0)
    def _():
        units, columns = parts[0].shape[0], rows.shape[1]
        for index, ref in enumerate(parts[:3]):
            pair[index * units : (index + 1) * units] = ref[...]
        pair[3 * units :, :columns] = parts[3][...]
        pair[3 * units :, columns:] = parts[4][...]

    ff_kernel(rows, pair, activated, slope, part)


def ff_back_kernel(rows, slope, pair, grad_pre, part):
    columns = rows.shape[1]
    grad_act = contract(rows[...], pair[:, columns:], 1, 1)
    grad_pre[...] = (grad_act * slope[...].astype(f32)).astype(bf16)
    part[...] = contract(grad_pre[...], pair[:, :columns], 1, 0).astype(part.dtype)


def by_rows(kernel, step_rows, row_operands, whole_operands, outs, whole_outs=()):
    rows = row_operands[0].shape[0]
    return pl.pallas_call(
        kernel,
        grid=(rows // step_rows,),
        in_specs=[
            pl.BlockSpec((step_rows, operand.shape[1]), lambda step: (step, 0))
            for operand in row_operands
        ]
        + [whole(operand.shape) for operand in whole_operands],
        out_specs=[pl.BlockSpec((step_rows, columns), lambda step: (step, 0)) for columns, _ in outs]
        + [whole(shape) for shape in whole_outs],
        out_shape=[jax.ShapeDtypeStruct((rows, columns), kind) for columns, kind in outs]
        + [jax.ShapeDtypeStruct(shape, bf16) for shape in whole_outs],
        compiler_params=pltpu.CompilerParams(vmem_limit_bytes=10 * 2**20),
        cost_estimate=pl.CostEstimate(
            flops=4 * rows * outs[0][0] * row_operands[0].shape[1],
            bytes_accessed=6 * 2**20,
            transcendentals=0,
        ),
    )(*row_operands, *whole_operands)


def ff_grads_kernel(
    pre_near, pre_far, act_near, act_far, normed_near, normed_far, low_near, low_far, *outs
):
    columns = normed_near.shape[1]
    units = outs[0].shape[0]
    up = (
        contract(pre_near[...], normed_near[...], 0, 0)
        + contract(pre_far[...], normed_far[...], 0, 0)
    ).astype(bf16)
    down = (
        contract(act_near[...], low_near[...], 0, 0) + contract(act_far[...], low_far[...], 0, 0)
    ).astype(bf16)

    @pl.when(pl.program_id(0) == 0)
    def _():
        for index in range(2):
            block = slice(index * units, (index + 1) * units)
            outs[index][:, :columns] = up[block]
            outs[index][:, columns:] = down[block]

    @pl.when(pl.program_id(0) == 1)
    def _():
        outs[2][:, :columns] = up[:units]
        outs[2][:, columns:] = down[:units]
        outs[3][...] = up[units:]
        outs[4][...] = down[units:]


def ff_grads(pre, act, normed, low):
    rows, hidden_units = pre[0].shape
    columns = normed[0].shape[1]
    shapes = [(hidden_units // 4, 2 * columns)] * 3 + [(hidden_units // 4, columns)] * 2
    return pl.pallas_call(
        ff_grads_kernel,
        grid=(2,),
        in_specs=[pl.BlockSpec((rows, hidden_units // 2), lambda step: (0, step))] * 4
        + [whole((rows, columns))] * 4,
        out_specs=[whole(shape) for shape in shapes],
        out_shape=[jax.ShapeDtypeStruct(shape, bf16) for shape in shapes],
        compiler_params=pltpu.CompilerParams(vmem_limit_bytes=14 * 2**20),
        cost_estimate=pl.CostEstimate(
            flops=8 * rows * hidden_units * columns, bytes_accessed=8 * 2**20, transcendentals=0
        ),
    )(*pre, *act, *normed, *low)


def in_grads_kernel(place, near, far, grad_qkv, *refs):
    ends, outs, (total, extra) = refs[:-6], refs[-6:-2], refs[-2:]
    half = near.shape[0]
    columns = grad_qkv.shape[1]
    total[:, :columns] = (
        contract(near[...], grad_qkv[:half], 0, 0) + contract(far[...], grad_qkv[half:], 0, 0)
    ).astype(bf16)
    rows = outs[0].shape[0] // 8
    if ends:
        gain_0, gain_1, table_0, table_1 = ends
        lines = lax.broadcasted_iota(jnp.int32, (tile, gain_0.shape[1]), 0)
        gains = jnp.where(lines == 0, gain_0[...], jnp.where(lines == 1, gain_1[...], 0.0))
        extra[...] = jnp.transpose(gains)
        table = table_0[...] + table_1[...]
        buckets = table.shape[0] // 8
        blank = jnp.zeros((8 - buckets, tile), f32)
        for block in range(8):
            row = pl.multiple_of((place[0] // 2 * 8 + block) * rows, rows)
            extra[pl.ds(row, 8)] += jnp.concatenate(
                [table[block * buckets : (block + 1) * buckets], blank]
            )
        total[:, columns:] = extra[...].astype(bf16)
    for out, offset in zip(outs, (0, 3, 1, 2)):
        plane = (place[8] + offset) % 4
        for index in range(8):
            owner = place[index]
            row = row_of(owner // 2, plane, owner % 2, rows)
            out[index * rows : (index + 1) * rows] = total[pl.ds(row, rows)]


def in_grads(place, near, far, grad_qkv, *ends):
    columns = grad_qkv.shape[1] + (tile if ends else 0)
    shape = (near.shape[1] // 4, columns)
    return pl.pallas_call(
        in_grads_kernel,
        in_specs=[pl.BlockSpec(memory_space=pltpu.SMEM)]
        + [pl.BlockSpec(memory_space=pltpu.VMEM)] * (3 + len(ends)),
        out_specs=[pl.BlockSpec(memory_space=pltpu.VMEM)] * 4,
        out_shape=[jax.ShapeDtypeStruct(shape, bf16)] * 4,
        scratch_shapes=[
            pltpu.VMEM((near.shape[1], columns), bf16),
            pltpu.VMEM((near.shape[1], tile), f32),
        ],
        compiler_params=pltpu.CompilerParams(vmem_limit_bytes=12 * 2**20),
        cost_estimate=pl.CostEstimate(
            flops=4 * near.shape[0] * near.shape[1] * columns,
            bytes_accessed=4 * 2**20,
            transcendentals=0,
        ),
    )(place, near, far, grad_qkv, *ends)


def add_in_kernel(own, lower, upper, opposite, near, far):
    total = sum_of_four([own, lower, upper, opposite]).astype(bf16)
    half = near.shape[0]
    near[...] = total[:half]
    far[...] = total[half:]


def combine_kernel(near_part, arrived, own, x_part, y_part, xy_part):
    rows = own.shape[0]
    own[...] = near_part[:rows] + arrived[:rows].astype(f32)
    for bits, out in ((1, x_part), (2, y_part), (3, xy_part)):
        block = slice(bits * rows, (bits + 1) * rows)
        out[...] = (near_part[block] + arrived[block].astype(f32)).astype(bf16)


def added(own, x_part, y_part, xy_part):
    return (own[...] + x_part[...].astype(f32)) + (
        y_part[...].astype(f32) + xy_part[...].astype(f32)
    )


def close_kernel(kept, own, x_part, y_part, xy_part, hidden, units):
    total = kept[...] + added(own, x_part, y_part, xy_part)
    hidden[...] = total
    units[...] = (total * inverse_rms(total)).astype(bf16)


def close_gain_kernel(kept, own, x_part, y_part, xy_part, gain, hidden, normed):
    total = kept[...] + added(own, x_part, y_part, xy_part)
    hidden[...] = total
    normed[...] = (total * inverse_rms(total) * gain[...]).astype(bf16)


def last_kernel(kept, own, x_part, y_part, xy_part, hidden):
    hidden[...] = (kept[...] + added(own, x_part, y_part, xy_part)).astype(bf16)


def middle_back_kernel(
    upstream, own, x_part, y_part, xy_part, middle, gain, grad_middle, branch, grad_gain
):
    grad_normed = added(own, x_part, y_part, xy_part)
    inverse = inverse_rms(middle[...])
    grad_gain[...] = jnp.sum(grad_normed * middle[...] * inverse, axis=0, keepdims=True)
    total = upstream[...].astype(f32) + unit_norm_back(
        middle[...], inverse, grad_normed * gain[...]
    )
    grad_middle[...] = total
    branch[...] = total.astype(bf16)


def layer_back_kernel(grad_middle, own, x_part, y_part, xy_part, hidden, upstream, low):
    total = grad_middle[...] + unit_norm_back(
        hidden[...], inverse_rms(hidden[...]), added(own, x_part, y_part, xy_part)
    )
    upstream[...] = total
    low[...] = total.astype(bf16)


def pair_kernel(axis, near, arrived, *outs):
    rows = near.shape[0] // len(outs)
    for index, out in enumerate(outs):
        block = slice(index * rows, (index + 1) * rows)
        if axis == 0:
            out[:rows] = near[block]
            out[rows:] = arrived[block]
        else:
            columns = near.shape[1]
            out[:, :columns] = near[block]
            out[:, columns:] = arrived[block]


def unit_kernel(tokens, hidden, units):
    total = tokens[...].astype(f32)
    hidden[...] = total
    units[...] = (total * inverse_rms(total)).astype(bf16)


def finish_in_kernel(layers, place, *refs):
    shares, (attn_in, gains, grad_in, grad_gain, ends) = refs[:4], refs[4:]
    rows = attn_in.shape[1]
    width = shares[0].shape[1] // 14
    members = attn_in.shape[2] // (3 * width)
    for layer_id in range(layers):
        row_dot = jnp.zeros((rows, 1), f32)
        for index in range(members):
            share = shares[index % 4]
            first = (index // 4 * 7 + layer_id * 4) * width
            member = place[index]
            for part in range(3):
                block = share[:, first + part * width : first + (part + 1) * width].astype(f32)
                columns = pl.ds(pl.multiple_of((part * members + member) * width, width), width)
                grad_in[layer_id, :, columns] = block * gains[layer_id]
                row_dot = row_dot + jnp.sum(
                    block * attn_in[layer_id, :, columns].astype(f32), axis=1, keepdims=True
                )
            if layer_id == 0:
                block = share[:, first + 3 * width : first + 4 * width].astype(f32)
                ends[...] = block if index == 0 else ends[...] + block
        grad_gain[layer_id] = jnp.concatenate(
            [row_dot, ends[:, layer_id : layer_id + 1]], axis=1
        )


def sum_of_four(parts):
    return (parts[0][...].astype(f32) + parts[1][...].astype(f32)) + (
        parts[2][...].astype(f32) + parts[3][...].astype(f32)
    )


def finish_ff_kernel(*refs):
    grads = refs[-2:]
    columns = grads[0].shape[2]
    for layer_id in range(grads[0].shape[0]):
        parts = refs[5 * layer_id : 5 * layer_id + 5]
        for side, out in enumerate(grads):
            halves = [part.at[:, side * columns : (side + 1) * columns] for part in parts[:3]]
            out[layer_id] = sum_of_four(halves + [parts[3 + side]])


def add_out_kernel(place, *refs):
    parts, (own, other) = refs[:-2], refs[-2:]
    for layer_id in range(own.shape[0]):
        total = parts[2 * layer_id][...].astype(f32) + parts[2 * layer_id + 1][...].astype(f32)
        rows = total.shape[0] // 2
        second = place[0] % 2 == 1
        own[layer_id] = jnp.where(second, total[rows:], total[:rows])
        other[layer_id] = jnp.where(second, total[:rows], total[rows:]).astype(bf16)


def finish_out_kernel(own, arrived, out):
    out[...] = own[...] + arrived[...].astype(f32)


def inverse_rms(hidden):
    return lax.rsqrt(jnp.mean(hidden * hidden, axis=-1, keepdims=True) + epsilon)


def prepare(bias_table, first_head, heads_dev):
    table = lax.dynamic_slice_in_dim(bias_table, first_head, heads_dev, 1)
    (near,) = call(near_kernel, [((heads_dev, tile, 3 * tile), f32)], table, smem=1)
    return table, near


def bucket_grads(first_lane, grads, bucket_count):
    (total,) = call(bucket_kernel, [((bucket_count, tile), f32)], first_lane, *grads, smem=1)
    return total


def gelu_parts(pre_act):
    cumulative = 0.5 * (1.0 + lax.erf(pre_act * np.float32(0.5**0.5)))
    slope = cumulative + pre_act * jnp.exp(-0.5 * pre_act * pre_act) * np.float32(
        (2 * np.pi) ** -0.5
    )
    return (pre_act * cumulative).astype(bf16), slope


def unit_norm_back(hidden, inverse, grad_unit):
    unit = hidden * inverse
    return inverse * (grad_unit - unit * jnp.mean(grad_unit * unit, axis=-1, keepdims=True))


def gather_rows(block, axes):
    return lax.all_gather(block, axes, axis=0, tiled=True)


def toggle(array, axis, bits):
    return lax.ppermute(array, axis, [(i, i ^ bits) for i in range(lax.axis_size(axis))])


def shift(array, by):
    planes = lax.axis_size("z")
    return lax.ppermute(array, "z", [(i, (i + by) % planes) for i in range(planes)])


def plane_gather(block, *holds):
    near = jnp.concatenate([block] + [toggle(block, "head", bits) for bits in (1, 2, 3)])
    near, *holds = tie(near, *holds)
    return (near, toggle(near, "core", 1), *holds)


def plane_scatter(near_part, far_part):
    rows, columns = near_part.shape[0] // 4, near_part.shape[1]
    own, *others = call(
        combine_kernel,
        [((rows, columns), f32)] + [((rows, columns), bf16)] * 3,
        near_part,
        toggle(far_part, "core", 1),
    )
    shares = [own] + [toggle(other, "head", bits) for bits, other in zip((1, 2, 3), others)]
    return shares, own


def tie(*arrays):
    return lax.optimization_barrier(arrays)


def after(array, other):
    return lax.optimization_barrier((array, other))[0]


def scatter_sum(partial, axes, members):
    blocks = partial.astype(bf16).reshape(members, -1, partial.shape[1])
    return jnp.sum(lax.all_to_all(blocks, axes, 0, 0, tiled=True).astype(f32), axis=0)


def local_general(tokens, doc_start, bias_table, attn_in, attn_out, ff_in, ff_out, gains, cotangent):
    heads_n, z_n, core_n = (lax.axis_size(axis) for axis in everyone)
    devices = heads_n * z_n * core_n
    group, spare = ("z", "core"), "head"
    ff_group, ff_spare, ff_members = ("head", "core"), "z", heads_n * core_n
    blocks = z_n * core_n
    block_rows, model_width = tokens.shape[1:]
    layer_count, weight_rows = attn_in.shape[:2]
    length = block_rows * blocks
    heads_all = bias_table.shape[1]
    member = lax.axis_index("z") * core_n + lax.axis_index("core")
    heads_dev = max(1, heads_all // blocks)
    head_groups = heads_all // heads_dev
    split = blocks // head_groups
    head_group, query_part = member // split, member % split
    query_rows = length // split
    width = heads_dev * head_dim
    first = (query_part * (query_rows // tile)).astype(jnp.int32).reshape(1)
    place = jnp.arange(length // tile, dtype=jnp.int32)
    out_row = head_group * width

    def swap(array):
        return lax.all_to_all(array, everyone, 0, 0, tiled=True)

    starts = jnp.broadcast_to(
        doc_start.astype(f32)[:, None], (heads_n, blocks, block_rows)
    ).reshape(devices, block_rows)
    ff_gains = gains[:, :, 1].astype(f32).reshape(1, -1)
    small = swap(
        jnp.concatenate(
            [starts, jnp.broadcast_to(ff_gains, (devices, layer_count * weight_rows))], axis=1
        )
    )
    doc_row = small[:blocks, :block_rows].reshape(1, length)
    doc_col = lax.dynamic_slice_in_dim(
        doc_row.reshape(length, 1), query_part * query_rows, query_rows, 0
    )
    gain_ff = jnp.transpose(
        small[:, block_rows:].reshape(devices, layer_count, weight_rows), (1, 0, 2)
    ).reshape(layer_count, 1, model_width)
    table, near = prepare(bias_table, head_group * heads_dev, heads_dev)

    gain_attn = gains[:, :, 0].astype(f32)[:, :, None]
    own_in = attn_in.astype(f32)

    def fetch_in(layer_id):
        scaled = (own_in[layer_id] * gain_attn[layer_id]).astype(bf16)
        columns = jnp.transpose(
            scaled.reshape(weight_rows, 3, head_groups, width), (2, 0, 1, 3)
        ).reshape(head_groups, weight_rows, 3 * width)
        columns = jnp.repeat(columns, split, axis=0)
        columns = jnp.broadcast_to(columns[None], (heads_n, *columns.shape))
        return swap(columns.reshape(devices, weight_rows, 3 * width)).reshape(
            model_width, 3 * width
        )

    def fetch_ff(layer_id):
        pair = jnp.concatenate([ff_in[layer_id], ff_out[layer_id]], axis=1)
        pair = gather_rows(pair, ff_spare)
        return pair[:, :model_width], pair[:, model_width:]

    hidden, upstream = tokens[0].astype(f32), cotangent[0]
    weights_in = [fetch_in(layer_id) for layer_id in range(layer_count)]
    weights_out = lax.dynamic_slice_in_dim(
        lax.all_gather(attn_out, everyone, axis=1, tiled=True), out_row, width, 1
    )
    weights_ff = [fetch_ff(layer_id) for layer_id in range(layer_count)]

    records = []
    for layer_id in range(layer_count):
        w_in, w_out, (w_up, w_down) = (
            weights_in[layer_id], weights_out[layer_id], weights_ff[layer_id],
        )
        inverse = inverse_rms(hidden)
        units = gather_rows((hidden * inverse).astype(bf16), group)
        qkv = jnp.dot(units, w_in, preferred_element_type=f32).astype(bf16)
        attended, _, stats = attention(
            qkv, doc_row, doc_col, first, place, table, near, query_rows
        )
        mixed = jnp.dot(attended, w_out, preferred_element_type=f32)
        if split > 1:
            mixed = lax.dynamic_update_slice_in_dim(
                jnp.zeros((length, model_width), f32), mixed, query_part * query_rows, 0
            )
        middle = hidden + scatter_sum(mixed, group, blocks)
        inverse_ff = inverse_rms(middle)
        normed_ff = gather_rows((middle * inverse_ff * gain_ff[layer_id]).astype(bf16), ff_group)
        activated, slope = gelu_parts(contract(normed_ff, w_up, 1, 1))
        ff_result = jnp.dot(activated, w_down, preferred_element_type=f32)
        records.append(
            (hidden, inverse, units, qkv, attended, stats, middle, inverse_ff, normed_ff,
             activated, slope)
        )
        hidden = middle + scatter_sum(ff_result, ff_group, ff_members)
    output = hidden

    grads_ff, grads_in, grads_out, grads_gain_ff, grads_table = (
        [None] * layer_count for _ in range(5)
    )
    for layer_id in reversed(range(layer_count)):
        w_in, w_out, (w_up, w_down) = (
            weights_in[layer_id], weights_out[layer_id], weights_ff[layer_id],
        )
        (hidden, inverse, units, qkv, attended, stats, middle, inverse_ff, normed_ff,
         activated, slope) = records[layer_id]
        grad_low = gather_rows(upstream.astype(bf16), ff_group)
        grad_pre = (contract(grad_low, w_down, 1, 1) * slope).astype(bf16)
        grad_normed = scatter_sum(
            jnp.dot(grad_pre, w_up, preferred_element_type=f32), ff_group, ff_members
        )
        grad_pair = jnp.concatenate(
            [contract(grad_pre, normed_ff, 0, 0), contract(activated, grad_low, 0, 0)], axis=1
        ).astype(bf16)
        grads_ff[layer_id] = lax.psum_scatter(
            grad_pair, ff_spare, scatter_dimension=0, tiled=True
        ).astype(f32)
        grads_gain_ff[layer_id] = jnp.sum(grad_normed * middle * inverse_ff, axis=0)
        grad_middle = upstream + unit_norm_back(
            middle, inverse_ff, grad_normed * gain_ff[layer_id]
        )
        branch = gather_rows(grad_middle.astype(bf16), group)
        if split > 1:
            branch = lax.dynamic_slice_in_dim(branch, query_part * query_rows, query_rows, 0)
        grad_attended = contract(branch, w_out, 1, 1).astype(bf16)
        grad_qkv, grad_near, grad_far = attention_back(
            qkv, doc_row, doc_col, attended, grad_attended, stats, first, place, table, near, split
        )
        grads_table[layer_id] = (grad_near, grad_far)
        grad_units = scatter_sum(contract(grad_qkv, w_in, 1, 1), group, blocks)
        upstream = grad_middle + unit_norm_back(hidden, inverse, grad_units)
        grad_out = lax.dynamic_update_slice_in_dim(
            jnp.zeros((model_width, model_width), bf16),
            contract(attended, branch, 0, 0).astype(bf16),
            out_row,
            0,
        )
        grads_out[layer_id] = lax.psum_scatter(
            grad_out, everyone, scatter_dimension=0, tiled=True
        ).astype(f32)
        grads_in[layer_id] = contract(units, grad_qkv, 0, 0).astype(bf16)

    bucket_count = table.shape[0]
    grad_table = sum(
        bucket_grads(jnp.zeros((1,), jnp.int32), entry, bucket_count) for entry in grads_table
    )[:, :heads_dev]
    grad_table = lax.dynamic_update_slice_in_dim(
        jnp.zeros((bucket_count, heads_all), f32), grad_table, head_group * heads_dev, 1
    )
    grad_table = jnp.transpose(
        grad_table.reshape(blocks, bucket_count // blocks, heads_n, heads_all // heads_n),
        (2, 0, 1, 3),
    ).reshape(devices, -1)
    grad_gain_ff = jnp.transpose(
        jnp.stack(grads_gain_ff).reshape(layer_count, devices, weight_rows), (1, 0, 2)
    ).reshape(devices, -1)
    ends = jnp.sum(swap(jnp.concatenate([grad_gain_ff, grad_table], axis=1)), axis=0)
    grad_gain_ff = ends[: layer_count * weight_rows].reshape(layer_count, weight_rows)
    grad_bias_table = ends[layer_count * weight_rows :].reshape(
        bucket_count // blocks, heads_all // heads_n
    )
    grads_attn_in, grads_gains = [], []
    for layer_id in range(layer_count):
        parts = swap(grads_in[layer_id].reshape(devices, weight_rows, 3 * width)).astype(f32)
        parts = jnp.sum(parts.reshape(heads_n, blocks, weight_rows, 3 * width), axis=0)
        parts = jnp.sum(parts.reshape(head_groups, split, weight_rows, 3, width), axis=1)
        unit_grad = jnp.transpose(parts, (1, 2, 0, 3)).reshape(weight_rows, 3 * model_width)
        grads_attn_in.append(unit_grad * gain_attn[layer_id])
        grads_gains.append(
            jnp.stack(
                [jnp.sum(unit_grad * own_in[layer_id], axis=1), grad_gain_ff[layer_id]], axis=1
            )
        )
    return (
        output[None],
        upstream[None],
        jnp.stack(grads_attn_in),
        jnp.stack(grads_out),
        jnp.stack([entry[:, :model_width] for entry in grads_ff]),
        jnp.stack([entry[:, model_width:] for entry in grads_ff]),
        jnp.stack(grads_gains),
        grad_bias_table,
    )


def local_plane(tokens, doc_start, bias_table, attn_in, attn_out, ff_in, ff_out, gains, cotangent):
    heads_n, z_n, core_n = (lax.axis_size(axis) for axis in everyone)
    devices = heads_n * z_n * core_n
    at_head, at_z, at_core = (lax.axis_index(axis) for axis in everyone)
    members = heads_n * core_n
    block_rows, model_width = tokens.shape[1:]
    layer_count, weight_rows = attn_in.shape[:2]
    length = block_rows * members
    heads_all = bias_table.shape[1]
    heads_dev = heads_all // members
    width = heads_dev * head_dim
    member = at_head * core_n + at_core
    turn = [
        ((h * z_n + z) * core_n + c, ((h ^ z) * z_n + h) * core_n + c)
        for h in range(heads_n)
        for z in range(z_n)
        for c in range(core_n)
    ]
    turn_back = [(target, source) for source, target in turn]
    place = jnp.stack(
        [
            (at_head ^ bits) * core_n + (at_core ^ other)
            for other in range(core_n)
            for bits in range(heads_n)
        ]
        + [at_z]
        + [
            (at_head ^ bits ^ at_z) * core_n + (at_core ^ other)
            for other in range(core_n)
            for bits in range(heads_n)
        ]
    ).astype(jnp.int32)

    def relay(array):
        return lax.ppermute(array, everyone, turn)

    def relay_back(array):
        return lax.ppermute(array, everyone, turn_back)

    def swap(array):
        return lax.all_to_all(array, everyone, 0, 0, tiled=True)

    row_shape = (block_rows, model_width)
    gain_attn = gains[:, :, 0].astype(f32)[:, :, None]
    near_share, far_share = call(
        share_in_kernel,
        [((members // 2 * layer_count * weight_rows, 3 * width), bf16)] * 2,
        place,
        attn_in,
        gain_attn,
        smem=1,
    )

    half_turns = [
        [
            (z * core_n + c, (2 * c + (a ^ z % 2)) * core_n + z // 2)
            for z in range(z_n)
            for c in range(core_n)
        ]
        for a in range(2)
    ]

    def fetch_out(layer_id, hold):
        own = attn_out[layer_id]
        other = toggle(own, "core", 1)
        head = jnp.where(
            at_core == 0, jnp.concatenate([own, other]), jnp.concatenate([other, own])
        )
        head = after(head, hold)
        return [
            lax.ppermute(head, ("z", "core"), [(holder, user) for user, holder in turns])
            for turns in half_turns
        ]

    def owners_halves(halves):
        return [
            lax.ppermute(half, ("z", "core"), turns) for half, turns in zip(halves, half_turns)
        ]

    def pair_chips(near, arrived, axis):
        rows, columns = near.shape[0] // 4, near.shape[1]
        shape = (2 * rows, columns) if axis == 0 else (rows, 2 * columns)
        return call(functools.partial(pair_kernel, axis), [(shape, bf16)] * 4, near, arrived)

    def share_chips(blocks):
        return [blocks[0]] + [toggle(blocks[bits], "head", bits) for bits in (1, 2, 3)]

    units_shape = [(row_shape, f32), (row_shape, bf16)]

    starts = jnp.broadcast_to(
        doc_start.astype(f32)[None, :, None], (heads_n, z_n, core_n, block_rows)
    )
    ff_gains = gains[:, :, 1].astype(f32).reshape(1, -1)
    small = jnp.concatenate(
        [
            starts.reshape(devices, block_rows),
            jnp.broadcast_to(ff_gains, (devices, layer_count * weight_rows)),
        ],
        axis=1,
    )
    table, strip = prepare(bias_table, member * heads_dev, heads_dev)
    hidden, strip = tie(relay(tokens[0]), strip)
    hidden, shares, cotangent_low, halves, small = tie(
        hidden,
        share_chips(pair_chips(near_share, toggle(far_share, "core", 1), 0)),
        cotangent[0].astype(bf16),
        fetch_out(0, near_share),
        swap(after(small, near_share)),
    )
    hidden, unit_rows = call(unit_kernel, units_shape, hidden)
    doc_row = small[:members, :block_rows].reshape(2, 2, core_n, block_rows)
    at_block = at_head ^ at_z
    for axis, bit in ((0, at_block // 2), (1, at_block % 2), (2, at_core)):
        doc_row = jnp.where(bit == 1, jnp.flip(doc_row, axis), doc_row)
    doc_row = jnp.transpose(doc_row, (2, 0, 1, 3)).reshape(1, length)
    doc_col = doc_row.reshape(length, 1)
    gain_ff = jnp.transpose(
        small[:, block_rows:].reshape(devices, layer_count, weight_rows), (1, 0, 2)
    ).reshape(layer_count, 1, model_width)

    def round_planes(array, by, hold):
        return shift(after(array, hold), by)

    ff_pairs = [
        jnp.concatenate([ff_in[layer_id], ff_out[layer_id]], axis=1) for layer_id in range(layer_count)
    ]

    def ff_both(kernel, row_operands, pair, columns):
        return zip(
            *(
                by_rows(
                    kernel,
                    256,
                    operands,
                    [pair],
                    [(pair.shape[0], bf16)] * columns + [(model_width, kind)],
                )
                for operands, kind in zip(zip(*row_operands), (f32, bf16))
            )
        )

    def ff_forward(normed, *parts):
        units = 4 * parts[0].shape[0]
        outs = [(units, bf16), (units, bf16)]
        *near, pair = by_rows(
            ff_first_kernel,
            256,
            [normed[0]],
            parts,
            outs + [(model_width, f32)],
            [(units, 2 * model_width)],
        )
        far = by_rows(ff_kernel, 256, [normed[1]], [pair], outs + [(model_width, bf16)])
        return pair, *zip(near, far)

    def ff_backward(low, slopes, pair):
        return ff_both(ff_back_kernel, [low, slopes], pair, 1)

    def assemble_in(share, lower, upper, opposite):
        return call(
            assemble_in_kernel,
            [((model_width, 3 * width), bf16)],
            place,
            share,
            lower,
            upper,
            opposite,
            smem=1,
        )[0]

    share, later_share = call(
        join_kernel, [((members * weight_rows, 3 * width), bf16)] * layer_count, *shares
    )
    near, far, lower, upper, opposite, doc_row, doc_col, gain_ff, *ff_pairs = plane_gather(
        unit_rows,
        shift(share, 1),
        shift(share, -1),
        shift(share, 2),
        doc_row,
        doc_col,
        gain_ff,
        *ff_pairs,
    )
    units = (near, far)
    w_in = assemble_in(share, lower, upper, opposite)
    w_out, qkv, attended, stats, *parts = plane_attention(
        *units, w_in, halves, doc_row, doc_col, place, table, strip
    )
    parts, upstream = tie(parts, relay(after(cotangent_low, near)))
    parts, own = plane_scatter(*parts)
    parts, lower, upper = tie(
        parts, round_planes(ff_pairs[0], 1, own), round_planes(ff_pairs[0], -1, own)
    )
    middle, normed_rows = call(close_gain_kernel, units_shape, hidden, *parts, gain_ff[0])
    *normed, opposite_in, opposite_out = plane_gather(
        normed_rows,
        round_planes(ff_in[0], 2, normed_rows),
        round_planes(ff_out[0], 2, normed_rows),
    )
    pair, acts, slopes, parts = ff_forward(
        normed, ff_pairs[0], lower, upper, opposite_in, opposite_out
    )
    records = [
        (hidden, units, w_in, w_out, pair, qkv, attended, stats, middle, normed, acts, slopes)
    ]
    parts, own = plane_scatter(*parts)
    parts, lower, upper = tie(
        parts, round_planes(later_share, 1, own), round_planes(later_share, -1, own)
    )
    hidden, unit_rows = call(close_kernel, units_shape, middle, *parts)

    near, far, opposite, halves = plane_gather(
        unit_rows, round_planes(later_share, 2, unit_rows), fetch_out(1, unit_rows)
    )
    units = (near, far)
    w_in = assemble_in(later_share, lower, upper, opposite)
    w_out, qkv, attended, stats, *parts = plane_attention(
        *units, w_in, halves, doc_row, doc_col, place, table, strip
    )
    low = plane_gather(after(upstream, far))
    parts, near_low, lower = tie(parts, low[0], round_planes(ff_pairs[1], 1, far))
    low = (near_low, low[1])
    parts, own = plane_scatter(*parts)
    parts, upper, opposite_in = tie(
        parts, round_planes(ff_pairs[1], -1, own), round_planes(ff_in[1], 2, own)
    )
    middle, normed_rows = call(close_gain_kernel, units_shape, hidden, *parts, gain_ff[1])
    *normed, opposite_out = plane_gather(normed_rows, round_planes(ff_out[1], 2, normed_rows))
    pair, acts, slopes, last_parts = ff_forward(
        normed, ff_pairs[1], lower, upper, opposite_in, opposite_out
    )
    records.append(
        (hidden, units, w_in, w_out, pair, qkv, attended, stats, middle, normed, acts, slopes)
    )

    def back_to_middle(parts, upstream, middle, gain):
        return call(
            middle_back_kernel, units_shape + [((1, model_width), f32)], upstream, *parts, middle, gain
        )

    def attention_grads(record, branch):
        _, _, w_in, w_out, _, qkv, attended, stats, *_ = record
        grad_qkv, grad_near, grad_far, near_part, far_part, *halves = plane_attention_back(
            qkv, doc_row, doc_col, attended, stats, *branch, w_in, w_out, place, table, strip
        )
        return grad_qkv, (grad_near, grad_far), (near_part, far_part), halves

    def table_grads(near_and_far):
        return bucket_grads(at_core.reshape(1) * heads_dev + 8, near_and_far, table.shape[0])

    def add_in(own, lower, upper, opposite):
        shape = (own.shape[0] // 2, own.shape[1])
        return call(add_in_kernel, [(shape, bf16)] * 2, own, lower, upper, opposite)

    record = records[1]
    hidden, units, _, _, pair, *_, middle, normed, acts, slopes = record
    pres, parts = ff_backward(low, slopes, pair)
    parts, own = plane_scatter(*parts)
    planes = ff_grads(after(pres, own), acts, normed, low)
    parts, ff_lower = tie(parts, shift(planes[1], -1))
    last_parts, _ = plane_scatter(*after(last_parts, parts))
    grad_middle, branch_rows, gain_1 = back_to_middle(parts, upstream, middle, gain_ff[1])
    *branch, ff_upper = plane_gather(branch_rows, round_planes(planes[2], 1, branch_rows))
    grad_qkv, strips_1, parts, halves_1 = attention_grads(record, branch)
    parts, last_parts, opposite_up = tie(
        parts, last_parts, round_planes(planes[3], 2, branch[1])
    )
    parts, own = plane_scatter(*parts)
    parts, opposite_down, output = tie(
        parts,
        round_planes(planes[4], 2, own),
        call(last_kernel, [(row_shape, bf16)], middle, *after(last_parts, own))[0],
    )
    grads_ff = [planes[0], ff_lower, ff_upper, opposite_up, opposite_down]
    upstream, low_rows = call(layer_back_kernel, units_shape, grad_middle, *parts, hidden)

    record = records[0]
    hidden, units, _, _, pair, *_, middle, normed, acts, slopes = record
    grad_in = in_grads(place, *records[1][1], after(grad_qkv, low_rows))
    *low, in_opposite, table_1, halves_1 = plane_gather(
        low_rows,
        shift(grad_in[3], 2),
        table_grads(after(strips_1, low_rows)),
        owners_halves(after(halves_1, low_rows)),
    )
    pres, parts = ff_backward(low, slopes, pair)
    parts, own = plane_scatter(*parts)
    planes = ff_grads(after(pres, own), acts, normed, low)
    parts, ff_lower, in_lower, in_upper = tie(
        parts,
        shift(planes[1], -1),
        round_planes(grad_in[1], -1, own),
        round_planes(grad_in[2], 1, own),
    )
    adds_1 = add_in(grad_in[0], in_lower, in_upper, in_opposite)
    grad_middle, branch_rows, gain_0 = back_to_middle(parts, upstream, middle, gain_ff[0])
    *branch, ff_upper, adds_1 = plane_gather(
        branch_rows,
        round_planes(planes[2], 1, branch_rows),
        after(adds_1, branch_rows),
    )
    grad_qkv, strips_0, parts, halves_0 = attention_grads(record, branch)
    parts, output = tie(parts, relay_back(after(output, branch[1])))
    parts, own = plane_scatter(*parts)
    table_0 = table_grads(after(strips_0, own))
    grad_in = in_grads(
        place, *units, after(grad_qkv, own), gain_0, gain_1, table_0, table_1
    )
    parts, opposite_up, opposite_down, grad_in, output = tie(
        parts,
        round_planes(planes[3], 2, own),
        round_planes(planes[4], 2, own),
        grad_in,
        after(output, own).astype(f32),
    )
    upstream, low_rows = call(layer_back_kernel, units_shape, grad_middle, *parts, hidden)
    in_opposite = round_planes(grad_in[3], 2, low_rows)
    in_lower = round_planes(grad_in[1], -1, low_rows)
    in_upper = round_planes(grad_in[2], 1, low_rows)
    grad_tokens = relay_back(low_rows)
    halves_0 = owners_halves(after(halves_0, low_rows))
    grads_ff = [planes[0], ff_lower, ff_upper, opposite_up, opposite_down] + grads_ff
    grad_up, grad_down = call(finish_ff_kernel, [(ff_in.shape, f32)] * 2, *after(grads_ff, low_rows))
    own_out, other_out = call(
        add_out_kernel, [(attn_out.shape, f32), (attn_out.shape, bf16)], place, *halves_0, *halves_1, smem=1
    )
    (grad_attn_out,) = call(
        finish_out_kernel, [(attn_out.shape, f32)], own_out, toggle(other_out, "core", 1)
    )
    adds_0 = add_in(grad_in[0], in_lower, in_upper, in_opposite)
    near_in, far_in = (jnp.concatenate(pair, axis=1) for pair in zip(adds_0, adds_1))
    shares_in = share_chips(pair_chips(near_in, toggle(far_in, "core", 1), 1))
    own_buckets = table.shape[0] // (z_n * core_n)
    grad_attn_in, grad_gains, ends = call(
        functools.partial(finish_in_kernel, layer_count),
        [(attn_in.shape, f32), (gains.shape, f32), ((weight_rows, tile), f32)],
        place,
        *shares_in,
        attn_in,
        gain_attn,
        smem=1,
    )
    return (
        output[None],
        grad_tokens.astype(f32)[None],
        grad_attn_in,
        grad_attn_out,
        grad_up,
        grad_down,
        grad_gains,
        ends[:own_buckets, 8 : 8 + heads_all // heads_n],
    )


def solution(mesh):
    sizes = dict(mesh.shape)
    cores = 2
    fine = Mesh(
        mesh.devices.reshape(sizes["head"], sizes["blk"] // cores, cores), everyone
    )
    blk = ("z", "core")
    in_specs = (
        P("head", blk, None),
        P(None, blk),
        P(),
        P(None, everyone, None),
        P(None, everyone, None),
        P(None, everyone, None),
        P(None, everyone, None),
        P(None, everyone, None),
        P("head", blk, None),
    )
    out_specs = (
        P("head", blk, None),
        P("head", blk, None),
        P(None, everyone, None),
        P(None, everyone, None),
        P(None, everyone, None),
        P(None, everyone, None),
        P(None, everyone, None),
        P(blk, "head"),
    )
    plane = sizes["head"] == 4 and sizes["blk"] == 8
    local = local_plane if plane else local_general
    return jax.shard_map(local, mesh=fine, in_specs=in_specs, out_specs=out_specs, check_vma=False)
```

```python
import functools

import jax
import jax.numpy as jnp
import numpy as np
from jax import lax
from jax.experimental import pallas as pl
from jax.experimental.pallas import tpu as pltpu
from jax.sharding import Mesh
from jax.sharding import PartitionSpec as P

bounds = (1, 2, 3, 4, 5, 6, 7, 8, 12, 16, 23, 32, 46, 64, 91)
epsilon = 1e-06
masked = -1e30
score_scale = 0.125
head_dim = 64
tile = 128
everyone = ("head", "z", "core")
bf16 = jnp.bfloat16
f32 = jnp.float32


def contract(lhs, rhs, lhs_dim, rhs_dim):
    return lax.dot_general(
        lhs, rhs, (((lhs_dim,), (rhs_dim,)), ((), ())), preferred_element_type=f32
    )


def near_buckets(shape):
    offsets = (
        lax.broadcasted_iota(jnp.int32, shape, 1) - tile - lax.broadcasted_iota(jnp.int32, shape, 0)
    )
    distance = jnp.abs(offsets)
    bucket = jnp.where(offsets > 0, 16, 0)
    for boundary in bounds:
        bucket = bucket + jnp.where(distance >= boundary, 1, 0)
    return bucket


def near_kernel(table, near):
    bucket = near_buckets(near.shape[1:])
    for head in range(near.shape[0]):
        values = jnp.zeros(near.shape[1:], f32)
        for bucket_id in range(table.shape[0]):
            values = jnp.where(bucket == bucket_id, table[bucket_id, head], values)
        near[head] = values


def bucket_kernel(first_lane, near, far, out):
    bucket = near_buckets(near.shape[1:])
    rows = lax.broadcasted_iota(jnp.int32, out.shape, 0)
    lanes = lax.broadcasted_iota(jnp.int32, out.shape, 1)
    total = jnp.zeros(out.shape, f32)
    for head in range(near.shape[0]):
        strip = near[head]
        for bucket_id in range(out.shape[0]):
            value = jnp.sum(jnp.where(bucket == bucket_id, strip, 0.0), axis=0, keepdims=True)
            value = jnp.sum(value, axis=1, keepdims=True)
            if bucket_id in (15, 31):
                value = value + far[head, bucket_id // 16, :1, :1]
            total = jnp.where((rows == bucket_id) & (lanes == head + first_lane[0]), value, total)
    out[...] = total


def fill_band(band, table, near, heads_dev, length):
    for head in range(heads_dev):
        band[head, :, : length - tile] = jnp.full((tile, length - tile), table[15, head], f32)
        band[head, :, length - tile : length + 2 * tile] = near[head]
        band[head, :, length + 2 * tile :] = jnp.full(
            (tile, length - 2 * tile), table[31, head], f32
        )


def band_starts(place, at, length, skip=0):
    return [
        pl.multiple_of(length + (place[skip + block] - place[skip + at]) * tile, tile)
        for block in range(length // tile)
    ]


def attention_kernel(
    heads_dev, length, first, place, table, near, qkv, doc_row, doc_col, out, local, stats, band
):
    step = pl.program_id(0)
    width = heads_dev * head_dim

    @pl.when(step == 0)
    def _():
        fill_band(band, table, near, heads_dev, length)

    row = pl.multiple_of((first[0] + step) * tile, tile)
    out_row = pl.multiple_of((place[first[0] + step] - first[0]) * tile, tile)
    starts = band_starts(place, first[0] + step, length)
    same_doc = doc_col[...] == doc_row[...]
    queries = qkv[pl.ds(row, tile), :width] * bf16(score_scale)
    lanes = lax.broadcasted_iota(jnp.int32, (tile, tile), 1)
    collected = jnp.zeros((tile, tile), f32)
    for head in range(heads_dev):
        own = slice(head * head_dim, (head + 1) * head_dim)
        keys = qkv[:, width + own.start : width + own.stop]
        values = qkv[:, 2 * width + own.start : 2 * width + own.stop]
        scores = contract(queries[:, own], keys, 1, 1)
        scores = scores + jnp.concatenate(
            [band[head, :, pl.ds(start, tile)] for start in starts], axis=1
        )
        scores = jnp.where(same_doc, scores, masked)
        peak = jnp.max(scores, axis=1, keepdims=True)
        weights = jnp.exp(scores - peak)
        total = jnp.sum(weights, axis=1, keepdims=True)
        mixed = contract(weights.astype(bf16), values, 1, 0) / total
        out[pl.ds(out_row, tile), own] = mixed.astype(bf16)
        local[:, own] = mixed.astype(bf16)
        collected = jnp.where(lanes == head, peak + jnp.log(total), collected)
    stats[...] = collected


def attention_back_kernel(
    heads_dev, length, split, first, place, table, near, qkv, doc_row, doc_col, attended, grad_out, stats,
    grad_qkv, grad_near, grad_far, band, grad_band, grad_keys, grad_values,
):
    step = pl.program_id(0)
    width = heads_dev * head_dim

    @pl.when(step == 0)
    def _():
        fill_band(band, table, near, heads_dev, length)
        grad_band[...] = jnp.zeros_like(grad_band)
        grad_keys[...] = jnp.zeros_like(grad_keys)
        grad_values[...] = jnp.zeros_like(grad_values)
        if split > 1:
            grad_qkv[...] = jnp.zeros_like(grad_qkv)

    row = pl.multiple_of((first[0] + step) * tile, tile)
    out_row = pl.multiple_of((place[first[0] + step] - first[0]) * tile, tile)
    starts = band_starts(place, first[0] + step, length)
    same_doc = doc_col[...] == doc_row[...]
    at_step = pl.multiple_of(step * tile, tile)
    queries = qkv[pl.ds(row, tile), :width] * bf16(score_scale)
    for head in range(heads_dev):
        own = slice(head * head_dim, (head + 1) * head_dim)
        keys = qkv[:, width + own.start : width + own.stop]
        values = qkv[:, 2 * width + own.start : 2 * width + own.stop]
        upstream = grad_out[pl.ds(out_row, tile), own]
        scores = contract(queries[:, own], keys, 1, 1) + jnp.concatenate(
            [band[head, :, pl.ds(start, tile)] for start in starts], axis=1
        )
        scores = jnp.where(same_doc, scores, masked)
        weights = jnp.exp(scores - stats[:, head : head + 1])
        delta = jnp.sum(
            upstream.astype(f32) * attended[pl.ds(at_step, tile), own].astype(f32),
            axis=1,
            keepdims=True,
        )
        grad_scores = weights * (contract(upstream, values, 1, 1) - delta)
        for block, start in enumerate(starts):
            grad_band[head, :, pl.ds(start, tile)] += grad_scores[
                :, block * tile : (block + 1) * tile
            ]
        grad_low = grad_scores.astype(bf16)
        grad_values[:, own] += contract(weights.astype(bf16), upstream, 0, 0)
        grad_keys[:, own] += contract(grad_low, queries[:, own], 0, 0)
        grad_qkv[pl.ds(row, tile), own] = (
            contract(grad_low, keys, 1, 0) * score_scale
        ).astype(bf16)

    @pl.when(step == pl.num_programs(0) - 1)
    def _():
        grad_qkv[:, width : 2 * width] = grad_keys[...].astype(bf16)
        grad_qkv[:, 2 * width :] = grad_values[...].astype(bf16)
        for head in range(heads_dev):
            grad_near[head] = grad_band[head, :, length - tile : length + 2 * tile]
            grad_far[head, 0] = jnp.full(
                (8, tile), jnp.sum(grad_band[head, :, : length - tile]), f32
            )
            grad_far[head, 1] = jnp.full(
                (8, tile), jnp.sum(grad_band[head, :, length + 2 * tile :]), f32
            )


def whole(shape):
    return pl.BlockSpec(shape, lambda step: (0,) * len(shape), pipeline_mode=pl.Buffered(1))


def attention(qkv, doc_row, doc_col, first, place, table, near, rows):
    length = qkv.shape[0]
    heads_dev = table.shape[1]
    width = heads_dev * head_dim
    return pl.pallas_call(
        functools.partial(attention_kernel, heads_dev, length),
        grid=(rows // tile,),
        in_specs=[
            pl.BlockSpec(memory_space=pltpu.SMEM),
            pl.BlockSpec(memory_space=pltpu.SMEM),
            pl.BlockSpec(memory_space=pltpu.SMEM),
            whole(near.shape),
            whole(qkv.shape),
            whole(doc_row.shape),
            pl.BlockSpec((tile, 1), lambda step: (step, 0)),
        ],
        out_specs=[
            whole((rows, width)),
            pl.BlockSpec((tile, width), lambda step: (step, 0)),
            pl.BlockSpec((tile, tile), lambda step: (step, 0)),
        ],
        out_shape=[
            jax.ShapeDtypeStruct((rows, width), bf16),
            jax.ShapeDtypeStruct((rows, width), bf16),
            jax.ShapeDtypeStruct((rows, tile), f32),
        ],
        scratch_shapes=[pltpu.VMEM((heads_dev, tile, 2 * length), f32)],
        compiler_params=pltpu.CompilerParams(vmem_limit_bytes=40 * 2**20),
        cost_estimate=pl.CostEstimate(
            flops=4 * rows * length * width,
            bytes_accessed=4 * length * width * 2,
            transcendentals=rows * length * heads_dev,
        ),
    )(first, place, table, near, qkv, doc_row, doc_col)


def attention_back(
    qkv, doc_row, doc_col, attended, grad_out, stats, first, place, table, near, split
):
    length = qkv.shape[0]
    rows = grad_out.shape[0]
    heads_dev = table.shape[1]
    width = heads_dev * head_dim
    return pl.pallas_call(
        functools.partial(attention_back_kernel, heads_dev, length, split),
        grid=(rows // tile,),
        in_specs=[
            pl.BlockSpec(memory_space=pltpu.SMEM),
            pl.BlockSpec(memory_space=pltpu.SMEM),
            pl.BlockSpec(memory_space=pltpu.SMEM),
            whole(near.shape),
            whole(qkv.shape),
            whole(doc_row.shape),
            pl.BlockSpec((tile, 1), lambda step: (step, 0)),
            whole((rows, width)),
            whole((rows, width)),
            pl.BlockSpec((tile, tile), lambda step: (step, 0)),
        ],
        out_specs=[
            whole((length, 3 * width)),
            whole((heads_dev, tile, 3 * tile)),
            whole((heads_dev, 2, 8, tile)),
        ],
        out_shape=[
            jax.ShapeDtypeStruct((length, 3 * width), bf16),
            jax.ShapeDtypeStruct((heads_dev, tile, 3 * tile), f32),
            jax.ShapeDtypeStruct((heads_dev, 2, 8, tile), f32),
        ],
        scratch_shapes=[
            pltpu.VMEM((heads_dev, tile, 2 * length), f32),
            pltpu.VMEM((heads_dev, tile, 2 * length), f32),
            pltpu.VMEM((length, width), f32),
            pltpu.VMEM((length, width), f32),
        ],
        compiler_params=pltpu.CompilerParams(vmem_limit_bytes=48 * 2**20),
        cost_estimate=pl.CostEstimate(
            flops=10 * rows * length * width,
            bytes_accessed=8 * length * width * 2,
            transcendentals=rows * length * heads_dev,
        ),
    )(first, place, table, near, qkv, doc_row, doc_col, attended, grad_out, stats)


def call(kernel, shapes, *operands, smem=0):
    return pl.pallas_call(
        kernel,
        in_specs=[pl.BlockSpec(memory_space=pltpu.SMEM)] * smem
        + [pl.BlockSpec(memory_space=pltpu.VMEM)] * (len(operands) - smem),
        out_specs=[pl.BlockSpec(memory_space=pltpu.VMEM)] * len(shapes),
        out_shape=[jax.ShapeDtypeStruct(shape, kind) for shape, kind in shapes],
        compiler_params=pltpu.CompilerParams(vmem_limit_bytes=10 * 2**20),
    )(*operands)


def share_in_kernel(place, attn_in, gains, near, far):
    layers, rows = attn_in.shape[:2]
    half = near.shape[0] // (layers * rows)
    width = near.shape[1] // 3
    for index in range(2 * half):
        member = place[index]
        for layer_id in range(layers):
            block = jnp.concatenate(
                [
                    attn_in[
                        layer_id,
                        :,
                        pl.ds(pl.multiple_of((part * 2 * half + member) * width, width), width),
                    ]
                    for part in range(3)
                ],
                axis=1,
            )
            at = (index % half * layers + layer_id) * rows
            out = near if index < half else far
            out[at : at + rows] = (block.astype(f32) * gains[layer_id]).astype(bf16)


def join_kernel(*refs):
    shares, outs = refs[:4], refs[4:]
    rows = outs[0].shape[0] // 8
    for chip, share in enumerate(shares):
        for core in range(2):
            for layer_id, out in enumerate(outs):
                source = (core * len(outs) + layer_id) * rows
                target = (chip * 2 + core) * rows
                out[target : target + rows] = share[source : source + rows]


def row_of(chip, plane, core, rows, planes=4):
    return pl.multiple_of(((chip * planes + plane) * 2 + core) * rows, rows)


def plane_attention_kernel(
    length, place, table, strip, near, far, *refs
):
    shares, halves, (doc_row, doc_col, w_in, w_out), (qkv, attended, stats, near_part, far_part) = (
        refs[:4], refs[4:6], refs[6:10], refs[10:15],
    )
    band, done = refs[15:]
    step = pl.program_id(0)
    half = length // 2
    heads_dev = table.shape[1]
    width = heads_dev * head_dim

    @pl.when(step == 0)
    def _():
        at_z, at_core, at_head = place[length // tile], place[0] % 2, place[0] // 2
        rows = shares[0].shape[0] // 8
        copies = []
        for share, offset in zip(shares, (0, 3, 1, 2)):
            for index in range(8):
                row = row_of(
                    at_head ^ (index // 2), (at_z + offset) % 4, at_core ^ (index % 2), rows
                )
                copies.append(
                    pltpu.make_async_copy(
                        share.at[index * rows : (index + 1) * rows],
                        w_in.at[pl.ds(row, rows)],
                        done.at[len(copies)],
                    )
                )
        for index, part in enumerate(halves):
            row = pl.multiple_of((index ^ at_z % 2) * part.shape[0], part.shape[0])
            copies.append(
                pltpu.make_async_copy(
                    part, w_out.at[pl.ds(row, part.shape[0])], done.at[len(copies)]
                )
            )
        for copy in copies:
            copy.start()
        fill_band(band, table, strip, heads_dev, length)
        for copy in copies:
            copy.wait()
        qkv[:half] = contract(near[...], w_in[...], 1, 0).astype(bf16)
        qkv[half:] = contract(far[...], w_in[...], 1, 0).astype(bf16)

    row = pl.multiple_of(step * half, half)
    queries = qkv[pl.ds(row, half), :width] * bf16(score_scale)
    lanes = lax.broadcasted_iota(jnp.int32, (tile, tile), 1)
    blocks = half // tile
    collected = [jnp.zeros((tile, tile), f32)] * blocks
    results = []
    for head in range(heads_dev):
        own = slice(head * head_dim, (head + 1) * head_dim)
        keys = qkv[:, width + own.start : width + own.stop]
        values = qkv[:, 2 * width + own.start : 2 * width + own.stop]
        raw_scores = contract(queries[:, own], keys, 1, 1)
        weights, totals = [], []
        for block in range(blocks):
            lines = slice(block * tile, (block + 1) * tile)
            starts = band_starts(place, step * blocks + block, length, length // tile + 1)
            scores = raw_scores[lines] + jnp.concatenate(
                [band[head, :, pl.ds(start, tile)] for start in starts], axis=1
            )
            scores = jnp.where(doc_col[lines] == doc_row[...], scores, masked)
            peak = jnp.max(scores, axis=1, keepdims=True)
            exp_scores = jnp.exp(scores - peak)
            total = jnp.sum(exp_scores, axis=1, keepdims=True)
            weights.append(exp_scores.astype(bf16))
            totals.append(total)
            collected[block] = jnp.where(lanes == head, peak + jnp.log(total), collected[block])
        mixed = contract(jnp.concatenate(weights), values, 1, 0) / jnp.concatenate(totals)
        results.append(mixed.astype(bf16))
    stats[...] = jnp.concatenate(collected)
    merged = jnp.concatenate(results, axis=1)
    attended[...] = merged
    part = contract(merged, w_out[...], 1, 0)

    @pl.when(step == 0)
    def _():
        near_part[...] = part

    @pl.when(step == 1)
    def _():
        far_part[...] = part.astype(bf16)


def plane_attention(near, far, shares, halves, doc_row, doc_col, place, table, strip):
    length, model_width = 2 * near.shape[0], near.shape[1]
    half = length // 2
    heads_dev = table.shape[1]
    width = heads_dev * head_dim
    return pl.pallas_call(
        functools.partial(plane_attention_kernel, length),
        grid=(2,),
        in_specs=[
            pl.BlockSpec(memory_space=pltpu.SMEM),
            pl.BlockSpec(memory_space=pltpu.SMEM),
            whole(strip.shape),
            whole(near.shape),
            whole(far.shape),
            *[pl.BlockSpec(memory_space=pl.ANY)] * 6,
            whole(doc_row.shape),
            pl.BlockSpec((half, 1), lambda step: (step, 0)),
        ],
        out_specs=[
            whole((model_width, 3 * width)),
            whole((width, model_width)),
            whole((length, 3 * width)),
            pl.BlockSpec((half, width), lambda step: (step, 0)),
            pl.BlockSpec((half, tile), lambda step: (step, 0)),
            whole((half, model_width)),
            whole((half, model_width)),
        ],
        out_shape=[
            jax.ShapeDtypeStruct((model_width, 3 * width), bf16),
            jax.ShapeDtypeStruct((width, model_width), bf16),
            jax.ShapeDtypeStruct((length, 3 * width), bf16),
            jax.ShapeDtypeStruct((length, width), bf16),
            jax.ShapeDtypeStruct((length, tile), f32),
            jax.ShapeDtypeStruct((length // 2, model_width), f32),
            jax.ShapeDtypeStruct((length // 2, model_width), bf16),
        ],
        scratch_shapes=[
            pltpu.VMEM((heads_dev, tile, 2 * length), f32),
            pltpu.SemaphoreType.DMA((34,)),
        ],
        compiler_params=pltpu.CompilerParams(vmem_limit_bytes=24 * 2**20),
        cost_estimate=pl.CostEstimate(
            flops=4 * length * length * width + 8 * length * model_width * width,
            bytes_accessed=12 * 2**20,
            transcendentals=length * length * heads_dev,
        ),
    )(place, table, strip, near, far, *shares, *halves, doc_row, doc_col)


def plane_attention_back_kernel(
    length, place, table, strip, qkv, doc_row, doc_col, attended, stats, near, far, w_in, w_out,
    grad_qkv, grad_near, grad_far, near_part, far_part, *rest
):
    halves, (band, grad_band, grad_keys, grad_values, out_sum) = rest[:2], rest[2:]
    step = pl.program_id(0)
    half = length // 2
    heads_dev = table.shape[1]
    width = heads_dev * head_dim

    @pl.when(step == 0)
    def _():
        fill_band(band, table, strip, heads_dev, length)
        grad_band[...] = jnp.zeros_like(grad_band)
        grad_keys[...] = jnp.zeros_like(grad_keys)
        grad_values[...] = jnp.zeros_like(grad_values)
        out_sum[...] = jnp.zeros_like(out_sum)

    row = pl.multiple_of(step * half, half)
    branch = jnp.where(step == 0, near[...], far[...])
    merged = attended[...]
    grad_merged = contract(branch, w_out[...], 1, 1).astype(bf16)
    out_sum[...] += contract(merged, branch, 0, 0)
    products = grad_merged.astype(f32) * merged.astype(f32)
    queries = qkv[pl.ds(row, half), :width] * bf16(score_scale)
    blocks = half // tile
    for head in range(heads_dev):
        own = slice(head * head_dim, (head + 1) * head_dim)
        keys = qkv[:, width + own.start : width + own.stop]
        values = qkv[:, 2 * width + own.start : 2 * width + own.stop]
        upstream = grad_merged[:, own]
        raw_scores = contract(queries[:, own], keys, 1, 1)
        grad_weights = contract(upstream, values, 1, 1)
        delta = jnp.sum(products[:, own], axis=1, keepdims=True)
        weights_low, grads_low = [], []
        for block in range(blocks):
            lines = slice(block * tile, (block + 1) * tile)
            starts = band_starts(place, step * blocks + block, length, length // tile + 1)
            scores = raw_scores[lines] + jnp.concatenate(
                [band[head, :, pl.ds(start, tile)] for start in starts], axis=1
            )
            scores = jnp.where(doc_col[lines] == doc_row[...], scores, masked)
            weights = jnp.exp(scores - stats[lines, head : head + 1])
            grad_scores = weights * (grad_weights[lines] - delta[lines])
            for index, start in enumerate(starts):
                grad_band[head, :, pl.ds(start, tile)] += grad_scores[
                    :, index * tile : (index + 1) * tile
                ]
            weights_low.append(weights.astype(bf16))
            grads_low.append(grad_scores.astype(bf16))
        weights_low, grads_low = jnp.concatenate(weights_low), jnp.concatenate(grads_low)
        grad_values[:, own] += contract(weights_low, upstream, 0, 0)
        grad_keys[:, own] += contract(grads_low, queries[:, own], 0, 0)
        grad_qkv[pl.ds(row, half), own] = (
            contract(grads_low, keys, 1, 0) * score_scale
        ).astype(bf16)

    @pl.when(step == pl.num_programs(0) - 1)
    def _():
        grad_qkv[:, width : 2 * width] = grad_keys[...].astype(bf16)
        grad_qkv[:, 2 * width :] = grad_values[...].astype(bf16)
        far_part[...] = contract(grad_qkv[half:], w_in[...], 1, 1).astype(bf16)
        near_part[...] = contract(grad_qkv[:half], w_in[...], 1, 1)
        rows = width // 2
        for index, part in enumerate(halves):
            block = index ^ place[length // tile] % 2
            part[...] = out_sum[pl.ds(pl.multiple_of(block * rows, rows), rows)].astype(bf16)
        for head in range(heads_dev):
            grad_near[head] = grad_band[head, :, length - tile : length + 2 * tile]
            grad_far[head, 0] = jnp.full(
                (8, tile), jnp.sum(grad_band[head, :, : length - tile]), f32
            )
            grad_far[head, 1] = jnp.full(
                (8, tile), jnp.sum(grad_band[head, :, length + 2 * tile :]), f32
            )


def plane_attention_back(
    qkv, doc_row, doc_col, attended, stats, near, far, w_in, w_out, place, table, strip
):
    length, model_width = 2 * near.shape[0], near.shape[1]
    half = length // 2
    heads_dev = table.shape[1]
    width = heads_dev * head_dim
    shapes = [
        ((length, 3 * width), bf16),
        ((heads_dev, tile, 3 * tile), f32),
        ((heads_dev, 2, 8, tile), f32),
        ((length // 2, model_width), f32),
        ((length // 2, model_width), bf16),
    ] + [((width // 2, model_width), bf16)] * 2
    return pl.pallas_call(
        functools.partial(plane_attention_back_kernel, length),
        grid=(2,),
        in_specs=[
            pl.BlockSpec(memory_space=pltpu.SMEM),
            pl.BlockSpec(memory_space=pltpu.SMEM),
            whole(strip.shape),
            whole(qkv.shape),
            whole(doc_row.shape),
            pl.BlockSpec((half, 1), lambda step: (step, 0)),
            pl.BlockSpec((half, width), lambda step: (step, 0)),
            pl.BlockSpec((half, tile), lambda step: (step, 0)),
            whole((half, model_width)),
            whole((half, model_width)),
            whole(w_in.shape),
            whole(w_out.shape),
        ],
        out_specs=[whole(shape) for shape, _ in shapes],
        out_shape=[jax.ShapeDtypeStruct(shape, kind) for shape, kind in shapes],
        scratch_shapes=[
            pltpu.VMEM((heads_dev, tile, 2 * length), f32),
            pltpu.VMEM((heads_dev, tile, 2 * length), f32),
            pltpu.VMEM((length, width), f32),
            pltpu.VMEM((length, width), f32),
            pltpu.VMEM((width, model_width), f32),
        ],
        compiler_params=pltpu.CompilerParams(vmem_limit_bytes=32 * 2**20),
        cost_estimate=pl.CostEstimate(
            flops=10 * length * length * width + 10 * length * model_width * width,
            bytes_accessed=12 * 2**20,
            transcendentals=length * length * heads_dev,
        ),
    )(place, table, strip, qkv, doc_row, doc_col, attended, stats, near, far, w_in, w_out)


def gelu_and_slope(pre_act):
    size = jnp.abs(pre_act)
    gauss = jnp.exp(-0.5 * pre_act * pre_act)
    ratio = 1.0 / (1.0 + np.float32(0.3275911 * 0.5**0.5) * size)
    series = np.float32(1.061405429)
    for factor in (-1.453152027, 1.421413741, -0.284496736, 0.254829592):
        series = series * ratio + np.float32(factor)
    tail = 0.5 * series * ratio * gauss
    cumulative = jnp.where(pre_act < 0, tail, 1.0 - tail)
    slope = cumulative + pre_act * gauss * np.float32((2 * np.pi) ** -0.5)
    return pre_act * cumulative, slope


def ff_kernel(rows, pair, activated, slope, part):
    columns = rows.shape[1]
    value, gradient = gelu_and_slope(contract(rows[...], pair[:, :columns], 1, 1))
    activated[...] = value.astype(bf16)
    slope[...] = gradient.astype(bf16)
    part[...] = contract(activated[...], pair[:, columns:], 1, 0).astype(part.dtype)


def ff_first_kernel(rows, *refs):
    parts, (activated, slope, part, pair) = refs[:5], refs[5:]

    @pl.when(pl.program_id(0) == 0)
    def _():
        units, columns = parts[0].shape[0], rows.shape[1]
        for index, ref in enumerate(parts[:3]):
            pair[index * units : (index + 1) * units] = ref[...]
        pair[3 * units :, :columns] = parts[3][...]
        pair[3 * units :, columns:] = parts[4][...]

    ff_kernel(rows, pair, activated, slope, part)


def ff_back_kernel(rows, slope, pair, grad_pre, part):
    columns = rows.shape[1]
    grad_act = contract(rows[...], pair[:, columns:], 1, 1)
    grad_pre[...] = (grad_act * slope[...].astype(f32)).astype(bf16)
    part[...] = contract(grad_pre[...], pair[:, :columns], 1, 0).astype(part.dtype)


def by_rows(kernel, step_rows, row_operands, whole_operands, outs, whole_outs=()):
    rows = row_operands[0].shape[0]
    return pl.pallas_call(
        kernel,
        grid=(rows // step_rows,),
        in_specs=[
            pl.BlockSpec((step_rows, operand.shape[1]), lambda step: (step, 0))
            for operand in row_operands
        ]
        + [whole(operand.shape) for operand in whole_operands],
        out_specs=[pl.BlockSpec((step_rows, columns), lambda step: (step, 0)) for columns, _ in outs]
        + [whole(shape) for shape in whole_outs],
        out_shape=[jax.ShapeDtypeStruct((rows, columns), kind) for columns, kind in outs]
        + [jax.ShapeDtypeStruct(shape, bf16) for shape in whole_outs],
        compiler_params=pltpu.CompilerParams(vmem_limit_bytes=10 * 2**20),
        cost_estimate=pl.CostEstimate(
            flops=4 * rows * outs[0][0] * row_operands[0].shape[1],
            bytes_accessed=6 * 2**20,
            transcendentals=0,
        ),
    )(*row_operands, *whole_operands)


def ff_grads_kernel(
    pre_near, pre_far, act_near, act_far, normed_near, normed_far, low_near, low_far, *outs
):
    columns = normed_near.shape[1]
    units = outs[0].shape[0]
    up = (
        contract(pre_near[...], normed_near[...], 0, 0)
        + contract(pre_far[...], normed_far[...], 0, 0)
    ).astype(bf16)
    down = (
        contract(act_near[...], low_near[...], 0, 0) + contract(act_far[...], low_far[...], 0, 0)
    ).astype(bf16)

    @pl.when(pl.program_id(0) == 0)
    def _():
        for index in range(2):
            block = slice(index * units, (index + 1) * units)
            outs[index][:, :columns] = up[block]
            outs[index][:, columns:] = down[block]

    @pl.when(pl.program_id(0) == 1)
    def _():
        outs[2][:, :columns] = up[:units]
        outs[2][:, columns:] = down[:units]
        outs[3][...] = up[units:]
        outs[4][...] = down[units:]


def ff_grads(pre, act, normed, low):
    rows, hidden_units = pre[0].shape
    columns = normed[0].shape[1]
    shapes = [(hidden_units // 4, 2 * columns)] * 3 + [(hidden_units // 4, columns)] * 2
    return pl.pallas_call(
        ff_grads_kernel,
        grid=(2,),
        in_specs=[pl.BlockSpec((rows, hidden_units // 2), lambda step: (0, step))] * 4
        + [whole((rows, columns))] * 4,
        out_specs=[whole(shape) for shape in shapes],
        out_shape=[jax.ShapeDtypeStruct(shape, bf16) for shape in shapes],
        compiler_params=pltpu.CompilerParams(vmem_limit_bytes=14 * 2**20),
        cost_estimate=pl.CostEstimate(
            flops=8 * rows * hidden_units * columns, bytes_accessed=8 * 2**20, transcendentals=0
        ),
    )(*pre, *act, *normed, *low)


def in_grads_kernel(place, near, far, grad_qkv, *refs):
    ends, outs, (total, extra) = refs[:-6], refs[-6:-2], refs[-2:]
    half = near.shape[0]
    columns = grad_qkv.shape[1]
    total[:, :columns] = (
        contract(near[...], grad_qkv[:half], 0, 0) + contract(far[...], grad_qkv[half:], 0, 0)
    ).astype(bf16)
    rows = outs[0].shape[0] // 8
    if ends:
        gain_0, gain_1, table_0, table_1 = ends
        lines = lax.broadcasted_iota(jnp.int32, (tile, gain_0.shape[1]), 0)
        gains = jnp.where(lines == 0, gain_0[...], jnp.where(lines == 1, gain_1[...], 0.0))
        extra[...] = jnp.transpose(gains)
        table = table_0[...] + table_1[...]
        buckets = table.shape[0] // 8
        blank = jnp.zeros((8 - buckets, tile), f32)
        for block in range(8):
            row = pl.multiple_of((place[0] // 2 * 8 + block) * rows, rows)
            extra[pl.ds(row, 8)] += jnp.concatenate(
                [table[block * buckets : (block + 1) * buckets], blank]
            )
        total[:, columns:] = extra[...].astype(bf16)
    for out, offset in zip(outs, (0, 3, 1, 2)):
        plane = (place[8] + offset) % 4
        for index in range(8):
            owner = place[index]
            row = row_of(owner // 2, plane, owner % 2, rows)
            out[index * rows : (index + 1) * rows] = total[pl.ds(row, rows)]


def in_grads(place, near, far, grad_qkv, *ends):
    columns = grad_qkv.shape[1] + (tile if ends else 0)
    shape = (near.shape[1] // 4, columns)
    return pl.pallas_call(
        in_grads_kernel,
        in_specs=[pl.BlockSpec(memory_space=pltpu.SMEM)]
        + [pl.BlockSpec(memory_space=pltpu.VMEM)] * (3 + len(ends)),
        out_specs=[pl.BlockSpec(memory_space=pltpu.VMEM)] * 4,
        out_shape=[jax.ShapeDtypeStruct(shape, bf16)] * 4,
        scratch_shapes=[
            pltpu.VMEM((near.shape[1], columns), bf16),
            pltpu.VMEM((near.shape[1], tile), f32),
        ],
        compiler_params=pltpu.CompilerParams(vmem_limit_bytes=12 * 2**20),
        cost_estimate=pl.CostEstimate(
            flops=4 * near.shape[0] * near.shape[1] * columns,
            bytes_accessed=4 * 2**20,
            transcendentals=0,
        ),
    )(place, near, far, grad_qkv, *ends)


def add_in_kernel(own, lower, upper, opposite, near, far):
    total = sum_of_four([own, lower, upper, opposite]).astype(bf16)
    half = near.shape[0]
    near[...] = total[:half]
    far[...] = total[half:]


def combine_kernel(near_part, arrived, own, x_part, y_part, xy_part):
    rows = own.shape[0]
    own[...] = near_part[:rows] + arrived[:rows].astype(f32)
    for bits, out in ((1, x_part), (2, y_part), (3, xy_part)):
        block = slice(bits * rows, (bits + 1) * rows)
        out[...] = (near_part[block] + arrived[block].astype(f32)).astype(bf16)


def added(own, x_part, y_part, xy_part):
    return (own[...] + x_part[...].astype(f32)) + (
        y_part[...].astype(f32) + xy_part[...].astype(f32)
    )


def close_kernel(kept, own, x_part, y_part, xy_part, hidden, units):
    total = kept[...] + added(own, x_part, y_part, xy_part)
    hidden[...] = total
    units[...] = (total * inverse_rms(total)).astype(bf16)


def close_gain_kernel(kept, own, x_part, y_part, xy_part, gain, hidden, normed):
    total = kept[...] + added(own, x_part, y_part, xy_part)
    hidden[...] = total
    normed[...] = (total * inverse_rms(total) * gain[...]).astype(bf16)


def last_kernel(kept, own, x_part, y_part, xy_part, hidden):
    hidden[...] = (kept[...] + added(own, x_part, y_part, xy_part)).astype(bf16)


def middle_back_kernel(
    upstream, own, x_part, y_part, xy_part, middle, gain, grad_middle, branch, grad_gain
):
    grad_normed = added(own, x_part, y_part, xy_part)
    inverse = inverse_rms(middle[...])
    grad_gain[...] = jnp.sum(grad_normed * middle[...] * inverse, axis=0, keepdims=True)
    total = upstream[...].astype(f32) + unit_norm_back(
        middle[...], inverse, grad_normed * gain[...]
    )
    grad_middle[...] = total
    branch[...] = total.astype(bf16)


def layer_back_kernel(grad_middle, own, x_part, y_part, xy_part, hidden, upstream, low):
    total = grad_middle[...] + unit_norm_back(
        hidden[...], inverse_rms(hidden[...]), added(own, x_part, y_part, xy_part)
    )
    upstream[...] = total
    low[...] = total.astype(bf16)


def pair_kernel(axis, near, arrived, *outs):
    rows = near.shape[0] // len(outs)
    for index, out in enumerate(outs):
        block = slice(index * rows, (index + 1) * rows)
        if axis == 0:
            out[:rows] = near[block]
            out[rows:] = arrived[block]
        else:
            columns = near.shape[1]
            out[:, :columns] = near[block]
            out[:, columns:] = arrived[block]


def unit_kernel(tokens, hidden, units):
    total = tokens[...].astype(f32)
    hidden[...] = total
    units[...] = (total * inverse_rms(total)).astype(bf16)


def finish_in_kernel(layers, place, *refs):
    shares, (attn_in, gains, grad_in, grad_gain, ends) = refs[:4], refs[4:]
    rows = attn_in.shape[1]
    width = shares[0].shape[1] // 14
    members = attn_in.shape[2] // (3 * width)
    for layer_id in range(layers):
        row_dot = jnp.zeros((rows, 1), f32)
        for index in range(members):
            share = shares[index % 4]
            first = (index // 4 * 7 + layer_id * 4) * width
            member = place[index]
            for part in range(3):
                block = share[:, first + part * width : first + (part + 1) * width].astype(f32)
                columns = pl.ds(pl.multiple_of((part * members + member) * width, width), width)
                grad_in[layer_id, :, columns] = block * gains[layer_id]
                row_dot = row_dot + jnp.sum(
                    block * attn_in[layer_id, :, columns].astype(f32), axis=1, keepdims=True
                )
            if layer_id == 0:
                block = share[:, first + 3 * width : first + 4 * width].astype(f32)
                ends[...] = block if index == 0 else ends[...] + block
        grad_gain[layer_id] = jnp.concatenate(
            [row_dot, ends[:, layer_id : layer_id + 1]], axis=1
        )


def sum_of_four(parts):
    return (parts[0][...].astype(f32) + parts[1][...].astype(f32)) + (
        parts[2][...].astype(f32) + parts[3][...].astype(f32)
    )


def finish_ff_kernel(*refs):
    count = (len(refs) - 3) // 2
    sources, grads, held, done = refs[:count], refs[count : count + 2], refs[count + 2 : -1], refs[-1]
    copies = [
        pltpu.make_async_copy(source, target, done.at[index])
        for index, (source, target) in enumerate(zip(sources, held))
    ]
    for copy in copies:
        copy.start()
    for copy in copies:
        copy.wait()
    refs = held
    columns = grads[0].shape[2]
    for layer_id in range(grads[0].shape[0]):
        parts = refs[5 * layer_id : 5 * layer_id + 5]
        for side, out in enumerate(grads):
            halves = [part.at[:, side * columns : (side + 1) * columns] for part in parts[:3]]
            out[layer_id] = sum_of_four(halves + [parts[3 + side]])


def finish_ff(grads, shape):
    return pl.pallas_call(
        finish_ff_kernel,
        in_specs=[pl.BlockSpec(memory_space=pl.ANY)] * len(grads),
        out_specs=[pl.BlockSpec(memory_space=pltpu.VMEM)] * 2,
        out_shape=[jax.ShapeDtypeStruct(shape, f32)] * 2,
        scratch_shapes=[pltpu.VMEM(grad.shape, bf16) for grad in grads]
        + [pltpu.SemaphoreType.DMA((len(grads),))],
        compiler_params=pltpu.CompilerParams(vmem_limit_bytes=14 * 2**20),
    )(*grads)


def add_out_kernel(place, *refs):
    parts, (own, other) = refs[:-2], refs[-2:]
    for layer_id in range(own.shape[0]):
        total = parts[2 * layer_id][...].astype(f32) + parts[2 * layer_id + 1][...].astype(f32)
        rows = total.shape[0] // 2
        second = place[0] % 2 == 1
        own[layer_id] = jnp.where(second, total[rows:], total[:rows])
        other[layer_id] = jnp.where(second, total[:rows], total[rows:]).astype(bf16)


def finish_out_kernel(own, arrived, out):
    out[...] = own[...] + arrived[...].astype(f32)


def inverse_rms(hidden):
    return lax.rsqrt(jnp.mean(hidden * hidden, axis=-1, keepdims=True) + epsilon)


def prepare(bias_table, first_head, heads_dev):
    table = lax.dynamic_slice_in_dim(bias_table, first_head, heads_dev, 1)
    (near,) = call(near_kernel, [((heads_dev, tile, 3 * tile), f32)], table, smem=1)
    return table, near


def bucket_grads(first_lane, grads, bucket_count):
    (total,) = call(bucket_kernel, [((bucket_count, tile), f32)], first_lane, *grads, smem=1)
    return total


def gelu_parts(pre_act):
    cumulative = 0.5 * (1.0 + lax.erf(pre_act * np.float32(0.5**0.5)))
    slope = cumulative + pre_act * jnp.exp(-0.5 * pre_act * pre_act) * np.float32(
        (2 * np.pi) ** -0.5
    )
    return (pre_act * cumulative).astype(bf16), slope


def unit_norm_back(hidden, inverse, grad_unit):
    unit = hidden * inverse
    return inverse * (grad_unit - unit * jnp.mean(grad_unit * unit, axis=-1, keepdims=True))


def gather_rows(block, axes):
    return lax.all_gather(block, axes, axis=0, tiled=True)


def toggle(array, axis, bits):
    return lax.ppermute(array, axis, [(i, i ^ bits) for i in range(lax.axis_size(axis))])


def shift(array, by):
    planes = lax.axis_size("z")
    return lax.ppermute(array, "z", [(i, (i + by) % planes) for i in range(planes)])


def plane_gather(block, *holds):
    near = jnp.concatenate([block] + [toggle(block, "head", bits) for bits in (1, 2, 3)])
    near, *holds = tie(near, *holds)
    return (near, toggle(near, "core", 1), *holds)


def plane_scatter(near_part, far_part):
    rows, columns = near_part.shape[0] // 4, near_part.shape[1]
    own, *others = call(
        combine_kernel,
        [((rows, columns), f32)] + [((rows, columns), bf16)] * 3,
        near_part,
        toggle(far_part, "core", 1),
    )
    shares = [own] + [toggle(other, "head", bits) for bits, other in zip((1, 2, 3), others)]
    return shares, own


def tie(*arrays):
    return lax.optimization_barrier(arrays)


def after(array, other):
    return lax.optimization_barrier((array, other))[0]


def scatter_sum(partial, axes, members):
    blocks = partial.astype(bf16).reshape(members, -1, partial.shape[1])
    return jnp.sum(lax.all_to_all(blocks, axes, 0, 0, tiled=True).astype(f32), axis=0)


def local_general(tokens, doc_start, bias_table, attn_in, attn_out, ff_in, ff_out, gains, cotangent):
    heads_n, z_n, core_n = (lax.axis_size(axis) for axis in everyone)
    devices = heads_n * z_n * core_n
    group, spare = ("z", "core"), "head"
    ff_group, ff_spare, ff_members = ("head", "core"), "z", heads_n * core_n
    blocks = z_n * core_n
    block_rows, model_width = tokens.shape[1:]
    layer_count, weight_rows = attn_in.shape[:2]
    length = block_rows * blocks
    heads_all = bias_table.shape[1]
    member = lax.axis_index("z") * core_n + lax.axis_index("core")
    heads_dev = max(1, heads_all // blocks)
    head_groups = heads_all // heads_dev
    split = blocks // head_groups
    head_group, query_part = member // split, member % split
    query_rows = length // split
    width = heads_dev * head_dim
    first = (query_part * (query_rows // tile)).astype(jnp.int32).reshape(1)
    place = jnp.arange(length // tile, dtype=jnp.int32)
    out_row = head_group * width

    def swap(array):
        return lax.all_to_all(array, everyone, 0, 0, tiled=True)

    starts = jnp.broadcast_to(
        doc_start.astype(f32)[:, None], (heads_n, blocks, block_rows)
    ).reshape(devices, block_rows)
    ff_gains = gains[:, :, 1].astype(f32).reshape(1, -1)
    small = swap(
        jnp.concatenate(
            [starts, jnp.broadcast_to(ff_gains, (devices, layer_count * weight_rows))], axis=1
        )
    )
    doc_row = small[:blocks, :block_rows].reshape(1, length)
    doc_col = lax.dynamic_slice_in_dim(
        doc_row.reshape(length, 1), query_part * query_rows, query_rows, 0
    )
    gain_ff = jnp.transpose(
        small[:, block_rows:].reshape(devices, layer_count, weight_rows), (1, 0, 2)
    ).reshape(layer_count, 1, model_width)
    table, near = prepare(bias_table, head_group * heads_dev, heads_dev)

    gain_attn = gains[:, :, 0].astype(f32)[:, :, None]
    own_in = attn_in.astype(f32)

    def fetch_in(layer_id):
        scaled = (own_in[layer_id] * gain_attn[layer_id]).astype(bf16)
        columns = jnp.transpose(
            scaled.reshape(weight_rows, 3, head_groups, width), (2, 0, 1, 3)
        ).reshape(head_groups, weight_rows, 3 * width)
        columns = jnp.repeat(columns, split, axis=0)
        columns = jnp.broadcast_to(columns[None], (heads_n, *columns.shape))
        return swap(columns.reshape(devices, weight_rows, 3 * width)).reshape(
            model_width, 3 * width
        )

    def fetch_ff(layer_id):
        pair = jnp.concatenate([ff_in[layer_id], ff_out[layer_id]], axis=1)
        pair = gather_rows(pair, ff_spare)
        return pair[:, :model_width], pair[:, model_width:]

    hidden, upstream = tokens[0].astype(f32), cotangent[0]
    weights_in = [fetch_in(layer_id) for layer_id in range(layer_count)]
    weights_out = lax.dynamic_slice_in_dim(
        lax.all_gather(attn_out, everyone, axis=1, tiled=True), out_row, width, 1
    )
    weights_ff = [fetch_ff(layer_id) for layer_id in range(layer_count)]

    records = []
    for layer_id in range(layer_count):
        w_in, w_out, (w_up, w_down) = (
            weights_in[layer_id], weights_out[layer_id], weights_ff[layer_id],
        )
        inverse = inverse_rms(hidden)
        units = gather_rows((hidden * inverse).astype(bf16), group)
        qkv = jnp.dot(units, w_in, preferred_element_type=f32).astype(bf16)
        attended, _, stats = attention(
            qkv, doc_row, doc_col, first, place, table, near, query_rows
        )
        mixed = jnp.dot(attended, w_out, preferred_element_type=f32)
        if split > 1:
            mixed = lax.dynamic_update_slice_in_dim(
                jnp.zeros((length, model_width), f32), mixed, query_part * query_rows, 0
            )
        middle = hidden + scatter_sum(mixed, group, blocks)
        inverse_ff = inverse_rms(middle)
        normed_ff = gather_rows((middle * inverse_ff * gain_ff[layer_id]).astype(bf16), ff_group)
        activated, slope = gelu_parts(contract(normed_ff, w_up, 1, 1))
        ff_result = jnp.dot(activated, w_down, preferred_element_type=f32)
        records.append(
            (hidden, inverse, units, qkv, attended, stats, middle, inverse_ff, normed_ff,
             activated, slope)
        )
        hidden = middle + scatter_sum(ff_result, ff_group, ff_members)
    output = hidden

    grads_ff, grads_in, grads_out, grads_gain_ff, grads_table = (
        [None] * layer_count for _ in range(5)
    )
    for layer_id in reversed(range(layer_count)):
        w_in, w_out, (w_up, w_down) = (
            weights_in[layer_id], weights_out[layer_id], weights_ff[layer_id],
        )
        (hidden, inverse, units, qkv, attended, stats, middle, inverse_ff, normed_ff,
         activated, slope) = records[layer_id]
        grad_low = gather_rows(upstream.astype(bf16), ff_group)
        grad_pre = (contract(grad_low, w_down, 1, 1) * slope).astype(bf16)
        grad_normed = scatter_sum(
            jnp.dot(grad_pre, w_up, preferred_element_type=f32), ff_group, ff_members
        )
        grad_pair = jnp.concatenate(
            [contract(grad_pre, normed_ff, 0, 0), contract(activated, grad_low, 0, 0)], axis=1
        ).astype(bf16)
        grads_ff[layer_id] = lax.psum_scatter(
            grad_pair, ff_spare, scatter_dimension=0, tiled=True
        ).astype(f32)
        grads_gain_ff[layer_id] = jnp.sum(grad_normed * middle * inverse_ff, axis=0)
        grad_middle = upstream + unit_norm_back(
            middle, inverse_ff, grad_normed * gain_ff[layer_id]
        )
        branch = gather_rows(grad_middle.astype(bf16), group)
        if split > 1:
            branch = lax.dynamic_slice_in_dim(branch, query_part * query_rows, query_rows, 0)
        grad_attended = contract(branch, w_out, 1, 1).astype(bf16)
        grad_qkv, grad_near, grad_far = attention_back(
            qkv, doc_row, doc_col, attended, grad_attended, stats, first, place, table, near, split
        )
        grads_table[layer_id] = (grad_near, grad_far)
        grad_units = scatter_sum(contract(grad_qkv, w_in, 1, 1), group, blocks)
        upstream = grad_middle + unit_norm_back(hidden, inverse, grad_units)
        grad_out = lax.dynamic_update_slice_in_dim(
            jnp.zeros((model_width, model_width), bf16),
            contract(attended, branch, 0, 0).astype(bf16),
            out_row,
            0,
        )
        grads_out[layer_id] = lax.psum_scatter(
            grad_out, everyone, scatter_dimension=0, tiled=True
        ).astype(f32)
        grads_in[layer_id] = contract(units, grad_qkv, 0, 0).astype(bf16)

    bucket_count = table.shape[0]
    grad_table = sum(
        bucket_grads(jnp.zeros((1,), jnp.int32), entry, bucket_count) for entry in grads_table
    )[:, :heads_dev]
    grad_table = lax.dynamic_update_slice_in_dim(
        jnp.zeros((bucket_count, heads_all), f32), grad_table, head_group * heads_dev, 1
    )
    grad_table = jnp.transpose(
        grad_table.reshape(blocks, bucket_count // blocks, heads_n, heads_all // heads_n),
        (2, 0, 1, 3),
    ).reshape(devices, -1)
    grad_gain_ff = jnp.transpose(
        jnp.stack(grads_gain_ff).reshape(layer_count, devices, weight_rows), (1, 0, 2)
    ).reshape(devices, -1)
    ends = jnp.sum(swap(jnp.concatenate([grad_gain_ff, grad_table], axis=1)), axis=0)
    grad_gain_ff = ends[: layer_count * weight_rows].reshape(layer_count, weight_rows)
    grad_bias_table = ends[layer_count * weight_rows :].reshape(
        bucket_count // blocks, heads_all // heads_n
    )
    grads_attn_in, grads_gains = [], []
    for layer_id in range(layer_count):
        parts = swap(grads_in[layer_id].reshape(devices, weight_rows, 3 * width)).astype(f32)
        parts = jnp.sum(parts.reshape(heads_n, blocks, weight_rows, 3 * width), axis=0)
        parts = jnp.sum(parts.reshape(head_groups, split, weight_rows, 3, width), axis=1)
        unit_grad = jnp.transpose(parts, (1, 2, 0, 3)).reshape(weight_rows, 3 * model_width)
        grads_attn_in.append(unit_grad * gain_attn[layer_id])
        grads_gains.append(
            jnp.stack(
                [jnp.sum(unit_grad * own_in[layer_id], axis=1), grad_gain_ff[layer_id]], axis=1
            )
        )
    return (
        output[None],
        upstream[None],
        jnp.stack(grads_attn_in),
        jnp.stack(grads_out),
        jnp.stack([entry[:, :model_width] for entry in grads_ff]),
        jnp.stack([entry[:, model_width:] for entry in grads_ff]),
        jnp.stack(grads_gains),
        grad_bias_table,
    )


def local_plane(tokens, doc_start, bias_table, attn_in, attn_out, ff_in, ff_out, gains, cotangent):
    heads_n, z_n, core_n = (lax.axis_size(axis) for axis in everyone)
    devices = heads_n * z_n * core_n
    at_head, at_z, at_core = (lax.axis_index(axis) for axis in everyone)
    members = heads_n * core_n
    block_rows, model_width = tokens.shape[1:]
    layer_count, weight_rows = attn_in.shape[:2]
    length = block_rows * members
    heads_all = bias_table.shape[1]
    heads_dev = heads_all // members
    width = heads_dev * head_dim
    member = at_head * core_n + at_core
    turn = [
        ((h * z_n + z) * core_n + c, ((h ^ z) * z_n + h) * core_n + c)
        for h in range(heads_n)
        for z in range(z_n)
        for c in range(core_n)
    ]
    everywhere = [(h, z, c) for h in range(heads_n) for z in range(z_n) for c in range(core_n)]

    def device(h, z, c):
        return (h * z_n + z) * core_n + c

    plane_turn = [(device(h, z, c), device(h ^ z, z, c)) for h, z, c in everywhere]
    line_turn = [(device(h, z, c), device(h, z ^ h, c)) for h, z, c in everywhere]
    place = jnp.stack(
        [
            (at_head ^ bits) * core_n + (at_core ^ other)
            for other in range(core_n)
            for bits in range(heads_n)
        ]
        + [at_z]
        + [
            (at_head ^ bits ^ at_z) * core_n + (at_core ^ other)
            for other in range(core_n)
            for bits in range(heads_n)
        ]
    ).astype(jnp.int32)

    def relay(array):
        return lax.ppermute(array, everyone, turn)

    def turn_in_plane(array):
        return lax.ppermute(array, everyone, plane_turn)

    def turn_in_line(array):
        return lax.ppermute(array, everyone, line_turn)

    def swap(array):
        return lax.all_to_all(array, everyone, 0, 0, tiled=True)

    row_shape = (block_rows, model_width)
    gain_attn = gains[:, :, 0].astype(f32)[:, :, None]
    near_share, far_share = call(
        share_in_kernel,
        [((members // 2 * layer_count * weight_rows, 3 * width), bf16)] * 2,
        place,
        attn_in,
        gain_attn,
        smem=1,
    )

    half_turns = [
        [
            (z * core_n + c, (2 * c + (a ^ z % 2)) * core_n + z // 2)
            for z in range(z_n)
            for c in range(core_n)
        ]
        for a in range(2)
    ]

    def fetch_out(layer_id, hold):
        own = attn_out[layer_id]
        other = toggle(own, "core", 1)
        head = jnp.where(
            at_core == 0, jnp.concatenate([own, other]), jnp.concatenate([other, own])
        )
        head = after(head, hold)
        return [
            lax.ppermute(head, ("z", "core"), [(holder, user) for user, holder in turns])
            for turns in half_turns
        ]

    def owners_halves(halves):
        return [
            lax.ppermute(half, ("z", "core"), turns) for half, turns in zip(halves, half_turns)
        ]

    def pair_chips(near, arrived, axis):
        rows, columns = near.shape[0] // 4, near.shape[1]
        shape = (2 * rows, columns) if axis == 0 else (rows, 2 * columns)
        return call(functools.partial(pair_kernel, axis), [(shape, bf16)] * 4, near, arrived)

    def share_chips(blocks):
        return [blocks[0]] + [toggle(blocks[bits], "head", bits) for bits in (1, 2, 3)]

    units_shape = [(row_shape, f32), (row_shape, bf16)]

    starts = jnp.broadcast_to(
        doc_start.astype(f32)[None, :, None], (heads_n, z_n, core_n, block_rows)
    )
    ff_gains = gains[:, :, 1].astype(f32).reshape(1, -1)
    small = jnp.concatenate(
        [
            starts.reshape(devices, block_rows),
            jnp.broadcast_to(ff_gains, (devices, layer_count * weight_rows)),
        ],
        axis=1,
    )
    table, strip = prepare(bias_table, member * heads_dev, heads_dev)
    hidden, strip = tie(relay(tokens[0]), strip)
    hidden, shares, cotangent_low, halves, small = tie(
        hidden,
        share_chips(pair_chips(near_share, toggle(far_share, "core", 1), 0)),
        turn_in_plane(cotangent[0].astype(bf16)),
        fetch_out(0, near_share),
        swap(after(small, near_share)),
    )
    hidden, unit_rows = call(unit_kernel, units_shape, hidden)
    doc_row = small[:members, :block_rows].reshape(2, 2, core_n, block_rows)
    at_block = at_head ^ at_z
    for axis, bit in ((0, at_block // 2), (1, at_block % 2), (2, at_core)):
        doc_row = jnp.where(bit == 1, jnp.flip(doc_row, axis), doc_row)
    doc_row = jnp.transpose(doc_row, (2, 0, 1, 3)).reshape(1, length)
    doc_col = doc_row.reshape(length, 1)
    gain_ff = jnp.transpose(
        small[:, block_rows:].reshape(devices, layer_count, weight_rows), (1, 0, 2)
    ).reshape(layer_count, 1, model_width)

    def round_planes(array, by, hold):
        return shift(after(array, hold), by)

    ff_pairs = [
        jnp.concatenate([ff_in[layer_id], ff_out[layer_id]], axis=1) for layer_id in range(layer_count)
    ]

    def ff_both(kernel, row_operands, pair, columns):
        return zip(
            *(
                by_rows(
                    kernel,
                    256,
                    operands,
                    [pair],
                    [(pair.shape[0], bf16)] * columns + [(model_width, kind)],
                )
                for operands, kind in zip(zip(*row_operands), (f32, bf16))
            )
        )

    def ff_forward(normed, *parts):
        units = 4 * parts[0].shape[0]
        outs = [(units, bf16), (units, bf16)]
        *near, pair = by_rows(
            ff_first_kernel,
            256,
            [normed[0]],
            parts,
            outs + [(model_width, f32)],
            [(units, 2 * model_width)],
        )
        far = by_rows(ff_kernel, 256, [normed[1]], [pair], outs + [(model_width, bf16)])
        return pair, *zip(near, far)

    def ff_backward(low, slopes, pair):
        return ff_both(ff_back_kernel, [low, slopes], pair, 1)

    share, later_share = call(
        join_kernel, [((members * weight_rows, 3 * width), bf16)] * layer_count, *shares
    )
    near, far, lower, upper, opposite, doc_row, doc_col, gain_ff, *ff_pairs = plane_gather(
        unit_rows,
        shift(share, 1),
        shift(share, -1),
        shift(share, 2),
        doc_row,
        doc_col,
        gain_ff,
        *ff_pairs,
    )
    units = (near, far)
    w_in, w_out, qkv, attended, stats, *parts = plane_attention(
        *units, [share, lower, upper, opposite], halves, doc_row, doc_col, place, table, strip
    )
    parts, upstream, lower = tie(
        parts, turn_in_line(after(cotangent_low, near)), round_planes(ff_pairs[0], 1, near)
    )
    parts, own = plane_scatter(*parts)
    parts, upper = tie(parts, round_planes(ff_pairs[0], -1, own))
    middle, normed_rows = call(close_gain_kernel, units_shape, hidden, *parts, gain_ff[0])
    *normed, opposite_in, opposite_out = plane_gather(
        normed_rows,
        round_planes(ff_in[0], 2, normed_rows),
        round_planes(ff_out[0], 2, normed_rows),
    )
    pair, acts, slopes, parts = ff_forward(
        normed, ff_pairs[0], lower, upper, opposite_in, opposite_out
    )
    records = [
        (hidden, units, w_in, w_out, pair, qkv, attended, stats, middle, normed, acts, slopes)
    ]
    parts, lower, upper = tie(
        parts,
        round_planes(later_share, 1, normed[0]),
        round_planes(later_share, -1, normed[0]),
    )
    parts, own = plane_scatter(*parts)
    parts, opposite = tie(parts, round_planes(later_share, 2, own))
    shares = [later_share, lower, upper, opposite]
    hidden, unit_rows = call(close_kernel, units_shape, middle, *parts)

    near, far, lower, halves = plane_gather(
        unit_rows, round_planes(ff_pairs[1], 1, unit_rows), fetch_out(1, unit_rows)
    )
    units = (near, far)
    w_in, w_out, qkv, attended, stats, *parts = plane_attention(
        *units, shares, halves, doc_row, doc_col, place, table, strip
    )
    low = plane_gather(after(upstream, far))
    parts, near_low, upper = tie(parts, low[0], round_planes(ff_pairs[1], -1, far))
    low = (near_low, low[1])
    parts, own = plane_scatter(*parts)
    parts, opposite_in = tie(parts, round_planes(ff_in[1], 2, own))
    middle, normed_rows = call(close_gain_kernel, units_shape, hidden, *parts, gain_ff[1])
    *normed, opposite_out = plane_gather(normed_rows, round_planes(ff_out[1], 2, normed_rows))
    pair, acts, slopes, last_parts = ff_forward(
        normed, ff_pairs[1], lower, upper, opposite_in, opposite_out
    )
    records.append(
        (hidden, units, w_in, w_out, pair, qkv, attended, stats, middle, normed, acts, slopes)
    )

    def back_to_middle(parts, upstream, middle, gain):
        return call(
            middle_back_kernel, units_shape + [((1, model_width), f32)], upstream, *parts, middle, gain
        )

    def attention_grads(record, branch):
        _, _, w_in, w_out, _, qkv, attended, stats, *_ = record
        grad_qkv, grad_near, grad_far, near_part, far_part, *halves = plane_attention_back(
            qkv, doc_row, doc_col, attended, stats, *branch, w_in, w_out, place, table, strip
        )
        return grad_qkv, (grad_near, grad_far), (near_part, far_part), halves

    def table_grads(near_and_far):
        return bucket_grads(at_core.reshape(1) * heads_dev + 8, near_and_far, table.shape[0])

    def add_in(own, lower, upper, opposite):
        shape = (own.shape[0] // 2, own.shape[1])
        return call(add_in_kernel, [(shape, bf16)] * 2, own, lower, upper, opposite)

    record = records[1]
    hidden, units, _, _, pair, *_, middle, normed, acts, slopes = record
    pres, parts = ff_backward(low, slopes, pair)
    parts, own = plane_scatter(*parts)
    planes = ff_grads(after(pres, own), acts, normed, low)
    parts, ff_lower = tie(parts, shift(planes[1], -1))
    last_parts, _ = plane_scatter(*after(last_parts, parts))
    grad_middle, branch_rows, gain_1 = back_to_middle(parts, upstream, middle, gain_ff[1])
    *branch, ff_upper = plane_gather(branch_rows, round_planes(planes[2], 1, branch_rows))
    grad_qkv, strips_1, parts, halves_1 = attention_grads(record, branch)
    parts, last_parts, opposite_up = tie(
        parts, last_parts, round_planes(planes[3], 2, branch[1])
    )
    parts, own = plane_scatter(*parts)
    parts, opposite_down, output = tie(
        parts,
        round_planes(planes[4], 2, own),
        call(last_kernel, [(row_shape, bf16)], middle, *after(last_parts, own))[0],
    )
    grads_ff = [planes[0], ff_lower, ff_upper, opposite_up, opposite_down]
    upstream, low_rows = call(layer_back_kernel, units_shape, grad_middle, *parts, hidden)

    record = records[0]
    hidden, units, _, _, pair, *_, middle, normed, acts, slopes = record
    grad_in = in_grads(place, *records[1][1], after(grad_qkv, low_rows))
    *low, in_opposite, table_1, halves_1 = plane_gather(
        low_rows,
        shift(grad_in[3], 2),
        table_grads(after(strips_1, low_rows)),
        owners_halves(after(halves_1, low_rows)),
    )
    pres, parts = ff_backward(low, slopes, pair)
    parts, own = plane_scatter(*parts)
    planes = ff_grads(after(pres, own), acts, normed, low)
    parts, ff_lower = tie(parts, shift(planes[1], -1))
    grad_middle, branch_rows, gain_0 = back_to_middle(parts, upstream, middle, gain_ff[0])
    *branch, ff_upper, in_lower, in_upper = plane_gather(
        branch_rows,
        round_planes(planes[2], 1, branch_rows),
        round_planes(grad_in[1], -1, branch_rows),
        round_planes(grad_in[2], 1, branch_rows),
    )
    shares_1 = [grad_in[0], in_lower, in_upper, in_opposite]
    grad_qkv, strips_0, parts, halves_0 = attention_grads(record, branch)
    parts, output, opposite_up = tie(
        parts, turn_in_line(after(output, branch[1])), round_planes(planes[3], 2, branch[1])
    )
    parts, own = plane_scatter(*parts)
    table_0 = table_grads(after(strips_0, parts[1]))
    grad_in = in_grads(
        place, *units, after(grad_qkv, parts[1]), gain_0, gain_1, table_0, table_1
    )
    parts, opposite_down, in_opposite, adds_1 = tie(
        parts,
        round_planes(planes[4], 2, own),
        shift(grad_in[3], 2),
        add_in(*after(shares_1, parts[1])),
    )
    upstream, low_rows = call(layer_back_kernel, units_shape, grad_middle, *parts, hidden)
    in_lower = round_planes(grad_in[1], -1, low_rows)
    in_upper = round_planes(grad_in[2], 1, low_rows)
    grad_tokens = turn_in_plane(turn_in_line(low_rows))
    output = turn_in_plane(after(output, low_rows)).astype(f32)
    halves_0 = owners_halves(after(halves_0, low_rows))
    grads_ff = [planes[0], ff_lower, ff_upper, opposite_up, opposite_down] + grads_ff
    grad_up, grad_down = finish_ff(after(grads_ff, low_rows), ff_in.shape)
    own_out, other_out = call(
        add_out_kernel, [(attn_out.shape, f32), (attn_out.shape, bf16)], place, *halves_0, *halves_1, smem=1
    )
    (grad_attn_out,) = call(
        finish_out_kernel, [(attn_out.shape, f32)], own_out, toggle(other_out, "core", 1)
    )
    adds_0 = add_in(grad_in[0], in_lower, in_upper, in_opposite)
    near_in, far_in = (jnp.concatenate(pair, axis=1) for pair in zip(adds_0, adds_1))
    shares_in = share_chips(pair_chips(near_in, toggle(far_in, "core", 1), 1))
    own_buckets = table.shape[0] // (z_n * core_n)
    grad_attn_in, grad_gains, ends = call(
        functools.partial(finish_in_kernel, layer_count),
        [(attn_in.shape, f32), (gains.shape, f32), ((weight_rows, tile), f32)],
        place,
        *shares_in,
        attn_in,
        gain_attn,
        smem=1,
    )
    return (
        output[None],
        grad_tokens.astype(f32)[None],
        grad_attn_in,
        grad_attn_out,
        grad_up,
        grad_down,
        grad_gains,
        ends[:own_buckets, 8 : 8 + heads_all // heads_n],
    )


def solution(mesh):
    sizes = dict(mesh.shape)
    cores = 2
    fine = Mesh(
        mesh.devices.reshape(sizes["head"], sizes["blk"] // cores, cores), everyone
    )
    blk = ("z", "core")
    in_specs = (
        P("head", blk, None),
        P(None, blk),
        P(),
        P(None, everyone, None),
        P(None, everyone, None),
        P(None, everyone, None),
        P(None, everyone, None),
        P(None, everyone, None),
        P("head", blk, None),
    )
    out_specs = (
        P("head", blk, None),
        P("head", blk, None),
        P(None, everyone, None),
        P(None, everyone, None),
        P(None, everyone, None),
        P(None, everyone, None),
        P(None, everyone, None),
        P(blk, "head"),
    )
    plane = sizes["head"] == 4 and sizes["blk"] == 8
    local = local_plane if plane else local_general
    return jax.shard_map(local, mesh=fine, in_specs=in_specs, out_specs=out_specs, check_vma=False)
```

```python
import functools

import jax
import jax.numpy as jnp
import numpy as np
from jax import lax
from jax.experimental import pallas as pl
from jax.experimental.pallas import tpu as pltpu
from jax.sharding import Mesh
from jax.sharding import PartitionSpec as P

bounds = (1, 2, 3, 4, 5, 6, 7, 8, 12, 16, 23, 32, 46, 64, 91)
epsilon = 1e-06
masked = -1e30
score_scale = 0.125
head_dim = 64
tile = 128
everyone = ("head", "z", "core")
bf16 = jnp.bfloat16
f32 = jnp.float32


def contract(lhs, rhs, lhs_dim, rhs_dim):
    return lax.dot_general(
        lhs, rhs, (((lhs_dim,), (rhs_dim,)), ((), ())), preferred_element_type=f32
    )


def near_buckets(shape):
    offsets = (
        lax.broadcasted_iota(jnp.int32, shape, 1) - tile - lax.broadcasted_iota(jnp.int32, shape, 0)
    )
    distance = jnp.abs(offsets)
    bucket = jnp.where(offsets > 0, 16, 0)
    for boundary in bounds:
        bucket = bucket + jnp.where(distance >= boundary, 1, 0)
    return bucket


def near_kernel(table, near):
    bucket = near_buckets(near.shape[1:])
    for head in range(near.shape[0]):
        values = jnp.zeros(near.shape[1:], f32)
        for bucket_id in range(table.shape[0]):
            values = jnp.where(bucket == bucket_id, table[bucket_id, head], values)
        near[head] = values


def bucket_kernel(first_lane, near, far, out):
    bucket = near_buckets(near.shape[1:])
    rows = lax.broadcasted_iota(jnp.int32, out.shape, 0)
    lanes = lax.broadcasted_iota(jnp.int32, out.shape, 1)
    total = jnp.zeros(out.shape, f32)
    for head in range(near.shape[0]):
        strip = near[head]
        for bucket_id in range(out.shape[0]):
            value = jnp.sum(jnp.where(bucket == bucket_id, strip, 0.0), axis=0, keepdims=True)
            value = jnp.sum(value, axis=1, keepdims=True)
            if bucket_id in (15, 31):
                value = value + far[head, bucket_id // 16, :1, :1]
            total = jnp.where((rows == bucket_id) & (lanes == head + first_lane[0]), value, total)
    out[...] = total


def fill_band(band, table, near, heads_dev, length):
    for head in range(heads_dev):
        band[head, :, : length - tile] = jnp.full((tile, length - tile), table[15, head], f32)
        band[head, :, length - tile : length + 2 * tile] = near[head]
        band[head, :, length + 2 * tile :] = jnp.full(
            (tile, length - 2 * tile), table[31, head], f32
        )


def band_starts(place, at, length, skip=0):
    return [
        pl.multiple_of(length + (place[skip + block] - place[skip + at]) * tile, tile)
        for block in range(length // tile)
    ]


def attention_kernel(
    heads_dev, length, first, place, table, near, qkv, doc_row, doc_col, out, local, stats, band
):
    step = pl.program_id(0)
    width = heads_dev * head_dim

    @pl.when(step == 0)
    def _():
        fill_band(band, table, near, heads_dev, length)

    row = pl.multiple_of((first[0] + step) * tile, tile)
    out_row = pl.multiple_of((place[first[0] + step] - first[0]) * tile, tile)
    starts = band_starts(place, first[0] + step, length)
    same_doc = doc_col[...] == doc_row[...]
    queries = qkv[pl.ds(row, tile), :width] * bf16(score_scale)
    lanes = lax.broadcasted_iota(jnp.int32, (tile, tile), 1)
    collected = jnp.zeros((tile, tile), f32)
    for head in range(heads_dev):
        own = slice(head * head_dim, (head + 1) * head_dim)
        keys = qkv[:, width + own.start : width + own.stop]
        values = qkv[:, 2 * width + own.start : 2 * width + own.stop]
        scores = contract(queries[:, own], keys, 1, 1)
        scores = scores + jnp.concatenate(
            [band[head, :, pl.ds(start, tile)] for start in starts], axis=1
        )
        scores = jnp.where(same_doc, scores, masked)
        peak = jnp.max(scores, axis=1, keepdims=True)
        weights = jnp.exp(scores - peak)
        total = jnp.sum(weights, axis=1, keepdims=True)
        mixed = contract(weights.astype(bf16), values, 1, 0) / total
        out[pl.ds(out_row, tile), own] = mixed.astype(bf16)
        local[:, own] = mixed.astype(bf16)
        collected = jnp.where(lanes == head, peak + jnp.log(total), collected)
    stats[...] = collected


def attention_back_kernel(
    heads_dev, length, split, first, place, table, near, qkv, doc_row, doc_col, attended, grad_out, stats,
    grad_qkv, grad_near, grad_far, band, grad_band, grad_keys, grad_values,
):
    step = pl.program_id(0)
    width = heads_dev * head_dim

    @pl.when(step == 0)
    def _():
        fill_band(band, table, near, heads_dev, length)
        grad_band[...] = jnp.zeros_like(grad_band)
        grad_keys[...] = jnp.zeros_like(grad_keys)
        grad_values[...] = jnp.zeros_like(grad_values)
        if split > 1:
            grad_qkv[...] = jnp.zeros_like(grad_qkv)

    row = pl.multiple_of((first[0] + step) * tile, tile)
    out_row = pl.multiple_of((place[first[0] + step] - first[0]) * tile, tile)
    starts = band_starts(place, first[0] + step, length)
    same_doc = doc_col[...] == doc_row[...]
    at_step = pl.multiple_of(step * tile, tile)
    queries = qkv[pl.ds(row, tile), :width] * bf16(score_scale)
    for head in range(heads_dev):
        own = slice(head * head_dim, (head + 1) * head_dim)
        keys = qkv[:, width + own.start : width + own.stop]
        values = qkv[:, 2 * width + own.start : 2 * width + own.stop]
        upstream = grad_out[pl.ds(out_row, tile), own]
        scores = contract(queries[:, own], keys, 1, 1) + jnp.concatenate(
            [band[head, :, pl.ds(start, tile)] for start in starts], axis=1
        )
        scores = jnp.where(same_doc, scores, masked)
        weights = jnp.exp(scores - stats[:, head : head + 1])
        delta = jnp.sum(
            upstream.astype(f32) * attended[pl.ds(at_step, tile), own].astype(f32),
            axis=1,
            keepdims=True,
        )
        grad_scores = weights * (contract(upstream, values, 1, 1) - delta)
        for block, start in enumerate(starts):
            grad_band[head, :, pl.ds(start, tile)] += grad_scores[
                :, block * tile : (block + 1) * tile
            ]
        grad_low = grad_scores.astype(bf16)
        grad_values[:, own] += contract(weights.astype(bf16), upstream, 0, 0)
        grad_keys[:, own] += contract(grad_low, queries[:, own], 0, 0)
        grad_qkv[pl.ds(row, tile), own] = (
            contract(grad_low, keys, 1, 0) * score_scale
        ).astype(bf16)

    @pl.when(step == pl.num_programs(0) - 1)
    def _():
        grad_qkv[:, width : 2 * width] = grad_keys[...].astype(bf16)
        grad_qkv[:, 2 * width :] = grad_values[...].astype(bf16)
        for head in range(heads_dev):
            grad_near[head] = grad_band[head, :, length - tile : length + 2 * tile]
            grad_far[head, 0] = jnp.full(
                (8, tile), jnp.sum(grad_band[head, :, : length - tile]), f32
            )
            grad_far[head, 1] = jnp.full(
                (8, tile), jnp.sum(grad_band[head, :, length + 2 * tile :]), f32
            )


def whole(shape):
    return pl.BlockSpec(shape, lambda step: (0,) * len(shape), pipeline_mode=pl.Buffered(1))


def attention(qkv, doc_row, doc_col, first, place, table, near, rows):
    length = qkv.shape[0]
    heads_dev = table.shape[1]
    width = heads_dev * head_dim
    return pl.pallas_call(
        functools.partial(attention_kernel, heads_dev, length),
        grid=(rows // tile,),
        in_specs=[
            pl.BlockSpec(memory_space=pltpu.SMEM),
            pl.BlockSpec(memory_space=pltpu.SMEM),
            pl.BlockSpec(memory_space=pltpu.SMEM),
            whole(near.shape),
            whole(qkv.shape),
            whole(doc_row.shape),
            pl.BlockSpec((tile, 1), lambda step: (step, 0)),
        ],
        out_specs=[
            whole((rows, width)),
            pl.BlockSpec((tile, width), lambda step: (step, 0)),
            pl.BlockSpec((tile, tile), lambda step: (step, 0)),
        ],
        out_shape=[
            jax.ShapeDtypeStruct((rows, width), bf16),
            jax.ShapeDtypeStruct((rows, width), bf16),
            jax.ShapeDtypeStruct((rows, tile), f32),
        ],
        scratch_shapes=[pltpu.VMEM((heads_dev, tile, 2 * length), f32)],
        compiler_params=pltpu.CompilerParams(vmem_limit_bytes=40 * 2**20),
        cost_estimate=pl.CostEstimate(
            flops=4 * rows * length * width,
            bytes_accessed=4 * length * width * 2,
            transcendentals=rows * length * heads_dev,
        ),
    )(first, place, table, near, qkv, doc_row, doc_col)


def attention_back(
    qkv, doc_row, doc_col, attended, grad_out, stats, first, place, table, near, split
):
    length = qkv.shape[0]
    rows = grad_out.shape[0]
    heads_dev = table.shape[1]
    width = heads_dev * head_dim
    return pl.pallas_call(
        functools.partial(attention_back_kernel, heads_dev, length, split),
        grid=(rows // tile,),
        in_specs=[
            pl.BlockSpec(memory_space=pltpu.SMEM),
            pl.BlockSpec(memory_space=pltpu.SMEM),
            pl.BlockSpec(memory_space=pltpu.SMEM),
            whole(near.shape),
            whole(qkv.shape),
            whole(doc_row.shape),
            pl.BlockSpec((tile, 1), lambda step: (step, 0)),
            whole((rows, width)),
            whole((rows, width)),
            pl.BlockSpec((tile, tile), lambda step: (step, 0)),
        ],
        out_specs=[
            whole((length, 3 * width)),
            whole((heads_dev, tile, 3 * tile)),
            whole((heads_dev, 2, 8, tile)),
        ],
        out_shape=[
            jax.ShapeDtypeStruct((length, 3 * width), bf16),
            jax.ShapeDtypeStruct((heads_dev, tile, 3 * tile), f32),
            jax.ShapeDtypeStruct((heads_dev, 2, 8, tile), f32),
        ],
        scratch_shapes=[
            pltpu.VMEM((heads_dev, tile, 2 * length), f32),
            pltpu.VMEM((heads_dev, tile, 2 * length), f32),
            pltpu.VMEM((length, width), f32),
            pltpu.VMEM((length, width), f32),
        ],
        compiler_params=pltpu.CompilerParams(vmem_limit_bytes=48 * 2**20),
        cost_estimate=pl.CostEstimate(
            flops=10 * rows * length * width,
            bytes_accessed=8 * length * width * 2,
            transcendentals=rows * length * heads_dev,
        ),
    )(first, place, table, near, qkv, doc_row, doc_col, attended, grad_out, stats)


def call(kernel, shapes, *operands, smem=0):
    return pl.pallas_call(
        kernel,
        in_specs=[pl.BlockSpec(memory_space=pltpu.SMEM)] * smem
        + [pl.BlockSpec(memory_space=pltpu.VMEM)] * (len(operands) - smem),
        out_specs=[pl.BlockSpec(memory_space=pltpu.VMEM)] * len(shapes),
        out_shape=[jax.ShapeDtypeStruct(shape, kind) for shape, kind in shapes],
        compiler_params=pltpu.CompilerParams(vmem_limit_bytes=10 * 2**20),
    )(*operands)


def share_in_kernel(place, attn_in, gains, near, far):
    layers, rows = attn_in.shape[:2]
    half = near.shape[0] // (layers * rows)
    width = near.shape[1] // 3
    for index in range(2 * half):
        member = place[index]
        for layer_id in range(layers):
            block = jnp.concatenate(
                [
                    attn_in[
                        layer_id,
                        :,
                        pl.ds(pl.multiple_of((part * 2 * half + member) * width, width), width),
                    ]
                    for part in range(3)
                ],
                axis=1,
            )
            at = (index % half * layers + layer_id) * rows
            out = near if index < half else far
            out[at : at + rows] = (block.astype(f32) * gains[layer_id]).astype(bf16)


def join_kernel(*refs):
    shares, outs = refs[:4], refs[4:]
    rows = outs[0].shape[0] // 8
    for chip, share in enumerate(shares):
        for core in range(2):
            for layer_id, out in enumerate(outs):
                source = (core * len(outs) + layer_id) * rows
                target = (chip * 2 + core) * rows
                out[target : target + rows] = share[source : source + rows]


def row_of(chip, plane, core, rows, planes=4):
    return pl.multiple_of(((chip * planes + plane) * 2 + core) * rows, rows)


def assemble_in_kernel(place, own, lower, upper, opposite, out):
    at_z, at_core, at_head = place[8], place[0] % 2, place[0] // 2
    rows = own.shape[0] // 8
    for part, offset in ((own, 0), (lower, 3), (upper, 1), (opposite, 2)):
        plane = (at_z + offset) % 4
        for index in range(8):
            row = row_of(at_head ^ (index // 2), plane, at_core ^ (index % 2), rows)
            out[pl.ds(row, rows)] = part[index * rows : (index + 1) * rows]


def plane_attention_kernel(
    length, place, table, strip, near, far, w_in, *refs
):
    halves, (doc_row, doc_col, w_out, qkv, attended, stats, near_part, far_part, band) = (
        refs[:2], refs[2:],
    )
    step = pl.program_id(0)
    half = length // 2
    heads_dev = table.shape[1]
    width = heads_dev * head_dim

    @pl.when(step == 0)
    def _():
        fill_band(band, table, strip, heads_dev, length)
        swapped = place[length // tile] % 2 == 1
        rows = width // 2
        w_out[:rows] = jnp.where(swapped, halves[1][...], halves[0][...])
        w_out[rows:] = jnp.where(swapped, halves[0][...], halves[1][...])
        qkv[:half] = contract(near[...], w_in[...], 1, 0).astype(bf16)
        qkv[half:] = contract(far[...], w_in[...], 1, 0).astype(bf16)

    row = pl.multiple_of(step * tile, tile)
    starts = band_starts(place, step, length, length // tile + 1)
    same_doc = doc_col[...] == doc_row[...]
    queries = qkv[pl.ds(row, tile), :width] * bf16(score_scale)
    lanes = lax.broadcasted_iota(jnp.int32, (tile, tile), 1)
    collected = jnp.zeros((tile, tile), f32)
    results = []
    for head in range(heads_dev):
        own = slice(head * head_dim, (head + 1) * head_dim)
        keys = qkv[:, width + own.start : width + own.stop]
        values = qkv[:, 2 * width + own.start : 2 * width + own.stop]
        scores = contract(queries[:, own], keys, 1, 1) + jnp.concatenate(
            [band[head, :, pl.ds(start, tile)] for start in starts], axis=1
        )
        scores = jnp.where(same_doc, scores, masked)
        peak = jnp.max(scores, axis=1, keepdims=True)
        weights = jnp.exp(scores - peak)
        total = jnp.sum(weights, axis=1, keepdims=True)
        results.append((contract(weights.astype(bf16), values, 1, 0) / total).astype(bf16))
        collected = jnp.where(lanes == head, peak + jnp.log(total), collected)
    stats[...] = collected
    merged = jnp.concatenate(results, axis=1)
    attended[...] = merged
    part = contract(merged, w_out[...], 1, 0)

    @pl.when(row < half)
    def _():
        near_part[...] = part

    @pl.when(row >= half)
    def _():
        far_part[...] = part.astype(bf16)


def near_block(steps, columns):
    return pl.BlockSpec((tile, columns), lambda step: (jnp.minimum(step, steps // 2 - 1), 0))


def far_block(steps, columns):
    return pl.BlockSpec((tile, columns), lambda step: (jnp.maximum(step - steps // 2, 0), 0))


def plane_attention(near, far, w_in, halves, doc_row, doc_col, place, table, strip):
    length, model_width = 2 * near.shape[0], near.shape[1]
    steps = length // tile
    heads_dev = table.shape[1]
    width = heads_dev * head_dim
    return pl.pallas_call(
        functools.partial(plane_attention_kernel, length),
        grid=(steps,),
        in_specs=[
            pl.BlockSpec(memory_space=pltpu.SMEM),
            pl.BlockSpec(memory_space=pltpu.SMEM),
            whole(strip.shape),
            whole(near.shape),
            whole(far.shape),
            whole(w_in.shape),
            *[whole(half.shape) for half in halves],
            whole(doc_row.shape),
            pl.BlockSpec((tile, 1), lambda step: (step, 0)),
        ],
        out_specs=[
            whole((width, model_width)),
            whole((length, 3 * width)),
            pl.BlockSpec((tile, width), lambda step: (step, 0)),
            pl.BlockSpec((tile, tile), lambda step: (step, 0)),
            near_block(steps, model_width),
            far_block(steps, model_width),
        ],
        out_shape=[
            jax.ShapeDtypeStruct((width, model_width), bf16),
            jax.ShapeDtypeStruct((length, 3 * width), bf16),
            jax.ShapeDtypeStruct((length, width), bf16),
            jax.ShapeDtypeStruct((length, tile), f32),
            jax.ShapeDtypeStruct((length // 2, model_width), f32),
            jax.ShapeDtypeStruct((length // 2, model_width), bf16),
        ],
        scratch_shapes=[pltpu.VMEM((heads_dev, tile, 2 * length), f32)],
        compiler_params=pltpu.CompilerParams(vmem_limit_bytes=14 * 2**20),
        cost_estimate=pl.CostEstimate(
            flops=4 * length * length * width + 8 * length * model_width * width,
            bytes_accessed=12 * 2**20,
            transcendentals=length * length * heads_dev,
        ),
    )(place, table, strip, near, far, w_in, *halves, doc_row, doc_col)


def plane_attention_back_kernel(
    length, place, table, strip, qkv, doc_row, doc_col, attended, stats, near, far, w_in, w_out,
    grad_qkv, grad_near, grad_far, near_part, far_part, *rest
):
    halves, (band, grad_band, grad_keys, grad_values, out_sum) = rest[:2], rest[2:]
    step = pl.program_id(0)
    half = length // 2
    heads_dev = table.shape[1]
    width = heads_dev * head_dim

    @pl.when(step == 0)
    def _():
        fill_band(band, table, strip, heads_dev, length)
        grad_band[...] = jnp.zeros_like(grad_band)
        grad_keys[...] = jnp.zeros_like(grad_keys)
        grad_values[...] = jnp.zeros_like(grad_values)
        out_sum[...] = jnp.zeros_like(out_sum)

    row = pl.multiple_of(step * half, half)
    branch = jnp.where(step == 0, near[...], far[...])
    merged = attended[...]
    grad_merged = contract(branch, w_out[...], 1, 1).astype(bf16)
    out_sum[...] += contract(merged, branch, 0, 0)
    products = grad_merged.astype(f32) * merged.astype(f32)
    queries = qkv[pl.ds(row, half), :width] * bf16(score_scale)
    blocks = half // tile
    for head in range(heads_dev):
        own = slice(head * head_dim, (head + 1) * head_dim)
        keys = qkv[:, width + own.start : width + own.stop]
        values = qkv[:, 2 * width + own.start : 2 * width + own.stop]
        upstream = grad_merged[:, own]
        raw_scores = contract(queries[:, own], keys, 1, 1)
        grad_weights = contract(upstream, values, 1, 1)
        delta = jnp.sum(products[:, own], axis=1, keepdims=True)
        weights_low, grads_low = [], []
        for block in range(blocks):
            lines = slice(block * tile, (block + 1) * tile)
            starts = band_starts(place, step * blocks + block, length, length // tile + 1)
            scores = raw_scores[lines] + jnp.concatenate(
                [band[head, :, pl.ds(start, tile)] for start in starts], axis=1
            )
            scores = jnp.where(doc_col[lines] == doc_row[...], scores, masked)
            weights = jnp.exp(scores - stats[lines, head : head + 1])
            grad_scores = weights * (grad_weights[lines] - delta[lines])
            for index, start in enumerate(starts):
                grad_band[head, :, pl.ds(start, tile)] += grad_scores[
                    :, index * tile : (index + 1) * tile
                ]
            weights_low.append(weights.astype(bf16))
            grads_low.append(grad_scores.astype(bf16))
        weights_low, grads_low = jnp.concatenate(weights_low), jnp.concatenate(grads_low)
        grad_values[:, own] += contract(weights_low, upstream, 0, 0)
        grad_keys[:, own] += contract(grads_low, queries[:, own], 0, 0)
        grad_qkv[pl.ds(row, half), own] = (
            contract(grads_low, keys, 1, 0) * score_scale
        ).astype(bf16)

    @pl.when(step == pl.num_programs(0) - 1)
    def _():
        grad_qkv[:, width : 2 * width] = grad_keys[...].astype(bf16)
        grad_qkv[:, 2 * width :] = grad_values[...].astype(bf16)
        far_part[...] = contract(grad_qkv[half:], w_in[...], 1, 1).astype(bf16)
        near_part[...] = contract(grad_qkv[:half], w_in[...], 1, 1)
        rows = width // 2
        for index, part in enumerate(halves):
            block = index ^ place[length // tile] % 2
            part[...] = out_sum[pl.ds(pl.multiple_of(block * rows, rows), rows)].astype(bf16)
        for head in range(heads_dev):
            grad_near[head] = grad_band[head, :, length - tile : length + 2 * tile]
            grad_far[head, 0] = jnp.full(
                (8, tile), jnp.sum(grad_band[head, :, : length - tile]), f32
            )
            grad_far[head, 1] = jnp.full(
                (8, tile), jnp.sum(grad_band[head, :, length + 2 * tile :]), f32
            )


def plane_attention_back(
    qkv, doc_row, doc_col, attended, stats, near, far, w_in, w_out, place, table, strip
):
    length, model_width = 2 * near.shape[0], near.shape[1]
    half = length // 2
    heads_dev = table.shape[1]
    width = heads_dev * head_dim
    shapes = [
        ((length, 3 * width), bf16),
        ((heads_dev, tile, 3 * tile), f32),
        ((heads_dev, 2, 8, tile), f32),
        ((length // 2, model_width), f32),
        ((length // 2, model_width), bf16),
    ] + [((width // 2, model_width), bf16)] * 2
    return pl.pallas_call(
        functools.partial(plane_attention_back_kernel, length),
        grid=(2,),
        in_specs=[
            pl.BlockSpec(memory_space=pltpu.SMEM),
            pl.BlockSpec(memory_space=pltpu.SMEM),
            whole(strip.shape),
            whole(qkv.shape),
            whole(doc_row.shape),
            pl.BlockSpec((half, 1), lambda step: (step, 0)),
            pl.BlockSpec((half, width), lambda step: (step, 0)),
            pl.BlockSpec((half, tile), lambda step: (step, 0)),
            whole((half, model_width)),
            whole((half, model_width)),
            whole(w_in.shape),
            whole(w_out.shape),
        ],
        out_specs=[whole(shape) for shape, _ in shapes],
        out_shape=[jax.ShapeDtypeStruct(shape, kind) for shape, kind in shapes],
        scratch_shapes=[
            pltpu.VMEM((heads_dev, tile, 2 * length), f32),
            pltpu.VMEM((heads_dev, tile, 2 * length), f32),
            pltpu.VMEM((length, width), f32),
            pltpu.VMEM((length, width), f32),
            pltpu.VMEM((width, model_width), f32),
        ],
        compiler_params=pltpu.CompilerParams(vmem_limit_bytes=32 * 2**20),
        cost_estimate=pl.CostEstimate(
            flops=10 * length * length * width + 10 * length * model_width * width,
            bytes_accessed=12 * 2**20,
            transcendentals=length * length * heads_dev,
        ),
    )(place, table, strip, qkv, doc_row, doc_col, attended, stats, near, far, w_in, w_out)


def gelu_and_slope(pre_act):
    size = jnp.abs(pre_act)
    gauss = jnp.exp(-0.5 * pre_act * pre_act)
    ratio = 1.0 / (1.0 + np.float32(0.3275911 * 0.5**0.5) * size)
    series = np.float32(1.061405429)
    for factor in (-1.453152027, 1.421413741, -0.284496736, 0.254829592):
        series = series * ratio + np.float32(factor)
    tail = 0.5 * series * ratio * gauss
    cumulative = jnp.where(pre_act < 0, tail, 1.0 - tail)
    slope = cumulative + pre_act * gauss * np.float32((2 * np.pi) ** -0.5)
    return pre_act * cumulative, slope


def ff_kernel(rows, pair, activated, slope, part):
    columns = rows.shape[1]
    value, gradient = gelu_and_slope(contract(rows[...], pair[:, :columns], 1, 1))
    activated[...] = value.astype(bf16)
    slope[...] = gradient.astype(bf16)
    part[...] = contract(activated[...], pair[:, columns:], 1, 0).astype(part.dtype)


def ff_first_kernel(rows, *refs):
    parts, (activated, slope, part, pair) = refs[:5], refs[5:]

    @pl.when(pl.program_id(0) == 0)
    def _():
        units, columns = parts[0].shape[0], rows.shape[1]
        for index, ref in enumerate(parts[:3]):
            pair[index * units : (index + 1) * units] = ref[...]
        pair[3 * units :, :columns] = parts[3][...]
        pair[3 * units :, columns:] = parts[4][...]

    ff_kernel(rows, pair, activated, slope, part)


def ff_back_kernel(rows, slope, pair, grad_pre, part):
    columns = rows.shape[1]
    grad_act = contract(rows[...], pair[:, columns:], 1, 1)
    grad_pre[...] = (grad_act * slope[...].astype(f32)).astype(bf16)
    part[...] = contract(grad_pre[...], pair[:, :columns], 1, 0).astype(part.dtype)


def by_rows(kernel, step_rows, row_operands, whole_operands, outs, whole_outs=()):
    rows = row_operands[0].shape[0]
    return pl.pallas_call(
        kernel,
        grid=(rows // step_rows,),
        in_specs=[
            pl.BlockSpec((step_rows, operand.shape[1]), lambda step: (step, 0))
            for operand in row_operands
        ]
        + [whole(operand.shape) for operand in whole_operands],
        out_specs=[pl.BlockSpec((step_rows, columns), lambda step: (step, 0)) for columns, _ in outs]
        + [whole(shape) for shape in whole_outs],
        out_shape=[jax.ShapeDtypeStruct((rows, columns), kind) for columns, kind in outs]
        + [jax.ShapeDtypeStruct(shape, bf16) for shape in whole_outs],
        compiler_params=pltpu.CompilerParams(vmem_limit_bytes=10 * 2**20),
        cost_estimate=pl.CostEstimate(
            flops=4 * rows * outs[0][0] * row_operands[0].shape[1],
            bytes_accessed=6 * 2**20,
            transcendentals=0,
        ),
    )(*row_operands, *whole_operands)


def ff_grads_kernel(
    pre_near, pre_far, act_near, act_far, normed_near, normed_far, low_near, low_far, *outs
):
    columns = normed_near.shape[1]
    units = outs[0].shape[0]
    up = (
        contract(pre_near[...], normed_near[...], 0, 0)
        + contract(pre_far[...], normed_far[...], 0, 0)
    ).astype(bf16)
    down = (
        contract(act_near[...], low_near[...], 0, 0) + contract(act_far[...], low_far[...], 0, 0)
    ).astype(bf16)

    @pl.when(pl.program_id(0) == 0)
    def _():
        for index in range(2):
            block = slice(index * units, (index + 1) * units)
            outs[index][:, :columns] = up[block]
            outs[index][:, columns:] = down[block]

    @pl.when(pl.program_id(0) == 1)
    def _():
        outs[2][:, :columns] = up[:units]
        outs[2][:, columns:] = down[:units]
        outs[3][...] = up[units:]
        outs[4][...] = down[units:]


def ff_grads(pre, act, normed, low):
    rows, hidden_units = pre[0].shape
    columns = normed[0].shape[1]
    shapes = [(hidden_units // 4, 2 * columns)] * 3 + [(hidden_units // 4, columns)] * 2
    return pl.pallas_call(
        ff_grads_kernel,
        grid=(2,),
        in_specs=[pl.BlockSpec((rows, hidden_units // 2), lambda step: (0, step))] * 4
        + [whole((rows, columns))] * 4,
        out_specs=[whole(shape) for shape in shapes],
        out_shape=[jax.ShapeDtypeStruct(shape, bf16) for shape in shapes],
        compiler_params=pltpu.CompilerParams(vmem_limit_bytes=14 * 2**20),
        cost_estimate=pl.CostEstimate(
            flops=8 * rows * hidden_units * columns, bytes_accessed=8 * 2**20, transcendentals=0
        ),
    )(*pre, *act, *normed, *low)


def in_grads_kernel(place, near, far, grad_qkv, *refs):
    ends, outs, (total, extra) = refs[:-6], refs[-6:-2], refs[-2:]
    half = near.shape[0]
    columns = grad_qkv.shape[1]
    total[:, :columns] = (
        contract(near[...], grad_qkv[:half], 0, 0) + contract(far[...], grad_qkv[half:], 0, 0)
    ).astype(bf16)
    rows = outs[0].shape[0] // 8
    if ends:
        gain_0, gain_1, table_0, table_1 = ends
        lines = lax.broadcasted_iota(jnp.int32, (tile, gain_0.shape[1]), 0)
        gains = jnp.where(lines == 0, gain_0[...], jnp.where(lines == 1, gain_1[...], 0.0))
        extra[...] = jnp.transpose(gains)
        table = table_0[...] + table_1[...]
        buckets = table.shape[0] // 8
        blank = jnp.zeros((8 - buckets, tile), f32)
        for block in range(8):
            row = pl.multiple_of((place[0] // 2 * 8 + block) * rows, rows)
            extra[pl.ds(row, 8)] += jnp.concatenate(
                [table[block * buckets : (block + 1) * buckets], blank]
            )
        total[:, columns:] = extra[...].astype(bf16)
    for out, offset in zip(outs, (0, 3, 1, 2)):
        plane = (place[8] + offset) % 4
        for index in range(8):
            owner = place[index]
            row = row_of(owner // 2, plane, owner % 2, rows)
            out[index * rows : (index + 1) * rows] = total[pl.ds(row, rows)]


def in_grads(place, near, far, grad_qkv, *ends):
    columns = grad_qkv.shape[1] + (tile if ends else 0)
    shape = (near.shape[1] // 4, columns)
    return pl.pallas_call(
        in_grads_kernel,
        in_specs=[pl.BlockSpec(memory_space=pltpu.SMEM)]
        + [pl.BlockSpec(memory_space=pltpu.VMEM)] * (3 + len(ends)),
        out_specs=[pl.BlockSpec(memory_space=pltpu.VMEM)] * 4,
        out_shape=[jax.ShapeDtypeStruct(shape, bf16)] * 4,
        scratch_shapes=[
            pltpu.VMEM((near.shape[1], columns), bf16),
            pltpu.VMEM((near.shape[1], tile), f32),
        ],
        compiler_params=pltpu.CompilerParams(vmem_limit_bytes=12 * 2**20),
        cost_estimate=pl.CostEstimate(
            flops=4 * near.shape[0] * near.shape[1] * columns,
            bytes_accessed=4 * 2**20,
            transcendentals=0,
        ),
    )(place, near, far, grad_qkv, *ends)


def add_in_kernel(*refs):
    near, far = refs[-2:]
    half, at = near.shape[0], 0
    for layer_id in range(len(refs) // 4):
        parts = refs[4 * layer_id : 4 * layer_id + 4]
        total = sum_of_four(parts).astype(bf16)
        columns = slice(at, at + parts[0].shape[1])
        near[:, columns] = total[:half]
        far[:, columns] = total[half:]
        at = columns.stop


def combine_kernel(near_part, arrived, own, x_part, y_part, xy_part):
    rows = own.shape[0]
    own[...] = near_part[:rows] + arrived[:rows].astype(f32)
    for bits, out in ((1, x_part), (2, y_part), (3, xy_part)):
        block = slice(bits * rows, (bits + 1) * rows)
        out[...] = (near_part[block] + arrived[block].astype(f32)).astype(bf16)


def added(own, x_part, y_part, xy_part):
    return (own[...] + x_part[...].astype(f32)) + (
        y_part[...].astype(f32) + xy_part[...].astype(f32)
    )


def close_kernel(kept, own, x_part, y_part, xy_part, hidden, units):
    total = kept[...] + added(own, x_part, y_part, xy_part)
    hidden[...] = total
    units[...] = (total * inverse_rms(total)).astype(bf16)


def close_gain_kernel(kept, own, x_part, y_part, xy_part, gain, hidden, normed):
    total = kept[...] + added(own, x_part, y_part, xy_part)
    hidden[...] = total
    normed[...] = (total * inverse_rms(total) * gain[...]).astype(bf16)


def last_kernel(kept, own, x_part, y_part, xy_part, hidden):
    hidden[...] = (kept[...] + added(own, x_part, y_part, xy_part)).astype(bf16)


def middle_back_kernel(
    upstream, own, x_part, y_part, xy_part, middle, gain, grad_middle, branch, grad_gain
):
    grad_normed = added(own, x_part, y_part, xy_part)
    inverse = inverse_rms(middle[...])
    grad_gain[...] = jnp.sum(grad_normed * middle[...] * inverse, axis=0, keepdims=True)
    total = upstream[...].astype(f32) + unit_norm_back(
        middle[...], inverse, grad_normed * gain[...]
    )
    grad_middle[...] = total
    branch[...] = total.astype(bf16)


def layer_back_kernel(grad_middle, own, x_part, y_part, xy_part, hidden, upstream, low):
    total = grad_middle[...] + unit_norm_back(
        hidden[...], inverse_rms(hidden[...]), added(own, x_part, y_part, xy_part)
    )
    upstream[...] = total
    low[...] = total.astype(bf16)


def pair_kernel(axis, near, arrived, *outs):
    rows = near.shape[0] // len(outs)
    for index, out in enumerate(outs):
        block = slice(index * rows, (index + 1) * rows)
        if axis == 0:
            out[:rows] = near[block]
            out[rows:] = arrived[block]
        else:
            columns = near.shape[1]
            out[:, :columns] = near[block]
            out[:, columns:] = arrived[block]


def unit_kernel(tokens, hidden, units):
    total = tokens[...].astype(f32)
    hidden[...] = total
    units[...] = (total * inverse_rms(total)).astype(bf16)


def finish_in_kernel(layers, place, *refs):
    shares, (attn_in, gains, grad_in, grad_gain, ends) = refs[:4], refs[4:]
    rows = attn_in.shape[1]
    width = shares[0].shape[1] // 14
    members = attn_in.shape[2] // (3 * width)
    for layer_id in range(layers):
        row_dot = jnp.zeros((rows, 1), f32)
        for index in range(members):
            share = shares[index % 4]
            first = (index // 4 * 7 + layer_id * 4) * width
            member = place[index]
            for part in range(3):
                block = share[:, first + part * width : first + (part + 1) * width].astype(f32)
                columns = pl.ds(pl.multiple_of((part * members + member) * width, width), width)
                grad_in[layer_id, :, columns] = block * gains[layer_id]
                row_dot = row_dot + jnp.sum(
                    block * attn_in[layer_id, :, columns].astype(f32), axis=1, keepdims=True
                )
            if layer_id == 0:
                block = share[:, first + 3 * width : first + 4 * width].astype(f32)
                ends[...] = block if index == 0 else ends[...] + block
        grad_gain[layer_id] = jnp.concatenate(
            [row_dot, ends[:, layer_id : layer_id + 1]], axis=1
        )


def sum_of_four(parts):
    return (parts[0][...].astype(f32) + parts[1][...].astype(f32)) + (
        parts[2][...].astype(f32) + parts[3][...].astype(f32)
    )


def finish_ff_kernel(*refs):
    count = (len(refs) - 3) // 2
    sources, grads, held, done = refs[:count], refs[count : count + 2], refs[count + 2 : -1], refs[-1]
    copies = [
        pltpu.make_async_copy(source, target, done.at[index])
        for index, (source, target) in enumerate(zip(sources, held))
    ]
    for copy in copies:
        copy.start()
    for copy in copies:
        copy.wait()
    refs = held
    columns = grads[0].shape[2]
    for layer_id in range(grads[0].shape[0]):
        parts = refs[5 * layer_id : 5 * layer_id + 5]
        for side, out in enumerate(grads):
            halves = [part.at[:, side * columns : (side + 1) * columns] for part in parts[:3]]
            out[layer_id] = sum_of_four(halves + [parts[3 + side]])


def finish_ff(grads, shape):
    return pl.pallas_call(
        finish_ff_kernel,
        in_specs=[pl.BlockSpec(memory_space=pl.ANY)] * len(grads),
        out_specs=[pl.BlockSpec(memory_space=pltpu.VMEM)] * 2,
        out_shape=[jax.ShapeDtypeStruct(shape, f32)] * 2,
        scratch_shapes=[pltpu.VMEM(grad.shape, bf16) for grad in grads]
        + [pltpu.SemaphoreType.DMA((len(grads),))],
        compiler_params=pltpu.CompilerParams(vmem_limit_bytes=14 * 2**20),
    )(*grads)


def add_out_kernel(place, *refs):
    parts, (own, other) = refs[:-2], refs[-2:]
    both = parts[0][...].astype(f32) + parts[1][...].astype(f32)
    for layer_id in range(own.shape[0]):
        rows = own.shape[1]
        total = both[2 * layer_id * rows : 2 * (layer_id + 1) * rows]
        second = place[0] % 2 == 1
        own[layer_id] = jnp.where(second, total[rows:], total[:rows])
        other[layer_id] = jnp.where(second, total[:rows], total[rows:]).astype(bf16)


def finish_out_kernel(own, arrived, out):
    out[...] = own[...] + arrived[...].astype(f32)


def inverse_rms(hidden):
    return lax.rsqrt(jnp.mean(hidden * hidden, axis=-1, keepdims=True) + epsilon)


def prepare(bias_table, first_head, heads_dev):
    table = lax.dynamic_slice_in_dim(bias_table, first_head, heads_dev, 1)
    (near,) = call(near_kernel, [((heads_dev, tile, 3 * tile), f32)], table, smem=1)
    return table, near


def bucket_grads(first_lane, grads, bucket_count):
    (total,) = call(bucket_kernel, [((bucket_count, tile), f32)], first_lane, *grads, smem=1)
    return total


def gelu_parts(pre_act):
    cumulative = 0.5 * (1.0 + lax.erf(pre_act * np.float32(0.5**0.5)))
    slope = cumulative + pre_act * jnp.exp(-0.5 * pre_act * pre_act) * np.float32(
        (2 * np.pi) ** -0.5
    )
    return (pre_act * cumulative).astype(bf16), slope


def unit_norm_back(hidden, inverse, grad_unit):
    unit = hidden * inverse
    return inverse * (grad_unit - unit * jnp.mean(grad_unit * unit, axis=-1, keepdims=True))


def gather_rows(block, axes):
    return lax.all_gather(block, axes, axis=0, tiled=True)


def toggle(array, axis, bits):
    return lax.ppermute(array, axis, [(i, i ^ bits) for i in range(lax.axis_size(axis))])


def shift(array, by):
    planes = lax.axis_size("z")
    return lax.ppermute(array, "z", [(i, (i + by) % planes) for i in range(planes)])


def plane_gather(block, *holds):
    near = jnp.concatenate([block] + [toggle(block, "head", bits) for bits in (1, 2, 3)])
    near, *holds = tie(near, *holds)
    return (near, toggle(near, "core", 1), *holds)


def plane_scatter(near_part, far_part):
    rows, columns = near_part.shape[0] // 4, near_part.shape[1]
    own, *others = call(
        combine_kernel,
        [((rows, columns), f32)] + [((rows, columns), bf16)] * 3,
        near_part,
        toggle(far_part, "core", 1),
    )
    shares = [own] + [toggle(other, "head", bits) for bits, other in zip((1, 2, 3), others)]
    return shares, own


def tie(*arrays):
    return lax.optimization_barrier(arrays)


def after(array, other):
    return lax.optimization_barrier((array, other))[0]


def scatter_sum(partial, axes, members):
    blocks = partial.astype(bf16).reshape(members, -1, partial.shape[1])
    return jnp.sum(lax.all_to_all(blocks, axes, 0, 0, tiled=True).astype(f32), axis=0)


def local_general(tokens, doc_start, bias_table, attn_in, attn_out, ff_in, ff_out, gains, cotangent):
    heads_n, z_n, core_n = (lax.axis_size(axis) for axis in everyone)
    devices = heads_n * z_n * core_n
    group, spare = ("z", "core"), "head"
    ff_group, ff_spare, ff_members = ("head", "core"), "z", heads_n * core_n
    blocks = z_n * core_n
    block_rows, model_width = tokens.shape[1:]
    layer_count, weight_rows = attn_in.shape[:2]
    length = block_rows * blocks
    heads_all = bias_table.shape[1]
    member = lax.axis_index("z") * core_n + lax.axis_index("core")
    heads_dev = max(1, heads_all // blocks)
    head_groups = heads_all // heads_dev
    split = blocks // head_groups
    head_group, query_part = member // split, member % split
    query_rows = length // split
    width = heads_dev * head_dim
    first = (query_part * (query_rows // tile)).astype(jnp.int32).reshape(1)
    place = jnp.arange(length // tile, dtype=jnp.int32)
    out_row = head_group * width

    def swap(array):
        return lax.all_to_all(array, everyone, 0, 0, tiled=True)

    starts = jnp.broadcast_to(
        doc_start.astype(f32)[:, None], (heads_n, blocks, block_rows)
    ).reshape(devices, block_rows)
    ff_gains = gains[:, :, 1].astype(f32).reshape(1, -1)
    small = swap(
        jnp.concatenate(
            [starts, jnp.broadcast_to(ff_gains, (devices, layer_count * weight_rows))], axis=1
        )
    )
    doc_row = small[:blocks, :block_rows].reshape(1, length)
    doc_col = lax.dynamic_slice_in_dim(
        doc_row.reshape(length, 1), query_part * query_rows, query_rows, 0
    )
    gain_ff = jnp.transpose(
        small[:, block_rows:].reshape(devices, layer_count, weight_rows), (1, 0, 2)
    ).reshape(layer_count, 1, model_width)
    table, near = prepare(bias_table, head_group * heads_dev, heads_dev)

    gain_attn = gains[:, :, 0].astype(f32)[:, :, None]
    own_in = attn_in.astype(f32)

    def fetch_in(layer_id):
        scaled = (own_in[layer_id] * gain_attn[layer_id]).astype(bf16)
        columns = jnp.transpose(
            scaled.reshape(weight_rows, 3, head_groups, width), (2, 0, 1, 3)
        ).reshape(head_groups, weight_rows, 3 * width)
        columns = jnp.repeat(columns, split, axis=0)
        columns = jnp.broadcast_to(columns[None], (heads_n, *columns.shape))
        return swap(columns.reshape(devices, weight_rows, 3 * width)).reshape(
            model_width, 3 * width
        )

    def fetch_ff(layer_id):
        pair = jnp.concatenate([ff_in[layer_id], ff_out[layer_id]], axis=1)
        pair = gather_rows(pair, ff_spare)
        return pair[:, :model_width], pair[:, model_width:]

    hidden, upstream = tokens[0].astype(f32), cotangent[0]
    weights_in = [fetch_in(layer_id) for layer_id in range(layer_count)]
    weights_out = lax.dynamic_slice_in_dim(
        lax.all_gather(attn_out, everyone, axis=1, tiled=True), out_row, width, 1
    )
    weights_ff = [fetch_ff(layer_id) for layer_id in range(layer_count)]

    records = []
    for layer_id in range(layer_count):
        w_in, w_out, (w_up, w_down) = (
            weights_in[layer_id], weights_out[layer_id], weights_ff[layer_id],
        )
        inverse = inverse_rms(hidden)
        units = gather_rows((hidden * inverse).astype(bf16), group)
        qkv = jnp.dot(units, w_in, preferred_element_type=f32).astype(bf16)
        attended, _, stats = attention(
            qkv, doc_row, doc_col, first, place, table, near, query_rows
        )
        mixed = jnp.dot(attended, w_out, preferred_element_type=f32)
        if split > 1:
            mixed = lax.dynamic_update_slice_in_dim(
                jnp.zeros((length, model_width), f32), mixed, query_part * query_rows, 0
            )
        middle = hidden + scatter_sum(mixed, group, blocks)
        inverse_ff = inverse_rms(middle)
        normed_ff = gather_rows((middle * inverse_ff * gain_ff[layer_id]).astype(bf16), ff_group)
        activated, slope = gelu_parts(contract(normed_ff, w_up, 1, 1))
        ff_result = jnp.dot(activated, w_down, preferred_element_type=f32)
        records.append(
            (hidden, inverse, units, qkv, attended, stats, middle, inverse_ff, normed_ff,
             activated, slope)
        )
        hidden = middle + scatter_sum(ff_result, ff_group, ff_members)
    output = hidden

    grads_ff, grads_in, grads_out, grads_gain_ff, grads_table = (
        [None] * layer_count for _ in range(5)
    )
    for layer_id in reversed(range(layer_count)):
        w_in, w_out, (w_up, w_down) = (
            weights_in[layer_id], weights_out[layer_id], weights_ff[layer_id],
        )
        (hidden, inverse, units, qkv, attended, stats, middle, inverse_ff, normed_ff,
         activated, slope) = records[layer_id]
        grad_low = gather_rows(upstream.astype(bf16), ff_group)
        grad_pre = (contract(grad_low, w_down, 1, 1) * slope).astype(bf16)
        grad_normed = scatter_sum(
            jnp.dot(grad_pre, w_up, preferred_element_type=f32), ff_group, ff_members
        )
        grad_pair = jnp.concatenate(
            [contract(grad_pre, normed_ff, 0, 0), contract(activated, grad_low, 0, 0)], axis=1
        ).astype(bf16)
        grads_ff[layer_id] = lax.psum_scatter(
            grad_pair, ff_spare, scatter_dimension=0, tiled=True
        ).astype(f32)
        grads_gain_ff[layer_id] = jnp.sum(grad_normed * middle * inverse_ff, axis=0)
        grad_middle = upstream + unit_norm_back(
            middle, inverse_ff, grad_normed * gain_ff[layer_id]
        )
        branch = gather_rows(grad_middle.astype(bf16), group)
        if split > 1:
            branch = lax.dynamic_slice_in_dim(branch, query_part * query_rows, query_rows, 0)
        grad_attended = contract(branch, w_out, 1, 1).astype(bf16)
        grad_qkv, grad_near, grad_far = attention_back(
            qkv, doc_row, doc_col, attended, grad_attended, stats, first, place, table, near, split
        )
        grads_table[layer_id] = (grad_near, grad_far)
        grad_units = scatter_sum(contract(grad_qkv, w_in, 1, 1), group, blocks)
        upstream = grad_middle + unit_norm_back(hidden, inverse, grad_units)
        grad_out = lax.dynamic_update_slice_in_dim(
            jnp.zeros((model_width, model_width), bf16),
            contract(attended, branch, 0, 0).astype(bf16),
            out_row,
            0,
        )
        grads_out[layer_id] = lax.psum_scatter(
            grad_out, everyone, scatter_dimension=0, tiled=True
        ).astype(f32)
        grads_in[layer_id] = contract(units, grad_qkv, 0, 0).astype(bf16)

    bucket_count = table.shape[0]
    grad_table = sum(
        bucket_grads(jnp.zeros((1,), jnp.int32), entry, bucket_count) for entry in grads_table
    )[:, :heads_dev]
    grad_table = lax.dynamic_update_slice_in_dim(
        jnp.zeros((bucket_count, heads_all), f32), grad_table, head_group * heads_dev, 1
    )
    grad_table = jnp.transpose(
        grad_table.reshape(blocks, bucket_count // blocks, heads_n, heads_all // heads_n),
        (2, 0, 1, 3),
    ).reshape(devices, -1)
    grad_gain_ff = jnp.transpose(
        jnp.stack(grads_gain_ff).reshape(layer_count, devices, weight_rows), (1, 0, 2)
    ).reshape(devices, -1)
    ends = jnp.sum(swap(jnp.concatenate([grad_gain_ff, grad_table], axis=1)), axis=0)
    grad_gain_ff = ends[: layer_count * weight_rows].reshape(layer_count, weight_rows)
    grad_bias_table = ends[layer_count * weight_rows :].reshape(
        bucket_count // blocks, heads_all // heads_n
    )
    grads_attn_in, grads_gains = [], []
    for layer_id in range(layer_count):
        parts = swap(grads_in[layer_id].reshape(devices, weight_rows, 3 * width)).astype(f32)
        parts = jnp.sum(parts.reshape(heads_n, blocks, weight_rows, 3 * width), axis=0)
        parts = jnp.sum(parts.reshape(head_groups, split, weight_rows, 3, width), axis=1)
        unit_grad = jnp.transpose(parts, (1, 2, 0, 3)).reshape(weight_rows, 3 * model_width)
        grads_attn_in.append(unit_grad * gain_attn[layer_id])
        grads_gains.append(
            jnp.stack(
                [jnp.sum(unit_grad * own_in[layer_id], axis=1), grad_gain_ff[layer_id]], axis=1
            )
        )
    return (
        output[None],
        upstream[None],
        jnp.stack(grads_attn_in),
        jnp.stack(grads_out),
        jnp.stack([entry[:, :model_width] for entry in grads_ff]),
        jnp.stack([entry[:, model_width:] for entry in grads_ff]),
        jnp.stack(grads_gains),
        grad_bias_table,
    )


def local_plane(tokens, doc_start, bias_table, attn_in, attn_out, ff_in, ff_out, gains, cotangent):
    heads_n, z_n, core_n = (lax.axis_size(axis) for axis in everyone)
    devices = heads_n * z_n * core_n
    at_head, at_z, at_core = (lax.axis_index(axis) for axis in everyone)
    members = heads_n * core_n
    block_rows, model_width = tokens.shape[1:]
    layer_count, weight_rows = attn_in.shape[:2]
    length = block_rows * members
    heads_all = bias_table.shape[1]
    heads_dev = heads_all // members
    width = heads_dev * head_dim
    member = at_head * core_n + at_core
    turn = [
        ((h * z_n + z) * core_n + c, ((h ^ z) * z_n + h) * core_n + c)
        for h in range(heads_n)
        for z in range(z_n)
        for c in range(core_n)
    ]
    everywhere = [(h, z, c) for h in range(heads_n) for z in range(z_n) for c in range(core_n)]

    def device(h, z, c):
        return (h * z_n + z) * core_n + c

    plane_turn = [(device(h, z, c), device(h ^ z, z, c)) for h, z, c in everywhere]
    line_turn = [(device(h, z, c), device(h, z ^ h, c)) for h, z, c in everywhere]
    place = jnp.stack(
        [
            (at_head ^ bits) * core_n + (at_core ^ other)
            for other in range(core_n)
            for bits in range(heads_n)
        ]
        + [at_z]
        + [
            (at_head ^ bits ^ at_z) * core_n + (at_core ^ other)
            for other in range(core_n)
            for bits in range(heads_n)
        ]
    ).astype(jnp.int32)

    def relay(array):
        return lax.ppermute(array, everyone, turn)

    def turn_in_plane(array):
        return lax.ppermute(array, everyone, plane_turn)

    def turn_in_line(array):
        return lax.ppermute(array, everyone, line_turn)

    def swap(array):
        return lax.all_to_all(array, everyone, 0, 0, tiled=True)

    row_shape = (block_rows, model_width)
    gain_attn = gains[:, :, 0].astype(f32)[:, :, None]
    near_share, far_share = call(
        share_in_kernel,
        [((members // 2 * layer_count * weight_rows, 3 * width), bf16)] * 2,
        place,
        attn_in,
        gain_attn,
        smem=1,
    )

    half_turns = [
        [
            (z * core_n + c, (2 * c + (a ^ z % 2)) * core_n + z // 2)
            for z in range(z_n)
            for c in range(core_n)
        ]
        for a in range(2)
    ]

    def fetch_out(layer_id, hold):
        own = attn_out[layer_id]
        other = toggle(own, "core", 1)
        head = jnp.where(
            at_core == 0, jnp.concatenate([own, other]), jnp.concatenate([other, own])
        )
        head = after(head, hold)
        return [
            lax.ppermute(head, ("z", "core"), [(holder, user) for user, holder in turns])
            for turns in half_turns
        ]

    def owners_halves(halves):
        return [
            lax.ppermute(half, ("z", "core"), turns) for half, turns in zip(halves, half_turns)
        ]

    def pair_chips(near, arrived, axis):
        rows, columns = near.shape[0] // 4, near.shape[1]
        shape = (2 * rows, columns) if axis == 0 else (rows, 2 * columns)
        return call(functools.partial(pair_kernel, axis), [(shape, bf16)] * 4, near, arrived)

    def share_chips(blocks):
        return [blocks[0]] + [toggle(blocks[bits], "head", bits) for bits in (1, 2, 3)]

    units_shape = [(row_shape, f32), (row_shape, bf16)]

    starts = jnp.broadcast_to(
        doc_start.astype(f32)[None, :, None], (heads_n, z_n, core_n, block_rows)
    )
    ff_gains = gains[:, :, 1].astype(f32).reshape(1, -1)
    small = jnp.concatenate(
        [
            starts.reshape(devices, block_rows),
            jnp.broadcast_to(ff_gains, (devices, layer_count * weight_rows)),
        ],
        axis=1,
    )
    table, strip = prepare(bias_table, member * heads_dev, heads_dev)
    hidden, strip = tie(relay(tokens[0]), strip)
    hidden, shares, cotangent_low, halves, small = tie(
        hidden,
        share_chips(pair_chips(near_share, toggle(far_share, "core", 1), 0)),
        turn_in_plane(after(cotangent[0].astype(bf16), near_share)),
        fetch_out(0, near_share),
        swap(after(small, near_share)),
    )
    hidden, unit_rows = call(unit_kernel, units_shape, hidden)
    doc_row = small[:members, :block_rows].reshape(2, 2, core_n, block_rows)
    at_block = at_head ^ at_z
    for axis, bit in ((0, at_block // 2), (1, at_block % 2), (2, at_core)):
        doc_row = jnp.where(bit == 1, jnp.flip(doc_row, axis), doc_row)
    doc_row = jnp.transpose(doc_row, (2, 0, 1, 3)).reshape(1, length)
    doc_col = doc_row.reshape(length, 1)
    gain_ff = jnp.transpose(
        small[:, block_rows:].reshape(devices, layer_count, weight_rows), (1, 0, 2)
    ).reshape(layer_count, 1, model_width)

    def round_planes(array, by, hold):
        return shift(after(array, hold), by)

    ff_pairs = [
        jnp.concatenate([ff_in[layer_id], ff_out[layer_id]], axis=1) for layer_id in range(layer_count)
    ]

    def ff_both(kernel, row_operands, pair, columns):
        return zip(
            *(
                by_rows(
                    kernel,
                    256,
                    operands,
                    [pair],
                    [(pair.shape[0], bf16)] * columns + [(model_width, kind)],
                )
                for operands, kind in zip(zip(*row_operands), (f32, bf16))
            )
        )

    def ff_forward(normed, *parts):
        units = 4 * parts[0].shape[0]
        outs = [(units, bf16), (units, bf16)]
        *near, pair = by_rows(
            ff_first_kernel,
            256,
            [normed[0]],
            parts,
            outs + [(model_width, f32)],
            [(units, 2 * model_width)],
        )
        far = by_rows(ff_kernel, 256, [normed[1]], [pair], outs + [(model_width, bf16)])
        return pair, *zip(near, far)

    def ff_backward(low, slopes, pair):
        return ff_both(ff_back_kernel, [low, slopes], pair, 1)

    def assemble_in(share, lower, upper, opposite):
        return call(
            assemble_in_kernel,
            [((model_width, 3 * width), bf16)],
            place,
            share,
            lower,
            upper,
            opposite,
            smem=1,
        )[0]

    share, later_share = call(
        join_kernel, [((members * weight_rows, 3 * width), bf16)] * layer_count, *shares
    )
    near, far, lower, upper, opposite, doc_row, doc_col, gain_ff, *ff_pairs = plane_gather(
        unit_rows,
        shift(share, 1),
        shift(share, -1),
        shift(share, 2),
        doc_row,
        doc_col,
        gain_ff,
        *ff_pairs,
    )
    w_in = assemble_in(share, lower, upper, opposite)
    far, lower = tie(far, shift(ff_pairs[0], 1))
    units = (near, far)
    w_out, qkv, attended, stats, *parts = plane_attention(
        *units, w_in, halves, doc_row, doc_col, place, table, strip
    )
    parts, upstream, upper = tie(
        parts, turn_in_line(after(cotangent_low, near)), round_planes(ff_pairs[0], -1, far)
    )
    parts, own = plane_scatter(*parts)
    parts, opposite_in = tie(parts, round_planes(ff_in[0], 2, own))
    middle, normed_rows = call(close_gain_kernel, units_shape, hidden, *parts, gain_ff[0])
    *normed, opposite_out = plane_gather(normed_rows, round_planes(ff_out[0], 2, normed_rows))
    pair, acts, slopes, parts = ff_forward(
        normed, ff_pairs[0], lower, upper, opposite_in, opposite_out
    )
    records = [
        (hidden, units, w_in, w_out, pair, qkv, attended, stats, middle, normed, acts, slopes)
    ]
    parts, lower, upper = tie(
        parts,
        round_planes(later_share, 1, normed[0]),
        round_planes(later_share, -1, normed[0]),
    )
    parts, own = plane_scatter(*parts)
    parts, opposite = tie(parts, round_planes(later_share, 2, own))
    shares = [later_share, lower, upper, opposite]
    hidden, unit_rows = call(close_kernel, units_shape, middle, *parts)

    near, far, lower, halves = plane_gather(
        unit_rows, round_planes(ff_pairs[1], 1, unit_rows), fetch_out(1, unit_rows)
    )
    units = (near, far)
    w_in = assemble_in(*shares)
    w_out, qkv, attended, stats, *parts = plane_attention(
        *units, w_in, halves, doc_row, doc_col, place, table, strip
    )
    low = plane_gather(after(upstream, far))
    parts, near_low, upper = tie(parts, low[0], round_planes(ff_pairs[1], -1, far))
    low = (near_low, low[1])
    parts, own = plane_scatter(*parts)
    parts, opposite_in = tie(parts, round_planes(ff_in[1], 2, own))
    middle, normed_rows = call(close_gain_kernel, units_shape, hidden, *parts, gain_ff[1])
    *normed, opposite_out = plane_gather(normed_rows, round_planes(ff_out[1], 2, normed_rows))
    pair, acts, slopes, last_parts = ff_forward(
        normed, ff_pairs[1], lower, upper, opposite_in, opposite_out
    )
    records.append(
        (hidden, units, w_in, w_out, pair, qkv, attended, stats, middle, normed, acts, slopes)
    )

    def back_to_middle(parts, upstream, middle, gain):
        return call(
            middle_back_kernel, units_shape + [((1, model_width), f32)], upstream, *parts, middle, gain
        )

    def attention_grads(record, branch):
        _, _, w_in, w_out, _, qkv, attended, stats, *_ = record
        grad_qkv, grad_near, grad_far, near_part, far_part, *halves = plane_attention_back(
            qkv, doc_row, doc_col, attended, stats, *branch, w_in, w_out, place, table, strip
        )
        return grad_qkv, (grad_near, grad_far), (near_part, far_part), halves

    def table_grads(near_and_far):
        return bucket_grads(at_core.reshape(1) * heads_dev + 8, near_and_far, table.shape[0])

    record = records[1]
    hidden, units, _, _, pair, *_, middle, normed, acts, slopes = record
    pres, parts = ff_backward(low, slopes, pair)
    parts, own = plane_scatter(*parts)
    planes = ff_grads(after(pres, own), acts, normed, low)
    parts, ff_lower = tie(parts, shift(planes[1], -1))
    last_parts, _ = plane_scatter(*after(last_parts, parts))
    grad_middle, branch_rows, gain_1 = back_to_middle(parts, upstream, middle, gain_ff[1])
    *branch, ff_upper = plane_gather(branch_rows, round_planes(planes[2], 1, branch_rows))
    grad_qkv, strips_1, parts, halves_1 = attention_grads(record, branch)
    parts, last_parts, opposite_up = tie(
        parts, last_parts, round_planes(planes[3], 2, branch[1])
    )
    parts, own = plane_scatter(*parts)
    parts, opposite_down, output = tie(
        parts,
        round_planes(planes[4], 2, own),
        call(last_kernel, [(row_shape, bf16)], middle, *after(last_parts, own))[0],
    )
    grads_ff = [planes[0], ff_lower, ff_upper, opposite_up, opposite_down]
    upstream, low_rows = call(layer_back_kernel, units_shape, grad_middle, *parts, hidden)

    record = records[0]
    hidden, units, _, _, pair, *_, middle, normed, acts, slopes = record
    grad_in = in_grads(place, *records[1][1], after(grad_qkv, low_rows))
    *low, in_opposite, table_1 = plane_gather(
        low_rows, shift(grad_in[3], 2), table_grads(after(strips_1, low_rows))
    )
    pres, parts = ff_backward(low, slopes, pair)
    parts, in_lower, in_upper = tie(
        parts, round_planes(grad_in[1], -1, low[0]), round_planes(grad_in[2], 1, low[0])
    )
    parts, own = plane_scatter(*parts)
    planes = ff_grads(after(pres, own), acts, normed, low)
    parts, ff_lower = tie(parts, shift(planes[1], -1))
    grad_middle, branch_rows, gain_0 = back_to_middle(parts, upstream, middle, gain_ff[0])
    *branch, ff_upper = plane_gather(branch_rows, round_planes(planes[2], 1, branch_rows))
    shares_1 = [grad_in[0], in_lower, in_upper, in_opposite]
    grad_qkv, strips_0, parts, halves_0 = attention_grads(record, branch)
    parts, output, opposite_up = tie(
        parts, turn_in_line(after(output, branch[1])), round_planes(planes[3], 2, branch[1])
    )
    parts, own = plane_scatter(*parts)
    table_0 = table_grads(after(strips_0, parts[1]))
    grad_in = in_grads(
        place, *units, after(grad_qkv, parts[1]), gain_0, gain_1, table_0, table_1
    )
    parts, opposite_down, in_opposite, *halves = tie(
        parts,
        round_planes(planes[4], 2, own),
        shift(grad_in[3], 2),
        *(jnp.concatenate(after(pair, parts[1])) for pair in zip(halves_0, halves_1)),
    )
    upstream, low_rows = call(layer_back_kernel, units_shape, grad_middle, *parts, hidden)
    in_lower = round_planes(grad_in[1], -1, low_rows)
    in_upper = round_planes(grad_in[2], 1, low_rows)
    grad_tokens = turn_in_line(low_rows)
    columns = grad_in[0].shape[1] + shares_1[0].shape[1]
    near_in, far_in = call(
        add_in_kernel,
        [((members // 2 * weight_rows, columns), bf16)] * 2,
        grad_in[0],
        in_lower,
        in_upper,
        in_opposite,
        *shares_1,
    )
    arrived = toggle(far_in, "core", 1)
    halves = owners_halves(after(halves, arrived))
    shares_in = share_chips(pair_chips(near_in, arrived, 1))
    grad_tokens = turn_in_plane(grad_tokens)
    output = turn_in_plane(after(output, arrived)).astype(f32)
    grads_ff = [planes[0], ff_lower, ff_upper, opposite_up, opposite_down] + grads_ff
    grad_up, grad_down = finish_ff(after(grads_ff, near_in), ff_in.shape)
    own_out, other_out = call(
        add_out_kernel,
        [(attn_out.shape, f32), (attn_out.shape, bf16)],
        place,
        *after(halves, shares_in[1]),
        smem=1,
    )
    (grad_attn_out,) = call(
        finish_out_kernel, [(attn_out.shape, f32)], own_out, toggle(other_out, "core", 1)
    )
    own_buckets = table.shape[0] // (z_n * core_n)
    grad_attn_in, grad_gains, ends = call(
        functools.partial(finish_in_kernel, layer_count),
        [(attn_in.shape, f32), (gains.shape, f32), ((weight_rows, tile), f32)],
        place,
        *shares_in,
        attn_in,
        gain_attn,
        smem=1,
    )
    return (
        output[None],
        grad_tokens.astype(f32)[None],
        grad_attn_in,
        grad_attn_out,
        grad_up,
        grad_down,
        grad_gains,
        ends[:own_buckets, 8 : 8 + heads_all // heads_n],
    )


def solution(mesh):
    sizes = dict(mesh.shape)
    cores = 2
    fine = Mesh(
        mesh.devices.reshape(sizes["head"], sizes["blk"] // cores, cores), everyone
    )
    blk = ("z", "core")
    in_specs = (
        P("head", blk, None),
        P(None, blk),
        P(),
        P(None, everyone, None),
        P(None, everyone, None),
        P(None, everyone, None),
        P(None, everyone, None),
        P(None, everyone, None),
        P("head", blk, None),
    )
    out_specs = (
        P("head", blk, None),
        P("head", blk, None),
        P(None, everyone, None),
        P(None, everyone, None),
        P(None, everyone, None),
        P(None, everyone, None),
        P(None, everyone, None),
        P(blk, "head"),
    )
    plane = sizes["head"] == 4 and sizes["blk"] == 8
    local = local_plane if plane else local_general
    return jax.shard_map(local, mesh=fine, in_specs=in_specs, out_specs=out_specs, check_vma=False)
```

```python
import functools

import jax
import jax.numpy as jnp
import numpy as np
from jax import lax
from jax.experimental import pallas as pl
from jax.experimental.pallas import tpu as pltpu
from jax.sharding import Mesh
from jax.sharding import PartitionSpec as P

bounds = (1, 2, 3, 4, 5, 6, 7, 8, 12, 16, 23, 32, 46, 64, 91)
epsilon = 1e-06
masked = -1e30
score_scale = 0.125
head_dim = 64
tile = 128
everyone = ("head", "z", "core")
bf16 = jnp.bfloat16
f32 = jnp.float32


def contract(lhs, rhs, lhs_dim, rhs_dim):
    return lax.dot_general(
        lhs, rhs, (((lhs_dim,), (rhs_dim,)), ((), ())), preferred_element_type=f32
    )


def near_buckets(shape):
    offsets = (
        lax.broadcasted_iota(jnp.int32, shape, 1) - tile - lax.broadcasted_iota(jnp.int32, shape, 0)
    )
    distance = jnp.abs(offsets)
    bucket = jnp.where(offsets > 0, 16, 0)
    for boundary in bounds:
        bucket = bucket + jnp.where(distance >= boundary, 1, 0)
    return bucket


def near_kernel(table, near):
    bucket = near_buckets(near.shape[1:])
    for head in range(near.shape[0]):
        values = jnp.zeros(near.shape[1:], f32)
        for bucket_id in range(table.shape[0]):
            values = jnp.where(bucket == bucket_id, table[bucket_id, head], values)
        near[head] = values


def bucket_kernel(first_lane, near, far, out):
    bucket = near_buckets(near.shape[1:])
    rows = lax.broadcasted_iota(jnp.int32, out.shape, 0)
    lanes = lax.broadcasted_iota(jnp.int32, out.shape, 1)
    total = jnp.zeros(out.shape, f32)
    for head in range(near.shape[0]):
        strip = near[head]
        for bucket_id in range(out.shape[0]):
            value = jnp.sum(jnp.where(bucket == bucket_id, strip, 0.0), axis=0, keepdims=True)
            value = jnp.sum(value, axis=1, keepdims=True)
            if bucket_id in (15, 31):
                value = value + far[head, bucket_id // 16, :1, :1]
            total = jnp.where((rows == bucket_id) & (lanes == head + first_lane[0]), value, total)
    out[...] = total


def fill_band(band, table, near, heads_dev, length):
    for head in range(heads_dev):
        band[head, :, : length - tile] = jnp.full((tile, length - tile), table[15, head], f32)
        band[head, :, length - tile : length + 2 * tile] = near[head]
        band[head, :, length + 2 * tile :] = jnp.full(
            (tile, length - 2 * tile), table[31, head], f32
        )


def band_starts(place, at, length, skip=0):
    return [
        pl.multiple_of(length + (place[skip + block] - place[skip + at]) * tile, tile)
        for block in range(length // tile)
    ]


def attention_kernel(
    heads_dev, length, first, place, table, near, qkv, doc_row, doc_col, out, local, stats, band
):
    step = pl.program_id(0)
    width = heads_dev * head_dim

    @pl.when(step == 0)
    def _():
        fill_band(band, table, near, heads_dev, length)

    row = pl.multiple_of((first[0] + step) * tile, tile)
    out_row = pl.multiple_of((place[first[0] + step] - first[0]) * tile, tile)
    starts = band_starts(place, first[0] + step, length)
    same_doc = doc_col[...] == doc_row[...]
    queries = qkv[pl.ds(row, tile), :width] * bf16(score_scale)
    lanes = lax.broadcasted_iota(jnp.int32, (tile, tile), 1)
    collected = jnp.zeros((tile, tile), f32)
    for head in range(heads_dev):
        own = slice(head * head_dim, (head + 1) * head_dim)
        keys = qkv[:, width + own.start : width + own.stop]
        values = qkv[:, 2 * width + own.start : 2 * width + own.stop]
        scores = contract(queries[:, own], keys, 1, 1)
        scores = scores + jnp.concatenate(
            [band[head, :, pl.ds(start, tile)] for start in starts], axis=1
        )
        scores = jnp.where(same_doc, scores, masked)
        peak = jnp.max(scores, axis=1, keepdims=True)
        weights = jnp.exp(scores - peak)
        total = jnp.sum(weights, axis=1, keepdims=True)
        mixed = contract(weights.astype(bf16), values, 1, 0) / total
        out[pl.ds(out_row, tile), own] = mixed.astype(bf16)
        local[:, own] = mixed.astype(bf16)
        collected = jnp.where(lanes == head, peak + jnp.log(total), collected)
    stats[...] = collected


def attention_back_kernel(
    heads_dev, length, split, first, place, table, near, qkv, doc_row, doc_col, attended, grad_out, stats,
    grad_qkv, grad_near, grad_far, band, grad_band, grad_keys, grad_values,
):
    step = pl.program_id(0)
    width = heads_dev * head_dim

    @pl.when(step == 0)
    def _():
        fill_band(band, table, near, heads_dev, length)
        grad_band[...] = jnp.zeros_like(grad_band)
        grad_keys[...] = jnp.zeros_like(grad_keys)
        grad_values[...] = jnp.zeros_like(grad_values)
        if split > 1:
            grad_qkv[...] = jnp.zeros_like(grad_qkv)

    row = pl.multiple_of((first[0] + step) * tile, tile)
    out_row = pl.multiple_of((place[first[0] + step] - first[0]) * tile, tile)
    starts = band_starts(place, first[0] + step, length)
    same_doc = doc_col[...] == doc_row[...]
    at_step = pl.multiple_of(step * tile, tile)
    queries = qkv[pl.ds(row, tile), :width] * bf16(score_scale)
    for head in range(heads_dev):
        own = slice(head * head_dim, (head + 1) * head_dim)
        keys = qkv[:, width + own.start : width + own.stop]
        values = qkv[:, 2 * width + own.start : 2 * width + own.stop]
        upstream = grad_out[pl.ds(out_row, tile), own]
        scores = contract(queries[:, own], keys, 1, 1) + jnp.concatenate(
            [band[head, :, pl.ds(start, tile)] for start in starts], axis=1
        )
        scores = jnp.where(same_doc, scores, masked)
        weights = jnp.exp(scores - stats[:, head : head + 1])
        delta = jnp.sum(
            upstream.astype(f32) * attended[pl.ds(at_step, tile), own].astype(f32),
            axis=1,
            keepdims=True,
        )
        grad_scores = weights * (contract(upstream, values, 1, 1) - delta)
        for block, start in enumerate(starts):
            grad_band[head, :, pl.ds(start, tile)] += grad_scores[
                :, block * tile : (block + 1) * tile
            ]
        grad_low = grad_scores.astype(bf16)
        grad_values[:, own] += contract(weights.astype(bf16), upstream, 0, 0)
        grad_keys[:, own] += contract(grad_low, queries[:, own], 0, 0)
        grad_qkv[pl.ds(row, tile), own] = (
            contract(grad_low, keys, 1, 0) * score_scale
        ).astype(bf16)

    @pl.when(step == pl.num_programs(0) - 1)
    def _():
        grad_qkv[:, width : 2 * width] = grad_keys[...].astype(bf16)
        grad_qkv[:, 2 * width :] = grad_values[...].astype(bf16)
        for head in range(heads_dev):
            grad_near[head] = grad_band[head, :, length - tile : length + 2 * tile]
            grad_far[head, 0] = jnp.full(
                (8, tile), jnp.sum(grad_band[head, :, : length - tile]), f32
            )
            grad_far[head, 1] = jnp.full(
                (8, tile), jnp.sum(grad_band[head, :, length + 2 * tile :]), f32
            )


def whole(shape):
    return pl.BlockSpec(shape, lambda step: (0,) * len(shape), pipeline_mode=pl.Buffered(1))


def attention(qkv, doc_row, doc_col, first, place, table, near, rows):
    length = qkv.shape[0]
    heads_dev = table.shape[1]
    width = heads_dev * head_dim
    return pl.pallas_call(
        functools.partial(attention_kernel, heads_dev, length),
        grid=(rows // tile,),
        in_specs=[
            pl.BlockSpec(memory_space=pltpu.SMEM),
            pl.BlockSpec(memory_space=pltpu.SMEM),
            pl.BlockSpec(memory_space=pltpu.SMEM),
            whole(near.shape),
            whole(qkv.shape),
            whole(doc_row.shape),
            pl.BlockSpec((tile, 1), lambda step: (step, 0)),
        ],
        out_specs=[
            whole((rows, width)),
            pl.BlockSpec((tile, width), lambda step: (step, 0)),
            pl.BlockSpec((tile, tile), lambda step: (step, 0)),
        ],
        out_shape=[
            jax.ShapeDtypeStruct((rows, width), bf16),
            jax.ShapeDtypeStruct((rows, width), bf16),
            jax.ShapeDtypeStruct((rows, tile), f32),
        ],
        scratch_shapes=[pltpu.VMEM((heads_dev, tile, 2 * length), f32)],
        compiler_params=pltpu.CompilerParams(vmem_limit_bytes=40 * 2**20),
        cost_estimate=pl.CostEstimate(
            flops=4 * rows * length * width,
            bytes_accessed=4 * length * width * 2,
            transcendentals=rows * length * heads_dev,
        ),
    )(first, place, table, near, qkv, doc_row, doc_col)


def attention_back(
    qkv, doc_row, doc_col, attended, grad_out, stats, first, place, table, near, split
):
    length = qkv.shape[0]
    rows = grad_out.shape[0]
    heads_dev = table.shape[1]
    width = heads_dev * head_dim
    return pl.pallas_call(
        functools.partial(attention_back_kernel, heads_dev, length, split),
        grid=(rows // tile,),
        in_specs=[
            pl.BlockSpec(memory_space=pltpu.SMEM),
            pl.BlockSpec(memory_space=pltpu.SMEM),
            pl.BlockSpec(memory_space=pltpu.SMEM),
            whole(near.shape),
            whole(qkv.shape),
            whole(doc_row.shape),
            pl.BlockSpec((tile, 1), lambda step: (step, 0)),
            whole((rows, width)),
            whole((rows, width)),
            pl.BlockSpec((tile, tile), lambda step: (step, 0)),
        ],
        out_specs=[
            whole((length, 3 * width)),
            whole((heads_dev, tile, 3 * tile)),
            whole((heads_dev, 2, 8, tile)),
        ],
        out_shape=[
            jax.ShapeDtypeStruct((length, 3 * width), bf16),
            jax.ShapeDtypeStruct((heads_dev, tile, 3 * tile), f32),
            jax.ShapeDtypeStruct((heads_dev, 2, 8, tile), f32),
        ],
        scratch_shapes=[
            pltpu.VMEM((heads_dev, tile, 2 * length), f32),
            pltpu.VMEM((heads_dev, tile, 2 * length), f32),
            pltpu.VMEM((length, width), f32),
            pltpu.VMEM((length, width), f32),
        ],
        compiler_params=pltpu.CompilerParams(vmem_limit_bytes=48 * 2**20),
        cost_estimate=pl.CostEstimate(
            flops=10 * rows * length * width,
            bytes_accessed=8 * length * width * 2,
            transcendentals=rows * length * heads_dev,
        ),
    )(first, place, table, near, qkv, doc_row, doc_col, attended, grad_out, stats)


def call(kernel, shapes, *operands, smem=0):
    return pl.pallas_call(
        kernel,
        in_specs=[pl.BlockSpec(memory_space=pltpu.SMEM)] * smem
        + [pl.BlockSpec(memory_space=pltpu.VMEM)] * (len(operands) - smem),
        out_specs=[pl.BlockSpec(memory_space=pltpu.VMEM)] * len(shapes),
        out_shape=[jax.ShapeDtypeStruct(shape, kind) for shape, kind in shapes],
        compiler_params=pltpu.CompilerParams(vmem_limit_bytes=10 * 2**20),
    )(*operands)


def share_in_kernel(place, attn_in, gains, near, far):
    layers, rows = attn_in.shape[:2]
    half = near.shape[0] // (layers * rows)
    width = near.shape[1] // 3
    for index in range(2 * half):
        member = place[index]
        for layer_id in range(layers):
            block = jnp.concatenate(
                [
                    attn_in[
                        layer_id,
                        :,
                        pl.ds(pl.multiple_of((part * 2 * half + member) * width, width), width),
                    ]
                    for part in range(3)
                ],
                axis=1,
            )
            at = (index % half * layers + layer_id) * rows
            out = near if index < half else far
            out[at : at + rows] = (block.astype(f32) * gains[layer_id]).astype(bf16)


def join_kernel(*refs):
    shares, outs = refs[:4], refs[4:]
    rows = outs[0].shape[0] // 8
    for chip, share in enumerate(shares):
        for core in range(2):
            for layer_id, out in enumerate(outs):
                source = (core * len(outs) + layer_id) * rows
                target = (chip * 2 + core) * rows
                out[target : target + rows] = share[source : source + rows]


def row_of(chip, plane, core, rows, planes=4):
    return pl.multiple_of(((chip * planes + plane) * 2 + core) * rows, rows)


def assemble_in_kernel(place, own, lower, upper, opposite, out):
    at_z, at_core, at_head = place[8], place[0] % 2, place[0] // 2
    rows = own.shape[0] // 8
    for part, offset in ((own, 0), (lower, 3), (upper, 1), (opposite, 2)):
        plane = (at_z + offset) % 4
        for index in range(8):
            row = row_of(at_head ^ (index // 2), plane, at_core ^ (index % 2), rows)
            out[pl.ds(row, rows)] = part[index * rows : (index + 1) * rows]


def plane_attention_kernel(
    length, place, table, strip, near, far, w_in, *refs
):
    halves, (doc_row, doc_col, w_out, qkv, attended, stats, near_part, far_part, band) = (
        refs[:2], refs[2:],
    )
    step = pl.program_id(0)
    half = length // 2
    heads_dev = table.shape[1]
    width = heads_dev * head_dim

    @pl.when(step == 0)
    def _():
        fill_band(band, table, strip, heads_dev, length)
        swapped = place[length // tile] % 2 == 1
        rows = width // 2
        w_out[:rows] = jnp.where(swapped, halves[1][...], halves[0][...])
        w_out[rows:] = jnp.where(swapped, halves[0][...], halves[1][...])
        qkv[:half] = contract(near[...], w_in[...], 1, 0).astype(bf16)
        qkv[half:] = contract(far[...], w_in[...], 1, 0).astype(bf16)

    row = pl.multiple_of(step * tile, tile)
    starts = band_starts(place, step, length, length // tile + 1)
    same_doc = doc_col[...] == doc_row[...]
    queries = qkv[pl.ds(row, tile), :width] * bf16(score_scale)
    lanes = lax.broadcasted_iota(jnp.int32, (tile, tile), 1)
    collected = jnp.zeros((tile, tile), f32)
    results = []
    for head in range(heads_dev):
        own = slice(head * head_dim, (head + 1) * head_dim)
        keys = qkv[:, width + own.start : width + own.stop]
        values = qkv[:, 2 * width + own.start : 2 * width + own.stop]
        scores = contract(queries[:, own], keys, 1, 1) + jnp.concatenate(
            [band[head, :, pl.ds(start, tile)] for start in starts], axis=1
        )
        scores = jnp.where(same_doc, scores, masked)
        peak = jnp.max(scores, axis=1, keepdims=True)
        weights = jnp.exp(scores - peak)
        total = jnp.sum(weights, axis=1, keepdims=True)
        results.append((contract(weights.astype(bf16), values, 1, 0) / total).astype(bf16))
        collected = jnp.where(lanes == head, peak + jnp.log(total), collected)
    stats[...] = collected
    merged = jnp.concatenate(results, axis=1)
    attended[...] = merged
    part = contract(merged, w_out[...], 1, 0)

    @pl.when(row < half)
    def _():
        near_part[...] = part

    @pl.when(row >= half)
    def _():
        far_part[...] = part.astype(bf16)


def near_block(steps, columns):
    return pl.BlockSpec((tile, columns), lambda step: (jnp.minimum(step, steps // 2 - 1), 0))


def far_block(steps, columns):
    return pl.BlockSpec((tile, columns), lambda step: (jnp.maximum(step - steps // 2, 0), 0))


def plane_attention(near, far, w_in, halves, doc_row, doc_col, place, table, strip):
    length, model_width = 2 * near.shape[0], near.shape[1]
    steps = length // tile
    heads_dev = table.shape[1]
    width = heads_dev * head_dim
    return pl.pallas_call(
        functools.partial(plane_attention_kernel, length),
        grid=(steps,),
        in_specs=[
            pl.BlockSpec(memory_space=pltpu.SMEM),
            pl.BlockSpec(memory_space=pltpu.SMEM),
            whole(strip.shape),
            whole(near.shape),
            whole(far.shape),
            whole(w_in.shape),
            *[whole(half.shape) for half in halves],
            whole(doc_row.shape),
            pl.BlockSpec((tile, 1), lambda step: (step, 0)),
        ],
        out_specs=[
            whole((width, model_width)),
            whole((length, 3 * width)),
            pl.BlockSpec((tile, width), lambda step: (step, 0)),
            pl.BlockSpec((tile, tile), lambda step: (step, 0)),
            near_block(steps, model_width),
            far_block(steps, model_width),
        ],
        out_shape=[
            jax.ShapeDtypeStruct((width, model_width), bf16),
            jax.ShapeDtypeStruct((length, 3 * width), bf16),
            jax.ShapeDtypeStruct((length, width), bf16),
            jax.ShapeDtypeStruct((length, tile), f32),
            jax.ShapeDtypeStruct((length // 2, model_width), f32),
            jax.ShapeDtypeStruct((length // 2, model_width), bf16),
        ],
        scratch_shapes=[pltpu.VMEM((heads_dev, tile, 2 * length), f32)],
        compiler_params=pltpu.CompilerParams(vmem_limit_bytes=14 * 2**20),
        cost_estimate=pl.CostEstimate(
            flops=4 * length * length * width + 8 * length * model_width * width,
            bytes_accessed=12 * 2**20,
            transcendentals=length * length * heads_dev,
        ),
    )(place, table, strip, near, far, w_in, *halves, doc_row, doc_col)


def plane_attention_back_kernel(
    length, place, table, strip, qkv, doc_row, doc_col, attended, stats, near, far, w_in, w_out,
    grad_qkv, grad_near, grad_far, near_part, far_part, *rest
):
    halves, (band, grad_band, grad_keys, grad_values, out_sum) = rest[:2], rest[2:]
    step = pl.program_id(0)
    half = length // 2
    heads_dev = table.shape[1]
    width = heads_dev * head_dim

    @pl.when(step == 0)
    def _():
        fill_band(band, table, strip, heads_dev, length)
        grad_band[...] = jnp.zeros_like(grad_band)
        grad_keys[...] = jnp.zeros_like(grad_keys)
        grad_values[...] = jnp.zeros_like(grad_values)
        out_sum[...] = jnp.zeros_like(out_sum)

    row = pl.multiple_of(step * half, half)
    branch = jnp.where(step == 0, near[...], far[...])
    merged = attended[...]
    grad_merged = contract(branch, w_out[...], 1, 1).astype(bf16)
    out_sum[...] += contract(merged, branch, 0, 0)
    products = grad_merged.astype(f32) * merged.astype(f32)
    queries = qkv[pl.ds(row, half), :width] * bf16(score_scale)
    blocks = half // tile
    for head in range(heads_dev):
        own = slice(head * head_dim, (head + 1) * head_dim)
        keys = qkv[:, width + own.start : width + own.stop]
        values = qkv[:, 2 * width + own.start : 2 * width + own.stop]
        upstream = grad_merged[:, own]
        raw_scores = contract(queries[:, own], keys, 1, 1)
        grad_weights = contract(upstream, values, 1, 1)
        delta = jnp.sum(products[:, own], axis=1, keepdims=True)
        weights_low, grads_low = [], []
        for block in range(blocks):
            lines = slice(block * tile, (block + 1) * tile)
            starts = band_starts(place, step * blocks + block, length, length // tile + 1)
            scores = raw_scores[lines] + jnp.concatenate(
                [band[head, :, pl.ds(start, tile)] for start in starts], axis=1
            )
            scores = jnp.where(doc_col[lines] == doc_row[...], scores, masked)
            weights = jnp.exp(scores - stats[lines, head : head + 1])
            grad_scores = weights * (grad_weights[lines] - delta[lines])
            for index, start in enumerate(starts):
                grad_band[head, :, pl.ds(start, tile)] += grad_scores[
                    :, index * tile : (index + 1) * tile
                ]
            weights_low.append(weights.astype(bf16))
            grads_low.append(grad_scores.astype(bf16))
        weights_low, grads_low = jnp.concatenate(weights_low), jnp.concatenate(grads_low)
        grad_values[:, own] += contract(weights_low, upstream, 0, 0)
        grad_keys[:, own] += contract(grads_low, queries[:, own], 0, 0)
        grad_qkv[pl.ds(row, half), own] = (
            contract(grads_low, keys, 1, 0) * score_scale
        ).astype(bf16)

    @pl.when(step == pl.num_programs(0) - 1)
    def _():
        grad_qkv[:, width : 2 * width] = grad_keys[...].astype(bf16)
        grad_qkv[:, 2 * width :] = grad_values[...].astype(bf16)
        far_part[...] = contract(grad_qkv[half:], w_in[...], 1, 1).astype(bf16)
        near_part[...] = contract(grad_qkv[:half], w_in[...], 1, 1)
        rows = width // 2
        for index, part in enumerate(halves):
            block = index ^ place[length // tile] % 2
            part[...] = out_sum[pl.ds(pl.multiple_of(block * rows, rows), rows)].astype(bf16)
        for head in range(heads_dev):
            grad_near[head] = grad_band[head, :, length - tile : length + 2 * tile]
            grad_far[head, 0] = jnp.full(
                (8, tile), jnp.sum(grad_band[head, :, : length - tile]), f32
            )
            grad_far[head, 1] = jnp.full(
                (8, tile), jnp.sum(grad_band[head, :, length + 2 * tile :]), f32
            )


def plane_attention_back(
    qkv, doc_row, doc_col, attended, stats, near, far, w_in, w_out, place, table, strip
):
    length, model_width = 2 * near.shape[0], near.shape[1]
    half = length // 2
    heads_dev = table.shape[1]
    width = heads_dev * head_dim
    shapes = [
        ((length, 3 * width), bf16),
        ((heads_dev, tile, 3 * tile), f32),
        ((heads_dev, 2, 8, tile), f32),
        ((length // 2, model_width), f32),
        ((length // 2, model_width), bf16),
    ] + [((width // 2, model_width), bf16)] * 2
    return pl.pallas_call(
        functools.partial(plane_attention_back_kernel, length),
        grid=(2,),
        in_specs=[
            pl.BlockSpec(memory_space=pltpu.SMEM),
            pl.BlockSpec(memory_space=pltpu.SMEM),
            whole(strip.shape),
            whole(qkv.shape),
            whole(doc_row.shape),
            pl.BlockSpec((half, 1), lambda step: (step, 0)),
            pl.BlockSpec((half, width), lambda step: (step, 0)),
            pl.BlockSpec((half, tile), lambda step: (step, 0)),
            whole((half, model_width)),
            whole((half, model_width)),
            whole(w_in.shape),
            whole(w_out.shape),
        ],
        out_specs=[whole(shape) for shape, _ in shapes],
        out_shape=[jax.ShapeDtypeStruct(shape, kind) for shape, kind in shapes],
        scratch_shapes=[
            pltpu.VMEM((heads_dev, tile, 2 * length), f32),
            pltpu.VMEM((heads_dev, tile, 2 * length), f32),
            pltpu.VMEM((length, width), f32),
            pltpu.VMEM((length, width), f32),
            pltpu.VMEM((width, model_width), f32),
        ],
        compiler_params=pltpu.CompilerParams(vmem_limit_bytes=32 * 2**20),
        cost_estimate=pl.CostEstimate(
            flops=10 * length * length * width + 10 * length * model_width * width,
            bytes_accessed=12 * 2**20,
            transcendentals=length * length * heads_dev,
        ),
    )(place, table, strip, qkv, doc_row, doc_col, attended, stats, near, far, w_in, w_out)


def gelu_and_slope(pre_act):
    size = jnp.abs(pre_act)
    gauss = jnp.exp(-0.5 * pre_act * pre_act)
    ratio = 1.0 / (1.0 + np.float32(0.3275911 * 0.5**0.5) * size)
    series = np.float32(1.061405429)
    for factor in (-1.453152027, 1.421413741, -0.284496736, 0.254829592):
        series = series * ratio + np.float32(factor)
    tail = 0.5 * series * ratio * gauss
    cumulative = jnp.where(pre_act < 0, tail, 1.0 - tail)
    slope = cumulative + pre_act * gauss * np.float32((2 * np.pi) ** -0.5)
    return pre_act * cumulative, slope


def ff_kernel(rows, pair, activated, slope, part):
    columns = rows.shape[1]
    value, gradient = gelu_and_slope(contract(rows[...], pair[:, :columns], 1, 1))
    activated[...] = value.astype(bf16)
    slope[...] = gradient.astype(bf16)
    part[...] = contract(activated[...], pair[:, columns:], 1, 0).astype(part.dtype)


def ff_first_kernel(rows, *refs):
    parts, (activated, slope, part, pair) = refs[:5], refs[5:]

    @pl.when(pl.program_id(0) == 0)
    def _():
        units, columns = parts[0].shape[0], rows.shape[1]
        for index, ref in enumerate(parts[:3]):
            pair[index * units : (index + 1) * units] = ref[...]
        pair[3 * units :, :columns] = parts[3][...]
        pair[3 * units :, columns:] = parts[4][...]

    ff_kernel(rows, pair, activated, slope, part)


def ff_back_kernel(rows, slope, pair, grad_pre, part):
    columns = rows.shape[1]
    grad_act = contract(rows[...], pair[:, columns:], 1, 1)
    grad_pre[...] = (grad_act * slope[...].astype(f32)).astype(bf16)
    part[...] = contract(grad_pre[...], pair[:, :columns], 1, 0).astype(part.dtype)


def by_rows(kernel, step_rows, row_operands, whole_operands, outs, whole_outs=()):
    rows = row_operands[0].shape[0]
    return pl.pallas_call(
        kernel,
        grid=(rows // step_rows,),
        in_specs=[
            pl.BlockSpec((step_rows, operand.shape[1]), lambda step: (step, 0))
            for operand in row_operands
        ]
        + [whole(operand.shape) for operand in whole_operands],
        out_specs=[pl.BlockSpec((step_rows, columns), lambda step: (step, 0)) for columns, _ in outs]
        + [whole(shape) for shape in whole_outs],
        out_shape=[jax.ShapeDtypeStruct((rows, columns), kind) for columns, kind in outs]
        + [jax.ShapeDtypeStruct(shape, bf16) for shape in whole_outs],
        compiler_params=pltpu.CompilerParams(vmem_limit_bytes=10 * 2**20),
        cost_estimate=pl.CostEstimate(
            flops=4 * rows * outs[0][0] * row_operands[0].shape[1],
            bytes_accessed=6 * 2**20,
            transcendentals=0,
        ),
    )(*row_operands, *whole_operands)


def ff_grads_kernel(
    pre_near, pre_far, act_near, act_far, normed_near, normed_far, low_near, low_far, *outs
):
    columns = normed_near.shape[1]
    units = outs[0].shape[0]
    up = (
        contract(pre_near[...], normed_near[...], 0, 0)
        + contract(pre_far[...], normed_far[...], 0, 0)
    ).astype(bf16)
    down = (
        contract(act_near[...], low_near[...], 0, 0) + contract(act_far[...], low_far[...], 0, 0)
    ).astype(bf16)

    @pl.when(pl.program_id(0) == 0)
    def _():
        for index in range(2):
            block = slice(index * units, (index + 1) * units)
            outs[index][:, :columns] = up[block]
            outs[index][:, columns:] = down[block]

    @pl.when(pl.program_id(0) == 1)
    def _():
        outs[2][:, :columns] = up[:units]
        outs[2][:, columns:] = down[:units]
        outs[3][...] = up[units:]
        outs[4][...] = down[units:]


def ff_grads(pre, act, normed, low):
    rows, hidden_units = pre[0].shape
    columns = normed[0].shape[1]
    shapes = [(hidden_units // 4, 2 * columns)] * 3 + [(hidden_units // 4, columns)] * 2
    return pl.pallas_call(
        ff_grads_kernel,
        grid=(2,),
        in_specs=[pl.BlockSpec((rows, hidden_units // 2), lambda step: (0, step))] * 4
        + [whole((rows, columns))] * 4,
        out_specs=[whole(shape) for shape in shapes],
        out_shape=[jax.ShapeDtypeStruct(shape, bf16) for shape in shapes],
        compiler_params=pltpu.CompilerParams(vmem_limit_bytes=14 * 2**20),
        cost_estimate=pl.CostEstimate(
            flops=8 * rows * hidden_units * columns, bytes_accessed=8 * 2**20, transcendentals=0
        ),
    )(*pre, *act, *normed, *low)


def in_grads_kernel(place, near, far, grad_qkv, *refs):
    ends, (total, extra) = refs[:-2], refs[-2:]
    half = near.shape[0]
    columns = grad_qkv.shape[1]
    total[:, :columns] = (
        contract(near[...], grad_qkv[:half], 0, 0) + contract(far[...], grad_qkv[half:], 0, 0)
    ).astype(bf16)
    if ends:
        gain_0, gain_1, table_0, table_1 = ends
        rows = near.shape[1] // 32
        lines = lax.broadcasted_iota(jnp.int32, (tile, gain_0.shape[1]), 0)
        gains = jnp.where(lines == 0, gain_0[...], jnp.where(lines == 1, gain_1[...], 0.0))
        extra[...] = jnp.transpose(gains)
        table = table_0[...] + table_1[...]
        buckets = table.shape[0] // 8
        blank = jnp.zeros((8 - buckets, tile), f32)
        for block in range(8):
            row = pl.multiple_of((place[0] // 2 * 8 + block) * rows, rows)
            extra[pl.ds(row, 8)] += jnp.concatenate(
                [table[block * buckets : (block + 1) * buckets], blank]
            )
        total[:, columns:] = extra[...].astype(bf16)


def in_grads(place, near, far, grad_qkv, *ends):
    columns = grad_qkv.shape[1] + (tile if ends else 0)
    return pl.pallas_call(
        in_grads_kernel,
        in_specs=[pl.BlockSpec(memory_space=pltpu.SMEM)]
        + [pl.BlockSpec(memory_space=pltpu.VMEM)] * (3 + len(ends)),
        out_specs=pl.BlockSpec(memory_space=pltpu.VMEM),
        out_shape=jax.ShapeDtypeStruct((near.shape[1], columns), bf16),
        scratch_shapes=[pltpu.VMEM((near.shape[1], tile), f32)],
        compiler_params=pltpu.CompilerParams(vmem_limit_bytes=14 * 2**20),
        cost_estimate=pl.CostEstimate(
            flops=4 * near.shape[0] * near.shape[1] * columns,
            bytes_accessed=4 * 2**20,
            transcendentals=0,
        ),
    )(place, near, far, grad_qkv, *ends)


def combine_kernel(near_part, arrived, own, x_part, y_part, xy_part):
    rows = own.shape[0]
    own[...] = near_part[:rows] + arrived[:rows].astype(f32)
    for bits, out in ((1, x_part), (2, y_part), (3, xy_part)):
        block = slice(bits * rows, (bits + 1) * rows)
        out[...] = (near_part[block] + arrived[block].astype(f32)).astype(bf16)


def added(own, x_part, y_part, xy_part):
    return (own[...] + x_part[...].astype(f32)) + (
        y_part[...].astype(f32) + xy_part[...].astype(f32)
    )


def close_kernel(kept, own, x_part, y_part, xy_part, hidden, units):
    total = kept[...] + added(own, x_part, y_part, xy_part)
    hidden[...] = total
    units[...] = (total * inverse_rms(total)).astype(bf16)


def close_gain_kernel(kept, own, x_part, y_part, xy_part, gain, hidden, normed):
    total = kept[...] + added(own, x_part, y_part, xy_part)
    hidden[...] = total
    normed[...] = (total * inverse_rms(total) * gain[...]).astype(bf16)


def last_kernel(kept, own, x_part, y_part, xy_part, hidden):
    hidden[...] = (kept[...] + added(own, x_part, y_part, xy_part)).astype(bf16)


def middle_back_kernel(
    upstream, own, x_part, y_part, xy_part, middle, gain, grad_middle, branch, grad_gain
):
    grad_normed = added(own, x_part, y_part, xy_part)
    inverse = inverse_rms(middle[...])
    grad_gain[...] = jnp.sum(grad_normed * middle[...] * inverse, axis=0, keepdims=True)
    total = upstream[...].astype(f32) + unit_norm_back(
        middle[...], inverse, grad_normed * gain[...]
    )
    grad_middle[...] = total
    branch[...] = total.astype(bf16)


def layer_back_kernel(grad_middle, own, x_part, y_part, xy_part, hidden, upstream, low):
    total = grad_middle[...] + unit_norm_back(
        hidden[...], inverse_rms(hidden[...]), added(own, x_part, y_part, xy_part)
    )
    upstream[...] = total
    low[...] = total.astype(bf16)


def pair_kernel(axis, near, arrived, *outs):
    rows = near.shape[0] // len(outs)
    for index, out in enumerate(outs):
        block = slice(index * rows, (index + 1) * rows)
        if axis == 0:
            out[:rows] = near[block]
            out[rows:] = arrived[block]
        else:
            columns = near.shape[1]
            out[:, :columns] = near[block]
            out[:, columns:] = arrived[block]


def unit_kernel(tokens, hidden, units):
    total = tokens[...].astype(f32)
    hidden[...] = total
    units[...] = (total * inverse_rms(total)).astype(bf16)


def finish_in_kernel(*refs):
    attn_in, gains, grad_in, grad_gain, ends = refs[-5:]
    layers, rows = attn_in.shape[:2]
    width = tile
    members = attn_in.shape[2] // (3 * width)
    ends[...] = jnp.zeros_like(ends)
    for layer_id in range(layers):
        shares = refs[layer_id]
        row_dot = jnp.zeros((rows, 1), f32)
        for member in range(members):
            total = sum_of_four(
                [shares.at[(member // 2 * 4 + plane) * 2 + member % 2] for plane in range(4)]
            )
            for part in range(3):
                block = total[:, part * width : (part + 1) * width]
                columns = slice((part * members + member) * width, (part * members + member + 1) * width)
                grad_in[layer_id, :, columns] = block * gains[layer_id]
                row_dot = row_dot + jnp.sum(
                    block * attn_in[layer_id, :, columns].astype(f32), axis=1, keepdims=True
                )
            if layer_id == 0:
                ends[...] += total[:, 3 * width :]
        grad_gain[layer_id] = jnp.concatenate(
            [row_dot, ends[:, layer_id : layer_id + 1]], axis=1
        )


def sum_of_four(parts):
    return (parts[0][...].astype(f32) + parts[1][...].astype(f32)) + (
        parts[2][...].astype(f32) + parts[3][...].astype(f32)
    )


def finish_ff_kernel(*refs):
    count = (len(refs) - 3) // 2
    sources, grads, held, done = refs[:count], refs[count : count + 2], refs[count + 2 : -1], refs[-1]
    copies = [
        pltpu.make_async_copy(source, target, done.at[index])
        for index, (source, target) in enumerate(zip(sources, held))
    ]
    for copy in copies:
        copy.start()
    for copy in copies:
        copy.wait()
    refs = held
    columns = grads[0].shape[2]
    for layer_id in range(grads[0].shape[0]):
        parts = refs[5 * layer_id : 5 * layer_id + 5]
        for side, out in enumerate(grads):
            halves = [part.at[:, side * columns : (side + 1) * columns] for part in parts[:3]]
            out[layer_id] = sum_of_four(halves + [parts[3 + side]])


def finish_ff(grads, shape):
    return pl.pallas_call(
        finish_ff_kernel,
        in_specs=[pl.BlockSpec(memory_space=pl.ANY)] * len(grads),
        out_specs=[pl.BlockSpec(memory_space=pltpu.VMEM)] * 2,
        out_shape=[jax.ShapeDtypeStruct(shape, f32)] * 2,
        scratch_shapes=[pltpu.VMEM(grad.shape, bf16) for grad in grads]
        + [pltpu.SemaphoreType.DMA((len(grads),))],
        compiler_params=pltpu.CompilerParams(vmem_limit_bytes=14 * 2**20),
    )(*grads)


def add_out_kernel(place, *refs):
    parts, (own, other) = refs[:-2], refs[-2:]
    both = parts[0][...].astype(f32) + parts[1][...].astype(f32)
    for layer_id in range(own.shape[0]):
        rows = own.shape[1]
        total = both[2 * layer_id * rows : 2 * (layer_id + 1) * rows]
        second = place[0] % 2 == 1
        own[layer_id] = jnp.where(second, total[rows:], total[:rows])
        other[layer_id] = jnp.where(second, total[:rows], total[rows:]).astype(bf16)


def finish_out_kernel(own, arrived, out):
    out[...] = own[...] + arrived[...].astype(f32)


def inverse_rms(hidden):
    return lax.rsqrt(jnp.mean(hidden * hidden, axis=-1, keepdims=True) + epsilon)


def prepare(bias_table, first_head, heads_dev):
    table = lax.dynamic_slice_in_dim(bias_table, first_head, heads_dev, 1)
    (near,) = call(near_kernel, [((heads_dev, tile, 3 * tile), f32)], table, smem=1)
    return table, near


def bucket_grads(first_lane, grads, bucket_count):
    (total,) = call(bucket_kernel, [((bucket_count, tile), f32)], first_lane, *grads, smem=1)
    return total


def gelu_parts(pre_act):
    cumulative = 0.5 * (1.0 + lax.erf(pre_act * np.float32(0.5**0.5)))
    slope = cumulative + pre_act * jnp.exp(-0.5 * pre_act * pre_act) * np.float32(
        (2 * np.pi) ** -0.5
    )
    return (pre_act * cumulative).astype(bf16), slope


def unit_norm_back(hidden, inverse, grad_unit):
    unit = hidden * inverse
    return inverse * (grad_unit - unit * jnp.mean(grad_unit * unit, axis=-1, keepdims=True))


def gather_rows(block, axes):
    return lax.all_gather(block, axes, axis=0, tiled=True)


def toggle(array, axis, bits):
    return lax.ppermute(array, axis, [(i, i ^ bits) for i in range(lax.axis_size(axis))])


def shift(array, by):
    planes = lax.axis_size("z")
    return lax.ppermute(array, "z", [(i, (i + by) % planes) for i in range(planes)])


def plane_gather(block, *holds):
    near = jnp.concatenate([block] + [toggle(block, "head", bits) for bits in (1, 2, 3)])
    near, *holds = tie(near, *holds)
    return (near, toggle(near, "core", 1), *holds)


def plane_scatter(near_part, far_part):
    rows, columns = near_part.shape[0] // 4, near_part.shape[1]
    own, *others = call(
        combine_kernel,
        [((rows, columns), f32)] + [((rows, columns), bf16)] * 3,
        near_part,
        toggle(far_part, "core", 1),
    )
    shares = [own] + [toggle(other, "head", bits) for bits, other in zip((1, 2, 3), others)]
    return shares, own


def tie(*arrays):
    return lax.optimization_barrier(arrays)


def after(array, other):
    return lax.optimization_barrier((array, other))[0]


def scatter_sum(partial, axes, members):
    blocks = partial.astype(bf16).reshape(members, -1, partial.shape[1])
    return jnp.sum(lax.all_to_all(blocks, axes, 0, 0, tiled=True).astype(f32), axis=0)


def local_general(tokens, doc_start, bias_table, attn_in, attn_out, ff_in, ff_out, gains, cotangent):
    heads_n, z_n, core_n = (lax.axis_size(axis) for axis in everyone)
    devices = heads_n * z_n * core_n
    group, spare = ("z", "core"), "head"
    ff_group, ff_spare, ff_members = ("head", "core"), "z", heads_n * core_n
    blocks = z_n * core_n
    block_rows, model_width = tokens.shape[1:]
    layer_count, weight_rows = attn_in.shape[:2]
    length = block_rows * blocks
    heads_all = bias_table.shape[1]
    member = lax.axis_index("z") * core_n + lax.axis_index("core")
    heads_dev = max(1, heads_all // blocks)
    head_groups = heads_all // heads_dev
    split = blocks // head_groups
    head_group, query_part = member // split, member % split
    query_rows = length // split
    width = heads_dev * head_dim
    first = (query_part * (query_rows // tile)).astype(jnp.int32).reshape(1)
    place = jnp.arange(length // tile, dtype=jnp.int32)
    out_row = head_group * width

    def swap(array):
        return lax.all_to_all(array, everyone, 0, 0, tiled=True)

    starts = jnp.broadcast_to(
        doc_start.astype(f32)[:, None], (heads_n, blocks, block_rows)
    ).reshape(devices, block_rows)
    ff_gains = gains[:, :, 1].astype(f32).reshape(1, -1)
    small = swap(
        jnp.concatenate(
            [starts, jnp.broadcast_to(ff_gains, (devices, layer_count * weight_rows))], axis=1
        )
    )
    doc_row = small[:blocks, :block_rows].reshape(1, length)
    doc_col = lax.dynamic_slice_in_dim(
        doc_row.reshape(length, 1), query_part * query_rows, query_rows, 0
    )
    gain_ff = jnp.transpose(
        small[:, block_rows:].reshape(devices, layer_count, weight_rows), (1, 0, 2)
    ).reshape(layer_count, 1, model_width)
    table, near = prepare(bias_table, head_group * heads_dev, heads_dev)

    gain_attn = gains[:, :, 0].astype(f32)[:, :, None]
    own_in = attn_in.astype(f32)

    def fetch_in(layer_id):
        scaled = (own_in[layer_id] * gain_attn[layer_id]).astype(bf16)
        columns = jnp.transpose(
            scaled.reshape(weight_rows, 3, head_groups, width), (2, 0, 1, 3)
        ).reshape(head_groups, weight_rows, 3 * width)
        columns = jnp.repeat(columns, split, axis=0)
        columns = jnp.broadcast_to(columns[None], (heads_n, *columns.shape))
        return swap(columns.reshape(devices, weight_rows, 3 * width)).reshape(
            model_width, 3 * width
        )

    def fetch_ff(layer_id):
        pair = jnp.concatenate([ff_in[layer_id], ff_out[layer_id]], axis=1)
        pair = gather_rows(pair, ff_spare)
        return pair[:, :model_width], pair[:, model_width:]

    hidden, upstream = tokens[0].astype(f32), cotangent[0]
    weights_in = [fetch_in(layer_id) for layer_id in range(layer_count)]
    weights_out = lax.dynamic_slice_in_dim(
        lax.all_gather(attn_out, everyone, axis=1, tiled=True), out_row, width, 1
    )
    weights_ff = [fetch_ff(layer_id) for layer_id in range(layer_count)]

    records = []
    for layer_id in range(layer_count):
        w_in, w_out, (w_up, w_down) = (
            weights_in[layer_id], weights_out[layer_id], weights_ff[layer_id],
        )
        inverse = inverse_rms(hidden)
        units = gather_rows((hidden * inverse).astype(bf16), group)
        qkv = jnp.dot(units, w_in, preferred_element_type=f32).astype(bf16)
        attended, _, stats = attention(
            qkv, doc_row, doc_col, first, place, table, near, query_rows
        )
        mixed = jnp.dot(attended, w_out, preferred_element_type=f32)
        if split > 1:
            mixed = lax.dynamic_update_slice_in_dim(
                jnp.zeros((length, model_width), f32), mixed, query_part * query_rows, 0
            )
        middle = hidden + scatter_sum(mixed, group, blocks)
        inverse_ff = inverse_rms(middle)
        normed_ff = gather_rows((middle * inverse_ff * gain_ff[layer_id]).astype(bf16), ff_group)
        activated, slope = gelu_parts(contract(normed_ff, w_up, 1, 1))
        ff_result = jnp.dot(activated, w_down, preferred_element_type=f32)
        records.append(
            (hidden, inverse, units, qkv, attended, stats, middle, inverse_ff, normed_ff,
             activated, slope)
        )
        hidden = middle + scatter_sum(ff_result, ff_group, ff_members)
    output = hidden

    grads_ff, grads_in, grads_out, grads_gain_ff, grads_table = (
        [None] * layer_count for _ in range(5)
    )
    for layer_id in reversed(range(layer_count)):
        w_in, w_out, (w_up, w_down) = (
            weights_in[layer_id], weights_out[layer_id], weights_ff[layer_id],
        )
        (hidden, inverse, units, qkv, attended, stats, middle, inverse_ff, normed_ff,
         activated, slope) = records[layer_id]
        grad_low = gather_rows(upstream.astype(bf16), ff_group)
        grad_pre = (contract(grad_low, w_down, 1, 1) * slope).astype(bf16)
        grad_normed = scatter_sum(
            jnp.dot(grad_pre, w_up, preferred_element_type=f32), ff_group, ff_members
        )
        grad_pair = jnp.concatenate(
            [contract(grad_pre, normed_ff, 0, 0), contract(activated, grad_low, 0, 0)], axis=1
        ).astype(bf16)
        grads_ff[layer_id] = lax.psum_scatter(
            grad_pair, ff_spare, scatter_dimension=0, tiled=True
        ).astype(f32)
        grads_gain_ff[layer_id] = jnp.sum(grad_normed * middle * inverse_ff, axis=0)
        grad_middle = upstream + unit_norm_back(
            middle, inverse_ff, grad_normed * gain_ff[layer_id]
        )
        branch = gather_rows(grad_middle.astype(bf16), group)
        if split > 1:
            branch = lax.dynamic_slice_in_dim(branch, query_part * query_rows, query_rows, 0)
        grad_attended = contract(branch, w_out, 1, 1).astype(bf16)
        grad_qkv, grad_near, grad_far = attention_back(
            qkv, doc_row, doc_col, attended, grad_attended, stats, first, place, table, near, split
        )
        grads_table[layer_id] = (grad_near, grad_far)
        grad_units = scatter_sum(contract(grad_qkv, w_in, 1, 1), group, blocks)
        upstream = grad_middle + unit_norm_back(hidden, inverse, grad_units)
        grad_out = lax.dynamic_update_slice_in_dim(
            jnp.zeros((model_width, model_width), bf16),
            contract(attended, branch, 0, 0).astype(bf16),
            out_row,
            0,
        )
        grads_out[layer_id] = lax.psum_scatter(
            grad_out, everyone, scatter_dimension=0, tiled=True
        ).astype(f32)
        grads_in[layer_id] = contract(units, grad_qkv, 0, 0).astype(bf16)

    bucket_count = table.shape[0]
    grad_table = sum(
        bucket_grads(jnp.zeros((1,), jnp.int32), entry, bucket_count) for entry in grads_table
    )[:, :heads_dev]
    grad_table = lax.dynamic_update_slice_in_dim(
        jnp.zeros((bucket_count, heads_all), f32), grad_table, head_group * heads_dev, 1
    )
    grad_table = jnp.transpose(
        grad_table.reshape(blocks, bucket_count // blocks, heads_n, heads_all // heads_n),
        (2, 0, 1, 3),
    ).reshape(devices, -1)
    grad_gain_ff = jnp.transpose(
        jnp.stack(grads_gain_ff).reshape(layer_count, devices, weight_rows), (1, 0, 2)
    ).reshape(devices, -1)
    ends = jnp.sum(swap(jnp.concatenate([grad_gain_ff, grad_table], axis=1)), axis=0)
    grad_gain_ff = ends[: layer_count * weight_rows].reshape(layer_count, weight_rows)
    grad_bias_table = ends[layer_count * weight_rows :].reshape(
        bucket_count // blocks, heads_all // heads_n
    )
    grads_attn_in, grads_gains = [], []
    for layer_id in range(layer_count):
        parts = swap(grads_in[layer_id].reshape(devices, weight_rows, 3 * width)).astype(f32)
        parts = jnp.sum(parts.reshape(heads_n, blocks, weight_rows, 3 * width), axis=0)
        parts = jnp.sum(parts.reshape(head_groups, split, weight_rows, 3, width), axis=1)
        unit_grad = jnp.transpose(parts, (1, 2, 0, 3)).reshape(weight_rows, 3 * model_width)
        grads_attn_in.append(unit_grad * gain_attn[layer_id])
        grads_gains.append(
            jnp.stack(
                [jnp.sum(unit_grad * own_in[layer_id], axis=1), grad_gain_ff[layer_id]], axis=1
            )
        )
    return (
        output[None],
        upstream[None],
        jnp.stack(grads_attn_in),
        jnp.stack(grads_out),
        jnp.stack([entry[:, :model_width] for entry in grads_ff]),
        jnp.stack([entry[:, model_width:] for entry in grads_ff]),
        jnp.stack(grads_gains),
        grad_bias_table,
    )


def local_plane(tokens, doc_start, bias_table, attn_in, attn_out, ff_in, ff_out, gains, cotangent):
    heads_n, z_n, core_n = (lax.axis_size(axis) for axis in everyone)
    devices = heads_n * z_n * core_n
    at_head, at_z, at_core = (lax.axis_index(axis) for axis in everyone)
    members = heads_n * core_n
    block_rows, model_width = tokens.shape[1:]
    layer_count, weight_rows = attn_in.shape[:2]
    length = block_rows * members
    heads_all = bias_table.shape[1]
    heads_dev = heads_all // members
    width = heads_dev * head_dim
    member = at_head * core_n + at_core
    turn = [
        ((h * z_n + z) * core_n + c, ((h ^ z) * z_n + h) * core_n + c)
        for h in range(heads_n)
        for z in range(z_n)
        for c in range(core_n)
    ]
    everywhere = [(h, z, c) for h in range(heads_n) for z in range(z_n) for c in range(core_n)]

    def device(h, z, c):
        return (h * z_n + z) * core_n + c

    plane_turn = [(device(h, z, c), device(h ^ z, z, c)) for h, z, c in everywhere]
    line_turn = [(device(h, z, c), device(h, z ^ h, c)) for h, z, c in everywhere]
    place = jnp.stack(
        [
            (at_head ^ bits) * core_n + (at_core ^ other)
            for other in range(core_n)
            for bits in range(heads_n)
        ]
        + [at_z]
        + [
            (at_head ^ bits ^ at_z) * core_n + (at_core ^ other)
            for other in range(core_n)
            for bits in range(heads_n)
        ]
    ).astype(jnp.int32)

    def relay(array):
        return lax.ppermute(array, everyone, turn)

    def turn_in_plane(array):
        return lax.ppermute(array, everyone, plane_turn)

    def turn_in_line(array):
        return lax.ppermute(array, everyone, line_turn)

    def swap(array):
        return lax.all_to_all(array, everyone, 0, 0, tiled=True)

    row_shape = (block_rows, model_width)
    gain_attn = gains[:, :, 0].astype(f32)[:, :, None]
    near_share, far_share = call(
        share_in_kernel,
        [((members // 2 * layer_count * weight_rows, 3 * width), bf16)] * 2,
        place,
        attn_in,
        gain_attn,
        smem=1,
    )

    half_turns = [
        [
            (z * core_n + c, (2 * c + (a ^ z % 2)) * core_n + z // 2)
            for z in range(z_n)
            for c in range(core_n)
        ]
        for a in range(2)
    ]

    def fetch_out(layer_id, hold):
        own = attn_out[layer_id]
        other = toggle(own, "core", 1)
        head = jnp.where(
            at_core == 0, jnp.concatenate([own, other]), jnp.concatenate([other, own])
        )
        head = after(head, hold)
        return [
            lax.ppermute(head, ("z", "core"), [(holder, user) for user, holder in turns])
            for turns in half_turns
        ]

    def owners_halves(halves):
        return [
            lax.ppermute(half, ("z", "core"), turns) for half, turns in zip(halves, half_turns)
        ]

    def pair_chips(near, arrived, axis):
        rows, columns = near.shape[0] // 4, near.shape[1]
        shape = (2 * rows, columns) if axis == 0 else (rows, 2 * columns)
        return call(functools.partial(pair_kernel, axis), [(shape, bf16)] * 4, near, arrived)

    def share_chips(blocks):
        return [blocks[0]] + [toggle(blocks[bits], "head", bits) for bits in (1, 2, 3)]

    units_shape = [(row_shape, f32), (row_shape, bf16)]

    starts = jnp.broadcast_to(
        doc_start.astype(f32)[None, :, None], (heads_n, z_n, core_n, block_rows)
    )
    ff_gains = gains[:, :, 1].astype(f32).reshape(1, -1)
    small = jnp.concatenate(
        [
            starts.reshape(devices, block_rows),
            jnp.broadcast_to(ff_gains, (devices, layer_count * weight_rows)),
        ],
        axis=1,
    )
    table, strip = prepare(bias_table, member * heads_dev, heads_dev)
    hidden, strip = tie(relay(tokens[0]), strip)
    hidden, shares, cotangent_low, halves, small = tie(
        hidden,
        share_chips(pair_chips(near_share, toggle(far_share, "core", 1), 0)),
        turn_in_plane(after(cotangent[0].astype(bf16), near_share)),
        fetch_out(0, near_share),
        swap(after(small, near_share)),
    )
    hidden, unit_rows = call(unit_kernel, units_shape, hidden)
    doc_row = small[:members, :block_rows].reshape(2, 2, core_n, block_rows)
    at_block = at_head ^ at_z
    for axis, bit in ((0, at_block // 2), (1, at_block % 2), (2, at_core)):
        doc_row = jnp.where(bit == 1, jnp.flip(doc_row, axis), doc_row)
    doc_row = jnp.transpose(doc_row, (2, 0, 1, 3)).reshape(1, length)
    doc_col = doc_row.reshape(length, 1)
    gain_ff = jnp.transpose(
        small[:, block_rows:].reshape(devices, layer_count, weight_rows), (1, 0, 2)
    ).reshape(layer_count, 1, model_width)

    def round_planes(array, by, hold):
        return shift(after(array, hold), by)

    ff_pairs = [
        jnp.concatenate([ff_in[layer_id], ff_out[layer_id]], axis=1) for layer_id in range(layer_count)
    ]

    def ff_both(kernel, row_operands, pair, columns):
        return zip(
            *(
                by_rows(
                    kernel,
                    256,
                    operands,
                    [pair],
                    [(pair.shape[0], bf16)] * columns + [(model_width, kind)],
                )
                for operands, kind in zip(zip(*row_operands), (f32, bf16))
            )
        )

    def ff_forward(normed, *parts):
        units = 4 * parts[0].shape[0]
        outs = [(units, bf16), (units, bf16)]
        *near, pair = by_rows(
            ff_first_kernel,
            256,
            [normed[0]],
            parts,
            outs + [(model_width, f32)],
            [(units, 2 * model_width)],
        )
        far = by_rows(ff_kernel, 256, [normed[1]], [pair], outs + [(model_width, bf16)])
        return pair, *zip(near, far)

    def ff_backward(low, slopes, pair):
        return ff_both(ff_back_kernel, [low, slopes], pair, 1)

    def assemble_in(share, lower, upper, opposite):
        return call(
            assemble_in_kernel,
            [((model_width, 3 * width), bf16)],
            place,
            share,
            lower,
            upper,
            opposite,
            smem=1,
        )[0]

    share, later_share = call(
        join_kernel, [((members * weight_rows, 3 * width), bf16)] * layer_count, *shares
    )
    near, far, lower, upper, opposite, doc_row, doc_col, gain_ff, *ff_pairs = plane_gather(
        unit_rows,
        shift(share, 1),
        shift(share, -1),
        shift(share, 2),
        doc_row,
        doc_col,
        gain_ff,
        *ff_pairs,
    )
    w_in = assemble_in(share, lower, upper, opposite)
    units = (near, far)
    w_out, qkv, attended, stats, *parts = plane_attention(
        *units, w_in, halves, doc_row, doc_col, place, table, strip
    )
    parts, lower, upper = tie(
        parts, round_planes(ff_pairs[0], 1, near), round_planes(ff_pairs[0], -1, near)
    )
    parts, own = plane_scatter(*parts)
    parts, opposite_in = tie(parts, round_planes(ff_in[0], 2, own))
    middle, normed_rows = call(close_gain_kernel, units_shape, hidden, *parts, gain_ff[0])
    *normed, opposite_out = plane_gather(normed_rows, round_planes(ff_out[0], 2, normed_rows))
    pair, acts, slopes, parts = ff_forward(
        normed, ff_pairs[0], lower, upper, opposite_in, opposite_out
    )
    records = [
        (hidden, units, w_in, w_out, pair, qkv, attended, stats, middle, normed, acts, slopes)
    ]
    parts, lower, upper = tie(
        parts,
        round_planes(later_share, 1, normed[0]),
        round_planes(later_share, -1, normed[0]),
    )
    parts, own = plane_scatter(*parts)
    parts, opposite, upstream = tie(
        parts, round_planes(later_share, 2, own), turn_in_line(after(cotangent_low, own))
    )
    shares = [later_share, lower, upper, opposite]
    hidden, unit_rows = call(close_kernel, units_shape, middle, *parts)

    near, far, lower, halves = plane_gather(
        unit_rows, round_planes(ff_pairs[1], 1, unit_rows), fetch_out(1, unit_rows)
    )
    units = (near, far)
    w_in = assemble_in(*shares)
    w_out, qkv, attended, stats, *parts = plane_attention(
        *units, w_in, halves, doc_row, doc_col, place, table, strip
    )
    low = plane_gather(after(upstream, far))
    parts, near_low, upper = tie(parts, low[0], round_planes(ff_pairs[1], -1, far))
    low = (near_low, low[1])
    parts, own = plane_scatter(*parts)
    parts, opposite_in = tie(parts, round_planes(ff_in[1], 2, own))
    middle, normed_rows = call(close_gain_kernel, units_shape, hidden, *parts, gain_ff[1])
    *normed, opposite_out = plane_gather(normed_rows, round_planes(ff_out[1], 2, normed_rows))
    pair, acts, slopes, last_parts = ff_forward(
        normed, ff_pairs[1], lower, upper, opposite_in, opposite_out
    )
    records.append(
        (hidden, units, w_in, w_out, pair, qkv, attended, stats, middle, normed, acts, slopes)
    )

    def back_to_middle(parts, upstream, middle, gain):
        return call(
            middle_back_kernel, units_shape + [((1, model_width), f32)], upstream, *parts, middle, gain
        )

    def attention_grads(record, branch):
        _, _, w_in, w_out, _, qkv, attended, stats, *_ = record
        grad_qkv, grad_near, grad_far, near_part, far_part, *halves = plane_attention_back(
            qkv, doc_row, doc_col, attended, stats, *branch, w_in, w_out, place, table, strip
        )
        return grad_qkv, (grad_near, grad_far), (near_part, far_part), halves

    def table_grads(near_and_far):
        return bucket_grads(at_core.reshape(1) * heads_dev + 8, near_and_far, table.shape[0])

    record = records[1]
    hidden, units, _, _, pair, *_, middle, normed, acts, slopes = record
    pres, parts = ff_backward(low, slopes, pair)
    parts, own = plane_scatter(*parts)
    planes = ff_grads(after(pres, own), acts, normed, low)
    parts, ff_lower = tie(parts, shift(planes[1], -1))
    last_parts, _ = plane_scatter(*after(last_parts, parts))
    grad_middle, branch_rows, gain_1 = back_to_middle(parts, upstream, middle, gain_ff[1])
    *branch, ff_upper = plane_gather(branch_rows, round_planes(planes[2], 1, branch_rows))
    grad_qkv, strips_1, parts, halves_1 = attention_grads(record, branch)
    parts, last_parts, opposite_up = tie(
        parts, last_parts, round_planes(planes[3], 2, branch[1])
    )
    parts, own = plane_scatter(*parts)
    parts, opposite_down, output = tie(
        parts,
        round_planes(planes[4], 2, own),
        call(last_kernel, [(row_shape, bf16)], middle, *after(last_parts, own))[0],
    )
    grads_ff = [planes[0], ff_lower, ff_upper, opposite_up, opposite_down]
    upstream, low_rows = call(layer_back_kernel, units_shape, grad_middle, *parts, hidden)

    record = records[0]
    hidden, units, _, _, pair, *_, middle, normed, acts, slopes = record
    grad_in = in_grads(place, *records[1][1], after(grad_qkv, low_rows))
    *low, grads_in_1, table_1 = plane_gather(
        low_rows,
        swap(grad_in.reshape(devices, weight_rows, 3 * width)),
        table_grads(after(strips_1, low_rows)),
    )
    pres, parts = ff_backward(low, slopes, pair)
    parts, own = plane_scatter(*parts)
    planes = ff_grads(after(pres, own), acts, normed, low)
    parts, ff_lower = tie(parts, shift(planes[1], -1))
    grad_middle, branch_rows, gain_0 = back_to_middle(parts, upstream, middle, gain_ff[0])
    *branch, ff_upper = plane_gather(branch_rows, round_planes(planes[2], 1, branch_rows))
    grad_qkv, strips_0, parts, halves_0 = attention_grads(record, branch)
    parts, output, opposite_up = tie(
        parts, turn_in_line(after(output, branch[1])), round_planes(planes[3], 2, branch[1])
    )
    parts, own = plane_scatter(*parts)
    table_0 = table_grads(after(strips_0, own))
    grad_in = in_grads(
        place, *units, after(grad_qkv, own), gain_0, gain_1, table_0, table_1
    )
    parts, opposite_down, grad_in, *halves = tie(
        parts,
        round_planes(planes[4], 2, own),
        grad_in,
        *(jnp.concatenate(after(pair, own)) for pair in zip(halves_0, halves_1)),
    )
    upstream, low_rows = call(layer_back_kernel, units_shape, grad_middle, *parts, hidden)
    grads_in_0 = swap(grad_in.reshape(devices, weight_rows, 3 * width + tile))
    line = turn_in_line(low_rows)
    halves = owners_halves(after(halves, low_rows))
    grad_tokens = turn_in_plane(line)
    output = turn_in_plane(after(output, low_rows)).astype(f32)
    grads_ff = [planes[0], ff_lower, ff_upper, opposite_up, opposite_down] + grads_ff
    grad_up, grad_down = finish_ff(after(grads_ff, low_rows), ff_in.shape)
    own_out, other_out = call(
        add_out_kernel,
        [(attn_out.shape, f32), (attn_out.shape, bf16)],
        place,
        *halves,
        smem=1,
    )
    (grad_attn_out,) = call(
        finish_out_kernel, [(attn_out.shape, f32)], own_out, toggle(other_out, "core", 1)
    )
    own_buckets = table.shape[0] // (z_n * core_n)
    grad_attn_in, grad_gains, ends = call(
        finish_in_kernel,
        [(attn_in.shape, f32), (gains.shape, f32), ((weight_rows, tile), f32)],
        grads_in_0,
        grads_in_1,
        attn_in,
        gain_attn,
    )
    return (
        output[None],
        grad_tokens.astype(f32)[None],
        grad_attn_in,
        grad_attn_out,
        grad_up,
        grad_down,
        grad_gains,
        ends[:own_buckets, 8 : 8 + heads_all // heads_n],
    )


def solution(mesh):
    sizes = dict(mesh.shape)
    cores = 2
    fine = Mesh(
        mesh.devices.reshape(sizes["head"], sizes["blk"] // cores, cores), everyone
    )
    blk = ("z", "core")
    in_specs = (
        P("head", blk, None),
        P(None, blk),
        P(),
        P(None, everyone, None),
        P(None, everyone, None),
        P(None, everyone, None),
        P(None, everyone, None),
        P(None, everyone, None),
        P("head", blk, None),
    )
    out_specs = (
        P("head", blk, None),
        P("head", blk, None),
        P(None, everyone, None),
        P(None, everyone, None),
        P(None, everyone, None),
        P(None, everyone, None),
        P(None, everyone, None),
        P(blk, "head"),
    )
    plane = sizes["head"] == 4 and sizes["blk"] == 8
    local = local_plane if plane else local_general
    return jax.shard_map(local, mesh=fine, in_specs=in_specs, out_specs=out_specs, check_vma=False)
```

```python
import functools

import jax
import jax.numpy as jnp
import numpy as np
from jax import lax
from jax.experimental import pallas as pl
from jax.experimental.pallas import tpu as pltpu
from jax.sharding import Mesh
from jax.sharding import PartitionSpec as P

bounds = (1, 2, 3, 4, 5, 6, 7, 8, 12, 16, 23, 32, 46, 64, 91)
epsilon = 1e-06
masked = -1e30
score_scale = 0.125
head_dim = 64
tile = 128
everyone = ("head", "z", "core")
bf16 = jnp.bfloat16
f32 = jnp.float32


def contract(lhs, rhs, lhs_dim, rhs_dim):
    return lax.dot_general(
        lhs, rhs, (((lhs_dim,), (rhs_dim,)), ((), ())), preferred_element_type=f32
    )


def near_buckets(shape):
    offsets = (
        lax.broadcasted_iota(jnp.int32, shape, 1) - tile - lax.broadcasted_iota(jnp.int32, shape, 0)
    )
    distance = jnp.abs(offsets)
    bucket = jnp.where(offsets > 0, 16, 0)
    for boundary in bounds:
        bucket = bucket + jnp.where(distance >= boundary, 1, 0)
    return bucket


def near_kernel(table, near):
    bucket = near_buckets(near.shape[1:])
    for head in range(near.shape[0]):
        values = jnp.zeros(near.shape[1:], f32)
        for bucket_id in range(table.shape[0]):
            values = jnp.where(bucket == bucket_id, table[bucket_id, head], values)
        near[head] = values


def bucket_kernel(first_lane, near, far, out):
    bucket = near_buckets(near.shape[1:])
    rows = lax.broadcasted_iota(jnp.int32, out.shape, 0)
    lanes = lax.broadcasted_iota(jnp.int32, out.shape, 1)
    total = jnp.zeros(out.shape, f32)
    for head in range(near.shape[0]):
        strip = near[head]
        for bucket_id in range(out.shape[0]):
            value = jnp.sum(jnp.where(bucket == bucket_id, strip, 0.0), axis=0, keepdims=True)
            value = jnp.sum(value, axis=1, keepdims=True)
            if bucket_id in (15, 31):
                value = value + far[head, bucket_id // 16, :1, :1]
            total = jnp.where((rows == bucket_id) & (lanes == head + first_lane[0]), value, total)
    out[...] = total


def fill_band(band, table, near, heads_dev, length):
    for head in range(heads_dev):
        band[head, :, : length - tile] = jnp.full((tile, length - tile), table[15, head], f32)
        band[head, :, length - tile : length + 2 * tile] = near[head]
        band[head, :, length + 2 * tile :] = jnp.full(
            (tile, length - 2 * tile), table[31, head], f32
        )


def band_starts(place, at, length, skip=0):
    return [
        pl.multiple_of(length + (place[skip + block] - place[skip + at]) * tile, tile)
        for block in range(length // tile)
    ]


def attention_kernel(
    heads_dev, length, first, place, table, near, qkv, doc_row, doc_col, out, local, stats, band
):
    step = pl.program_id(0)
    width = heads_dev * head_dim

    @pl.when(step == 0)
    def _():
        fill_band(band, table, near, heads_dev, length)

    row = pl.multiple_of((first[0] + step) * tile, tile)
    out_row = pl.multiple_of((place[first[0] + step] - first[0]) * tile, tile)
    starts = band_starts(place, first[0] + step, length)
    same_doc = doc_col[...] == doc_row[...]
    queries = qkv[pl.ds(row, tile), :width] * bf16(score_scale)
    lanes = lax.broadcasted_iota(jnp.int32, (tile, tile), 1)
    collected = jnp.zeros((tile, tile), f32)
    for head in range(heads_dev):
        own = slice(head * head_dim, (head + 1) * head_dim)
        keys = qkv[:, width + own.start : width + own.stop]
        values = qkv[:, 2 * width + own.start : 2 * width + own.stop]
        scores = contract(queries[:, own], keys, 1, 1)
        scores = scores + jnp.concatenate(
            [band[head, :, pl.ds(start, tile)] for start in starts], axis=1
        )
        scores = jnp.where(same_doc, scores, masked)
        peak = jnp.max(scores, axis=1, keepdims=True)
        weights = jnp.exp(scores - peak)
        total = jnp.sum(weights, axis=1, keepdims=True)
        mixed = contract(weights.astype(bf16), values, 1, 0) / total
        out[pl.ds(out_row, tile), own] = mixed.astype(bf16)
        local[:, own] = mixed.astype(bf16)
        collected = jnp.where(lanes == head, peak + jnp.log(total), collected)
    stats[...] = collected


def attention_back_kernel(
    heads_dev, length, split, first, place, table, near, qkv, doc_row, doc_col, attended, grad_out, stats,
    grad_qkv, grad_near, grad_far, band, grad_band, grad_keys, grad_values,
):
    step = pl.program_id(0)
    width = heads_dev * head_dim

    @pl.when(step == 0)
    def _():
        fill_band(band, table, near, heads_dev, length)
        grad_band[...] = jnp.zeros_like(grad_band)
        grad_keys[...] = jnp.zeros_like(grad_keys)
        grad_values[...] = jnp.zeros_like(grad_values)
        if split > 1:
            grad_qkv[...] = jnp.zeros_like(grad_qkv)

    row = pl.multiple_of((first[0] + step) * tile, tile)
    out_row = pl.multiple_of((place[first[0] + step] - first[0]) * tile, tile)
    starts = band_starts(place, first[0] + step, length)
    same_doc = doc_col[...] == doc_row[...]
    at_step = pl.multiple_of(step * tile, tile)
    queries = qkv[pl.ds(row, tile), :width] * bf16(score_scale)
    for head in range(heads_dev):
        own = slice(head * head_dim, (head + 1) * head_dim)
        keys = qkv[:, width + own.start : width + own.stop]
        values = qkv[:, 2 * width + own.start : 2 * width + own.stop]
        upstream = grad_out[pl.ds(out_row, tile), own]
        scores = contract(queries[:, own], keys, 1, 1) + jnp.concatenate(
            [band[head, :, pl.ds(start, tile)] for start in starts], axis=1
        )
        scores = jnp.where(same_doc, scores, masked)
        weights = jnp.exp(scores - stats[:, head : head + 1])
        delta = jnp.sum(
            upstream.astype(f32) * attended[pl.ds(at_step, tile), own].astype(f32),
            axis=1,
            keepdims=True,
        )
        grad_scores = weights * (contract(upstream, values, 1, 1) - delta)
        for block, start in enumerate(starts):
            grad_band[head, :, pl.ds(start, tile)] += grad_scores[
                :, block * tile : (block + 1) * tile
            ]
        grad_low = grad_scores.astype(bf16)
        grad_values[:, own] += contract(weights.astype(bf16), upstream, 0, 0)
        grad_keys[:, own] += contract(grad_low, queries[:, own], 0, 0)
        grad_qkv[pl.ds(row, tile), own] = (
            contract(grad_low, keys, 1, 0) * score_scale
        ).astype(bf16)

    @pl.when(step == pl.num_programs(0) - 1)
    def _():
        grad_qkv[:, width : 2 * width] = grad_keys[...].astype(bf16)
        grad_qkv[:, 2 * width :] = grad_values[...].astype(bf16)
        for head in range(heads_dev):
            grad_near[head] = grad_band[head, :, length - tile : length + 2 * tile]
            grad_far[head, 0] = jnp.full(
                (8, tile), jnp.sum(grad_band[head, :, : length - tile]), f32
            )
            grad_far[head, 1] = jnp.full(
                (8, tile), jnp.sum(grad_band[head, :, length + 2 * tile :]), f32
            )


def whole(shape):
    return pl.BlockSpec(shape, lambda step: (0,) * len(shape), pipeline_mode=pl.Buffered(1))


def attention(qkv, doc_row, doc_col, first, place, table, near, rows):
    length = qkv.shape[0]
    heads_dev = table.shape[1]
    width = heads_dev * head_dim
    return pl.pallas_call(
        functools.partial(attention_kernel, heads_dev, length),
        grid=(rows // tile,),
        in_specs=[
            pl.BlockSpec(memory_space=pltpu.SMEM),
            pl.BlockSpec(memory_space=pltpu.SMEM),
            pl.BlockSpec(memory_space=pltpu.SMEM),
            whole(near.shape),
            whole(qkv.shape),
            whole(doc_row.shape),
            pl.BlockSpec((tile, 1), lambda step: (step, 0)),
        ],
        out_specs=[
            whole((rows, width)),
            pl.BlockSpec((tile, width), lambda step: (step, 0)),
            pl.BlockSpec((tile, tile), lambda step: (step, 0)),
        ],
        out_shape=[
            jax.ShapeDtypeStruct((rows, width), bf16),
            jax.ShapeDtypeStruct((rows, width), bf16),
            jax.ShapeDtypeStruct((rows, tile), f32),
        ],
        scratch_shapes=[pltpu.VMEM((heads_dev, tile, 2 * length), f32)],
        compiler_params=pltpu.CompilerParams(vmem_limit_bytes=40 * 2**20),
        cost_estimate=pl.CostEstimate(
            flops=4 * rows * length * width,
            bytes_accessed=4 * length * width * 2,
            transcendentals=rows * length * heads_dev,
        ),
    )(first, place, table, near, qkv, doc_row, doc_col)


def attention_back(
    qkv, doc_row, doc_col, attended, grad_out, stats, first, place, table, near, split
):
    length = qkv.shape[0]
    rows = grad_out.shape[0]
    heads_dev = table.shape[1]
    width = heads_dev * head_dim
    return pl.pallas_call(
        functools.partial(attention_back_kernel, heads_dev, length, split),
        grid=(rows // tile,),
        in_specs=[
            pl.BlockSpec(memory_space=pltpu.SMEM),
            pl.BlockSpec(memory_space=pltpu.SMEM),
            pl.BlockSpec(memory_space=pltpu.SMEM),
            whole(near.shape),
            whole(qkv.shape),
            whole(doc_row.shape),
            pl.BlockSpec((tile, 1), lambda step: (step, 0)),
            whole((rows, width)),
            whole((rows, width)),
            pl.BlockSpec((tile, tile), lambda step: (step, 0)),
        ],
        out_specs=[
            whole((length, 3 * width)),
            whole((heads_dev, tile, 3 * tile)),
            whole((heads_dev, 2, 8, tile)),
        ],
        out_shape=[
            jax.ShapeDtypeStruct((length, 3 * width), bf16),
            jax.ShapeDtypeStruct((heads_dev, tile, 3 * tile), f32),
            jax.ShapeDtypeStruct((heads_dev, 2, 8, tile), f32),
        ],
        scratch_shapes=[
            pltpu.VMEM((heads_dev, tile, 2 * length), f32),
            pltpu.VMEM((heads_dev, tile, 2 * length), f32),
            pltpu.VMEM((length, width), f32),
            pltpu.VMEM((length, width), f32),
        ],
        compiler_params=pltpu.CompilerParams(vmem_limit_bytes=48 * 2**20),
        cost_estimate=pl.CostEstimate(
            flops=10 * rows * length * width,
            bytes_accessed=8 * length * width * 2,
            transcendentals=rows * length * heads_dev,
        ),
    )(first, place, table, near, qkv, doc_row, doc_col, attended, grad_out, stats)


def call(kernel, shapes, *operands, smem=0):
    return pl.pallas_call(
        kernel,
        in_specs=[pl.BlockSpec(memory_space=pltpu.SMEM)] * smem
        + [pl.BlockSpec(memory_space=pltpu.VMEM)] * (len(operands) - smem),
        out_specs=[pl.BlockSpec(memory_space=pltpu.VMEM)] * len(shapes),
        out_shape=[jax.ShapeDtypeStruct(shape, kind) for shape, kind in shapes],
        compiler_params=pltpu.CompilerParams(vmem_limit_bytes=10 * 2**20),
    )(*operands)


def share_in_kernel(place, attn_in, gains, near, far):
    layers, rows = attn_in.shape[:2]
    half = near.shape[0] // (layers * rows)
    width = near.shape[1] // 3
    for index in range(2 * half):
        member = place[index]
        for layer_id in range(layers):
            block = jnp.concatenate(
                [
                    attn_in[
                        layer_id,
                        :,
                        pl.ds(pl.multiple_of((part * 2 * half + member) * width, width), width),
                    ]
                    for part in range(3)
                ],
                axis=1,
            )
            at = (index % half * layers + layer_id) * rows
            out = near if index < half else far
            out[at : at + rows] = (block.astype(f32) * gains[layer_id]).astype(bf16)


def join_kernel(*refs):
    shares, outs = refs[:4], refs[4:]
    rows = outs[0].shape[0] // 8
    for chip, share in enumerate(shares):
        for core in range(2):
            for layer_id, out in enumerate(outs):
                source = (core * len(outs) + layer_id) * rows
                target = (chip * 2 + core) * rows
                out[target : target + rows] = share[source : source + rows]


def row_of(chip, plane, core, rows, planes=4):
    return pl.multiple_of(((chip * planes + plane) * 2 + core) * rows, rows)


def assemble_in_kernel(place, own, lower, upper, opposite, out):
    at_z, at_core, at_head = place[8], place[0] % 2, place[0] // 2
    rows = own.shape[0] // 8
    for part, offset in ((own, 0), (lower, 3), (upper, 1), (opposite, 2)):
        plane = (at_z + offset) % 4
        for index in range(8):
            row = row_of(at_head ^ (index // 2), plane, at_core ^ (index % 2), rows)
            out[pl.ds(row, rows)] = part[index * rows : (index + 1) * rows]


def plane_attention_kernel(
    length, place, table, strip, near, far, w_in, *refs
):
    halves, (doc_row, doc_col, w_out, qkv, attended, stats, near_part, far_part, band) = (
        refs[:2], refs[2:],
    )
    step = pl.program_id(0)
    half = length // 2
    heads_dev = table.shape[1]
    width = heads_dev * head_dim

    @pl.when(step == 0)
    def _():
        fill_band(band, table, strip, heads_dev, length)
        swapped = place[length // tile] % 2 == 1
        rows = width // 2
        w_out[:rows] = jnp.where(swapped, halves[1][...], halves[0][...])
        w_out[rows:] = jnp.where(swapped, halves[0][...], halves[1][...])
        qkv[:half] = contract(near[...], w_in[...], 1, 0).astype(bf16)
        qkv[half:] = contract(far[...], w_in[...], 1, 0).astype(bf16)

    row = pl.multiple_of(step * tile, tile)
    starts = band_starts(place, step, length, length // tile + 1)
    same_doc = doc_col[...] == doc_row[...]
    queries = qkv[pl.ds(row, tile), :width] * bf16(score_scale)
    lanes = lax.broadcasted_iota(jnp.int32, (tile, tile), 1)
    collected = jnp.zeros((tile, tile), f32)
    results = []
    for head in range(heads_dev):
        own = slice(head * head_dim, (head + 1) * head_dim)
        keys = qkv[:, width + own.start : width + own.stop]
        values = qkv[:, 2 * width + own.start : 2 * width + own.stop]
        scores = contract(queries[:, own], keys, 1, 1) + jnp.concatenate(
            [band[head, :, pl.ds(start, tile)] for start in starts], axis=1
        )
        scores = jnp.where(same_doc, scores, masked)
        peak = jnp.max(scores, axis=1, keepdims=True)
        weights = jnp.exp(scores - peak)
        total = jnp.sum(weights, axis=1, keepdims=True)
        results.append((contract(weights.astype(bf16), values, 1, 0) / total).astype(bf16))
        collected = jnp.where(lanes == head, peak + jnp.log(total), collected)
    stats[...] = collected
    merged = jnp.concatenate(results, axis=1)
    attended[...] = merged
    part = contract(merged, w_out[...], 1, 0)

    @pl.when(row < half)
    def _():
        near_part[...] = part

    @pl.when(row >= half)
    def _():
        far_part[...] = part.astype(bf16)


def near_block(steps, columns):
    return pl.BlockSpec((tile, columns), lambda step: (jnp.minimum(step, steps // 2 - 1), 0))


def far_block(steps, columns):
    return pl.BlockSpec((tile, columns), lambda step: (jnp.maximum(step - steps // 2, 0), 0))


def plane_attention(near, far, w_in, halves, doc_row, doc_col, place, table, strip):
    length, model_width = 2 * near.shape[0], near.shape[1]
    steps = length // tile
    heads_dev = table.shape[1]
    width = heads_dev * head_dim
    return pl.pallas_call(
        functools.partial(plane_attention_kernel, length),
        grid=(steps,),
        in_specs=[
            pl.BlockSpec(memory_space=pltpu.SMEM),
            pl.BlockSpec(memory_space=pltpu.SMEM),
            whole(strip.shape),
            whole(near.shape),
            whole(far.shape),
            whole(w_in.shape),
            *[whole(half.shape) for half in halves],
            whole(doc_row.shape),
            pl.BlockSpec((tile, 1), lambda step: (step, 0)),
        ],
        out_specs=[
            whole((width, model_width)),
            whole((length, 3 * width)),
            pl.BlockSpec((tile, width), lambda step: (step, 0)),
            pl.BlockSpec((tile, tile), lambda step: (step, 0)),
            near_block(steps, model_width),
            far_block(steps, model_width),
        ],
        out_shape=[
            jax.ShapeDtypeStruct((width, model_width), bf16),
            jax.ShapeDtypeStruct((length, 3 * width), bf16),
            jax.ShapeDtypeStruct((length, width), bf16),
            jax.ShapeDtypeStruct((length, tile), f32),
            jax.ShapeDtypeStruct((length // 2, model_width), f32),
            jax.ShapeDtypeStruct((length // 2, model_width), bf16),
        ],
        scratch_shapes=[pltpu.VMEM((heads_dev, tile, 2 * length), f32)],
        compiler_params=pltpu.CompilerParams(vmem_limit_bytes=14 * 2**20),
        cost_estimate=pl.CostEstimate(
            flops=4 * length * length * width + 8 * length * model_width * width,
            bytes_accessed=12 * 2**20,
            transcendentals=length * length * heads_dev,
        ),
    )(place, table, strip, near, far, w_in, *halves, doc_row, doc_col)


def plane_attention_back_kernel(
    length, place, table, strip, qkv, doc_row, doc_col, attended, stats, near, far, w_in, w_out,
    grad_qkv, grad_near, grad_far, near_part, far_part, *rest
):
    halves, (band, grad_band, grad_keys, grad_values, out_sum) = rest[:2], rest[2:]
    step = pl.program_id(0)
    half = length // 2
    heads_dev = table.shape[1]
    width = heads_dev * head_dim

    @pl.when(step == 0)
    def _():
        fill_band(band, table, strip, heads_dev, length)
        grad_band[...] = jnp.zeros_like(grad_band)
        grad_keys[...] = jnp.zeros_like(grad_keys)
        grad_values[...] = jnp.zeros_like(grad_values)
        out_sum[...] = jnp.zeros_like(out_sum)

    row = pl.multiple_of(step * half, half)
    branch = jnp.where(step == 0, near[...], far[...])
    merged = attended[...]
    grad_merged = contract(branch, w_out[...], 1, 1).astype(bf16)
    out_sum[...] += contract(merged, branch, 0, 0)
    products = grad_merged.astype(f32) * merged.astype(f32)
    queries = qkv[pl.ds(row, half), :width] * bf16(score_scale)
    blocks = half // tile
    for head in range(heads_dev):
        own = slice(head * head_dim, (head + 1) * head_dim)
        keys = qkv[:, width + own.start : width + own.stop]
        values = qkv[:, 2 * width + own.start : 2 * width + own.stop]
        upstream = grad_merged[:, own]
        raw_scores = contract(queries[:, own], keys, 1, 1)
        grad_weights = contract(upstream, values, 1, 1)
        delta = jnp.sum(products[:, own], axis=1, keepdims=True)
        weights_low, grads_low = [], []
        for block in range(blocks):
            lines = slice(block * tile, (block + 1) * tile)
            starts = band_starts(place, step * blocks + block, length, length // tile + 1)
            scores = raw_scores[lines] + jnp.concatenate(
                [band[head, :, pl.ds(start, tile)] for start in starts], axis=1
            )
            scores = jnp.where(doc_col[lines] == doc_row[...], scores, masked)
            weights = jnp.exp(scores - stats[lines, head : head + 1])
            grad_scores = weights * (grad_weights[lines] - delta[lines])
            for index, start in enumerate(starts):
                grad_band[head, :, pl.ds(start, tile)] += grad_scores[
                    :, index * tile : (index + 1) * tile
                ]
            weights_low.append(weights.astype(bf16))
            grads_low.append(grad_scores.astype(bf16))
        weights_low, grads_low = jnp.concatenate(weights_low), jnp.concatenate(grads_low)
        grad_values[:, own] += contract(weights_low, upstream, 0, 0)
        grad_keys[:, own] += contract(grads_low, queries[:, own], 0, 0)
        grad_qkv[pl.ds(row, half), own] = (
            contract(grads_low, keys, 1, 0) * score_scale
        ).astype(bf16)

    @pl.when(step == pl.num_programs(0) - 1)
    def _():
        grad_qkv[:, width : 2 * width] = grad_keys[...].astype(bf16)
        grad_qkv[:, 2 * width :] = grad_values[...].astype(bf16)
        far_part[...] = contract(grad_qkv[half:], w_in[...], 1, 1).astype(bf16)
        near_part[...] = contract(grad_qkv[:half], w_in[...], 1, 1)
        rows = width // 2
        for index, part in enumerate(halves):
            block = index ^ place[length // tile] % 2
            part[...] = out_sum[pl.ds(pl.multiple_of(block * rows, rows), rows)].astype(bf16)
        for head in range(heads_dev):
            grad_near[head] = grad_band[head, :, length - tile : length + 2 * tile]
            grad_far[head, 0] = jnp.full(
                (8, tile), jnp.sum(grad_band[head, :, : length - tile]), f32
            )
            grad_far[head, 1] = jnp.full(
                (8, tile), jnp.sum(grad_band[head, :, length + 2 * tile :]), f32
            )


def plane_attention_back(
    qkv, doc_row, doc_col, attended, stats, near, far, w_in, w_out, place, table, strip
):
    length, model_width = 2 * near.shape[0], near.shape[1]
    half = length // 2
    heads_dev = table.shape[1]
    width = heads_dev * head_dim
    shapes = [
        ((length, 3 * width), bf16),
        ((heads_dev, tile, 3 * tile), f32),
        ((heads_dev, 2, 8, tile), f32),
        ((length // 2, model_width), f32),
        ((length // 2, model_width), bf16),
    ] + [((width // 2, model_width), bf16)] * 2
    return pl.pallas_call(
        functools.partial(plane_attention_back_kernel, length),
        grid=(2,),
        in_specs=[
            pl.BlockSpec(memory_space=pltpu.SMEM),
            pl.BlockSpec(memory_space=pltpu.SMEM),
            whole(strip.shape),
            whole(qkv.shape),
            whole(doc_row.shape),
            pl.BlockSpec((half, 1), lambda step: (step, 0)),
            pl.BlockSpec((half, width), lambda step: (step, 0)),
            pl.BlockSpec((half, tile), lambda step: (step, 0)),
            whole((half, model_width)),
            whole((half, model_width)),
            whole(w_in.shape),
            whole(w_out.shape),
        ],
        out_specs=[whole(shape) for shape, _ in shapes],
        out_shape=[jax.ShapeDtypeStruct(shape, kind) for shape, kind in shapes],
        scratch_shapes=[
            pltpu.VMEM((heads_dev, tile, 2 * length), f32),
            pltpu.VMEM((heads_dev, tile, 2 * length), f32),
            pltpu.VMEM((length, width), f32),
            pltpu.VMEM((length, width), f32),
            pltpu.VMEM((width, model_width), f32),
        ],
        compiler_params=pltpu.CompilerParams(vmem_limit_bytes=32 * 2**20),
        cost_estimate=pl.CostEstimate(
            flops=10 * length * length * width + 10 * length * model_width * width,
            bytes_accessed=12 * 2**20,
            transcendentals=length * length * heads_dev,
        ),
    )(place, table, strip, qkv, doc_row, doc_col, attended, stats, near, far, w_in, w_out)


def gelu_and_slope(pre_act):
    size = jnp.abs(pre_act)
    gauss = jnp.exp(-0.5 * pre_act * pre_act)
    ratio = 1.0 / (1.0 + np.float32(0.3275911 * 0.5**0.5) * size)
    series = np.float32(1.061405429)
    for factor in (-1.453152027, 1.421413741, -0.284496736, 0.254829592):
        series = series * ratio + np.float32(factor)
    tail = 0.5 * series * ratio * gauss
    cumulative = jnp.where(pre_act < 0, tail, 1.0 - tail)
    slope = cumulative + pre_act * gauss * np.float32((2 * np.pi) ** -0.5)
    return pre_act * cumulative, slope


def ff_kernel(rows, pair, activated, slope, part):
    columns = rows.shape[1]
    value, gradient = gelu_and_slope(contract(rows[...], pair[:, :columns], 1, 1))
    activated[...] = value.astype(bf16)
    slope[...] = gradient.astype(bf16)
    part[...] = contract(activated[...], pair[:, columns:], 1, 0).astype(part.dtype)


def ff_first_kernel(rows, *refs):
    parts, (activated, slope, part, pair) = refs[:5], refs[5:]

    @pl.when(pl.program_id(0) == 0)
    def _():
        units, columns = parts[0].shape[0], rows.shape[1]
        for index, ref in enumerate(parts[:3]):
            pair[index * units : (index + 1) * units] = ref[...]
        pair[3 * units :, :columns] = parts[3][...]
        pair[3 * units :, columns:] = parts[4][...]

    ff_kernel(rows, pair, activated, slope, part)


def ff_back_kernel(rows, slope, pair, grad_pre, part):
    columns = rows.shape[1]
    grad_act = contract(rows[...], pair[:, columns:], 1, 1)
    grad_pre[...] = (grad_act * slope[...].astype(f32)).astype(bf16)
    part[...] = contract(grad_pre[...], pair[:, :columns], 1, 0).astype(part.dtype)


def by_rows(kernel, step_rows, row_operands, whole_operands, outs, whole_outs=()):
    rows = row_operands[0].shape[0]
    return pl.pallas_call(
        kernel,
        grid=(rows // step_rows,),
        in_specs=[
            pl.BlockSpec((step_rows, operand.shape[1]), lambda step: (step, 0))
            for operand in row_operands
        ]
        + [whole(operand.shape) for operand in whole_operands],
        out_specs=[pl.BlockSpec((step_rows, columns), lambda step: (step, 0)) for columns, _ in outs]
        + [whole(shape) for shape in whole_outs],
        out_shape=[jax.ShapeDtypeStruct((rows, columns), kind) for columns, kind in outs]
        + [jax.ShapeDtypeStruct(shape, bf16) for shape in whole_outs],
        compiler_params=pltpu.CompilerParams(vmem_limit_bytes=10 * 2**20),
        cost_estimate=pl.CostEstimate(
            flops=4 * rows * outs[0][0] * row_operands[0].shape[1],
            bytes_accessed=6 * 2**20,
            transcendentals=0,
        ),
    )(*row_operands, *whole_operands)


def ff_grads_kernel(
    pre_near, pre_far, act_near, act_far, normed_near, normed_far, low_near, low_far, *outs
):
    columns = normed_near.shape[1]
    units = outs[0].shape[0]
    up = (
        contract(pre_near[...], normed_near[...], 0, 0)
        + contract(pre_far[...], normed_far[...], 0, 0)
    ).astype(bf16)
    down = (
        contract(act_near[...], low_near[...], 0, 0) + contract(act_far[...], low_far[...], 0, 0)
    ).astype(bf16)

    @pl.when(pl.program_id(0) == 0)
    def _():
        for index in range(2):
            block = slice(index * units, (index + 1) * units)
            outs[index][:, :columns] = up[block]
            outs[index][:, columns:] = down[block]

    @pl.when(pl.program_id(0) == 1)
    def _():
        outs[2][:, :columns] = up[:units]
        outs[2][:, columns:] = down[:units]
        outs[3][...] = up[units:]
        outs[4][...] = down[units:]


def ff_grads(pre, act, normed, low):
    rows, hidden_units = pre[0].shape
    columns = normed[0].shape[1]
    shapes = [(hidden_units // 4, 2 * columns)] * 3 + [(hidden_units // 4, columns)] * 2
    return pl.pallas_call(
        ff_grads_kernel,
        grid=(2,),
        in_specs=[pl.BlockSpec((rows, hidden_units // 2), lambda step: (0, step))] * 4
        + [whole((rows, columns))] * 4,
        out_specs=[whole(shape) for shape in shapes],
        out_shape=[jax.ShapeDtypeStruct(shape, bf16) for shape in shapes],
        compiler_params=pltpu.CompilerParams(vmem_limit_bytes=14 * 2**20),
        cost_estimate=pl.CostEstimate(
            flops=8 * rows * hidden_units * columns, bytes_accessed=8 * 2**20, transcendentals=0
        ),
    )(*pre, *act, *normed, *low)


def in_grads_kernel(place, near, far, grad_qkv, *refs):
    ends, (total, extra) = refs[:-2], refs[-2:]
    half = near.shape[0]
    columns = grad_qkv.shape[1]
    total[:, :columns] = (
        contract(near[...], grad_qkv[:half], 0, 0) + contract(far[...], grad_qkv[half:], 0, 0)
    ).astype(bf16)
    if ends:
        gain_0, gain_1, table_0, table_1 = ends
        rows = near.shape[1] // 32
        lines = lax.broadcasted_iota(jnp.int32, (tile, gain_0.shape[1]), 0)
        gains = jnp.where(lines == 0, gain_0[...], jnp.where(lines == 1, gain_1[...], 0.0))
        extra[...] = jnp.transpose(gains)
        table = table_0[...] + table_1[...]
        buckets = table.shape[0] // 8
        blank = jnp.zeros((8 - buckets, tile), f32)
        for block in range(8):
            row = pl.multiple_of((place[0] // 2 * 8 + block) * rows, rows)
            extra[pl.ds(row, 8)] += jnp.concatenate(
                [table[block * buckets : (block + 1) * buckets], blank]
            )
        total[:, columns:] = extra[...].astype(bf16)


def in_grads(place, near, far, grad_qkv, *ends):
    columns = grad_qkv.shape[1] + (tile if ends else 0)
    return pl.pallas_call(
        in_grads_kernel,
        in_specs=[pl.BlockSpec(memory_space=pltpu.SMEM)]
        + [pl.BlockSpec(memory_space=pltpu.VMEM)] * (3 + len(ends)),
        out_specs=pl.BlockSpec(memory_space=pltpu.VMEM),
        out_shape=jax.ShapeDtypeStruct((near.shape[1], columns), bf16),
        scratch_shapes=[pltpu.VMEM((near.shape[1], tile), f32)],
        compiler_params=pltpu.CompilerParams(vmem_limit_bytes=14 * 2**20),
        cost_estimate=pl.CostEstimate(
            flops=4 * near.shape[0] * near.shape[1] * columns,
            bytes_accessed=4 * 2**20,
            transcendentals=0,
        ),
    )(place, near, far, grad_qkv, *ends)


def combine_kernel(near_part, arrived, own, x_part, y_part, xy_part):
    rows = own.shape[0]
    own[...] = near_part[:rows] + arrived[:rows].astype(f32)
    for bits, out in ((1, x_part), (2, y_part), (3, xy_part)):
        block = slice(bits * rows, (bits + 1) * rows)
        out[...] = (near_part[block] + arrived[block].astype(f32)).astype(bf16)


def added(own, x_part, y_part, xy_part):
    return (own[...] + x_part[...].astype(f32)) + (
        y_part[...].astype(f32) + xy_part[...].astype(f32)
    )


def close_kernel(kept, own, x_part, y_part, xy_part, hidden, units):
    total = kept[...] + added(own, x_part, y_part, xy_part)
    hidden[...] = total
    units[...] = (total * inverse_rms(total)).astype(bf16)


def close_gain_kernel(kept, own, x_part, y_part, xy_part, gain, hidden, normed):
    total = kept[...] + added(own, x_part, y_part, xy_part)
    hidden[...] = total
    normed[...] = (total * inverse_rms(total) * gain[...]).astype(bf16)


def last_kernel(kept, own, x_part, y_part, xy_part, hidden):
    hidden[...] = (kept[...] + added(own, x_part, y_part, xy_part)).astype(bf16)


def middle_back_kernel(
    upstream, own, x_part, y_part, xy_part, middle, gain, grad_middle, branch, grad_gain
):
    grad_normed = added(own, x_part, y_part, xy_part)
    inverse = inverse_rms(middle[...])
    grad_gain[...] = jnp.sum(grad_normed * middle[...] * inverse, axis=0, keepdims=True)
    total = upstream[...].astype(f32) + unit_norm_back(
        middle[...], inverse, grad_normed * gain[...]
    )
    grad_middle[...] = total
    branch[...] = total.astype(bf16)


def layer_back_kernel(grad_middle, own, x_part, y_part, xy_part, hidden, upstream, low):
    total = grad_middle[...] + unit_norm_back(
        hidden[...], inverse_rms(hidden[...]), added(own, x_part, y_part, xy_part)
    )
    upstream[...] = total
    low[...] = total.astype(bf16)


def pair_kernel(axis, near, arrived, *outs):
    rows = near.shape[0] // len(outs)
    for index, out in enumerate(outs):
        block = slice(index * rows, (index + 1) * rows)
        if axis == 0:
            out[:rows] = near[block]
            out[rows:] = arrived[block]
        else:
            columns = near.shape[1]
            out[:, :columns] = near[block]
            out[:, columns:] = arrived[block]


def unit_kernel(tokens, hidden, units):
    total = tokens[...].astype(f32)
    hidden[...] = total
    units[...] = (total * inverse_rms(total)).astype(bf16)


def finish_in_kernel(*refs):
    attn_in, gains, grad_in, grad_gain, ends = refs[-5:]
    layers, rows = attn_in.shape[:2]
    width = tile
    members = attn_in.shape[2] // (3 * width)
    ends[...] = jnp.zeros_like(ends)
    for layer_id in range(layers):
        shares = refs[layer_id]
        row_dot = jnp.zeros((rows, 1), f32)
        for member in range(members):
            total = sum_of_four(
                [shares.at[(member // 2 * 4 + plane) * 2 + member % 2] for plane in range(4)]
            )
            for part in range(3):
                block = total[:, part * width : (part + 1) * width]
                columns = slice((part * members + member) * width, (part * members + member + 1) * width)
                grad_in[layer_id, :, columns] = block * gains[layer_id]
                row_dot = row_dot + jnp.sum(
                    block * attn_in[layer_id, :, columns].astype(f32), axis=1, keepdims=True
                )
            if layer_id == 0:
                ends[...] += total[:, 3 * width :]
        grad_gain[layer_id] = jnp.concatenate(
            [row_dot, ends[:, layer_id : layer_id + 1]], axis=1
        )


def sum_of_four(parts):
    return (parts[0][...].astype(f32) + parts[1][...].astype(f32)) + (
        parts[2][...].astype(f32) + parts[3][...].astype(f32)
    )


def finish_ff_kernel(*refs):
    count = (len(refs) - 3) // 2
    sources, grads, held, done = refs[:count], refs[count : count + 2], refs[count + 2 : -1], refs[-1]
    copies = [
        pltpu.make_async_copy(source, target, done.at[index])
        for index, (source, target) in enumerate(zip(sources, held))
    ]
    for copy in copies:
        copy.start()
    for copy in copies:
        copy.wait()
    refs = held
    columns = grads[0].shape[2]
    for layer_id in range(grads[0].shape[0]):
        parts = refs[5 * layer_id : 5 * layer_id + 5]
        for side, out in enumerate(grads):
            halves = [part.at[:, side * columns : (side + 1) * columns] for part in parts[:3]]
            out[layer_id] = sum_of_four(halves + [parts[3 + side]])


def finish_ff(grads, shape):
    return pl.pallas_call(
        finish_ff_kernel,
        in_specs=[pl.BlockSpec(memory_space=pl.ANY)] * len(grads),
        out_specs=[pl.BlockSpec(memory_space=pltpu.VMEM)] * 2,
        out_shape=[jax.ShapeDtypeStruct(shape, f32)] * 2,
        scratch_shapes=[pltpu.VMEM(grad.shape, bf16) for grad in grads]
        + [pltpu.SemaphoreType.DMA((len(grads),))],
        compiler_params=pltpu.CompilerParams(vmem_limit_bytes=14 * 2**20),
    )(*grads)


def add_out_kernel(place, *refs):
    parts, (own, other) = refs[:-2], refs[-2:]
    for layer_id in range(own.shape[0]):
        total = parts[2 * layer_id][...].astype(f32) + parts[2 * layer_id + 1][...].astype(f32)
        rows = total.shape[0] // 2
        second = place[0] % 2 == 1
        own[layer_id] = jnp.where(second, total[rows:], total[:rows])
        other[layer_id] = jnp.where(second, total[:rows], total[rows:]).astype(bf16)


def finish_out_kernel(own, arrived, out):
    out[...] = own[...] + arrived[...].astype(f32)


def inverse_rms(hidden):
    return lax.rsqrt(jnp.mean(hidden * hidden, axis=-1, keepdims=True) + epsilon)


def prepare(bias_table, first_head, heads_dev):
    table = lax.dynamic_slice_in_dim(bias_table, first_head, heads_dev, 1)
    (near,) = call(near_kernel, [((heads_dev, tile, 3 * tile), f32)], table, smem=1)
    return table, near


def bucket_grads(first_lane, grads, bucket_count):
    (total,) = call(bucket_kernel, [((bucket_count, tile), f32)], first_lane, *grads, smem=1)
    return total


def gelu_parts(pre_act):
    cumulative = 0.5 * (1.0 + lax.erf(pre_act * np.float32(0.5**0.5)))
    slope = cumulative + pre_act * jnp.exp(-0.5 * pre_act * pre_act) * np.float32(
        (2 * np.pi) ** -0.5
    )
    return (pre_act * cumulative).astype(bf16), slope


def unit_norm_back(hidden, inverse, grad_unit):
    unit = hidden * inverse
    return inverse * (grad_unit - unit * jnp.mean(grad_unit * unit, axis=-1, keepdims=True))


def gather_rows(block, axes):
    return lax.all_gather(block, axes, axis=0, tiled=True)


def toggle(array, axis, bits):
    return lax.ppermute(array, axis, [(i, i ^ bits) for i in range(lax.axis_size(axis))])


def shift(array, by):
    planes = lax.axis_size("z")
    return lax.ppermute(array, "z", [(i, (i + by) % planes) for i in range(planes)])


def plane_gather(block, *holds):
    near = jnp.concatenate([block] + [toggle(block, "head", bits) for bits in (1, 2, 3)])
    near, *holds = tie(near, *holds)
    return (near, toggle(near, "core", 1), *holds)


def plane_scatter(near_part, far_part):
    rows, columns = near_part.shape[0] // 4, near_part.shape[1]
    own, *others = call(
        combine_kernel,
        [((rows, columns), f32)] + [((rows, columns), bf16)] * 3,
        near_part,
        toggle(far_part, "core", 1),
    )
    shares = [own] + [toggle(other, "head", bits) for bits, other in zip((1, 2, 3), others)]
    return shares, own


def tie(*arrays):
    return lax.optimization_barrier(arrays)


def after(array, other):
    return lax.optimization_barrier((array, other))[0]


def scatter_sum(partial, axes, members):
    blocks = partial.astype(bf16).reshape(members, -1, partial.shape[1])
    return jnp.sum(lax.all_to_all(blocks, axes, 0, 0, tiled=True).astype(f32), axis=0)


def local_general(tokens, doc_start, bias_table, attn_in, attn_out, ff_in, ff_out, gains, cotangent):
    heads_n, z_n, core_n = (lax.axis_size(axis) for axis in everyone)
    devices = heads_n * z_n * core_n
    group, spare = ("z", "core"), "head"
    ff_group, ff_spare, ff_members = ("head", "core"), "z", heads_n * core_n
    blocks = z_n * core_n
    block_rows, model_width = tokens.shape[1:]
    layer_count, weight_rows = attn_in.shape[:2]
    length = block_rows * blocks
    heads_all = bias_table.shape[1]
    member = lax.axis_index("z") * core_n + lax.axis_index("core")
    heads_dev = max(1, heads_all // blocks)
    head_groups = heads_all // heads_dev
    split = blocks // head_groups
    head_group, query_part = member // split, member % split
    query_rows = length // split
    width = heads_dev * head_dim
    first = (query_part * (query_rows // tile)).astype(jnp.int32).reshape(1)
    place = jnp.arange(length // tile, dtype=jnp.int32)
    out_row = head_group * width

    def swap(array):
        return lax.all_to_all(array, everyone, 0, 0, tiled=True)

    starts = jnp.broadcast_to(
        doc_start.astype(f32)[:, None], (heads_n, blocks, block_rows)
    ).reshape(devices, block_rows)
    ff_gains = gains[:, :, 1].astype(f32).reshape(1, -1)
    small = swap(
        jnp.concatenate(
            [starts, jnp.broadcast_to(ff_gains, (devices, layer_count * weight_rows))], axis=1
        )
    )
    doc_row = small[:blocks, :block_rows].reshape(1, length)
    doc_col = lax.dynamic_slice_in_dim(
        doc_row.reshape(length, 1), query_part * query_rows, query_rows, 0
    )
    gain_ff = jnp.transpose(
        small[:, block_rows:].reshape(devices, layer_count, weight_rows), (1, 0, 2)
    ).reshape(layer_count, 1, model_width)
    table, near = prepare(bias_table, head_group * heads_dev, heads_dev)

    gain_attn = gains[:, :, 0].astype(f32)[:, :, None]
    own_in = attn_in.astype(f32)

    def fetch_in(layer_id):
        scaled = (own_in[layer_id] * gain_attn[layer_id]).astype(bf16)
        columns = jnp.transpose(
            scaled.reshape(weight_rows, 3, head_groups, width), (2, 0, 1, 3)
        ).reshape(head_groups, weight_rows, 3 * width)
        columns = jnp.repeat(columns, split, axis=0)
        columns = jnp.broadcast_to(columns[None], (heads_n, *columns.shape))
        return swap(columns.reshape(devices, weight_rows, 3 * width)).reshape(
            model_width, 3 * width
        )

    def fetch_ff(layer_id):
        pair = jnp.concatenate([ff_in[layer_id], ff_out[layer_id]], axis=1)
        pair = gather_rows(pair, ff_spare)
        return pair[:, :model_width], pair[:, model_width:]

    hidden, upstream = tokens[0].astype(f32), cotangent[0]
    weights_in = [fetch_in(layer_id) for layer_id in range(layer_count)]
    weights_out = lax.dynamic_slice_in_dim(
        lax.all_gather(attn_out, everyone, axis=1, tiled=True), out_row, width, 1
    )
    weights_ff = [fetch_ff(layer_id) for layer_id in range(layer_count)]

    records = []
    for layer_id in range(layer_count):
        w_in, w_out, (w_up, w_down) = (
            weights_in[layer_id], weights_out[layer_id], weights_ff[layer_id],
        )
        inverse = inverse_rms(hidden)
        units = gather_rows((hidden * inverse).astype(bf16), group)
        qkv = jnp.dot(units, w_in, preferred_element_type=f32).astype(bf16)
        attended, _, stats = attention(
            qkv, doc_row, doc_col, first, place, table, near, query_rows
        )
        mixed = jnp.dot(attended, w_out, preferred_element_type=f32)
        if split > 1:
            mixed = lax.dynamic_update_slice_in_dim(
                jnp.zeros((length, model_width), f32), mixed, query_part * query_rows, 0
            )
        middle = hidden + scatter_sum(mixed, group, blocks)
        inverse_ff = inverse_rms(middle)
        normed_ff = gather_rows((middle * inverse_ff * gain_ff[layer_id]).astype(bf16), ff_group)
        activated, slope = gelu_parts(contract(normed_ff, w_up, 1, 1))
        ff_result = jnp.dot(activated, w_down, preferred_element_type=f32)
        records.append(
            (hidden, inverse, units, qkv, attended, stats, middle, inverse_ff, normed_ff,
             activated, slope)
        )
        hidden = middle + scatter_sum(ff_result, ff_group, ff_members)
    output = hidden

    grads_ff, grads_in, grads_out, grads_gain_ff, grads_table = (
        [None] * layer_count for _ in range(5)
    )
    for layer_id in reversed(range(layer_count)):
        w_in, w_out, (w_up, w_down) = (
            weights_in[layer_id], weights_out[layer_id], weights_ff[layer_id],
        )
        (hidden, inverse, units, qkv, attended, stats, middle, inverse_ff, normed_ff,
         activated, slope) = records[layer_id]
        grad_low = gather_rows(upstream.astype(bf16), ff_group)
        grad_pre = (contract(grad_low, w_down, 1, 1) * slope).astype(bf16)
        grad_normed = scatter_sum(
            jnp.dot(grad_pre, w_up, preferred_element_type=f32), ff_group, ff_members
        )
        grad_pair = jnp.concatenate(
            [contract(grad_pre, normed_ff, 0, 0), contract(activated, grad_low, 0, 0)], axis=1
        ).astype(bf16)
        grads_ff[layer_id] = lax.psum_scatter(
            grad_pair, ff_spare, scatter_dimension=0, tiled=True
        ).astype(f32)
        grads_gain_ff[layer_id] = jnp.sum(grad_normed * middle * inverse_ff, axis=0)
        grad_middle = upstream + unit_norm_back(
            middle, inverse_ff, grad_normed * gain_ff[layer_id]
        )
        branch = gather_rows(grad_middle.astype(bf16), group)
        if split > 1:
            branch = lax.dynamic_slice_in_dim(branch, query_part * query_rows, query_rows, 0)
        grad_attended = contract(branch, w_out, 1, 1).astype(bf16)
        grad_qkv, grad_near, grad_far = attention_back(
            qkv, doc_row, doc_col, attended, grad_attended, stats, first, place, table, near, split
        )
        grads_table[layer_id] = (grad_near, grad_far)
        grad_units = scatter_sum(contract(grad_qkv, w_in, 1, 1), group, blocks)
        upstream = grad_middle + unit_norm_back(hidden, inverse, grad_units)
        grad_out = lax.dynamic_update_slice_in_dim(
            jnp.zeros((model_width, model_width), bf16),
            contract(attended, branch, 0, 0).astype(bf16),
            out_row,
            0,
        )
        grads_out[layer_id] = lax.psum_scatter(
            grad_out, everyone, scatter_dimension=0, tiled=True
        ).astype(f32)
        grads_in[layer_id] = contract(units, grad_qkv, 0, 0).astype(bf16)

    bucket_count = table.shape[0]
    grad_table = sum(
        bucket_grads(jnp.zeros((1,), jnp.int32), entry, bucket_count) for entry in grads_table
    )[:, :heads_dev]
    grad_table = lax.dynamic_update_slice_in_dim(
        jnp.zeros((bucket_count, heads_all), f32), grad_table, head_group * heads_dev, 1
    )
    grad_table = jnp.transpose(
        grad_table.reshape(blocks, bucket_count // blocks, heads_n, heads_all // heads_n),
        (2, 0, 1, 3),
    ).reshape(devices, -1)
    grad_gain_ff = jnp.transpose(
        jnp.stack(grads_gain_ff).reshape(layer_count, devices, weight_rows), (1, 0, 2)
    ).reshape(devices, -1)
    ends = jnp.sum(swap(jnp.concatenate([grad_gain_ff, grad_table], axis=1)), axis=0)
    grad_gain_ff = ends[: layer_count * weight_rows].reshape(layer_count, weight_rows)
    grad_bias_table = ends[layer_count * weight_rows :].reshape(
        bucket_count // blocks, heads_all // heads_n
    )
    grads_attn_in, grads_gains = [], []
    for layer_id in range(layer_count):
        parts = swap(grads_in[layer_id].reshape(devices, weight_rows, 3 * width)).astype(f32)
        parts = jnp.sum(parts.reshape(heads_n, blocks, weight_rows, 3 * width), axis=0)
        parts = jnp.sum(parts.reshape(head_groups, split, weight_rows, 3, width), axis=1)
        unit_grad = jnp.transpose(parts, (1, 2, 0, 3)).reshape(weight_rows, 3 * model_width)
        grads_attn_in.append(unit_grad * gain_attn[layer_id])
        grads_gains.append(
            jnp.stack(
                [jnp.sum(unit_grad * own_in[layer_id], axis=1), grad_gain_ff[layer_id]], axis=1
            )
        )
    return (
        output[None],
        upstream[None],
        jnp.stack(grads_attn_in),
        jnp.stack(grads_out),
        jnp.stack([entry[:, :model_width] for entry in grads_ff]),
        jnp.stack([entry[:, model_width:] for entry in grads_ff]),
        jnp.stack(grads_gains),
        grad_bias_table,
    )


def local_plane(tokens, doc_start, bias_table, attn_in, attn_out, ff_in, ff_out, gains, cotangent):
    heads_n, z_n, core_n = (lax.axis_size(axis) for axis in everyone)
    devices = heads_n * z_n * core_n
    at_head, at_z, at_core = (lax.axis_index(axis) for axis in everyone)
    members = heads_n * core_n
    block_rows, model_width = tokens.shape[1:]
    layer_count, weight_rows = attn_in.shape[:2]
    length = block_rows * members
    heads_all = bias_table.shape[1]
    heads_dev = heads_all // members
    width = heads_dev * head_dim
    member = at_head * core_n + at_core
    everywhere = [(h, z, c) for h in range(heads_n) for z in range(z_n) for c in range(core_n)]

    def swapped(bits):
        return bits % 2 * 2 + bits // 2

    def device(h, z, c):
        return (h * z_n + z) * core_n + c

    turn = [(device(h, z, c), device(h ^ swapped(z), h, c)) for h, z, c in everywhere]
    plane_turn = [(device(h, z, c), device(h ^ swapped(z), z, c)) for h, z, c in everywhere]
    line_turn = [(device(h, z, c), device(h, h ^ swapped(z), c)) for h, z, c in everywhere]
    line_back = [(target, source) for source, target in line_turn]
    place = jnp.stack(
        [
            (at_head ^ bits) * core_n + (at_core ^ other)
            for other in range(core_n)
            for bits in range(heads_n)
        ]
        + [at_z]
        + [
            swapped(at_head ^ bits ^ at_z) * core_n + (at_core ^ other)
            for other in range(core_n)
            for bits in range(heads_n)
        ]
    ).astype(jnp.int32)

    def relay(array):
        return lax.ppermute(array, everyone, turn)

    def turn_in_plane(array):
        return lax.ppermute(array, everyone, plane_turn)

    def turn_in_line(array, turns):
        return lax.ppermute(array, everyone, turns)

    def swap(array):
        return lax.all_to_all(array, everyone, 0, 0, tiled=True)

    row_shape = (block_rows, model_width)
    gain_attn = gains[:, :, 0].astype(f32)[:, :, None]
    near_share, far_share = call(
        share_in_kernel,
        [((members // 2 * layer_count * weight_rows, 3 * width), bf16)] * 2,
        place,
        attn_in,
        gain_attn,
        smem=1,
    )

    half_turns = [
        [
            (z * core_n + c, (2 * c + (a ^ z % 2)) * core_n + z // 2)
            for z in range(z_n)
            for c in range(core_n)
        ]
        for a in range(2)
    ]

    def fetch_out(layer_id, hold):
        own = attn_out[layer_id]
        other = toggle(own, "core", 1)
        head = jnp.where(
            at_core == 0, jnp.concatenate([own, other]), jnp.concatenate([other, own])
        )
        head = after(head, hold)
        return [
            lax.ppermute(head, ("z", "core"), [(holder, user) for user, holder in turns])
            for turns in half_turns
        ]

    def owners_halves(halves):
        return [
            lax.ppermute(half, ("z", "core"), turns) for half, turns in zip(halves, half_turns)
        ]

    def pair_chips(near, arrived, axis):
        rows, columns = near.shape[0] // 4, near.shape[1]
        shape = (2 * rows, columns) if axis == 0 else (rows, 2 * columns)
        return call(functools.partial(pair_kernel, axis), [(shape, bf16)] * 4, near, arrived)

    def share_chips(blocks):
        return [blocks[0]] + [toggle(blocks[bits], "head", bits) for bits in (1, 2, 3)]

    units_shape = [(row_shape, f32), (row_shape, bf16)]

    starts = jnp.broadcast_to(
        doc_start.astype(f32)[None, :, None], (heads_n, z_n, core_n, block_rows)
    )
    ff_gains = gains[:, :, 1].astype(f32).reshape(1, -1)
    small = jnp.concatenate(
        [
            starts.reshape(devices, block_rows),
            jnp.broadcast_to(ff_gains, (devices, layer_count * weight_rows)),
        ],
        axis=1,
    )
    table, strip = prepare(bias_table, member * heads_dev, heads_dev)
    hidden, strip = tie(relay(tokens[0]), strip)
    hidden, shares, cotangent_low, halves, small = tie(
        hidden,
        share_chips(pair_chips(near_share, toggle(far_share, "core", 1), 0)),
        turn_in_plane(after(cotangent[0].astype(bf16), near_share)),
        fetch_out(0, near_share),
        swap(after(small, near_share)),
    )
    hidden, unit_rows = call(unit_kernel, units_shape, hidden)
    doc_row = small[:members, :block_rows].reshape(2, 2, core_n, block_rows)
    at_block = swapped(at_head ^ at_z)
    for axis, bit in ((0, at_block // 2), (1, at_block % 2), (2, at_core)):
        doc_row = jnp.where(bit == 1, jnp.flip(doc_row, axis), doc_row)
    doc_row = jnp.transpose(doc_row, (2, 1, 0, 3)).reshape(1, length)
    doc_col = doc_row.reshape(length, 1)
    gain_ff = jnp.transpose(
        small[:, block_rows:].reshape(devices, layer_count, weight_rows), (1, 0, 2)
    ).reshape(layer_count, 1, model_width)

    def round_planes(array, by, hold):
        return shift(after(array, hold), by)

    ff_pairs = [
        jnp.concatenate([ff_in[layer_id], ff_out[layer_id]], axis=1) for layer_id in range(layer_count)
    ]

    def ff_both(kernel, row_operands, pair, columns):
        return zip(
            *(
                by_rows(
                    kernel,
                    256,
                    operands,
                    [pair],
                    [(pair.shape[0], bf16)] * columns + [(model_width, kind)],
                )
                for operands, kind in zip(zip(*row_operands), (f32, bf16))
            )
        )

    def ff_forward(normed, *parts):
        units = 4 * parts[0].shape[0]
        outs = [(units, bf16), (units, bf16)]
        *near, pair = by_rows(
            ff_first_kernel,
            256,
            [normed[0]],
            parts,
            outs + [(model_width, f32)],
            [(units, 2 * model_width)],
        )
        far = by_rows(ff_kernel, 256, [normed[1]], [pair], outs + [(model_width, bf16)])
        return pair, *zip(near, far)

    def ff_backward(low, slopes, pair):
        return ff_both(ff_back_kernel, [low, slopes], pair, 1)

    def assemble_in(share, lower, upper, opposite):
        return call(
            assemble_in_kernel,
            [((model_width, 3 * width), bf16)],
            place,
            share,
            lower,
            upper,
            opposite,
            smem=1,
        )[0]

    share, later_share = call(
        join_kernel, [((members * weight_rows, 3 * width), bf16)] * layer_count, *shares
    )
    near, far, lower, upper, opposite, doc_row, doc_col, gain_ff, *ff_pairs = plane_gather(
        unit_rows,
        shift(share, 1),
        shift(share, -1),
        shift(share, 2),
        doc_row,
        doc_col,
        gain_ff,
        *ff_pairs,
    )
    w_in = assemble_in(share, lower, upper, opposite)
    units = (near, far)
    w_out, qkv, attended, stats, *parts = plane_attention(
        *units, w_in, halves, doc_row, doc_col, place, table, strip
    )
    parts, lower, upper = tie(
        parts, round_planes(ff_pairs[0], 1, near), round_planes(ff_pairs[0], -1, near)
    )
    parts, own = plane_scatter(*parts)
    parts, opposite_in = tie(parts, round_planes(ff_in[0], 2, own))
    middle, normed_rows = call(close_gain_kernel, units_shape, hidden, *parts, gain_ff[0])
    *normed, opposite_out = plane_gather(normed_rows, round_planes(ff_out[0], 2, normed_rows))
    pair, acts, slopes, parts = ff_forward(
        normed, ff_pairs[0], lower, upper, opposite_in, opposite_out
    )
    records = [
        (hidden, units, w_in, w_out, pair, qkv, attended, stats, middle, normed, acts, slopes)
    ]
    parts, lower, upper = tie(
        parts,
        round_planes(later_share, 1, normed[0]),
        round_planes(later_share, -1, normed[0]),
    )
    parts, own = plane_scatter(*parts)
    parts, opposite, upstream = tie(
        parts, round_planes(later_share, 2, own), turn_in_line(after(cotangent_low, own), line_turn)
    )
    shares = [later_share, lower, upper, opposite]
    hidden, unit_rows = call(close_kernel, units_shape, middle, *parts)

    near, far, lower, halves = plane_gather(
        unit_rows, round_planes(ff_pairs[1], 1, unit_rows), fetch_out(1, unit_rows)
    )
    units = (near, far)
    w_in = assemble_in(*shares)
    w_out, qkv, attended, stats, *parts = plane_attention(
        *units, w_in, halves, doc_row, doc_col, place, table, strip
    )
    low = plane_gather(after(upstream, far))
    parts, near_low, upper = tie(parts, low[0], round_planes(ff_pairs[1], -1, far))
    low = (near_low, low[1])
    parts, own = plane_scatter(*parts)
    parts, opposite_in = tie(parts, round_planes(ff_in[1], 2, own))
    middle, normed_rows = call(close_gain_kernel, units_shape, hidden, *parts, gain_ff[1])
    *normed, opposite_out = plane_gather(normed_rows, round_planes(ff_out[1], 2, normed_rows))
    pair, acts, slopes, last_parts = ff_forward(
        normed, ff_pairs[1], lower, upper, opposite_in, opposite_out
    )
    records.append(
        (hidden, units, w_in, w_out, pair, qkv, attended, stats, middle, normed, acts, slopes)
    )

    def back_to_middle(parts, upstream, middle, gain):
        return call(
            middle_back_kernel, units_shape + [((1, model_width), f32)], upstream, *parts, middle, gain
        )

    def attention_grads(record, branch):
        _, _, w_in, w_out, _, qkv, attended, stats, *_ = record
        grad_qkv, grad_near, grad_far, near_part, far_part, *halves = plane_attention_back(
            qkv, doc_row, doc_col, attended, stats, *branch, w_in, w_out, place, table, strip
        )
        return grad_qkv, (grad_near, grad_far), (near_part, far_part), halves

    def table_grads(near_and_far):
        return bucket_grads(at_core.reshape(1) * heads_dev + 8, near_and_far, table.shape[0])

    record = records[1]
    hidden, units, _, _, pair, *_, middle, normed, acts, slopes = record
    pres, parts = ff_backward(low, slopes, pair)
    parts, own = plane_scatter(*parts)
    planes = ff_grads(after(pres, own), acts, normed, low)
    parts, ff_lower = tie(parts, shift(planes[1], -1))
    last_parts, _ = plane_scatter(*after(last_parts, parts))
    grad_middle, branch_rows, gain_1 = back_to_middle(parts, upstream, middle, gain_ff[1])
    *branch, ff_upper = plane_gather(branch_rows, round_planes(planes[2], 1, branch_rows))
    grad_qkv, strips_1, parts, halves_1 = attention_grads(record, branch)
    parts, last_parts, opposite_up = tie(
        parts, last_parts, round_planes(planes[3], 2, branch[1])
    )
    parts, own = plane_scatter(*parts)
    parts, opposite_down, output = tie(
        parts,
        round_planes(planes[4], 2, own),
        call(last_kernel, [(row_shape, bf16)], middle, *after(last_parts, own))[0],
    )
    grads_ff = [planes[0], ff_lower, ff_upper, opposite_up, opposite_down]
    upstream, low_rows = call(layer_back_kernel, units_shape, grad_middle, *parts, hidden)

    record = records[0]
    hidden, units, _, _, pair, *_, middle, normed, acts, slopes = record
    grad_in = in_grads(place, *records[1][1], after(grad_qkv, low_rows))
    near, far, grad_in, table_1, halves_1 = plane_gather(
        low_rows,
        grad_in,
        table_grads(after(strips_1, low_rows)),
        owners_halves(after(halves_1, low_rows)),
    )
    low = (near, far)
    grads_in_1 = swap(after(grad_in, far).reshape(devices, weight_rows, 3 * width))
    pres, parts = ff_backward(low, slopes, pair)
    parts, own = plane_scatter(*parts)
    planes = ff_grads(after(pres, own), acts, normed, low)
    parts, ff_lower = tie(parts, shift(planes[1], -1))
    grad_middle, branch_rows, gain_0 = back_to_middle(parts, upstream, middle, gain_ff[0])
    *branch, ff_upper = plane_gather(branch_rows, round_planes(planes[2], 1, branch_rows))
    grad_qkv, strips_0, parts, halves_0 = attention_grads(record, branch)
    parts, output, opposite_up = tie(
        parts, turn_in_line(after(output, branch[1]), line_back), round_planes(planes[3], 2, branch[1])
    )
    parts, own = plane_scatter(*parts)
    table_0 = table_grads(after(strips_0, own))
    grad_in = in_grads(
        place, *units, after(grad_qkv, own), gain_0, gain_1, table_0, table_1
    )
    parts, opposite_down, grad_in = tie(parts, round_planes(planes[4], 2, own), grad_in)
    upstream, low_rows = call(layer_back_kernel, units_shape, grad_middle, *parts, hidden)
    grads_in_0 = swap(grad_in.reshape(devices, weight_rows, 3 * width + tile))
    line = turn_in_line(low_rows, line_back)
    halves_0 = owners_halves(after(halves_0, low_rows))
    grad_tokens = turn_in_plane(line)
    output = turn_in_plane(after(output, low_rows)).astype(f32)
    grads_ff = [planes[0], ff_lower, ff_upper, opposite_up, opposite_down] + grads_ff
    grad_up, grad_down = finish_ff(after(grads_ff, low_rows), ff_in.shape)
    own_out, other_out = call(
        add_out_kernel,
        [(attn_out.shape, f32), (attn_out.shape, bf16)],
        place,
        *halves_0,
        *halves_1,
        smem=1,
    )
    (grad_attn_out,) = call(
        finish_out_kernel, [(attn_out.shape, f32)], own_out, toggle(other_out, "core", 1)
    )
    own_buckets = table.shape[0] // (z_n * core_n)
    grad_attn_in, grad_gains, ends = call(
        finish_in_kernel,
        [(attn_in.shape, f32), (gains.shape, f32), ((weight_rows, tile), f32)],
        grads_in_0,
        grads_in_1,
        attn_in,
        gain_attn,
    )
    return (
        output[None],
        grad_tokens.astype(f32)[None],
        grad_attn_in,
        grad_attn_out,
        grad_up,
        grad_down,
        grad_gains,
        ends[:own_buckets, 8 : 8 + heads_all // heads_n],
    )


def solution(mesh):
    sizes = dict(mesh.shape)
    cores = 2
    fine = Mesh(
        mesh.devices.reshape(sizes["head"], sizes["blk"] // cores, cores), everyone
    )
    blk = ("z", "core")
    in_specs = (
        P("head", blk, None),
        P(None, blk),
        P(),
        P(None, everyone, None),
        P(None, everyone, None),
        P(None, everyone, None),
        P(None, everyone, None),
        P(None, everyone, None),
        P("head", blk, None),
    )
    out_specs = (
        P("head", blk, None),
        P("head", blk, None),
        P(None, everyone, None),
        P(None, everyone, None),
        P(None, everyone, None),
        P(None, everyone, None),
        P(None, everyone, None),
        P(blk, "head"),
    )
    plane = sizes["head"] == 4 and sizes["blk"] == 8
    local = local_plane if plane else local_general
    return jax.shard_map(local, mesh=fine, in_specs=in_specs, out_specs=out_specs, check_vma=False)
```

```python
import functools

import jax
import jax.numpy as jnp
import numpy as np
from jax import lax
from jax.experimental import pallas as pl
from jax.experimental.pallas import tpu as pltpu
from jax.sharding import Mesh
from jax.sharding import PartitionSpec as P

bounds = (1, 2, 3, 4, 5, 6, 7, 8, 12, 16, 23, 32, 46, 64, 91)
epsilon = 1e-06
masked = -1e30
score_scale = 0.125
head_dim = 64
tile = 128
everyone = ("head", "z", "core")
bf16 = jnp.bfloat16
f32 = jnp.float32


def contract(lhs, rhs, lhs_dim, rhs_dim):
    return lax.dot_general(
        lhs, rhs, (((lhs_dim,), (rhs_dim,)), ((), ())), preferred_element_type=f32
    )


def near_buckets(shape):
    offsets = (
        lax.broadcasted_iota(jnp.int32, shape, 1) - tile - lax.broadcasted_iota(jnp.int32, shape, 0)
    )
    distance = jnp.abs(offsets)
    bucket = jnp.where(offsets > 0, 16, 0)
    for boundary in bounds:
        bucket = bucket + jnp.where(distance >= boundary, 1, 0)
    return bucket


def near_kernel(table, near):
    bucket = near_buckets(near.shape[1:])
    for head in range(near.shape[0]):
        values = jnp.zeros(near.shape[1:], f32)
        for bucket_id in range(table.shape[0]):
            values = jnp.where(bucket == bucket_id, table[bucket_id, head], values)
        near[head] = values


def bucket_kernel(first_lane, near, far, out):
    bucket = near_buckets(near.shape[1:])
    rows = lax.broadcasted_iota(jnp.int32, out.shape, 0)
    lanes = lax.broadcasted_iota(jnp.int32, out.shape, 1)
    total = jnp.zeros(out.shape, f32)
    for head in range(near.shape[0]):
        strip = near[head]
        for bucket_id in range(out.shape[0]):
            value = jnp.sum(jnp.where(bucket == bucket_id, strip, 0.0), axis=0, keepdims=True)
            value = jnp.sum(value, axis=1, keepdims=True)
            if bucket_id in (15, 31):
                value = value + far[head, bucket_id // 16, :1, :1]
            total = jnp.where((rows == bucket_id) & (lanes == head + first_lane[0]), value, total)
    out[...] = total


def fill_band(band, table, near, heads_dev, length):
    for head in range(heads_dev):
        band[head, :, : length - tile] = jnp.full((tile, length - tile), table[15, head], f32)
        band[head, :, length - tile : length + 2 * tile] = near[head]
        band[head, :, length + 2 * tile :] = jnp.full(
            (tile, length - 2 * tile), table[31, head], f32
        )


def band_starts(place, at, length, skip=0):
    return [
        pl.multiple_of(length + (place[skip + block] - place[skip + at]) * tile, tile)
        for block in range(length // tile)
    ]


def attention_kernel(
    heads_dev, length, first, place, table, near, qkv, doc_row, doc_col, out, local, stats, band
):
    step = pl.program_id(0)
    width = heads_dev * head_dim

    @pl.when(step == 0)
    def _():
        fill_band(band, table, near, heads_dev, length)

    row = pl.multiple_of((first[0] + step) * tile, tile)
    out_row = pl.multiple_of((place[first[0] + step] - first[0]) * tile, tile)
    starts = band_starts(place, first[0] + step, length)
    same_doc = doc_col[...] == doc_row[...]
    queries = qkv[pl.ds(row, tile), :width] * bf16(score_scale)
    lanes = lax.broadcasted_iota(jnp.int32, (tile, tile), 1)
    collected = jnp.zeros((tile, tile), f32)
    for head in range(heads_dev):
        own = slice(head * head_dim, (head + 1) * head_dim)
        keys = qkv[:, width + own.start : width + own.stop]
        values = qkv[:, 2 * width + own.start : 2 * width + own.stop]
        scores = contract(queries[:, own], keys, 1, 1)
        scores = scores + jnp.concatenate(
            [band[head, :, pl.ds(start, tile)] for start in starts], axis=1
        )
        scores = jnp.where(same_doc, scores, masked)
        peak = jnp.max(scores, axis=1, keepdims=True)
        weights = jnp.exp(scores - peak)
        total = jnp.sum(weights, axis=1, keepdims=True)
        mixed = contract(weights.astype(bf16), values, 1, 0) / total
        out[pl.ds(out_row, tile), own] = mixed.astype(bf16)
        local[:, own] = mixed.astype(bf16)
        collected = jnp.where(lanes == head, peak + jnp.log(total), collected)
    stats[...] = collected


def attention_back_kernel(
    heads_dev, length, split, first, place, table, near, qkv, doc_row, doc_col, attended, grad_out, stats,
    grad_qkv, grad_near, grad_far, band, grad_band, grad_keys, grad_values,
):
    step = pl.program_id(0)
    width = heads_dev * head_dim

    @pl.when(step == 0)
    def _():
        fill_band(band, table, near, heads_dev, length)
        grad_band[...] = jnp.zeros_like(grad_band)
        grad_keys[...] = jnp.zeros_like(grad_keys)
        grad_values[...] = jnp.zeros_like(grad_values)
        if split > 1:
            grad_qkv[...] = jnp.zeros_like(grad_qkv)

    row = pl.multiple_of((first[0] + step) * tile, tile)
    out_row = pl.multiple_of((place[first[0] + step] - first[0]) * tile, tile)
    starts = band_starts(place, first[0] + step, length)
    same_doc = doc_col[...] == doc_row[...]
    at_step = pl.multiple_of(step * tile, tile)
    queries = qkv[pl.ds(row, tile), :width] * bf16(score_scale)
    for head in range(heads_dev):
        own = slice(head * head_dim, (head + 1) * head_dim)
        keys = qkv[:, width + own.start : width + own.stop]
        values = qkv[:, 2 * width + own.start : 2 * width + own.stop]
        upstream = grad_out[pl.ds(out_row, tile), own]
        scores = contract(queries[:, own], keys, 1, 1) + jnp.concatenate(
            [band[head, :, pl.ds(start, tile)] for start in starts], axis=1
        )
        scores = jnp.where(same_doc, scores, masked)
        weights = jnp.exp(scores - stats[:, head : head + 1])
        delta = jnp.sum(
            upstream.astype(f32) * attended[pl.ds(at_step, tile), own].astype(f32),
            axis=1,
            keepdims=True,
        )
        grad_scores = weights * (contract(upstream, values, 1, 1) - delta)
        for block, start in enumerate(starts):
            grad_band[head, :, pl.ds(start, tile)] += grad_scores[
                :, block * tile : (block + 1) * tile
            ]
        grad_low = grad_scores.astype(bf16)
        grad_values[:, own] += contract(weights.astype(bf16), upstream, 0, 0)
        grad_keys[:, own] += contract(grad_low, queries[:, own], 0, 0)
        grad_qkv[pl.ds(row, tile), own] = (
            contract(grad_low, keys, 1, 0) * score_scale
        ).astype(bf16)

    @pl.when(step == pl.num_programs(0) - 1)
    def _():
        grad_qkv[:, width : 2 * width] = grad_keys[...].astype(bf16)
        grad_qkv[:, 2 * width :] = grad_values[...].astype(bf16)
        for head in range(heads_dev):
            grad_near[head] = grad_band[head, :, length - tile : length + 2 * tile]
            grad_far[head, 0] = jnp.full(
                (8, tile), jnp.sum(grad_band[head, :, : length - tile]), f32
            )
            grad_far[head, 1] = jnp.full(
                (8, tile), jnp.sum(grad_band[head, :, length + 2 * tile :]), f32
            )


def whole(shape):
    return pl.BlockSpec(shape, lambda step: (0,) * len(shape), pipeline_mode=pl.Buffered(1))


def attention(qkv, doc_row, doc_col, first, place, table, near, rows):
    length = qkv.shape[0]
    heads_dev = table.shape[1]
    width = heads_dev * head_dim
    return pl.pallas_call(
        functools.partial(attention_kernel, heads_dev, length),
        grid=(rows // tile,),
        in_specs=[
            pl.BlockSpec(memory_space=pltpu.SMEM),
            pl.BlockSpec(memory_space=pltpu.SMEM),
            pl.BlockSpec(memory_space=pltpu.SMEM),
            whole(near.shape),
            whole(qkv.shape),
            whole(doc_row.shape),
            pl.BlockSpec((tile, 1), lambda step: (step, 0)),
        ],
        out_specs=[
            whole((rows, width)),
            pl.BlockSpec((tile, width), lambda step: (step, 0)),
            pl.BlockSpec((tile, tile), lambda step: (step, 0)),
        ],
        out_shape=[
            jax.ShapeDtypeStruct((rows, width), bf16),
            jax.ShapeDtypeStruct((rows, width), bf16),
            jax.ShapeDtypeStruct((rows, tile), f32),
        ],
        scratch_shapes=[pltpu.VMEM((heads_dev, tile, 2 * length), f32)],
        compiler_params=pltpu.CompilerParams(vmem_limit_bytes=40 * 2**20),
        cost_estimate=pl.CostEstimate(
            flops=4 * rows * length * width,
            bytes_accessed=4 * length * width * 2,
            transcendentals=rows * length * heads_dev,
        ),
    )(first, place, table, near, qkv, doc_row, doc_col)


def attention_back(
    qkv, doc_row, doc_col, attended, grad_out, stats, first, place, table, near, split
):
    length = qkv.shape[0]
    rows = grad_out.shape[0]
    heads_dev = table.shape[1]
    width = heads_dev * head_dim
    return pl.pallas_call(
        functools.partial(attention_back_kernel, heads_dev, length, split),
        grid=(rows // tile,),
        in_specs=[
            pl.BlockSpec(memory_space=pltpu.SMEM),
            pl.BlockSpec(memory_space=pltpu.SMEM),
            pl.BlockSpec(memory_space=pltpu.SMEM),
            whole(near.shape),
            whole(qkv.shape),
            whole(doc_row.shape),
            pl.BlockSpec((tile, 1), lambda step: (step, 0)),
            whole((rows, width)),
            whole((rows, width)),
            pl.BlockSpec((tile, tile), lambda step: (step, 0)),
        ],
        out_specs=[
            whole((length, 3 * width)),
            whole((heads_dev, tile, 3 * tile)),
            whole((heads_dev, 2, 8, tile)),
        ],
        out_shape=[
            jax.ShapeDtypeStruct((length, 3 * width), bf16),
            jax.ShapeDtypeStruct((heads_dev, tile, 3 * tile), f32),
            jax.ShapeDtypeStruct((heads_dev, 2, 8, tile), f32),
        ],
        scratch_shapes=[
            pltpu.VMEM((heads_dev, tile, 2 * length), f32),
            pltpu.VMEM((heads_dev, tile, 2 * length), f32),
            pltpu.VMEM((length, width), f32),
            pltpu.VMEM((length, width), f32),
        ],
        compiler_params=pltpu.CompilerParams(vmem_limit_bytes=48 * 2**20),
        cost_estimate=pl.CostEstimate(
            flops=10 * rows * length * width,
            bytes_accessed=8 * length * width * 2,
            transcendentals=rows * length * heads_dev,
        ),
    )(first, place, table, near, qkv, doc_row, doc_col, attended, grad_out, stats)


def call(kernel, shapes, *operands, smem=0):
    return pl.pallas_call(
        kernel,
        in_specs=[pl.BlockSpec(memory_space=pltpu.SMEM)] * smem
        + [pl.BlockSpec(memory_space=pltpu.VMEM)] * (len(operands) - smem),
        out_specs=[pl.BlockSpec(memory_space=pltpu.VMEM)] * len(shapes),
        out_shape=[jax.ShapeDtypeStruct(shape, kind) for shape, kind in shapes],
        compiler_params=pltpu.CompilerParams(vmem_limit_bytes=10 * 2**20),
    )(*operands)


def share_in_kernel(place, attn_in, gains, near, far):
    layers, rows = attn_in.shape[:2]
    half = near.shape[0] // (layers * rows)
    width = near.shape[1] // 3
    for index in range(2 * half):
        member = place[index]
        for layer_id in range(layers):
            block = jnp.concatenate(
                [
                    attn_in[
                        layer_id,
                        :,
                        pl.ds(pl.multiple_of((part * 2 * half + member) * width, width), width),
                    ]
                    for part in range(3)
                ],
                axis=1,
            )
            at = (index % half * layers + layer_id) * rows
            out = near if index < half else far
            out[at : at + rows] = (block.astype(f32) * gains[layer_id]).astype(bf16)


def join_kernel(*refs):
    shares, outs = refs[:4], refs[4:]
    rows = outs[0].shape[0] // 8
    for chip, share in enumerate(shares):
        for core in range(2):
            for layer_id, out in enumerate(outs):
                source = (core * len(outs) + layer_id) * rows
                target = (chip * 2 + core) * rows
                out[target : target + rows] = share[source : source + rows]


def row_of(chip, plane, core, rows, planes=4):
    return pl.multiple_of(((chip * planes + plane) * 2 + core) * rows, rows)


def assemble_in_kernel(place, own, lower, upper, opposite, out):
    at_z, at_core, at_head = place[8], place[0] % 2, place[0] // 2
    rows = own.shape[0] // 8
    for part, offset in ((own, 0), (lower, 3), (upper, 1), (opposite, 2)):
        plane = (at_z + offset) % 4
        for index in range(8):
            row = row_of(at_head ^ (index // 2), plane, at_core ^ (index % 2), rows)
            out[pl.ds(row, rows)] = part[index * rows : (index + 1) * rows]


def plane_attention_kernel(
    length, place, table, strip, near, far, w_in, *refs
):
    halves, (doc_row, doc_col, w_out, qkv, attended, stats, near_part, far_part, band) = (
        refs[:2], refs[2:],
    )
    step = pl.program_id(0)
    half = length // 2
    heads_dev = table.shape[1]
    width = heads_dev * head_dim

    @pl.when(step == 0)
    def _():
        fill_band(band, table, strip, heads_dev, length)
        swapped = place[length // tile] % 2 == 1
        rows = width // 2
        w_out[:rows] = jnp.where(swapped, halves[1][...], halves[0][...])
        w_out[rows:] = jnp.where(swapped, halves[0][...], halves[1][...])
        qkv[:half] = contract(near[...], w_in[...], 1, 0).astype(bf16)
        qkv[half:] = contract(far[...], w_in[...], 1, 0).astype(bf16)

    row = pl.multiple_of(step * tile, tile)
    starts = band_starts(place, step, length, length // tile + 1)
    same_doc = doc_col[...] == doc_row[...]
    queries = qkv[pl.ds(row, tile), :width] * bf16(score_scale)
    lanes = lax.broadcasted_iota(jnp.int32, (tile, tile), 1)
    collected = jnp.zeros((tile, tile), f32)
    results = []
    for head in range(heads_dev):
        own = slice(head * head_dim, (head + 1) * head_dim)
        keys = qkv[:, width + own.start : width + own.stop]
        values = qkv[:, 2 * width + own.start : 2 * width + own.stop]
        scores = contract(queries[:, own], keys, 1, 1) + jnp.concatenate(
            [band[head, :, pl.ds(start, tile)] for start in starts], axis=1
        )
        scores = jnp.where(same_doc, scores, masked)
        peak = jnp.max(scores, axis=1, keepdims=True)
        weights = jnp.exp(scores - peak)
        total = jnp.sum(weights, axis=1, keepdims=True)
        results.append((contract(weights.astype(bf16), values, 1, 0) / total).astype(bf16))
        collected = jnp.where(lanes == head, peak + jnp.log(total), collected)
    stats[...] = collected
    merged = jnp.concatenate(results, axis=1)
    attended[...] = merged
    part = contract(merged, w_out[...], 1, 0)

    @pl.when(row < half)
    def _():
        near_part[...] = part

    @pl.when(row >= half)
    def _():
        far_part[...] = part.astype(bf16)


def near_block(steps, columns):
    return pl.BlockSpec((tile, columns), lambda step: (jnp.minimum(step, steps // 2 - 1), 0))


def far_block(steps, columns):
    return pl.BlockSpec((tile, columns), lambda step: (jnp.maximum(step - steps // 2, 0), 0))


def plane_attention(near, far, w_in, halves, doc_row, doc_col, place, table, strip):
    length, model_width = 2 * near.shape[0], near.shape[1]
    steps = length // tile
    heads_dev = table.shape[1]
    width = heads_dev * head_dim
    return pl.pallas_call(
        functools.partial(plane_attention_kernel, length),
        grid=(steps,),
        in_specs=[
            pl.BlockSpec(memory_space=pltpu.SMEM),
            pl.BlockSpec(memory_space=pltpu.SMEM),
            whole(strip.shape),
            whole(near.shape),
            whole(far.shape),
            whole(w_in.shape),
            *[whole(half.shape) for half in halves],
            whole(doc_row.shape),
            pl.BlockSpec((tile, 1), lambda step: (step, 0)),
        ],
        out_specs=[
            whole((width, model_width)),
            whole((length, 3 * width)),
            pl.BlockSpec((tile, width), lambda step: (step, 0)),
            pl.BlockSpec((tile, tile), lambda step: (step, 0)),
            near_block(steps, model_width),
            far_block(steps, model_width),
        ],
        out_shape=[
            jax.ShapeDtypeStruct((width, model_width), bf16),
            jax.ShapeDtypeStruct((length, 3 * width), bf16),
            jax.ShapeDtypeStruct((length, width), bf16),
            jax.ShapeDtypeStruct((length, tile), f32),
            jax.ShapeDtypeStruct((length // 2, model_width), f32),
            jax.ShapeDtypeStruct((length // 2, model_width), bf16),
        ],
        scratch_shapes=[pltpu.VMEM((heads_dev, tile, 2 * length), f32)],
        compiler_params=pltpu.CompilerParams(vmem_limit_bytes=14 * 2**20),
        cost_estimate=pl.CostEstimate(
            flops=4 * length * length * width + 8 * length * model_width * width,
            bytes_accessed=12 * 2**20,
            transcendentals=length * length * heads_dev,
        ),
    )(place, table, strip, near, far, w_in, *halves, doc_row, doc_col)


def plane_attention_back_kernel(
    length, place, table, strip, qkv, doc_row, doc_col, attended, stats, near, far, w_in, w_out,
    grad_qkv, grad_near, grad_far, near_part, far_part, *rest
):
    halves, (band, grad_band, grad_keys, grad_values, out_sum) = rest[:2], rest[2:]
    step = pl.program_id(0)
    half = length // 2
    heads_dev = table.shape[1]
    width = heads_dev * head_dim

    @pl.when(step == 0)
    def _():
        fill_band(band, table, strip, heads_dev, length)
        grad_band[...] = jnp.zeros_like(grad_band)
        grad_keys[...] = jnp.zeros_like(grad_keys)
        grad_values[...] = jnp.zeros_like(grad_values)
        out_sum[...] = jnp.zeros_like(out_sum)

    row = pl.multiple_of(step * half, half)
    branch = jnp.where(step == 0, near[...], far[...])
    merged = attended[...]
    grad_merged = contract(branch, w_out[...], 1, 1).astype(bf16)
    out_sum[...] += contract(merged, branch, 0, 0)
    products = grad_merged.astype(f32) * merged.astype(f32)
    queries = qkv[pl.ds(row, half), :width] * bf16(score_scale)
    blocks = half // tile
    for head in range(heads_dev):
        own = slice(head * head_dim, (head + 1) * head_dim)
        keys = qkv[:, width + own.start : width + own.stop]
        values = qkv[:, 2 * width + own.start : 2 * width + own.stop]
        upstream = grad_merged[:, own]
        raw_scores = contract(queries[:, own], keys, 1, 1)
        grad_weights = contract(upstream, values, 1, 1)
        delta = jnp.sum(products[:, own], axis=1, keepdims=True)
        weights_low, grads_low = [], []
        for block in range(blocks):
            lines = slice(block * tile, (block + 1) * tile)
            starts = band_starts(place, step * blocks + block, length, length // tile + 1)
            scores = raw_scores[lines] + jnp.concatenate(
                [band[head, :, pl.ds(start, tile)] for start in starts], axis=1
            )
            scores = jnp.where(doc_col[lines] == doc_row[...], scores, masked)
            weights = jnp.exp(scores - stats[lines, head : head + 1])
            grad_scores = weights * (grad_weights[lines] - delta[lines])
            for index, start in enumerate(starts):
                grad_band[head, :, pl.ds(start, tile)] += grad_scores[
                    :, index * tile : (index + 1) * tile
                ]
            weights_low.append(weights.astype(bf16))
            grads_low.append(grad_scores.astype(bf16))
        weights_low, grads_low = jnp.concatenate(weights_low), jnp.concatenate(grads_low)
        grad_values[:, own] += contract(weights_low, upstream, 0, 0)
        grad_keys[:, own] += contract(grads_low, queries[:, own], 0, 0)
        grad_qkv[pl.ds(row, half), own] = (
            contract(grads_low, keys, 1, 0) * score_scale
        ).astype(bf16)

    @pl.when(step == pl.num_programs(0) - 1)
    def _():
        grad_qkv[:, width : 2 * width] = grad_keys[...].astype(bf16)
        grad_qkv[:, 2 * width :] = grad_values[...].astype(bf16)
        far_part[...] = contract(grad_qkv[half:], w_in[...], 1, 1).astype(bf16)
        near_part[...] = contract(grad_qkv[:half], w_in[...], 1, 1)
        rows = width // 2
        for index, part in enumerate(halves):
            block = index ^ place[length // tile] % 2
            part[...] = out_sum[pl.ds(pl.multiple_of(block * rows, rows), rows)].astype(bf16)
        for head in range(heads_dev):
            grad_near[head] = grad_band[head, :, length - tile : length + 2 * tile]
            grad_far[head, 0] = jnp.full(
                (8, tile), jnp.sum(grad_band[head, :, : length - tile]), f32
            )
            grad_far[head, 1] = jnp.full(
                (8, tile), jnp.sum(grad_band[head, :, length + 2 * tile :]), f32
            )


def plane_attention_back(
    qkv, doc_row, doc_col, attended, stats, near, far, w_in, w_out, place, table, strip
):
    length, model_width = 2 * near.shape[0], near.shape[1]
    half = length // 2
    heads_dev = table.shape[1]
    width = heads_dev * head_dim
    shapes = [
        ((length, 3 * width), bf16),
        ((heads_dev, tile, 3 * tile), f32),
        ((heads_dev, 2, 8, tile), f32),
        ((length // 2, model_width), f32),
        ((length // 2, model_width), bf16),
    ] + [((width // 2, model_width), bf16)] * 2
    return pl.pallas_call(
        functools.partial(plane_attention_back_kernel, length),
        grid=(2,),
        in_specs=[
            pl.BlockSpec(memory_space=pltpu.SMEM),
            pl.BlockSpec(memory_space=pltpu.SMEM),
            whole(strip.shape),
            whole(qkv.shape),
            whole(doc_row.shape),
            pl.BlockSpec((half, 1), lambda step: (step, 0)),
            pl.BlockSpec((half, width), lambda step: (step, 0)),
            pl.BlockSpec((half, tile), lambda step: (step, 0)),
            whole((half, model_width)),
            whole((half, model_width)),
            whole(w_in.shape),
            whole(w_out.shape),
        ],
        out_specs=[whole(shape) for shape, _ in shapes],
        out_shape=[jax.ShapeDtypeStruct(shape, kind) for shape, kind in shapes],
        scratch_shapes=[
            pltpu.VMEM((heads_dev, tile, 2 * length), f32),
            pltpu.VMEM((heads_dev, tile, 2 * length), f32),
            pltpu.VMEM((length, width), f32),
            pltpu.VMEM((length, width), f32),
            pltpu.VMEM((width, model_width), f32),
        ],
        compiler_params=pltpu.CompilerParams(vmem_limit_bytes=32 * 2**20),
        cost_estimate=pl.CostEstimate(
            flops=10 * length * length * width + 10 * length * model_width * width,
            bytes_accessed=12 * 2**20,
            transcendentals=length * length * heads_dev,
        ),
    )(place, table, strip, qkv, doc_row, doc_col, attended, stats, near, far, w_in, w_out)


def gelu_and_slope(pre_act):
    size = jnp.abs(pre_act)
    gauss = jnp.exp(-0.5 * pre_act * pre_act)
    ratio = 1.0 / (1.0 + np.float32(0.3275911 * 0.5**0.5) * size)
    series = np.float32(1.061405429)
    for factor in (-1.453152027, 1.421413741, -0.284496736, 0.254829592):
        series = series * ratio + np.float32(factor)
    tail = 0.5 * series * ratio * gauss
    cumulative = jnp.where(pre_act < 0, tail, 1.0 - tail)
    slope = cumulative + pre_act * gauss * np.float32((2 * np.pi) ** -0.5)
    return pre_act * cumulative, slope


def ff_kernel(rows, pair, activated, slope, part):
    columns = rows.shape[1]
    value, gradient = gelu_and_slope(contract(rows[...], pair[:, :columns], 1, 1))
    activated[...] = value.astype(bf16)
    slope[...] = gradient.astype(bf16)
    part[...] = contract(activated[...], pair[:, columns:], 1, 0).astype(part.dtype)


def ff_first_kernel(rows, *refs):
    parts, (activated, slope, part, pair) = refs[:5], refs[5:]

    @pl.when(pl.program_id(0) == 0)
    def _():
        units, columns = parts[0].shape[0], rows.shape[1]
        for index, ref in enumerate(parts[:3]):
            pair[index * units : (index + 1) * units] = ref[...]
        pair[3 * units :, :columns] = parts[3][...]
        pair[3 * units :, columns:] = parts[4][...]

    ff_kernel(rows, pair, activated, slope, part)


def ff_back_kernel(rows, slope, pair, grad_pre, part):
    columns = rows.shape[1]
    grad_act = contract(rows[...], pair[:, columns:], 1, 1)
    grad_pre[...] = (grad_act * slope[...].astype(f32)).astype(bf16)
    part[...] = contract(grad_pre[...], pair[:, :columns], 1, 0).astype(part.dtype)


def by_rows(kernel, step_rows, row_operands, whole_operands, outs, whole_outs=()):
    rows = row_operands[0].shape[0]
    return pl.pallas_call(
        kernel,
        grid=(rows // step_rows,),
        in_specs=[
            pl.BlockSpec((step_rows, operand.shape[1]), lambda step: (step, 0))
            for operand in row_operands
        ]
        + [whole(operand.shape) for operand in whole_operands],
        out_specs=[pl.BlockSpec((step_rows, columns), lambda step: (step, 0)) for columns, _ in outs]
        + [whole(shape) for shape in whole_outs],
        out_shape=[jax.ShapeDtypeStruct((rows, columns), kind) for columns, kind in outs]
        + [jax.ShapeDtypeStruct(shape, bf16) for shape in whole_outs],
        compiler_params=pltpu.CompilerParams(vmem_limit_bytes=10 * 2**20),
        cost_estimate=pl.CostEstimate(
            flops=4 * rows * outs[0][0] * row_operands[0].shape[1],
            bytes_accessed=6 * 2**20,
            transcendentals=0,
        ),
    )(*row_operands, *whole_operands)


def ff_grads_kernel(
    pre_near, pre_far, act_near, act_far, normed_near, normed_far, low_near, low_far, *outs
):
    columns = normed_near.shape[1]
    units = outs[0].shape[0]
    up = (
        contract(pre_near[...], normed_near[...], 0, 0)
        + contract(pre_far[...], normed_far[...], 0, 0)
    ).astype(bf16)
    down = (
        contract(act_near[...], low_near[...], 0, 0) + contract(act_far[...], low_far[...], 0, 0)
    ).astype(bf16)

    @pl.when(pl.program_id(0) == 0)
    def _():
        for index in range(2):
            block = slice(index * units, (index + 1) * units)
            outs[index][:, :columns] = up[block]
            outs[index][:, columns:] = down[block]

    @pl.when(pl.program_id(0) == 1)
    def _():
        outs[2][:, :columns] = up[:units]
        outs[2][:, columns:] = down[:units]
        outs[3][...] = up[units:]
        outs[4][...] = down[units:]


def ff_grads(pre, act, normed, low):
    rows, hidden_units = pre[0].shape
    columns = normed[0].shape[1]
    shapes = [(hidden_units // 4, 2 * columns)] * 3 + [(hidden_units // 4, columns)] * 2
    return pl.pallas_call(
        ff_grads_kernel,
        grid=(2,),
        in_specs=[pl.BlockSpec((rows, hidden_units // 2), lambda step: (0, step))] * 4
        + [whole((rows, columns))] * 4,
        out_specs=[whole(shape) for shape in shapes],
        out_shape=[jax.ShapeDtypeStruct(shape, bf16) for shape in shapes],
        compiler_params=pltpu.CompilerParams(vmem_limit_bytes=14 * 2**20),
        cost_estimate=pl.CostEstimate(
            flops=8 * rows * hidden_units * columns, bytes_accessed=8 * 2**20, transcendentals=0
        ),
    )(*pre, *act, *normed, *low)


def in_grads_kernel(place, near, far, grad_qkv, *refs):
    ends, (total, extra) = refs[:-2], refs[-2:]
    half = near.shape[0]
    columns = grad_qkv.shape[1]
    total[:, :columns] = (
        contract(near[...], grad_qkv[:half], 0, 0) + contract(far[...], grad_qkv[half:], 0, 0)
    ).astype(bf16)
    if ends:
        gain_0, gain_1, table_0, table_1 = ends
        rows = near.shape[1] // 32
        lines = lax.broadcasted_iota(jnp.int32, (tile, gain_0.shape[1]), 0)
        gains = jnp.where(lines == 0, gain_0[...], jnp.where(lines == 1, gain_1[...], 0.0))
        extra[...] = jnp.transpose(gains)
        table = table_0[...] + table_1[...]
        buckets = table.shape[0] // 8
        blank = jnp.zeros((8 - buckets, tile), f32)
        for block in range(8):
            row = pl.multiple_of((place[0] // 2 * 8 + block) * rows, rows)
            extra[pl.ds(row, 8)] += jnp.concatenate(
                [table[block * buckets : (block + 1) * buckets], blank]
            )
        total[:, columns:] = extra[...].astype(bf16)


def in_grads(place, near, far, grad_qkv, *ends):
    columns = grad_qkv.shape[1] + (tile if ends else 0)
    return pl.pallas_call(
        in_grads_kernel,
        in_specs=[pl.BlockSpec(memory_space=pltpu.SMEM)]
        + [pl.BlockSpec(memory_space=pltpu.VMEM)] * (3 + len(ends)),
        out_specs=pl.BlockSpec(memory_space=pltpu.VMEM),
        out_shape=jax.ShapeDtypeStruct((near.shape[1], columns), bf16),
        scratch_shapes=[pltpu.VMEM((near.shape[1], tile), f32)],
        compiler_params=pltpu.CompilerParams(vmem_limit_bytes=14 * 2**20),
        cost_estimate=pl.CostEstimate(
            flops=4 * near.shape[0] * near.shape[1] * columns,
            bytes_accessed=4 * 2**20,
            transcendentals=0,
        ),
    )(place, near, far, grad_qkv, *ends)


def in_planes_kernel(place, near, far, grad_qkv, *refs):
    outs, total = refs[:4], refs[4]
    half = near.shape[0]
    total[...] = (
        contract(near[...], grad_qkv[:half], 0, 0) + contract(far[...], grad_qkv[half:], 0, 0)
    ).astype(bf16)
    rows = outs[0].shape[0] // 8
    for out, offset in zip(outs, (0, 3, 1, 2)):
        plane = (place[8] + offset) % 4
        for index in range(8):
            owner = place[index]
            row = row_of(owner // 2, plane, owner % 2, rows)
            out[index * rows : (index + 1) * rows] = total[pl.ds(row, rows)]


def in_planes(place, near, far, grad_qkv):
    columns = grad_qkv.shape[1]
    shape = (near.shape[1] // 4, columns)
    return pl.pallas_call(
        in_planes_kernel,
        in_specs=[pl.BlockSpec(memory_space=pltpu.SMEM)]
        + [pl.BlockSpec(memory_space=pltpu.VMEM)] * 3,
        out_specs=[pl.BlockSpec(memory_space=pltpu.VMEM)] * 4,
        out_shape=[jax.ShapeDtypeStruct(shape, bf16)] * 4,
        scratch_shapes=[pltpu.VMEM((near.shape[1], columns), bf16)],
        compiler_params=pltpu.CompilerParams(vmem_limit_bytes=14 * 2**20),
        cost_estimate=pl.CostEstimate(
            flops=4 * near.shape[0] * near.shape[1] * columns,
            bytes_accessed=4 * 2**20,
            transcendentals=0,
        ),
    )(place, near, far, grad_qkv)


def add_in_kernel(own, lower, upper, opposite, near, far):
    total = sum_of_four([own, lower, upper, opposite]).astype(bf16)
    half = near.shape[0]
    near[...] = total[:half]
    far[...] = total[half:]


def combine_kernel(near_part, arrived, own, x_part, y_part, xy_part):
    rows = own.shape[0]
    own[...] = near_part[:rows] + arrived[:rows].astype(f32)
    for bits, out in ((1, x_part), (2, y_part), (3, xy_part)):
        block = slice(bits * rows, (bits + 1) * rows)
        out[...] = (near_part[block] + arrived[block].astype(f32)).astype(bf16)


def added(own, x_part, y_part, xy_part):
    return (own[...] + x_part[...].astype(f32)) + (
        y_part[...].astype(f32) + xy_part[...].astype(f32)
    )


def close_kernel(kept, own, x_part, y_part, xy_part, hidden, units):
    total = kept[...] + added(own, x_part, y_part, xy_part)
    hidden[...] = total
    units[...] = (total * inverse_rms(total)).astype(bf16)


def close_gain_kernel(kept, own, x_part, y_part, xy_part, gain, hidden, normed):
    total = kept[...] + added(own, x_part, y_part, xy_part)
    hidden[...] = total
    normed[...] = (total * inverse_rms(total) * gain[...]).astype(bf16)


def last_kernel(kept, own, x_part, y_part, xy_part, hidden):
    hidden[...] = (kept[...] + added(own, x_part, y_part, xy_part)).astype(bf16)


def middle_back_kernel(
    upstream, own, x_part, y_part, xy_part, middle, gain, grad_middle, branch, grad_gain
):
    grad_normed = added(own, x_part, y_part, xy_part)
    inverse = inverse_rms(middle[...])
    grad_gain[...] = jnp.sum(grad_normed * middle[...] * inverse, axis=0, keepdims=True)
    total = upstream[...].astype(f32) + unit_norm_back(
        middle[...], inverse, grad_normed * gain[...]
    )
    grad_middle[...] = total
    branch[...] = total.astype(bf16)


def layer_back_kernel(grad_middle, own, x_part, y_part, xy_part, hidden, upstream, low):
    total = grad_middle[...] + unit_norm_back(
        hidden[...], inverse_rms(hidden[...]), added(own, x_part, y_part, xy_part)
    )
    upstream[...] = total
    low[...] = total.astype(bf16)


def pair_kernel(axis, near, arrived, *outs):
    rows = near.shape[0] // len(outs)
    for index, out in enumerate(outs):
        block = slice(index * rows, (index + 1) * rows)
        if axis == 0:
            out[:rows] = near[block]
            out[rows:] = arrived[block]
        else:
            columns = near.shape[1]
            out[:, :columns] = near[block]
            out[:, columns:] = arrived[block]


def unit_kernel(tokens, hidden, units):
    total = tokens[...].astype(f32)
    hidden[...] = total
    units[...] = (total * inverse_rms(total)).astype(bf16)


def finish_in_kernel(place, *refs):
    blocks, chips, (attn_in, gains, grad_in, grad_gain, ends) = refs[0], refs[1:5], refs[5:]
    rows = attn_in.shape[1]
    width = tile
    members = attn_in.shape[2] // (3 * width)
    ends[...] = jnp.zeros_like(ends)
    for layer_id in range(2):
        row_dot = jnp.zeros((rows, 1), f32)
        for index in range(members):
            if layer_id == 0:
                member = index
                total = sum_of_four(
                    [blocks.at[(member // 2 * 4 + plane) * 2 + member % 2] for plane in range(4)]
                )
                ends[...] += total[:, 3 * width :]
            else:
                member = place[index]
                first = index // 4 * 3 * width
                total = chips[index % 4][:, first : first + 3 * width].astype(f32)
            for part in range(3):
                block = total[:, part * width : (part + 1) * width]
                columns = pl.ds(pl.multiple_of((part * members + member) * width, width), width)
                grad_in[layer_id, :, columns] = block * gains[layer_id]
                row_dot = row_dot + jnp.sum(
                    block * attn_in[layer_id, :, columns].astype(f32), axis=1, keepdims=True
                )
        grad_gain[layer_id] = jnp.concatenate(
            [row_dot, ends[:, layer_id : layer_id + 1]], axis=1
        )


def sum_of_four(parts):
    return (parts[0][...].astype(f32) + parts[1][...].astype(f32)) + (
        parts[2][...].astype(f32) + parts[3][...].astype(f32)
    )


def finish_ff_kernel(*refs):
    count = (len(refs) - 3) // 2
    sources, grads, held, done = refs[:count], refs[count : count + 2], refs[count + 2 : -1], refs[-1]
    copies = [
        pltpu.make_async_copy(source, target, done.at[index])
        for index, (source, target) in enumerate(zip(sources, held))
    ]
    for copy in copies:
        copy.start()
    for copy in copies:
        copy.wait()
    refs = held
    columns = grads[0].shape[2]
    for layer_id in range(grads[0].shape[0]):
        parts = refs[5 * layer_id : 5 * layer_id + 5]
        for side, out in enumerate(grads):
            halves = [part.at[:, side * columns : (side + 1) * columns] for part in parts[:3]]
            out[layer_id] = sum_of_four(halves + [parts[3 + side]])


def finish_ff(grads, shape):
    return pl.pallas_call(
        finish_ff_kernel,
        in_specs=[pl.BlockSpec(memory_space=pl.ANY)] * len(grads),
        out_specs=[pl.BlockSpec(memory_space=pltpu.VMEM)] * 2,
        out_shape=[jax.ShapeDtypeStruct(shape, f32)] * 2,
        scratch_shapes=[pltpu.VMEM(grad.shape, bf16) for grad in grads]
        + [pltpu.SemaphoreType.DMA((len(grads),))],
        compiler_params=pltpu.CompilerParams(vmem_limit_bytes=14 * 2**20),
    )(*grads)


def add_out_kernel(place, *refs):
    parts, (own, other) = refs[:-2], refs[-2:]
    for layer_id in range(own.shape[0]):
        total = parts[2 * layer_id][...].astype(f32) + parts[2 * layer_id + 1][...].astype(f32)
        rows = total.shape[0] // 2
        second = place[0] % 2 == 1
        own[layer_id] = jnp.where(second, total[rows:], total[:rows])
        other[layer_id] = jnp.where(second, total[:rows], total[rows:]).astype(bf16)


def finish_out_kernel(own, arrived, out):
    out[...] = own[...] + arrived[...].astype(f32)


def inverse_rms(hidden):
    return lax.rsqrt(jnp.mean(hidden * hidden, axis=-1, keepdims=True) + epsilon)


def prepare(bias_table, first_head, heads_dev):
    table = lax.dynamic_slice_in_dim(bias_table, first_head, heads_dev, 1)
    (near,) = call(near_kernel, [((heads_dev, tile, 3 * tile), f32)], table, smem=1)
    return table, near


def bucket_grads(first_lane, grads, bucket_count):
    (total,) = call(bucket_kernel, [((bucket_count, tile), f32)], first_lane, *grads, smem=1)
    return total


def gelu_parts(pre_act):
    cumulative = 0.5 * (1.0 + lax.erf(pre_act * np.float32(0.5**0.5)))
    slope = cumulative + pre_act * jnp.exp(-0.5 * pre_act * pre_act) * np.float32(
        (2 * np.pi) ** -0.5
    )
    return (pre_act * cumulative).astype(bf16), slope


def unit_norm_back(hidden, inverse, grad_unit):
    unit = hidden * inverse
    return inverse * (grad_unit - unit * jnp.mean(grad_unit * unit, axis=-1, keepdims=True))


def gather_rows(block, axes):
    return lax.all_gather(block, axes, axis=0, tiled=True)


def toggle(array, axis, bits):
    return lax.ppermute(array, axis, [(i, i ^ bits) for i in range(lax.axis_size(axis))])


def shift(array, by):
    planes = lax.axis_size("z")
    return lax.ppermute(array, "z", [(i, (i + by) % planes) for i in range(planes)])


def plane_gather(block, *holds):
    near = jnp.concatenate([block] + [toggle(block, "head", bits) for bits in (1, 2, 3)])
    near, *holds = tie(near, *holds)
    return (near, toggle(near, "core", 1), *holds)


def plane_scatter(near_part, far_part):
    rows, columns = near_part.shape[0] // 4, near_part.shape[1]
    own, *others = call(
        combine_kernel,
        [((rows, columns), f32)] + [((rows, columns), bf16)] * 3,
        near_part,
        toggle(far_part, "core", 1),
    )
    shares = [own] + [toggle(other, "head", bits) for bits, other in zip((1, 2, 3), others)]
    return shares, own


def tie(*arrays):
    return lax.optimization_barrier(arrays)


def after(array, other):
    return lax.optimization_barrier((array, other))[0]


def scatter_sum(partial, axes, members):
    blocks = partial.astype(bf16).reshape(members, -1, partial.shape[1])
    return jnp.sum(lax.all_to_all(blocks, axes, 0, 0, tiled=True).astype(f32), axis=0)


def local_general(tokens, doc_start, bias_table, attn_in, attn_out, ff_in, ff_out, gains, cotangent):
    heads_n, z_n, core_n = (lax.axis_size(axis) for axis in everyone)
    devices = heads_n * z_n * core_n
    group, spare = ("z", "core"), "head"
    ff_group, ff_spare, ff_members = ("head", "core"), "z", heads_n * core_n
    blocks = z_n * core_n
    block_rows, model_width = tokens.shape[1:]
    layer_count, weight_rows = attn_in.shape[:2]
    length = block_rows * blocks
    heads_all = bias_table.shape[1]
    member = lax.axis_index("z") * core_n + lax.axis_index("core")
    heads_dev = max(1, heads_all // blocks)
    head_groups = heads_all // heads_dev
    split = blocks // head_groups
    head_group, query_part = member // split, member % split
    query_rows = length // split
    width = heads_dev * head_dim
    first = (query_part * (query_rows // tile)).astype(jnp.int32).reshape(1)
    place = jnp.arange(length // tile, dtype=jnp.int32)
    out_row = head_group * width

    def swap(array):
        return lax.all_to_all(array, everyone, 0, 0, tiled=True)

    starts = jnp.broadcast_to(
        doc_start.astype(f32)[:, None], (heads_n, blocks, block_rows)
    ).reshape(devices, block_rows)
    ff_gains = gains[:, :, 1].astype(f32).reshape(1, -1)
    small = swap(
        jnp.concatenate(
            [starts, jnp.broadcast_to(ff_gains, (devices, layer_count * weight_rows))], axis=1
        )
    )
    doc_row = small[:blocks, :block_rows].reshape(1, length)
    doc_col = lax.dynamic_slice_in_dim(
        doc_row.reshape(length, 1), query_part * query_rows, query_rows, 0
    )
    gain_ff = jnp.transpose(
        small[:, block_rows:].reshape(devices, layer_count, weight_rows), (1, 0, 2)
    ).reshape(layer_count, 1, model_width)
    table, near = prepare(bias_table, head_group * heads_dev, heads_dev)

    gain_attn = gains[:, :, 0].astype(f32)[:, :, None]
    own_in = attn_in.astype(f32)

    def fetch_in(layer_id):
        scaled = (own_in[layer_id] * gain_attn[layer_id]).astype(bf16)
        columns = jnp.transpose(
            scaled.reshape(weight_rows, 3, head_groups, width), (2, 0, 1, 3)
        ).reshape(head_groups, weight_rows, 3 * width)
        columns = jnp.repeat(columns, split, axis=0)
        columns = jnp.broadcast_to(columns[None], (heads_n, *columns.shape))
        return swap(columns.reshape(devices, weight_rows, 3 * width)).reshape(
            model_width, 3 * width
        )

    def fetch_ff(layer_id):
        pair = jnp.concatenate([ff_in[layer_id], ff_out[layer_id]], axis=1)
        pair = gather_rows(pair, ff_spare)
        return pair[:, :model_width], pair[:, model_width:]

    hidden, upstream = tokens[0].astype(f32), cotangent[0]
    weights_in = [fetch_in(layer_id) for layer_id in range(layer_count)]
    weights_out = lax.dynamic_slice_in_dim(
        lax.all_gather(attn_out, everyone, axis=1, tiled=True), out_row, width, 1
    )
    weights_ff = [fetch_ff(layer_id) for layer_id in range(layer_count)]

    records = []
    for layer_id in range(layer_count):
        w_in, w_out, (w_up, w_down) = (
            weights_in[layer_id], weights_out[layer_id], weights_ff[layer_id],
        )
        inverse = inverse_rms(hidden)
        units = gather_rows((hidden * inverse).astype(bf16), group)
        qkv = jnp.dot(units, w_in, preferred_element_type=f32).astype(bf16)
        attended, _, stats = attention(
            qkv, doc_row, doc_col, first, place, table, near, query_rows
        )
        mixed = jnp.dot(attended, w_out, preferred_element_type=f32)
        if split > 1:
            mixed = lax.dynamic_update_slice_in_dim(
                jnp.zeros((length, model_width), f32), mixed, query_part * query_rows, 0
            )
        middle = hidden + scatter_sum(mixed, group, blocks)
        inverse_ff = inverse_rms(middle)
        normed_ff = gather_rows((middle * inverse_ff * gain_ff[layer_id]).astype(bf16), ff_group)
        activated, slope = gelu_parts(contract(normed_ff, w_up, 1, 1))
        ff_result = jnp.dot(activated, w_down, preferred_element_type=f32)
        records.append(
            (hidden, inverse, units, qkv, attended, stats, middle, inverse_ff, normed_ff,
             activated, slope)
        )
        hidden = middle + scatter_sum(ff_result, ff_group, ff_members)
    output = hidden

    grads_ff, grads_in, grads_out, grads_gain_ff, grads_table = (
        [None] * layer_count for _ in range(5)
    )
    for layer_id in reversed(range(layer_count)):
        w_in, w_out, (w_up, w_down) = (
            weights_in[layer_id], weights_out[layer_id], weights_ff[layer_id],
        )
        (hidden, inverse, units, qkv, attended, stats, middle, inverse_ff, normed_ff,
         activated, slope) = records[layer_id]
        grad_low = gather_rows(upstream.astype(bf16), ff_group)
        grad_pre = (contract(grad_low, w_down, 1, 1) * slope).astype(bf16)
        grad_normed = scatter_sum(
            jnp.dot(grad_pre, w_up, preferred_element_type=f32), ff_group, ff_members
        )
        grad_pair = jnp.concatenate(
            [contract(grad_pre, normed_ff, 0, 0), contract(activated, grad_low, 0, 0)], axis=1
        ).astype(bf16)
        grads_ff[layer_id] = lax.psum_scatter(
            grad_pair, ff_spare, scatter_dimension=0, tiled=True
        ).astype(f32)
        grads_gain_ff[layer_id] = jnp.sum(grad_normed * middle * inverse_ff, axis=0)
        grad_middle = upstream + unit_norm_back(
            middle, inverse_ff, grad_normed * gain_ff[layer_id]
        )
        branch = gather_rows(grad_middle.astype(bf16), group)
        if split > 1:
            branch = lax.dynamic_slice_in_dim(branch, query_part * query_rows, query_rows, 0)
        grad_attended = contract(branch, w_out, 1, 1).astype(bf16)
        grad_qkv, grad_near, grad_far = attention_back(
            qkv, doc_row, doc_col, attended, grad_attended, stats, first, place, table, near, split
        )
        grads_table[layer_id] = (grad_near, grad_far)
        grad_units = scatter_sum(contract(grad_qkv, w_in, 1, 1), group, blocks)
        upstream = grad_middle + unit_norm_back(hidden, inverse, grad_units)
        grad_out = lax.dynamic_update_slice_in_dim(
            jnp.zeros((model_width, model_width), bf16),
            contract(attended, branch, 0, 0).astype(bf16),
            out_row,
            0,
        )
        grads_out[layer_id] = lax.psum_scatter(
            grad_out, everyone, scatter_dimension=0, tiled=True
        ).astype(f32)
        grads_in[layer_id] = contract(units, grad_qkv, 0, 0).astype(bf16)

    bucket_count = table.shape[0]
    grad_table = sum(
        bucket_grads(jnp.zeros((1,), jnp.int32), entry, bucket_count) for entry in grads_table
    )[:, :heads_dev]
    grad_table = lax.dynamic_update_slice_in_dim(
        jnp.zeros((bucket_count, heads_all), f32), grad_table, head_group * heads_dev, 1
    )
    grad_table = jnp.transpose(
        grad_table.reshape(blocks, bucket_count // blocks, heads_n, heads_all // heads_n),
        (2, 0, 1, 3),
    ).reshape(devices, -1)
    grad_gain_ff = jnp.transpose(
        jnp.stack(grads_gain_ff).reshape(layer_count, devices, weight_rows), (1, 0, 2)
    ).reshape(devices, -1)
    ends = jnp.sum(swap(jnp.concatenate([grad_gain_ff, grad_table], axis=1)), axis=0)
    grad_gain_ff = ends[: layer_count * weight_rows].reshape(layer_count, weight_rows)
    grad_bias_table = ends[layer_count * weight_rows :].reshape(
        bucket_count // blocks, heads_all // heads_n
    )
    grads_attn_in, grads_gains = [], []
    for layer_id in range(layer_count):
        parts = swap(grads_in[layer_id].reshape(devices, weight_rows, 3 * width)).astype(f32)
        parts = jnp.sum(parts.reshape(heads_n, blocks, weight_rows, 3 * width), axis=0)
        parts = jnp.sum(parts.reshape(head_groups, split, weight_rows, 3, width), axis=1)
        unit_grad = jnp.transpose(parts, (1, 2, 0, 3)).reshape(weight_rows, 3 * model_width)
        grads_attn_in.append(unit_grad * gain_attn[layer_id])
        grads_gains.append(
            jnp.stack(
                [jnp.sum(unit_grad * own_in[layer_id], axis=1), grad_gain_ff[layer_id]], axis=1
            )
        )
    return (
        output[None],
        upstream[None],
        jnp.stack(grads_attn_in),
        jnp.stack(grads_out),
        jnp.stack([entry[:, :model_width] for entry in grads_ff]),
        jnp.stack([entry[:, model_width:] for entry in grads_ff]),
        jnp.stack(grads_gains),
        grad_bias_table,
    )


def local_plane(tokens, doc_start, bias_table, attn_in, attn_out, ff_in, ff_out, gains, cotangent):
    heads_n, z_n, core_n = (lax.axis_size(axis) for axis in everyone)
    devices = heads_n * z_n * core_n
    at_head, at_z, at_core = (lax.axis_index(axis) for axis in everyone)
    members = heads_n * core_n
    block_rows, model_width = tokens.shape[1:]
    layer_count, weight_rows = attn_in.shape[:2]
    length = block_rows * members
    heads_all = bias_table.shape[1]
    heads_dev = heads_all // members
    width = heads_dev * head_dim
    member = at_head * core_n + at_core
    everywhere = [(h, z, c) for h in range(heads_n) for z in range(z_n) for c in range(core_n)]

    def swapped(bits):
        return bits % 2 * 2 + bits // 2

    def device(h, z, c):
        return (h * z_n + z) * core_n + c

    turn = [(device(h, z, c), device(h ^ swapped(z), h, c)) for h, z, c in everywhere]
    plane_turn = [(device(h, z, c), device(h ^ swapped(z), z, c)) for h, z, c in everywhere]
    line_turn = [(device(h, z, c), device(h, h ^ swapped(z), c)) for h, z, c in everywhere]
    line_back = [(target, source) for source, target in line_turn]
    place = jnp.stack(
        [
            (at_head ^ bits) * core_n + (at_core ^ other)
            for other in range(core_n)
            for bits in range(heads_n)
        ]
        + [at_z]
        + [
            swapped(at_head ^ bits ^ at_z) * core_n + (at_core ^ other)
            for other in range(core_n)
            for bits in range(heads_n)
        ]
    ).astype(jnp.int32)

    def relay(array):
        return lax.ppermute(array, everyone, turn)

    def turn_in_plane(array):
        return lax.ppermute(array, everyone, plane_turn)

    def turn_in_line(array, turns):
        return lax.ppermute(array, everyone, turns)

    def swap(array):
        return lax.all_to_all(array, everyone, 0, 0, tiled=True)

    row_shape = (block_rows, model_width)
    gain_attn = gains[:, :, 0].astype(f32)[:, :, None]
    near_share, far_share = call(
        share_in_kernel,
        [((members // 2 * layer_count * weight_rows, 3 * width), bf16)] * 2,
        place,
        attn_in,
        gain_attn,
        smem=1,
    )

    half_turns = [
        [
            (z * core_n + c, (2 * c + (a ^ z % 2)) * core_n + z // 2)
            for z in range(z_n)
            for c in range(core_n)
        ]
        for a in range(2)
    ]

    def fetch_out(layer_id, hold):
        own = attn_out[layer_id]
        other = toggle(own, "core", 1)
        head = jnp.where(
            at_core == 0, jnp.concatenate([own, other]), jnp.concatenate([other, own])
        )
        head = after(head, hold)
        return [
            lax.ppermute(head, ("z", "core"), [(holder, user) for user, holder in turns])
            for turns in half_turns
        ]

    def owners_halves(halves):
        return [
            lax.ppermute(half, ("z", "core"), turns) for half, turns in zip(halves, half_turns)
        ]

    def pair_chips(near, arrived, axis):
        rows, columns = near.shape[0] // 4, near.shape[1]
        shape = (2 * rows, columns) if axis == 0 else (rows, 2 * columns)
        return call(functools.partial(pair_kernel, axis), [(shape, bf16)] * 4, near, arrived)

    def share_chips(blocks):
        return [blocks[0]] + [toggle(blocks[bits], "head", bits) for bits in (1, 2, 3)]

    units_shape = [(row_shape, f32), (row_shape, bf16)]

    starts = jnp.broadcast_to(
        doc_start.astype(f32)[None, :, None], (heads_n, z_n, core_n, block_rows)
    )
    ff_gains = gains[:, :, 1].astype(f32).reshape(1, -1)
    small = jnp.concatenate(
        [
            starts.reshape(devices, block_rows),
            jnp.broadcast_to(ff_gains, (devices, layer_count * weight_rows)),
        ],
        axis=1,
    )
    table, strip = prepare(bias_table, member * heads_dev, heads_dev)
    hidden, strip = tie(relay(tokens[0]), strip)
    hidden, shares, cotangent_low, halves, small = tie(
        hidden,
        share_chips(pair_chips(near_share, toggle(far_share, "core", 1), 0)),
        turn_in_plane(after(cotangent[0].astype(bf16), near_share)),
        fetch_out(0, near_share),
        swap(after(small, near_share)),
    )
    hidden, unit_rows = call(unit_kernel, units_shape, hidden)
    doc_row = small[:members, :block_rows].reshape(2, 2, core_n, block_rows)
    at_block = swapped(at_head ^ at_z)
    for axis, bit in ((0, at_block // 2), (1, at_block % 2), (2, at_core)):
        doc_row = jnp.where(bit == 1, jnp.flip(doc_row, axis), doc_row)
    doc_row = jnp.transpose(doc_row, (2, 1, 0, 3)).reshape(1, length)
    doc_col = doc_row.reshape(length, 1)
    gain_ff = jnp.transpose(
        small[:, block_rows:].reshape(devices, layer_count, weight_rows), (1, 0, 2)
    ).reshape(layer_count, 1, model_width)

    def round_planes(array, by, hold):
        return shift(after(array, hold), by)

    ff_pairs = [
        jnp.concatenate([ff_in[layer_id], ff_out[layer_id]], axis=1) for layer_id in range(layer_count)
    ]

    def ff_both(kernel, row_operands, pair, columns):
        return zip(
            *(
                by_rows(
                    kernel,
                    256,
                    operands,
                    [pair],
                    [(pair.shape[0], bf16)] * columns + [(model_width, kind)],
                )
                for operands, kind in zip(zip(*row_operands), (f32, bf16))
            )
        )

    def ff_forward(normed, *parts):
        units = 4 * parts[0].shape[0]
        outs = [(units, bf16), (units, bf16)]
        *near, pair = by_rows(
            ff_first_kernel,
            256,
            [normed[0]],
            parts,
            outs + [(model_width, f32)],
            [(units, 2 * model_width)],
        )
        far = by_rows(ff_kernel, 256, [normed[1]], [pair], outs + [(model_width, bf16)])
        return pair, *zip(near, far)

    def ff_backward(low, slopes, pair):
        return ff_both(ff_back_kernel, [low, slopes], pair, 1)

    def assemble_in(share, lower, upper, opposite):
        return call(
            assemble_in_kernel,
            [((model_width, 3 * width), bf16)],
            place,
            share,
            lower,
            upper,
            opposite,
            smem=1,
        )[0]

    share, later_share = call(
        join_kernel, [((members * weight_rows, 3 * width), bf16)] * layer_count, *shares
    )
    near, far, lower, upper, opposite, doc_row, doc_col, gain_ff, *ff_pairs = plane_gather(
        unit_rows,
        shift(share, 1),
        shift(share, -1),
        shift(share, 2),
        doc_row,
        doc_col,
        gain_ff,
        *ff_pairs,
    )
    w_in = assemble_in(share, lower, upper, opposite)
    units = (near, far)
    w_out, qkv, attended, stats, *parts = plane_attention(
        *units, w_in, halves, doc_row, doc_col, place, table, strip
    )
    parts, lower, upper = tie(
        parts, round_planes(ff_pairs[0], 1, near), round_planes(ff_pairs[0], -1, near)
    )
    parts, own = plane_scatter(*parts)
    parts, opposite_in = tie(parts, round_planes(ff_in[0], 2, own))
    middle, normed_rows = call(close_gain_kernel, units_shape, hidden, *parts, gain_ff[0])
    *normed, opposite_out = plane_gather(normed_rows, round_planes(ff_out[0], 2, normed_rows))
    pair, acts, slopes, parts = ff_forward(
        normed, ff_pairs[0], lower, upper, opposite_in, opposite_out
    )
    records = [
        (hidden, units, w_in, w_out, pair, qkv, attended, stats, middle, normed, acts, slopes)
    ]
    halves_1 = fetch_out(1, normed[0])
    parts, lower, upper, first_half = tie(
        parts,
        round_planes(later_share, 1, normed[0]),
        round_planes(later_share, -1, normed[0]),
        halves_1[0],
    )
    parts, own = plane_scatter(*parts)
    parts, opposite, upstream = tie(
        parts, round_planes(later_share, 2, own), turn_in_line(after(cotangent_low, own), line_turn)
    )
    shares = [later_share, lower, upper, opposite]
    hidden, unit_rows = call(close_kernel, units_shape, middle, *parts)

    near, far, lower, second_half = plane_gather(
        unit_rows, round_planes(ff_pairs[1], 1, unit_rows), halves_1[1]
    )
    halves = [first_half, second_half]
    units = (near, far)
    w_in = assemble_in(*shares)
    w_out, qkv, attended, stats, *parts = plane_attention(
        *units, w_in, halves, doc_row, doc_col, place, table, strip
    )
    low = plane_gather(after(upstream, far))
    parts, near_low, upper = tie(parts, low[0], round_planes(ff_pairs[1], -1, far))
    low = (near_low, low[1])
    parts, own = plane_scatter(*parts)
    parts, opposite_in = tie(parts, round_planes(ff_in[1], 2, own))
    middle, normed_rows = call(close_gain_kernel, units_shape, hidden, *parts, gain_ff[1])
    *normed, opposite_out = plane_gather(normed_rows, round_planes(ff_out[1], 2, normed_rows))
    pair, acts, slopes, last_parts = ff_forward(
        normed, ff_pairs[1], lower, upper, opposite_in, opposite_out
    )
    records.append(
        (hidden, units, w_in, w_out, pair, qkv, attended, stats, middle, normed, acts, slopes)
    )

    def back_to_middle(parts, upstream, middle, gain):
        return call(
            middle_back_kernel, units_shape + [((1, model_width), f32)], upstream, *parts, middle, gain
        )

    def attention_grads(record, branch):
        _, _, w_in, w_out, _, qkv, attended, stats, *_ = record
        grad_qkv, grad_near, grad_far, near_part, far_part, *halves = plane_attention_back(
            qkv, doc_row, doc_col, attended, stats, *branch, w_in, w_out, place, table, strip
        )
        return grad_qkv, (grad_near, grad_far), (near_part, far_part), halves

    def table_grads(near_and_far):
        return bucket_grads(at_core.reshape(1) * heads_dev + 8, near_and_far, table.shape[0])

    record = records[1]
    hidden, units, _, _, pair, *_, middle, normed, acts, slopes = record
    pres, parts = ff_backward(low, slopes, pair)
    parts, own = plane_scatter(*parts)
    planes = ff_grads(after(pres, own), acts, normed, low)
    parts, ff_lower = tie(parts, shift(planes[1], -1))
    last_parts, _ = plane_scatter(*after(last_parts, parts))
    grad_middle, branch_rows, gain_1 = back_to_middle(parts, upstream, middle, gain_ff[1])
    *branch, ff_upper = plane_gather(branch_rows, round_planes(planes[2], 1, branch_rows))
    grad_qkv, strips_1, parts, halves_1 = attention_grads(record, branch)
    parts, last_parts, opposite_up = tie(
        parts, last_parts, round_planes(planes[3], 2, branch[1])
    )
    parts, own = plane_scatter(*parts)
    parts, opposite_down, output = tie(
        parts,
        round_planes(planes[4], 2, own),
        call(last_kernel, [(row_shape, bf16)], middle, *after(last_parts, own))[0],
    )
    grads_ff = [planes[0], ff_lower, ff_upper, opposite_up, opposite_down]
    upstream, low_rows = call(layer_back_kernel, units_shape, grad_middle, *parts, hidden)

    record = records[0]
    hidden, units, _, _, pair, *_, middle, normed, acts, slopes = record
    grad_in = in_planes(place, *records[1][1], after(grad_qkv, low_rows))
    *low, in_opposite, in_upper, table_1 = plane_gather(
        low_rows, shift(grad_in[3], 2), shift(grad_in[2], 1), table_grads(after(strips_1, low_rows))
    )
    pres, parts = ff_backward(low, slopes, pair)
    parts, in_lower = tie(parts, round_planes(grad_in[1], -1, low[0]))
    parts, own = plane_scatter(*parts)
    planes = ff_grads(after(pres, own), acts, normed, low)
    near_in, far_in = call(
        add_in_kernel,
        [((members // 2 * weight_rows, 3 * width), bf16)] * 2,
        *after([grad_in[0], in_lower, in_upper, in_opposite], own),
    )
    parts, ff_lower, first_half, arrived = tie(
        parts,
        shift(planes[1], -1),
        owners_halves(after(halves_1, own))[0],
        toggle(far_in, "core", 1),
    )
    grad_middle, branch_rows, gain_0 = back_to_middle(parts, upstream, middle, gain_ff[0])
    *branch, ff_upper, second_half, shares_1 = plane_gather(
        branch_rows,
        round_planes(planes[2], 1, branch_rows),
        owners_halves(after(halves_1, branch_rows))[1],
        pair_chips(near_in, after(arrived, branch_rows), 1),
    )
    halves_1 = [first_half, second_half]
    grad_qkv, strips_0, parts, halves_0 = attention_grads(record, branch)
    parts, shares_1, output, opposite_up = tie(
        parts,
        share_chips(after(shares_1, branch[1])), turn_in_line(after(output, branch[1]), line_back), round_planes(planes[3], 2, branch[1])
    )
    parts, own = plane_scatter(*parts)
    table_0 = table_grads(after(strips_0, own))
    grad_in = in_grads(
        place, *units, after(grad_qkv, own), gain_0, gain_1, table_0, table_1
    )
    parts, opposite_down, grad_in = tie(parts, round_planes(planes[4], 2, own), grad_in)
    upstream, low_rows = call(layer_back_kernel, units_shape, grad_middle, *parts, hidden)
    line = turn_in_line(low_rows, line_back)
    grads_in_0 = swap(after(grad_in, low_rows).reshape(devices, weight_rows, 3 * width + tile))
    halves_0 = owners_halves(after(halves_0, low_rows))
    grad_tokens = turn_in_plane(line)
    output = turn_in_plane(after(output, low_rows)).astype(f32)
    grads_ff = [planes[0], ff_lower, ff_upper, opposite_up, opposite_down] + grads_ff
    grad_up, grad_down = finish_ff(after(grads_ff, low_rows), ff_in.shape)
    own_out, other_out = call(
        add_out_kernel,
        [(attn_out.shape, f32), (attn_out.shape, bf16)],
        place,
        *halves_0,
        *halves_1,
        smem=1,
    )
    (grad_attn_out,) = call(
        finish_out_kernel, [(attn_out.shape, f32)], own_out, toggle(other_out, "core", 1)
    )
    own_buckets = table.shape[0] // (z_n * core_n)
    grad_attn_in, grad_gains, ends = call(
        finish_in_kernel,
        [(attn_in.shape, f32), (gains.shape, f32), ((weight_rows, tile), f32)],
        place,
        grads_in_0,
        *shares_1,
        attn_in,
        gain_attn,
        smem=1,
    )
    return (
        output[None],
        grad_tokens.astype(f32)[None],
        grad_attn_in,
        grad_attn_out,
        grad_up,
        grad_down,
        grad_gains,
        ends[:own_buckets, 8 : 8 + heads_all // heads_n],
    )


def solution(mesh):
    sizes = dict(mesh.shape)
    cores = 2
    fine = Mesh(
        mesh.devices.reshape(sizes["head"], sizes["blk"] // cores, cores), everyone
    )
    blk = ("z", "core")
    in_specs = (
        P("head", blk, None),
        P(None, blk),
        P(),
        P(None, everyone, None),
        P(None, everyone, None),
        P(None, everyone, None),
        P(None, everyone, None),
        P(None, everyone, None),
        P("head", blk, None),
    )
    out_specs = (
        P("head", blk, None),
        P("head", blk, None),
        P(None, everyone, None),
        P(None, everyone, None),
        P(None, everyone, None),
        P(None, everyone, None),
        P(None, everyone, None),
        P(blk, "head"),
    )
    plane = sizes["head"] == 4 and sizes["blk"] == 8
    local = local_plane if plane else local_general
    return jax.shard_map(local, mesh=fine, in_specs=in_specs, out_specs=out_specs, check_vma=False)
```

```python
import functools

import jax
import jax.numpy as jnp
import numpy as np
from jax import lax
from jax.experimental import pallas as pl
from jax.experimental.pallas import tpu as pltpu
from jax.sharding import Mesh
from jax.sharding import PartitionSpec as P

bounds = (1, 2, 3, 4, 5, 6, 7, 8, 12, 16, 23, 32, 46, 64, 91)
epsilon = 1e-06
masked = -1e30
score_scale = 0.125
head_dim = 64
tile = 128
everyone = ("head", "z", "core")
bf16 = jnp.bfloat16
f32 = jnp.float32


def contract(lhs, rhs, lhs_dim, rhs_dim):
    return lax.dot_general(
        lhs, rhs, (((lhs_dim,), (rhs_dim,)), ((), ())), preferred_element_type=f32
    )


def near_buckets(shape):
    offsets = (
        lax.broadcasted_iota(jnp.int32, shape, 1) - tile - lax.broadcasted_iota(jnp.int32, shape, 0)
    )
    distance = jnp.abs(offsets)
    bucket = jnp.where(offsets > 0, 16, 0)
    for boundary in bounds:
        bucket = bucket + jnp.where(distance >= boundary, 1, 0)
    return bucket


def near_kernel(table, near):
    bucket = near_buckets(near.shape[1:])
    for head in range(near.shape[0]):
        values = jnp.zeros(near.shape[1:], f32)
        for bucket_id in range(table.shape[0]):
            values = jnp.where(bucket == bucket_id, table[bucket_id, head], values)
        near[head] = values


def bucket_kernel(first_lane, near, far, out):
    bucket = near_buckets(near.shape[1:])
    rows = lax.broadcasted_iota(jnp.int32, out.shape, 0)
    lanes = lax.broadcasted_iota(jnp.int32, out.shape, 1)
    total = jnp.zeros(out.shape, f32)
    for head in range(near.shape[0]):
        strip = near[head]
        for bucket_id in range(out.shape[0]):
            value = jnp.sum(jnp.where(bucket == bucket_id, strip, 0.0), axis=0, keepdims=True)
            value = jnp.sum(value, axis=1, keepdims=True)
            if bucket_id in (15, 31):
                value = value + far[head, bucket_id // 16, :1, :1]
            total = jnp.where((rows == bucket_id) & (lanes == head + first_lane[0]), value, total)
    out[...] = total


def fill_band(band, table, near, heads_dev, length):
    for head in range(heads_dev):
        band[head, :, : length - tile] = jnp.full((tile, length - tile), table[15, head], f32)
        band[head, :, length - tile : length + 2 * tile] = near[head]
        band[head, :, length + 2 * tile :] = jnp.full(
            (tile, length - 2 * tile), table[31, head], f32
        )


def band_starts(place, at, length, skip=0):
    return [
        pl.multiple_of(length + (place[skip + block] - place[skip + at]) * tile, tile)
        for block in range(length // tile)
    ]


def attention_kernel(
    heads_dev, length, first, place, table, near, qkv, doc_row, doc_col, out, local, stats, band
):
    step = pl.program_id(0)
    width = heads_dev * head_dim

    @pl.when(step == 0)
    def _():
        fill_band(band, table, near, heads_dev, length)

    row = pl.multiple_of((first[0] + step) * tile, tile)
    out_row = pl.multiple_of((place[first[0] + step] - first[0]) * tile, tile)
    starts = band_starts(place, first[0] + step, length)
    same_doc = doc_col[...] == doc_row[...]
    queries = qkv[pl.ds(row, tile), :width] * bf16(score_scale)
    lanes = lax.broadcasted_iota(jnp.int32, (tile, tile), 1)
    collected = jnp.zeros((tile, tile), f32)
    for head in range(heads_dev):
        own = slice(head * head_dim, (head + 1) * head_dim)
        keys = qkv[:, width + own.start : width + own.stop]
        values = qkv[:, 2 * width + own.start : 2 * width + own.stop]
        scores = contract(queries[:, own], keys, 1, 1)
        scores = scores + jnp.concatenate(
            [band[head, :, pl.ds(start, tile)] for start in starts], axis=1
        )
        scores = jnp.where(same_doc, scores, masked)
        peak = jnp.max(scores, axis=1, keepdims=True)
        weights = jnp.exp(scores - peak)
        total = jnp.sum(weights, axis=1, keepdims=True)
        mixed = contract(weights.astype(bf16), values, 1, 0) / total
        out[pl.ds(out_row, tile), own] = mixed.astype(bf16)
        local[:, own] = mixed.astype(bf16)
        collected = jnp.where(lanes == head, peak + jnp.log(total), collected)
    stats[...] = collected


def attention_back_kernel(
    heads_dev, length, split, first, place, table, near, qkv, doc_row, doc_col, attended, grad_out, stats,
    grad_qkv, grad_near, grad_far, band, grad_band, grad_keys, grad_values,
):
    step = pl.program_id(0)
    width = heads_dev * head_dim

    @pl.when(step == 0)
    def _():
        fill_band(band, table, near, heads_dev, length)
        grad_band[...] = jnp.zeros_like(grad_band)
        grad_keys[...] = jnp.zeros_like(grad_keys)
        grad_values[...] = jnp.zeros_like(grad_values)
        if split > 1:
            grad_qkv[...] = jnp.zeros_like(grad_qkv)

    row = pl.multiple_of((first[0] + step) * tile, tile)
    out_row = pl.multiple_of((place[first[0] + step] - first[0]) * tile, tile)
    starts = band_starts(place, first[0] + step, length)
    same_doc = doc_col[...] == doc_row[...]
    at_step = pl.multiple_of(step * tile, tile)
    queries = qkv[pl.ds(row, tile), :width] * bf16(score_scale)
    for head in range(heads_dev):
        own = slice(head * head_dim, (head + 1) * head_dim)
        keys = qkv[:, width + own.start : width + own.stop]
        values = qkv[:, 2 * width + own.start : 2 * width + own.stop]
        upstream = grad_out[pl.ds(out_row, tile), own]
        scores = contract(queries[:, own], keys, 1, 1) + jnp.concatenate(
            [band[head, :, pl.ds(start, tile)] for start in starts], axis=1
        )
        scores = jnp.where(same_doc, scores, masked)
        weights = jnp.exp(scores - stats[:, head : head + 1])
        delta = jnp.sum(
            upstream.astype(f32) * attended[pl.ds(at_step, tile), own].astype(f32),
            axis=1,
            keepdims=True,
        )
        grad_scores = weights * (contract(upstream, values, 1, 1) - delta)
        for block, start in enumerate(starts):
            grad_band[head, :, pl.ds(start, tile)] += grad_scores[
                :, block * tile : (block + 1) * tile
            ]
        grad_low = grad_scores.astype(bf16)
        grad_values[:, own] += contract(weights.astype(bf16), upstream, 0, 0)
        grad_keys[:, own] += contract(grad_low, queries[:, own], 0, 0)
        grad_qkv[pl.ds(row, tile), own] = (
            contract(grad_low, keys, 1, 0) * score_scale
        ).astype(bf16)

    @pl.when(step == pl.num_programs(0) - 1)
    def _():
        grad_qkv[:, width : 2 * width] = grad_keys[...].astype(bf16)
        grad_qkv[:, 2 * width :] = grad_values[...].astype(bf16)
        for head in range(heads_dev):
            grad_near[head] = grad_band[head, :, length - tile : length + 2 * tile]
            grad_far[head, 0] = jnp.full(
                (8, tile), jnp.sum(grad_band[head, :, : length - tile]), f32
            )
            grad_far[head, 1] = jnp.full(
                (8, tile), jnp.sum(grad_band[head, :, length + 2 * tile :]), f32
            )


def whole(shape):
    return pl.BlockSpec(shape, lambda step: (0,) * len(shape), pipeline_mode=pl.Buffered(1))


def attention(qkv, doc_row, doc_col, first, place, table, near, rows):
    length = qkv.shape[0]
    heads_dev = table.shape[1]
    width = heads_dev * head_dim
    return pl.pallas_call(
        functools.partial(attention_kernel, heads_dev, length),
        grid=(rows // tile,),
        in_specs=[
            pl.BlockSpec(memory_space=pltpu.SMEM),
            pl.BlockSpec(memory_space=pltpu.SMEM),
            pl.BlockSpec(memory_space=pltpu.SMEM),
            whole(near.shape),
            whole(qkv.shape),
            whole(doc_row.shape),
            pl.BlockSpec((tile, 1), lambda step: (step, 0)),
        ],
        out_specs=[
            whole((rows, width)),
            pl.BlockSpec((tile, width), lambda step: (step, 0)),
            pl.BlockSpec((tile, tile), lambda step: (step, 0)),
        ],
        out_shape=[
            jax.ShapeDtypeStruct((rows, width), bf16),
            jax.ShapeDtypeStruct((rows, width), bf16),
            jax.ShapeDtypeStruct((rows, tile), f32),
        ],
        scratch_shapes=[pltpu.VMEM((heads_dev, tile, 2 * length), f32)],
        compiler_params=pltpu.CompilerParams(vmem_limit_bytes=40 * 2**20),
        cost_estimate=pl.CostEstimate(
            flops=4 * rows * length * width,
            bytes_accessed=4 * length * width * 2,
            transcendentals=rows * length * heads_dev,
        ),
    )(first, place, table, near, qkv, doc_row, doc_col)


def attention_back(
    qkv, doc_row, doc_col, attended, grad_out, stats, first, place, table, near, split
):
    length = qkv.shape[0]
    rows = grad_out.shape[0]
    heads_dev = table.shape[1]
    width = heads_dev * head_dim
    return pl.pallas_call(
        functools.partial(attention_back_kernel, heads_dev, length, split),
        grid=(rows // tile,),
        in_specs=[
            pl.BlockSpec(memory_space=pltpu.SMEM),
            pl.BlockSpec(memory_space=pltpu.SMEM),
            pl.BlockSpec(memory_space=pltpu.SMEM),
            whole(near.shape),
            whole(qkv.shape),
            whole(doc_row.shape),
            pl.BlockSpec((tile, 1), lambda step: (step, 0)),
            whole((rows, width)),
            whole((rows, width)),
            pl.BlockSpec((tile, tile), lambda step: (step, 0)),
        ],
        out_specs=[
            whole((length, 3 * width)),
            whole((heads_dev, tile, 3 * tile)),
            whole((heads_dev, 2, 8, tile)),
        ],
        out_shape=[
            jax.ShapeDtypeStruct((length, 3 * width), bf16),
            jax.ShapeDtypeStruct((heads_dev, tile, 3 * tile), f32),
            jax.ShapeDtypeStruct((heads_dev, 2, 8, tile), f32),
        ],
        scratch_shapes=[
            pltpu.VMEM((heads_dev, tile, 2 * length), f32),
            pltpu.VMEM((heads_dev, tile, 2 * length), f32),
            pltpu.VMEM((length, width), f32),
            pltpu.VMEM((length, width), f32),
        ],
        compiler_params=pltpu.CompilerParams(vmem_limit_bytes=48 * 2**20),
        cost_estimate=pl.CostEstimate(
            flops=10 * rows * length * width,
            bytes_accessed=8 * length * width * 2,
            transcendentals=rows * length * heads_dev,
        ),
    )(first, place, table, near, qkv, doc_row, doc_col, attended, grad_out, stats)


def call(kernel, shapes, *operands, smem=0):
    return pl.pallas_call(
        kernel,
        in_specs=[pl.BlockSpec(memory_space=pltpu.SMEM)] * smem
        + [pl.BlockSpec(memory_space=pltpu.VMEM)] * (len(operands) - smem),
        out_specs=[pl.BlockSpec(memory_space=pltpu.VMEM)] * len(shapes),
        out_shape=[jax.ShapeDtypeStruct(shape, kind) for shape, kind in shapes],
        compiler_params=pltpu.CompilerParams(vmem_limit_bytes=10 * 2**20),
    )(*operands)


def share_in_kernel(place, attn_in, gains, near, far):
    layers, rows = attn_in.shape[:2]
    half = near.shape[0] // (layers * rows)
    width = near.shape[1] // 3
    for index in range(2 * half):
        member = place[index]
        for layer_id in range(layers):
            block = jnp.concatenate(
                [
                    attn_in[
                        layer_id,
                        :,
                        pl.ds(pl.multiple_of((part * 2 * half + member) * width, width), width),
                    ]
                    for part in range(3)
                ],
                axis=1,
            )
            at = (index % half * layers + layer_id) * rows
            out = near if index < half else far
            out[at : at + rows] = (block.astype(f32) * gains[layer_id]).astype(bf16)


def join_kernel(*refs):
    shares, outs = refs[:4], refs[4:]
    rows = outs[0].shape[0] // 8
    for chip, share in enumerate(shares):
        for core in range(2):
            for layer_id, out in enumerate(outs):
                source = (core * len(outs) + layer_id) * rows
                target = (chip * 2 + core) * rows
                out[target : target + rows] = share[source : source + rows]


def row_of(chip, plane, core, rows, planes=4):
    return pl.multiple_of(((chip * planes + plane) * 2 + core) * rows, rows)


def assemble_in_kernel(place, own, lower, upper, opposite, out):
    at_z, at_core, at_head = place[8], place[0] % 2, place[0] // 2
    rows = own.shape[0] // 8
    for part, offset in ((own, 0), (lower, 3), (upper, 1), (opposite, 2)):
        plane = (at_z + offset) % 4
        for index in range(8):
            row = row_of(at_head ^ (index // 2), plane, at_core ^ (index % 2), rows)
            out[pl.ds(row, rows)] = part[index * rows : (index + 1) * rows]


def plane_attention_kernel(
    length, place, table, strip, near, far, w_in, *refs
):
    halves, (doc_row, doc_col, w_out, qkv, attended, stats, near_part, far_part, band) = (
        refs[:2], refs[2:],
    )
    step = pl.program_id(0)
    half = length // 2
    heads_dev = table.shape[1]
    width = heads_dev * head_dim

    @pl.when(step == 0)
    def _():
        fill_band(band, table, strip, heads_dev, length)
        swapped = place[length // tile] % 2 == 1
        rows = width // 2
        w_out[:rows] = jnp.where(swapped, halves[1][...], halves[0][...])
        w_out[rows:] = jnp.where(swapped, halves[0][...], halves[1][...])
        qkv[:half] = contract(near[...], w_in[...], 1, 0).astype(bf16)
        qkv[half:] = contract(far[...], w_in[...], 1, 0).astype(bf16)

    row = pl.multiple_of(step * tile, tile)
    starts = band_starts(place, step, length, length // tile + 1)
    same_doc = doc_col[...] == doc_row[...]
    queries = qkv[pl.ds(row, tile), :width] * bf16(score_scale)
    lanes = lax.broadcasted_iota(jnp.int32, (tile, tile), 1)
    collected = jnp.zeros((tile, tile), f32)
    results = []
    for head in range(heads_dev):
        own = slice(head * head_dim, (head + 1) * head_dim)
        keys = qkv[:, width + own.start : width + own.stop]
        values = qkv[:, 2 * width + own.start : 2 * width + own.stop]
        scores = contract(queries[:, own], keys, 1, 1) + jnp.concatenate(
            [band[head, :, pl.ds(start, tile)] for start in starts], axis=1
        )
        scores = jnp.where(same_doc, scores, masked)
        peak = jnp.max(scores, axis=1, keepdims=True)
        weights = jnp.exp(scores - peak)
        total = jnp.sum(weights, axis=1, keepdims=True)
        results.append((contract(weights.astype(bf16), values, 1, 0) / total).astype(bf16))
        collected = jnp.where(lanes == head, peak + jnp.log(total), collected)
    stats[...] = collected
    merged = jnp.concatenate(results, axis=1)
    attended[...] = merged
    part = contract(merged, w_out[...], 1, 0)

    @pl.when(row < half)
    def _():
        near_part[...] = part

    @pl.when(row >= half)
    def _():
        far_part[...] = part.astype(bf16)


def near_block(steps, columns):
    return pl.BlockSpec((tile, columns), lambda step: (jnp.minimum(step, steps // 2 - 1), 0))


def far_block(steps, columns):
    return pl.BlockSpec((tile, columns), lambda step: (jnp.maximum(step - steps // 2, 0), 0))


def plane_attention(near, far, w_in, halves, doc_row, doc_col, place, table, strip):
    length, model_width = 2 * near.shape[0], near.shape[1]
    steps = length // tile
    heads_dev = table.shape[1]
    width = heads_dev * head_dim
    return pl.pallas_call(
        functools.partial(plane_attention_kernel, length),
        grid=(steps,),
        in_specs=[
            pl.BlockSpec(memory_space=pltpu.SMEM),
            pl.BlockSpec(memory_space=pltpu.SMEM),
            whole(strip.shape),
            whole(near.shape),
            whole(far.shape),
            whole(w_in.shape),
            *[whole(half.shape) for half in halves],
            whole(doc_row.shape),
            pl.BlockSpec((tile, 1), lambda step: (step, 0)),
        ],
        out_specs=[
            whole((width, model_width)),
            whole((length, 3 * width)),
            pl.BlockSpec((tile, width), lambda step: (step, 0)),
            pl.BlockSpec((tile, tile), lambda step: (step, 0)),
            near_block(steps, model_width),
            far_block(steps, model_width),
        ],
        out_shape=[
            jax.ShapeDtypeStruct((width, model_width), bf16),
            jax.ShapeDtypeStruct((length, 3 * width), bf16),
            jax.ShapeDtypeStruct((length, width), bf16),
            jax.ShapeDtypeStruct((length, tile), f32),
            jax.ShapeDtypeStruct((length // 2, model_width), f32),
            jax.ShapeDtypeStruct((length // 2, model_width), bf16),
        ],
        scratch_shapes=[pltpu.VMEM((heads_dev, tile, 2 * length), f32)],
        compiler_params=pltpu.CompilerParams(vmem_limit_bytes=14 * 2**20),
        cost_estimate=pl.CostEstimate(
            flops=4 * length * length * width + 8 * length * model_width * width,
            bytes_accessed=12 * 2**20,
            transcendentals=length * length * heads_dev,
        ),
    )(place, table, strip, near, far, w_in, *halves, doc_row, doc_col)


def plane_attention_back_kernel(
    length, place, table, strip, qkv, doc_row, doc_col, attended, stats, near, far, w_in, w_out,
    grad_qkv, grad_near, grad_far, near_part, far_part, *rest
):
    halves, (band, grad_band, grad_keys, grad_values, out_sum) = rest[:2], rest[2:]
    step = pl.program_id(0)
    half = length // 2
    heads_dev = table.shape[1]
    width = heads_dev * head_dim

    @pl.when(step == 0)
    def _():
        fill_band(band, table, strip, heads_dev, length)
        grad_band[...] = jnp.zeros_like(grad_band)
        grad_keys[...] = jnp.zeros_like(grad_keys)
        grad_values[...] = jnp.zeros_like(grad_values)
        out_sum[...] = jnp.zeros_like(out_sum)

    row = pl.multiple_of(step * half, half)
    branch = jnp.where(step == 0, near[...], far[...])
    merged = attended[...]
    grad_merged = contract(branch, w_out[...], 1, 1).astype(bf16)
    out_sum[...] += contract(merged, branch, 0, 0)
    products = grad_merged.astype(f32) * merged.astype(f32)
    queries = qkv[pl.ds(row, half), :width] * bf16(score_scale)
    blocks = half // tile
    for head in range(heads_dev):
        own = slice(head * head_dim, (head + 1) * head_dim)
        keys = qkv[:, width + own.start : width + own.stop]
        values = qkv[:, 2 * width + own.start : 2 * width + own.stop]
        upstream = grad_merged[:, own]
        raw_scores = contract(queries[:, own], keys, 1, 1)
        grad_weights = contract(upstream, values, 1, 1)
        delta = jnp.sum(products[:, own], axis=1, keepdims=True)
        weights_low, grads_low = [], []
        for block in range(blocks):
            lines = slice(block * tile, (block + 1) * tile)
            starts = band_starts(place, step * blocks + block, length, length // tile + 1)
            scores = raw_scores[lines] + jnp.concatenate(
                [band[head, :, pl.ds(start, tile)] for start in starts], axis=1
            )
            scores = jnp.where(doc_col[lines] == doc_row[...], scores, masked)
            weights = jnp.exp(scores - stats[lines, head : head + 1])
            grad_scores = weights * (grad_weights[lines] - delta[lines])
            for index, start in enumerate(starts):
                grad_band[head, :, pl.ds(start, tile)] += grad_scores[
                    :, index * tile : (index + 1) * tile
                ]
            weights_low.append(weights.astype(bf16))
            grads_low.append(grad_scores.astype(bf16))
        weights_low, grads_low = jnp.concatenate(weights_low), jnp.concatenate(grads_low)
        grad_values[:, own] += contract(weights_low, upstream, 0, 0)
        grad_keys[:, own] += contract(grads_low, queries[:, own], 0, 0)
        grad_qkv[pl.ds(row, half), own] = (
            contract(grads_low, keys, 1, 0) * score_scale
        ).astype(bf16)

    @pl.when(step == pl.num_programs(0) - 1)
    def _():
        grad_qkv[:, width : 2 * width] = grad_keys[...].astype(bf16)
        grad_qkv[:, 2 * width :] = grad_values[...].astype(bf16)
        far_part[...] = contract(grad_qkv[half:], w_in[...], 1, 1).astype(bf16)
        near_part[...] = contract(grad_qkv[:half], w_in[...], 1, 1)
        rows = width // 2
        for index, part in enumerate(halves):
            block = index ^ place[length // tile] % 2
            part[...] = out_sum[pl.ds(pl.multiple_of(block * rows, rows), rows)].astype(bf16)
        for head in range(heads_dev):
            grad_near[head] = grad_band[head, :, length - tile : length + 2 * tile]
            grad_far[head, 0] = jnp.full(
                (8, tile), jnp.sum(grad_band[head, :, : length - tile]), f32
            )
            grad_far[head, 1] = jnp.full(
                (8, tile), jnp.sum(grad_band[head, :, length + 2 * tile :]), f32
            )


def plane_attention_back(
    qkv, doc_row, doc_col, attended, stats, near, far, w_in, w_out, place, table, strip
):
    length, model_width = 2 * near.shape[0], near.shape[1]
    half = length // 2
    heads_dev = table.shape[1]
    width = heads_dev * head_dim
    shapes = [
        ((length, 3 * width), bf16),
        ((heads_dev, tile, 3 * tile), f32),
        ((heads_dev, 2, 8, tile), f32),
        ((length // 2, model_width), f32),
        ((length // 2, model_width), bf16),
    ] + [((width // 2, model_width), bf16)] * 2
    return pl.pallas_call(
        functools.partial(plane_attention_back_kernel, length),
        grid=(2,),
        in_specs=[
            pl.BlockSpec(memory_space=pltpu.SMEM),
            pl.BlockSpec(memory_space=pltpu.SMEM),
            whole(strip.shape),
            whole(qkv.shape),
            whole(doc_row.shape),
            pl.BlockSpec((half, 1), lambda step: (step, 0)),
            pl.BlockSpec((half, width), lambda step: (step, 0)),
            pl.BlockSpec((half, tile), lambda step: (step, 0)),
            whole((half, model_width)),
            whole((half, model_width)),
            whole(w_in.shape),
            whole(w_out.shape),
        ],
        out_specs=[whole(shape) for shape, _ in shapes],
        out_shape=[jax.ShapeDtypeStruct(shape, kind) for shape, kind in shapes],
        scratch_shapes=[
            pltpu.VMEM((heads_dev, tile, 2 * length), f32),
            pltpu.VMEM((heads_dev, tile, 2 * length), f32),
            pltpu.VMEM((length, width), f32),
            pltpu.VMEM((length, width), f32),
            pltpu.VMEM((width, model_width), f32),
        ],
        compiler_params=pltpu.CompilerParams(vmem_limit_bytes=32 * 2**20),
        cost_estimate=pl.CostEstimate(
            flops=10 * length * length * width + 10 * length * model_width * width,
            bytes_accessed=12 * 2**20,
            transcendentals=length * length * heads_dev,
        ),
    )(place, table, strip, qkv, doc_row, doc_col, attended, stats, near, far, w_in, w_out)


def gelu_and_slope(pre_act):
    size = jnp.abs(pre_act)
    gauss = jnp.exp(-0.5 * pre_act * pre_act)
    ratio = 1.0 / (1.0 + np.float32(0.3275911 * 0.5**0.5) * size)
    series = np.float32(1.061405429)
    for factor in (-1.453152027, 1.421413741, -0.284496736, 0.254829592):
        series = series * ratio + np.float32(factor)
    tail = 0.5 * series * ratio * gauss
    cumulative = jnp.where(pre_act < 0, tail, 1.0 - tail)
    slope = cumulative + pre_act * gauss * np.float32((2 * np.pi) ** -0.5)
    return pre_act * cumulative, slope


def ff_kernel(rows, pair, activated, slope, part):
    columns = rows.shape[1]
    value, gradient = gelu_and_slope(contract(rows[...], pair[:, :columns], 1, 1))
    activated[...] = value.astype(bf16)
    slope[...] = gradient.astype(bf16)
    part[...] = contract(activated[...], pair[:, columns:], 1, 0).astype(part.dtype)


def ff_first_kernel(rows, *refs):
    parts, (activated, slope, part, pair) = refs[:5], refs[5:]

    @pl.when(pl.program_id(0) == 0)
    def _():
        units, columns = parts[0].shape[0], rows.shape[1]
        for index, ref in enumerate(parts[:3]):
            pair[index * units : (index + 1) * units] = ref[...]
        pair[3 * units :, :columns] = parts[3][...]
        pair[3 * units :, columns:] = parts[4][...]

    ff_kernel(rows, pair, activated, slope, part)


def ff_back_kernel(rows, slope, pair, grad_pre, part):
    columns = rows.shape[1]
    grad_act = contract(rows[...], pair[:, columns:], 1, 1)
    grad_pre[...] = (grad_act * slope[...].astype(f32)).astype(bf16)
    part[...] = contract(grad_pre[...], pair[:, :columns], 1, 0).astype(part.dtype)


def by_rows(kernel, step_rows, row_operands, whole_operands, outs, whole_outs=()):
    rows = row_operands[0].shape[0]
    return pl.pallas_call(
        kernel,
        grid=(rows // step_rows,),
        in_specs=[
            pl.BlockSpec((step_rows, operand.shape[1]), lambda step: (step, 0))
            for operand in row_operands
        ]
        + [whole(operand.shape) for operand in whole_operands],
        out_specs=[pl.BlockSpec((step_rows, columns), lambda step: (step, 0)) for columns, _ in outs]
        + [whole(shape) for shape in whole_outs],
        out_shape=[jax.ShapeDtypeStruct((rows, columns), kind) for columns, kind in outs]
        + [jax.ShapeDtypeStruct(shape, bf16) for shape in whole_outs],
        compiler_params=pltpu.CompilerParams(vmem_limit_bytes=10 * 2**20),
        cost_estimate=pl.CostEstimate(
            flops=4 * rows * outs[0][0] * row_operands[0].shape[1],
            bytes_accessed=6 * 2**20,
            transcendentals=0,
        ),
    )(*row_operands, *whole_operands)


def ff_grads_kernel(
    pre_near, pre_far, act_near, act_far, normed_near, normed_far, low_near, low_far, *outs
):
    columns = normed_near.shape[1]
    units = outs[0].shape[0]
    up = (
        contract(pre_near[...], normed_near[...], 0, 0)
        + contract(pre_far[...], normed_far[...], 0, 0)
    ).astype(bf16)
    down = (
        contract(act_near[...], low_near[...], 0, 0) + contract(act_far[...], low_far[...], 0, 0)
    ).astype(bf16)

    @pl.when(pl.program_id(0) == 0)
    def _():
        for index in range(2):
            block = slice(index * units, (index + 1) * units)
            outs[index][:, :columns] = up[block]
            outs[index][:, columns:] = down[block]

    @pl.when(pl.program_id(0) == 1)
    def _():
        outs[2][:, :columns] = up[:units]
        outs[2][:, columns:] = down[:units]
        outs[3][...] = up[units:]
        outs[4][...] = down[units:]


def ff_grads(pre, act, normed, low):
    rows, hidden_units = pre[0].shape
    columns = normed[0].shape[1]
    shapes = [(hidden_units // 4, 2 * columns)] * 3 + [(hidden_units // 4, columns)] * 2
    return pl.pallas_call(
        ff_grads_kernel,
        grid=(2,),
        in_specs=[pl.BlockSpec((rows, hidden_units // 2), lambda step: (0, step))] * 4
        + [whole((rows, columns))] * 4,
        out_specs=[whole(shape) for shape in shapes],
        out_shape=[jax.ShapeDtypeStruct(shape, bf16) for shape in shapes],
        compiler_params=pltpu.CompilerParams(vmem_limit_bytes=14 * 2**20),
        cost_estimate=pl.CostEstimate(
            flops=8 * rows * hidden_units * columns, bytes_accessed=8 * 2**20, transcendentals=0
        ),
    )(*pre, *act, *normed, *low)


def in_grads_kernel(place, near, far, grad_qkv, *refs):
    ends, outs, (total, extra) = refs[:-6], refs[-6:-2], refs[-2:]
    half = near.shape[0]
    columns = grad_qkv.shape[1]
    total[:, :columns] = (
        contract(near[...], grad_qkv[:half], 0, 0) + contract(far[...], grad_qkv[half:], 0, 0)
    ).astype(bf16)
    rows = outs[0].shape[0] // 8
    if ends:
        gain_0, gain_1, table_0, table_1 = ends
        lines = lax.broadcasted_iota(jnp.int32, (tile, gain_0.shape[1]), 0)
        gains = jnp.where(lines == 0, gain_0[...], jnp.where(lines == 1, gain_1[...], 0.0))
        extra[...] = jnp.transpose(gains)
        table = table_0[...] + table_1[...]
        buckets = table.shape[0] // 8
        blank = jnp.zeros((8 - buckets, tile), f32)
        for block in range(8):
            row = pl.multiple_of((place[0] // 2 * 8 + block) * rows, rows)
            extra[pl.ds(row, 8)] += jnp.concatenate(
                [table[block * buckets : (block + 1) * buckets], blank]
            )
        total[:, columns:] = extra[...].astype(bf16)
    for out, offset in zip(outs, (0, 3, 1, 2)):
        plane = (place[8] + offset) % 4
        for index in range(8):
            owner = place[index]
            row = row_of(owner // 2, plane, owner % 2, rows)
            out[index * rows : (index + 1) * rows] = total[pl.ds(row, rows)]


def in_grads(place, near, far, grad_qkv, *ends):
    columns = grad_qkv.shape[1] + (tile if ends else 0)
    shape = (near.shape[1] // 4, columns)
    return pl.pallas_call(
        in_grads_kernel,
        in_specs=[pl.BlockSpec(memory_space=pltpu.SMEM)]
        + [pl.BlockSpec(memory_space=pltpu.VMEM)] * (3 + len(ends)),
        out_specs=[pl.BlockSpec(memory_space=pltpu.VMEM)] * 4,
        out_shape=[jax.ShapeDtypeStruct(shape, bf16)] * 4,
        scratch_shapes=[
            pltpu.VMEM((near.shape[1], columns), bf16),
            pltpu.VMEM((near.shape[1], tile), f32),
        ],
        compiler_params=pltpu.CompilerParams(vmem_limit_bytes=14 * 2**20),
        cost_estimate=pl.CostEstimate(
            flops=4 * near.shape[0] * near.shape[1] * columns,
            bytes_accessed=4 * 2**20,
            transcendentals=0,
        ),
    )(place, near, far, grad_qkv, *ends)


def add_in_kernel(own, lower, upper, opposite, near, far):
    total = sum_of_four([own, lower, upper, opposite]).astype(bf16)
    half = near.shape[0]
    near[...] = total[:half]
    far[...] = total[half:]


def combine_kernel(near_part, arrived, own, x_part, y_part, xy_part):
    rows = own.shape[0]
    own[...] = near_part[:rows] + arrived[:rows].astype(f32)
    for bits, out in ((1, x_part), (2, y_part), (3, xy_part)):
        block = slice(bits * rows, (bits + 1) * rows)
        out[...] = (near_part[block] + arrived[block].astype(f32)).astype(bf16)


def added(own, x_part, y_part, xy_part):
    return (own[...] + x_part[...].astype(f32)) + (
        y_part[...].astype(f32) + xy_part[...].astype(f32)
    )


def close_kernel(kept, own, x_part, y_part, xy_part, hidden, units):
    total = kept[...] + added(own, x_part, y_part, xy_part)
    hidden[...] = total
    units[...] = (total * inverse_rms(total)).astype(bf16)


def close_gain_kernel(kept, own, x_part, y_part, xy_part, gain, hidden, normed):
    total = kept[...] + added(own, x_part, y_part, xy_part)
    hidden[...] = total
    normed[...] = (total * inverse_rms(total) * gain[...]).astype(bf16)


def last_kernel(kept, own, x_part, y_part, xy_part, hidden):
    hidden[...] = (kept[...] + added(own, x_part, y_part, xy_part)).astype(bf16)


def middle_back_kernel(
    upstream, own, x_part, y_part, xy_part, middle, gain, grad_middle, branch, grad_gain
):
    grad_normed = added(own, x_part, y_part, xy_part)
    inverse = inverse_rms(middle[...])
    grad_gain[...] = jnp.sum(grad_normed * middle[...] * inverse, axis=0, keepdims=True)
    total = upstream[...].astype(f32) + unit_norm_back(
        middle[...], inverse, grad_normed * gain[...]
    )
    grad_middle[...] = total
    branch[...] = total.astype(bf16)


def layer_back_kernel(grad_middle, own, x_part, y_part, xy_part, hidden, upstream, low):
    total = grad_middle[...] + unit_norm_back(
        hidden[...], inverse_rms(hidden[...]), added(own, x_part, y_part, xy_part)
    )
    upstream[...] = total
    low[...] = total.astype(bf16)


def pair_kernel(axis, near, arrived, *outs):
    rows = near.shape[0] // len(outs)
    for index, out in enumerate(outs):
        block = slice(index * rows, (index + 1) * rows)
        if axis == 0:
            out[:rows] = near[block]
            out[rows:] = arrived[block]
        else:
            columns = near.shape[1]
            out[:, :columns] = near[block]
            out[:, columns:] = arrived[block]


def unit_kernel(tokens, hidden, units):
    total = tokens[...].astype(f32)
    hidden[...] = total
    units[...] = (total * inverse_rms(total)).astype(bf16)


def finish_in_kernel(place, *refs):
    chips, (attn_in, gains, grad_in, grad_gain, ends) = refs[:8], refs[8:]
    rows = attn_in.shape[1]
    width = tile
    members = attn_in.shape[2] // (3 * width)
    ends[...] = jnp.zeros_like(ends)
    for layer_id in range(2):
        row_dot = jnp.zeros((rows, 1), f32)
        for index in range(members):
            member = place[index]
            chip = chips[4 * layer_id + index % 4]
            half = chip.shape[1] // 2
            total = chip[:, index // 4 * half : (index // 4 + 1) * half].astype(f32)
            if layer_id == 0:
                ends[...] += total[:, 3 * width :]
            for part in range(3):
                block = total[:, part * width : (part + 1) * width]
                columns = pl.ds(pl.multiple_of((part * members + member) * width, width), width)
                grad_in[layer_id, :, columns] = block * gains[layer_id]
                row_dot = row_dot + jnp.sum(
                    block * attn_in[layer_id, :, columns].astype(f32), axis=1, keepdims=True
                )
        grad_gain[layer_id] = jnp.concatenate(
            [row_dot, ends[:, layer_id : layer_id + 1]], axis=1
        )


def sum_of_four(parts):
    return (parts[0][...].astype(f32) + parts[1][...].astype(f32)) + (
        parts[2][...].astype(f32) + parts[3][...].astype(f32)
    )


def finish_ff_kernel(*refs):
    count = (len(refs) - 3) // 2
    sources, grads, held, done = refs[:count], refs[count : count + 2], refs[count + 2 : -1], refs[-1]
    copies = [
        pltpu.make_async_copy(source, target, done.at[index])
        for index, (source, target) in enumerate(zip(sources, held))
    ]
    for copy in copies:
        copy.start()
    for copy in copies:
        copy.wait()
    refs = held
    columns = grads[0].shape[2]
    for layer_id in range(grads[0].shape[0]):
        parts = refs[5 * layer_id : 5 * layer_id + 5]
        for side, out in enumerate(grads):
            halves = [part.at[:, side * columns : (side + 1) * columns] for part in parts[:3]]
            out[layer_id] = sum_of_four(halves + [parts[3 + side]])


def finish_ff(grads, shape):
    return pl.pallas_call(
        finish_ff_kernel,
        in_specs=[pl.BlockSpec(memory_space=pl.ANY)] * len(grads),
        out_specs=[pl.BlockSpec(memory_space=pltpu.VMEM)] * 2,
        out_shape=[jax.ShapeDtypeStruct(shape, f32)] * 2,
        scratch_shapes=[pltpu.VMEM(grad.shape, bf16) for grad in grads]
        + [pltpu.SemaphoreType.DMA((len(grads),))],
        compiler_params=pltpu.CompilerParams(vmem_limit_bytes=14 * 2**20),
    )(*grads)


def add_out_kernel(place, *refs):
    parts, (own, other) = refs[:-2], refs[-2:]
    for layer_id in range(own.shape[0]):
        total = parts[2 * layer_id][...].astype(f32) + parts[2 * layer_id + 1][...].astype(f32)
        rows = total.shape[0] // 2
        second = place[0] % 2 == 1
        own[layer_id] = jnp.where(second, total[rows:], total[:rows])
        other[layer_id] = jnp.where(second, total[:rows], total[rows:]).astype(bf16)


def finish_out_kernel(own, arrived, out):
    out[...] = own[...] + arrived[...].astype(f32)


def inverse_rms(hidden):
    return lax.rsqrt(jnp.mean(hidden * hidden, axis=-1, keepdims=True) + epsilon)


def prepare(bias_table, first_head, heads_dev):
    table = lax.dynamic_slice_in_dim(bias_table, first_head, heads_dev, 1)
    (near,) = call(near_kernel, [((heads_dev, tile, 3 * tile), f32)], table, smem=1)
    return table, near


def bucket_grads(first_lane, grads, bucket_count):
    (total,) = call(bucket_kernel, [((bucket_count, tile), f32)], first_lane, *grads, smem=1)
    return total


def gelu_parts(pre_act):
    cumulative = 0.5 * (1.0 + lax.erf(pre_act * np.float32(0.5**0.5)))
    slope = cumulative + pre_act * jnp.exp(-0.5 * pre_act * pre_act) * np.float32(
        (2 * np.pi) ** -0.5
    )
    return (pre_act * cumulative).astype(bf16), slope


def unit_norm_back(hidden, inverse, grad_unit):
    unit = hidden * inverse
    return inverse * (grad_unit - unit * jnp.mean(grad_unit * unit, axis=-1, keepdims=True))


def gather_rows(block, axes):
    return lax.all_gather(block, axes, axis=0, tiled=True)


def toggle(array, axis, bits):
    return lax.ppermute(array, axis, [(i, i ^ bits) for i in range(lax.axis_size(axis))])


def shift(array, by):
    planes = lax.axis_size("z")
    return lax.ppermute(array, "z", [(i, (i + by) % planes) for i in range(planes)])


def plane_gather(block, *holds):
    near = jnp.concatenate([block] + [toggle(block, "head", bits) for bits in (1, 2, 3)])
    near, *holds = tie(near, *holds)
    return (near, toggle(near, "core", 1), *holds)


def plane_scatter(near_part, far_part):
    rows, columns = near_part.shape[0] // 4, near_part.shape[1]
    own, *others = call(
        combine_kernel,
        [((rows, columns), f32)] + [((rows, columns), bf16)] * 3,
        near_part,
        toggle(far_part, "core", 1),
    )
    shares = [own] + [toggle(other, "head", bits) for bits, other in zip((1, 2, 3), others)]
    return shares, own


def tie(*arrays):
    return lax.optimization_barrier(arrays)


def after(array, other):
    return lax.optimization_barrier((array, other))[0]


def scatter_sum(partial, axes, members):
    blocks = partial.astype(bf16).reshape(members, -1, partial.shape[1])
    return jnp.sum(lax.all_to_all(blocks, axes, 0, 0, tiled=True).astype(f32), axis=0)


def local_general(tokens, doc_start, bias_table, attn_in, attn_out, ff_in, ff_out, gains, cotangent):
    heads_n, z_n, core_n = (lax.axis_size(axis) for axis in everyone)
    devices = heads_n * z_n * core_n
    group, spare = ("z", "core"), "head"
    ff_group, ff_spare, ff_members = ("head", "core"), "z", heads_n * core_n
    blocks = z_n * core_n
    block_rows, model_width = tokens.shape[1:]
    layer_count, weight_rows = attn_in.shape[:2]
    length = block_rows * blocks
    heads_all = bias_table.shape[1]
    member = lax.axis_index("z") * core_n + lax.axis_index("core")
    heads_dev = max(1, heads_all // blocks)
    head_groups = heads_all // heads_dev
    split = blocks // head_groups
    head_group, query_part = member // split, member % split
    query_rows = length // split
    width = heads_dev * head_dim
    first = (query_part * (query_rows // tile)).astype(jnp.int32).reshape(1)
    place = jnp.arange(length // tile, dtype=jnp.int32)
    out_row = head_group * width

    def swap(array):
        return lax.all_to_all(array, everyone, 0, 0, tiled=True)

    starts = jnp.broadcast_to(
        doc_start.astype(f32)[:, None], (heads_n, blocks, block_rows)
    ).reshape(devices, block_rows)
    ff_gains = gains[:, :, 1].astype(f32).reshape(1, -1)
    small = swap(
        jnp.concatenate(
            [starts, jnp.broadcast_to(ff_gains, (devices, layer_count * weight_rows))], axis=1
        )
    )
    doc_row = small[:blocks, :block_rows].reshape(1, length)
    doc_col = lax.dynamic_slice_in_dim(
        doc_row.reshape(length, 1), query_part * query_rows, query_rows, 0
    )
    gain_ff = jnp.transpose(
        small[:, block_rows:].reshape(devices, layer_count, weight_rows), (1, 0, 2)
    ).reshape(layer_count, 1, model_width)
    table, near = prepare(bias_table, head_group * heads_dev, heads_dev)

    gain_attn = gains[:, :, 0].astype(f32)[:, :, None]
    own_in = attn_in.astype(f32)

    def fetch_in(layer_id):
        scaled = (own_in[layer_id] * gain_attn[layer_id]).astype(bf16)
        columns = jnp.transpose(
            scaled.reshape(weight_rows, 3, head_groups, width), (2, 0, 1, 3)
        ).reshape(head_groups, weight_rows, 3 * width)
        columns = jnp.repeat(columns, split, axis=0)
        columns = jnp.broadcast_to(columns[None], (heads_n, *columns.shape))
        return swap(columns.reshape(devices, weight_rows, 3 * width)).reshape(
            model_width, 3 * width
        )

    def fetch_ff(layer_id):
        pair = jnp.concatenate([ff_in[layer_id], ff_out[layer_id]], axis=1)
        pair = gather_rows(pair, ff_spare)
        return pair[:, :model_width], pair[:, model_width:]

    hidden, upstream = tokens[0].astype(f32), cotangent[0]
    weights_in = [fetch_in(layer_id) for layer_id in range(layer_count)]
    weights_out = lax.dynamic_slice_in_dim(
        lax.all_gather(attn_out, everyone, axis=1, tiled=True), out_row, width, 1
    )
    weights_ff = [fetch_ff(layer_id) for layer_id in range(layer_count)]

    records = []
    for layer_id in range(layer_count):
        w_in, w_out, (w_up, w_down) = (
            weights_in[layer_id], weights_out[layer_id], weights_ff[layer_id],
        )
        inverse = inverse_rms(hidden)
        units = gather_rows((hidden * inverse).astype(bf16), group)
        qkv = jnp.dot(units, w_in, preferred_element_type=f32).astype(bf16)
        attended, _, stats = attention(
            qkv, doc_row, doc_col, first, place, table, near, query_rows
        )
        mixed = jnp.dot(attended, w_out, preferred_element_type=f32)
        if split > 1:
            mixed = lax.dynamic_update_slice_in_dim(
                jnp.zeros((length, model_width), f32), mixed, query_part * query_rows, 0
            )
        middle = hidden + scatter_sum(mixed, group, blocks)
        inverse_ff = inverse_rms(middle)
        normed_ff = gather_rows((middle * inverse_ff * gain_ff[layer_id]).astype(bf16), ff_group)
        activated, slope = gelu_parts(contract(normed_ff, w_up, 1, 1))
        ff_result = jnp.dot(activated, w_down, preferred_element_type=f32)
        records.append(
            (hidden, inverse, units, qkv, attended, stats, middle, inverse_ff, normed_ff,
             activated, slope)
        )
        hidden = middle + scatter_sum(ff_result, ff_group, ff_members)
    output = hidden

    grads_ff, grads_in, grads_out, grads_gain_ff, grads_table = (
        [None] * layer_count for _ in range(5)
    )
    for layer_id in reversed(range(layer_count)):
        w_in, w_out, (w_up, w_down) = (
            weights_in[layer_id], weights_out[layer_id], weights_ff[layer_id],
        )
        (hidden, inverse, units, qkv, attended, stats, middle, inverse_ff, normed_ff,
         activated, slope) = records[layer_id]
        grad_low = gather_rows(upstream.astype(bf16), ff_group)
        grad_pre = (contract(grad_low, w_down, 1, 1) * slope).astype(bf16)
        grad_normed = scatter_sum(
            jnp.dot(grad_pre, w_up, preferred_element_type=f32), ff_group, ff_members
        )
        grad_pair = jnp.concatenate(
            [contract(grad_pre, normed_ff, 0, 0), contract(activated, grad_low, 0, 0)], axis=1
        ).astype(bf16)
        grads_ff[layer_id] = lax.psum_scatter(
            grad_pair, ff_spare, scatter_dimension=0, tiled=True
        ).astype(f32)
        grads_gain_ff[layer_id] = jnp.sum(grad_normed * middle * inverse_ff, axis=0)
        grad_middle = upstream + unit_norm_back(
            middle, inverse_ff, grad_normed * gain_ff[layer_id]
        )
        branch = gather_rows(grad_middle.astype(bf16), group)
        if split > 1:
            branch = lax.dynamic_slice_in_dim(branch, query_part * query_rows, query_rows, 0)
        grad_attended = contract(branch, w_out, 1, 1).astype(bf16)
        grad_qkv, grad_near, grad_far = attention_back(
            qkv, doc_row, doc_col, attended, grad_attended, stats, first, place, table, near, split
        )
        grads_table[layer_id] = (grad_near, grad_far)
        grad_units = scatter_sum(contract(grad_qkv, w_in, 1, 1), group, blocks)
        upstream = grad_middle + unit_norm_back(hidden, inverse, grad_units)
        grad_out = lax.dynamic_update_slice_in_dim(
            jnp.zeros((model_width, model_width), bf16),
            contract(attended, branch, 0, 0).astype(bf16),
            out_row,
            0,
        )
        grads_out[layer_id] = lax.psum_scatter(
            grad_out, everyone, scatter_dimension=0, tiled=True
        ).astype(f32)
        grads_in[layer_id] = contract(units, grad_qkv, 0, 0).astype(bf16)

    bucket_count = table.shape[0]
    grad_table = sum(
        bucket_grads(jnp.zeros((1,), jnp.int32), entry, bucket_count) for entry in grads_table
    )[:, :heads_dev]
    grad_table = lax.dynamic_update_slice_in_dim(
        jnp.zeros((bucket_count, heads_all), f32), grad_table, head_group * heads_dev, 1
    )
    grad_table = jnp.transpose(
        grad_table.reshape(blocks, bucket_count // blocks, heads_n, heads_all // heads_n),
        (2, 0, 1, 3),
    ).reshape(devices, -1)
    grad_gain_ff = jnp.transpose(
        jnp.stack(grads_gain_ff).reshape(layer_count, devices, weight_rows), (1, 0, 2)
    ).reshape(devices, -1)
    ends = jnp.sum(swap(jnp.concatenate([grad_gain_ff, grad_table], axis=1)), axis=0)
    grad_gain_ff = ends[: layer_count * weight_rows].reshape(layer_count, weight_rows)
    grad_bias_table = ends[layer_count * weight_rows :].reshape(
        bucket_count // blocks, heads_all // heads_n
    )
    grads_attn_in, grads_gains = [], []
    for layer_id in range(layer_count):
        parts = swap(grads_in[layer_id].reshape(devices, weight_rows, 3 * width)).astype(f32)
        parts = jnp.sum(parts.reshape(heads_n, blocks, weight_rows, 3 * width), axis=0)
        parts = jnp.sum(parts.reshape(head_groups, split, weight_rows, 3, width), axis=1)
        unit_grad = jnp.transpose(parts, (1, 2, 0, 3)).reshape(weight_rows, 3 * model_width)
        grads_attn_in.append(unit_grad * gain_attn[layer_id])
        grads_gains.append(
            jnp.stack(
                [jnp.sum(unit_grad * own_in[layer_id], axis=1), grad_gain_ff[layer_id]], axis=1
            )
        )
    return (
        output[None],
        upstream[None],
        jnp.stack(grads_attn_in),
        jnp.stack(grads_out),
        jnp.stack([entry[:, :model_width] for entry in grads_ff]),
        jnp.stack([entry[:, model_width:] for entry in grads_ff]),
        jnp.stack(grads_gains),
        grad_bias_table,
    )


def local_plane(tokens, doc_start, bias_table, attn_in, attn_out, ff_in, ff_out, gains, cotangent):
    heads_n, z_n, core_n = (lax.axis_size(axis) for axis in everyone)
    devices = heads_n * z_n * core_n
    at_head, at_z, at_core = (lax.axis_index(axis) for axis in everyone)
    members = heads_n * core_n
    block_rows, model_width = tokens.shape[1:]
    layer_count, weight_rows = attn_in.shape[:2]
    length = block_rows * members
    heads_all = bias_table.shape[1]
    heads_dev = heads_all // members
    width = heads_dev * head_dim
    member = at_head * core_n + at_core
    everywhere = [(h, z, c) for h in range(heads_n) for z in range(z_n) for c in range(core_n)]

    def swapped(bits):
        return bits % 2 * 2 + bits // 2

    def device(h, z, c):
        return (h * z_n + z) * core_n + c

    turn = [(device(h, z, c), device(h ^ swapped(z), h, c)) for h, z, c in everywhere]
    plane_turn = [(device(h, z, c), device(h ^ swapped(z), z, c)) for h, z, c in everywhere]
    line_turn = [(device(h, z, c), device(h, h ^ swapped(z), c)) for h, z, c in everywhere]
    line_back = [(target, source) for source, target in line_turn]
    place = jnp.stack(
        [
            (at_head ^ bits) * core_n + (at_core ^ other)
            for other in range(core_n)
            for bits in range(heads_n)
        ]
        + [at_z]
        + [
            swapped(at_head ^ bits ^ at_z) * core_n + (at_core ^ other)
            for other in range(core_n)
            for bits in range(heads_n)
        ]
    ).astype(jnp.int32)

    def relay(array):
        return lax.ppermute(array, everyone, turn)

    def turn_in_plane(array):
        return lax.ppermute(array, everyone, plane_turn)

    def turn_in_line(array, turns):
        return lax.ppermute(array, everyone, turns)

    def swap(array):
        return lax.all_to_all(array, everyone, 0, 0, tiled=True)

    row_shape = (block_rows, model_width)
    gain_attn = gains[:, :, 0].astype(f32)[:, :, None]
    near_share, far_share = call(
        share_in_kernel,
        [((members // 2 * layer_count * weight_rows, 3 * width), bf16)] * 2,
        place,
        attn_in,
        gain_attn,
        smem=1,
    )

    half_turns = [
        [
            (z * core_n + c, (2 * c + (a ^ z % 2)) * core_n + z // 2)
            for z in range(z_n)
            for c in range(core_n)
        ]
        for a in range(2)
    ]

    def fetch_out(layer_id, hold):
        own = attn_out[layer_id]
        other = toggle(own, "core", 1)
        head = jnp.where(
            at_core == 0, jnp.concatenate([own, other]), jnp.concatenate([other, own])
        )
        head = after(head, hold)
        return [
            lax.ppermute(head, ("z", "core"), [(holder, user) for user, holder in turns])
            for turns in half_turns
        ]

    def owners_halves(halves):
        return [
            lax.ppermute(half, ("z", "core"), turns) for half, turns in zip(halves, half_turns)
        ]

    def pair_chips(near, arrived, axis):
        rows, columns = near.shape[0] // 4, near.shape[1]
        shape = (2 * rows, columns) if axis == 0 else (rows, 2 * columns)
        return call(functools.partial(pair_kernel, axis), [(shape, bf16)] * 4, near, arrived)

    def share_chips(blocks):
        return [blocks[0]] + [toggle(blocks[bits], "head", bits) for bits in (1, 2, 3)]

    units_shape = [(row_shape, f32), (row_shape, bf16)]

    starts = jnp.broadcast_to(
        doc_start.astype(f32)[None, :, None], (heads_n, z_n, core_n, block_rows)
    )
    ff_gains = gains[:, :, 1].astype(f32).reshape(1, -1)
    small = jnp.concatenate(
        [
            starts.reshape(devices, block_rows),
            jnp.broadcast_to(ff_gains, (devices, layer_count * weight_rows)),
        ],
        axis=1,
    )
    table, strip = prepare(bias_table, member * heads_dev, heads_dev)
    hidden, strip = tie(relay(tokens[0]), strip)
    hidden, shares, cotangent_low, halves, small = tie(
        hidden,
        share_chips(pair_chips(near_share, toggle(far_share, "core", 1), 0)),
        turn_in_plane(after(cotangent[0].astype(bf16), near_share)),
        fetch_out(0, near_share),
        swap(after(small, near_share)),
    )
    hidden, unit_rows = call(unit_kernel, units_shape, hidden)
    doc_row = small[:members, :block_rows].reshape(2, 2, core_n, block_rows)
    at_block = swapped(at_head ^ at_z)
    for axis, bit in ((0, at_block // 2), (1, at_block % 2), (2, at_core)):
        doc_row = jnp.where(bit == 1, jnp.flip(doc_row, axis), doc_row)
    doc_row = jnp.transpose(doc_row, (2, 1, 0, 3)).reshape(1, length)
    doc_col = doc_row.reshape(length, 1)
    gain_ff = jnp.transpose(
        small[:, block_rows:].reshape(devices, layer_count, weight_rows), (1, 0, 2)
    ).reshape(layer_count, 1, model_width)

    def round_planes(array, by, hold):
        return shift(after(array, hold), by)

    ff_pairs = [
        jnp.concatenate([ff_in[layer_id], ff_out[layer_id]], axis=1) for layer_id in range(layer_count)
    ]

    def ff_both(kernel, row_operands, pair, columns):
        return zip(
            *(
                by_rows(
                    kernel,
                    256,
                    operands,
                    [pair],
                    [(pair.shape[0], bf16)] * columns + [(model_width, kind)],
                )
                for operands, kind in zip(zip(*row_operands), (f32, bf16))
            )
        )

    def ff_forward(normed, *parts):
        units = 4 * parts[0].shape[0]
        outs = [(units, bf16), (units, bf16)]
        *near, pair = by_rows(
            ff_first_kernel,
            256,
            [normed[0]],
            parts,
            outs + [(model_width, f32)],
            [(units, 2 * model_width)],
        )
        far = by_rows(ff_kernel, 256, [normed[1]], [pair], outs + [(model_width, bf16)])
        return pair, *zip(near, far)

    def ff_backward(low, slopes, pair):
        return ff_both(ff_back_kernel, [low, slopes], pair, 1)

    def assemble_in(share, lower, upper, opposite):
        return call(
            assemble_in_kernel,
            [((model_width, 3 * width), bf16)],
            place,
            share,
            lower,
            upper,
            opposite,
            smem=1,
        )[0]

    share, later_share = call(
        join_kernel, [((members * weight_rows, 3 * width), bf16)] * layer_count, *shares
    )
    near, far, lower, upper, opposite, doc_row, doc_col, gain_ff, *ff_pairs = plane_gather(
        unit_rows,
        shift(share, 1),
        shift(share, -1),
        shift(share, 2),
        doc_row,
        doc_col,
        gain_ff,
        *ff_pairs,
    )
    w_in = assemble_in(share, lower, upper, opposite)
    units = (near, far)
    w_out, qkv, attended, stats, *parts = plane_attention(
        *units, w_in, halves, doc_row, doc_col, place, table, strip
    )
    parts, lower, upper = tie(
        parts, round_planes(ff_pairs[0], 1, near), round_planes(ff_pairs[0], -1, near)
    )
    parts, own = plane_scatter(*parts)
    parts, opposite_in = tie(parts, round_planes(ff_in[0], 2, own))
    middle, normed_rows = call(close_gain_kernel, units_shape, hidden, *parts, gain_ff[0])
    *normed, opposite_out = plane_gather(normed_rows, round_planes(ff_out[0], 2, normed_rows))
    pair, acts, slopes, parts = ff_forward(
        normed, ff_pairs[0], lower, upper, opposite_in, opposite_out
    )
    records = [
        (hidden, units, w_in, w_out, pair, qkv, attended, stats, middle, normed, acts, slopes)
    ]
    halves_1 = fetch_out(1, normed[0])
    parts, lower, upper, first_half = tie(
        parts,
        round_planes(later_share, 1, normed[0]),
        round_planes(later_share, -1, normed[0]),
        halves_1[0],
    )
    parts, own = plane_scatter(*parts)
    parts, opposite, upstream = tie(
        parts, round_planes(later_share, 2, own), turn_in_line(after(cotangent_low, own), line_turn)
    )
    shares = [later_share, lower, upper, opposite]
    hidden, unit_rows = call(close_kernel, units_shape, middle, *parts)

    near, far, lower, second_half = plane_gather(
        unit_rows, round_planes(ff_pairs[1], 1, unit_rows), halves_1[1]
    )
    halves = [first_half, second_half]
    units = (near, far)
    w_in = assemble_in(*shares)
    w_out, qkv, attended, stats, *parts = plane_attention(
        *units, w_in, halves, doc_row, doc_col, place, table, strip
    )
    low = plane_gather(after(upstream, far))
    parts, near_low, upper = tie(parts, low[0], round_planes(ff_pairs[1], -1, far))
    low = (near_low, low[1])
    parts, own = plane_scatter(*parts)
    parts, opposite_in = tie(parts, round_planes(ff_in[1], 2, own))
    middle, normed_rows = call(close_gain_kernel, units_shape, hidden, *parts, gain_ff[1])
    *normed, opposite_out = plane_gather(normed_rows, round_planes(ff_out[1], 2, normed_rows))
    pair, acts, slopes, last_parts = ff_forward(
        normed, ff_pairs[1], lower, upper, opposite_in, opposite_out
    )
    records.append(
        (hidden, units, w_in, w_out, pair, qkv, attended, stats, middle, normed, acts, slopes)
    )

    def back_to_middle(parts, upstream, middle, gain):
        return call(
            middle_back_kernel, units_shape + [((1, model_width), f32)], upstream, *parts, middle, gain
        )

    def attention_grads(record, branch):
        _, _, w_in, w_out, _, qkv, attended, stats, *_ = record
        grad_qkv, grad_near, grad_far, near_part, far_part, *halves = plane_attention_back(
            qkv, doc_row, doc_col, attended, stats, *branch, w_in, w_out, place, table, strip
        )
        return grad_qkv, (grad_near, grad_far), (near_part, far_part), halves

    def table_grads(near_and_far):
        return bucket_grads(at_core.reshape(1) * heads_dev + 8, near_and_far, table.shape[0])

    record = records[1]
    hidden, units, _, _, pair, *_, middle, normed, acts, slopes = record
    pres, parts = ff_backward(low, slopes, pair)
    parts, own = plane_scatter(*parts)
    planes = ff_grads(after(pres, own), acts, normed, low)
    parts, ff_lower = tie(parts, shift(planes[1], -1))
    last_parts, _ = plane_scatter(*after(last_parts, parts))
    grad_middle, branch_rows, gain_1 = back_to_middle(parts, upstream, middle, gain_ff[1])
    *branch, ff_upper = plane_gather(branch_rows, round_planes(planes[2], 1, branch_rows))
    grad_qkv, strips_1, parts, halves_1 = attention_grads(record, branch)
    parts, last_parts, opposite_up = tie(
        parts, last_parts, round_planes(planes[3], 2, branch[1])
    )
    parts, own = plane_scatter(*parts)
    parts, opposite_down, output = tie(
        parts,
        round_planes(planes[4], 2, own),
        call(last_kernel, [(row_shape, bf16)], middle, *after(last_parts, own))[0],
    )
    grads_ff = [planes[0], ff_lower, ff_upper, opposite_up, opposite_down]
    upstream, low_rows = call(layer_back_kernel, units_shape, grad_middle, *parts, hidden)

    record = records[0]
    hidden, units, _, _, pair, *_, middle, normed, acts, slopes = record
    grad_in = in_grads(place, *records[1][1], after(grad_qkv, low_rows))
    *low, in_opposite, in_upper, table_1 = plane_gather(
        low_rows, shift(grad_in[3], 2), shift(grad_in[2], 1), table_grads(after(strips_1, low_rows))
    )
    pres, parts = ff_backward(low, slopes, pair)
    parts, in_lower = tie(parts, round_planes(grad_in[1], -1, low[0]))
    parts, own = plane_scatter(*parts)
    planes = ff_grads(after(pres, own), acts, normed, low)
    near_in, far_in = call(
        add_in_kernel,
        [((members // 2 * weight_rows, 3 * width), bf16)] * 2,
        *after([grad_in[0], in_lower, in_upper, in_opposite], own),
    )
    parts, ff_lower, first_half, arrived = tie(
        parts,
        shift(planes[1], -1),
        owners_halves(after(halves_1, own))[0],
        toggle(far_in, "core", 1),
    )
    grad_middle, branch_rows, gain_0 = back_to_middle(parts, upstream, middle, gain_ff[0])
    *branch, ff_upper, second_half, shares_1 = plane_gather(
        branch_rows,
        round_planes(planes[2], 1, branch_rows),
        owners_halves(after(halves_1, branch_rows))[1],
        pair_chips(near_in, after(arrived, branch_rows), 1),
    )
    halves_1 = [first_half, second_half]
    grad_qkv, strips_0, parts, halves_0 = attention_grads(record, branch)
    parts, shares_1, output, opposite_up = tie(
        parts,
        share_chips(after(shares_1, branch[1])), turn_in_line(after(output, branch[1]), line_back), round_planes(planes[3], 2, branch[1])
    )
    parts, own = plane_scatter(*parts)
    table_0 = table_grads(after(strips_0, own))
    grad_in = in_grads(
        place, *units, after(grad_qkv, own), gain_0, gain_1, table_0, table_1
    )
    parts, in_opposite, halves_0 = tie(
        parts, shift(grad_in[3], 2), owners_halves(after(halves_0, own))
    )
    upstream, low_rows = call(layer_back_kernel, units_shape, grad_middle, *parts, hidden)
    in_lower = round_planes(grad_in[1], -1, low_rows)
    in_upper = round_planes(grad_in[2], 1, low_rows)
    line = turn_in_line(low_rows, line_back)
    near_in, far_in = call(
        add_in_kernel,
        [((members // 2 * weight_rows, 3 * width + tile), bf16)] * 2,
        grad_in[0],
        in_lower,
        in_upper,
        in_opposite,
    )
    arrived = toggle(far_in, "core", 1)
    shares_0 = share_chips(pair_chips(near_in, arrived, 1))
    opposite_down = round_planes(planes[4], 2, near_in)
    grad_tokens = turn_in_plane(line)
    output = turn_in_plane(after(output, arrived)).astype(f32)
    grads_ff = [planes[0], ff_lower, ff_upper, opposite_up, opposite_down] + grads_ff
    grad_up, grad_down = finish_ff(after(grads_ff, arrived), ff_in.shape)
    own_out, other_out = call(
        add_out_kernel,
        [(attn_out.shape, f32), (attn_out.shape, bf16)],
        place,
        *after(halves_0 + halves_1, near_in),
        smem=1,
    )
    (grad_attn_out,) = call(
        finish_out_kernel, [(attn_out.shape, f32)], own_out, toggle(other_out, "core", 1)
    )
    own_buckets = table.shape[0] // (z_n * core_n)
    grad_attn_in, grad_gains, ends = call(
        finish_in_kernel,
        [(attn_in.shape, f32), (gains.shape, f32), ((weight_rows, tile), f32)],
        place,
        *shares_0,
        *shares_1,
        attn_in,
        gain_attn,
        smem=1,
    )
    return (
        output[None],
        grad_tokens.astype(f32)[None],
        grad_attn_in,
        grad_attn_out,
        grad_up,
        grad_down,
        grad_gains,
        ends[:own_buckets, 8 : 8 + heads_all // heads_n],
    )


def solution(mesh):
    sizes = dict(mesh.shape)
    cores = 2
    fine = Mesh(
        mesh.devices.reshape(sizes["head"], sizes["blk"] // cores, cores), everyone
    )
    blk = ("z", "core")
    in_specs = (
        P("head", blk, None),
        P(None, blk),
        P(),
        P(None, everyone, None),
        P(None, everyone, None),
        P(None, everyone, None),
        P(None, everyone, None),
        P(None, everyone, None),
        P("head", blk, None),
    )
    out_specs = (
        P("head", blk, None),
        P("head", blk, None),
        P(None, everyone, None),
        P(None, everyone, None),
        P(None, everyone, None),
        P(None, everyone, None),
        P(None, everyone, None),
        P(blk, "head"),
    )
    plane = sizes["head"] == 4 and sizes["blk"] == 8
    local = local_plane if plane else local_general
    return jax.shard_map(local, mesh=fine, in_specs=in_specs, out_specs=out_specs, check_vma=False)
```

```python
import functools

import jax
import jax.numpy as jnp
import numpy as np
from jax import lax
from jax.experimental import pallas as pl
from jax.experimental.pallas import tpu as pltpu
from jax.sharding import Mesh
from jax.sharding import PartitionSpec as P

bounds = (1, 2, 3, 4, 5, 6, 7, 8, 12, 16, 23, 32, 46, 64, 91)
epsilon = 1e-06
masked = -1e30
score_scale = 0.125
head_dim = 64
tile = 128
everyone = ("head", "z", "core")
bf16 = jnp.bfloat16
f32 = jnp.float32


def contract(lhs, rhs, lhs_dim, rhs_dim):
    return lax.dot_general(
        lhs, rhs, (((lhs_dim,), (rhs_dim,)), ((), ())), preferred_element_type=f32
    )


def near_buckets(shape):
    offsets = (
        lax.broadcasted_iota(jnp.int32, shape, 1) - tile - lax.broadcasted_iota(jnp.int32, shape, 0)
    )
    distance = jnp.abs(offsets)
    bucket = jnp.where(offsets > 0, 16, 0)
    for boundary in bounds:
        bucket = bucket + jnp.where(distance >= boundary, 1, 0)
    return bucket


def near_kernel(table, near):
    bucket = near_buckets(near.shape[1:])
    for head in range(near.shape[0]):
        values = jnp.zeros(near.shape[1:], f32)
        for bucket_id in range(table.shape[0]):
            values = jnp.where(bucket == bucket_id, table[bucket_id, head], values)
        near[head] = values


def bucket_kernel(first_lane, near, far, out):
    bucket = near_buckets(near.shape[1:])
    rows = lax.broadcasted_iota(jnp.int32, out.shape, 0)
    lanes = lax.broadcasted_iota(jnp.int32, out.shape, 1)
    total = jnp.zeros(out.shape, f32)
    for head in range(near.shape[0]):
        strip = near[head]
        for bucket_id in range(out.shape[0]):
            value = jnp.sum(jnp.where(bucket == bucket_id, strip, 0.0), axis=0, keepdims=True)
            value = jnp.sum(value, axis=1, keepdims=True)
            if bucket_id in (15, 31):
                value = value + far[head, bucket_id // 16, :1, :1]
            total = jnp.where((rows == bucket_id) & (lanes == head + first_lane[0]), value, total)
    out[...] = total


def fill_band(band, table, near, heads_dev, length):
    for head in range(heads_dev):
        band[head, :, : length - tile] = jnp.full((tile, length - tile), table[15, head], f32)
        band[head, :, length - tile : length + 2 * tile] = near[head]
        band[head, :, length + 2 * tile :] = jnp.full(
            (tile, length - 2 * tile), table[31, head], f32
        )


def band_starts(place, at, length, skip=0):
    return [
        pl.multiple_of(length + (place[skip + block] - place[skip + at]) * tile, tile)
        for block in range(length // tile)
    ]


def attention_kernel(
    heads_dev, length, first, place, table, near, qkv, doc_row, doc_col, out, local, stats, band
):
    step = pl.program_id(0)
    width = heads_dev * head_dim

    @pl.when(step == 0)
    def _():
        fill_band(band, table, near, heads_dev, length)

    row = pl.multiple_of((first[0] + step) * tile, tile)
    out_row = pl.multiple_of((place[first[0] + step] - first[0]) * tile, tile)
    starts = band_starts(place, first[0] + step, length)
    same_doc = doc_col[...] == doc_row[...]
    queries = qkv[pl.ds(row, tile), :width] * bf16(score_scale)
    lanes = lax.broadcasted_iota(jnp.int32, (tile, tile), 1)
    collected = jnp.zeros((tile, tile), f32)
    for head in range(heads_dev):
        own = slice(head * head_dim, (head + 1) * head_dim)
        keys = qkv[:, width + own.start : width + own.stop]
        values = qkv[:, 2 * width + own.start : 2 * width + own.stop]
        scores = contract(queries[:, own], keys, 1, 1)
        scores = scores + jnp.concatenate(
            [band[head, :, pl.ds(start, tile)] for start in starts], axis=1
        )
        scores = jnp.where(same_doc, scores, masked)
        peak = jnp.max(scores, axis=1, keepdims=True)
        weights = jnp.exp(scores - peak)
        total = jnp.sum(weights, axis=1, keepdims=True)
        mixed = contract(weights.astype(bf16), values, 1, 0) / total
        out[pl.ds(out_row, tile), own] = mixed.astype(bf16)
        local[:, own] = mixed.astype(bf16)
        collected = jnp.where(lanes == head, peak + jnp.log(total), collected)
    stats[...] = collected


def attention_back_kernel(
    heads_dev, length, split, first, place, table, near, qkv, doc_row, doc_col, attended, grad_out, stats,
    grad_qkv, grad_near, grad_far, band, grad_band, grad_keys, grad_values,
):
    step = pl.program_id(0)
    width = heads_dev * head_dim

    @pl.when(step == 0)
    def _():
        fill_band(band, table, near, heads_dev, length)
        grad_band[...] = jnp.zeros_like(grad_band)
        grad_keys[...] = jnp.zeros_like(grad_keys)
        grad_values[...] = jnp.zeros_like(grad_values)
        if split > 1:
            grad_qkv[...] = jnp.zeros_like(grad_qkv)

    row = pl.multiple_of((first[0] + step) * tile, tile)
    out_row = pl.multiple_of((place[first[0] + step] - first[0]) * tile, tile)
    starts = band_starts(place, first[0] + step, length)
    same_doc = doc_col[...] == doc_row[...]
    at_step = pl.multiple_of(step * tile, tile)
    queries = qkv[pl.ds(row, tile), :width] * bf16(score_scale)
    for head in range(heads_dev):
        own = slice(head * head_dim, (head + 1) * head_dim)
        keys = qkv[:, width + own.start : width + own.stop]
        values = qkv[:, 2 * width + own.start : 2 * width + own.stop]
        upstream = grad_out[pl.ds(out_row, tile), own]
        scores = contract(queries[:, own], keys, 1, 1) + jnp.concatenate(
            [band[head, :, pl.ds(start, tile)] for start in starts], axis=1
        )
        scores = jnp.where(same_doc, scores, masked)
        weights = jnp.exp(scores - stats[:, head : head + 1])
        delta = jnp.sum(
            upstream.astype(f32) * attended[pl.ds(at_step, tile), own].astype(f32),
            axis=1,
            keepdims=True,
        )
        grad_scores = weights * (contract(upstream, values, 1, 1) - delta)
        for block, start in enumerate(starts):
            grad_band[head, :, pl.ds(start, tile)] += grad_scores[
                :, block * tile : (block + 1) * tile
            ]
        grad_low = grad_scores.astype(bf16)
        grad_values[:, own] += contract(weights.astype(bf16), upstream, 0, 0)
        grad_keys[:, own] += contract(grad_low, queries[:, own], 0, 0)
        grad_qkv[pl.ds(row, tile), own] = (
            contract(grad_low, keys, 1, 0) * score_scale
        ).astype(bf16)

    @pl.when(step == pl.num_programs(0) - 1)
    def _():
        grad_qkv[:, width : 2 * width] = grad_keys[...].astype(bf16)
        grad_qkv[:, 2 * width :] = grad_values[...].astype(bf16)
        for head in range(heads_dev):
            grad_near[head] = grad_band[head, :, length - tile : length + 2 * tile]
            grad_far[head, 0] = jnp.full(
                (8, tile), jnp.sum(grad_band[head, :, : length - tile]), f32
            )
            grad_far[head, 1] = jnp.full(
                (8, tile), jnp.sum(grad_band[head, :, length + 2 * tile :]), f32
            )


def whole(shape):
    return pl.BlockSpec(shape, lambda step: (0,) * len(shape), pipeline_mode=pl.Buffered(1))


def attention(qkv, doc_row, doc_col, first, place, table, near, rows):
    length = qkv.shape[0]
    heads_dev = table.shape[1]
    width = heads_dev * head_dim
    return pl.pallas_call(
        functools.partial(attention_kernel, heads_dev, length),
        grid=(rows // tile,),
        in_specs=[
            pl.BlockSpec(memory_space=pltpu.SMEM),
            pl.BlockSpec(memory_space=pltpu.SMEM),
            pl.BlockSpec(memory_space=pltpu.SMEM),
            whole(near.shape),
            whole(qkv.shape),
            whole(doc_row.shape),
            pl.BlockSpec((tile, 1), lambda step: (step, 0)),
        ],
        out_specs=[
            whole((rows, width)),
            pl.BlockSpec((tile, width), lambda step: (step, 0)),
            pl.BlockSpec((tile, tile), lambda step: (step, 0)),
        ],
        out_shape=[
            jax.ShapeDtypeStruct((rows, width), bf16),
            jax.ShapeDtypeStruct((rows, width), bf16),
            jax.ShapeDtypeStruct((rows, tile), f32),
        ],
        scratch_shapes=[pltpu.VMEM((heads_dev, tile, 2 * length), f32)],
        compiler_params=pltpu.CompilerParams(vmem_limit_bytes=40 * 2**20),
        cost_estimate=pl.CostEstimate(
            flops=4 * rows * length * width,
            bytes_accessed=4 * length * width * 2,
            transcendentals=rows * length * heads_dev,
        ),
    )(first, place, table, near, qkv, doc_row, doc_col)


def attention_back(
    qkv, doc_row, doc_col, attended, grad_out, stats, first, place, table, near, split
):
    length = qkv.shape[0]
    rows = grad_out.shape[0]
    heads_dev = table.shape[1]
    width = heads_dev * head_dim
    return pl.pallas_call(
        functools.partial(attention_back_kernel, heads_dev, length, split),
        grid=(rows // tile,),
        in_specs=[
            pl.BlockSpec(memory_space=pltpu.SMEM),
            pl.BlockSpec(memory_space=pltpu.SMEM),
            pl.BlockSpec(memory_space=pltpu.SMEM),
            whole(near.shape),
            whole(qkv.shape),
            whole(doc_row.shape),
            pl.BlockSpec((tile, 1), lambda step: (step, 0)),
            whole((rows, width)),
            whole((rows, width)),
            pl.BlockSpec((tile, tile), lambda step: (step, 0)),
        ],
        out_specs=[
            whole((length, 3 * width)),
            whole((heads_dev, tile, 3 * tile)),
            whole((heads_dev, 2, 8, tile)),
        ],
        out_shape=[
            jax.ShapeDtypeStruct((length, 3 * width), bf16),
            jax.ShapeDtypeStruct((heads_dev, tile, 3 * tile), f32),
            jax.ShapeDtypeStruct((heads_dev, 2, 8, tile), f32),
        ],
        scratch_shapes=[
            pltpu.VMEM((heads_dev, tile, 2 * length), f32),
            pltpu.VMEM((heads_dev, tile, 2 * length), f32),
            pltpu.VMEM((length, width), f32),
            pltpu.VMEM((length, width), f32),
        ],
        compiler_params=pltpu.CompilerParams(vmem_limit_bytes=48 * 2**20),
        cost_estimate=pl.CostEstimate(
            flops=10 * rows * length * width,
            bytes_accessed=8 * length * width * 2,
            transcendentals=rows * length * heads_dev,
        ),
    )(first, place, table, near, qkv, doc_row, doc_col, attended, grad_out, stats)


def call(kernel, shapes, *operands, smem=0):
    return pl.pallas_call(
        kernel,
        in_specs=[pl.BlockSpec(memory_space=pltpu.SMEM)] * smem
        + [pl.BlockSpec(memory_space=pltpu.VMEM)] * (len(operands) - smem),
        out_specs=[pl.BlockSpec(memory_space=pltpu.VMEM)] * len(shapes),
        out_shape=[jax.ShapeDtypeStruct(shape, kind) for shape, kind in shapes],
        compiler_params=pltpu.CompilerParams(vmem_limit_bytes=10 * 2**20),
    )(*operands)


def share_in_kernel(place, attn_in, gains, near, far):
    layers, rows = attn_in.shape[:2]
    half = near.shape[0] // (layers * rows)
    width = near.shape[1] // 3
    for index in range(2 * half):
        member = place[index]
        for layer_id in range(layers):
            block = jnp.concatenate(
                [
                    attn_in[
                        layer_id,
                        :,
                        pl.ds(pl.multiple_of((part * 2 * half + member) * width, width), width),
                    ]
                    for part in range(3)
                ],
                axis=1,
            )
            at = (index % half * layers + layer_id) * rows
            out = near if index < half else far
            out[at : at + rows] = (block.astype(f32) * gains[layer_id]).astype(bf16)


def join_kernel(*refs):
    shares, outs = refs[:4], refs[4:]
    rows = outs[0].shape[0] // 8
    for chip, share in enumerate(shares):
        for core in range(2):
            for layer_id, out in enumerate(outs):
                source = (core * len(outs) + layer_id) * rows
                target = (chip * 2 + core) * rows
                out[target : target + rows] = share[source : source + rows]


def row_of(chip, plane, core, rows, planes=4):
    return pl.multiple_of(((chip * planes + plane) * 2 + core) * rows, rows)


def assemble_in_kernel(place, own, lower, upper, opposite, out):
    at_z, at_core, at_head = place[8], place[0] % 2, place[0] // 2
    rows = own.shape[0] // 8
    for part, offset in ((own, 0), (lower, 3), (upper, 1), (opposite, 2)):
        plane = (at_z + offset) % 4
        for index in range(8):
            row = row_of(at_head ^ (index // 2), plane, at_core ^ (index % 2), rows)
            out[pl.ds(row, rows)] = part[index * rows : (index + 1) * rows]


def plane_attention_kernel(
    length, place, table, strip, near, far, w_in, *refs
):
    halves, (doc_row, doc_col, w_out, qkv, attended, stats, near_part, far_part, band) = (
        refs[:2], refs[2:],
    )
    step = pl.program_id(0)
    half = length // 2
    heads_dev = table.shape[1]
    width = heads_dev * head_dim

    @pl.when(step == 0)
    def _():
        fill_band(band, table, strip, heads_dev, length)
        swapped = place[length // tile] % 2 == 1
        rows = width // 2
        w_out[:rows] = jnp.where(swapped, halves[1][...], halves[0][...])
        w_out[rows:] = jnp.where(swapped, halves[0][...], halves[1][...])
        qkv[:half] = contract(near[...], w_in[...], 1, 0).astype(bf16)
        qkv[half:] = contract(far[...], w_in[...], 1, 0).astype(bf16)

    row = pl.multiple_of(step * tile, tile)
    starts = band_starts(place, step, length, length // tile + 1)
    same_doc = doc_col[...] == doc_row[...]
    queries = qkv[pl.ds(row, tile), :width] * bf16(score_scale)
    lanes = lax.broadcasted_iota(jnp.int32, (tile, tile), 1)
    collected = jnp.zeros((tile, tile), f32)
    results = []
    for head in range(heads_dev):
        own = slice(head * head_dim, (head + 1) * head_dim)
        keys = qkv[:, width + own.start : width + own.stop]
        values = qkv[:, 2 * width + own.start : 2 * width + own.stop]
        scores = contract(queries[:, own], keys, 1, 1) + jnp.concatenate(
            [band[head, :, pl.ds(start, tile)] for start in starts], axis=1
        )
        scores = jnp.where(same_doc, scores, masked)
        peak = jnp.max(scores, axis=1, keepdims=True)
        weights = jnp.exp(scores - peak)
        total = jnp.sum(weights, axis=1, keepdims=True)
        results.append((contract(weights.astype(bf16), values, 1, 0) / total).astype(bf16))
        collected = jnp.where(lanes == head, peak + jnp.log(total), collected)
    stats[...] = collected
    merged = jnp.concatenate(results, axis=1)
    attended[...] = merged
    part = contract(merged, w_out[...], 1, 0)

    @pl.when(row < half)
    def _():
        near_part[...] = part

    @pl.when(row >= half)
    def _():
        far_part[...] = part.astype(bf16)


def near_block(steps, columns):
    return pl.BlockSpec((tile, columns), lambda step: (jnp.minimum(step, steps // 2 - 1), 0))


def far_block(steps, columns):
    return pl.BlockSpec((tile, columns), lambda step: (jnp.maximum(step - steps // 2, 0), 0))


def plane_attention(near, far, w_in, halves, doc_row, doc_col, place, table, strip):
    length, model_width = 2 * near.shape[0], near.shape[1]
    steps = length // tile
    heads_dev = table.shape[1]
    width = heads_dev * head_dim
    return pl.pallas_call(
        functools.partial(plane_attention_kernel, length),
        grid=(steps,),
        in_specs=[
            pl.BlockSpec(memory_space=pltpu.SMEM),
            pl.BlockSpec(memory_space=pltpu.SMEM),
            whole(strip.shape),
            whole(near.shape),
            whole(far.shape),
            whole(w_in.shape),
            *[whole(half.shape) for half in halves],
            whole(doc_row.shape),
            pl.BlockSpec((tile, 1), lambda step: (step, 0)),
        ],
        out_specs=[
            whole((width, model_width)),
            whole((length, 3 * width)),
            pl.BlockSpec((tile, width), lambda step: (step, 0)),
            pl.BlockSpec((tile, tile), lambda step: (step, 0)),
            near_block(steps, model_width),
            far_block(steps, model_width),
        ],
        out_shape=[
            jax.ShapeDtypeStruct((width, model_width), bf16),
            jax.ShapeDtypeStruct((length, 3 * width), bf16),
            jax.ShapeDtypeStruct((length, width), bf16),
            jax.ShapeDtypeStruct((length, tile), f32),
            jax.ShapeDtypeStruct((length // 2, model_width), f32),
            jax.ShapeDtypeStruct((length // 2, model_width), bf16),
        ],
        scratch_shapes=[pltpu.VMEM((heads_dev, tile, 2 * length), f32)],
        compiler_params=pltpu.CompilerParams(vmem_limit_bytes=14 * 2**20),
        cost_estimate=pl.CostEstimate(
            flops=4 * length * length * width + 8 * length * model_width * width,
            bytes_accessed=12 * 2**20,
            transcendentals=length * length * heads_dev,
        ),
    )(place, table, strip, near, far, w_in, *halves, doc_row, doc_col)


def plane_attention_back_kernel(
    length, place, table, strip, qkv, doc_row, doc_col, attended, stats, near, far, w_in, w_out,
    grad_qkv, grad_near, grad_far, near_part, far_part, *rest
):
    halves, (band, grad_band, grad_keys, grad_values, out_sum) = rest[:2], rest[2:]
    step = pl.program_id(0)
    half = length // 2
    heads_dev = table.shape[1]
    width = heads_dev * head_dim

    @pl.when(step == 0)
    def _():
        fill_band(band, table, strip, heads_dev, length)
        grad_band[...] = jnp.zeros_like(grad_band)
        grad_keys[...] = jnp.zeros_like(grad_keys)
        grad_values[...] = jnp.zeros_like(grad_values)
        out_sum[...] = jnp.zeros_like(out_sum)

    row = pl.multiple_of(step * half, half)
    branch = jnp.where(step == 0, near[...], far[...])
    merged = attended[...]
    grad_merged = contract(branch, w_out[...], 1, 1).astype(bf16)
    out_sum[...] += contract(merged, branch, 0, 0)
    products = grad_merged.astype(f32) * merged.astype(f32)
    queries = qkv[pl.ds(row, half), :width] * bf16(score_scale)
    blocks = half // tile
    for head in range(heads_dev):
        own = slice(head * head_dim, (head + 1) * head_dim)
        keys = qkv[:, width + own.start : width + own.stop]
        values = qkv[:, 2 * width + own.start : 2 * width + own.stop]
        upstream = grad_merged[:, own]
        raw_scores = contract(queries[:, own], keys, 1, 1)
        grad_weights = contract(upstream, values, 1, 1)
        delta = jnp.sum(products[:, own], axis=1, keepdims=True)
        weights_low, grads_low = [], []
        for block in range(blocks):
            lines = slice(block * tile, (block + 1) * tile)
            starts = band_starts(place, step * blocks + block, length, length // tile + 1)
            scores = raw_scores[lines] + jnp.concatenate(
                [band[head, :, pl.ds(start, tile)] for start in starts], axis=1
            )
            scores = jnp.where(doc_col[lines] == doc_row[...], scores, masked)
            weights = jnp.exp(scores - stats[lines, head : head + 1])
            grad_scores = weights * (grad_weights[lines] - delta[lines])
            for index, start in enumerate(starts):
                grad_band[head, :, pl.ds(start, tile)] += grad_scores[
                    :, index * tile : (index + 1) * tile
                ]
            weights_low.append(weights.astype(bf16))
            grads_low.append(grad_scores.astype(bf16))
        weights_low, grads_low = jnp.concatenate(weights_low), jnp.concatenate(grads_low)
        grad_values[:, own] += contract(weights_low, upstream, 0, 0)
        grad_keys[:, own] += contract(grads_low, queries[:, own], 0, 0)
        grad_qkv[pl.ds(row, half), own] = (
            contract(grads_low, keys, 1, 0) * score_scale
        ).astype(bf16)

    @pl.when(step == pl.num_programs(0) - 1)
    def _():
        grad_qkv[:, width : 2 * width] = grad_keys[...].astype(bf16)
        grad_qkv[:, 2 * width :] = grad_values[...].astype(bf16)
        far_part[...] = contract(grad_qkv[half:], w_in[...], 1, 1).astype(bf16)
        near_part[...] = contract(grad_qkv[:half], w_in[...], 1, 1)
        rows = width // 2
        for index, part in enumerate(halves):
            block = index ^ place[length // tile] % 2
            part[...] = out_sum[pl.ds(pl.multiple_of(block * rows, rows), rows)].astype(bf16)
        for head in range(heads_dev):
            grad_near[head] = grad_band[head, :, length - tile : length + 2 * tile]
            grad_far[head, 0] = jnp.full(
                (8, tile), jnp.sum(grad_band[head, :, : length - tile]), f32
            )
            grad_far[head, 1] = jnp.full(
                (8, tile), jnp.sum(grad_band[head, :, length + 2 * tile :]), f32
            )


def plane_attention_back(
    qkv, doc_row, doc_col, attended, stats, near, far, w_in, w_out, place, table, strip
):
    length, model_width = 2 * near.shape[0], near.shape[1]
    half = length // 2
    heads_dev = table.shape[1]
    width = heads_dev * head_dim
    shapes = [
        ((length, 3 * width), bf16),
        ((heads_dev, tile, 3 * tile), f32),
        ((heads_dev, 2, 8, tile), f32),
        ((length // 2, model_width), f32),
        ((length // 2, model_width), bf16),
    ] + [((width // 2, model_width), bf16)] * 2
    return pl.pallas_call(
        functools.partial(plane_attention_back_kernel, length),
        grid=(2,),
        in_specs=[
            pl.BlockSpec(memory_space=pltpu.SMEM),
            pl.BlockSpec(memory_space=pltpu.SMEM),
            whole(strip.shape),
            whole(qkv.shape),
            whole(doc_row.shape),
            pl.BlockSpec((half, 1), lambda step: (step, 0)),
            pl.BlockSpec((half, width), lambda step: (step, 0)),
            pl.BlockSpec((half, tile), lambda step: (step, 0)),
            whole((half, model_width)),
            whole((half, model_width)),
            whole(w_in.shape),
            whole(w_out.shape),
        ],
        out_specs=[whole(shape) for shape, _ in shapes],
        out_shape=[jax.ShapeDtypeStruct(shape, kind) for shape, kind in shapes],
        scratch_shapes=[
            pltpu.VMEM((heads_dev, tile, 2 * length), f32),
            pltpu.VMEM((heads_dev, tile, 2 * length), f32),
            pltpu.VMEM((length, width), f32),
            pltpu.VMEM((length, width), f32),
            pltpu.VMEM((width, model_width), f32),
        ],
        compiler_params=pltpu.CompilerParams(vmem_limit_bytes=32 * 2**20),
        cost_estimate=pl.CostEstimate(
            flops=10 * length * length * width + 10 * length * model_width * width,
            bytes_accessed=12 * 2**20,
            transcendentals=length * length * heads_dev,
        ),
    )(place, table, strip, qkv, doc_row, doc_col, attended, stats, near, far, w_in, w_out)


def gelu_and_slope(pre_act):
    size = jnp.abs(pre_act)
    gauss = jnp.exp(-0.5 * pre_act * pre_act)
    ratio = 1.0 / (1.0 + np.float32(0.3275911 * 0.5**0.5) * size)
    series = np.float32(1.061405429)
    for factor in (-1.453152027, 1.421413741, -0.284496736, 0.254829592):
        series = series * ratio + np.float32(factor)
    tail = 0.5 * series * ratio * gauss
    cumulative = jnp.where(pre_act < 0, tail, 1.0 - tail)
    slope = cumulative + pre_act * gauss * np.float32((2 * np.pi) ** -0.5)
    return pre_act * cumulative, slope


def ff_kernel(rows, pair, activated, slope, part):
    columns = rows.shape[1]
    value, gradient = gelu_and_slope(contract(rows[...], pair[:, :columns], 1, 1))
    activated[...] = value.astype(bf16)
    slope[...] = gradient.astype(bf16)
    part[...] = contract(activated[...], pair[:, columns:], 1, 0).astype(part.dtype)


def ff_first_kernel(rows, *refs):
    parts, (activated, slope, part, pair) = refs[:5], refs[5:]

    @pl.when(pl.program_id(0) == 0)
    def _():
        units, columns = parts[0].shape[0], rows.shape[1]
        for index, ref in enumerate(parts[:3]):
            pair[index * units : (index + 1) * units] = ref[...]
        pair[3 * units :, :columns] = parts[3][...]
        pair[3 * units :, columns:] = parts[4][...]

    ff_kernel(rows, pair, activated, slope, part)


def ff_back_kernel(rows, slope, pair, grad_pre, part):
    columns = rows.shape[1]
    grad_act = contract(rows[...], pair[:, columns:], 1, 1)
    grad_pre[...] = (grad_act * slope[...].astype(f32)).astype(bf16)
    part[...] = contract(grad_pre[...], pair[:, :columns], 1, 0).astype(part.dtype)


def by_rows(kernel, step_rows, row_operands, whole_operands, outs, whole_outs=()):
    rows = row_operands[0].shape[0]
    return pl.pallas_call(
        kernel,
        grid=(rows // step_rows,),
        in_specs=[
            pl.BlockSpec((step_rows, operand.shape[1]), lambda step: (step, 0))
            for operand in row_operands
        ]
        + [whole(operand.shape) for operand in whole_operands],
        out_specs=[pl.BlockSpec((step_rows, columns), lambda step: (step, 0)) for columns, _ in outs]
        + [whole(shape) for shape in whole_outs],
        out_shape=[jax.ShapeDtypeStruct((rows, columns), kind) for columns, kind in outs]
        + [jax.ShapeDtypeStruct(shape, bf16) for shape in whole_outs],
        compiler_params=pltpu.CompilerParams(vmem_limit_bytes=10 * 2**20),
        cost_estimate=pl.CostEstimate(
            flops=4 * rows * outs[0][0] * row_operands[0].shape[1],
            bytes_accessed=6 * 2**20,
            transcendentals=0,
        ),
    )(*row_operands, *whole_operands)


def ff_grads_kernel(
    pre_near, pre_far, act_near, act_far, normed_near, normed_far, low_near, low_far, *outs
):
    columns = normed_near.shape[1]
    units = outs[0].shape[0]
    up = (
        contract(pre_near[...], normed_near[...], 0, 0)
        + contract(pre_far[...], normed_far[...], 0, 0)
    ).astype(bf16)
    down = (
        contract(act_near[...], low_near[...], 0, 0) + contract(act_far[...], low_far[...], 0, 0)
    ).astype(bf16)

    @pl.when(pl.program_id(0) == 0)
    def _():
        for index in range(2):
            block = slice(index * units, (index + 1) * units)
            outs[index][:, :columns] = up[block]
            outs[index][:, columns:] = down[block]

    @pl.when(pl.program_id(0) == 1)
    def _():
        outs[2][:, :columns] = up[:units]
        outs[2][:, columns:] = down[:units]
        outs[3][...] = up[units:]
        outs[4][...] = down[units:]


def ff_grads(pre, act, normed, low):
    rows, hidden_units = pre[0].shape
    columns = normed[0].shape[1]
    shapes = [(hidden_units // 4, 2 * columns)] * 3 + [(hidden_units // 4, columns)] * 2
    return pl.pallas_call(
        ff_grads_kernel,
        grid=(2,),
        in_specs=[pl.BlockSpec((rows, hidden_units // 2), lambda step: (0, step))] * 4
        + [whole((rows, columns))] * 4,
        out_specs=[whole(shape) for shape in shapes],
        out_shape=[jax.ShapeDtypeStruct(shape, bf16) for shape in shapes],
        compiler_params=pltpu.CompilerParams(vmem_limit_bytes=14 * 2**20),
        cost_estimate=pl.CostEstimate(
            flops=8 * rows * hidden_units * columns, bytes_accessed=8 * 2**20, transcendentals=0
        ),
    )(*pre, *act, *normed, *low)


def in_grads_kernel(place, near, far, grad_qkv, *refs):
    ends, outs, (total, extra) = refs[:-6], refs[-6:-2], refs[-2:]
    half = near.shape[0]
    columns = grad_qkv.shape[1]
    total[:, :columns] = (
        contract(near[...], grad_qkv[:half], 0, 0) + contract(far[...], grad_qkv[half:], 0, 0)
    ).astype(bf16)
    rows = outs[0].shape[0] // 8
    if ends:
        gain_0, gain_1, table_0, table_1 = ends
        lines = lax.broadcasted_iota(jnp.int32, (tile, gain_0.shape[1]), 0)
        gains = jnp.where(lines == 0, gain_0[...], jnp.where(lines == 1, gain_1[...], 0.0))
        extra[...] = jnp.transpose(gains)
        table = table_0[...] + table_1[...]
        buckets = table.shape[0] // 8
        blank = jnp.zeros((8 - buckets, tile), f32)
        for block in range(8):
            row = pl.multiple_of((place[0] // 2 * 8 + block) * rows, rows)
            extra[pl.ds(row, 8)] += jnp.concatenate(
                [table[block * buckets : (block + 1) * buckets], blank]
            )
        total[:, columns:] = extra[...].astype(bf16)
    for out, offset in zip(outs, (0, 3, 1, 2)):
        plane = (place[8] + offset) % 4
        for index in range(8):
            owner = place[index]
            row = row_of(owner // 2, plane, owner % 2, rows)
            out[index * rows : (index + 1) * rows] = total[pl.ds(row, rows)]


def in_grads(place, near, far, grad_qkv, *ends):
    columns = grad_qkv.shape[1] + (tile if ends else 0)
    shape = (near.shape[1] // 4, columns)
    return pl.pallas_call(
        in_grads_kernel,
        in_specs=[pl.BlockSpec(memory_space=pltpu.SMEM)]
        + [pl.BlockSpec(memory_space=pltpu.VMEM)] * (3 + len(ends)),
        out_specs=[pl.BlockSpec(memory_space=pltpu.VMEM)] * 4,
        out_shape=[jax.ShapeDtypeStruct(shape, bf16)] * 4,
        scratch_shapes=[
            pltpu.VMEM((near.shape[1], columns), bf16),
            pltpu.VMEM((near.shape[1], tile), f32),
        ],
        compiler_params=pltpu.CompilerParams(vmem_limit_bytes=14 * 2**20),
        cost_estimate=pl.CostEstimate(
            flops=4 * near.shape[0] * near.shape[1] * columns,
            bytes_accessed=4 * 2**20,
            transcendentals=0,
        ),
    )(place, near, far, grad_qkv, *ends)


def add_in_kernel(own, lower, upper, opposite, near, far):
    total = sum_of_four([own, lower, upper, opposite]).astype(bf16)
    half = near.shape[0]
    near[...] = total[:half]
    far[...] = total[half:]


def combine_kernel(near_part, arrived, own, x_part, y_part, xy_part):
    rows = own.shape[0]
    own[...] = near_part[:rows] + arrived[:rows].astype(f32)
    for bits, out in ((1, x_part), (2, y_part), (3, xy_part)):
        block = slice(bits * rows, (bits + 1) * rows)
        out[...] = (near_part[block] + arrived[block].astype(f32)).astype(bf16)


def added(own, x_part, y_part, xy_part):
    return (own[...] + x_part[...].astype(f32)) + (
        y_part[...].astype(f32) + xy_part[...].astype(f32)
    )


def close_kernel(kept, own, x_part, y_part, xy_part, hidden, units):
    total = kept[...] + added(own, x_part, y_part, xy_part)
    hidden[...] = total
    units[...] = (total * inverse_rms(total)).astype(bf16)


def close_gain_kernel(kept, own, x_part, y_part, xy_part, gain, hidden, normed):
    total = kept[...] + added(own, x_part, y_part, xy_part)
    hidden[...] = total
    normed[...] = (total * inverse_rms(total) * gain[...]).astype(bf16)


def last_kernel(kept, own, x_part, y_part, xy_part, hidden):
    hidden[...] = (kept[...] + added(own, x_part, y_part, xy_part)).astype(bf16)


def middle_back_kernel(
    upstream, own, x_part, y_part, xy_part, middle, gain, grad_middle, branch, grad_gain
):
    grad_normed = added(own, x_part, y_part, xy_part)
    inverse = inverse_rms(middle[...])
    grad_gain[...] = jnp.sum(grad_normed * middle[...] * inverse, axis=0, keepdims=True)
    total = upstream[...].astype(f32) + unit_norm_back(
        middle[...], inverse, grad_normed * gain[...]
    )
    grad_middle[...] = total
    branch[...] = total.astype(bf16)


def layer_back_kernel(grad_middle, own, x_part, y_part, xy_part, hidden, upstream, low):
    total = grad_middle[...] + unit_norm_back(
        hidden[...], inverse_rms(hidden[...]), added(own, x_part, y_part, xy_part)
    )
    upstream[...] = total
    low[...] = total.astype(bf16)


def pair_kernel(axis, near, arrived, *outs):
    rows = near.shape[0] // len(outs)
    for index, out in enumerate(outs):
        block = slice(index * rows, (index + 1) * rows)
        if axis == 0:
            out[:rows] = near[block]
            out[rows:] = arrived[block]
        else:
            columns = near.shape[1]
            out[:, :columns] = near[block]
            out[:, columns:] = arrived[block]


def unit_kernel(tokens, hidden, units):
    total = tokens[...].astype(f32)
    hidden[...] = total
    units[...] = (total * inverse_rms(total)).astype(bf16)


def finish_in_kernel(place, *refs):
    chips, (attn_in, gains, grad_in, grad_gain, ends) = refs[:8], refs[8:]
    rows = attn_in.shape[1]
    width = tile
    members = attn_in.shape[2] // (3 * width)
    ends[...] = jnp.zeros_like(ends)
    for layer_id in range(2):
        row_dot = jnp.zeros((rows, 1), f32)
        for index in range(members):
            member = place[index]
            chip = chips[4 * layer_id + index % 4]
            half = chip.shape[1] // 2
            total = chip[:, index // 4 * half : (index // 4 + 1) * half].astype(f32)
            if layer_id == 0:
                ends[...] += total[:, 3 * width :]
            for part in range(3):
                block = total[:, part * width : (part + 1) * width]
                columns = pl.ds(pl.multiple_of((part * members + member) * width, width), width)
                grad_in[layer_id, :, columns] = block * gains[layer_id]
                row_dot = row_dot + jnp.sum(
                    block * attn_in[layer_id, :, columns].astype(f32), axis=1, keepdims=True
                )
        grad_gain[layer_id] = jnp.concatenate(
            [row_dot, ends[:, layer_id : layer_id + 1]], axis=1
        )


def sum_of_four(parts):
    return (parts[0][...].astype(f32) + parts[1][...].astype(f32)) + (
        parts[2][...].astype(f32) + parts[3][...].astype(f32)
    )


def finish_ff_kernel(*refs):
    count = (len(refs) - 3) // 2
    sources, grads, held, done = refs[:count], refs[count : count + 2], refs[count + 2 : -1], refs[-1]
    copies = [
        pltpu.make_async_copy(source, target, done.at[index])
        for index, (source, target) in enumerate(zip(sources, held))
    ]
    for copy in copies:
        copy.start()
    for copy in copies:
        copy.wait()
    refs = held
    columns = grads[0].shape[2]
    for layer_id in range(grads[0].shape[0]):
        parts = refs[5 * layer_id : 5 * layer_id + 5]
        for side, out in enumerate(grads):
            halves = [part.at[:, side * columns : (side + 1) * columns] for part in parts[:3]]
            out[layer_id] = sum_of_four(halves + [parts[3 + side]])


def finish_ff(grads, shape):
    return pl.pallas_call(
        finish_ff_kernel,
        in_specs=[pl.BlockSpec(memory_space=pl.ANY)] * len(grads),
        out_specs=[pl.BlockSpec(memory_space=pltpu.VMEM)] * 2,
        out_shape=[jax.ShapeDtypeStruct(shape, f32)] * 2,
        scratch_shapes=[pltpu.VMEM(grad.shape, bf16) for grad in grads]
        + [pltpu.SemaphoreType.DMA((len(grads),))],
        compiler_params=pltpu.CompilerParams(vmem_limit_bytes=14 * 2**20),
    )(*grads)


def add_out_kernel(place, *refs):
    parts, (own, other) = refs[:-2], refs[-2:]
    for layer_id in range(own.shape[0]):
        total = parts[2 * layer_id][...].astype(f32) + parts[2 * layer_id + 1][...].astype(f32)
        rows = total.shape[0] // 2
        second = place[0] % 2 == 1
        own[layer_id] = jnp.where(second, total[rows:], total[:rows])
        other[layer_id] = jnp.where(second, total[:rows], total[rows:]).astype(bf16)


def finish_out_kernel(own, arrived, out):
    out[...] = own[...] + arrived[...].astype(f32)


def inverse_rms(hidden):
    return lax.rsqrt(jnp.mean(hidden * hidden, axis=-1, keepdims=True) + epsilon)


def prepare(bias_table, first_head, heads_dev):
    table = lax.dynamic_slice_in_dim(bias_table, first_head, heads_dev, 1)
    (near,) = call(near_kernel, [((heads_dev, tile, 3 * tile), f32)], table, smem=1)
    return table, near


def bucket_grads(first_lane, grads, bucket_count):
    (total,) = call(bucket_kernel, [((bucket_count, tile), f32)], first_lane, *grads, smem=1)
    return total


def gelu_parts(pre_act):
    cumulative = 0.5 * (1.0 + lax.erf(pre_act * np.float32(0.5**0.5)))
    slope = cumulative + pre_act * jnp.exp(-0.5 * pre_act * pre_act) * np.float32(
        (2 * np.pi) ** -0.5
    )
    return (pre_act * cumulative).astype(bf16), slope


def unit_norm_back(hidden, inverse, grad_unit):
    unit = hidden * inverse
    return inverse * (grad_unit - unit * jnp.mean(grad_unit * unit, axis=-1, keepdims=True))


def gather_rows(block, axes):
    return lax.all_gather(block, axes, axis=0, tiled=True)


def toggle(array, axis, bits):
    return lax.ppermute(array, axis, [(i, i ^ bits) for i in range(lax.axis_size(axis))])


def shift(array, by):
    planes = lax.axis_size("z")
    return lax.ppermute(array, "z", [(i, (i + by) % planes) for i in range(planes)])


def plane_gather(block, *holds):
    near = jnp.concatenate([block] + [toggle(block, "head", bits) for bits in (1, 2, 3)])
    near, *holds = tie(near, *holds)
    return (near, toggle(near, "core", 1), *holds)


def plane_scatter(near_part, far_part):
    rows, columns = near_part.shape[0] // 4, near_part.shape[1]
    own, *others = call(
        combine_kernel,
        [((rows, columns), f32)] + [((rows, columns), bf16)] * 3,
        near_part,
        toggle(far_part, "core", 1),
    )
    shares = [own] + [toggle(other, "head", bits) for bits, other in zip((1, 2, 3), others)]
    return shares, own


def tie(*arrays):
    return lax.optimization_barrier(arrays)


def after(array, other):
    return lax.optimization_barrier((array, other))[0]


def scatter_sum(partial, axes, members):
    blocks = partial.astype(bf16).reshape(members, -1, partial.shape[1])
    return jnp.sum(lax.all_to_all(blocks, axes, 0, 0, tiled=True).astype(f32), axis=0)


def local_general(tokens, doc_start, bias_table, attn_in, attn_out, ff_in, ff_out, gains, cotangent):
    heads_n, z_n, core_n = (lax.axis_size(axis) for axis in everyone)
    devices = heads_n * z_n * core_n
    group, spare = ("z", "core"), "head"
    ff_group, ff_spare, ff_members = ("head", "core"), "z", heads_n * core_n
    blocks = z_n * core_n
    block_rows, model_width = tokens.shape[1:]
    layer_count, weight_rows = attn_in.shape[:2]
    length = block_rows * blocks
    heads_all = bias_table.shape[1]
    member = lax.axis_index("z") * core_n + lax.axis_index("core")
    heads_dev = max(1, heads_all // blocks)
    head_groups = heads_all // heads_dev
    split = blocks // head_groups
    head_group, query_part = member // split, member % split
    query_rows = length // split
    width = heads_dev * head_dim
    first = (query_part * (query_rows // tile)).astype(jnp.int32).reshape(1)
    place = jnp.arange(length // tile, dtype=jnp.int32)
    out_row = head_group * width

    def swap(array):
        return lax.all_to_all(array, everyone, 0, 0, tiled=True)

    starts = jnp.broadcast_to(
        doc_start.astype(f32)[:, None], (heads_n, blocks, block_rows)
    ).reshape(devices, block_rows)
    ff_gains = gains[:, :, 1].astype(f32).reshape(1, -1)
    small = swap(
        jnp.concatenate(
            [starts, jnp.broadcast_to(ff_gains, (devices, layer_count * weight_rows))], axis=1
        )
    )
    doc_row = small[:blocks, :block_rows].reshape(1, length)
    doc_col = lax.dynamic_slice_in_dim(
        doc_row.reshape(length, 1), query_part * query_rows, query_rows, 0
    )
    gain_ff = jnp.transpose(
        small[:, block_rows:].reshape(devices, layer_count, weight_rows), (1, 0, 2)
    ).reshape(layer_count, 1, model_width)
    table, near = prepare(bias_table, head_group * heads_dev, heads_dev)

    gain_attn = gains[:, :, 0].astype(f32)[:, :, None]
    own_in = attn_in.astype(f32)

    def fetch_in(layer_id):
        scaled = (own_in[layer_id] * gain_attn[layer_id]).astype(bf16)
        columns = jnp.transpose(
            scaled.reshape(weight_rows, 3, head_groups, width), (2, 0, 1, 3)
        ).reshape(head_groups, weight_rows, 3 * width)
        columns = jnp.repeat(columns, split, axis=0)
        columns = jnp.broadcast_to(columns[None], (heads_n, *columns.shape))
        return swap(columns.reshape(devices, weight_rows, 3 * width)).reshape(
            model_width, 3 * width
        )

    def fetch_ff(layer_id):
        pair = jnp.concatenate([ff_in[layer_id], ff_out[layer_id]], axis=1)
        pair = gather_rows(pair, ff_spare)
        return pair[:, :model_width], pair[:, model_width:]

    hidden, upstream = tokens[0].astype(f32), cotangent[0]
    weights_in = [fetch_in(layer_id) for layer_id in range(layer_count)]
    weights_out = lax.dynamic_slice_in_dim(
        lax.all_gather(attn_out, everyone, axis=1, tiled=True), out_row, width, 1
    )
    weights_ff = [fetch_ff(layer_id) for layer_id in range(layer_count)]

    records = []
    for layer_id in range(layer_count):
        w_in, w_out, (w_up, w_down) = (
            weights_in[layer_id], weights_out[layer_id], weights_ff[layer_id],
        )
        inverse = inverse_rms(hidden)
        units = gather_rows((hidden * inverse).astype(bf16), group)
        qkv = jnp.dot(units, w_in, preferred_element_type=f32).astype(bf16)
        attended, _, stats = attention(
            qkv, doc_row, doc_col, first, place, table, near, query_rows
        )
        mixed = jnp.dot(attended, w_out, preferred_element_type=f32)
        if split > 1:
            mixed = lax.dynamic_update_slice_in_dim(
                jnp.zeros((length, model_width), f32), mixed, query_part * query_rows, 0
            )
        middle = hidden + scatter_sum(mixed, group, blocks)
        inverse_ff = inverse_rms(middle)
        normed_ff = gather_rows((middle * inverse_ff * gain_ff[layer_id]).astype(bf16), ff_group)
        activated, slope = gelu_parts(contract(normed_ff, w_up, 1, 1))
        ff_result = jnp.dot(activated, w_down, preferred_element_type=f32)
        records.append(
            (hidden, inverse, units, qkv, attended, stats, middle, inverse_ff, normed_ff,
             activated, slope)
        )
        hidden = middle + scatter_sum(ff_result, ff_group, ff_members)
    output = hidden

    grads_ff, grads_in, grads_out, grads_gain_ff, grads_table = (
        [None] * layer_count for _ in range(5)
    )
    for layer_id in reversed(range(layer_count)):
        w_in, w_out, (w_up, w_down) = (
            weights_in[layer_id], weights_out[layer_id], weights_ff[layer_id],
        )
        (hidden, inverse, units, qkv, attended, stats, middle, inverse_ff, normed_ff,
         activated, slope) = records[layer_id]
        grad_low = gather_rows(upstream.astype(bf16), ff_group)
        grad_pre = (contract(grad_low, w_down, 1, 1) * slope).astype(bf16)
        grad_normed = scatter_sum(
            jnp.dot(grad_pre, w_up, preferred_element_type=f32), ff_group, ff_members
        )
        grad_pair = jnp.concatenate(
            [contract(grad_pre, normed_ff, 0, 0), contract(activated, grad_low, 0, 0)], axis=1
        ).astype(bf16)
        grads_ff[layer_id] = lax.psum_scatter(
            grad_pair, ff_spare, scatter_dimension=0, tiled=True
        ).astype(f32)
        grads_gain_ff[layer_id] = jnp.sum(grad_normed * middle * inverse_ff, axis=0)
        grad_middle = upstream + unit_norm_back(
            middle, inverse_ff, grad_normed * gain_ff[layer_id]
        )
        branch = gather_rows(grad_middle.astype(bf16), group)
        if split > 1:
            branch = lax.dynamic_slice_in_dim(branch, query_part * query_rows, query_rows, 0)
        grad_attended = contract(branch, w_out, 1, 1).astype(bf16)
        grad_qkv, grad_near, grad_far = attention_back(
            qkv, doc_row, doc_col, attended, grad_attended, stats, first, place, table, near, split
        )
        grads_table[layer_id] = (grad_near, grad_far)
        grad_units = scatter_sum(contract(grad_qkv, w_in, 1, 1), group, blocks)
        upstream = grad_middle + unit_norm_back(hidden, inverse, grad_units)
        grad_out = lax.dynamic_update_slice_in_dim(
            jnp.zeros((model_width, model_width), bf16),
            contract(attended, branch, 0, 0).astype(bf16),
            out_row,
            0,
        )
        grads_out[layer_id] = lax.psum_scatter(
            grad_out, everyone, scatter_dimension=0, tiled=True
        ).astype(f32)
        grads_in[layer_id] = contract(units, grad_qkv, 0, 0).astype(bf16)

    bucket_count = table.shape[0]
    grad_table = sum(
        bucket_grads(jnp.zeros((1,), jnp.int32), entry, bucket_count) for entry in grads_table
    )[:, :heads_dev]
    grad_table = lax.dynamic_update_slice_in_dim(
        jnp.zeros((bucket_count, heads_all), f32), grad_table, head_group * heads_dev, 1
    )
    grad_table = jnp.transpose(
        grad_table.reshape(blocks, bucket_count // blocks, heads_n, heads_all // heads_n),
        (2, 0, 1, 3),
    ).reshape(devices, -1)
    grad_gain_ff = jnp.transpose(
        jnp.stack(grads_gain_ff).reshape(layer_count, devices, weight_rows), (1, 0, 2)
    ).reshape(devices, -1)
    ends = jnp.sum(swap(jnp.concatenate([grad_gain_ff, grad_table], axis=1)), axis=0)
    grad_gain_ff = ends[: layer_count * weight_rows].reshape(layer_count, weight_rows)
    grad_bias_table = ends[layer_count * weight_rows :].reshape(
        bucket_count // blocks, heads_all // heads_n
    )
    grads_attn_in, grads_gains = [], []
    for layer_id in range(layer_count):
        parts = swap(grads_in[layer_id].reshape(devices, weight_rows, 3 * width)).astype(f32)
        parts = jnp.sum(parts.reshape(heads_n, blocks, weight_rows, 3 * width), axis=0)
        parts = jnp.sum(parts.reshape(head_groups, split, weight_rows, 3, width), axis=1)
        unit_grad = jnp.transpose(parts, (1, 2, 0, 3)).reshape(weight_rows, 3 * model_width)
        grads_attn_in.append(unit_grad * gain_attn[layer_id])
        grads_gains.append(
            jnp.stack(
                [jnp.sum(unit_grad * own_in[layer_id], axis=1), grad_gain_ff[layer_id]], axis=1
            )
        )
    return (
        output[None],
        upstream[None],
        jnp.stack(grads_attn_in),
        jnp.stack(grads_out),
        jnp.stack([entry[:, :model_width] for entry in grads_ff]),
        jnp.stack([entry[:, model_width:] for entry in grads_ff]),
        jnp.stack(grads_gains),
        grad_bias_table,
    )


def local_plane(tokens, doc_start, bias_table, attn_in, attn_out, ff_in, ff_out, gains, cotangent):
    heads_n, z_n, core_n = (lax.axis_size(axis) for axis in everyone)
    devices = heads_n * z_n * core_n
    at_head, at_z, at_core = (lax.axis_index(axis) for axis in everyone)
    members = heads_n * core_n
    block_rows, model_width = tokens.shape[1:]
    layer_count, weight_rows = attn_in.shape[:2]
    length = block_rows * members
    heads_all = bias_table.shape[1]
    heads_dev = heads_all // members
    width = heads_dev * head_dim
    member = at_head * core_n + at_core
    everywhere = [(h, z, c) for h in range(heads_n) for z in range(z_n) for c in range(core_n)]

    def swapped(bits):
        return bits % 2 * 2 + bits // 2

    def device(h, z, c):
        return (h * z_n + z) * core_n + c

    turn = [(device(h, z, c), device(h ^ swapped(z), h, c)) for h, z, c in everywhere]
    plane_turn = [(device(h, z, c), device(h ^ swapped(z), z, c)) for h, z, c in everywhere]
    line_turn = [(device(h, z, c), device(h, h ^ swapped(z), c)) for h, z, c in everywhere]
    line_back = [(target, source) for source, target in line_turn]
    place = jnp.stack(
        [
            (at_head ^ bits) * core_n + (at_core ^ other)
            for other in range(core_n)
            for bits in range(heads_n)
        ]
        + [at_z]
        + [
            swapped(at_head ^ bits ^ at_z) * core_n + (at_core ^ other)
            for other in range(core_n)
            for bits in range(heads_n)
        ]
    ).astype(jnp.int32)

    def relay(array):
        return lax.ppermute(array, everyone, turn)

    def turn_in_plane(array):
        return lax.ppermute(array, everyone, plane_turn)

    def turn_in_line(array, turns):
        return lax.ppermute(array, everyone, turns)

    def swap(array):
        return lax.all_to_all(array, everyone, 0, 0, tiled=True)

    row_shape = (block_rows, model_width)
    gain_attn = gains[:, :, 0].astype(f32)[:, :, None]
    near_share, far_share = call(
        share_in_kernel,
        [((members // 2 * layer_count * weight_rows, 3 * width), bf16)] * 2,
        place,
        attn_in,
        gain_attn,
        smem=1,
    )

    half_turns = [
        [
            (z * core_n + c, (2 * c + (a ^ z % 2)) * core_n + z // 2)
            for z in range(z_n)
            for c in range(core_n)
        ]
        for a in range(2)
    ]

    def fetch_out(layer_id, hold):
        own = attn_out[layer_id]
        other = toggle(own, "core", 1)
        head = jnp.where(
            at_core == 0, jnp.concatenate([own, other]), jnp.concatenate([other, own])
        )
        head = after(head, hold)
        return [
            lax.ppermute(head, ("z", "core"), [(holder, user) for user, holder in turns])
            for turns in half_turns
        ]

    def owners_halves(halves):
        return [
            lax.ppermute(half, ("z", "core"), turns) for half, turns in zip(halves, half_turns)
        ]

    def pair_chips(near, arrived, axis):
        rows, columns = near.shape[0] // 4, near.shape[1]
        shape = (2 * rows, columns) if axis == 0 else (rows, 2 * columns)
        return call(functools.partial(pair_kernel, axis), [(shape, bf16)] * 4, near, arrived)

    def share_chips(blocks):
        return [blocks[0]] + [toggle(blocks[bits], "head", bits) for bits in (1, 2, 3)]

    units_shape = [(row_shape, f32), (row_shape, bf16)]

    starts = jnp.broadcast_to(
        doc_start.astype(f32)[None, :, None], (heads_n, z_n, core_n, block_rows)
    )
    ff_gains = gains[:, :, 1].astype(f32).reshape(1, -1)
    small = jnp.concatenate(
        [
            starts.reshape(devices, block_rows),
            jnp.broadcast_to(ff_gains, (devices, layer_count * weight_rows)),
        ],
        axis=1,
    )
    table, strip = prepare(bias_table, member * heads_dev, heads_dev)
    hidden = relay(tokens[0])
    hidden, shares, halves, small = tie(
        hidden,
        share_chips(pair_chips(near_share, toggle(far_share, "core", 1), 0)),
        fetch_out(0, near_share),
        swap(after(small, near_share)),
    )
    hidden, unit_rows = call(unit_kernel, units_shape, hidden)
    doc_row = small[:members, :block_rows].reshape(2, 2, core_n, block_rows)
    at_block = swapped(at_head ^ at_z)
    for axis, bit in ((0, at_block // 2), (1, at_block % 2), (2, at_core)):
        doc_row = jnp.where(bit == 1, jnp.flip(doc_row, axis), doc_row)
    doc_row = jnp.transpose(doc_row, (2, 1, 0, 3)).reshape(1, length)
    doc_col = doc_row.reshape(length, 1)
    gain_ff = jnp.transpose(
        small[:, block_rows:].reshape(devices, layer_count, weight_rows), (1, 0, 2)
    ).reshape(layer_count, 1, model_width)

    def round_planes(array, by, hold):
        return shift(after(array, hold), by)

    ff_pairs = [
        jnp.concatenate([ff_in[layer_id], ff_out[layer_id]], axis=1) for layer_id in range(layer_count)
    ]

    def ff_both(kernel, row_operands, pair, columns):
        return zip(
            *(
                by_rows(
                    kernel,
                    256,
                    operands,
                    [pair],
                    [(pair.shape[0], bf16)] * columns + [(model_width, kind)],
                )
                for operands, kind in zip(zip(*row_operands), (f32, bf16))
            )
        )

    def ff_forward(normed, *parts):
        units = 4 * parts[0].shape[0]
        outs = [(units, bf16), (units, bf16)]
        *near, pair = by_rows(
            ff_first_kernel,
            256,
            [normed[0]],
            parts,
            outs + [(model_width, f32)],
            [(units, 2 * model_width)],
        )
        far = by_rows(ff_kernel, 256, [normed[1]], [pair], outs + [(model_width, bf16)])
        return pair, *zip(near, far)

    def ff_backward(low, slopes, pair):
        return ff_both(ff_back_kernel, [low, slopes], pair, 1)

    def assemble_in(share, lower, upper, opposite):
        return call(
            assemble_in_kernel,
            [((model_width, 3 * width), bf16)],
            place,
            share,
            lower,
            upper,
            opposite,
            smem=1,
        )[0]

    share, later_share = call(
        join_kernel, [((members * weight_rows, 3 * width), bf16)] * layer_count, *shares
    )
    near, far, lower, upper, opposite, strip, doc_row, doc_col, gain_ff, *ff_pairs = plane_gather(
        unit_rows,
        shift(share, 1),
        shift(share, -1),
        shift(share, 2),
        strip,
        doc_row,
        doc_col,
        gain_ff,
        *ff_pairs,
    )
    w_in = assemble_in(share, lower, upper, opposite)
    units = (near, far)
    w_out, qkv, attended, stats, *parts = plane_attention(
        *units, w_in, halves, doc_row, doc_col, place, table, strip
    )
    parts, lower, upper, cotangent_low = tie(
        parts,
        round_planes(ff_pairs[0], 1, near),
        round_planes(ff_pairs[0], -1, near),
        turn_in_plane(after(cotangent[0].astype(bf16), near)),
    )
    parts, own = plane_scatter(*parts)
    parts, opposite_in = tie(parts, round_planes(ff_in[0], 2, own))
    middle, normed_rows = call(close_gain_kernel, units_shape, hidden, *parts, gain_ff[0])
    halves_1 = fetch_out(1, normed_rows)
    *normed, opposite_out, first_half = plane_gather(
        normed_rows, round_planes(ff_out[0], 2, normed_rows), halves_1[0]
    )
    pair, acts, slopes, parts = ff_forward(
        normed, ff_pairs[0], lower, upper, opposite_in, opposite_out
    )
    records = [
        (hidden, units, w_in, w_out, pair, qkv, attended, stats, middle, normed, acts, slopes)
    ]
    parts, lower, upper = tie(
        parts,
        round_planes(later_share, 1, normed[0]),
        round_planes(later_share, -1, normed[0]),
    )
    parts, own = plane_scatter(*parts)
    parts, opposite, upstream = tie(
        parts, round_planes(later_share, 2, own), turn_in_line(after(cotangent_low, own), line_turn)
    )
    shares = [later_share, lower, upper, opposite]
    hidden, unit_rows = call(close_kernel, units_shape, middle, *parts)

    near, far, lower, second_half = plane_gather(
        unit_rows, round_planes(ff_pairs[1], 1, unit_rows), halves_1[1]
    )
    halves = [first_half, second_half]
    units = (near, far)
    w_in = assemble_in(*shares)
    w_out, qkv, attended, stats, *parts = plane_attention(
        *units, w_in, halves, doc_row, doc_col, place, table, strip
    )
    low = plane_gather(after(upstream, far))
    parts, near_low, upper = tie(parts, low[0], round_planes(ff_pairs[1], -1, far))
    low = (near_low, low[1])
    parts, own = plane_scatter(*parts)
    parts, opposite_in = tie(parts, round_planes(ff_in[1], 2, own))
    middle, normed_rows = call(close_gain_kernel, units_shape, hidden, *parts, gain_ff[1])
    *normed, opposite_out = plane_gather(normed_rows, round_planes(ff_out[1], 2, normed_rows))
    pair, acts, slopes, last_parts = ff_forward(
        normed, ff_pairs[1], lower, upper, opposite_in, opposite_out
    )
    records.append(
        (hidden, units, w_in, w_out, pair, qkv, attended, stats, middle, normed, acts, slopes)
    )

    def back_to_middle(parts, upstream, middle, gain):
        return call(
            middle_back_kernel, units_shape + [((1, model_width), f32)], upstream, *parts, middle, gain
        )

    def attention_grads(record, branch):
        _, _, w_in, w_out, _, qkv, attended, stats, *_ = record
        grad_qkv, grad_near, grad_far, near_part, far_part, *halves = plane_attention_back(
            qkv, doc_row, doc_col, attended, stats, *branch, w_in, w_out, place, table, strip
        )
        return grad_qkv, (grad_near, grad_far), (near_part, far_part), halves

    def table_grads(near_and_far):
        return bucket_grads(at_core.reshape(1) * heads_dev + 8, near_and_far, table.shape[0])

    record = records[1]
    hidden, units, _, _, pair, *_, middle, normed, acts, slopes = record
    pres, parts = ff_backward(low, slopes, pair)
    parts, own = plane_scatter(*parts)
    planes = ff_grads(after(pres, own), acts, normed, low)
    parts, ff_lower = tie(parts, shift(planes[1], -1))
    last_parts, _ = plane_scatter(*after(last_parts, parts))
    grad_middle, branch_rows, gain_1 = back_to_middle(parts, upstream, middle, gain_ff[1])
    *branch, ff_upper = plane_gather(branch_rows, round_planes(planes[2], 1, branch_rows))
    grad_qkv, strips_1, parts, halves_1 = attention_grads(record, branch)
    parts, last_parts, opposite_up = tie(
        parts, last_parts, round_planes(planes[3], 2, branch[1])
    )
    parts, own = plane_scatter(*parts)
    parts, opposite_down, output = tie(
        parts,
        round_planes(planes[4], 2, own),
        call(last_kernel, [(row_shape, bf16)], middle, *after(last_parts, own))[0],
    )
    grads_ff = [planes[0], ff_lower, ff_upper, opposite_up, opposite_down]
    upstream, low_rows = call(layer_back_kernel, units_shape, grad_middle, *parts, hidden)

    record = records[0]
    hidden, units, _, _, pair, *_, middle, normed, acts, slopes = record
    grad_in = in_grads(place, *records[1][1], after(grad_qkv, low_rows))
    *low, in_opposite, in_upper, table_1 = plane_gather(
        low_rows, shift(grad_in[3], 2), shift(grad_in[2], 1), table_grads(after(strips_1, low_rows))
    )
    pres, parts = ff_backward(low, slopes, pair)
    parts, in_lower = tie(parts, round_planes(grad_in[1], -1, low[0]))
    parts, own = plane_scatter(*parts)
    planes = ff_grads(after(pres, own), acts, normed, low)
    near_in, far_in = call(
        add_in_kernel,
        [((members // 2 * weight_rows, 3 * width), bf16)] * 2,
        *after([grad_in[0], in_lower, in_upper, in_opposite], own),
    )
    parts, ff_lower, first_half, arrived = tie(
        parts,
        shift(planes[1], -1),
        owners_halves(after(halves_1, own))[0],
        toggle(far_in, "core", 1),
    )
    grad_middle, branch_rows, gain_0 = back_to_middle(parts, upstream, middle, gain_ff[0])
    *branch, ff_upper, second_half, shares_1 = plane_gather(
        branch_rows,
        round_planes(planes[2], 1, branch_rows),
        owners_halves(after(halves_1, branch_rows))[1],
        pair_chips(near_in, after(arrived, branch_rows), 1),
    )
    halves_1 = [first_half, second_half]
    grad_qkv, strips_0, parts, halves_0 = attention_grads(record, branch)
    parts, shares_1, output, opposite_up = tie(
        parts,
        share_chips(after(shares_1, branch[1])), turn_in_line(after(output, branch[1]), line_back), round_planes(planes[3], 2, branch[1])
    )
    parts, own = plane_scatter(*parts)
    table_0 = table_grads(after(strips_0, own))
    grad_in = in_grads(
        place, *units, after(grad_qkv, own), gain_0, gain_1, table_0, table_1
    )
    parts, in_opposite, halves_0 = tie(
        parts, shift(grad_in[3], 2), owners_halves(after(halves_0, own))
    )
    upstream, low_rows = call(layer_back_kernel, units_shape, grad_middle, *parts, hidden)
    in_lower = round_planes(grad_in[1], -1, low_rows)
    in_upper = round_planes(grad_in[2], 1, low_rows)
    line = turn_in_line(low_rows, line_back)
    near_in, far_in = call(
        add_in_kernel,
        [((members // 2 * weight_rows, 3 * width + tile), bf16)] * 2,
        grad_in[0],
        in_lower,
        in_upper,
        in_opposite,
    )
    arrived = toggle(far_in, "core", 1)
    shares_0 = share_chips(pair_chips(near_in, arrived, 1))
    opposite_down = round_planes(planes[4], 2, near_in)
    grad_tokens = turn_in_plane(after(line, arrived))
    output = turn_in_plane(after(output, arrived)).astype(f32)
    grads_ff = [planes[0], ff_lower, ff_upper, opposite_up, opposite_down] + grads_ff
    grad_up, grad_down = finish_ff(after(grads_ff, arrived), ff_in.shape)
    own_out, other_out = call(
        add_out_kernel,
        [(attn_out.shape, f32), (attn_out.shape, bf16)],
        place,
        *after(halves_0 + halves_1, near_in),
        smem=1,
    )
    (grad_attn_out,) = call(
        finish_out_kernel, [(attn_out.shape, f32)], own_out, toggle(other_out, "core", 1)
    )
    own_buckets = table.shape[0] // (z_n * core_n)
    grad_attn_in, grad_gains, ends = call(
        finish_in_kernel,
        [(attn_in.shape, f32), (gains.shape, f32), ((weight_rows, tile), f32)],
        place,
        *shares_0,
        *shares_1,
        attn_in,
        gain_attn,
        smem=1,
    )
    return (
        output[None],
        grad_tokens.astype(f32)[None],
        grad_attn_in,
        grad_attn_out,
        grad_up,
        grad_down,
        grad_gains,
        ends[:own_buckets, 8 : 8 + heads_all // heads_n],
    )


def solution(mesh):
    sizes = dict(mesh.shape)
    cores = 2
    fine = Mesh(
        mesh.devices.reshape(sizes["head"], sizes["blk"] // cores, cores), everyone
    )
    blk = ("z", "core")
    in_specs = (
        P("head", blk, None),
        P(None, blk),
        P(),
        P(None, everyone, None),
        P(None, everyone, None),
        P(None, everyone, None),
        P(None, everyone, None),
        P(None, everyone, None),
        P("head", blk, None),
    )
    out_specs = (
        P("head", blk, None),
        P("head", blk, None),
        P(None, everyone, None),
        P(None, everyone, None),
        P(None, everyone, None),
        P(None, everyone, None),
        P(None, everyone, None),
        P(blk, "head"),
    )
    plane = sizes["head"] == 4 and sizes["blk"] == 8
    local = local_plane if plane else local_general
    return jax.shard_map(local, mesh=fine, in_specs=in_specs, out_specs=out_specs, check_vma=False)
```

```python
import functools

import jax
import jax.numpy as jnp
import numpy as np
from jax import lax
from jax.experimental import pallas as pl
from jax.experimental.pallas import tpu as pltpu
from jax.sharding import Mesh
from jax.sharding import PartitionSpec as P

bounds = (1, 2, 3, 4, 5, 6, 7, 8, 12, 16, 23, 32, 46, 64, 91)
epsilon = 1e-06
masked = -1e30
score_scale = 0.125
head_dim = 64
tile = 128
everyone = ("head", "z", "core")
bf16 = jnp.bfloat16
f32 = jnp.float32


def contract(lhs, rhs, lhs_dim, rhs_dim):
    return lax.dot_general(
        lhs, rhs, (((lhs_dim,), (rhs_dim,)), ((), ())), preferred_element_type=f32
    )


def near_buckets(shape):
    offsets = (
        lax.broadcasted_iota(jnp.int32, shape, 1) - tile - lax.broadcasted_iota(jnp.int32, shape, 0)
    )
    distance = jnp.abs(offsets)
    bucket = jnp.where(offsets > 0, 16, 0)
    for boundary in bounds:
        bucket = bucket + jnp.where(distance >= boundary, 1, 0)
    return bucket


def near_kernel(table, near):
    bucket = near_buckets(near.shape[1:])
    for head in range(near.shape[0]):
        values = jnp.zeros(near.shape[1:], f32)
        for bucket_id in range(table.shape[0]):
            values = jnp.where(bucket == bucket_id, table[bucket_id, head], values)
        near[head] = values


def bucket_kernel(first_lane, near, far, out):
    bucket = near_buckets(near.shape[1:])
    rows = lax.broadcasted_iota(jnp.int32, out.shape, 0)
    lanes = lax.broadcasted_iota(jnp.int32, out.shape, 1)
    total = jnp.zeros(out.shape, f32)
    for head in range(near.shape[0]):
        strip = near[head]
        for bucket_id in range(out.shape[0]):
            value = jnp.sum(jnp.where(bucket == bucket_id, strip, 0.0), axis=0, keepdims=True)
            value = jnp.sum(value, axis=1, keepdims=True)
            if bucket_id in (15, 31):
                value = value + far[head, bucket_id // 16, :1, :1]
            total = jnp.where((rows == bucket_id) & (lanes == head + first_lane[0]), value, total)
    out[...] = total


def fill_band(band, table, near, heads_dev, length):
    for head in range(heads_dev):
        band[head, :, : length - tile] = jnp.full((tile, length - tile), table[15, head], f32)
        band[head, :, length - tile : length + 2 * tile] = near[head]
        band[head, :, length + 2 * tile :] = jnp.full(
            (tile, length - 2 * tile), table[31, head], f32
        )


def band_starts(place, at, length, skip=0):
    return [
        pl.multiple_of(length + (place[skip + block] - place[skip + at]) * tile, tile)
        for block in range(length // tile)
    ]


def attention_kernel(
    heads_dev, length, first, place, table, near, qkv, doc_row, doc_col, out, local, stats, band
):
    step = pl.program_id(0)
    width = heads_dev * head_dim

    @pl.when(step == 0)
    def _():
        fill_band(band, table, near, heads_dev, length)

    row = pl.multiple_of((first[0] + step) * tile, tile)
    out_row = pl.multiple_of((place[first[0] + step] - first[0]) * tile, tile)
    starts = band_starts(place, first[0] + step, length)
    same_doc = doc_col[...] == doc_row[...]
    queries = qkv[pl.ds(row, tile), :width] * bf16(score_scale)
    lanes = lax.broadcasted_iota(jnp.int32, (tile, tile), 1)
    collected = jnp.zeros((tile, tile), f32)
    for head in range(heads_dev):
        own = slice(head * head_dim, (head + 1) * head_dim)
        keys = qkv[:, width + own.start : width + own.stop]
        values = qkv[:, 2 * width + own.start : 2 * width + own.stop]
        scores = contract(queries[:, own], keys, 1, 1)
        scores = scores + jnp.concatenate(
            [band[head, :, pl.ds(start, tile)] for start in starts], axis=1
        )
        scores = jnp.where(same_doc, scores, masked)
        peak = jnp.max(scores, axis=1, keepdims=True)
        weights = jnp.exp(scores - peak)
        total = jnp.sum(weights, axis=1, keepdims=True)
        mixed = contract(weights.astype(bf16), values, 1, 0) / total
        out[pl.ds(out_row, tile), own] = mixed.astype(bf16)
        local[:, own] = mixed.astype(bf16)
        collected = jnp.where(lanes == head, peak + jnp.log(total), collected)
    stats[...] = collected


def attention_back_kernel(
    heads_dev, length, split, first, place, table, near, qkv, doc_row, doc_col, attended, grad_out, stats,
    grad_qkv, grad_near, grad_far, band, grad_band, grad_keys, grad_values,
):
    step = pl.program_id(0)
    width = heads_dev * head_dim

    @pl.when(step == 0)
    def _():
        fill_band(band, table, near, heads_dev, length)
        grad_band[...] = jnp.zeros_like(grad_band)
        grad_keys[...] = jnp.zeros_like(grad_keys)
        grad_values[...] = jnp.zeros_like(grad_values)
        if split > 1:
            grad_qkv[...] = jnp.zeros_like(grad_qkv)

    row = pl.multiple_of((first[0] + step) * tile, tile)
    out_row = pl.multiple_of((place[first[0] + step] - first[0]) * tile, tile)
    starts = band_starts(place, first[0] + step, length)
    same_doc = doc_col[...] == doc_row[...]
    at_step = pl.multiple_of(step * tile, tile)
    queries = qkv[pl.ds(row, tile), :width] * bf16(score_scale)
    for head in range(heads_dev):
        own = slice(head * head_dim, (head + 1) * head_dim)
        keys = qkv[:, width + own.start : width + own.stop]
        values = qkv[:, 2 * width + own.start : 2 * width + own.stop]
        upstream = grad_out[pl.ds(out_row, tile), own]
        scores = contract(queries[:, own], keys, 1, 1) + jnp.concatenate(
            [band[head, :, pl.ds(start, tile)] for start in starts], axis=1
        )
        scores = jnp.where(same_doc, scores, masked)
        weights = jnp.exp(scores - stats[:, head : head + 1])
        delta = jnp.sum(
            upstream.astype(f32) * attended[pl.ds(at_step, tile), own].astype(f32),
            axis=1,
            keepdims=True,
        )
        grad_scores = weights * (contract(upstream, values, 1, 1) - delta)
        for block, start in enumerate(starts):
            grad_band[head, :, pl.ds(start, tile)] += grad_scores[
                :, block * tile : (block + 1) * tile
            ]
        grad_low = grad_scores.astype(bf16)
        grad_values[:, own] += contract(weights.astype(bf16), upstream, 0, 0)
        grad_keys[:, own] += contract(grad_low, queries[:, own], 0, 0)
        grad_qkv[pl.ds(row, tile), own] = (
            contract(grad_low, keys, 1, 0) * score_scale
        ).astype(bf16)

    @pl.when(step == pl.num_programs(0) - 1)
    def _():
        grad_qkv[:, width : 2 * width] = grad_keys[...].astype(bf16)
        grad_qkv[:, 2 * width :] = grad_values[...].astype(bf16)
        for head in range(heads_dev):
            grad_near[head] = grad_band[head, :, length - tile : length + 2 * tile]
            grad_far[head, 0] = jnp.full(
                (8, tile), jnp.sum(grad_band[head, :, : length - tile]), f32
            )
            grad_far[head, 1] = jnp.full(
                (8, tile), jnp.sum(grad_band[head, :, length + 2 * tile :]), f32
            )


def whole(shape):
    return pl.BlockSpec(shape, lambda step: (0,) * len(shape), pipeline_mode=pl.Buffered(1))


def attention(qkv, doc_row, doc_col, first, place, table, near, rows):
    length = qkv.shape[0]
    heads_dev = table.shape[1]
    width = heads_dev * head_dim
    return pl.pallas_call(
        functools.partial(attention_kernel, heads_dev, length),
        grid=(rows // tile,),
        in_specs=[
            pl.BlockSpec(memory_space=pltpu.SMEM),
            pl.BlockSpec(memory_space=pltpu.SMEM),
            pl.BlockSpec(memory_space=pltpu.SMEM),
            whole(near.shape),
            whole(qkv.shape),
            whole(doc_row.shape),
            pl.BlockSpec((tile, 1), lambda step: (step, 0)),
        ],
        out_specs=[
            whole((rows, width)),
            pl.BlockSpec((tile, width), lambda step: (step, 0)),
            pl.BlockSpec((tile, tile), lambda step: (step, 0)),
        ],
        out_shape=[
            jax.ShapeDtypeStruct((rows, width), bf16),
            jax.ShapeDtypeStruct((rows, width), bf16),
            jax.ShapeDtypeStruct((rows, tile), f32),
        ],
        scratch_shapes=[pltpu.VMEM((heads_dev, tile, 2 * length), f32)],
        compiler_params=pltpu.CompilerParams(vmem_limit_bytes=40 * 2**20),
        cost_estimate=pl.CostEstimate(
            flops=4 * rows * length * width,
            bytes_accessed=4 * length * width * 2,
            transcendentals=rows * length * heads_dev,
        ),
    )(first, place, table, near, qkv, doc_row, doc_col)


def attention_back(
    qkv, doc_row, doc_col, attended, grad_out, stats, first, place, table, near, split
):
    length = qkv.shape[0]
    rows = grad_out.shape[0]
    heads_dev = table.shape[1]
    width = heads_dev * head_dim
    return pl.pallas_call(
        functools.partial(attention_back_kernel, heads_dev, length, split),
        grid=(rows // tile,),
        in_specs=[
            pl.BlockSpec(memory_space=pltpu.SMEM),
            pl.BlockSpec(memory_space=pltpu.SMEM),
            pl.BlockSpec(memory_space=pltpu.SMEM),
            whole(near.shape),
            whole(qkv.shape),
            whole(doc_row.shape),
            pl.BlockSpec((tile, 1), lambda step: (step, 0)),
            whole((rows, width)),
            whole((rows, width)),
            pl.BlockSpec((tile, tile), lambda step: (step, 0)),
        ],
        out_specs=[
            whole((length, 3 * width)),
            whole((heads_dev, tile, 3 * tile)),
            whole((heads_dev, 2, 8, tile)),
        ],
        out_shape=[
            jax.ShapeDtypeStruct((length, 3 * width), bf16),
            jax.ShapeDtypeStruct((heads_dev, tile, 3 * tile), f32),
            jax.ShapeDtypeStruct((heads_dev, 2, 8, tile), f32),
        ],
        scratch_shapes=[
            pltpu.VMEM((heads_dev, tile, 2 * length), f32),
            pltpu.VMEM((heads_dev, tile, 2 * length), f32),
            pltpu.VMEM((length, width), f32),
            pltpu.VMEM((length, width), f32),
        ],
        compiler_params=pltpu.CompilerParams(vmem_limit_bytes=48 * 2**20),
        cost_estimate=pl.CostEstimate(
            flops=10 * rows * length * width,
            bytes_accessed=8 * length * width * 2,
            transcendentals=rows * length * heads_dev,
        ),
    )(first, place, table, near, qkv, doc_row, doc_col, attended, grad_out, stats)


def call(kernel, shapes, *operands, smem=0):
    return pl.pallas_call(
        kernel,
        in_specs=[pl.BlockSpec(memory_space=pltpu.SMEM)] * smem
        + [pl.BlockSpec(memory_space=pltpu.VMEM)] * (len(operands) - smem),
        out_specs=[pl.BlockSpec(memory_space=pltpu.VMEM)] * len(shapes),
        out_shape=[jax.ShapeDtypeStruct(shape, kind) for shape, kind in shapes],
        compiler_params=pltpu.CompilerParams(vmem_limit_bytes=10 * 2**20),
    )(*operands)


def share_in_kernel(place, attn_in, gains, near, far):
    layers, rows = attn_in.shape[:2]
    half = near.shape[0] // (layers * rows)
    width = near.shape[1] // 3
    for index in range(2 * half):
        member = place[index]
        for layer_id in range(layers):
            block = jnp.concatenate(
                [
                    attn_in[
                        layer_id,
                        :,
                        pl.ds(pl.multiple_of((part * 2 * half + member) * width, width), width),
                    ]
                    for part in range(3)
                ],
                axis=1,
            )
            at = (index % half * layers + layer_id) * rows
            out = near if index < half else far
            out[at : at + rows] = (block.astype(f32) * gains[layer_id]).astype(bf16)


def join_kernel(*refs):
    shares, outs = refs[:4], refs[4:]
    rows = outs[0].shape[0] // 8
    for chip, share in enumerate(shares):
        for core in range(2):
            for layer_id, out in enumerate(outs):
                source = (core * len(outs) + layer_id) * rows
                target = (chip * 2 + core) * rows
                out[target : target + rows] = share[source : source + rows]


def row_of(chip, plane, core, rows, planes=4):
    return pl.multiple_of(((chip * planes + plane) * 2 + core) * rows, rows)


def assemble_in_kernel(place, own, lower, upper, opposite, out):
    at_z, at_core, at_head = place[8], place[0] % 2, place[0] // 2
    rows = own.shape[0] // 8
    for part, offset in ((own, 0), (lower, 3), (upper, 1), (opposite, 2)):
        plane = (at_z + offset) % 4
        for index in range(8):
            row = row_of(at_head ^ (index // 2), plane, at_core ^ (index % 2), rows)
            out[pl.ds(row, rows)] = part[index * rows : (index + 1) * rows]


def plane_attention_kernel(
    length, place, table, strip, near, far, w_in, *refs
):
    halves, (doc_row, doc_col, w_out, qkv, attended, stats, near_part, far_part, band) = (
        refs[:2], refs[2:],
    )
    step = pl.program_id(0)
    half = length // 2
    heads_dev = table.shape[1]
    width = heads_dev * head_dim

    @pl.when(step == 0)
    def _():
        fill_band(band, table, strip, heads_dev, length)
        swapped = place[length // tile] % 2 == 1
        rows = width // 2
        w_out[:rows] = jnp.where(swapped, halves[1][...], halves[0][...])
        w_out[rows:] = jnp.where(swapped, halves[0][...], halves[1][...])
        qkv[:half] = contract(near[...], w_in[...], 1, 0).astype(bf16)
        qkv[half:] = contract(far[...], w_in[...], 1, 0).astype(bf16)

    row = pl.multiple_of(step * tile, tile)
    starts = band_starts(place, step, length, length // tile + 1)
    same_doc = doc_col[...] == doc_row[...]
    queries = qkv[pl.ds(row, tile), :width] * bf16(score_scale)
    lanes = lax.broadcasted_iota(jnp.int32, (tile, tile), 1)
    collected = jnp.zeros((tile, tile), f32)
    results = []
    for head in range(heads_dev):
        own = slice(head * head_dim, (head + 1) * head_dim)
        keys = qkv[:, width + own.start : width + own.stop]
        values = qkv[:, 2 * width + own.start : 2 * width + own.stop]
        scores = contract(queries[:, own], keys, 1, 1) + jnp.concatenate(
            [band[head, :, pl.ds(start, tile)] for start in starts], axis=1
        )
        scores = jnp.where(same_doc, scores, masked)
        peak = jnp.max(scores, axis=1, keepdims=True)
        weights = jnp.exp(scores - peak)
        total = jnp.sum(weights, axis=1, keepdims=True)
        results.append((contract(weights.astype(bf16), values, 1, 0) / total).astype(bf16))
        collected = jnp.where(lanes == head, peak + jnp.log(total), collected)
    stats[...] = collected
    merged = jnp.concatenate(results, axis=1)
    attended[...] = merged
    part = contract(merged, w_out[...], 1, 0)

    @pl.when(row < half)
    def _():
        near_part[...] = part

    @pl.when(row >= half)
    def _():
        far_part[...] = part.astype(bf16)


def near_block(steps, columns):
    return pl.BlockSpec((tile, columns), lambda step: (jnp.minimum(step, steps // 2 - 1), 0))


def far_block(steps, columns):
    return pl.BlockSpec((tile, columns), lambda step: (jnp.maximum(step - steps // 2, 0), 0))


def plane_attention(near, far, w_in, halves, doc_row, doc_col, place, table, strip):
    length, model_width = 2 * near.shape[0], near.shape[1]
    steps = length // tile
    heads_dev = table.shape[1]
    width = heads_dev * head_dim
    return pl.pallas_call(
        functools.partial(plane_attention_kernel, length),
        grid=(steps,),
        in_specs=[
            pl.BlockSpec(memory_space=pltpu.SMEM),
            pl.BlockSpec(memory_space=pltpu.SMEM),
            whole(strip.shape),
            whole(near.shape),
            whole(far.shape),
            whole(w_in.shape),
            *[whole(half.shape) for half in halves],
            whole(doc_row.shape),
            pl.BlockSpec((tile, 1), lambda step: (step, 0)),
        ],
        out_specs=[
            whole((width, model_width)),
            whole((length, 3 * width)),
            pl.BlockSpec((tile, width), lambda step: (step, 0)),
            pl.BlockSpec((tile, tile), lambda step: (step, 0)),
            near_block(steps, model_width),
            far_block(steps, model_width),
        ],
        out_shape=[
            jax.ShapeDtypeStruct((width, model_width), bf16),
            jax.ShapeDtypeStruct((length, 3 * width), bf16),
            jax.ShapeDtypeStruct((length, width), bf16),
            jax.ShapeDtypeStruct((length, tile), f32),
            jax.ShapeDtypeStruct((length // 2, model_width), f32),
            jax.ShapeDtypeStruct((length // 2, model_width), bf16),
        ],
        scratch_shapes=[pltpu.VMEM((heads_dev, tile, 2 * length), f32)],
        compiler_params=pltpu.CompilerParams(vmem_limit_bytes=14 * 2**20),
        cost_estimate=pl.CostEstimate(
            flops=4 * length * length * width + 8 * length * model_width * width,
            bytes_accessed=12 * 2**20,
            transcendentals=length * length * heads_dev,
        ),
    )(place, table, strip, near, far, w_in, *halves, doc_row, doc_col)


def plane_attention_back_kernel(
    length, place, table, strip, qkv, doc_row, doc_col, attended, stats, near, far, w_in, w_out,
    grad_qkv, grad_near, grad_far, near_part, far_part, *rest
):
    halves, (band, grad_band, grad_keys, grad_values, out_sum) = rest[:2], rest[2:]
    step = pl.program_id(0)
    half = length // 2
    heads_dev = table.shape[1]
    width = heads_dev * head_dim

    @pl.when(step == 0)
    def _():
        fill_band(band, table, strip, heads_dev, length)
        grad_band[...] = jnp.zeros_like(grad_band)
        grad_keys[...] = jnp.zeros_like(grad_keys)
        grad_values[...] = jnp.zeros_like(grad_values)
        out_sum[...] = jnp.zeros_like(out_sum)

    row = pl.multiple_of(step * half, half)
    branch = jnp.where(step == 0, near[...], far[...])
    merged = attended[...]
    grad_merged = contract(branch, w_out[...], 1, 1).astype(bf16)
    out_sum[...] += contract(merged, branch, 0, 0)
    products = grad_merged.astype(f32) * merged.astype(f32)
    queries = qkv[pl.ds(row, half), :width] * bf16(score_scale)
    blocks = half // tile
    for head in range(heads_dev):
        own = slice(head * head_dim, (head + 1) * head_dim)
        keys = qkv[:, width + own.start : width + own.stop]
        values = qkv[:, 2 * width + own.start : 2 * width + own.stop]
        upstream = grad_merged[:, own]
        raw_scores = contract(queries[:, own], keys, 1, 1)
        grad_weights = contract(upstream, values, 1, 1)
        delta = jnp.sum(products[:, own], axis=1, keepdims=True)
        weights_low, grads_low = [], []
        for block in range(blocks):
            lines = slice(block * tile, (block + 1) * tile)
            starts = band_starts(place, step * blocks + block, length, length // tile + 1)
            scores = raw_scores[lines] + jnp.concatenate(
                [band[head, :, pl.ds(start, tile)] for start in starts], axis=1
            )
            scores = jnp.where(doc_col[lines] == doc_row[...], scores, masked)
            weights = jnp.exp(scores - stats[lines, head : head + 1])
            grad_scores = weights * (grad_weights[lines] - delta[lines])
            for index, start in enumerate(starts):
                grad_band[head, :, pl.ds(start, tile)] += grad_scores[
                    :, index * tile : (index + 1) * tile
                ]
            weights_low.append(weights.astype(bf16))
            grads_low.append(grad_scores.astype(bf16))
        weights_low, grads_low = jnp.concatenate(weights_low), jnp.concatenate(grads_low)
        grad_values[:, own] += contract(weights_low, upstream, 0, 0)
        grad_keys[:, own] += contract(grads_low, queries[:, own], 0, 0)
        grad_qkv[pl.ds(row, half), own] = (
            contract(grads_low, keys, 1, 0) * score_scale
        ).astype(bf16)

    @pl.when(step == pl.num_programs(0) - 1)
    def _():
        grad_qkv[:, width : 2 * width] = grad_keys[...].astype(bf16)
        grad_qkv[:, 2 * width :] = grad_values[...].astype(bf16)
        far_part[...] = contract(grad_qkv[half:], w_in[...], 1, 1).astype(bf16)
        near_part[...] = contract(grad_qkv[:half], w_in[...], 1, 1)
        rows = width // 2
        for index, part in enumerate(halves):
            block = index ^ place[length // tile] % 2
            part[...] = out_sum[pl.ds(pl.multiple_of(block * rows, rows), rows)].astype(bf16)
        for head in range(heads_dev):
            grad_near[head] = grad_band[head, :, length - tile : length + 2 * tile]
            grad_far[head, 0] = jnp.full(
                (8, tile), jnp.sum(grad_band[head, :, : length - tile]), f32
            )
            grad_far[head, 1] = jnp.full(
                (8, tile), jnp.sum(grad_band[head, :, length + 2 * tile :]), f32
            )


def plane_attention_back(
    qkv, doc_row, doc_col, attended, stats, near, far, w_in, w_out, place, table, strip
):
    length, model_width = 2 * near.shape[0], near.shape[1]
    half = length // 2
    heads_dev = table.shape[1]
    width = heads_dev * head_dim
    shapes = [
        ((length, 3 * width), bf16),
        ((heads_dev, tile, 3 * tile), f32),
        ((heads_dev, 2, 8, tile), f32),
        ((length // 2, model_width), f32),
        ((length // 2, model_width), bf16),
    ] + [((width // 2, model_width), bf16)] * 2
    return pl.pallas_call(
        functools.partial(plane_attention_back_kernel, length),
        grid=(2,),
        in_specs=[
            pl.BlockSpec(memory_space=pltpu.SMEM),
            pl.BlockSpec(memory_space=pltpu.SMEM),
            whole(strip.shape),
            whole(qkv.shape),
            whole(doc_row.shape),
            pl.BlockSpec((half, 1), lambda step: (step, 0)),
            pl.BlockSpec((half, width), lambda step: (step, 0)),
            pl.BlockSpec((half, tile), lambda step: (step, 0)),
            whole((half, model_width)),
            whole((half, model_width)),
            whole(w_in.shape),
            whole(w_out.shape),
        ],
        out_specs=[whole(shape) for shape, _ in shapes],
        out_shape=[jax.ShapeDtypeStruct(shape, kind) for shape, kind in shapes],
        scratch_shapes=[
            pltpu.VMEM((heads_dev, tile, 2 * length), f32),
            pltpu.VMEM((heads_dev, tile, 2 * length), f32),
            pltpu.VMEM((length, width), f32),
            pltpu.VMEM((length, width), f32),
            pltpu.VMEM((width, model_width), f32),
        ],
        compiler_params=pltpu.CompilerParams(vmem_limit_bytes=32 * 2**20),
        cost_estimate=pl.CostEstimate(
            flops=10 * length * length * width + 10 * length * model_width * width,
            bytes_accessed=12 * 2**20,
            transcendentals=length * length * heads_dev,
        ),
    )(place, table, strip, qkv, doc_row, doc_col, attended, stats, near, far, w_in, w_out)


def gelu_and_slope(pre_act):
    size = jnp.abs(pre_act)
    gauss = jnp.exp(-0.5 * pre_act * pre_act)
    ratio = 1.0 / (1.0 + np.float32(0.3275911 * 0.5**0.5) * size)
    series = np.float32(1.061405429)
    for factor in (-1.453152027, 1.421413741, -0.284496736, 0.254829592):
        series = series * ratio + np.float32(factor)
    tail = 0.5 * series * ratio * gauss
    cumulative = jnp.where(pre_act < 0, tail, 1.0 - tail)
    slope = cumulative + pre_act * gauss * np.float32((2 * np.pi) ** -0.5)
    return pre_act * cumulative, slope


def ff_kernel(rows, pair, activated, slope, part):
    columns = rows.shape[1]
    value, gradient = gelu_and_slope(contract(rows[...], pair[:, :columns], 1, 1))
    activated[...] = value.astype(bf16)
    slope[...] = gradient.astype(bf16)
    part[...] = contract(activated[...], pair[:, columns:], 1, 0).astype(part.dtype)


def ff_first_kernel(rows, *refs):
    parts, (activated, slope, part, pair) = refs[:5], refs[5:]

    @pl.when(pl.program_id(0) == 0)
    def _():
        units, columns = parts[0].shape[0], rows.shape[1]
        for index, ref in enumerate(parts[:3]):
            pair[index * units : (index + 1) * units] = ref[...]
        pair[3 * units :, :columns] = parts[3][...]
        pair[3 * units :, columns:] = parts[4][...]

    ff_kernel(rows, pair, activated, slope, part)


def ff_back_kernel(rows, slope, pair, grad_pre, part):
    columns = rows.shape[1]
    grad_act = contract(rows[...], pair[:, columns:], 1, 1)
    grad_pre[...] = (grad_act * slope[...].astype(f32)).astype(bf16)
    part[...] = contract(grad_pre[...], pair[:, :columns], 1, 0).astype(part.dtype)


def by_rows(kernel, step_rows, row_operands, whole_operands, outs, whole_outs=()):
    rows = row_operands[0].shape[0]
    return pl.pallas_call(
        kernel,
        grid=(rows // step_rows,),
        in_specs=[
            pl.BlockSpec((step_rows, operand.shape[1]), lambda step: (step, 0))
            for operand in row_operands
        ]
        + [whole(operand.shape) for operand in whole_operands],
        out_specs=[pl.BlockSpec((step_rows, columns), lambda step: (step, 0)) for columns, _ in outs]
        + [whole(shape) for shape in whole_outs],
        out_shape=[jax.ShapeDtypeStruct((rows, columns), kind) for columns, kind in outs]
        + [jax.ShapeDtypeStruct(shape, bf16) for shape in whole_outs],
        compiler_params=pltpu.CompilerParams(vmem_limit_bytes=10 * 2**20),
        cost_estimate=pl.CostEstimate(
            flops=4 * rows * outs[0][0] * row_operands[0].shape[1],
            bytes_accessed=6 * 2**20,
            transcendentals=0,
        ),
    )(*row_operands, *whole_operands)


def ff_grads_kernel(
    pre_near, pre_far, act_near, act_far, normed_near, normed_far, low_near, low_far, *outs
):
    columns = normed_near.shape[1]
    units = outs[0].shape[0]
    up = (
        contract(pre_near[...], normed_near[...], 0, 0)
        + contract(pre_far[...], normed_far[...], 0, 0)
    ).astype(bf16)
    down = (
        contract(act_near[...], low_near[...], 0, 0) + contract(act_far[...], low_far[...], 0, 0)
    ).astype(bf16)

    @pl.when(pl.program_id(0) == 0)
    def _():
        for index in range(2):
            block = slice(index * units, (index + 1) * units)
            outs[index][:, :columns] = up[block]
            outs[index][:, columns:] = down[block]

    @pl.when(pl.program_id(0) == 1)
    def _():
        outs[2][:, :columns] = up[:units]
        outs[2][:, columns:] = down[:units]
        outs[3][...] = up[units:]
        outs[4][...] = down[units:]


def ff_grads(pre, act, normed, low):
    rows, hidden_units = pre[0].shape
    columns = normed[0].shape[1]
    shapes = [(hidden_units // 4, 2 * columns)] * 3 + [(hidden_units // 4, columns)] * 2
    return pl.pallas_call(
        ff_grads_kernel,
        grid=(2,),
        in_specs=[pl.BlockSpec((rows, hidden_units // 2), lambda step: (0, step))] * 4
        + [whole((rows, columns))] * 4,
        out_specs=[whole(shape) for shape in shapes],
        out_shape=[jax.ShapeDtypeStruct(shape, bf16) for shape in shapes],
        compiler_params=pltpu.CompilerParams(vmem_limit_bytes=14 * 2**20),
        cost_estimate=pl.CostEstimate(
            flops=8 * rows * hidden_units * columns, bytes_accessed=8 * 2**20, transcendentals=0
        ),
    )(*pre, *act, *normed, *low)


def in_grads_kernel(place, near, far, grad_qkv, *refs):
    ends, outs, (total, extra) = refs[:-6], refs[-6:-2], refs[-2:]
    half = near.shape[0]
    columns = grad_qkv.shape[1]
    total[:, :columns] = (
        contract(near[...], grad_qkv[:half], 0, 0) + contract(far[...], grad_qkv[half:], 0, 0)
    ).astype(bf16)
    rows = outs[0].shape[0] // 8
    if ends:
        gain_0, gain_1, table_0, table_1 = ends
        lines = lax.broadcasted_iota(jnp.int32, (tile, gain_0.shape[1]), 0)
        gains = jnp.where(lines == 0, gain_0[...], jnp.where(lines == 1, gain_1[...], 0.0))
        extra[...] = jnp.transpose(gains)
        table = table_0[...] + table_1[...]
        buckets = table.shape[0] // 8
        blank = jnp.zeros((8 - buckets, tile), f32)
        for block in range(8):
            row = pl.multiple_of((place[0] // 2 * 8 + block) * rows, rows)
            extra[pl.ds(row, 8)] += jnp.concatenate(
                [table[block * buckets : (block + 1) * buckets], blank]
            )
        total[:, columns:] = extra[...].astype(bf16)
    for out, offset in zip(outs, (0, 3, 1, 2)):
        plane = (place[8] + offset) % 4
        for index in range(8):
            owner = place[index]
            row = row_of(owner // 2, plane, owner % 2, rows)
            out[index * rows : (index + 1) * rows] = total[pl.ds(row, rows)]


def in_grads(place, near, far, grad_qkv, *ends):
    columns = grad_qkv.shape[1] + (tile if ends else 0)
    shape = (near.shape[1] // 4, columns)
    return pl.pallas_call(
        in_grads_kernel,
        in_specs=[pl.BlockSpec(memory_space=pltpu.SMEM)]
        + [pl.BlockSpec(memory_space=pltpu.VMEM)] * (3 + len(ends)),
        out_specs=[pl.BlockSpec(memory_space=pltpu.VMEM)] * 4,
        out_shape=[jax.ShapeDtypeStruct(shape, bf16)] * 4,
        scratch_shapes=[
            pltpu.VMEM((near.shape[1], columns), bf16),
            pltpu.VMEM((near.shape[1], tile), f32),
        ],
        compiler_params=pltpu.CompilerParams(vmem_limit_bytes=14 * 2**20),
        cost_estimate=pl.CostEstimate(
            flops=4 * near.shape[0] * near.shape[1] * columns,
            bytes_accessed=4 * 2**20,
            transcendentals=0,
        ),
    )(place, near, far, grad_qkv, *ends)


def add_in_kernel(own, lower, upper, opposite, near, far):
    total = sum_of_four([own, lower, upper, opposite]).astype(bf16)
    half = near.shape[0]
    near[...] = total[:half]
    far[...] = total[half:]


def combine_kernel(near_part, arrived, own, x_part, y_part, xy_part):
    rows = own.shape[0]
    own[...] = near_part[:rows] + arrived[:rows].astype(f32)
    for bits, out in ((1, x_part), (2, y_part), (3, xy_part)):
        block = slice(bits * rows, (bits + 1) * rows)
        out[...] = (near_part[block] + arrived[block].astype(f32)).astype(bf16)


def added(own, x_part, y_part, xy_part):
    return (own[...] + x_part[...].astype(f32)) + (
        y_part[...].astype(f32) + xy_part[...].astype(f32)
    )


def close_kernel(kept, own, x_part, y_part, xy_part, hidden, units):
    total = kept[...] + added(own, x_part, y_part, xy_part)
    hidden[...] = total
    units[...] = (total * inverse_rms(total)).astype(bf16)


def close_gain_kernel(kept, own, x_part, y_part, xy_part, gain, hidden, normed):
    total = kept[...] + added(own, x_part, y_part, xy_part)
    hidden[...] = total
    normed[...] = (total * inverse_rms(total) * gain[...]).astype(bf16)


def widen_kernel(low, out):
    out[...] = low[...].astype(f32)


def last_kernel(kept, own, x_part, y_part, xy_part, hidden):
    hidden[...] = (kept[...] + added(own, x_part, y_part, xy_part)).astype(bf16)


def middle_back_kernel(
    upstream, own, x_part, y_part, xy_part, middle, gain, grad_middle, branch, grad_gain
):
    grad_normed = added(own, x_part, y_part, xy_part)
    inverse = inverse_rms(middle[...])
    grad_gain[...] = jnp.sum(grad_normed * middle[...] * inverse, axis=0, keepdims=True)
    total = upstream[...].astype(f32) + unit_norm_back(
        middle[...], inverse, grad_normed * gain[...]
    )
    grad_middle[...] = total
    branch[...] = total.astype(bf16)


def layer_back_kernel(grad_middle, own, x_part, y_part, xy_part, hidden, upstream, low):
    total = grad_middle[...] + unit_norm_back(
        hidden[...], inverse_rms(hidden[...]), added(own, x_part, y_part, xy_part)
    )
    upstream[...] = total
    low[...] = total.astype(bf16)


def pair_kernel(axis, near, arrived, *outs):
    rows = near.shape[0] // len(outs)
    for index, out in enumerate(outs):
        block = slice(index * rows, (index + 1) * rows)
        if axis == 0:
            out[:rows] = near[block]
            out[rows:] = arrived[block]
        else:
            columns = near.shape[1]
            out[:, :columns] = near[block]
            out[:, columns:] = arrived[block]


def unit_kernel(tokens, hidden, units):
    total = tokens[...].astype(f32)
    hidden[...] = total
    units[...] = (total * inverse_rms(total)).astype(bf16)


def finish_in_kernel(place, *refs):
    chips, (attn_in, gains, grad_in, grad_gain, ends) = refs[:8], refs[8:]
    rows = attn_in.shape[1]
    width = tile
    members = attn_in.shape[2] // (3 * width)
    ends[...] = jnp.zeros_like(ends)
    for layer_id in range(2):
        row_dot = jnp.zeros((rows, 1), f32)
        for index in range(members):
            member = place[index]
            chip = chips[4 * layer_id + index % 4]
            half = chip.shape[1] // 2
            total = chip[:, index // 4 * half : (index // 4 + 1) * half].astype(f32)
            if layer_id == 0:
                ends[...] += total[:, 3 * width :]
            for part in range(3):
                block = total[:, part * width : (part + 1) * width]
                columns = pl.ds(pl.multiple_of((part * members + member) * width, width), width)
                grad_in[layer_id, :, columns] = block * gains[layer_id]
                row_dot = row_dot + jnp.sum(
                    block * attn_in[layer_id, :, columns].astype(f32), axis=1, keepdims=True
                )
        grad_gain[layer_id] = jnp.concatenate(
            [row_dot, ends[:, layer_id : layer_id + 1]], axis=1
        )


def sum_of_four(parts):
    return (parts[0][...].astype(f32) + parts[1][...].astype(f32)) + (
        parts[2][...].astype(f32) + parts[3][...].astype(f32)
    )


def finish_ff_kernel(*refs):
    count = (len(refs) - 3) // 2
    sources, grads, held, done = refs[:count], refs[count : count + 2], refs[count + 2 : -1], refs[-1]
    copies = [
        pltpu.make_async_copy(source, target, done.at[index])
        for index, (source, target) in enumerate(zip(sources, held))
    ]
    for copy in copies:
        copy.start()
    for copy in copies:
        copy.wait()
    refs = held
    columns = grads[0].shape[2]
    for layer_id in range(grads[0].shape[0]):
        parts = refs[5 * layer_id : 5 * layer_id + 5]
        for side, out in enumerate(grads):
            halves = [part.at[:, side * columns : (side + 1) * columns] for part in parts[:3]]
            out[layer_id] = sum_of_four(halves + [parts[3 + side]])


def finish_ff(grads, shape):
    return pl.pallas_call(
        finish_ff_kernel,
        in_specs=[pl.BlockSpec(memory_space=pl.ANY)] * len(grads),
        out_specs=[pl.BlockSpec(memory_space=pltpu.VMEM)] * 2,
        out_shape=[jax.ShapeDtypeStruct(shape, f32)] * 2,
        scratch_shapes=[pltpu.VMEM(grad.shape, bf16) for grad in grads]
        + [pltpu.SemaphoreType.DMA((len(grads),))],
        compiler_params=pltpu.CompilerParams(vmem_limit_bytes=14 * 2**20),
    )(*grads)


def add_out_kernel(place, *refs):
    parts, (own, other) = refs[:-2], refs[-2:]
    for layer_id in range(own.shape[0]):
        total = parts[2 * layer_id][...].astype(f32) + parts[2 * layer_id + 1][...].astype(f32)
        rows = total.shape[0] // 2
        second = place[0] % 2 == 1
        own[layer_id] = jnp.where(second, total[rows:], total[:rows])
        other[layer_id] = jnp.where(second, total[:rows], total[rows:]).astype(bf16)


def finish_out_kernel(own, arrived, out):
    out[...] = own[...] + arrived[...].astype(f32)


def inverse_rms(hidden):
    return lax.rsqrt(jnp.mean(hidden * hidden, axis=-1, keepdims=True) + epsilon)


def prepare(bias_table, first_head, heads_dev):
    table = lax.dynamic_slice_in_dim(bias_table, first_head, heads_dev, 1)
    (near,) = call(near_kernel, [((heads_dev, tile, 3 * tile), f32)], table, smem=1)
    return table, near


def bucket_grads(first_lane, grads, bucket_count):
    (total,) = call(bucket_kernel, [((bucket_count, tile), f32)], first_lane, *grads, smem=1)
    return total


def gelu_parts(pre_act):
    cumulative = 0.5 * (1.0 + lax.erf(pre_act * np.float32(0.5**0.5)))
    slope = cumulative + pre_act * jnp.exp(-0.5 * pre_act * pre_act) * np.float32(
        (2 * np.pi) ** -0.5
    )
    return (pre_act * cumulative).astype(bf16), slope


def unit_norm_back(hidden, inverse, grad_unit):
    unit = hidden * inverse
    return inverse * (grad_unit - unit * jnp.mean(grad_unit * unit, axis=-1, keepdims=True))


def gather_rows(block, axes):
    return lax.all_gather(block, axes, axis=0, tiled=True)


def toggle(array, axis, bits):
    return lax.ppermute(array, axis, [(i, i ^ bits) for i in range(lax.axis_size(axis))])


def shift(array, by):
    planes = lax.axis_size("z")
    return lax.ppermute(array, "z", [(i, (i + by) % planes) for i in range(planes)])


def plane_gather(block, *holds):
    near = jnp.concatenate([block] + [toggle(block, "head", bits) for bits in (1, 2, 3)])
    near, *holds = tie(near, *holds)
    return (near, toggle(near, "core", 1), *holds)


def plane_scatter(near_part, far_part):
    rows, columns = near_part.shape[0] // 4, near_part.shape[1]
    own, *others = call(
        combine_kernel,
        [((rows, columns), f32)] + [((rows, columns), bf16)] * 3,
        near_part,
        toggle(far_part, "core", 1),
    )
    shares = [own] + [toggle(other, "head", bits) for bits, other in zip((1, 2, 3), others)]
    return shares, own


def tie(*arrays):
    return lax.optimization_barrier(arrays)


def after(array, other):
    return lax.optimization_barrier((array, other))[0]


def scatter_sum(partial, axes, members):
    blocks = partial.astype(bf16).reshape(members, -1, partial.shape[1])
    return jnp.sum(lax.all_to_all(blocks, axes, 0, 0, tiled=True).astype(f32), axis=0)


def local_general(tokens, doc_start, bias_table, attn_in, attn_out, ff_in, ff_out, gains, cotangent):
    heads_n, z_n, core_n = (lax.axis_size(axis) for axis in everyone)
    devices = heads_n * z_n * core_n
    group, spare = ("z", "core"), "head"
    ff_group, ff_spare, ff_members = ("head", "core"), "z", heads_n * core_n
    blocks = z_n * core_n
    block_rows, model_width = tokens.shape[1:]
    layer_count, weight_rows = attn_in.shape[:2]
    length = block_rows * blocks
    heads_all = bias_table.shape[1]
    member = lax.axis_index("z") * core_n + lax.axis_index("core")
    heads_dev = max(1, heads_all // blocks)
    head_groups = heads_all // heads_dev
    split = blocks // head_groups
    head_group, query_part = member // split, member % split
    query_rows = length // split
    width = heads_dev * head_dim
    first = (query_part * (query_rows // tile)).astype(jnp.int32).reshape(1)
    place = jnp.arange(length // tile, dtype=jnp.int32)
    out_row = head_group * width

    def swap(array):
        return lax.all_to_all(array, everyone, 0, 0, tiled=True)

    starts = jnp.broadcast_to(
        doc_start.astype(f32)[:, None], (heads_n, blocks, block_rows)
    ).reshape(devices, block_rows)
    ff_gains = gains[:, :, 1].astype(f32).reshape(1, -1)
    small = swap(
        jnp.concatenate(
            [starts, jnp.broadcast_to(ff_gains, (devices, layer_count * weight_rows))], axis=1
        )
    )
    doc_row = small[:blocks, :block_rows].reshape(1, length)
    doc_col = lax.dynamic_slice_in_dim(
        doc_row.reshape(length, 1), query_part * query_rows, query_rows, 0
    )
    gain_ff = jnp.transpose(
        small[:, block_rows:].reshape(devices, layer_count, weight_rows), (1, 0, 2)
    ).reshape(layer_count, 1, model_width)
    table, near = prepare(bias_table, head_group * heads_dev, heads_dev)

    gain_attn = gains[:, :, 0].astype(f32)[:, :, None]
    own_in = attn_in.astype(f32)

    def fetch_in(layer_id):
        scaled = (own_in[layer_id] * gain_attn[layer_id]).astype(bf16)
        columns = jnp.transpose(
            scaled.reshape(weight_rows, 3, head_groups, width), (2, 0, 1, 3)
        ).reshape(head_groups, weight_rows, 3 * width)
        columns = jnp.repeat(columns, split, axis=0)
        columns = jnp.broadcast_to(columns[None], (heads_n, *columns.shape))
        return swap(columns.reshape(devices, weight_rows, 3 * width)).reshape(
            model_width, 3 * width
        )

    def fetch_ff(layer_id):
        pair = jnp.concatenate([ff_in[layer_id], ff_out[layer_id]], axis=1)
        pair = gather_rows(pair, ff_spare)
        return pair[:, :model_width], pair[:, model_width:]

    hidden, upstream = tokens[0].astype(f32), cotangent[0]
    weights_in = [fetch_in(layer_id) for layer_id in range(layer_count)]
    weights_out = lax.dynamic_slice_in_dim(
        lax.all_gather(attn_out, everyone, axis=1, tiled=True), out_row, width, 1
    )
    weights_ff = [fetch_ff(layer_id) for layer_id in range(layer_count)]

    records = []
    for layer_id in range(layer_count):
        w_in, w_out, (w_up, w_down) = (
            weights_in[layer_id], weights_out[layer_id], weights_ff[layer_id],
        )
        inverse = inverse_rms(hidden)
        units = gather_rows((hidden * inverse).astype(bf16), group)
        qkv = jnp.dot(units, w_in, preferred_element_type=f32).astype(bf16)
        attended, _, stats = attention(
            qkv, doc_row, doc_col, first, place, table, near, query_rows
        )
        mixed = jnp.dot(attended, w_out, preferred_element_type=f32)
        if split > 1:
            mixed = lax.dynamic_update_slice_in_dim(
                jnp.zeros((length, model_width), f32), mixed, query_part * query_rows, 0
            )
        middle = hidden + scatter_sum(mixed, group, blocks)
        inverse_ff = inverse_rms(middle)
        normed_ff = gather_rows((middle * inverse_ff * gain_ff[layer_id]).astype(bf16), ff_group)
        activated, slope = gelu_parts(contract(normed_ff, w_up, 1, 1))
        ff_result = jnp.dot(activated, w_down, preferred_element_type=f32)
        records.append(
            (hidden, inverse, units, qkv, attended, stats, middle, inverse_ff, normed_ff,
             activated, slope)
        )
        hidden = middle + scatter_sum(ff_result, ff_group, ff_members)
    output = hidden

    grads_ff, grads_in, grads_out, grads_gain_ff, grads_table = (
        [None] * layer_count for _ in range(5)
    )
    for layer_id in reversed(range(layer_count)):
        w_in, w_out, (w_up, w_down) = (
            weights_in[layer_id], weights_out[layer_id], weights_ff[layer_id],
        )
        (hidden, inverse, units, qkv, attended, stats, middle, inverse_ff, normed_ff,
         activated, slope) = records[layer_id]
        grad_low = gather_rows(upstream.astype(bf16), ff_group)
        grad_pre = (contract(grad_low, w_down, 1, 1) * slope).astype(bf16)
        grad_normed = scatter_sum(
            jnp.dot(grad_pre, w_up, preferred_element_type=f32), ff_group, ff_members
        )
        grad_pair = jnp.concatenate(
            [contract(grad_pre, normed_ff, 0, 0), contract(activated, grad_low, 0, 0)], axis=1
        ).astype(bf16)
        grads_ff[layer_id] = lax.psum_scatter(
            grad_pair, ff_spare, scatter_dimension=0, tiled=True
        ).astype(f32)
        grads_gain_ff[layer_id] = jnp.sum(grad_normed * middle * inverse_ff, axis=0)
        grad_middle = upstream + unit_norm_back(
            middle, inverse_ff, grad_normed * gain_ff[layer_id]
        )
        branch = gather_rows(grad_middle.astype(bf16), group)
        if split > 1:
            branch = lax.dynamic_slice_in_dim(branch, query_part * query_rows, query_rows, 0)
        grad_attended = contract(branch, w_out, 1, 1).astype(bf16)
        grad_qkv, grad_near, grad_far = attention_back(
            qkv, doc_row, doc_col, attended, grad_attended, stats, first, place, table, near, split
        )
        grads_table[layer_id] = (grad_near, grad_far)
        grad_units = scatter_sum(contract(grad_qkv, w_in, 1, 1), group, blocks)
        upstream = grad_middle + unit_norm_back(hidden, inverse, grad_units)
        grad_out = lax.dynamic_update_slice_in_dim(
            jnp.zeros((model_width, model_width), bf16),
            contract(attended, branch, 0, 0).astype(bf16),
            out_row,
            0,
        )
        grads_out[layer_id] = lax.psum_scatter(
            grad_out, everyone, scatter_dimension=0, tiled=True
        ).astype(f32)
        grads_in[layer_id] = contract(units, grad_qkv, 0, 0).astype(bf16)

    bucket_count = table.shape[0]
    grad_table = sum(
        bucket_grads(jnp.zeros((1,), jnp.int32), entry, bucket_count) for entry in grads_table
    )[:, :heads_dev]
    grad_table = lax.dynamic_update_slice_in_dim(
        jnp.zeros((bucket_count, heads_all), f32), grad_table, head_group * heads_dev, 1
    )
    grad_table = jnp.transpose(
        grad_table.reshape(blocks, bucket_count // blocks, heads_n, heads_all // heads_n),
        (2, 0, 1, 3),
    ).reshape(devices, -1)
    grad_gain_ff = jnp.transpose(
        jnp.stack(grads_gain_ff).reshape(layer_count, devices, weight_rows), (1, 0, 2)
    ).reshape(devices, -1)
    ends = jnp.sum(swap(jnp.concatenate([grad_gain_ff, grad_table], axis=1)), axis=0)
    grad_gain_ff = ends[: layer_count * weight_rows].reshape(layer_count, weight_rows)
    grad_bias_table = ends[layer_count * weight_rows :].reshape(
        bucket_count // blocks, heads_all // heads_n
    )
    grads_attn_in, grads_gains = [], []
    for layer_id in range(layer_count):
        parts = swap(grads_in[layer_id].reshape(devices, weight_rows, 3 * width)).astype(f32)
        parts = jnp.sum(parts.reshape(heads_n, blocks, weight_rows, 3 * width), axis=0)
        parts = jnp.sum(parts.reshape(head_groups, split, weight_rows, 3, width), axis=1)
        unit_grad = jnp.transpose(parts, (1, 2, 0, 3)).reshape(weight_rows, 3 * model_width)
        grads_attn_in.append(unit_grad * gain_attn[layer_id])
        grads_gains.append(
            jnp.stack(
                [jnp.sum(unit_grad * own_in[layer_id], axis=1), grad_gain_ff[layer_id]], axis=1
            )
        )
    return (
        output[None],
        upstream[None],
        jnp.stack(grads_attn_in),
        jnp.stack(grads_out),
        jnp.stack([entry[:, :model_width] for entry in grads_ff]),
        jnp.stack([entry[:, model_width:] for entry in grads_ff]),
        jnp.stack(grads_gains),
        grad_bias_table,
    )


def local_plane(tokens, doc_start, bias_table, attn_in, attn_out, ff_in, ff_out, gains, cotangent):
    heads_n, z_n, core_n = (lax.axis_size(axis) for axis in everyone)
    devices = heads_n * z_n * core_n
    at_head, at_z, at_core = (lax.axis_index(axis) for axis in everyone)
    members = heads_n * core_n
    block_rows, model_width = tokens.shape[1:]
    layer_count, weight_rows = attn_in.shape[:2]
    length = block_rows * members
    heads_all = bias_table.shape[1]
    heads_dev = heads_all // members
    width = heads_dev * head_dim
    member = at_head * core_n + at_core
    everywhere = [(h, z, c) for h in range(heads_n) for z in range(z_n) for c in range(core_n)]

    def swapped(bits):
        return bits % 2 * 2 + bits // 2

    def device(h, z, c):
        return (h * z_n + z) * core_n + c

    turn = [(device(h, z, c), device(h ^ swapped(z), h, c)) for h, z, c in everywhere]
    plane_turn = [(device(h, z, c), device(h ^ swapped(z), z, c)) for h, z, c in everywhere]
    line_turn = [(device(h, z, c), device(h, h ^ swapped(z), c)) for h, z, c in everywhere]
    line_back = [(target, source) for source, target in line_turn]
    place = jnp.stack(
        [
            (at_head ^ bits) * core_n + (at_core ^ other)
            for other in range(core_n)
            for bits in range(heads_n)
        ]
        + [at_z]
        + [
            swapped(at_head ^ bits ^ at_z) * core_n + (at_core ^ other)
            for other in range(core_n)
            for bits in range(heads_n)
        ]
    ).astype(jnp.int32)

    def relay(array):
        return lax.ppermute(array, everyone, turn)

    def turn_in_plane(array):
        return lax.ppermute(array, everyone, plane_turn)

    def turn_in_line(array, turns):
        return lax.ppermute(array, everyone, turns)

    def swap(array):
        return lax.all_to_all(array, everyone, 0, 0, tiled=True)

    row_shape = (block_rows, model_width)
    gain_attn = gains[:, :, 0].astype(f32)[:, :, None]
    near_share, far_share = call(
        share_in_kernel,
        [((members // 2 * layer_count * weight_rows, 3 * width), bf16)] * 2,
        place,
        attn_in,
        gain_attn,
        smem=1,
    )

    half_turns = [
        [
            (z * core_n + c, (2 * c + (a ^ z % 2)) * core_n + z // 2)
            for z in range(z_n)
            for c in range(core_n)
        ]
        for a in range(2)
    ]

    def fetch_out(layer_id, hold):
        own = attn_out[layer_id]
        other = toggle(own, "core", 1)
        head = jnp.where(
            at_core == 0, jnp.concatenate([own, other]), jnp.concatenate([other, own])
        )
        head = after(head, hold)
        return [
            lax.ppermute(head, ("z", "core"), [(holder, user) for user, holder in turns])
            for turns in half_turns
        ]

    def owners_halves(halves):
        return [
            lax.ppermute(half, ("z", "core"), turns) for half, turns in zip(halves, half_turns)
        ]

    def pair_chips(near, arrived, axis):
        rows, columns = near.shape[0] // 4, near.shape[1]
        shape = (2 * rows, columns) if axis == 0 else (rows, 2 * columns)
        return call(functools.partial(pair_kernel, axis), [(shape, bf16)] * 4, near, arrived)

    def share_chips(blocks):
        return [blocks[0]] + [toggle(blocks[bits], "head", bits) for bits in (1, 2, 3)]

    units_shape = [(row_shape, f32), (row_shape, bf16)]

    starts = jnp.broadcast_to(
        doc_start.astype(f32)[None, :, None], (heads_n, z_n, core_n, block_rows)
    )
    ff_gains = gains[:, :, 1].astype(f32).reshape(1, -1)
    small = jnp.concatenate(
        [
            starts.reshape(devices, block_rows),
            jnp.broadcast_to(ff_gains, (devices, layer_count * weight_rows)),
        ],
        axis=1,
    )
    table, strip = prepare(bias_table, member * heads_dev, heads_dev)
    hidden = relay(tokens[0])
    hidden, shares, halves, small = tie(
        hidden,
        share_chips(pair_chips(near_share, toggle(far_share, "core", 1), 0)),
        fetch_out(0, near_share),
        swap(after(small, near_share)),
    )
    hidden, unit_rows = call(unit_kernel, units_shape, hidden)
    doc_row = small[:members, :block_rows].reshape(2, 2, core_n, block_rows)
    at_block = swapped(at_head ^ at_z)
    for axis, bit in ((0, at_block // 2), (1, at_block % 2), (2, at_core)):
        doc_row = jnp.where(bit == 1, jnp.flip(doc_row, axis), doc_row)
    doc_row = jnp.transpose(doc_row, (2, 1, 0, 3)).reshape(1, length)
    doc_col = doc_row.reshape(length, 1)
    gain_ff = jnp.transpose(
        small[:, block_rows:].reshape(devices, layer_count, weight_rows), (1, 0, 2)
    ).reshape(layer_count, 1, model_width)

    def round_planes(array, by, hold):
        return shift(after(array, hold), by)

    ff_pairs = [
        jnp.concatenate([ff_in[layer_id], ff_out[layer_id]], axis=1) for layer_id in range(layer_count)
    ]

    def ff_both(kernel, row_operands, pair, columns):
        return zip(
            *(
                by_rows(
                    kernel,
                    256,
                    operands,
                    [pair],
                    [(pair.shape[0], bf16)] * columns + [(model_width, kind)],
                )
                for operands, kind in zip(zip(*row_operands), (f32, bf16))
            )
        )

    def ff_forward(normed, *parts):
        units = 4 * parts[0].shape[0]
        outs = [(units, bf16), (units, bf16)]
        *near, pair = by_rows(
            ff_first_kernel,
            256,
            [normed[0]],
            parts,
            outs + [(model_width, f32)],
            [(units, 2 * model_width)],
        )
        far = by_rows(ff_kernel, 256, [normed[1]], [pair], outs + [(model_width, bf16)])
        return pair, *zip(near, far)

    def ff_backward(low, slopes, pair):
        return ff_both(ff_back_kernel, [low, slopes], pair, 1)

    def assemble_in(share, lower, upper, opposite):
        return call(
            assemble_in_kernel,
            [((model_width, 3 * width), bf16)],
            place,
            share,
            lower,
            upper,
            opposite,
            smem=1,
        )[0]

    share, later_share = call(
        join_kernel, [((members * weight_rows, 3 * width), bf16)] * layer_count, *shares
    )
    near, far, lower, upper, opposite, cotangent_low, strip, doc_row, doc_col, gain_ff, *ff_pairs = plane_gather(
        unit_rows,
        shift(share, 1),
        shift(share, -1),
        shift(share, 2),
        cotangent[0].astype(bf16),
        strip,
        doc_row,
        doc_col,
        gain_ff,
        *ff_pairs,
    )
    w_in = assemble_in(share, lower, upper, opposite)
    units = (near, far)
    w_out, qkv, attended, stats, *parts = plane_attention(
        *units, w_in, halves, doc_row, doc_col, place, table, strip
    )
    halves_1 = fetch_out(1, near)
    parts, lower, upper, cotangent_low, first_half = tie(
        parts,
        round_planes(ff_pairs[0], 1, near),
        round_planes(ff_pairs[0], -1, near),
        turn_in_plane(cotangent_low),
        halves_1[0],
    )
    parts, own = plane_scatter(*parts)
    parts, opposite_in = tie(parts, round_planes(ff_in[0], 2, own))
    middle, normed_rows = call(close_gain_kernel, units_shape, hidden, *parts, gain_ff[0])
    *normed, opposite_out = plane_gather(normed_rows, round_planes(ff_out[0], 2, normed_rows))
    pair, acts, slopes, parts = ff_forward(
        normed, ff_pairs[0], lower, upper, opposite_in, opposite_out
    )
    records = [
        (hidden, units, w_in, w_out, pair, qkv, attended, stats, middle, normed, acts, slopes)
    ]
    parts, lower, upper = tie(
        parts,
        round_planes(later_share, 1, normed[0]),
        round_planes(later_share, -1, normed[0]),
    )
    parts, own = plane_scatter(*parts)
    parts, opposite, upstream = tie(
        parts, round_planes(later_share, 2, own), turn_in_line(after(cotangent_low, own), line_turn)
    )
    shares = [later_share, lower, upper, opposite]
    hidden, unit_rows = call(close_kernel, units_shape, middle, *parts)

    near, far, lower, second_half = plane_gather(
        unit_rows, round_planes(ff_pairs[1], 1, unit_rows), fetch_out(1, unit_rows)[1]
    )
    halves = [first_half, second_half]
    units = (near, far)
    w_in = assemble_in(*shares)
    w_out, qkv, attended, stats, *parts = plane_attention(
        *units, w_in, halves, doc_row, doc_col, place, table, strip
    )
    low = plane_gather(after(upstream, far))
    parts, near_low, upper = tie(parts, low[0], round_planes(ff_pairs[1], -1, far))
    low = (near_low, low[1])
    parts, own = plane_scatter(*parts)
    parts, opposite_in = tie(parts, round_planes(ff_in[1], 2, own))
    middle, normed_rows = call(close_gain_kernel, units_shape, hidden, *parts, gain_ff[1])
    *normed, opposite_out = plane_gather(normed_rows, round_planes(ff_out[1], 2, normed_rows))
    pair, acts, slopes, last_parts = ff_forward(
        normed, ff_pairs[1], lower, upper, opposite_in, opposite_out
    )
    records.append(
        (hidden, units, w_in, w_out, pair, qkv, attended, stats, middle, normed, acts, slopes)
    )

    def back_to_middle(parts, upstream, middle, gain):
        return call(
            middle_back_kernel, units_shape + [((1, model_width), f32)], upstream, *parts, middle, gain
        )

    def attention_grads(record, branch):
        _, _, w_in, w_out, _, qkv, attended, stats, *_ = record
        grad_qkv, grad_near, grad_far, near_part, far_part, *halves = plane_attention_back(
            qkv, doc_row, doc_col, attended, stats, *branch, w_in, w_out, place, table, strip
        )
        return grad_qkv, (grad_near, grad_far), (near_part, far_part), halves

    def table_grads(near_and_far):
        return bucket_grads(at_core.reshape(1) * heads_dev + 8, near_and_far, table.shape[0])

    record = records[1]
    hidden, units, _, _, pair, *_, middle, normed, acts, slopes = record
    pres, parts = ff_backward(low, slopes, pair)
    parts, own = plane_scatter(*parts)
    planes = ff_grads(after(pres, own), acts, normed, low)
    parts, ff_lower = tie(parts, shift(planes[1], -1))
    last_parts, _ = plane_scatter(*after(last_parts, parts))
    grad_middle, branch_rows, gain_1 = back_to_middle(parts, upstream, middle, gain_ff[1])
    *branch, ff_upper = plane_gather(branch_rows, round_planes(planes[2], 1, branch_rows))
    grad_qkv, strips_1, parts, halves_1 = attention_grads(record, branch)
    parts, last_parts, opposite_up = tie(
        parts, last_parts, round_planes(planes[3], 2, branch[1])
    )
    parts, own = plane_scatter(*parts)
    parts, opposite_down, output = tie(
        parts,
        round_planes(planes[4], 2, own),
        call(last_kernel, [(row_shape, bf16)], middle, *after(last_parts, own))[0],
    )
    grads_ff = [planes[0], ff_lower, ff_upper, opposite_up, opposite_down]
    upstream, low_rows = call(layer_back_kernel, units_shape, grad_middle, *parts, hidden)

    record = records[0]
    hidden, units, _, _, pair, *_, middle, normed, acts, slopes = record
    grad_in = in_grads(place, *records[1][1], after(grad_qkv, low_rows))
    *low, in_opposite, in_upper, table_1 = plane_gather(
        low_rows, shift(grad_in[3], 2), shift(grad_in[2], 1), table_grads(after(strips_1, low_rows))
    )
    pres, parts = ff_backward(low, slopes, pair)
    parts, in_lower = tie(parts, round_planes(grad_in[1], -1, low[0]))
    parts, own = plane_scatter(*parts)
    planes = ff_grads(after(pres, own), acts, normed, low)
    near_in, far_in = call(
        add_in_kernel,
        [((members // 2 * weight_rows, 3 * width), bf16)] * 2,
        *after([grad_in[0], in_lower, in_upper, in_opposite], own),
    )
    parts, ff_lower, first_half, arrived = tie(
        parts,
        shift(planes[1], -1),
        owners_halves(after(halves_1, own))[0],
        toggle(far_in, "core", 1),
    )
    grad_middle, branch_rows, gain_0 = back_to_middle(parts, upstream, middle, gain_ff[0])
    *branch, ff_upper, second_half, shares_1 = plane_gather(
        branch_rows,
        round_planes(planes[2], 1, branch_rows),
        owners_halves(after(halves_1, branch_rows))[1],
        pair_chips(near_in, after(arrived, branch_rows), 1),
    )
    halves_1 = [first_half, second_half]
    grad_qkv, strips_0, parts, halves_0 = attention_grads(record, branch)
    parts, shares_1, output, opposite_up = tie(
        parts,
        share_chips(after(shares_1, branch[1])), turn_in_line(after(output, branch[1]), line_back), round_planes(planes[3], 2, branch[1])
    )
    parts, own = plane_scatter(*parts)
    table_0 = table_grads(after(strips_0, own))
    grad_in = in_grads(
        place, *units, after(grad_qkv, own), gain_0, gain_1, table_0, table_1
    )
    parts, in_opposite, halves_0 = tie(
        parts, shift(grad_in[3], 2), owners_halves(after(halves_0, own))
    )
    upstream, low_rows = call(layer_back_kernel, units_shape, grad_middle, *parts, hidden)
    in_lower = round_planes(grad_in[1], -1, low_rows)
    in_upper = round_planes(grad_in[2], 1, low_rows)
    line = turn_in_line(low_rows, line_back)
    near_in, far_in = call(
        add_in_kernel,
        [((members // 2 * weight_rows, 3 * width + tile), bf16)] * 2,
        grad_in[0],
        in_lower,
        in_upper,
        in_opposite,
    )
    arrived = toggle(far_in, "core", 1)
    shares_0 = share_chips(pair_chips(near_in, arrived, 1))
    opposite_down = round_planes(planes[4], 2, near_in)
    grad_tokens = turn_in_plane(after(line, shares_0[1]))
    output = turn_in_plane(after(output, shares_0[1]))
    (output,) = call(widen_kernel, [(row_shape, f32)], output)
    (grad_tokens,) = call(widen_kernel, [(row_shape, f32)], grad_tokens)
    grads_ff = [planes[0], ff_lower, ff_upper, opposite_up, opposite_down] + grads_ff
    grad_up, grad_down = finish_ff(after(grads_ff, shares_0[1]), ff_in.shape)
    own_out, other_out = call(
        add_out_kernel,
        [(attn_out.shape, f32), (attn_out.shape, bf16)],
        place,
        *after(halves_0 + halves_1, shares_0[1]),
        smem=1,
    )
    (grad_attn_out,) = call(
        finish_out_kernel, [(attn_out.shape, f32)], own_out, toggle(other_out, "core", 1)
    )
    own_buckets = table.shape[0] // (z_n * core_n)
    grad_attn_in, grad_gains, ends = call(
        finish_in_kernel,
        [(attn_in.shape, f32), (gains.shape, f32), ((weight_rows, tile), f32)],
        place,
        *shares_0,
        *shares_1,
        attn_in,
        gain_attn,
        smem=1,
    )
    return (
        output[None],
        grad_tokens[None],
        grad_attn_in,
        grad_attn_out,
        grad_up,
        grad_down,
        grad_gains,
        ends[:own_buckets, 8 : 8 + heads_all // heads_n],
    )


def solution(mesh):
    sizes = dict(mesh.shape)
    cores = 2
    fine = Mesh(
        mesh.devices.reshape(sizes["head"], sizes["blk"] // cores, cores), everyone
    )
    blk = ("z", "core")
    in_specs = (
        P("head", blk, None),
        P(None, blk),
        P(),
        P(None, everyone, None),
        P(None, everyone, None),
        P(None, everyone, None),
        P(None, everyone, None),
        P(None, everyone, None),
        P("head", blk, None),
    )
    out_specs = (
        P("head", blk, None),
        P("head", blk, None),
        P(None, everyone, None),
        P(None, everyone, None),
        P(None, everyone, None),
        P(None, everyone, None),
        P(None, everyone, None),
        P(blk, "head"),
    )
    plane = sizes["head"] == 4 and sizes["blk"] == 8
    local = local_plane if plane else local_general
    return jax.shard_map(local, mesh=fine, in_specs=in_specs, out_specs=out_specs, check_vma=False)
```

```python
import functools

import jax
import jax.numpy as jnp
import numpy as np
from jax import lax
from jax.experimental import pallas as pl
from jax.experimental.pallas import tpu as pltpu
from jax.sharding import Mesh
from jax.sharding import PartitionSpec as P

bounds = (1, 2, 3, 4, 5, 6, 7, 8, 12, 16, 23, 32, 46, 64, 91)
epsilon = 1e-06
masked = -1e30
score_scale = 0.125
head_dim = 64
tile = 128
everyone = ("head", "z", "core")
bf16 = jnp.bfloat16
f32 = jnp.float32


def contract(lhs, rhs, lhs_dim, rhs_dim):
    return lax.dot_general(
        lhs, rhs, (((lhs_dim,), (rhs_dim,)), ((), ())), preferred_element_type=f32
    )


def near_buckets(shape):
    offsets = (
        lax.broadcasted_iota(jnp.int32, shape, 1) - tile - lax.broadcasted_iota(jnp.int32, shape, 0)
    )
    distance = jnp.abs(offsets)
    bucket = jnp.where(offsets > 0, 16, 0)
    for boundary in bounds:
        bucket = bucket + jnp.where(distance >= boundary, 1, 0)
    return bucket


def near_kernel(table, near):
    bucket = near_buckets(near.shape[1:])
    for head in range(near.shape[0]):
        values = jnp.zeros(near.shape[1:], f32)
        for bucket_id in range(table.shape[0]):
            values = jnp.where(bucket == bucket_id, table[bucket_id, head], values)
        near[head] = values


def bucket_kernel(first_lane, near, far, out):
    bucket = near_buckets(near.shape[1:])
    rows = lax.broadcasted_iota(jnp.int32, out.shape, 0)
    lanes = lax.broadcasted_iota(jnp.int32, out.shape, 1)
    total = jnp.zeros(out.shape, f32)
    for head in range(near.shape[0]):
        strip = near[head]
        for bucket_id in range(out.shape[0]):
            value = jnp.sum(jnp.where(bucket == bucket_id, strip, 0.0), axis=0, keepdims=True)
            value = jnp.sum(value, axis=1, keepdims=True)
            if bucket_id in (15, 31):
                value = value + far[head, bucket_id // 16, :1, :1]
            total = jnp.where((rows == bucket_id) & (lanes == head + first_lane[0]), value, total)
    out[...] = total


def fill_band(band, table, near, heads_dev, length):
    for head in range(heads_dev):
        band[head, :, : length - tile] = jnp.full((tile, length - tile), table[15, head], f32)
        band[head, :, length - tile : length + 2 * tile] = near[head]
        band[head, :, length + 2 * tile :] = jnp.full(
            (tile, length - 2 * tile), table[31, head], f32
        )


def band_starts(place, at, length, skip=0):
    return [
        pl.multiple_of(length + (place[skip + block] - place[skip + at]) * tile, tile)
        for block in range(length // tile)
    ]


def attention_kernel(
    heads_dev, length, first, place, table, near, qkv, doc_row, doc_col, out, local, stats, band
):
    step = pl.program_id(0)
    width = heads_dev * head_dim

    @pl.when(step == 0)
    def _():
        fill_band(band, table, near, heads_dev, length)

    row = pl.multiple_of((first[0] + step) * tile, tile)
    out_row = pl.multiple_of((place[first[0] + step] - first[0]) * tile, tile)
    starts = band_starts(place, first[0] + step, length)
    same_doc = doc_col[...] == doc_row[...]
    queries = qkv[pl.ds(row, tile), :width] * bf16(score_scale)
    lanes = lax.broadcasted_iota(jnp.int32, (tile, tile), 1)
    collected = jnp.zeros((tile, tile), f32)
    for head in range(heads_dev):
        own = slice(head * head_dim, (head + 1) * head_dim)
        keys = qkv[:, width + own.start : width + own.stop]
        values = qkv[:, 2 * width + own.start : 2 * width + own.stop]
        scores = contract(queries[:, own], keys, 1, 1)
        scores = scores + jnp.concatenate(
            [band[head, :, pl.ds(start, tile)] for start in starts], axis=1
        )
        scores = jnp.where(same_doc, scores, masked)
        peak = jnp.max(scores, axis=1, keepdims=True)
        weights = jnp.exp(scores - peak)
        total = jnp.sum(weights, axis=1, keepdims=True)
        mixed = contract(weights.astype(bf16), values, 1, 0) / total
        out[pl.ds(out_row, tile), own] = mixed.astype(bf16)
        local[:, own] = mixed.astype(bf16)
        collected = jnp.where(lanes == head, peak + jnp.log(total), collected)
    stats[...] = collected


def attention_back_kernel(
    heads_dev, length, split, first, place, table, near, qkv, doc_row, doc_col, attended, grad_out, stats,
    grad_qkv, grad_near, grad_far, band, grad_band, grad_keys, grad_values,
):
    step = pl.program_id(0)
    width = heads_dev * head_dim

    @pl.when(step == 0)
    def _():
        fill_band(band, table, near, heads_dev, length)
        grad_band[...] = jnp.zeros_like(grad_band)
        grad_keys[...] = jnp.zeros_like(grad_keys)
        grad_values[...] = jnp.zeros_like(grad_values)
        if split > 1:
            grad_qkv[...] = jnp.zeros_like(grad_qkv)

    row = pl.multiple_of((first[0] + step) * tile, tile)
    out_row = pl.multiple_of((place[first[0] + step] - first[0]) * tile, tile)
    starts = band_starts(place, first[0] + step, length)
    same_doc = doc_col[...] == doc_row[...]
    at_step = pl.multiple_of(step * tile, tile)
    queries = qkv[pl.ds(row, tile), :width] * bf16(score_scale)
    for head in range(heads_dev):
        own = slice(head * head_dim, (head + 1) * head_dim)
        keys = qkv[:, width + own.start : width + own.stop]
        values = qkv[:, 2 * width + own.start : 2 * width + own.stop]
        upstream = grad_out[pl.ds(out_row, tile), own]
        scores = contract(queries[:, own], keys, 1, 1) + jnp.concatenate(
            [band[head, :, pl.ds(start, tile)] for start in starts], axis=1
        )
        scores = jnp.where(same_doc, scores, masked)
        weights = jnp.exp(scores - stats[:, head : head + 1])
        delta = jnp.sum(
            upstream.astype(f32) * attended[pl.ds(at_step, tile), own].astype(f32),
            axis=1,
            keepdims=True,
        )
        grad_scores = weights * (contract(upstream, values, 1, 1) - delta)
        for block, start in enumerate(starts):
            grad_band[head, :, pl.ds(start, tile)] += grad_scores[
                :, block * tile : (block + 1) * tile
            ]
        grad_low = grad_scores.astype(bf16)
        grad_values[:, own] += contract(weights.astype(bf16), upstream, 0, 0)
        grad_keys[:, own] += contract(grad_low, queries[:, own], 0, 0)
        grad_qkv[pl.ds(row, tile), own] = (
            contract(grad_low, keys, 1, 0) * score_scale
        ).astype(bf16)

    @pl.when(step == pl.num_programs(0) - 1)
    def _():
        grad_qkv[:, width : 2 * width] = grad_keys[...].astype(bf16)
        grad_qkv[:, 2 * width :] = grad_values[...].astype(bf16)
        for head in range(heads_dev):
            grad_near[head] = grad_band[head, :, length - tile : length + 2 * tile]
            grad_far[head, 0] = jnp.full(
                (8, tile), jnp.sum(grad_band[head, :, : length - tile]), f32
            )
            grad_far[head, 1] = jnp.full(
                (8, tile), jnp.sum(grad_band[head, :, length + 2 * tile :]), f32
            )


def whole(shape):
    return pl.BlockSpec(shape, lambda step: (0,) * len(shape), pipeline_mode=pl.Buffered(1))


def attention(qkv, doc_row, doc_col, first, place, table, near, rows):
    length = qkv.shape[0]
    heads_dev = table.shape[1]
    width = heads_dev * head_dim
    return pl.pallas_call(
        functools.partial(attention_kernel, heads_dev, length),
        grid=(rows // tile,),
        in_specs=[
            pl.BlockSpec(memory_space=pltpu.SMEM),
            pl.BlockSpec(memory_space=pltpu.SMEM),
            pl.BlockSpec(memory_space=pltpu.SMEM),
            whole(near.shape),
            whole(qkv.shape),
            whole(doc_row.shape),
            pl.BlockSpec((tile, 1), lambda step: (step, 0)),
        ],
        out_specs=[
            whole((rows, width)),
            pl.BlockSpec((tile, width), lambda step: (step, 0)),
            pl.BlockSpec((tile, tile), lambda step: (step, 0)),
        ],
        out_shape=[
            jax.ShapeDtypeStruct((rows, width), bf16),
            jax.ShapeDtypeStruct((rows, width), bf16),
            jax.ShapeDtypeStruct((rows, tile), f32),
        ],
        scratch_shapes=[pltpu.VMEM((heads_dev, tile, 2 * length), f32)],
        compiler_params=pltpu.CompilerParams(vmem_limit_bytes=40 * 2**20),
        cost_estimate=pl.CostEstimate(
            flops=4 * rows * length * width,
            bytes_accessed=4 * length * width * 2,
            transcendentals=rows * length * heads_dev,
        ),
    )(first, place, table, near, qkv, doc_row, doc_col)


def attention_back(
    qkv, doc_row, doc_col, attended, grad_out, stats, first, place, table, near, split
):
    length = qkv.shape[0]
    rows = grad_out.shape[0]
    heads_dev = table.shape[1]
    width = heads_dev * head_dim
    return pl.pallas_call(
        functools.partial(attention_back_kernel, heads_dev, length, split),
        grid=(rows // tile,),
        in_specs=[
            pl.BlockSpec(memory_space=pltpu.SMEM),
            pl.BlockSpec(memory_space=pltpu.SMEM),
            pl.BlockSpec(memory_space=pltpu.SMEM),
            whole(near.shape),
            whole(qkv.shape),
            whole(doc_row.shape),
            pl.BlockSpec((tile, 1), lambda step: (step, 0)),
            whole((rows, width)),
            whole((rows, width)),
            pl.BlockSpec((tile, tile), lambda step: (step, 0)),
        ],
        out_specs=[
            whole((length, 3 * width)),
            whole((heads_dev, tile, 3 * tile)),
            whole((heads_dev, 2, 8, tile)),
        ],
        out_shape=[
            jax.ShapeDtypeStruct((length, 3 * width), bf16),
            jax.ShapeDtypeStruct((heads_dev, tile, 3 * tile), f32),
            jax.ShapeDtypeStruct((heads_dev, 2, 8, tile), f32),
        ],
        scratch_shapes=[
            pltpu.VMEM((heads_dev, tile, 2 * length), f32),
            pltpu.VMEM((heads_dev, tile, 2 * length), f32),
            pltpu.VMEM((length, width), f32),
            pltpu.VMEM((length, width), f32),
        ],
        compiler_params=pltpu.CompilerParams(vmem_limit_bytes=48 * 2**20),
        cost_estimate=pl.CostEstimate(
            flops=10 * rows * length * width,
            bytes_accessed=8 * length * width * 2,
            transcendentals=rows * length * heads_dev,
        ),
    )(first, place, table, near, qkv, doc_row, doc_col, attended, grad_out, stats)


def call(kernel, shapes, *operands, smem=0):
    return pl.pallas_call(
        kernel,
        in_specs=[pl.BlockSpec(memory_space=pltpu.SMEM)] * smem
        + [pl.BlockSpec(memory_space=pltpu.VMEM)] * (len(operands) - smem),
        out_specs=[pl.BlockSpec(memory_space=pltpu.VMEM)] * len(shapes),
        out_shape=[jax.ShapeDtypeStruct(shape, kind) for shape, kind in shapes],
        compiler_params=pltpu.CompilerParams(vmem_limit_bytes=10 * 2**20),
    )(*operands)


def share_in_kernel(place, attn_in, gains, near, far):
    layers, rows = attn_in.shape[:2]
    half = near.shape[0] // (layers * rows)
    width = near.shape[1] // 3
    for index in range(2 * half):
        member = place[index]
        for layer_id in range(layers):
            block = jnp.concatenate(
                [
                    attn_in[
                        layer_id,
                        :,
                        pl.ds(pl.multiple_of((part * 2 * half + member) * width, width), width),
                    ]
                    for part in range(3)
                ],
                axis=1,
            )
            at = (index % half * layers + layer_id) * rows
            out = near if index < half else far
            out[at : at + rows] = (block.astype(f32) * gains[layer_id]).astype(bf16)


def join_kernel(*refs):
    shares, outs = refs[:4], refs[4:]
    rows = outs[0].shape[0] // 8
    for chip, share in enumerate(shares):
        for core in range(2):
            for layer_id, out in enumerate(outs):
                source = (core * len(outs) + layer_id) * rows
                target = (chip * 2 + core) * rows
                out[target : target + rows] = share[source : source + rows]


def row_of(chip, plane, core, rows, planes=4):
    return pl.multiple_of(((chip * planes + plane) * 2 + core) * rows, rows)


def assemble_in_kernel(place, own, lower, upper, opposite, out):
    at_z, at_core, at_head = place[8], place[0] % 2, place[0] // 2
    rows = own.shape[0] // 8
    for part, offset in ((own, 0), (lower, 3), (upper, 1), (opposite, 2)):
        plane = (at_z + offset) % 4
        for index in range(8):
            row = row_of(at_head ^ (index // 2), plane, at_core ^ (index % 2), rows)
            out[pl.ds(row, rows)] = part[index * rows : (index + 1) * rows]


def plane_attention_kernel(
    length, place, table, strip, near, far, w_in, *refs
):
    halves, (doc_row, doc_col, w_out, qkv, attended, stats, near_part, far_part, band) = (
        refs[:2], refs[2:],
    )
    step = pl.program_id(0)
    half = length // 2
    heads_dev = table.shape[1]
    width = heads_dev * head_dim

    @pl.when(step == 0)
    def _():
        fill_band(band, table, strip, heads_dev, length)
        swapped = place[length // tile] % 2 == 1
        rows = width // 2
        w_out[:rows] = jnp.where(swapped, halves[1][...], halves[0][...])
        w_out[rows:] = jnp.where(swapped, halves[0][...], halves[1][...])
        qkv[:half] = contract(near[...], w_in[...], 1, 0).astype(bf16)
        qkv[half:] = contract(far[...], w_in[...], 1, 0).astype(bf16)

    row = pl.multiple_of(step * tile, tile)
    starts = band_starts(place, step, length, length // tile + 1)
    same_doc = doc_col[...] == doc_row[...]
    queries = qkv[pl.ds(row, tile), :width] * bf16(score_scale)
    lanes = lax.broadcasted_iota(jnp.int32, (tile, tile), 1)
    collected = jnp.zeros((tile, tile), f32)
    results = []
    for head in range(heads_dev):
        own = slice(head * head_dim, (head + 1) * head_dim)
        keys = qkv[:, width + own.start : width + own.stop]
        values = qkv[:, 2 * width + own.start : 2 * width + own.stop]
        scores = contract(queries[:, own], keys, 1, 1) + jnp.concatenate(
            [band[head, :, pl.ds(start, tile)] for start in starts], axis=1
        )
        scores = jnp.where(same_doc, scores, masked)
        peak = jnp.max(scores, axis=1, keepdims=True)
        weights = jnp.exp(scores - peak)
        total = jnp.sum(weights, axis=1, keepdims=True)
        results.append((contract(weights.astype(bf16), values, 1, 0) / total).astype(bf16))
        collected = jnp.where(lanes == head, peak + jnp.log(total), collected)
    stats[...] = collected
    merged = jnp.concatenate(results, axis=1)
    attended[...] = merged
    part = contract(merged, w_out[...], 1, 0)

    @pl.when(row < half)
    def _():
        near_part[...] = part

    @pl.when(row >= half)
    def _():
        far_part[...] = part.astype(bf16)


def near_block(steps, columns):
    return pl.BlockSpec((tile, columns), lambda step: (jnp.minimum(step, steps // 2 - 1), 0))


def far_block(steps, columns):
    return pl.BlockSpec((tile, columns), lambda step: (jnp.maximum(step - steps // 2, 0), 0))


def plane_attention(near, far, w_in, halves, doc_row, doc_col, place, table, strip):
    length, model_width = 2 * near.shape[0], near.shape[1]
    steps = length // tile
    heads_dev = table.shape[1]
    width = heads_dev * head_dim
    return pl.pallas_call(
        functools.partial(plane_attention_kernel, length),
        grid=(steps,),
        in_specs=[
            pl.BlockSpec(memory_space=pltpu.SMEM),
            pl.BlockSpec(memory_space=pltpu.SMEM),
            whole(strip.shape),
            whole(near.shape),
            whole(far.shape),
            whole(w_in.shape),
            *[whole(half.shape) for half in halves],
            whole(doc_row.shape),
            pl.BlockSpec((tile, 1), lambda step: (step, 0)),
        ],
        out_specs=[
            whole((width, model_width)),
            whole((length, 3 * width)),
            pl.BlockSpec((tile, width), lambda step: (step, 0)),
            pl.BlockSpec((tile, tile), lambda step: (step, 0)),
            near_block(steps, model_width),
            far_block(steps, model_width),
        ],
        out_shape=[
            jax.ShapeDtypeStruct((width, model_width), bf16),
            jax.ShapeDtypeStruct((length, 3 * width), bf16),
            jax.ShapeDtypeStruct((length, width), bf16),
            jax.ShapeDtypeStruct((length, tile), f32),
            jax.ShapeDtypeStruct((length // 2, model_width), f32),
            jax.ShapeDtypeStruct((length // 2, model_width), bf16),
        ],
        scratch_shapes=[pltpu.VMEM((heads_dev, tile, 2 * length), f32)],
        compiler_params=pltpu.CompilerParams(vmem_limit_bytes=14 * 2**20),
        cost_estimate=pl.CostEstimate(
            flops=4 * length * length * width + 8 * length * model_width * width,
            bytes_accessed=12 * 2**20,
            transcendentals=length * length * heads_dev,
        ),
    )(place, table, strip, near, far, w_in, *halves, doc_row, doc_col)


def plane_attention_back_kernel(
    length, place, table, strip, qkv, doc_row, doc_col, attended, stats, near, far, w_in, w_out,
    grad_qkv, grad_near, grad_far, near_part, far_part, *rest
):
    halves, (band, grad_band, grad_keys, grad_values, out_sum) = rest[:2], rest[2:]
    step = pl.program_id(0)
    half = length // 2
    heads_dev = table.shape[1]
    width = heads_dev * head_dim

    @pl.when(step == 0)
    def _():
        fill_band(band, table, strip, heads_dev, length)
        grad_band[...] = jnp.zeros_like(grad_band)
        grad_keys[...] = jnp.zeros_like(grad_keys)
        grad_values[...] = jnp.zeros_like(grad_values)
        out_sum[...] = jnp.zeros_like(out_sum)

    row = pl.multiple_of(step * half, half)
    branch = jnp.where(step == 0, near[...], far[...])
    merged = attended[...]
    grad_merged = contract(branch, w_out[...], 1, 1).astype(bf16)
    out_sum[...] += contract(merged, branch, 0, 0)
    products = grad_merged.astype(f32) * merged.astype(f32)
    queries = qkv[pl.ds(row, half), :width] * bf16(score_scale)
    blocks = half // tile
    for head in range(heads_dev):
        own = slice(head * head_dim, (head + 1) * head_dim)
        keys = qkv[:, width + own.start : width + own.stop]
        values = qkv[:, 2 * width + own.start : 2 * width + own.stop]
        upstream = grad_merged[:, own]
        raw_scores = contract(queries[:, own], keys, 1, 1)
        grad_weights = contract(upstream, values, 1, 1)
        delta = jnp.sum(products[:, own], axis=1, keepdims=True)
        weights_low, grads_low = [], []
        for block in range(blocks):
            lines = slice(block * tile, (block + 1) * tile)
            starts = band_starts(place, step * blocks + block, length, length // tile + 1)
            scores = raw_scores[lines] + jnp.concatenate(
                [band[head, :, pl.ds(start, tile)] for start in starts], axis=1
            )
            scores = jnp.where(doc_col[lines] == doc_row[...], scores, masked)
            weights = jnp.exp(scores - stats[lines, head : head + 1])
            grad_scores = weights * (grad_weights[lines] - delta[lines])
            for index, start in enumerate(starts):
                grad_band[head, :, pl.ds(start, tile)] += grad_scores[
                    :, index * tile : (index + 1) * tile
                ]
            weights_low.append(weights.astype(bf16))
            grads_low.append(grad_scores.astype(bf16))
        weights_low, grads_low = jnp.concatenate(weights_low), jnp.concatenate(grads_low)
        grad_values[:, own] += contract(weights_low, upstream, 0, 0)
        grad_keys[:, own] += contract(grads_low, queries[:, own], 0, 0)
        grad_qkv[pl.ds(row, half), own] = (
            contract(grads_low, keys, 1, 0) * score_scale
        ).astype(bf16)

    @pl.when(step == pl.num_programs(0) - 1)
    def _():
        grad_qkv[:, width : 2 * width] = grad_keys[...].astype(bf16)
        grad_qkv[:, 2 * width :] = grad_values[...].astype(bf16)
        far_part[...] = contract(grad_qkv[half:], w_in[...], 1, 1).astype(bf16)
        near_part[...] = contract(grad_qkv[:half], w_in[...], 1, 1)
        rows = width // 2
        for index, part in enumerate(halves):
            block = index ^ place[length // tile] % 2
            part[...] = out_sum[pl.ds(pl.multiple_of(block * rows, rows), rows)].astype(bf16)
        for head in range(heads_dev):
            grad_near[head] = grad_band[head, :, length - tile : length + 2 * tile]
            grad_far[head, 0] = jnp.full(
                (8, tile), jnp.sum(grad_band[head, :, : length - tile]), f32
            )
            grad_far[head, 1] = jnp.full(
                (8, tile), jnp.sum(grad_band[head, :, length + 2 * tile :]), f32
            )


def plane_attention_back(
    qkv, doc_row, doc_col, attended, stats, near, far, w_in, w_out, place, table, strip
):
    length, model_width = 2 * near.shape[0], near.shape[1]
    half = length // 2
    heads_dev = table.shape[1]
    width = heads_dev * head_dim
    shapes = [
        ((length, 3 * width), bf16),
        ((heads_dev, tile, 3 * tile), f32),
        ((heads_dev, 2, 8, tile), f32),
        ((length // 2, model_width), f32),
        ((length // 2, model_width), bf16),
    ] + [((width // 2, model_width), bf16)] * 2
    return pl.pallas_call(
        functools.partial(plane_attention_back_kernel, length),
        grid=(2,),
        in_specs=[
            pl.BlockSpec(memory_space=pltpu.SMEM),
            pl.BlockSpec(memory_space=pltpu.SMEM),
            whole(strip.shape),
            whole(qkv.shape),
            whole(doc_row.shape),
            pl.BlockSpec((half, 1), lambda step: (step, 0)),
            pl.BlockSpec((half, width), lambda step: (step, 0)),
            pl.BlockSpec((half, tile), lambda step: (step, 0)),
            whole((half, model_width)),
            whole((half, model_width)),
            whole(w_in.shape),
            whole(w_out.shape),
        ],
        out_specs=[whole(shape) for shape, _ in shapes],
        out_shape=[jax.ShapeDtypeStruct(shape, kind) for shape, kind in shapes],
        scratch_shapes=[
            pltpu.VMEM((heads_dev, tile, 2 * length), f32),
            pltpu.VMEM((heads_dev, tile, 2 * length), f32),
            pltpu.VMEM((length, width), f32),
            pltpu.VMEM((length, width), f32),
            pltpu.VMEM((width, model_width), f32),
        ],
        compiler_params=pltpu.CompilerParams(vmem_limit_bytes=32 * 2**20),
        cost_estimate=pl.CostEstimate(
            flops=10 * length * length * width + 10 * length * model_width * width,
            bytes_accessed=12 * 2**20,
            transcendentals=length * length * heads_dev,
        ),
    )(place, table, strip, qkv, doc_row, doc_col, attended, stats, near, far, w_in, w_out)


def gelu_and_slope(pre_act):
    size = jnp.abs(pre_act)
    gauss = jnp.exp(-0.5 * pre_act * pre_act)
    ratio = 1.0 / (1.0 + np.float32(0.3275911 * 0.5**0.5) * size)
    series = np.float32(1.061405429)
    for factor in (-1.453152027, 1.421413741, -0.284496736, 0.254829592):
        series = series * ratio + np.float32(factor)
    tail = 0.5 * series * ratio * gauss
    cumulative = jnp.where(pre_act < 0, tail, 1.0 - tail)
    slope = cumulative + pre_act * gauss * np.float32((2 * np.pi) ** -0.5)
    return pre_act * cumulative, slope


def ff_kernel(rows, pair, activated, slope, part):
    columns = rows.shape[1]
    value, gradient = gelu_and_slope(contract(rows[...], pair[:, :columns], 1, 1))
    activated[...] = value.astype(bf16)
    slope[...] = gradient.astype(bf16)
    part[...] = contract(activated[...], pair[:, columns:], 1, 0).astype(part.dtype)


def ff_first_kernel(rows, *refs):
    parts, (activated, slope, part, pair) = refs[:5], refs[5:]

    @pl.when(pl.program_id(0) == 0)
    def _():
        units, columns = parts[0].shape[0], rows.shape[1]
        for index, ref in enumerate(parts[:3]):
            pair[index * units : (index + 1) * units] = ref[...]
        pair[3 * units :, :columns] = parts[3][...]
        pair[3 * units :, columns:] = parts[4][...]

    ff_kernel(rows, pair, activated, slope, part)


def ff_back_kernel(rows, slope, pair, grad_pre, part):
    columns = rows.shape[1]
    grad_act = contract(rows[...], pair[:, columns:], 1, 1)
    grad_pre[...] = (grad_act * slope[...].astype(f32)).astype(bf16)
    part[...] = contract(grad_pre[...], pair[:, :columns], 1, 0).astype(part.dtype)


def by_rows(kernel, step_rows, row_operands, whole_operands, outs, whole_outs=()):
    rows = row_operands[0].shape[0]
    return pl.pallas_call(
        kernel,
        grid=(rows // step_rows,),
        in_specs=[
            pl.BlockSpec((step_rows, operand.shape[1]), lambda step: (step, 0))
            for operand in row_operands
        ]
        + [whole(operand.shape) for operand in whole_operands],
        out_specs=[pl.BlockSpec((step_rows, columns), lambda step: (step, 0)) for columns, _ in outs]
        + [whole(shape) for shape in whole_outs],
        out_shape=[jax.ShapeDtypeStruct((rows, columns), kind) for columns, kind in outs]
        + [jax.ShapeDtypeStruct(shape, bf16) for shape in whole_outs],
        compiler_params=pltpu.CompilerParams(vmem_limit_bytes=10 * 2**20),
        cost_estimate=pl.CostEstimate(
            flops=4 * rows * outs[0][0] * row_operands[0].shape[1],
            bytes_accessed=6 * 2**20,
            transcendentals=0,
        ),
    )(*row_operands, *whole_operands)


def ff_grads_kernel(
    pre_near, pre_far, act_near, act_far, normed_near, normed_far, low_near, low_far, *outs
):
    columns = normed_near.shape[1]
    units = outs[0].shape[0]
    up = (
        contract(pre_near[...], normed_near[...], 0, 0)
        + contract(pre_far[...], normed_far[...], 0, 0)
    ).astype(bf16)
    down = (
        contract(act_near[...], low_near[...], 0, 0) + contract(act_far[...], low_far[...], 0, 0)
    ).astype(bf16)

    @pl.when(pl.program_id(0) == 0)
    def _():
        for index in range(2):
            block = slice(index * units, (index + 1) * units)
            outs[index][:, :columns] = up[block]
            outs[index][:, columns:] = down[block]

    @pl.when(pl.program_id(0) == 1)
    def _():
        outs[2][:, :columns] = up[:units]
        outs[2][:, columns:] = down[:units]
        outs[3][...] = up[units:]
        outs[4][...] = down[units:]


def ff_grads(pre, act, normed, low):
    rows, hidden_units = pre[0].shape
    columns = normed[0].shape[1]
    shapes = [(hidden_units // 4, 2 * columns)] * 3 + [(hidden_units // 4, columns)] * 2
    return pl.pallas_call(
        ff_grads_kernel,
        grid=(2,),
        in_specs=[pl.BlockSpec((rows, hidden_units // 2), lambda step: (0, step))] * 4
        + [whole((rows, columns))] * 4,
        out_specs=[whole(shape) for shape in shapes],
        out_shape=[jax.ShapeDtypeStruct(shape, bf16) for shape in shapes],
        compiler_params=pltpu.CompilerParams(vmem_limit_bytes=14 * 2**20),
        cost_estimate=pl.CostEstimate(
            flops=8 * rows * hidden_units * columns, bytes_accessed=8 * 2**20, transcendentals=0
        ),
    )(*pre, *act, *normed, *low)


def in_grads_kernel(place, near, far, grad_qkv, *refs):
    ends, outs, (total, extra) = refs[:-6], refs[-6:-2], refs[-2:]
    half = near.shape[0]
    columns = grad_qkv.shape[1]
    total[:, :columns] = (
        contract(near[...], grad_qkv[:half], 0, 0) + contract(far[...], grad_qkv[half:], 0, 0)
    ).astype(bf16)
    rows = outs[0].shape[0] // 8
    if ends:
        gain_0, gain_1, table_0, table_1 = ends
        lines = lax.broadcasted_iota(jnp.int32, (tile, gain_0.shape[1]), 0)
        gains = jnp.where(lines == 0, gain_0[...], jnp.where(lines == 1, gain_1[...], 0.0))
        extra[...] = jnp.transpose(gains)
        table = table_0[...] + table_1[...]
        buckets = table.shape[0] // 8
        blank = jnp.zeros((8 - buckets, tile), f32)
        for block in range(8):
            row = pl.multiple_of((place[0] // 2 * 8 + block) * rows, rows)
            extra[pl.ds(row, 8)] += jnp.concatenate(
                [table[block * buckets : (block + 1) * buckets], blank]
            )
        total[:, columns:] = extra[...].astype(bf16)
    for out, offset in zip(outs, (0, 3, 1, 2)):
        plane = (place[8] + offset) % 4
        for index in range(8):
            owner = place[index]
            row = row_of(owner // 2, plane, owner % 2, rows)
            out[index * rows : (index + 1) * rows] = total[pl.ds(row, rows)]


def in_grads(place, near, far, grad_qkv, *ends):
    columns = grad_qkv.shape[1] + (tile if ends else 0)
    shape = (near.shape[1] // 4, columns)
    return pl.pallas_call(
        in_grads_kernel,
        in_specs=[pl.BlockSpec(memory_space=pltpu.SMEM)]
        + [pl.BlockSpec(memory_space=pltpu.VMEM)] * (3 + len(ends)),
        out_specs=[pl.BlockSpec(memory_space=pltpu.VMEM)] * 4,
        out_shape=[jax.ShapeDtypeStruct(shape, bf16)] * 4,
        scratch_shapes=[
            pltpu.VMEM((near.shape[1], columns), bf16),
            pltpu.VMEM((near.shape[1], tile), f32),
        ],
        compiler_params=pltpu.CompilerParams(vmem_limit_bytes=14 * 2**20),
        cost_estimate=pl.CostEstimate(
            flops=4 * near.shape[0] * near.shape[1] * columns,
            bytes_accessed=4 * 2**20,
            transcendentals=0,
        ),
    )(place, near, far, grad_qkv, *ends)


def add_in_kernel(own, lower, upper, opposite, near, far):
    total = sum_of_four([own, lower, upper, opposite]).astype(bf16)
    half = near.shape[0]
    near[...] = total[:half]
    far[...] = total[half:]


def combine_kernel(near_part, arrived, own, x_part, y_part, xy_part):
    rows = own.shape[0]
    own[...] = near_part[:rows] + arrived[:rows].astype(f32)
    for bits, out in ((1, x_part), (2, y_part), (3, xy_part)):
        block = slice(bits * rows, (bits + 1) * rows)
        out[...] = (near_part[block] + arrived[block].astype(f32)).astype(bf16)


def added(own, x_part, y_part, xy_part):
    return (own[...] + x_part[...].astype(f32)) + (
        y_part[...].astype(f32) + xy_part[...].astype(f32)
    )


def close_kernel(kept, own, x_part, y_part, xy_part, hidden, units):
    total = kept[...] + added(own, x_part, y_part, xy_part)
    hidden[...] = total
    units[...] = (total * inverse_rms(total)).astype(bf16)


def close_gain_kernel(kept, own, x_part, y_part, xy_part, gain, hidden, normed):
    total = kept[...] + added(own, x_part, y_part, xy_part)
    hidden[...] = total
    normed[...] = (total * inverse_rms(total) * gain[...]).astype(bf16)


def widen_kernel(low, out):
    out[...] = low[...].astype(f32)


def last_kernel(kept, own, x_part, y_part, xy_part, hidden):
    hidden[...] = (kept[...] + added(own, x_part, y_part, xy_part)).astype(bf16)


def middle_back_kernel(
    upstream, own, x_part, y_part, xy_part, middle, gain, grad_middle, branch, grad_gain
):
    grad_normed = added(own, x_part, y_part, xy_part)
    inverse = inverse_rms(middle[...])
    grad_gain[...] = jnp.sum(grad_normed * middle[...] * inverse, axis=0, keepdims=True)
    total = upstream[...].astype(f32) + unit_norm_back(
        middle[...], inverse, grad_normed * gain[...]
    )
    grad_middle[...] = total
    branch[...] = total.astype(bf16)


def layer_back_kernel(grad_middle, own, x_part, y_part, xy_part, hidden, upstream, low):
    total = grad_middle[...] + unit_norm_back(
        hidden[...], inverse_rms(hidden[...]), added(own, x_part, y_part, xy_part)
    )
    upstream[...] = total
    low[...] = total.astype(bf16)


def pair_kernel(axis, near, arrived, *outs):
    rows = near.shape[0] // len(outs)
    for index, out in enumerate(outs):
        block = slice(index * rows, (index + 1) * rows)
        if axis == 0:
            out[:rows] = near[block]
            out[rows:] = arrived[block]
        else:
            columns = near.shape[1]
            out[:, :columns] = near[block]
            out[:, columns:] = arrived[block]


def unit_kernel(tokens, hidden, units):
    total = tokens[...].astype(f32)
    hidden[...] = total
    units[...] = (total * inverse_rms(total)).astype(bf16)


def finish_in_kernel(place, *refs):
    chips, (attn_in, gains, grad_in, grad_gain, ends) = refs[:8], refs[8:]
    rows = attn_in.shape[1]
    width = tile
    members = attn_in.shape[2] // (3 * width)
    ends[...] = jnp.zeros_like(ends)
    for layer_id in range(2):
        row_dot = jnp.zeros((rows, 1), f32)
        for index in range(members):
            member = place[index]
            chip = chips[4 * layer_id + index % 4]
            half = chip.shape[1] // 2
            total = chip[:, index // 4 * half : (index // 4 + 1) * half].astype(f32)
            if layer_id == 0:
                ends[...] += total[:, 3 * width :]
            for part in range(3):
                block = total[:, part * width : (part + 1) * width]
                columns = pl.ds(pl.multiple_of((part * members + member) * width, width), width)
                grad_in[layer_id, :, columns] = block * gains[layer_id]
                row_dot = row_dot + jnp.sum(
                    block * attn_in[layer_id, :, columns].astype(f32), axis=1, keepdims=True
                )
        grad_gain[layer_id] = jnp.concatenate(
            [row_dot, ends[:, layer_id : layer_id + 1]], axis=1
        )


def sum_of_four(parts):
    return (parts[0][...].astype(f32) + parts[1][...].astype(f32)) + (
        parts[2][...].astype(f32) + parts[3][...].astype(f32)
    )


def finish_ff_kernel(*refs):
    count = (len(refs) - 3) // 2
    sources, grads, held, done = refs[:count], refs[count : count + 2], refs[count + 2 : -1], refs[-1]
    copies = [
        pltpu.make_async_copy(source, target, done.at[index])
        for index, (source, target) in enumerate(zip(sources, held))
    ]
    for copy in copies:
        copy.start()
    for copy in copies:
        copy.wait()
    refs = held
    columns = grads[0].shape[2]
    for layer_id in range(grads[0].shape[0]):
        parts = refs[5 * layer_id : 5 * layer_id + 5]
        for side, out in enumerate(grads):
            halves = [part.at[:, side * columns : (side + 1) * columns] for part in parts[:3]]
            out[layer_id] = sum_of_four(halves + [parts[3 + side]])


def finish_ff(grads, shape):
    return pl.pallas_call(
        finish_ff_kernel,
        in_specs=[pl.BlockSpec(memory_space=pl.ANY)] * len(grads),
        out_specs=[pl.BlockSpec(memory_space=pltpu.VMEM)] * 2,
        out_shape=[jax.ShapeDtypeStruct(shape, f32)] * 2,
        scratch_shapes=[pltpu.VMEM(grad.shape, bf16) for grad in grads]
        + [pltpu.SemaphoreType.DMA((len(grads),))],
        compiler_params=pltpu.CompilerParams(vmem_limit_bytes=14 * 2**20),
    )(*grads)


def add_out_kernel(place, *refs):
    parts, (own, other) = refs[:-2], refs[-2:]
    for layer_id in range(own.shape[0]):
        total = parts[2 * layer_id][...].astype(f32) + parts[2 * layer_id + 1][...].astype(f32)
        rows = total.shape[0] // 2
        second = place[0] % 2 == 1
        own[layer_id] = jnp.where(second, total[rows:], total[:rows])
        other[layer_id] = jnp.where(second, total[:rows], total[rows:]).astype(bf16)


def finish_out_kernel(own, arrived, out):
    out[...] = own[...] + arrived[...].astype(f32)


def inverse_rms(hidden):
    return lax.rsqrt(jnp.mean(hidden * hidden, axis=-1, keepdims=True) + epsilon)


def prepare(bias_table, first_head, heads_dev):
    table = lax.dynamic_slice_in_dim(bias_table, first_head, heads_dev, 1)
    (near,) = call(near_kernel, [((heads_dev, tile, 3 * tile), f32)], table, smem=1)
    return table, near


def bucket_grads(first_lane, grads, bucket_count):
    (total,) = call(bucket_kernel, [((bucket_count, tile), f32)], first_lane, *grads, smem=1)
    return total


def gelu_parts(pre_act):
    cumulative = 0.5 * (1.0 + lax.erf(pre_act * np.float32(0.5**0.5)))
    slope = cumulative + pre_act * jnp.exp(-0.5 * pre_act * pre_act) * np.float32(
        (2 * np.pi) ** -0.5
    )
    return (pre_act * cumulative).astype(bf16), slope


def unit_norm_back(hidden, inverse, grad_unit):
    unit = hidden * inverse
    return inverse * (grad_unit - unit * jnp.mean(grad_unit * unit, axis=-1, keepdims=True))


def gather_rows(block, axes):
    return lax.all_gather(block, axes, axis=0, tiled=True)


def toggle(array, axis, bits):
    return lax.ppermute(array, axis, [(i, i ^ bits) for i in range(lax.axis_size(axis))])


def shift(array, by):
    planes = lax.axis_size("z")
    return lax.ppermute(array, "z", [(i, (i + by) % planes) for i in range(planes)])


def plane_gather(block, *holds):
    near = jnp.concatenate([block] + [toggle(block, "head", bits) for bits in (1, 2, 3)])
    near, *holds = tie(near, *holds)
    return (near, toggle(near, "core", 1), *holds)


def plane_scatter(near_part, far_part):
    rows, columns = near_part.shape[0] // 4, near_part.shape[1]
    own, *others = call(
        combine_kernel,
        [((rows, columns), f32)] + [((rows, columns), bf16)] * 3,
        near_part,
        toggle(far_part, "core", 1),
    )
    shares = [own] + [toggle(other, "head", bits) for bits, other in zip((1, 2, 3), others)]
    return shares, own


def tie(*arrays):
    return lax.optimization_barrier(arrays)


def after(array, other):
    return lax.optimization_barrier((array, other))[0]


def scatter_sum(partial, axes, members):
    blocks = partial.astype(bf16).reshape(members, -1, partial.shape[1])
    return jnp.sum(lax.all_to_all(blocks, axes, 0, 0, tiled=True).astype(f32), axis=0)


def local_general(tokens, doc_start, bias_table, attn_in, attn_out, ff_in, ff_out, gains, cotangent):
    heads_n, z_n, core_n = (lax.axis_size(axis) for axis in everyone)
    devices = heads_n * z_n * core_n
    group, spare = ("z", "core"), "head"
    ff_group, ff_spare, ff_members = ("head", "core"), "z", heads_n * core_n
    blocks = z_n * core_n
    block_rows, model_width = tokens.shape[1:]
    layer_count, weight_rows = attn_in.shape[:2]
    length = block_rows * blocks
    heads_all = bias_table.shape[1]
    member = lax.axis_index("z") * core_n + lax.axis_index("core")
    heads_dev = max(1, heads_all // blocks)
    head_groups = heads_all // heads_dev
    split = blocks // head_groups
    head_group, query_part = member // split, member % split
    query_rows = length // split
    width = heads_dev * head_dim
    first = (query_part * (query_rows // tile)).astype(jnp.int32).reshape(1)
    place = jnp.arange(length // tile, dtype=jnp.int32)
    out_row = head_group * width

    def swap(array):
        return lax.all_to_all(array, everyone, 0, 0, tiled=True)

    starts = jnp.broadcast_to(
        doc_start.astype(f32)[:, None], (heads_n, blocks, block_rows)
    ).reshape(devices, block_rows)
    ff_gains = gains[:, :, 1].astype(f32).reshape(1, -1)
    small = swap(
        jnp.concatenate(
            [starts, jnp.broadcast_to(ff_gains, (devices, layer_count * weight_rows))], axis=1
        )
    )
    doc_row = small[:blocks, :block_rows].reshape(1, length)
    doc_col = lax.dynamic_slice_in_dim(
        doc_row.reshape(length, 1), query_part * query_rows, query_rows, 0
    )
    gain_ff = jnp.transpose(
        small[:, block_rows:].reshape(devices, layer_count, weight_rows), (1, 0, 2)
    ).reshape(layer_count, 1, model_width)
    table, near = prepare(bias_table, head_group * heads_dev, heads_dev)

    gain_attn = gains[:, :, 0].astype(f32)[:, :, None]
    own_in = attn_in.astype(f32)

    def fetch_in(layer_id):
        scaled = (own_in[layer_id] * gain_attn[layer_id]).astype(bf16)
        columns = jnp.transpose(
            scaled.reshape(weight_rows, 3, head_groups, width), (2, 0, 1, 3)
        ).reshape(head_groups, weight_rows, 3 * width)
        columns = jnp.repeat(columns, split, axis=0)
        columns = jnp.broadcast_to(columns[None], (heads_n, *columns.shape))
        return swap(columns.reshape(devices, weight_rows, 3 * width)).reshape(
            model_width, 3 * width
        )

    def fetch_ff(layer_id):
        pair = jnp.concatenate([ff_in[layer_id], ff_out[layer_id]], axis=1)
        pair = gather_rows(pair, ff_spare)
        return pair[:, :model_width], pair[:, model_width:]

    hidden, upstream = tokens[0].astype(f32), cotangent[0]
    weights_in = [fetch_in(layer_id) for layer_id in range(layer_count)]
    weights_out = lax.dynamic_slice_in_dim(
        lax.all_gather(attn_out, everyone, axis=1, tiled=True), out_row, width, 1
    )
    weights_ff = [fetch_ff(layer_id) for layer_id in range(layer_count)]

    records = []
    for layer_id in range(layer_count):
        w_in, w_out, (w_up, w_down) = (
            weights_in[layer_id], weights_out[layer_id], weights_ff[layer_id],
        )
        inverse = inverse_rms(hidden)
        units = gather_rows((hidden * inverse).astype(bf16), group)
        qkv = jnp.dot(units, w_in, preferred_element_type=f32).astype(bf16)
        attended, _, stats = attention(
            qkv, doc_row, doc_col, first, place, table, near, query_rows
        )
        mixed = jnp.dot(attended, w_out, preferred_element_type=f32)
        if split > 1:
            mixed = lax.dynamic_update_slice_in_dim(
                jnp.zeros((length, model_width), f32), mixed, query_part * query_rows, 0
            )
        middle = hidden + scatter_sum(mixed, group, blocks)
        inverse_ff = inverse_rms(middle)
        normed_ff = gather_rows((middle * inverse_ff * gain_ff[layer_id]).astype(bf16), ff_group)
        activated, slope = gelu_parts(contract(normed_ff, w_up, 1, 1))
        ff_result = jnp.dot(activated, w_down, preferred_element_type=f32)
        records.append(
            (hidden, inverse, units, qkv, attended, stats, middle, inverse_ff, normed_ff,
             activated, slope)
        )
        hidden = middle + scatter_sum(ff_result, ff_group, ff_members)
    output = hidden

    grads_ff, grads_in, grads_out, grads_gain_ff, grads_table = (
        [None] * layer_count for _ in range(5)
    )
    for layer_id in reversed(range(layer_count)):
        w_in, w_out, (w_up, w_down) = (
            weights_in[layer_id], weights_out[layer_id], weights_ff[layer_id],
        )
        (hidden, inverse, units, qkv, attended, stats, middle, inverse_ff, normed_ff,
         activated, slope) = records[layer_id]
        grad_low = gather_rows(upstream.astype(bf16), ff_group)
        grad_pre = (contract(grad_low, w_down, 1, 1) * slope).astype(bf16)
        grad_normed = scatter_sum(
            jnp.dot(grad_pre, w_up, preferred_element_type=f32), ff_group, ff_members
        )
        grad_pair = jnp.concatenate(
            [contract(grad_pre, normed_ff, 0, 0), contract(activated, grad_low, 0, 0)], axis=1
        ).astype(bf16)
        grads_ff[layer_id] = lax.psum_scatter(
            grad_pair, ff_spare, scatter_dimension=0, tiled=True
        ).astype(f32)
        grads_gain_ff[layer_id] = jnp.sum(grad_normed * middle * inverse_ff, axis=0)
        grad_middle = upstream + unit_norm_back(
            middle, inverse_ff, grad_normed * gain_ff[layer_id]
        )
        branch = gather_rows(grad_middle.astype(bf16), group)
        if split > 1:
            branch = lax.dynamic_slice_in_dim(branch, query_part * query_rows, query_rows, 0)
        grad_attended = contract(branch, w_out, 1, 1).astype(bf16)
        grad_qkv, grad_near, grad_far = attention_back(
            qkv, doc_row, doc_col, attended, grad_attended, stats, first, place, table, near, split
        )
        grads_table[layer_id] = (grad_near, grad_far)
        grad_units = scatter_sum(contract(grad_qkv, w_in, 1, 1), group, blocks)
        upstream = grad_middle + unit_norm_back(hidden, inverse, grad_units)
        grad_out = lax.dynamic_update_slice_in_dim(
            jnp.zeros((model_width, model_width), bf16),
            contract(attended, branch, 0, 0).astype(bf16),
            out_row,
            0,
        )
        grads_out[layer_id] = lax.psum_scatter(
            grad_out, everyone, scatter_dimension=0, tiled=True
        ).astype(f32)
        grads_in[layer_id] = contract(units, grad_qkv, 0, 0).astype(bf16)

    bucket_count = table.shape[0]
    grad_table = sum(
        bucket_grads(jnp.zeros((1,), jnp.int32), entry, bucket_count) for entry in grads_table
    )[:, :heads_dev]
    grad_table = lax.dynamic_update_slice_in_dim(
        jnp.zeros((bucket_count, heads_all), f32), grad_table, head_group * heads_dev, 1
    )
    grad_table = jnp.transpose(
        grad_table.reshape(blocks, bucket_count // blocks, heads_n, heads_all // heads_n),
        (2, 0, 1, 3),
    ).reshape(devices, -1)
    grad_gain_ff = jnp.transpose(
        jnp.stack(grads_gain_ff).reshape(layer_count, devices, weight_rows), (1, 0, 2)
    ).reshape(devices, -1)
    ends = jnp.sum(swap(jnp.concatenate([grad_gain_ff, grad_table], axis=1)), axis=0)
    grad_gain_ff = ends[: layer_count * weight_rows].reshape(layer_count, weight_rows)
    grad_bias_table = ends[layer_count * weight_rows :].reshape(
        bucket_count // blocks, heads_all // heads_n
    )
    grads_attn_in, grads_gains = [], []
    for layer_id in range(layer_count):
        parts = swap(grads_in[layer_id].reshape(devices, weight_rows, 3 * width)).astype(f32)
        parts = jnp.sum(parts.reshape(heads_n, blocks, weight_rows, 3 * width), axis=0)
        parts = jnp.sum(parts.reshape(head_groups, split, weight_rows, 3, width), axis=1)
        unit_grad = jnp.transpose(parts, (1, 2, 0, 3)).reshape(weight_rows, 3 * model_width)
        grads_attn_in.append(unit_grad * gain_attn[layer_id])
        grads_gains.append(
            jnp.stack(
                [jnp.sum(unit_grad * own_in[layer_id], axis=1), grad_gain_ff[layer_id]], axis=1
            )
        )
    return (
        output[None],
        upstream[None],
        jnp.stack(grads_attn_in),
        jnp.stack(grads_out),
        jnp.stack([entry[:, :model_width] for entry in grads_ff]),
        jnp.stack([entry[:, model_width:] for entry in grads_ff]),
        jnp.stack(grads_gains),
        grad_bias_table,
    )


def local_plane(tokens, doc_start, bias_table, attn_in, attn_out, ff_in, ff_out, gains, cotangent):
    heads_n, z_n, core_n = (lax.axis_size(axis) for axis in everyone)
    devices = heads_n * z_n * core_n
    at_head, at_z, at_core = (lax.axis_index(axis) for axis in everyone)
    members = heads_n * core_n
    block_rows, model_width = tokens.shape[1:]
    layer_count, weight_rows = attn_in.shape[:2]
    length = block_rows * members
    heads_all = bias_table.shape[1]
    heads_dev = heads_all // members
    width = heads_dev * head_dim
    member = at_head * core_n + at_core
    everywhere = [(h, z, c) for h in range(heads_n) for z in range(z_n) for c in range(core_n)]

    def swapped(bits):
        return bits % 2 * 2 + bits // 2

    def device(h, z, c):
        return (h * z_n + z) * core_n + c

    turn = [(device(h, z, c), device(h ^ swapped(z), h, c)) for h, z, c in everywhere]
    plane_turn = [(device(h, z, c), device(h ^ swapped(z), z, c)) for h, z, c in everywhere]
    line_turn = [(device(h, z, c), device(h, h ^ swapped(z), c)) for h, z, c in everywhere]
    line_back = [(target, source) for source, target in line_turn]
    place = jnp.stack(
        [
            (at_head ^ bits) * core_n + (at_core ^ other)
            for other in range(core_n)
            for bits in range(heads_n)
        ]
        + [at_z]
        + [
            swapped(at_head ^ bits ^ at_z) * core_n + (at_core ^ other)
            for other in range(core_n)
            for bits in range(heads_n)
        ]
    ).astype(jnp.int32)

    def relay(array):
        return lax.ppermute(array, everyone, turn)

    def turn_in_plane(array):
        return lax.ppermute(array, everyone, plane_turn)

    def turn_in_line(array, turns):
        return lax.ppermute(array, everyone, turns)

    def swap(array):
        return lax.all_to_all(array, everyone, 0, 0, tiled=True)

    row_shape = (block_rows, model_width)
    gain_attn = gains[:, :, 0].astype(f32)[:, :, None]
    near_share, far_share = call(
        share_in_kernel,
        [((members // 2 * layer_count * weight_rows, 3 * width), bf16)] * 2,
        place,
        attn_in,
        gain_attn,
        smem=1,
    )

    half_turns = [
        [
            (z * core_n + c, (2 * c + (a ^ z % 2)) * core_n + z // 2)
            for z in range(z_n)
            for c in range(core_n)
        ]
        for a in range(2)
    ]

    def fetch_out(layer_id, hold):
        own = attn_out[layer_id]
        other = toggle(own, "core", 1)
        head = jnp.where(
            at_core == 0, jnp.concatenate([own, other]), jnp.concatenate([other, own])
        )
        head = after(head, hold)
        return [
            lax.ppermute(head, ("z", "core"), [(holder, user) for user, holder in turns])
            for turns in half_turns
        ]

    def owners_halves(halves):
        return [
            lax.ppermute(half, ("z", "core"), turns) for half, turns in zip(halves, half_turns)
        ]

    def pair_chips(near, arrived, axis):
        rows, columns = near.shape[0] // 4, near.shape[1]
        shape = (2 * rows, columns) if axis == 0 else (rows, 2 * columns)
        return call(functools.partial(pair_kernel, axis), [(shape, bf16)] * 4, near, arrived)

    def share_chips(blocks):
        return [blocks[0]] + [toggle(blocks[bits], "head", bits) for bits in (1, 2, 3)]

    units_shape = [(row_shape, f32), (row_shape, bf16)]

    starts = jnp.broadcast_to(
        doc_start.astype(f32)[None, :, None], (heads_n, z_n, core_n, block_rows)
    )
    ff_gains = gains[:, :, 1].astype(f32).reshape(1, -1)
    small = jnp.concatenate(
        [
            starts.reshape(devices, block_rows),
            jnp.broadcast_to(ff_gains, (devices, layer_count * weight_rows)),
        ],
        axis=1,
    )
    table, strip = prepare(bias_table, member * heads_dev, heads_dev)
    hidden = relay(tokens[0])
    hidden, shares, halves, small = tie(
        hidden,
        share_chips(pair_chips(near_share, toggle(far_share, "core", 1), 0)),
        fetch_out(0, near_share),
        swap(after(small, near_share)),
    )
    hidden, unit_rows = call(unit_kernel, units_shape, hidden)
    doc_row = small[:members, :block_rows].reshape(2, 2, core_n, block_rows)
    at_block = swapped(at_head ^ at_z)
    for axis, bit in ((0, at_block // 2), (1, at_block % 2), (2, at_core)):
        doc_row = jnp.where(bit == 1, jnp.flip(doc_row, axis), doc_row)
    doc_row = jnp.transpose(doc_row, (2, 1, 0, 3)).reshape(1, length)
    doc_col = doc_row.reshape(length, 1)
    gain_ff = jnp.transpose(
        small[:, block_rows:].reshape(devices, layer_count, weight_rows), (1, 0, 2)
    ).reshape(layer_count, 1, model_width)

    def round_planes(array, by, hold):
        return shift(after(array, hold), by)

    ff_pairs = [
        jnp.concatenate([ff_in[layer_id], ff_out[layer_id]], axis=1) for layer_id in range(layer_count)
    ]

    def ff_both(kernel, row_operands, pair, columns):
        return zip(
            *(
                by_rows(
                    kernel,
                    256,
                    operands,
                    [pair],
                    [(pair.shape[0], bf16)] * columns + [(model_width, kind)],
                )
                for operands, kind in zip(zip(*row_operands), (f32, bf16))
            )
        )

    def ff_forward(normed, *parts):
        units = 4 * parts[0].shape[0]
        outs = [(units, bf16), (units, bf16)]
        *near, pair = by_rows(
            ff_first_kernel,
            256,
            [normed[0]],
            parts,
            outs + [(model_width, f32)],
            [(units, 2 * model_width)],
        )
        far = by_rows(ff_kernel, 256, [normed[1]], [pair], outs + [(model_width, bf16)])
        return pair, *zip(near, far)

    def ff_backward(low, slopes, pair):
        return ff_both(ff_back_kernel, [low, slopes], pair, 1)

    def assemble_in(share, lower, upper, opposite):
        return call(
            assemble_in_kernel,
            [((model_width, 3 * width), bf16)],
            place,
            share,
            lower,
            upper,
            opposite,
            smem=1,
        )[0]

    share, later_share = call(
        join_kernel, [((members * weight_rows, 3 * width), bf16)] * layer_count, *shares
    )
    near, far, lower, upper, opposite, cotangent_low, strip, doc_row, doc_col, gain_ff, *ff_pairs = plane_gather(
        unit_rows,
        shift(share, 1),
        shift(share, -1),
        shift(share, 2),
        cotangent[0].astype(bf16),
        strip,
        doc_row,
        doc_col,
        gain_ff,
        *ff_pairs,
    )
    w_in = assemble_in(share, lower, upper, opposite)
    units = (near, far)
    w_out, qkv, attended, stats, *parts = plane_attention(
        *units, w_in, halves, doc_row, doc_col, place, table, strip
    )
    parts, lower, upper, cotangent_low = tie(
        parts,
        round_planes(ff_pairs[0], 1, near),
        round_planes(ff_pairs[0], -1, near),
        turn_in_plane(after(cotangent_low, near)),
    )
    parts, own = plane_scatter(*parts)
    parts, opposite_in = tie(parts, round_planes(ff_in[0], 2, own))
    middle, normed_rows = call(close_gain_kernel, units_shape, hidden, *parts, gain_ff[0])
    *normed, opposite_out = plane_gather(normed_rows, round_planes(ff_out[0], 2, normed_rows))
    pair, acts, slopes, parts = ff_forward(
        normed, ff_pairs[0], lower, upper, opposite_in, opposite_out
    )
    records = [
        (hidden, units, w_in, w_out, pair, qkv, attended, stats, middle, normed, acts, slopes)
    ]
    parts, lower, upper = tie(
        parts,
        round_planes(later_share, 1, normed[0]),
        round_planes(later_share, -1, normed[0]),
    )
    parts, own = plane_scatter(*parts)
    parts, opposite, upstream = tie(
        parts, round_planes(later_share, 2, own), turn_in_line(after(cotangent_low, own), line_turn)
    )
    shares = [later_share, lower, upper, opposite]
    hidden, unit_rows = call(close_kernel, units_shape, middle, *parts)

    near, far, lower, halves = plane_gather(
        unit_rows, round_planes(ff_pairs[1], 1, unit_rows), fetch_out(1, unit_rows)
    )
    units = (near, far)
    w_in = assemble_in(*shares)
    w_out, qkv, attended, stats, *parts = plane_attention(
        *units, w_in, halves, doc_row, doc_col, place, table, strip
    )
    low = plane_gather(after(upstream, far))
    parts, near_low, upper = tie(parts, low[0], round_planes(ff_pairs[1], -1, far))
    low = (near_low, low[1])
    parts, own = plane_scatter(*parts)
    parts, opposite_in = tie(parts, round_planes(ff_in[1], 2, own))
    middle, normed_rows = call(close_gain_kernel, units_shape, hidden, *parts, gain_ff[1])
    *normed, opposite_out = plane_gather(normed_rows, round_planes(ff_out[1], 2, normed_rows))
    pair, acts, slopes, last_parts = ff_forward(
        normed, ff_pairs[1], lower, upper, opposite_in, opposite_out
    )
    records.append(
        (hidden, units, w_in, w_out, pair, qkv, attended, stats, middle, normed, acts, slopes)
    )

    def back_to_middle(parts, upstream, middle, gain):
        return call(
            middle_back_kernel, units_shape + [((1, model_width), f32)], upstream, *parts, middle, gain
        )

    def attention_grads(record, branch):
        _, _, w_in, w_out, _, qkv, attended, stats, *_ = record
        grad_qkv, grad_near, grad_far, near_part, far_part, *halves = plane_attention_back(
            qkv, doc_row, doc_col, attended, stats, *branch, w_in, w_out, place, table, strip
        )
        return grad_qkv, (grad_near, grad_far), (near_part, far_part), halves

    def table_grads(near_and_far):
        return bucket_grads(at_core.reshape(1) * heads_dev + 8, near_and_far, table.shape[0])

    record = records[1]
    hidden, units, _, _, pair, *_, middle, normed, acts, slopes = record
    pres, parts = ff_backward(low, slopes, pair)
    parts, own = plane_scatter(*parts)
    planes = ff_grads(after(pres, own), acts, normed, low)
    parts, ff_lower = tie(parts, shift(planes[1], -1))
    last_parts, _ = plane_scatter(*after(last_parts, parts))
    grad_middle, branch_rows, gain_1 = back_to_middle(parts, upstream, middle, gain_ff[1])
    *branch, ff_upper = plane_gather(branch_rows, round_planes(planes[2], 1, branch_rows))
    grad_qkv, strips_1, parts, halves_1 = attention_grads(record, branch)
    parts, last_parts, opposite_up = tie(
        parts, last_parts, round_planes(planes[3], 2, branch[1])
    )
    parts, own = plane_scatter(*parts)
    parts, opposite_down, output = tie(
        parts,
        round_planes(planes[4], 2, own),
        call(last_kernel, [(row_shape, bf16)], middle, *after(last_parts, own))[0],
    )
    grads_ff = [planes[0], ff_lower, ff_upper, opposite_up, opposite_down]
    upstream, low_rows = call(layer_back_kernel, units_shape, grad_middle, *parts, hidden)

    record = records[0]
    hidden, units, _, _, pair, *_, middle, normed, acts, slopes = record
    grad_in = in_grads(place, *records[1][1], after(grad_qkv, low_rows))
    *low, in_opposite, in_upper, table_1 = plane_gather(
        low_rows, shift(grad_in[3], 2), shift(grad_in[2], 1), table_grads(after(strips_1, low_rows))
    )
    pres, parts = ff_backward(low, slopes, pair)
    parts, in_lower = tie(parts, round_planes(grad_in[1], -1, low[0]))
    parts, own = plane_scatter(*parts)
    planes = ff_grads(after(pres, own), acts, normed, low)
    near_in, far_in = call(
        add_in_kernel,
        [((members // 2 * weight_rows, 3 * width), bf16)] * 2,
        *after([grad_in[0], in_lower, in_upper, in_opposite], own),
    )
    parts, ff_lower, first_half, arrived = tie(
        parts,
        shift(planes[1], -1),
        owners_halves(after(halves_1, own))[0],
        toggle(far_in, "core", 1),
    )
    grad_middle, branch_rows, gain_0 = back_to_middle(parts, upstream, middle, gain_ff[0])
    *branch, ff_upper, second_half, shares_1 = plane_gather(
        branch_rows,
        round_planes(planes[2], 1, branch_rows),
        owners_halves(after(halves_1, branch_rows))[1],
        pair_chips(near_in, after(arrived, branch_rows), 1),
    )
    halves_1 = [first_half, second_half]
    grad_qkv, strips_0, parts, halves_0 = attention_grads(record, branch)
    parts, shares_1, output, opposite_up = tie(
        parts,
        share_chips(after(shares_1, branch[1])), turn_in_line(after(output, branch[1]), line_back), round_planes(planes[3], 2, branch[1])
    )
    parts, own = plane_scatter(*parts)
    table_0 = table_grads(after(strips_0, own))
    grad_in = in_grads(
        place, *units, after(grad_qkv, own), gain_0, gain_1, table_0, table_1
    )
    parts, in_opposite, halves_0 = tie(
        parts, shift(grad_in[3], 2), owners_halves(after(halves_0, own))
    )
    upstream, low_rows = call(layer_back_kernel, units_shape, grad_middle, *parts, hidden)
    in_lower = round_planes(grad_in[1], -1, low_rows)
    in_upper = round_planes(grad_in[2], 1, low_rows)
    line = turn_in_line(low_rows, line_back)
    near_in, far_in = call(
        add_in_kernel,
        [((members // 2 * weight_rows, 3 * width + tile), bf16)] * 2,
        grad_in[0],
        in_lower,
        in_upper,
        in_opposite,
    )
    arrived = toggle(far_in, "core", 1)
    shares_0 = share_chips(pair_chips(near_in, arrived, 1))
    opposite_down = round_planes(planes[4], 2, near_in)
    grad_tokens = turn_in_plane(after(line, shares_0[1:]))
    output = turn_in_plane(after(output, shares_0[1:]))
    (output,) = call(widen_kernel, [(row_shape, f32)], output)
    (grad_tokens,) = call(widen_kernel, [(row_shape, f32)], grad_tokens)
    grads_ff = [planes[0], ff_lower, ff_upper, opposite_up, opposite_down] + grads_ff
    grad_up, grad_down = finish_ff(after(grads_ff, shares_0[1:]), ff_in.shape)
    own_out, other_out = call(
        add_out_kernel,
        [(attn_out.shape, f32), (attn_out.shape, bf16)],
        place,
        *after(halves_0 + halves_1, shares_0[1:]),
        smem=1,
    )
    (grad_attn_out,) = call(
        finish_out_kernel, [(attn_out.shape, f32)], own_out, toggle(other_out, "core", 1)
    )
    own_buckets = table.shape[0] // (z_n * core_n)
    grad_attn_in, grad_gains, ends = call(
        finish_in_kernel,
        [(attn_in.shape, f32), (gains.shape, f32), ((weight_rows, tile), f32)],
        place,
        *shares_0,
        *shares_1,
        attn_in,
        gain_attn,
        smem=1,
    )
    return (
        output[None],
        grad_tokens[None],
        grad_attn_in,
        grad_attn_out,
        grad_up,
        grad_down,
        grad_gains,
        ends[:own_buckets, 8 : 8 + heads_all // heads_n],
    )


def solution(mesh):
    sizes = dict(mesh.shape)
    cores = 2
    fine = Mesh(
        mesh.devices.reshape(sizes["head"], sizes["blk"] // cores, cores), everyone
    )
    blk = ("z", "core")
    in_specs = (
        P("head", blk, None),
        P(None, blk),
        P(),
        P(None, everyone, None),
        P(None, everyone, None),
        P(None, everyone, None),
        P(None, everyone, None),
        P(None, everyone, None),
        P("head", blk, None),
    )
    out_specs = (
        P("head", blk, None),
        P("head", blk, None),
        P(None, everyone, None),
        P(None, everyone, None),
        P(None, everyone, None),
        P(None, everyone, None),
        P(None, everyone, None),
        P(blk, "head"),
    )
    plane = sizes["head"] == 4 and sizes["blk"] == 8
    local = local_plane if plane else local_general
    return jax.shard_map(local, mesh=fine, in_specs=in_specs, out_specs=out_specs, check_vma=False)
```

```python
import functools

import jax
import jax.numpy as jnp
import numpy as np
from jax import lax
from jax.experimental import pallas as pl
from jax.experimental.pallas import tpu as pltpu
from jax.sharding import Mesh
from jax.sharding import PartitionSpec as P

bounds = (1, 2, 3, 4, 5, 6, 7, 8, 12, 16, 23, 32, 46, 64, 91)
epsilon = 1e-06
masked = -1e30
score_scale = 0.125
head_dim = 64
tile = 128
everyone = ("head", "z", "core")
bf16 = jnp.bfloat16
f32 = jnp.float32


def contract(lhs, rhs, lhs_dim, rhs_dim):
    return lax.dot_general(
        lhs, rhs, (((lhs_dim,), (rhs_dim,)), ((), ())), preferred_element_type=f32
    )


def near_buckets(shape):
    offsets = (
        lax.broadcasted_iota(jnp.int32, shape, 1) - tile - lax.broadcasted_iota(jnp.int32, shape, 0)
    )
    distance = jnp.abs(offsets)
    bucket = jnp.where(offsets > 0, 16, 0)
    for boundary in bounds:
        bucket = bucket + jnp.where(distance >= boundary, 1, 0)
    return bucket


def near_kernel(table, near):
    bucket = near_buckets(near.shape[1:])
    for head in range(near.shape[0]):
        values = jnp.zeros(near.shape[1:], f32)
        for bucket_id in range(table.shape[0]):
            values = jnp.where(bucket == bucket_id, table[bucket_id, head], values)
        near[head] = values


def bucket_kernel(first_lane, near, far, out):
    bucket = near_buckets(near.shape[1:])
    rows = lax.broadcasted_iota(jnp.int32, out.shape, 0)
    lanes = lax.broadcasted_iota(jnp.int32, out.shape, 1)
    total = jnp.zeros(out.shape, f32)
    for head in range(near.shape[0]):
        strip = near[head]
        for bucket_id in range(out.shape[0]):
            value = jnp.sum(jnp.where(bucket == bucket_id, strip, 0.0), axis=0, keepdims=True)
            value = jnp.sum(value, axis=1, keepdims=True)
            if bucket_id in (15, 31):
                value = value + far[head, bucket_id // 16, :1, :1]
            total = jnp.where((rows == bucket_id) & (lanes == head + first_lane[0]), value, total)
    out[...] = total


def fill_band(band, table, near, heads_dev, length):
    for head in range(heads_dev):
        band[head, :, : length - tile] = jnp.full((tile, length - tile), table[15, head], f32)
        band[head, :, length - tile : length + 2 * tile] = near[head]
        band[head, :, length + 2 * tile :] = jnp.full(
            (tile, length - 2 * tile), table[31, head], f32
        )


def band_starts(place, at, length, skip=0):
    return [
        pl.multiple_of(length + (place[skip + block] - place[skip + at]) * tile, tile)
        for block in range(length // tile)
    ]


def attention_kernel(
    heads_dev, length, first, place, table, near, qkv, doc_row, doc_col, out, local, stats, band
):
    step = pl.program_id(0)
    width = heads_dev * head_dim

    @pl.when(step == 0)
    def _():
        fill_band(band, table, near, heads_dev, length)

    row = pl.multiple_of((first[0] + step) * tile, tile)
    out_row = pl.multiple_of((place[first[0] + step] - first[0]) * tile, tile)
    starts = band_starts(place, first[0] + step, length)
    same_doc = doc_col[...] == doc_row[...]
    queries = qkv[pl.ds(row, tile), :width] * bf16(score_scale)
    lanes = lax.broadcasted_iota(jnp.int32, (tile, tile), 1)
    collected = jnp.zeros((tile, tile), f32)
    for head in range(heads_dev):
        own = slice(head * head_dim, (head + 1) * head_dim)
        keys = qkv[:, width + own.start : width + own.stop]
        values = qkv[:, 2 * width + own.start : 2 * width + own.stop]
        scores = contract(queries[:, own], keys, 1, 1)
        scores = scores + jnp.concatenate(
            [band[head, :, pl.ds(start, tile)] for start in starts], axis=1
        )
        scores = jnp.where(same_doc, scores, masked)
        peak = jnp.max(scores, axis=1, keepdims=True)
        weights = jnp.exp(scores - peak)
        total = jnp.sum(weights, axis=1, keepdims=True)
        mixed = contract(weights.astype(bf16), values, 1, 0) / total
        out[pl.ds(out_row, tile), own] = mixed.astype(bf16)
        local[:, own] = mixed.astype(bf16)
        collected = jnp.where(lanes == head, peak + jnp.log(total), collected)
    stats[...] = collected


def attention_back_kernel(
    heads_dev, length, split, first, place, table, near, qkv, doc_row, doc_col, attended, grad_out, stats,
    grad_qkv, grad_near, grad_far, band, grad_band, grad_keys, grad_values,
):
    step = pl.program_id(0)
    width = heads_dev * head_dim

    @pl.when(step == 0)
    def _():
        fill_band(band, table, near, heads_dev, length)
        grad_band[...] = jnp.zeros_like(grad_band)
        grad_keys[...] = jnp.zeros_like(grad_keys)
        grad_values[...] = jnp.zeros_like(grad_values)
        if split > 1:
            grad_qkv[...] = jnp.zeros_like(grad_qkv)

    row = pl.multiple_of((first[0] + step) * tile, tile)
    out_row = pl.multiple_of((place[first[0] + step] - first[0]) * tile, tile)
    starts = band_starts(place, first[0] + step, length)
    same_doc = doc_col[...] == doc_row[...]
    at_step = pl.multiple_of(step * tile, tile)
    queries = qkv[pl.ds(row, tile), :width] * bf16(score_scale)
    for head in range(heads_dev):
        own = slice(head * head_dim, (head + 1) * head_dim)
        keys = qkv[:, width + own.start : width + own.stop]
        values = qkv[:, 2 * width + own.start : 2 * width + own.stop]
        upstream = grad_out[pl.ds(out_row, tile), own]
        scores = contract(queries[:, own], keys, 1, 1) + jnp.concatenate(
            [band[head, :, pl.ds(start, tile)] for start in starts], axis=1
        )
        scores = jnp.where(same_doc, scores, masked)
        weights = jnp.exp(scores - stats[:, head : head + 1])
        delta = jnp.sum(
            upstream.astype(f32) * attended[pl.ds(at_step, tile), own].astype(f32),
            axis=1,
            keepdims=True,
        )
        grad_scores = weights * (contract(upstream, values, 1, 1) - delta)
        for block, start in enumerate(starts):
            grad_band[head, :, pl.ds(start, tile)] += grad_scores[
                :, block * tile : (block + 1) * tile
            ]
        grad_low = grad_scores.astype(bf16)
        grad_values[:, own] += contract(weights.astype(bf16), upstream, 0, 0)
        grad_keys[:, own] += contract(grad_low, queries[:, own], 0, 0)
        grad_qkv[pl.ds(row, tile), own] = (
            contract(grad_low, keys, 1, 0) * score_scale
        ).astype(bf16)

    @pl.when(step == pl.num_programs(0) - 1)
    def _():
        grad_qkv[:, width : 2 * width] = grad_keys[...].astype(bf16)
        grad_qkv[:, 2 * width :] = grad_values[...].astype(bf16)
        for head in range(heads_dev):
            grad_near[head] = grad_band[head, :, length - tile : length + 2 * tile]
            grad_far[head, 0] = jnp.full(
                (8, tile), jnp.sum(grad_band[head, :, : length - tile]), f32
            )
            grad_far[head, 1] = jnp.full(
                (8, tile), jnp.sum(grad_band[head, :, length + 2 * tile :]), f32
            )


def whole(shape):
    return pl.BlockSpec(shape, lambda step: (0,) * len(shape), pipeline_mode=pl.Buffered(1))


def attention(qkv, doc_row, doc_col, first, place, table, near, rows):
    length = qkv.shape[0]
    heads_dev = table.shape[1]
    width = heads_dev * head_dim
    return pl.pallas_call(
        functools.partial(attention_kernel, heads_dev, length),
        grid=(rows // tile,),
        in_specs=[
            pl.BlockSpec(memory_space=pltpu.SMEM),
            pl.BlockSpec(memory_space=pltpu.SMEM),
            pl.BlockSpec(memory_space=pltpu.SMEM),
            whole(near.shape),
            whole(qkv.shape),
            whole(doc_row.shape),
            pl.BlockSpec((tile, 1), lambda step: (step, 0)),
        ],
        out_specs=[
            whole((rows, width)),
            pl.BlockSpec((tile, width), lambda step: (step, 0)),
            pl.BlockSpec((tile, tile), lambda step: (step, 0)),
        ],
        out_shape=[
            jax.ShapeDtypeStruct((rows, width), bf16),
            jax.ShapeDtypeStruct((rows, width), bf16),
            jax.ShapeDtypeStruct((rows, tile), f32),
        ],
        scratch_shapes=[pltpu.VMEM((heads_dev, tile, 2 * length), f32)],
        compiler_params=pltpu.CompilerParams(vmem_limit_bytes=40 * 2**20),
        cost_estimate=pl.CostEstimate(
            flops=4 * rows * length * width,
            bytes_accessed=4 * length * width * 2,
            transcendentals=rows * length * heads_dev,
        ),
    )(first, place, table, near, qkv, doc_row, doc_col)


def attention_back(
    qkv, doc_row, doc_col, attended, grad_out, stats, first, place, table, near, split
):
    length = qkv.shape[0]
    rows = grad_out.shape[0]
    heads_dev = table.shape[1]
    width = heads_dev * head_dim
    return pl.pallas_call(
        functools.partial(attention_back_kernel, heads_dev, length, split),
        grid=(rows // tile,),
        in_specs=[
            pl.BlockSpec(memory_space=pltpu.SMEM),
            pl.BlockSpec(memory_space=pltpu.SMEM),
            pl.BlockSpec(memory_space=pltpu.SMEM),
            whole(near.shape),
            whole(qkv.shape),
            whole(doc_row.shape),
            pl.BlockSpec((tile, 1), lambda step: (step, 0)),
            whole((rows, width)),
            whole((rows, width)),
            pl.BlockSpec((tile, tile), lambda step: (step, 0)),
        ],
        out_specs=[
            whole((length, 3 * width)),
            whole((heads_dev, tile, 3 * tile)),
            whole((heads_dev, 2, 8, tile)),
        ],
        out_shape=[
            jax.ShapeDtypeStruct((length, 3 * width), bf16),
            jax.ShapeDtypeStruct((heads_dev, tile, 3 * tile), f32),
            jax.ShapeDtypeStruct((heads_dev, 2, 8, tile), f32),
        ],
        scratch_shapes=[
            pltpu.VMEM((heads_dev, tile, 2 * length), f32),
            pltpu.VMEM((heads_dev, tile, 2 * length), f32),
            pltpu.VMEM((length, width), f32),
            pltpu.VMEM((length, width), f32),
        ],
        compiler_params=pltpu.CompilerParams(vmem_limit_bytes=48 * 2**20),
        cost_estimate=pl.CostEstimate(
            flops=10 * rows * length * width,
            bytes_accessed=8 * length * width * 2,
            transcendentals=rows * length * heads_dev,
        ),
    )(first, place, table, near, qkv, doc_row, doc_col, attended, grad_out, stats)


def call(kernel, shapes, *operands, smem=0):
    return pl.pallas_call(
        kernel,
        in_specs=[pl.BlockSpec(memory_space=pltpu.SMEM)] * smem
        + [pl.BlockSpec(memory_space=pltpu.VMEM)] * (len(operands) - smem),
        out_specs=[pl.BlockSpec(memory_space=pltpu.VMEM)] * len(shapes),
        out_shape=[jax.ShapeDtypeStruct(shape, kind) for shape, kind in shapes],
        compiler_params=pltpu.CompilerParams(vmem_limit_bytes=10 * 2**20),
    )(*operands)


def share_in_kernel(place, attn_in, gains, near, far):
    layers, rows = attn_in.shape[:2]
    half = near.shape[0] // (layers * rows)
    width = near.shape[1] // 3
    for index in range(2 * half):
        member = place[index]
        for layer_id in range(layers):
            block = jnp.concatenate(
                [
                    attn_in[
                        layer_id,
                        :,
                        pl.ds(pl.multiple_of((part * 2 * half + member) * width, width), width),
                    ]
                    for part in range(3)
                ],
                axis=1,
            )
            at = (index % half * layers + layer_id) * rows
            out = near if index < half else far
            out[at : at + rows] = (block.astype(f32) * gains[layer_id]).astype(bf16)


def join_kernel(*refs):
    shares, outs = refs[:4], refs[4:]
    rows = outs[0].shape[0] // 8
    for chip, share in enumerate(shares):
        for core in range(2):
            for layer_id, out in enumerate(outs):
                source = (core * len(outs) + layer_id) * rows
                target = (chip * 2 + core) * rows
                out[target : target + rows] = share[source : source + rows]


def row_of(chip, plane, core, rows, planes=4):
    return pl.multiple_of(((chip * planes + plane) * 2 + core) * rows, rows)


def assemble_in_kernel(place, own, lower, upper, opposite, out):
    at_z, at_core, at_head = place[8], place[0] % 2, place[0] // 2
    rows = own.shape[0] // 8
    for part, offset in ((own, 0), (lower, 3), (upper, 1), (opposite, 2)):
        plane = (at_z + offset) % 4
        for index in range(8):
            row = row_of(at_head ^ (index // 2), plane, at_core ^ (index % 2), rows)
            out[pl.ds(row, rows)] = part[index * rows : (index + 1) * rows]


def plane_attention_kernel(
    length, place, table, strip, near, far, w_in, *refs
):
    halves, (doc_row, doc_col, w_out, qkv, attended, stats, near_part, far_part, band) = (
        refs[:2], refs[2:],
    )
    step = pl.program_id(0)
    half = length // 2
    heads_dev = table.shape[1]
    width = heads_dev * head_dim

    @pl.when(step == 0)
    def _():
        fill_band(band, table, strip, heads_dev, length)
        swapped = place[length // tile] % 2 == 1
        rows = width // 2
        w_out[:rows] = jnp.where(swapped, halves[1][...], halves[0][...])
        w_out[rows:] = jnp.where(swapped, halves[0][...], halves[1][...])
        qkv[:half] = contract(near[...], w_in[...], 1, 0).astype(bf16)
        qkv[half:] = contract(far[...], w_in[...], 1, 0).astype(bf16)

    row = pl.multiple_of(step * tile, tile)
    starts = band_starts(place, step, length, length // tile + 1)
    same_doc = doc_col[...] == doc_row[...]
    queries = qkv[pl.ds(row, tile), :width] * bf16(score_scale)
    lanes = lax.broadcasted_iota(jnp.int32, (tile, tile), 1)
    collected = jnp.zeros((tile, tile), f32)
    results = []
    for head in range(heads_dev):
        own = slice(head * head_dim, (head + 1) * head_dim)
        keys = qkv[:, width + own.start : width + own.stop]
        values = qkv[:, 2 * width + own.start : 2 * width + own.stop]
        scores = contract(queries[:, own], keys, 1, 1) + jnp.concatenate(
            [band[head, :, pl.ds(start, tile)] for start in starts], axis=1
        )
        scores = jnp.where(same_doc, scores, masked)
        peak = jnp.max(scores, axis=1, keepdims=True)
        weights = jnp.exp(scores - peak)
        total = jnp.sum(weights, axis=1, keepdims=True)
        results.append((contract(weights.astype(bf16), values, 1, 0) / total).astype(bf16))
        collected = jnp.where(lanes == head, peak + jnp.log(total), collected)
    stats[...] = collected
    merged = jnp.concatenate(results, axis=1)
    attended[...] = merged
    part = contract(merged, w_out[...], 1, 0)

    @pl.when(row < half)
    def _():
        near_part[...] = part

    @pl.when(row >= half)
    def _():
        far_part[...] = part.astype(bf16)


def near_block(steps, columns):
    return pl.BlockSpec((tile, columns), lambda step: (jnp.minimum(step, steps // 2 - 1), 0))


def far_block(steps, columns):
    return pl.BlockSpec((tile, columns), lambda step: (jnp.maximum(step - steps // 2, 0), 0))


def plane_attention(near, far, w_in, halves, doc_row, doc_col, place, table, strip):
    length, model_width = 2 * near.shape[0], near.shape[1]
    steps = length // tile
    heads_dev = table.shape[1]
    width = heads_dev * head_dim
    return pl.pallas_call(
        functools.partial(plane_attention_kernel, length),
        grid=(steps,),
        in_specs=[
            pl.BlockSpec(memory_space=pltpu.SMEM),
            pl.BlockSpec(memory_space=pltpu.SMEM),
            whole(strip.shape),
            whole(near.shape),
            whole(far.shape),
            whole(w_in.shape),
            *[whole(half.shape) for half in halves],
            whole(doc_row.shape),
            pl.BlockSpec((tile, 1), lambda step: (step, 0)),
        ],
        out_specs=[
            whole((width, model_width)),
            whole((length, 3 * width)),
            pl.BlockSpec((tile, width), lambda step: (step, 0)),
            pl.BlockSpec((tile, tile), lambda step: (step, 0)),
            near_block(steps, model_width),
            far_block(steps, model_width),
        ],
        out_shape=[
            jax.ShapeDtypeStruct((width, model_width), bf16),
            jax.ShapeDtypeStruct((length, 3 * width), bf16),
            jax.ShapeDtypeStruct((length, width), bf16),
            jax.ShapeDtypeStruct((length, tile), f32),
            jax.ShapeDtypeStruct((length // 2, model_width), f32),
            jax.ShapeDtypeStruct((length // 2, model_width), bf16),
        ],
        scratch_shapes=[pltpu.VMEM((heads_dev, tile, 2 * length), f32)],
        compiler_params=pltpu.CompilerParams(vmem_limit_bytes=14 * 2**20),
        cost_estimate=pl.CostEstimate(
            flops=4 * length * length * width + 8 * length * model_width * width,
            bytes_accessed=12 * 2**20,
            transcendentals=length * length * heads_dev,
        ),
    )(place, table, strip, near, far, w_in, *halves, doc_row, doc_col)


def plane_attention_back_kernel(
    length, place, table, strip, qkv, doc_row, doc_col, attended, stats, near, far, w_in, w_out,
    grad_qkv, grad_near, grad_far, near_part, far_part, *rest
):
    halves, (band, grad_band, grad_keys, grad_values, out_sum) = rest[:2], rest[2:]
    step = pl.program_id(0)
    half = length // 2
    heads_dev = table.shape[1]
    width = heads_dev * head_dim

    @pl.when(step == 0)
    def _():
        fill_band(band, table, strip, heads_dev, length)
        grad_band[...] = jnp.zeros_like(grad_band)
        grad_keys[...] = jnp.zeros_like(grad_keys)
        grad_values[...] = jnp.zeros_like(grad_values)
        out_sum[...] = jnp.zeros_like(out_sum)

    row = pl.multiple_of(step * half, half)
    branch = jnp.where(step == 0, near[...], far[...])
    merged = attended[...]
    grad_merged = contract(branch, w_out[...], 1, 1).astype(bf16)
    out_sum[...] += contract(merged, branch, 0, 0)
    products = grad_merged.astype(f32) * merged.astype(f32)
    queries = qkv[pl.ds(row, half), :width] * bf16(score_scale)
    blocks = half // tile
    for head in range(heads_dev):
        own = slice(head * head_dim, (head + 1) * head_dim)
        keys = qkv[:, width + own.start : width + own.stop]
        values = qkv[:, 2 * width + own.start : 2 * width + own.stop]
        upstream = grad_merged[:, own]
        raw_scores = contract(queries[:, own], keys, 1, 1)
        grad_weights = contract(upstream, values, 1, 1)
        delta = jnp.sum(products[:, own], axis=1, keepdims=True)
        weights_low, grads_low = [], []
        for block in range(blocks):
            lines = slice(block * tile, (block + 1) * tile)
            starts = band_starts(place, step * blocks + block, length, length // tile + 1)
            scores = raw_scores[lines] + jnp.concatenate(
                [band[head, :, pl.ds(start, tile)] for start in starts], axis=1
            )
            scores = jnp.where(doc_col[lines] == doc_row[...], scores, masked)
            weights = jnp.exp(scores - stats[lines, head : head + 1])
            grad_scores = weights * (grad_weights[lines] - delta[lines])
            for index, start in enumerate(starts):
                grad_band[head, :, pl.ds(start, tile)] += grad_scores[
                    :, index * tile : (index + 1) * tile
                ]
            weights_low.append(weights.astype(bf16))
            grads_low.append(grad_scores.astype(bf16))
        weights_low, grads_low = jnp.concatenate(weights_low), jnp.concatenate(grads_low)
        grad_values[:, own] += contract(weights_low, upstream, 0, 0)
        grad_keys[:, own] += contract(grads_low, queries[:, own], 0, 0)
        grad_qkv[pl.ds(row, half), own] = (
            contract(grads_low, keys, 1, 0) * score_scale
        ).astype(bf16)

    @pl.when(step == pl.num_programs(0) - 1)
    def _():
        grad_qkv[:, width : 2 * width] = grad_keys[...].astype(bf16)
        grad_qkv[:, 2 * width :] = grad_values[...].astype(bf16)
        far_part[...] = contract(grad_qkv[half:], w_in[...], 1, 1).astype(bf16)
        near_part[...] = contract(grad_qkv[:half], w_in[...], 1, 1)
        rows = width // 2
        for index, part in enumerate(halves):
            block = index ^ place[length // tile] % 2
            part[...] = out_sum[pl.ds(pl.multiple_of(block * rows, rows), rows)].astype(bf16)
        for head in range(heads_dev):
            grad_near[head] = grad_band[head, :, length - tile : length + 2 * tile]
            grad_far[head, 0] = jnp.full(
                (8, tile), jnp.sum(grad_band[head, :, : length - tile]), f32
            )
            grad_far[head, 1] = jnp.full(
                (8, tile), jnp.sum(grad_band[head, :, length + 2 * tile :]), f32
            )


def plane_attention_back(
    qkv, doc_row, doc_col, attended, stats, near, far, w_in, w_out, place, table, strip
):
    length, model_width = 2 * near.shape[0], near.shape[1]
    half = length // 2
    heads_dev = table.shape[1]
    width = heads_dev * head_dim
    shapes = [
        ((length, 3 * width), bf16),
        ((heads_dev, tile, 3 * tile), f32),
        ((heads_dev, 2, 8, tile), f32),
        ((length // 2, model_width), f32),
        ((length // 2, model_width), bf16),
    ] + [((width // 2, model_width), bf16)] * 2
    return pl.pallas_call(
        functools.partial(plane_attention_back_kernel, length),
        grid=(2,),
        in_specs=[
            pl.BlockSpec(memory_space=pltpu.SMEM),
            pl.BlockSpec(memory_space=pltpu.SMEM),
            whole(strip.shape),
            whole(qkv.shape),
            whole(doc_row.shape),
            pl.BlockSpec((half, 1), lambda step: (step, 0)),
            pl.BlockSpec((half, width), lambda step: (step, 0)),
            pl.BlockSpec((half, tile), lambda step: (step, 0)),
            whole((half, model_width)),
            whole((half, model_width)),
            whole(w_in.shape),
            whole(w_out.shape),
        ],
        out_specs=[whole(shape) for shape, _ in shapes],
        out_shape=[jax.ShapeDtypeStruct(shape, kind) for shape, kind in shapes],
        scratch_shapes=[
            pltpu.VMEM((heads_dev, tile, 2 * length), f32),
            pltpu.VMEM((heads_dev, tile, 2 * length), f32),
            pltpu.VMEM((length, width), f32),
            pltpu.VMEM((length, width), f32),
            pltpu.VMEM((width, model_width), f32),
        ],
        compiler_params=pltpu.CompilerParams(vmem_limit_bytes=32 * 2**20),
        cost_estimate=pl.CostEstimate(
            flops=10 * length * length * width + 10 * length * model_width * width,
            bytes_accessed=12 * 2**20,
            transcendentals=length * length * heads_dev,
        ),
    )(place, table, strip, qkv, doc_row, doc_col, attended, stats, near, far, w_in, w_out)


def gelu_and_slope(pre_act):
    size = jnp.abs(pre_act)
    gauss = jnp.exp(-0.5 * pre_act * pre_act)
    ratio = 1.0 / (1.0 + np.float32(0.3275911 * 0.5**0.5) * size)
    series = np.float32(1.061405429)
    for factor in (-1.453152027, 1.421413741, -0.284496736, 0.254829592):
        series = series * ratio + np.float32(factor)
    tail = 0.5 * series * ratio * gauss
    cumulative = jnp.where(pre_act < 0, tail, 1.0 - tail)
    slope = cumulative + pre_act * gauss * np.float32((2 * np.pi) ** -0.5)
    return pre_act * cumulative, slope


def ff_kernel(rows, pair, activated, slope, part):
    columns = rows.shape[1]
    value, gradient = gelu_and_slope(contract(rows[...], pair[:, :columns], 1, 1))
    activated[...] = value.astype(bf16)
    slope[...] = gradient.astype(bf16)
    part[...] = contract(activated[...], pair[:, columns:], 1, 0).astype(part.dtype)


def ff_first_kernel(rows, *refs):
    parts, (activated, slope, part, pair) = refs[:5], refs[5:]

    @pl.when(pl.program_id(0) == 0)
    def _():
        units, columns = parts[0].shape[0], rows.shape[1]
        for index, ref in enumerate(parts[:3]):
            pair[index * units : (index + 1) * units] = ref[...]
        pair[3 * units :, :columns] = parts[3][...]
        pair[3 * units :, columns:] = parts[4][...]

    ff_kernel(rows, pair, activated, slope, part)


def ff_back_kernel(rows, slope, pair, grad_pre, part):
    columns = rows.shape[1]
    grad_act = contract(rows[...], pair[:, columns:], 1, 1)
    grad_pre[...] = (grad_act * slope[...].astype(f32)).astype(bf16)
    part[...] = contract(grad_pre[...], pair[:, :columns], 1, 0).astype(part.dtype)


def by_rows(kernel, step_rows, row_operands, whole_operands, outs, whole_outs=()):
    rows = row_operands[0].shape[0]
    return pl.pallas_call(
        kernel,
        grid=(rows // step_rows,),
        in_specs=[
            pl.BlockSpec((step_rows, operand.shape[1]), lambda step: (step, 0))
            for operand in row_operands
        ]
        + [whole(operand.shape) for operand in whole_operands],
        out_specs=[pl.BlockSpec((step_rows, columns), lambda step: (step, 0)) for columns, _ in outs]
        + [whole(shape) for shape in whole_outs],
        out_shape=[jax.ShapeDtypeStruct((rows, columns), kind) for columns, kind in outs]
        + [jax.ShapeDtypeStruct(shape, bf16) for shape in whole_outs],
        compiler_params=pltpu.CompilerParams(vmem_limit_bytes=10 * 2**20),
        cost_estimate=pl.CostEstimate(
            flops=4 * rows * outs[0][0] * row_operands[0].shape[1],
            bytes_accessed=6 * 2**20,
            transcendentals=0,
        ),
    )(*row_operands, *whole_operands)


def ff_grads_kernel(
    pre_near, pre_far, act_near, act_far, normed_near, normed_far, low_near, low_far, *outs
):
    columns = normed_near.shape[1]
    units = outs[0].shape[0]
    up = (
        contract(pre_near[...], normed_near[...], 0, 0)
        + contract(pre_far[...], normed_far[...], 0, 0)
    ).astype(bf16)
    down = (
        contract(act_near[...], low_near[...], 0, 0) + contract(act_far[...], low_far[...], 0, 0)
    ).astype(bf16)

    @pl.when(pl.program_id(0) == 0)
    def _():
        for index in range(2):
            block = slice(index * units, (index + 1) * units)
            outs[index][:, :columns] = up[block]
            outs[index][:, columns:] = down[block]

    @pl.when(pl.program_id(0) == 1)
    def _():
        outs[2][:, :columns] = up[:units]
        outs[2][:, columns:] = down[:units]
        outs[3][...] = up[units:]
        outs[4][...] = down[units:]


def ff_grads(pre, act, normed, low):
    rows, hidden_units = pre[0].shape
    columns = normed[0].shape[1]
    shapes = [(hidden_units // 4, 2 * columns)] * 3 + [(hidden_units // 4, columns)] * 2
    return pl.pallas_call(
        ff_grads_kernel,
        grid=(2,),
        in_specs=[pl.BlockSpec((rows, hidden_units // 2), lambda step: (0, step))] * 4
        + [whole((rows, columns))] * 4,
        out_specs=[whole(shape) for shape in shapes],
        out_shape=[jax.ShapeDtypeStruct(shape, bf16) for shape in shapes],
        compiler_params=pltpu.CompilerParams(vmem_limit_bytes=14 * 2**20),
        cost_estimate=pl.CostEstimate(
            flops=8 * rows * hidden_units * columns, bytes_accessed=8 * 2**20, transcendentals=0
        ),
    )(*pre, *act, *normed, *low)


def in_grads_kernel(place, near, far, grad_qkv, *refs):
    ends, outs, (total, extra) = refs[:-6], refs[-6:-2], refs[-2:]
    half = near.shape[0]
    columns = grad_qkv.shape[1]
    total[:, :columns] = (
        contract(near[...], grad_qkv[:half], 0, 0) + contract(far[...], grad_qkv[half:], 0, 0)
    ).astype(bf16)
    rows = outs[0].shape[0] // 8
    if ends:
        gain_0, gain_1, table_0, table_1 = ends
        lines = lax.broadcasted_iota(jnp.int32, (tile, gain_0.shape[1]), 0)
        gains = jnp.where(lines == 0, gain_0[...], jnp.where(lines == 1, gain_1[...], 0.0))
        extra[...] = jnp.transpose(gains)
        table = table_0[...] + table_1[...]
        buckets = table.shape[0] // 8
        blank = jnp.zeros((8 - buckets, tile), f32)
        for block in range(8):
            row = pl.multiple_of((place[0] // 2 * 8 + block) * rows, rows)
            extra[pl.ds(row, 8)] += jnp.concatenate(
                [table[block * buckets : (block + 1) * buckets], blank]
            )
        total[:, columns:] = extra[...].astype(bf16)
    for out, offset in zip(outs, (0, 3, 1, 2)):
        plane = (place[8] + offset) % 4
        for index in range(8):
            owner = place[index]
            row = row_of(owner // 2, plane, owner % 2, rows)
            out[index * rows : (index + 1) * rows] = total[pl.ds(row, rows)]


def in_grads(place, near, far, grad_qkv, *ends):
    columns = grad_qkv.shape[1] + (tile if ends else 0)
    shape = (near.shape[1] // 4, columns)
    return pl.pallas_call(
        in_grads_kernel,
        in_specs=[pl.BlockSpec(memory_space=pltpu.SMEM)]
        + [pl.BlockSpec(memory_space=pltpu.VMEM)] * (3 + len(ends)),
        out_specs=[pl.BlockSpec(memory_space=pltpu.VMEM)] * 4,
        out_shape=[jax.ShapeDtypeStruct(shape, bf16)] * 4,
        scratch_shapes=[
            pltpu.VMEM((near.shape[1], columns), bf16),
            pltpu.VMEM((near.shape[1], tile), f32),
        ],
        compiler_params=pltpu.CompilerParams(vmem_limit_bytes=14 * 2**20),
        cost_estimate=pl.CostEstimate(
            flops=4 * near.shape[0] * near.shape[1] * columns,
            bytes_accessed=4 * 2**20,
            transcendentals=0,
        ),
    )(place, near, far, grad_qkv, *ends)


def add_in_kernel(own, lower, upper, opposite, near, far):
    total = sum_of_four([own, lower, upper, opposite]).astype(bf16)
    half = near.shape[0]
    near[...] = total[:half]
    far[...] = total[half:]


def combine_kernel(near_part, arrived, own, x_part, y_part, xy_part):
    rows = own.shape[0]
    own[...] = near_part[:rows] + arrived[:rows].astype(f32)
    for bits, out in ((1, x_part), (2, y_part), (3, xy_part)):
        block = slice(bits * rows, (bits + 1) * rows)
        out[...] = (near_part[block] + arrived[block].astype(f32)).astype(bf16)


def added(own, x_part, y_part, xy_part):
    return (own[...] + x_part[...].astype(f32)) + (
        y_part[...].astype(f32) + xy_part[...].astype(f32)
    )


def close_kernel(kept, own, x_part, y_part, xy_part, hidden, units):
    total = kept[...] + added(own, x_part, y_part, xy_part)
    hidden[...] = total
    units[...] = (total * inverse_rms(total)).astype(bf16)


def close_gain_kernel(kept, own, x_part, y_part, xy_part, gain, hidden, normed):
    total = kept[...] + added(own, x_part, y_part, xy_part)
    hidden[...] = total
    normed[...] = (total * inverse_rms(total) * gain[...]).astype(bf16)


def widen_kernel(low, out):
    out[...] = low[...].astype(f32)


def last_kernel(kept, own, x_part, y_part, xy_part, hidden):
    hidden[...] = (kept[...] + added(own, x_part, y_part, xy_part)).astype(bf16)


def middle_back_kernel(
    upstream, own, x_part, y_part, xy_part, middle, gain, grad_middle, branch, grad_gain
):
    grad_normed = added(own, x_part, y_part, xy_part)
    inverse = inverse_rms(middle[...])
    grad_gain[...] = jnp.sum(grad_normed * middle[...] * inverse, axis=0, keepdims=True)
    total = upstream[...].astype(f32) + unit_norm_back(
        middle[...], inverse, grad_normed * gain[...]
    )
    grad_middle[...] = total
    branch[...] = total.astype(bf16)


def layer_back_kernel(grad_middle, own, x_part, y_part, xy_part, hidden, upstream, low):
    total = grad_middle[...] + unit_norm_back(
        hidden[...], inverse_rms(hidden[...]), added(own, x_part, y_part, xy_part)
    )
    upstream[...] = total
    low[...] = total.astype(bf16)


def pair_kernel(axis, near, arrived, *outs):
    rows = near.shape[0] // len(outs)
    for index, out in enumerate(outs):
        block = slice(index * rows, (index + 1) * rows)
        if axis == 0:
            out[:rows] = near[block]
            out[rows:] = arrived[block]
        else:
            columns = near.shape[1]
            out[:, :columns] = near[block]
            out[:, columns:] = arrived[block]


def unit_kernel(tokens, hidden, units):
    total = tokens[...].astype(f32)
    hidden[...] = total
    units[...] = (total * inverse_rms(total)).astype(bf16)


def finish_in_kernel(place, *refs):
    chips, (attn_in, gains, grad_in, grad_gain, ends) = refs[:8], refs[8:]
    rows = attn_in.shape[1]
    width = tile
    members = attn_in.shape[2] // (3 * width)
    ends[...] = jnp.zeros_like(ends)
    for layer_id in range(2):
        row_dot = jnp.zeros((rows, 1), f32)
        for index in range(members):
            member = place[index]
            chip = chips[4 * layer_id + index % 4]
            half = chip.shape[1] // 2
            total = chip[:, index // 4 * half : (index // 4 + 1) * half].astype(f32)
            if layer_id == 0:
                ends[...] += total[:, 3 * width :]
            for part in range(3):
                block = total[:, part * width : (part + 1) * width]
                columns = pl.ds(pl.multiple_of((part * members + member) * width, width), width)
                grad_in[layer_id, :, columns] = block * gains[layer_id]
                row_dot = row_dot + jnp.sum(
                    block * attn_in[layer_id, :, columns].astype(f32), axis=1, keepdims=True
                )
        grad_gain[layer_id] = jnp.concatenate(
            [row_dot, ends[:, layer_id : layer_id + 1]], axis=1
        )


def sum_of_four(parts):
    return (parts[0][...].astype(f32) + parts[1][...].astype(f32)) + (
        parts[2][...].astype(f32) + parts[3][...].astype(f32)
    )


def finish_ff_kernel(*refs):
    count = (len(refs) - 3) // 2
    sources, grads, held, done = refs[:count], refs[count : count + 2], refs[count + 2 : -1], refs[-1]
    copies = [
        pltpu.make_async_copy(source, target, done.at[index])
        for index, (source, target) in enumerate(zip(sources, held))
    ]
    for copy in copies:
        copy.start()
    for copy in copies:
        copy.wait()
    refs = held
    columns = grads[0].shape[2]
    for layer_id in range(grads[0].shape[0]):
        parts = refs[5 * layer_id : 5 * layer_id + 5]
        for side, out in enumerate(grads):
            halves = [part.at[:, side * columns : (side + 1) * columns] for part in parts[:3]]
            out[layer_id] = sum_of_four(halves + [parts[3 + side]])


def finish_ff(grads, shape):
    return pl.pallas_call(
        finish_ff_kernel,
        in_specs=[pl.BlockSpec(memory_space=pl.ANY)] * len(grads),
        out_specs=[pl.BlockSpec(memory_space=pltpu.VMEM)] * 2,
        out_shape=[jax.ShapeDtypeStruct(shape, f32)] * 2,
        scratch_shapes=[pltpu.VMEM(grad.shape, bf16) for grad in grads]
        + [pltpu.SemaphoreType.DMA((len(grads),))],
        compiler_params=pltpu.CompilerParams(vmem_limit_bytes=14 * 2**20),
    )(*grads)


def add_out_kernel(place, *refs):
    parts, (own, other) = refs[:-2], refs[-2:]
    for layer_id in range(own.shape[0]):
        total = parts[2 * layer_id][...].astype(f32) + parts[2 * layer_id + 1][...].astype(f32)
        rows = total.shape[0] // 2
        second = place[0] % 2 == 1
        own[layer_id] = jnp.where(second, total[rows:], total[:rows])
        other[layer_id] = jnp.where(second, total[:rows], total[rows:]).astype(bf16)


def finish_out_kernel(own, arrived, out):
    out[...] = own[...] + arrived[...].astype(f32)


def inverse_rms(hidden):
    return lax.rsqrt(jnp.mean(hidden * hidden, axis=-1, keepdims=True) + epsilon)


def prepare(bias_table, first_head, heads_dev):
    table = lax.dynamic_slice_in_dim(bias_table, first_head, heads_dev, 1)
    (near,) = call(near_kernel, [((heads_dev, tile, 3 * tile), f32)], table, smem=1)
    return table, near


def bucket_grads(first_lane, grads, bucket_count):
    (total,) = call(bucket_kernel, [((bucket_count, tile), f32)], first_lane, *grads, smem=1)
    return total


def gelu_parts(pre_act):
    cumulative = 0.5 * (1.0 + lax.erf(pre_act * np.float32(0.5**0.5)))
    slope = cumulative + pre_act * jnp.exp(-0.5 * pre_act * pre_act) * np.float32(
        (2 * np.pi) ** -0.5
    )
    return (pre_act * cumulative).astype(bf16), slope


def unit_norm_back(hidden, inverse, grad_unit):
    unit = hidden * inverse
    return inverse * (grad_unit - unit * jnp.mean(grad_unit * unit, axis=-1, keepdims=True))


def gather_rows(block, axes):
    return lax.all_gather(block, axes, axis=0, tiled=True)


def toggle(array, axis, bits):
    return lax.ppermute(array, axis, [(i, i ^ bits) for i in range(lax.axis_size(axis))])


def shift(array, by):
    planes = lax.axis_size("z")
    return lax.ppermute(array, "z", [(i, (i + by) % planes) for i in range(planes)])


def plane_gather(block, *holds):
    near = jnp.concatenate([block] + [toggle(block, "head", bits) for bits in (1, 2, 3)])
    near, *holds = tie(near, *holds)
    return (near, toggle(near, "core", 1), *holds)


def plane_scatter(near_part, far_part):
    rows, columns = near_part.shape[0] // 4, near_part.shape[1]
    own, *others = call(
        combine_kernel,
        [((rows, columns), f32)] + [((rows, columns), bf16)] * 3,
        near_part,
        toggle(far_part, "core", 1),
    )
    shares = [own] + [toggle(other, "head", bits) for bits, other in zip((1, 2, 3), others)]
    return shares, own


def tie(*arrays):
    return lax.optimization_barrier(arrays)


def after(array, other):
    return lax.optimization_barrier((array, other))[0]


def scatter_sum(partial, axes, members):
    blocks = partial.astype(bf16).reshape(members, -1, partial.shape[1])
    return jnp.sum(lax.all_to_all(blocks, axes, 0, 0, tiled=True).astype(f32), axis=0)


def local_general(tokens, doc_start, bias_table, attn_in, attn_out, ff_in, ff_out, gains, cotangent):
    heads_n, z_n, core_n = (lax.axis_size(axis) for axis in everyone)
    devices = heads_n * z_n * core_n
    group, spare = ("z", "core"), "head"
    ff_group, ff_spare, ff_members = ("head", "core"), "z", heads_n * core_n
    blocks = z_n * core_n
    block_rows, model_width = tokens.shape[1:]
    layer_count, weight_rows = attn_in.shape[:2]
    length = block_rows * blocks
    heads_all = bias_table.shape[1]
    member = lax.axis_index("z") * core_n + lax.axis_index("core")
    heads_dev = max(1, heads_all // blocks)
    head_groups = heads_all // heads_dev
    split = blocks // head_groups
    head_group, query_part = member // split, member % split
    query_rows = length // split
    width = heads_dev * head_dim
    first = (query_part * (query_rows // tile)).astype(jnp.int32).reshape(1)
    place = jnp.arange(length // tile, dtype=jnp.int32)
    out_row = head_group * width

    def swap(array):
        return lax.all_to_all(array, everyone, 0, 0, tiled=True)

    starts = jnp.broadcast_to(
        doc_start.astype(f32)[:, None], (heads_n, blocks, block_rows)
    ).reshape(devices, block_rows)
    ff_gains = gains[:, :, 1].astype(f32).reshape(1, -1)
    small = swap(
        jnp.concatenate(
            [starts, jnp.broadcast_to(ff_gains, (devices, layer_count * weight_rows))], axis=1
        )
    )
    doc_row = small[:blocks, :block_rows].reshape(1, length)
    doc_col = lax.dynamic_slice_in_dim(
        doc_row.reshape(length, 1), query_part * query_rows, query_rows, 0
    )
    gain_ff = jnp.transpose(
        small[:, block_rows:].reshape(devices, layer_count, weight_rows), (1, 0, 2)
    ).reshape(layer_count, 1, model_width)
    table, near = prepare(bias_table, head_group * heads_dev, heads_dev)

    gain_attn = gains[:, :, 0].astype(f32)[:, :, None]
    own_in = attn_in.astype(f32)

    def fetch_in(layer_id):
        scaled = (own_in[layer_id] * gain_attn[layer_id]).astype(bf16)
        columns = jnp.transpose(
            scaled.reshape(weight_rows, 3, head_groups, width), (2, 0, 1, 3)
        ).reshape(head_groups, weight_rows, 3 * width)
        columns = jnp.repeat(columns, split, axis=0)
        columns = jnp.broadcast_to(columns[None], (heads_n, *columns.shape))
        return swap(columns.reshape(devices, weight_rows, 3 * width)).reshape(
            model_width, 3 * width
        )

    def fetch_ff(layer_id):
        pair = jnp.concatenate([ff_in[layer_id], ff_out[layer_id]], axis=1)
        pair = gather_rows(pair, ff_spare)
        return pair[:, :model_width], pair[:, model_width:]

    hidden, upstream = tokens[0].astype(f32), cotangent[0]
    weights_in = [fetch_in(layer_id) for layer_id in range(layer_count)]
    weights_out = lax.dynamic_slice_in_dim(
        lax.all_gather(attn_out, everyone, axis=1, tiled=True), out_row, width, 1
    )
    weights_ff = [fetch_ff(layer_id) for layer_id in range(layer_count)]

    records = []
    for layer_id in range(layer_count):
        w_in, w_out, (w_up, w_down) = (
            weights_in[layer_id], weights_out[layer_id], weights_ff[layer_id],
        )
        inverse = inverse_rms(hidden)
        units = gather_rows((hidden * inverse).astype(bf16), group)
        qkv = jnp.dot(units, w_in, preferred_element_type=f32).astype(bf16)
        attended, _, stats = attention(
            qkv, doc_row, doc_col, first, place, table, near, query_rows
        )
        mixed = jnp.dot(attended, w_out, preferred_element_type=f32)
        if split > 1:
            mixed = lax.dynamic_update_slice_in_dim(
                jnp.zeros((length, model_width), f32), mixed, query_part * query_rows, 0
            )
        middle = hidden + scatter_sum(mixed, group, blocks)
        inverse_ff = inverse_rms(middle)
        normed_ff = gather_rows((middle * inverse_ff * gain_ff[layer_id]).astype(bf16), ff_group)
        activated, slope = gelu_parts(contract(normed_ff, w_up, 1, 1))
        ff_result = jnp.dot(activated, w_down, preferred_element_type=f32)
        records.append(
            (hidden, inverse, units, qkv, attended, stats, middle, inverse_ff, normed_ff,
             activated, slope)
        )
        hidden = middle + scatter_sum(ff_result, ff_group, ff_members)
    output = hidden

    grads_ff, grads_in, grads_out, grads_gain_ff, grads_table = (
        [None] * layer_count for _ in range(5)
    )
    for layer_id in reversed(range(layer_count)):
        w_in, w_out, (w_up, w_down) = (
            weights_in[layer_id], weights_out[layer_id], weights_ff[layer_id],
        )
        (hidden, inverse, units, qkv, attended, stats, middle, inverse_ff, normed_ff,
         activated, slope) = records[layer_id]
        grad_low = gather_rows(upstream.astype(bf16), ff_group)
        grad_pre = (contract(grad_low, w_down, 1, 1) * slope).astype(bf16)
        grad_normed = scatter_sum(
            jnp.dot(grad_pre, w_up, preferred_element_type=f32), ff_group, ff_members
        )
        grad_pair = jnp.concatenate(
            [contract(grad_pre, normed_ff, 0, 0), contract(activated, grad_low, 0, 0)], axis=1
        ).astype(bf16)
        grads_ff[layer_id] = lax.psum_scatter(
            grad_pair, ff_spare, scatter_dimension=0, tiled=True
        ).astype(f32)
        grads_gain_ff[layer_id] = jnp.sum(grad_normed * middle * inverse_ff, axis=0)
        grad_middle = upstream + unit_norm_back(
            middle, inverse_ff, grad_normed * gain_ff[layer_id]
        )
        branch = gather_rows(grad_middle.astype(bf16), group)
        if split > 1:
            branch = lax.dynamic_slice_in_dim(branch, query_part * query_rows, query_rows, 0)
        grad_attended = contract(branch, w_out, 1, 1).astype(bf16)
        grad_qkv, grad_near, grad_far = attention_back(
            qkv, doc_row, doc_col, attended, grad_attended, stats, first, place, table, near, split
        )
        grads_table[layer_id] = (grad_near, grad_far)
        grad_units = scatter_sum(contract(grad_qkv, w_in, 1, 1), group, blocks)
        upstream = grad_middle + unit_norm_back(hidden, inverse, grad_units)
        grad_out = lax.dynamic_update_slice_in_dim(
            jnp.zeros((model_width, model_width), bf16),
            contract(attended, branch, 0, 0).astype(bf16),
            out_row,
            0,
        )
        grads_out[layer_id] = lax.psum_scatter(
            grad_out, everyone, scatter_dimension=0, tiled=True
        ).astype(f32)
        grads_in[layer_id] = contract(units, grad_qkv, 0, 0).astype(bf16)

    bucket_count = table.shape[0]
    grad_table = sum(
        bucket_grads(jnp.zeros((1,), jnp.int32), entry, bucket_count) for entry in grads_table
    )[:, :heads_dev]
    grad_table = lax.dynamic_update_slice_in_dim(
        jnp.zeros((bucket_count, heads_all), f32), grad_table, head_group * heads_dev, 1
    )
    grad_table = jnp.transpose(
        grad_table.reshape(blocks, bucket_count // blocks, heads_n, heads_all // heads_n),
        (2, 0, 1, 3),
    ).reshape(devices, -1)
    grad_gain_ff = jnp.transpose(
        jnp.stack(grads_gain_ff).reshape(layer_count, devices, weight_rows), (1, 0, 2)
    ).reshape(devices, -1)
    ends = jnp.sum(swap(jnp.concatenate([grad_gain_ff, grad_table], axis=1)), axis=0)
    grad_gain_ff = ends[: layer_count * weight_rows].reshape(layer_count, weight_rows)
    grad_bias_table = ends[layer_count * weight_rows :].reshape(
        bucket_count // blocks, heads_all // heads_n
    )
    grads_attn_in, grads_gains = [], []
    for layer_id in range(layer_count):
        parts = swap(grads_in[layer_id].reshape(devices, weight_rows, 3 * width)).astype(f32)
        parts = jnp.sum(parts.reshape(heads_n, blocks, weight_rows, 3 * width), axis=0)
        parts = jnp.sum(parts.reshape(head_groups, split, weight_rows, 3, width), axis=1)
        unit_grad = jnp.transpose(parts, (1, 2, 0, 3)).reshape(weight_rows, 3 * model_width)
        grads_attn_in.append(unit_grad * gain_attn[layer_id])
        grads_gains.append(
            jnp.stack(
                [jnp.sum(unit_grad * own_in[layer_id], axis=1), grad_gain_ff[layer_id]], axis=1
            )
        )
    return (
        output[None],
        upstream[None],
        jnp.stack(grads_attn_in),
        jnp.stack(grads_out),
        jnp.stack([entry[:, :model_width] for entry in grads_ff]),
        jnp.stack([entry[:, model_width:] for entry in grads_ff]),
        jnp.stack(grads_gains),
        grad_bias_table,
    )


def local_plane(tokens, doc_start, bias_table, attn_in, attn_out, ff_in, ff_out, gains, cotangent):
    heads_n, z_n, core_n = (lax.axis_size(axis) for axis in everyone)
    devices = heads_n * z_n * core_n
    at_head, at_z, at_core = (lax.axis_index(axis) for axis in everyone)
    members = heads_n * core_n
    block_rows, model_width = tokens.shape[1:]
    layer_count, weight_rows = attn_in.shape[:2]
    length = block_rows * members
    heads_all = bias_table.shape[1]
    heads_dev = heads_all // members
    width = heads_dev * head_dim
    member = at_head * core_n + at_core
    everywhere = [(h, z, c) for h in range(heads_n) for z in range(z_n) for c in range(core_n)]

    def swapped(bits):
        return bits % 2 * 2 + bits // 2

    def device(h, z, c):
        return (h * z_n + z) * core_n + c

    turn = [(device(h, z, c), device(h ^ swapped(z), h, c)) for h, z, c in everywhere]
    plane_turn = [(device(h, z, c), device(h ^ swapped(z), z, c)) for h, z, c in everywhere]
    line_turn = [(device(h, z, c), device(h, h ^ swapped(z), c)) for h, z, c in everywhere]
    line_back = [(target, source) for source, target in line_turn]
    place = jnp.stack(
        [
            (at_head ^ bits) * core_n + (at_core ^ other)
            for other in range(core_n)
            for bits in range(heads_n)
        ]
        + [at_z]
        + [
            swapped(at_head ^ bits ^ at_z) * core_n + (at_core ^ other)
            for other in range(core_n)
            for bits in range(heads_n)
        ]
    ).astype(jnp.int32)

    def relay(array):
        return lax.ppermute(array, everyone, turn)

    def turn_in_plane(array):
        return lax.ppermute(array, everyone, plane_turn)

    def turn_in_line(array, turns):
        return lax.ppermute(array, everyone, turns)

    def swap(array):
        return lax.all_to_all(array, everyone, 0, 0, tiled=True)

    row_shape = (block_rows, model_width)
    gain_attn = gains[:, :, 0].astype(f32)[:, :, None]
    near_share, far_share = call(
        share_in_kernel,
        [((members // 2 * layer_count * weight_rows, 3 * width), bf16)] * 2,
        place,
        attn_in,
        gain_attn,
        smem=1,
    )

    half_turns = [
        [
            (z * core_n + c, (2 * c + (a ^ z % 2)) * core_n + z // 2)
            for z in range(z_n)
            for c in range(core_n)
        ]
        for a in range(2)
    ]

    def fetch_out(layer_id, hold):
        own = attn_out[layer_id]
        other = toggle(own, "core", 1)
        head = jnp.where(
            at_core == 0, jnp.concatenate([own, other]), jnp.concatenate([other, own])
        )
        head = after(head, hold)
        return [
            lax.ppermute(head, ("z", "core"), [(holder, user) for user, holder in turns])
            for turns in half_turns
        ]

    def owners_halves(halves):
        return [
            lax.ppermute(half, ("z", "core"), turns) for half, turns in zip(halves, half_turns)
        ]

    def pair_chips(near, arrived, axis):
        rows, columns = near.shape[0] // 4, near.shape[1]
        shape = (2 * rows, columns) if axis == 0 else (rows, 2 * columns)
        return call(functools.partial(pair_kernel, axis), [(shape, bf16)] * 4, near, arrived)

    def share_chips(blocks):
        return [blocks[0]] + [toggle(blocks[bits], "head", bits) for bits in (1, 2, 3)]

    units_shape = [(row_shape, f32), (row_shape, bf16)]

    starts = jnp.broadcast_to(
        doc_start.astype(f32)[None, :, None], (heads_n, z_n, core_n, block_rows)
    )
    ff_gains = gains[:, :, 1].astype(f32).reshape(1, -1)
    small = jnp.concatenate(
        [
            starts.reshape(devices, block_rows),
            jnp.broadcast_to(ff_gains, (devices, layer_count * weight_rows)),
        ],
        axis=1,
    )
    table, strip = prepare(bias_table, member * heads_dev, heads_dev)
    hidden = relay(tokens[0])
    hidden, shares, halves, small = tie(
        hidden,
        share_chips(pair_chips(near_share, toggle(far_share, "core", 1), 0)),
        fetch_out(0, near_share),
        swap(after(small, near_share)),
    )
    hidden, unit_rows = call(unit_kernel, units_shape, hidden)
    doc_row = small[:members, :block_rows].reshape(2, 2, core_n, block_rows)
    at_block = swapped(at_head ^ at_z)
    for axis, bit in ((0, at_block // 2), (1, at_block % 2), (2, at_core)):
        doc_row = jnp.where(bit == 1, jnp.flip(doc_row, axis), doc_row)
    doc_row = jnp.transpose(doc_row, (2, 1, 0, 3)).reshape(1, length)
    doc_col = doc_row.reshape(length, 1)
    gain_ff = jnp.transpose(
        small[:, block_rows:].reshape(devices, layer_count, weight_rows), (1, 0, 2)
    ).reshape(layer_count, 1, model_width)

    def round_planes(array, by, hold):
        return shift(after(array, hold), by)

    ff_pairs = [
        jnp.concatenate([ff_in[layer_id], ff_out[layer_id]], axis=1) for layer_id in range(layer_count)
    ]

    def ff_both(kernel, row_operands, pair, columns):
        return zip(
            *(
                by_rows(
                    kernel,
                    256,
                    operands,
                    [pair],
                    [(pair.shape[0], bf16)] * columns + [(model_width, kind)],
                )
                for operands, kind in zip(zip(*row_operands), (f32, bf16))
            )
        )

    def ff_forward(normed, *parts):
        units = 4 * parts[0].shape[0]
        outs = [(units, bf16), (units, bf16)]
        *near, pair = by_rows(
            ff_first_kernel,
            256,
            [normed[0]],
            parts,
            outs + [(model_width, f32)],
            [(units, 2 * model_width)],
        )
        far = by_rows(ff_kernel, 256, [normed[1]], [pair], outs + [(model_width, bf16)])
        return pair, *zip(near, far)

    def ff_backward(low, slopes, pair):
        return ff_both(ff_back_kernel, [low, slopes], pair, 1)

    def assemble_in(share, lower, upper, opposite):
        return call(
            assemble_in_kernel,
            [((model_width, 3 * width), bf16)],
            place,
            share,
            lower,
            upper,
            opposite,
            smem=1,
        )[0]

    share, later_share = call(
        join_kernel, [((members * weight_rows, 3 * width), bf16)] * layer_count, *shares
    )
    near, far, lower, upper, opposite, cotangent_low, strip, doc_row, doc_col, gain_ff, *ff_pairs = plane_gather(
        unit_rows,
        shift(share, 1),
        shift(share, -1),
        shift(share, 2),
        cotangent[0].astype(bf16),
        strip,
        doc_row,
        doc_col,
        gain_ff,
        *ff_pairs,
    )
    w_in = assemble_in(share, lower, upper, opposite)
    units = (near, far)
    w_out, qkv, attended, stats, *parts = plane_attention(
        *units, w_in, halves, doc_row, doc_col, place, table, strip
    )
    parts, lower, upper, cotangent_low = tie(
        parts,
        round_planes(ff_pairs[0], 1, near),
        round_planes(ff_pairs[0], -1, near),
        turn_in_plane(after(cotangent_low, near)),
    )
    parts, own = plane_scatter(*parts)
    parts, opposite_in = tie(parts, round_planes(ff_in[0], 2, own))
    middle, normed_rows = call(close_gain_kernel, units_shape, hidden, *parts, gain_ff[0])
    *normed, opposite_out = plane_gather(normed_rows, round_planes(ff_out[0], 2, normed_rows))
    pair, acts, slopes, parts = ff_forward(
        normed, ff_pairs[0], lower, upper, opposite_in, opposite_out
    )
    records = [
        (hidden, units, w_in, w_out, pair, qkv, attended, stats, middle, normed, acts, slopes)
    ]
    parts, lower, upper = tie(
        parts,
        round_planes(later_share, 1, normed[0]),
        round_planes(later_share, -1, normed[0]),
    )
    parts, own = plane_scatter(*parts)
    parts, opposite, upstream = tie(
        parts, round_planes(later_share, 2, own), turn_in_line(after(cotangent_low, own), line_turn)
    )
    shares = [later_share, lower, upper, opposite]
    hidden, unit_rows = call(close_kernel, units_shape, middle, *parts)

    near, far, lower, halves = plane_gather(
        unit_rows, round_planes(ff_pairs[1], 1, unit_rows), fetch_out(1, unit_rows)
    )
    units = (near, far)
    w_in = assemble_in(*shares)
    w_out, qkv, attended, stats, *parts = plane_attention(
        *units, w_in, halves, doc_row, doc_col, place, table, strip
    )
    low = plane_gather(after(upstream, far))
    parts, near_low, upper = tie(parts, low[0], round_planes(ff_pairs[1], -1, far))
    low = (near_low, low[1])
    parts, own = plane_scatter(*parts)
    parts, opposite_in = tie(parts, round_planes(ff_in[1], 2, own))
    middle, normed_rows = call(close_gain_kernel, units_shape, hidden, *parts, gain_ff[1])
    *normed, opposite_out = plane_gather(normed_rows, round_planes(ff_out[1], 2, normed_rows))
    pair, acts, slopes, last_parts = ff_forward(
        normed, ff_pairs[1], lower, upper, opposite_in, opposite_out
    )
    records.append(
        (hidden, units, w_in, w_out, pair, qkv, attended, stats, middle, normed, acts, slopes)
    )

    def back_to_middle(parts, upstream, middle, gain):
        return call(
            middle_back_kernel, units_shape + [((1, model_width), f32)], upstream, *parts, middle, gain
        )

    def attention_grads(record, branch):
        _, _, w_in, w_out, _, qkv, attended, stats, *_ = record
        grad_qkv, grad_near, grad_far, near_part, far_part, *halves = plane_attention_back(
            qkv, doc_row, doc_col, attended, stats, *branch, w_in, w_out, place, table, strip
        )
        return grad_qkv, (grad_near, grad_far), (near_part, far_part), halves

    def table_grads(near_and_far):
        return bucket_grads(at_core.reshape(1) * heads_dev + 8, near_and_far, table.shape[0])

    record = records[1]
    hidden, units, _, _, pair, *_, middle, normed, acts, slopes = record
    pres, parts = ff_backward(low, slopes, pair)
    parts, own = plane_scatter(*parts)
    planes = ff_grads(after(pres, own), acts, normed, low)
    parts, ff_lower = tie(parts, shift(planes[1], -1))
    last_parts, _ = plane_scatter(*after(last_parts, parts))
    grad_middle, branch_rows, gain_1 = back_to_middle(parts, upstream, middle, gain_ff[1])
    *branch, ff_upper = plane_gather(branch_rows, round_planes(planes[2], 1, branch_rows))
    grad_qkv, strips_1, parts, halves_1 = attention_grads(record, branch)
    parts, last_parts, opposite_up = tie(
        parts, last_parts, round_planes(planes[3], 2, branch[1])
    )
    parts, own = plane_scatter(*parts)
    parts, opposite_down, output = tie(
        parts,
        round_planes(planes[4], 2, own),
        call(last_kernel, [(row_shape, bf16)], middle, *after(last_parts, own))[0],
    )
    grads_ff = [planes[0], ff_lower, ff_upper, opposite_up, opposite_down]
    upstream, low_rows = call(layer_back_kernel, units_shape, grad_middle, *parts, hidden)

    record = records[0]
    hidden, units, _, _, pair, *_, middle, normed, acts, slopes = record
    grad_in = in_grads(place, *records[1][1], after(grad_qkv, low_rows))
    *low, in_opposite, in_upper, table_1 = plane_gather(
        low_rows, shift(grad_in[3], 2), shift(grad_in[2], 1), table_grads(after(strips_1, low_rows))
    )
    pres, parts = ff_backward(low, slopes, pair)
    parts, in_lower = tie(parts, round_planes(grad_in[1], -1, low[0]))
    parts, own = plane_scatter(*parts)
    planes = ff_grads(after(pres, own), acts, normed, low)
    near_in, far_in = call(
        add_in_kernel,
        [((members // 2 * weight_rows, 3 * width), bf16)] * 2,
        *after([grad_in[0], in_lower, in_upper, in_opposite], own),
    )
    parts, ff_lower, first_half, arrived = tie(
        parts,
        shift(planes[1], -1),
        owners_halves(after(halves_1, own))[0],
        toggle(far_in, "core", 1),
    )
    grad_middle, branch_rows, gain_0 = back_to_middle(parts, upstream, middle, gain_ff[0])
    *branch, ff_upper, second_half, shares_1 = plane_gather(
        branch_rows,
        round_planes(planes[2], 1, branch_rows),
        owners_halves(after(halves_1, branch_rows))[1],
        pair_chips(near_in, after(arrived, branch_rows), 1),
    )
    halves_1 = [first_half, second_half]
    grad_qkv, strips_0, parts, halves_0 = attention_grads(record, branch)
    parts, shares_1, output, opposite_up = tie(
        parts,
        share_chips(after(shares_1, branch[1])), turn_in_line(after(output, branch[1]), line_back), round_planes(planes[3], 2, branch[1])
    )
    parts, own = plane_scatter(*parts)
    table_0 = table_grads(after(strips_0, own))
    grad_in = in_grads(
        place, *units, after(grad_qkv, own), gain_0, gain_1, table_0, table_1
    )
    parts, in_opposite = tie(parts, shift(grad_in[3], 2))
    upstream, low_rows = call(layer_back_kernel, units_shape, grad_middle, *parts, hidden)
    in_lower = round_planes(grad_in[1], -1, low_rows)
    in_upper = round_planes(grad_in[2], 1, low_rows)
    line = turn_in_line(low_rows, line_back)
    near_in, far_in = call(
        add_in_kernel,
        [((members // 2 * weight_rows, 3 * width + tile), bf16)] * 2,
        grad_in[0],
        in_lower,
        in_upper,
        in_opposite,
    )
    arrived = toggle(far_in, "core", 1)
    shares_0 = share_chips(pair_chips(near_in, arrived, 1))
    halves_0 = owners_halves(after(halves_0, shares_0[1:]))
    opposite_down = round_planes(planes[4], 2, near_in)
    grad_tokens = turn_in_plane(after(line, shares_0[1:]))
    output = turn_in_plane(after(output, shares_0[1:]))
    (output,) = call(widen_kernel, [(row_shape, f32)], output)
    (grad_tokens,) = call(widen_kernel, [(row_shape, f32)], grad_tokens)
    grads_ff = [planes[0], ff_lower, ff_upper, opposite_up, opposite_down] + grads_ff
    grad_up, grad_down = finish_ff(after(grads_ff, shares_0[1:]), ff_in.shape)
    own_out, other_out = call(
        add_out_kernel,
        [(attn_out.shape, f32), (attn_out.shape, bf16)],
        place,
        *halves_0,
        *halves_1,
        smem=1,
    )
    (grad_attn_out,) = call(
        finish_out_kernel, [(attn_out.shape, f32)], own_out, toggle(other_out, "core", 1)
    )
    own_buckets = table.shape[0] // (z_n * core_n)
    grad_attn_in, grad_gains, ends = call(
        finish_in_kernel,
        [(attn_in.shape, f32), (gains.shape, f32), ((weight_rows, tile), f32)],
        place,
        *shares_0,
        *shares_1,
        attn_in,
        gain_attn,
        smem=1,
    )
    return (
        output[None],
        grad_tokens[None],
        grad_attn_in,
        grad_attn_out,
        grad_up,
        grad_down,
        grad_gains,
        ends[:own_buckets, 8 : 8 + heads_all // heads_n],
    )


def solution(mesh):
    sizes = dict(mesh.shape)
    cores = 2
    fine = Mesh(
        mesh.devices.reshape(sizes["head"], sizes["blk"] // cores, cores), everyone
    )
    blk = ("z", "core")
    in_specs = (
        P("head", blk, None),
        P(None, blk),
        P(),
        P(None, everyone, None),
        P(None, everyone, None),
        P(None, everyone, None),
        P(None, everyone, None),
        P(None, everyone, None),
        P("head", blk, None),
    )
    out_specs = (
        P("head", blk, None),
        P("head", blk, None),
        P(None, everyone, None),
        P(None, everyone, None),
        P(None, everyone, None),
        P(None, everyone, None),
        P(None, everyone, None),
        P(blk, "head"),
    )
    plane = sizes["head"] == 4 and sizes["blk"] == 8
    local = local_plane if plane else local_general
    return jax.shard_map(local, mesh=fine, in_specs=in_specs, out_specs=out_specs, check_vma=False)
```

```python
import functools

import jax
import jax.numpy as jnp
import numpy as np
from jax import lax
from jax.experimental import pallas as pl
from jax.experimental.pallas import tpu as pltpu
from jax.sharding import Mesh
from jax.sharding import PartitionSpec as P

bounds = (1, 2, 3, 4, 5, 6, 7, 8, 12, 16, 23, 32, 46, 64, 91)
epsilon = 1e-06
masked = -1e30
score_scale = 0.125
head_dim = 64
tile = 128
everyone = ("head", "z", "core")
bf16 = jnp.bfloat16
f32 = jnp.float32


def contract(lhs, rhs, lhs_dim, rhs_dim):
    return lax.dot_general(
        lhs, rhs, (((lhs_dim,), (rhs_dim,)), ((), ())), preferred_element_type=f32
    )


def near_buckets(shape):
    offsets = (
        lax.broadcasted_iota(jnp.int32, shape, 1) - tile - lax.broadcasted_iota(jnp.int32, shape, 0)
    )
    distance = jnp.abs(offsets)
    bucket = jnp.where(offsets > 0, 16, 0)
    for boundary in bounds:
        bucket = bucket + jnp.where(distance >= boundary, 1, 0)
    return bucket


def near_kernel(table, near):
    bucket = near_buckets(near.shape[1:])
    for head in range(near.shape[0]):
        values = jnp.zeros(near.shape[1:], f32)
        for bucket_id in range(table.shape[0]):
            values = jnp.where(bucket == bucket_id, table[bucket_id, head], values)
        near[head] = values


def bucket_kernel(first_lane, near, far, out):
    bucket = near_buckets(near.shape[1:])
    rows = lax.broadcasted_iota(jnp.int32, out.shape, 0)
    lanes = lax.broadcasted_iota(jnp.int32, out.shape, 1)
    total = jnp.zeros(out.shape, f32)
    for head in range(near.shape[0]):
        strip = near[head]
        for bucket_id in range(out.shape[0]):
            value = jnp.sum(jnp.where(bucket == bucket_id, strip, 0.0), axis=0, keepdims=True)
            value = jnp.sum(value, axis=1, keepdims=True)
            if bucket_id in (15, 31):
                value = value + far[head, bucket_id // 16, :1, :1]
            total = jnp.where((rows == bucket_id) & (lanes == head + first_lane[0]), value, total)
    out[...] = total


def fill_band(band, table, near, heads_dev, length):
    for head in range(heads_dev):
        band[head, :, : length - tile] = jnp.full((tile, length - tile), table[15, head], f32)
        band[head, :, length - tile : length + 2 * tile] = near[head]
        band[head, :, length + 2 * tile :] = jnp.full(
            (tile, length - 2 * tile), table[31, head], f32
        )


def band_starts(place, at, length, skip=0):
    return [
        pl.multiple_of(length + (place[skip + block] - place[skip + at]) * tile, tile)
        for block in range(length // tile)
    ]


def attention_kernel(
    heads_dev, length, first, place, table, near, qkv, doc_row, doc_col, out, local, stats, band
):
    step = pl.program_id(0)
    width = heads_dev * head_dim

    @pl.when(step == 0)
    def _():
        fill_band(band, table, near, heads_dev, length)

    row = pl.multiple_of((first[0] + step) * tile, tile)
    out_row = pl.multiple_of((place[first[0] + step] - first[0]) * tile, tile)
    starts = band_starts(place, first[0] + step, length)
    same_doc = doc_col[...] == doc_row[...]
    queries = qkv[pl.ds(row, tile), :width] * bf16(score_scale)
    lanes = lax.broadcasted_iota(jnp.int32, (tile, tile), 1)
    collected = jnp.zeros((tile, tile), f32)
    for head in range(heads_dev):
        own = slice(head * head_dim, (head + 1) * head_dim)
        keys = qkv[:, width + own.start : width + own.stop]
        values = qkv[:, 2 * width + own.start : 2 * width + own.stop]
        scores = contract(queries[:, own], keys, 1, 1)
        scores = scores + jnp.concatenate(
            [band[head, :, pl.ds(start, tile)] for start in starts], axis=1
        )
        scores = jnp.where(same_doc, scores, masked)
        peak = jnp.max(scores, axis=1, keepdims=True)
        weights = jnp.exp(scores - peak)
        total = jnp.sum(weights, axis=1, keepdims=True)
        mixed = contract(weights.astype(bf16), values, 1, 0) / total
        out[pl.ds(out_row, tile), own] = mixed.astype(bf16)
        local[:, own] = mixed.astype(bf16)
        collected = jnp.where(lanes == head, peak + jnp.log(total), collected)
    stats[...] = collected


def attention_back_kernel(
    heads_dev, length, split, first, place, table, near, qkv, doc_row, doc_col, attended, grad_out, stats,
    grad_qkv, grad_near, grad_far, band, grad_band, grad_keys, grad_values,
):
    step = pl.program_id(0)
    width = heads_dev * head_dim

    @pl.when(step == 0)
    def _():
        fill_band(band, table, near, heads_dev, length)
        grad_band[...] = jnp.zeros_like(grad_band)
        grad_keys[...] = jnp.zeros_like(grad_keys)
        grad_values[...] = jnp.zeros_like(grad_values)
        if split > 1:
            grad_qkv[...] = jnp.zeros_like(grad_qkv)

    row = pl.multiple_of((first[0] + step) * tile, tile)
    out_row = pl.multiple_of((place[first[0] + step] - first[0]) * tile, tile)
    starts = band_starts(place, first[0] + step, length)
    same_doc = doc_col[...] == doc_row[...]
    at_step = pl.multiple_of(step * tile, tile)
    queries = qkv[pl.ds(row, tile), :width] * bf16(score_scale)
    for head in range(heads_dev):
        own = slice(head * head_dim, (head + 1) * head_dim)
        keys = qkv[:, width + own.start : width + own.stop]
        values = qkv[:, 2 * width + own.start : 2 * width + own.stop]
        upstream = grad_out[pl.ds(out_row, tile), own]
        scores = contract(queries[:, own], keys, 1, 1) + jnp.concatenate(
            [band[head, :, pl.ds(start, tile)] for start in starts], axis=1
        )
        scores = jnp.where(same_doc, scores, masked)
        weights = jnp.exp(scores - stats[:, head : head + 1])
        delta = jnp.sum(
            upstream.astype(f32) * attended[pl.ds(at_step, tile), own].astype(f32),
            axis=1,
            keepdims=True,
        )
        grad_scores = weights * (contract(upstream, values, 1, 1) - delta)
        for block, start in enumerate(starts):
            grad_band[head, :, pl.ds(start, tile)] += grad_scores[
                :, block * tile : (block + 1) * tile
            ]
        grad_low = grad_scores.astype(bf16)
        grad_values[:, own] += contract(weights.astype(bf16), upstream, 0, 0)
        grad_keys[:, own] += contract(grad_low, queries[:, own], 0, 0)
        grad_qkv[pl.ds(row, tile), own] = (
            contract(grad_low, keys, 1, 0) * score_scale
        ).astype(bf16)

    @pl.when(step == pl.num_programs(0) - 1)
    def _():
        grad_qkv[:, width : 2 * width] = grad_keys[...].astype(bf16)
        grad_qkv[:, 2 * width :] = grad_values[...].astype(bf16)
        for head in range(heads_dev):
            grad_near[head] = grad_band[head, :, length - tile : length + 2 * tile]
            grad_far[head, 0] = jnp.full(
                (8, tile), jnp.sum(grad_band[head, :, : length - tile]), f32
            )
            grad_far[head, 1] = jnp.full(
                (8, tile), jnp.sum(grad_band[head, :, length + 2 * tile :]), f32
            )


def whole(shape):
    return pl.BlockSpec(shape, lambda step: (0,) * len(shape), pipeline_mode=pl.Buffered(1))


def attention(qkv, doc_row, doc_col, first, place, table, near, rows):
    length = qkv.shape[0]
    heads_dev = table.shape[1]
    width = heads_dev * head_dim
    return pl.pallas_call(
        functools.partial(attention_kernel, heads_dev, length),
        grid=(rows // tile,),
        in_specs=[
            pl.BlockSpec(memory_space=pltpu.SMEM),
            pl.BlockSpec(memory_space=pltpu.SMEM),
            pl.BlockSpec(memory_space=pltpu.SMEM),
            whole(near.shape),
            whole(qkv.shape),
            whole(doc_row.shape),
            pl.BlockSpec((tile, 1), lambda step: (step, 0)),
        ],
        out_specs=[
            whole((rows, width)),
            pl.BlockSpec((tile, width), lambda step: (step, 0)),
            pl.BlockSpec((tile, tile), lambda step: (step, 0)),
        ],
        out_shape=[
            jax.ShapeDtypeStruct((rows, width), bf16),
            jax.ShapeDtypeStruct((rows, width), bf16),
            jax.ShapeDtypeStruct((rows, tile), f32),
        ],
        scratch_shapes=[pltpu.VMEM((heads_dev, tile, 2 * length), f32)],
        compiler_params=pltpu.CompilerParams(vmem_limit_bytes=40 * 2**20),
        cost_estimate=pl.CostEstimate(
            flops=4 * rows * length * width,
            bytes_accessed=4 * length * width * 2,
            transcendentals=rows * length * heads_dev,
        ),
    )(first, place, table, near, qkv, doc_row, doc_col)


def attention_back(
    qkv, doc_row, doc_col, attended, grad_out, stats, first, place, table, near, split
):
    length = qkv.shape[0]
    rows = grad_out.shape[0]
    heads_dev = table.shape[1]
    width = heads_dev * head_dim
    return pl.pallas_call(
        functools.partial(attention_back_kernel, heads_dev, length, split),
        grid=(rows // tile,),
        in_specs=[
            pl.BlockSpec(memory_space=pltpu.SMEM),
            pl.BlockSpec(memory_space=pltpu.SMEM),
            pl.BlockSpec(memory_space=pltpu.SMEM),
            whole(near.shape),
            whole(qkv.shape),
            whole(doc_row.shape),
            pl.BlockSpec((tile, 1), lambda step: (step, 0)),
            whole((rows, width)),
            whole((rows, width)),
            pl.BlockSpec((tile, tile), lambda step: (step, 0)),
        ],
        out_specs=[
            whole((length, 3 * width)),
            whole((heads_dev, tile, 3 * tile)),
            whole((heads_dev, 2, 8, tile)),
        ],
        out_shape=[
            jax.ShapeDtypeStruct((length, 3 * width), bf16),
            jax.ShapeDtypeStruct((heads_dev, tile, 3 * tile), f32),
            jax.ShapeDtypeStruct((heads_dev, 2, 8, tile), f32),
        ],
        scratch_shapes=[
            pltpu.VMEM((heads_dev, tile, 2 * length), f32),
            pltpu.VMEM((heads_dev, tile, 2 * length), f32),
            pltpu.VMEM((length, width), f32),
            pltpu.VMEM((length, width), f32),
        ],
        compiler_params=pltpu.CompilerParams(vmem_limit_bytes=48 * 2**20),
        cost_estimate=pl.CostEstimate(
            flops=10 * rows * length * width,
            bytes_accessed=8 * length * width * 2,
            transcendentals=rows * length * heads_dev,
        ),
    )(first, place, table, near, qkv, doc_row, doc_col, attended, grad_out, stats)


def call(kernel, shapes, *operands, smem=0):
    return pl.pallas_call(
        kernel,
        in_specs=[pl.BlockSpec(memory_space=pltpu.SMEM)] * smem
        + [pl.BlockSpec(memory_space=pltpu.VMEM)] * (len(operands) - smem),
        out_specs=[pl.BlockSpec(memory_space=pltpu.VMEM)] * len(shapes),
        out_shape=[jax.ShapeDtypeStruct(shape, kind) for shape, kind in shapes],
        compiler_params=pltpu.CompilerParams(vmem_limit_bytes=10 * 2**20),
    )(*operands)


def share_in_kernel(place, attn_in, gains, near, far):
    layers, rows = attn_in.shape[:2]
    half = near.shape[0] // (layers * rows)
    width = near.shape[1] // 3
    for index in range(2 * half):
        member = place[index]
        for layer_id in range(layers):
            block = jnp.concatenate(
                [
                    attn_in[
                        layer_id,
                        :,
                        pl.ds(pl.multiple_of((part * 2 * half + member) * width, width), width),
                    ]
                    for part in range(3)
                ],
                axis=1,
            )
            at = (index % half * layers + layer_id) * rows
            out = near if index < half else far
            out[at : at + rows] = (block.astype(f32) * gains[layer_id]).astype(bf16)


def join_kernel(*refs):
    shares, outs = refs[:4], refs[4:]
    rows = outs[0].shape[0] // 8
    for chip, share in enumerate(shares):
        for core in range(2):
            for layer_id, out in enumerate(outs):
                source = (core * len(outs) + layer_id) * rows
                target = (chip * 2 + core) * rows
                out[target : target + rows] = share[source : source + rows]


def row_of(chip, plane, core, rows, planes=4):
    return pl.multiple_of(((chip * planes + plane) * 2 + core) * rows, rows)


def assemble_in_kernel(place, own, lower, upper, opposite, out):
    at_z, at_core, at_head = place[8], place[0] % 2, place[0] // 2
    rows = own.shape[0] // 8
    for part, offset in ((own, 0), (lower, 3), (upper, 1), (opposite, 2)):
        plane = (at_z + offset) % 4
        for index in range(8):
            row = row_of(at_head ^ (index // 2), plane, at_core ^ (index % 2), rows)
            out[pl.ds(row, rows)] = part[index * rows : (index + 1) * rows]


def plane_attention_kernel(
    length, place, table, strip, near, far, w_in, *refs
):
    halves, (doc_row, doc_col, w_out, qkv, attended, stats, near_part, far_part, band) = (
        refs[:2], refs[2:],
    )
    step = pl.program_id(0)
    half = length // 2
    heads_dev = table.shape[1]
    width = heads_dev * head_dim

    @pl.when(step == 0)
    def _():
        fill_band(band, table, strip, heads_dev, length)
        swapped = place[length // tile] % 2 == 1
        rows = width // 2
        w_out[:rows] = jnp.where(swapped, halves[1][...], halves[0][...])
        w_out[rows:] = jnp.where(swapped, halves[0][...], halves[1][...])
        qkv[:half] = contract(near[...], w_in[...], 1, 0).astype(bf16)
        qkv[half:] = contract(far[...], w_in[...], 1, 0).astype(bf16)

    row = pl.multiple_of(step * tile, tile)
    starts = band_starts(place, step, length, length // tile + 1)
    same_doc = doc_col[...] == doc_row[...]
    queries = qkv[pl.ds(row, tile), :width] * bf16(score_scale)
    lanes = lax.broadcasted_iota(jnp.int32, (tile, tile), 1)
    collected = jnp.zeros((tile, tile), f32)
    results = []
    for head in range(heads_dev):
        own = slice(head * head_dim, (head + 1) * head_dim)
        keys = qkv[:, width + own.start : width + own.stop]
        values = qkv[:, 2 * width + own.start : 2 * width + own.stop]
        scores = contract(queries[:, own], keys, 1, 1) + jnp.concatenate(
            [band[head, :, pl.ds(start, tile)] for start in starts], axis=1
        )
        scores = jnp.where(same_doc, scores, masked)
        peak = jnp.max(scores, axis=1, keepdims=True)
        weights = jnp.exp(scores - peak)
        total = jnp.sum(weights, axis=1, keepdims=True)
        results.append((contract(weights.astype(bf16), values, 1, 0) / total).astype(bf16))
        collected = jnp.where(lanes == head, peak + jnp.log(total), collected)
    stats[...] = collected
    merged = jnp.concatenate(results, axis=1)
    attended[...] = merged
    part = contract(merged, w_out[...], 1, 0)

    @pl.when(row < half)
    def _():
        near_part[...] = part

    @pl.when(row >= half)
    def _():
        far_part[...] = part.astype(bf16)


def near_block(steps, columns):
    return pl.BlockSpec((tile, columns), lambda step: (jnp.minimum(step, steps // 2 - 1), 0))


def far_block(steps, columns):
    return pl.BlockSpec((tile, columns), lambda step: (jnp.maximum(step - steps // 2, 0), 0))


def plane_attention(near, far, w_in, halves, doc_row, doc_col, place, table, strip):
    length, model_width = 2 * near.shape[0], near.shape[1]
    steps = length // tile
    heads_dev = table.shape[1]
    width = heads_dev * head_dim
    return pl.pallas_call(
        functools.partial(plane_attention_kernel, length),
        grid=(steps,),
        in_specs=[
            pl.BlockSpec(memory_space=pltpu.SMEM),
            pl.BlockSpec(memory_space=pltpu.SMEM),
            whole(strip.shape),
            whole(near.shape),
            whole(far.shape),
            whole(w_in.shape),
            *[whole(half.shape) for half in halves],
            whole(doc_row.shape),
            pl.BlockSpec((tile, 1), lambda step: (step, 0)),
        ],
        out_specs=[
            whole((width, model_width)),
            whole((length, 3 * width)),
            pl.BlockSpec((tile, width), lambda step: (step, 0)),
            pl.BlockSpec((tile, tile), lambda step: (step, 0)),
            near_block(steps, model_width),
            far_block(steps, model_width),
        ],
        out_shape=[
            jax.ShapeDtypeStruct((width, model_width), bf16),
            jax.ShapeDtypeStruct((length, 3 * width), bf16),
            jax.ShapeDtypeStruct((length, width), bf16),
            jax.ShapeDtypeStruct((length, tile), f32),
            jax.ShapeDtypeStruct((length // 2, model_width), f32),
            jax.ShapeDtypeStruct((length // 2, model_width), bf16),
        ],
        scratch_shapes=[pltpu.VMEM((heads_dev, tile, 2 * length), f32)],
        compiler_params=pltpu.CompilerParams(vmem_limit_bytes=14 * 2**20),
        cost_estimate=pl.CostEstimate(
            flops=4 * length * length * width + 8 * length * model_width * width,
            bytes_accessed=12 * 2**20,
            transcendentals=length * length * heads_dev,
        ),
    )(place, table, strip, near, far, w_in, *halves, doc_row, doc_col)


def plane_attention_back_kernel(
    length, place, table, strip, qkv, doc_row, doc_col, attended, stats, near, far, w_in, w_out,
    grad_qkv, grad_near, grad_far, near_part, far_part, *rest
):
    halves, (band, grad_band, grad_keys, grad_values, out_sum) = rest[:2], rest[2:]
    step = pl.program_id(0)
    half = length // 2
    heads_dev = table.shape[1]
    width = heads_dev * head_dim

    @pl.when(step == 0)
    def _():
        fill_band(band, table, strip, heads_dev, length)
        grad_band[...] = jnp.zeros_like(grad_band)
        grad_keys[...] = jnp.zeros_like(grad_keys)
        grad_values[...] = jnp.zeros_like(grad_values)
        out_sum[...] = jnp.zeros_like(out_sum)

    row = pl.multiple_of(step * half, half)
    branch = jnp.where(step == 0, near[...], far[...])
    merged = attended[...]
    grad_merged = contract(branch, w_out[...], 1, 1).astype(bf16)
    out_sum[...] += contract(merged, branch, 0, 0)
    products = grad_merged.astype(f32) * merged.astype(f32)
    queries = qkv[pl.ds(row, half), :width] * bf16(score_scale)
    blocks = half // tile
    for head in range(heads_dev):
        own = slice(head * head_dim, (head + 1) * head_dim)
        keys = qkv[:, width + own.start : width + own.stop]
        values = qkv[:, 2 * width + own.start : 2 * width + own.stop]
        upstream = grad_merged[:, own]
        raw_scores = contract(queries[:, own], keys, 1, 1)
        grad_weights = contract(upstream, values, 1, 1)
        delta = jnp.sum(products[:, own], axis=1, keepdims=True)
        weights_low, grads_low = [], []
        for block in range(blocks):
            lines = slice(block * tile, (block + 1) * tile)
            starts = band_starts(place, step * blocks + block, length, length // tile + 1)
            scores = raw_scores[lines] + jnp.concatenate(
                [band[head, :, pl.ds(start, tile)] for start in starts], axis=1
            )
            scores = jnp.where(doc_col[lines] == doc_row[...], scores, masked)
            weights = jnp.exp(scores - stats[lines, head : head + 1])
            grad_scores = weights * (grad_weights[lines] - delta[lines])
            for index, start in enumerate(starts):
                grad_band[head, :, pl.ds(start, tile)] += grad_scores[
                    :, index * tile : (index + 1) * tile
                ]
            weights_low.append(weights.astype(bf16))
            grads_low.append(grad_scores.astype(bf16))
        weights_low, grads_low = jnp.concatenate(weights_low), jnp.concatenate(grads_low)
        grad_values[:, own] += contract(weights_low, upstream, 0, 0)
        grad_keys[:, own] += contract(grads_low, queries[:, own], 0, 0)
        grad_qkv[pl.ds(row, half), own] = (
            contract(grads_low, keys, 1, 0) * score_scale
        ).astype(bf16)

    @pl.when(step == pl.num_programs(0) - 1)
    def _():
        grad_qkv[:, width : 2 * width] = grad_keys[...].astype(bf16)
        grad_qkv[:, 2 * width :] = grad_values[...].astype(bf16)
        far_part[...] = contract(grad_qkv[half:], w_in[...], 1, 1).astype(bf16)
        near_part[...] = contract(grad_qkv[:half], w_in[...], 1, 1)
        rows = width // 2
        for index, part in enumerate(halves):
            block = index ^ place[length // tile] % 2
            part[...] = out_sum[pl.ds(pl.multiple_of(block * rows, rows), rows)].astype(bf16)
        for head in range(heads_dev):
            grad_near[head] = grad_band[head, :, length - tile : length + 2 * tile]
            grad_far[head, 0] = jnp.full(
                (8, tile), jnp.sum(grad_band[head, :, : length - tile]), f32
            )
            grad_far[head, 1] = jnp.full(
                (8, tile), jnp.sum(grad_band[head, :, length + 2 * tile :]), f32
            )


def plane_attention_back(
    qkv, doc_row, doc_col, attended, stats, near, far, w_in, w_out, place, table, strip
):
    length, model_width = 2 * near.shape[0], near.shape[1]
    half = length // 2
    heads_dev = table.shape[1]
    width = heads_dev * head_dim
    shapes = [
        ((length, 3 * width), bf16),
        ((heads_dev, tile, 3 * tile), f32),
        ((heads_dev, 2, 8, tile), f32),
        ((length // 2, model_width), f32),
        ((length // 2, model_width), bf16),
    ] + [((width // 2, model_width), bf16)] * 2
    return pl.pallas_call(
        functools.partial(plane_attention_back_kernel, length),
        grid=(2,),
        in_specs=[
            pl.BlockSpec(memory_space=pltpu.SMEM),
            pl.BlockSpec(memory_space=pltpu.SMEM),
            whole(strip.shape),
            whole(qkv.shape),
            whole(doc_row.shape),
            pl.BlockSpec((half, 1), lambda step: (step, 0)),
            pl.BlockSpec((half, width), lambda step: (step, 0)),
            pl.BlockSpec((half, tile), lambda step: (step, 0)),
            whole((half, model_width)),
            whole((half, model_width)),
            whole(w_in.shape),
            whole(w_out.shape),
        ],
        out_specs=[whole(shape) for shape, _ in shapes],
        out_shape=[jax.ShapeDtypeStruct(shape, kind) for shape, kind in shapes],
        scratch_shapes=[
            pltpu.VMEM((heads_dev, tile, 2 * length), f32),
            pltpu.VMEM((heads_dev, tile, 2 * length), f32),
            pltpu.VMEM((length, width), f32),
            pltpu.VMEM((length, width), f32),
            pltpu.VMEM((width, model_width), f32),
        ],
        compiler_params=pltpu.CompilerParams(vmem_limit_bytes=32 * 2**20),
        cost_estimate=pl.CostEstimate(
            flops=10 * length * length * width + 10 * length * model_width * width,
            bytes_accessed=12 * 2**20,
            transcendentals=length * length * heads_dev,
        ),
    )(place, table, strip, qkv, doc_row, doc_col, attended, stats, near, far, w_in, w_out)


def gelu_and_slope(pre_act):
    size = jnp.abs(pre_act)
    gauss = jnp.exp(-0.5 * pre_act * pre_act)
    ratio = 1.0 / (1.0 + np.float32(0.3275911 * 0.5**0.5) * size)
    series = np.float32(1.061405429)
    for factor in (-1.453152027, 1.421413741, -0.284496736, 0.254829592):
        series = series * ratio + np.float32(factor)
    tail = 0.5 * series * ratio * gauss
    cumulative = jnp.where(pre_act < 0, tail, 1.0 - tail)
    slope = cumulative + pre_act * gauss * np.float32((2 * np.pi) ** -0.5)
    return pre_act * cumulative, slope


def ff_kernel(rows, pair, activated, slope, part):
    columns = rows.shape[1]
    value, gradient = gelu_and_slope(contract(rows[...], pair[:, :columns], 1, 1))
    activated[...] = value.astype(bf16)
    slope[...] = gradient.astype(bf16)
    part[...] = contract(activated[...], pair[:, columns:], 1, 0).astype(part.dtype)


def ff_first_kernel(rows, *refs):
    parts, (activated, slope, part, pair) = refs[:5], refs[5:]

    @pl.when(pl.program_id(0) == 0)
    def _():
        units, columns = parts[0].shape[0], rows.shape[1]
        for index, ref in enumerate(parts[:3]):
            pair[index * units : (index + 1) * units] = ref[...]
        pair[3 * units :, :columns] = parts[3][...]
        pair[3 * units :, columns:] = parts[4][...]

    ff_kernel(rows, pair, activated, slope, part)


def ff_back_kernel(rows, slope, pair, grad_pre, part):
    columns = rows.shape[1]
    grad_act = contract(rows[...], pair[:, columns:], 1, 1)
    grad_pre[...] = (grad_act * slope[...].astype(f32)).astype(bf16)
    part[...] = contract(grad_pre[...], pair[:, :columns], 1, 0).astype(part.dtype)


def by_rows(kernel, step_rows, row_operands, whole_operands, outs, whole_outs=()):
    rows = row_operands[0].shape[0]
    return pl.pallas_call(
        kernel,
        grid=(rows // step_rows,),
        in_specs=[
            pl.BlockSpec((step_rows, operand.shape[1]), lambda step: (step, 0))
            for operand in row_operands
        ]
        + [whole(operand.shape) for operand in whole_operands],
        out_specs=[pl.BlockSpec((step_rows, columns), lambda step: (step, 0)) for columns, _ in outs]
        + [whole(shape) for shape in whole_outs],
        out_shape=[jax.ShapeDtypeStruct((rows, columns), kind) for columns, kind in outs]
        + [jax.ShapeDtypeStruct(shape, bf16) for shape in whole_outs],
        compiler_params=pltpu.CompilerParams(vmem_limit_bytes=10 * 2**20),
        cost_estimate=pl.CostEstimate(
            flops=4 * rows * outs[0][0] * row_operands[0].shape[1],
            bytes_accessed=6 * 2**20,
            transcendentals=0,
        ),
    )(*row_operands, *whole_operands)


def ff_grads_kernel(
    pre_near, pre_far, act_near, act_far, normed_near, normed_far, low_near, low_far, *outs
):
    columns = normed_near.shape[1]
    units = outs[0].shape[0]
    up = (
        contract(pre_near[...], normed_near[...], 0, 0)
        + contract(pre_far[...], normed_far[...], 0, 0)
    ).astype(bf16)
    down = (
        contract(act_near[...], low_near[...], 0, 0) + contract(act_far[...], low_far[...], 0, 0)
    ).astype(bf16)

    @pl.when(pl.program_id(0) == 0)
    def _():
        for index in range(2):
            block = slice(index * units, (index + 1) * units)
            outs[index][:, :columns] = up[block]
            outs[index][:, columns:] = down[block]

    @pl.when(pl.program_id(0) == 1)
    def _():
        outs[2][:, :columns] = up[:units]
        outs[2][:, columns:] = down[:units]
        outs[3][...] = up[units:]
        outs[4][...] = down[units:]


def ff_grads(pre, act, normed, low):
    rows, hidden_units = pre[0].shape
    columns = normed[0].shape[1]
    shapes = [(hidden_units // 4, 2 * columns)] * 3 + [(hidden_units // 4, columns)] * 2
    return pl.pallas_call(
        ff_grads_kernel,
        grid=(2,),
        in_specs=[pl.BlockSpec((rows, hidden_units // 2), lambda step: (0, step))] * 4
        + [whole((rows, columns))] * 4,
        out_specs=[whole(shape) for shape in shapes],
        out_shape=[jax.ShapeDtypeStruct(shape, bf16) for shape in shapes],
        compiler_params=pltpu.CompilerParams(vmem_limit_bytes=14 * 2**20),
        cost_estimate=pl.CostEstimate(
            flops=8 * rows * hidden_units * columns, bytes_accessed=8 * 2**20, transcendentals=0
        ),
    )(*pre, *act, *normed, *low)


def in_grads_kernel(place, near, far, grad_qkv, *refs):
    ends, outs, (total, extra) = refs[:-6], refs[-6:-2], refs[-2:]
    half = near.shape[0]
    columns = grad_qkv.shape[1]
    total[:, :columns] = (
        contract(near[...], grad_qkv[:half], 0, 0) + contract(far[...], grad_qkv[half:], 0, 0)
    ).astype(bf16)
    rows = outs[0].shape[0] // 8
    if ends:
        gain_0, gain_1, table_0, table_1 = ends
        lines = lax.broadcasted_iota(jnp.int32, (tile, gain_0.shape[1]), 0)
        gains = jnp.where(lines == 0, gain_0[...], jnp.where(lines == 1, gain_1[...], 0.0))
        extra[...] = jnp.transpose(gains)
        table = table_0[...] + table_1[...]
        buckets = table.shape[0] // 8
        blank = jnp.zeros((8 - buckets, tile), f32)
        for block in range(8):
            row = pl.multiple_of((place[0] // 2 * 8 + block) * rows, rows)
            extra[pl.ds(row, 8)] += jnp.concatenate(
                [table[block * buckets : (block + 1) * buckets], blank]
            )
        total[:, columns:] = extra[...].astype(bf16)
    for out, offset in zip(outs, (0, 3, 1, 2)):
        plane = (place[8] + offset) % 4
        for index in range(8):
            owner = place[index]
            row = row_of(owner // 2, plane, owner % 2, rows)
            out[index * rows : (index + 1) * rows] = total[pl.ds(row, rows)]


def in_grads(place, near, far, grad_qkv, *ends):
    columns = grad_qkv.shape[1] + (tile if ends else 0)
    shape = (near.shape[1] // 4, columns)
    return pl.pallas_call(
        in_grads_kernel,
        in_specs=[pl.BlockSpec(memory_space=pltpu.SMEM)]
        + [pl.BlockSpec(memory_space=pltpu.VMEM)] * (3 + len(ends)),
        out_specs=[pl.BlockSpec(memory_space=pltpu.VMEM)] * 4,
        out_shape=[jax.ShapeDtypeStruct(shape, bf16)] * 4,
        scratch_shapes=[
            pltpu.VMEM((near.shape[1], columns), bf16),
            pltpu.VMEM((near.shape[1], tile), f32),
        ],
        compiler_params=pltpu.CompilerParams(vmem_limit_bytes=14 * 2**20),
        cost_estimate=pl.CostEstimate(
            flops=4 * near.shape[0] * near.shape[1] * columns,
            bytes_accessed=4 * 2**20,
            transcendentals=0,
        ),
    )(place, near, far, grad_qkv, *ends)


def add_in_kernel(own, lower, upper, opposite, near, far):
    total = sum_of_four([own, lower, upper, opposite]).astype(bf16)
    half = near.shape[0]
    near[...] = total[:half]
    far[...] = total[half:]


def combine_kernel(near_part, arrived, own, x_part, y_part, xy_part):
    rows = own.shape[0]
    own[...] = near_part[:rows] + arrived[:rows].astype(f32)
    for bits, out in ((1, x_part), (2, y_part), (3, xy_part)):
        block = slice(bits * rows, (bits + 1) * rows)
        out[...] = (near_part[block] + arrived[block].astype(f32)).astype(bf16)


def added(own, x_part, y_part, xy_part):
    return (own[...] + x_part[...].astype(f32)) + (
        y_part[...].astype(f32) + xy_part[...].astype(f32)
    )


def close_kernel(kept, own, x_part, y_part, xy_part, hidden, units):
    total = kept[...] + added(own, x_part, y_part, xy_part)
    hidden[...] = total
    units[...] = (total * inverse_rms(total)).astype(bf16)


def close_gain_kernel(kept, own, x_part, y_part, xy_part, gain, hidden, normed):
    total = kept[...] + added(own, x_part, y_part, xy_part)
    hidden[...] = total
    normed[...] = (total * inverse_rms(total) * gain[...]).astype(bf16)


def widen_kernel(low, out):
    out[...] = low[...].astype(f32)


def last_kernel(kept, own, x_part, y_part, xy_part, hidden):
    hidden[...] = (kept[...] + added(own, x_part, y_part, xy_part)).astype(bf16)


def middle_back_kernel(
    upstream, own, x_part, y_part, xy_part, middle, gain, grad_middle, branch, grad_gain
):
    grad_normed = added(own, x_part, y_part, xy_part)
    inverse = inverse_rms(middle[...])
    grad_gain[...] = jnp.sum(grad_normed * middle[...] * inverse, axis=0, keepdims=True)
    total = upstream[...].astype(f32) + unit_norm_back(
        middle[...], inverse, grad_normed * gain[...]
    )
    grad_middle[...] = total
    branch[...] = total.astype(bf16)


def layer_back_kernel(grad_middle, own, x_part, y_part, xy_part, hidden, upstream, low):
    total = grad_middle[...] + unit_norm_back(
        hidden[...], inverse_rms(hidden[...]), added(own, x_part, y_part, xy_part)
    )
    upstream[...] = total
    low[...] = total.astype(bf16)


def pair_kernel(axis, near, arrived, *outs):
    rows = near.shape[0] // len(outs)
    for index, out in enumerate(outs):
        block = slice(index * rows, (index + 1) * rows)
        if axis == 0:
            out[:rows] = near[block]
            out[rows:] = arrived[block]
        else:
            columns = near.shape[1]
            out[:, :columns] = near[block]
            out[:, columns:] = arrived[block]


def unit_kernel(tokens, hidden, units):
    total = tokens[...].astype(f32)
    hidden[...] = total
    units[...] = (total * inverse_rms(total)).astype(bf16)


def finish_in_kernel(place, *refs):
    chips, (attn_in, gains, grad_in, grad_gain, ends) = refs[:8], refs[8:]
    rows = attn_in.shape[1]
    width = tile
    members = attn_in.shape[2] // (3 * width)
    ends[...] = jnp.zeros_like(ends)
    for layer_id in range(2):
        row_dot = jnp.zeros((rows, 1), f32)
        for index in range(members):
            member = place[index]
            chip = chips[4 * layer_id + index % 4]
            half = chip.shape[1] // 2
            total = chip[:, index // 4 * half : (index // 4 + 1) * half].astype(f32)
            if layer_id == 0:
                ends[...] += total[:, 3 * width :]
            for part in range(3):
                block = total[:, part * width : (part + 1) * width]
                columns = pl.ds(pl.multiple_of((part * members + member) * width, width), width)
                grad_in[layer_id, :, columns] = block * gains[layer_id]
                row_dot = row_dot + jnp.sum(
                    block * attn_in[layer_id, :, columns].astype(f32), axis=1, keepdims=True
                )
        grad_gain[layer_id] = jnp.concatenate(
            [row_dot, ends[:, layer_id : layer_id + 1]], axis=1
        )


def sum_of_four(parts):
    return (parts[0][...].astype(f32) + parts[1][...].astype(f32)) + (
        parts[2][...].astype(f32) + parts[3][...].astype(f32)
    )


def finish_ff_kernel(*refs):
    count = (len(refs) - 3) // 2
    sources, grads, held, done = refs[:count], refs[count : count + 2], refs[count + 2 : -1], refs[-1]
    copies = [
        pltpu.make_async_copy(source, target, done.at[index])
        for index, (source, target) in enumerate(zip(sources, held))
    ]
    for copy in copies:
        copy.start()
    for copy in copies:
        copy.wait()
    refs = held
    columns = grads[0].shape[2]
    for layer_id in range(grads[0].shape[0]):
        parts = refs[5 * layer_id : 5 * layer_id + 5]
        for side, out in enumerate(grads):
            halves = [part.at[:, side * columns : (side + 1) * columns] for part in parts[:3]]
            out[layer_id] = sum_of_four(halves + [parts[3 + side]])


def finish_ff(grads, shape):
    return pl.pallas_call(
        finish_ff_kernel,
        in_specs=[pl.BlockSpec(memory_space=pl.ANY)] * len(grads),
        out_specs=[pl.BlockSpec(memory_space=pltpu.VMEM)] * 2,
        out_shape=[jax.ShapeDtypeStruct(shape, f32)] * 2,
        scratch_shapes=[pltpu.VMEM(grad.shape, bf16) for grad in grads]
        + [pltpu.SemaphoreType.DMA((len(grads),))],
        compiler_params=pltpu.CompilerParams(vmem_limit_bytes=14 * 2**20),
    )(*grads)


def add_out_kernel(place, *refs):
    parts, (own, other) = refs[:-2], refs[-2:]
    for layer_id in range(own.shape[0]):
        total = parts[2 * layer_id][...].astype(f32) + parts[2 * layer_id + 1][...].astype(f32)
        rows = total.shape[0] // 2
        second = place[0] % 2 == 1
        own[layer_id] = jnp.where(second, total[rows:], total[:rows])
        other[layer_id] = jnp.where(second, total[:rows], total[rows:]).astype(bf16)


def finish_out_kernel(own, arrived, out):
    out[...] = own[...] + arrived[...].astype(f32)


def inverse_rms(hidden):
    return lax.rsqrt(jnp.mean(hidden * hidden, axis=-1, keepdims=True) + epsilon)


def prepare(bias_table, first_head, heads_dev):
    table = lax.dynamic_slice_in_dim(bias_table, first_head, heads_dev, 1)
    (near,) = call(near_kernel, [((heads_dev, tile, 3 * tile), f32)], table, smem=1)
    return table, near


def bucket_grads(first_lane, grads, bucket_count):
    (total,) = call(bucket_kernel, [((bucket_count, tile), f32)], first_lane, *grads, smem=1)
    return total


def gelu_parts(pre_act):
    cumulative = 0.5 * (1.0 + lax.erf(pre_act * np.float32(0.5**0.5)))
    slope = cumulative + pre_act * jnp.exp(-0.5 * pre_act * pre_act) * np.float32(
        (2 * np.pi) ** -0.5
    )
    return (pre_act * cumulative).astype(bf16), slope


def unit_norm_back(hidden, inverse, grad_unit):
    unit = hidden * inverse
    return inverse * (grad_unit - unit * jnp.mean(grad_unit * unit, axis=-1, keepdims=True))


def gather_rows(block, axes):
    return lax.all_gather(block, axes, axis=0, tiled=True)


def toggle(array, axis, bits):
    return lax.ppermute(array, axis, [(i, i ^ bits) for i in range(lax.axis_size(axis))])


def shift(array, by):
    planes = lax.axis_size("z")
    return lax.ppermute(array, "z", [(i, (i + by) % planes) for i in range(planes)])


def plane_gather(block, *holds):
    near = jnp.concatenate([block] + [toggle(block, "head", bits) for bits in (1, 2, 3)])
    near, *holds = tie(near, *holds)
    return (near, toggle(near, "core", 1), *holds)


def plane_scatter(near_part, far_part):
    rows, columns = near_part.shape[0] // 4, near_part.shape[1]
    own, *others = call(
        combine_kernel,
        [((rows, columns), f32)] + [((rows, columns), bf16)] * 3,
        near_part,
        toggle(far_part, "core", 1),
    )
    shares = [own] + [toggle(other, "head", bits) for bits, other in zip((1, 2, 3), others)]
    return shares, own


def tie(*arrays):
    return lax.optimization_barrier(arrays)


def after(array, other):
    return lax.optimization_barrier((array, other))[0]


def scatter_sum(partial, axes, members):
    blocks = partial.astype(bf16).reshape(members, -1, partial.shape[1])
    return jnp.sum(lax.all_to_all(blocks, axes, 0, 0, tiled=True).astype(f32), axis=0)


def local_general(tokens, doc_start, bias_table, attn_in, attn_out, ff_in, ff_out, gains, cotangent):
    heads_n, z_n, core_n = (lax.axis_size(axis) for axis in everyone)
    devices = heads_n * z_n * core_n
    group, spare = ("z", "core"), "head"
    ff_group, ff_spare, ff_members = ("head", "core"), "z", heads_n * core_n
    blocks = z_n * core_n
    block_rows, model_width = tokens.shape[1:]
    layer_count, weight_rows = attn_in.shape[:2]
    length = block_rows * blocks
    heads_all = bias_table.shape[1]
    member = lax.axis_index("z") * core_n + lax.axis_index("core")
    heads_dev = max(1, heads_all // blocks)
    head_groups = heads_all // heads_dev
    split = blocks // head_groups
    head_group, query_part = member // split, member % split
    query_rows = length // split
    width = heads_dev * head_dim
    first = (query_part * (query_rows // tile)).astype(jnp.int32).reshape(1)
    place = jnp.arange(length // tile, dtype=jnp.int32)
    out_row = head_group * width

    def swap(array):
        return lax.all_to_all(array, everyone, 0, 0, tiled=True)

    starts = jnp.broadcast_to(
        doc_start.astype(f32)[:, None], (heads_n, blocks, block_rows)
    ).reshape(devices, block_rows)
    ff_gains = gains[:, :, 1].astype(f32).reshape(1, -1)
    small = swap(
        jnp.concatenate(
            [starts, jnp.broadcast_to(ff_gains, (devices, layer_count * weight_rows))], axis=1
        )
    )
    doc_row = small[:blocks, :block_rows].reshape(1, length)
    doc_col = lax.dynamic_slice_in_dim(
        doc_row.reshape(length, 1), query_part * query_rows, query_rows, 0
    )
    gain_ff = jnp.transpose(
        small[:, block_rows:].reshape(devices, layer_count, weight_rows), (1, 0, 2)
    ).reshape(layer_count, 1, model_width)
    table, near = prepare(bias_table, head_group * heads_dev, heads_dev)

    gain_attn = gains[:, :, 0].astype(f32)[:, :, None]
    own_in = attn_in.astype(f32)

    def fetch_in(layer_id):
        scaled = (own_in[layer_id] * gain_attn[layer_id]).astype(bf16)
        columns = jnp.transpose(
            scaled.reshape(weight_rows, 3, head_groups, width), (2, 0, 1, 3)
        ).reshape(head_groups, weight_rows, 3 * width)
        columns = jnp.repeat(columns, split, axis=0)
        columns = jnp.broadcast_to(columns[None], (heads_n, *columns.shape))
        return swap(columns.reshape(devices, weight_rows, 3 * width)).reshape(
            model_width, 3 * width
        )

    def fetch_ff(layer_id):
        pair = jnp.concatenate([ff_in[layer_id], ff_out[layer_id]], axis=1)
        pair = gather_rows(pair, ff_spare)
        return pair[:, :model_width], pair[:, model_width:]

    hidden, upstream = tokens[0].astype(f32), cotangent[0]
    weights_in = [fetch_in(layer_id) for layer_id in range(layer_count)]
    weights_out = lax.dynamic_slice_in_dim(
        lax.all_gather(attn_out, everyone, axis=1, tiled=True), out_row, width, 1
    )
    weights_ff = [fetch_ff(layer_id) for layer_id in range(layer_count)]

    records = []
    for layer_id in range(layer_count):
        w_in, w_out, (w_up, w_down) = (
            weights_in[layer_id], weights_out[layer_id], weights_ff[layer_id],
        )
        inverse = inverse_rms(hidden)
        units = gather_rows((hidden * inverse).astype(bf16), group)
        qkv = jnp.dot(units, w_in, preferred_element_type=f32).astype(bf16)
        attended, _, stats = attention(
            qkv, doc_row, doc_col, first, place, table, near, query_rows
        )
        mixed = jnp.dot(attended, w_out, preferred_element_type=f32)
        if split > 1:
            mixed = lax.dynamic_update_slice_in_dim(
                jnp.zeros((length, model_width), f32), mixed, query_part * query_rows, 0
            )
        middle = hidden + scatter_sum(mixed, group, blocks)
        inverse_ff = inverse_rms(middle)
        normed_ff = gather_rows((middle * inverse_ff * gain_ff[layer_id]).astype(bf16), ff_group)
        activated, slope = gelu_parts(contract(normed_ff, w_up, 1, 1))
        ff_result = jnp.dot(activated, w_down, preferred_element_type=f32)
        records.append(
            (hidden, inverse, units, qkv, attended, stats, middle, inverse_ff, normed_ff,
             activated, slope)
        )
        hidden = middle + scatter_sum(ff_result, ff_group, ff_members)
    output = hidden

    grads_ff, grads_in, grads_out, grads_gain_ff, grads_table = (
        [None] * layer_count for _ in range(5)
    )
    for layer_id in reversed(range(layer_count)):
        w_in, w_out, (w_up, w_down) = (
            weights_in[layer_id], weights_out[layer_id], weights_ff[layer_id],
        )
        (hidden, inverse, units, qkv, attended, stats, middle, inverse_ff, normed_ff,
         activated, slope) = records[layer_id]
        grad_low = gather_rows(upstream.astype(bf16), ff_group)
        grad_pre = (contract(grad_low, w_down, 1, 1) * slope).astype(bf16)
        grad_normed = scatter_sum(
            jnp.dot(grad_pre, w_up, preferred_element_type=f32), ff_group, ff_members
        )
        grad_pair = jnp.concatenate(
            [contract(grad_pre, normed_ff, 0, 0), contract(activated, grad_low, 0, 0)], axis=1
        ).astype(bf16)
        grads_ff[layer_id] = lax.psum_scatter(
            grad_pair, ff_spare, scatter_dimension=0, tiled=True
        ).astype(f32)
        grads_gain_ff[layer_id] = jnp.sum(grad_normed * middle * inverse_ff, axis=0)
        grad_middle = upstream + unit_norm_back(
            middle, inverse_ff, grad_normed * gain_ff[layer_id]
        )
        branch = gather_rows(grad_middle.astype(bf16), group)
        if split > 1:
            branch = lax.dynamic_slice_in_dim(branch, query_part * query_rows, query_rows, 0)
        grad_attended = contract(branch, w_out, 1, 1).astype(bf16)
        grad_qkv, grad_near, grad_far = attention_back(
            qkv, doc_row, doc_col, attended, grad_attended, stats, first, place, table, near, split
        )
        grads_table[layer_id] = (grad_near, grad_far)
        grad_units = scatter_sum(contract(grad_qkv, w_in, 1, 1), group, blocks)
        upstream = grad_middle + unit_norm_back(hidden, inverse, grad_units)
        grad_out = lax.dynamic_update_slice_in_dim(
            jnp.zeros((model_width, model_width), bf16),
            contract(attended, branch, 0, 0).astype(bf16),
            out_row,
            0,
        )
        grads_out[layer_id] = lax.psum_scatter(
            grad_out, everyone, scatter_dimension=0, tiled=True
        ).astype(f32)
        grads_in[layer_id] = contract(units, grad_qkv, 0, 0).astype(bf16)

    bucket_count = table.shape[0]
    grad_table = sum(
        bucket_grads(jnp.zeros((1,), jnp.int32), entry, bucket_count) for entry in grads_table
    )[:, :heads_dev]
    grad_table = lax.dynamic_update_slice_in_dim(
        jnp.zeros((bucket_count, heads_all), f32), grad_table, head_group * heads_dev, 1
    )
    grad_table = jnp.transpose(
        grad_table.reshape(blocks, bucket_count // blocks, heads_n, heads_all // heads_n),
        (2, 0, 1, 3),
    ).reshape(devices, -1)
    grad_gain_ff = jnp.transpose(
        jnp.stack(grads_gain_ff).reshape(layer_count, devices, weight_rows), (1, 0, 2)
    ).reshape(devices, -1)
    ends = jnp.sum(swap(jnp.concatenate([grad_gain_ff, grad_table], axis=1)), axis=0)
    grad_gain_ff = ends[: layer_count * weight_rows].reshape(layer_count, weight_rows)
    grad_bias_table = ends[layer_count * weight_rows :].reshape(
        bucket_count // blocks, heads_all // heads_n
    )
    grads_attn_in, grads_gains = [], []
    for layer_id in range(layer_count):
        parts = swap(grads_in[layer_id].reshape(devices, weight_rows, 3 * width)).astype(f32)
        parts = jnp.sum(parts.reshape(heads_n, blocks, weight_rows, 3 * width), axis=0)
        parts = jnp.sum(parts.reshape(head_groups, split, weight_rows, 3, width), axis=1)
        unit_grad = jnp.transpose(parts, (1, 2, 0, 3)).reshape(weight_rows, 3 * model_width)
        grads_attn_in.append(unit_grad * gain_attn[layer_id])
        grads_gains.append(
            jnp.stack(
                [jnp.sum(unit_grad * own_in[layer_id], axis=1), grad_gain_ff[layer_id]], axis=1
            )
        )
    return (
        output[None],
        upstream[None],
        jnp.stack(grads_attn_in),
        jnp.stack(grads_out),
        jnp.stack([entry[:, :model_width] for entry in grads_ff]),
        jnp.stack([entry[:, model_width:] for entry in grads_ff]),
        jnp.stack(grads_gains),
        grad_bias_table,
    )


def local_plane(tokens, doc_start, bias_table, attn_in, attn_out, ff_in, ff_out, gains, cotangent):
    heads_n, z_n, core_n = (lax.axis_size(axis) for axis in everyone)
    devices = heads_n * z_n * core_n
    at_head, at_z, at_core = (lax.axis_index(axis) for axis in everyone)
    members = heads_n * core_n
    block_rows, model_width = tokens.shape[1:]
    layer_count, weight_rows = attn_in.shape[:2]
    length = block_rows * members
    heads_all = bias_table.shape[1]
    heads_dev = heads_all // members
    width = heads_dev * head_dim
    member = at_head * core_n + at_core
    everywhere = [(h, z, c) for h in range(heads_n) for z in range(z_n) for c in range(core_n)]

    def swapped(bits):
        return bits % 2 * 2 + bits // 2

    def device(h, z, c):
        return (h * z_n + z) * core_n + c

    turn = [(device(h, z, c), device(h ^ swapped(z), h, c)) for h, z, c in everywhere]
    plane_turn = [(device(h, z, c), device(h ^ swapped(z), z, c)) for h, z, c in everywhere]
    line_turn = [(device(h, z, c), device(h, h ^ swapped(z), c)) for h, z, c in everywhere]
    line_back = [(target, source) for source, target in line_turn]
    place = jnp.stack(
        [
            (at_head ^ bits) * core_n + (at_core ^ other)
            for other in range(core_n)
            for bits in range(heads_n)
        ]
        + [at_z]
        + [
            swapped(at_head ^ bits ^ at_z) * core_n + (at_core ^ other)
            for other in range(core_n)
            for bits in range(heads_n)
        ]
    ).astype(jnp.int32)

    def relay(array):
        return lax.ppermute(array, everyone, turn)

    def turn_in_plane(array):
        return lax.ppermute(array, everyone, plane_turn)

    def turn_in_line(array, turns):
        return lax.ppermute(array, everyone, turns)

    def swap(array):
        return lax.all_to_all(array, everyone, 0, 0, tiled=True)

    row_shape = (block_rows, model_width)
    gain_attn = gains[:, :, 0].astype(f32)[:, :, None]
    near_share, far_share = call(
        share_in_kernel,
        [((members // 2 * layer_count * weight_rows, 3 * width), bf16)] * 2,
        place,
        attn_in,
        gain_attn,
        smem=1,
    )

    half_turns = [
        [
            (z * core_n + c, (2 * c + (a ^ z % 2)) * core_n + z // 2)
            for z in range(z_n)
            for c in range(core_n)
        ]
        for a in range(2)
    ]

    def fetch_out(layer_id, hold):
        own = attn_out[layer_id]
        other = toggle(own, "core", 1)
        head = jnp.where(
            at_core == 0, jnp.concatenate([own, other]), jnp.concatenate([other, own])
        )
        head = after(head, hold)
        return [
            lax.ppermute(head, ("z", "core"), [(holder, user) for user, holder in turns])
            for turns in half_turns
        ]

    def owners_halves(halves):
        return [
            lax.ppermute(half, ("z", "core"), turns) for half, turns in zip(halves, half_turns)
        ]

    def pair_chips(near, arrived, axis):
        rows, columns = near.shape[0] // 4, near.shape[1]
        shape = (2 * rows, columns) if axis == 0 else (rows, 2 * columns)
        return call(functools.partial(pair_kernel, axis), [(shape, bf16)] * 4, near, arrived)

    def share_chips(blocks):
        return [blocks[0]] + [toggle(blocks[bits], "head", bits) for bits in (1, 2, 3)]

    units_shape = [(row_shape, f32), (row_shape, bf16)]

    starts = jnp.broadcast_to(
        doc_start.astype(f32)[None, :, None], (heads_n, z_n, core_n, block_rows)
    )
    ff_gains = gains[:, :, 1].astype(f32).reshape(1, -1)
    small = jnp.concatenate(
        [
            starts.reshape(devices, block_rows),
            jnp.broadcast_to(ff_gains, (devices, layer_count * weight_rows)),
        ],
        axis=1,
    )
    table, strip = prepare(bias_table, member * heads_dev, heads_dev)
    hidden = relay(tokens[0])
    hidden, shares, halves, small = tie(
        hidden,
        share_chips(pair_chips(near_share, toggle(far_share, "core", 1), 0)),
        fetch_out(0, near_share),
        swap(after(small, near_share)),
    )
    hidden, unit_rows = call(unit_kernel, units_shape, hidden)
    doc_row = small[:members, :block_rows].reshape(2, 2, core_n, block_rows)
    at_block = swapped(at_head ^ at_z)
    for axis, bit in ((0, at_block // 2), (1, at_block % 2), (2, at_core)):
        doc_row = jnp.where(bit == 1, jnp.flip(doc_row, axis), doc_row)
    doc_row = jnp.transpose(doc_row, (2, 1, 0, 3)).reshape(1, length)
    doc_col = doc_row.reshape(length, 1)
    gain_ff = jnp.transpose(
        small[:, block_rows:].reshape(devices, layer_count, weight_rows), (1, 0, 2)
    ).reshape(layer_count, 1, model_width)

    def round_planes(array, by, hold):
        return shift(after(array, hold), by)

    ff_pairs = [
        jnp.concatenate([ff_in[layer_id], ff_out[layer_id]], axis=1) for layer_id in range(layer_count)
    ]

    def ff_both(kernel, row_operands, pair, columns):
        return zip(
            *(
                by_rows(
                    kernel,
                    256,
                    operands,
                    [pair],
                    [(pair.shape[0], bf16)] * columns + [(model_width, kind)],
                )
                for operands, kind in zip(zip(*row_operands), (f32, bf16))
            )
        )

    def ff_forward(normed, *parts):
        units = 4 * parts[0].shape[0]
        outs = [(units, bf16), (units, bf16)]
        *near, pair = by_rows(
            ff_first_kernel,
            256,
            [normed[0]],
            parts,
            outs + [(model_width, f32)],
            [(units, 2 * model_width)],
        )
        far = by_rows(ff_kernel, 256, [normed[1]], [pair], outs + [(model_width, bf16)])
        return pair, *zip(near, far)

    def ff_backward(low, slopes, pair):
        return ff_both(ff_back_kernel, [low, slopes], pair, 1)

    def assemble_in(share, lower, upper, opposite):
        return call(
            assemble_in_kernel,
            [((model_width, 3 * width), bf16)],
            place,
            share,
            lower,
            upper,
            opposite,
            smem=1,
        )[0]

    share, later_share = call(
        join_kernel, [((members * weight_rows, 3 * width), bf16)] * layer_count, *shares
    )
    near, far, w_in, cotangent_low, strip, doc_row, doc_col, gain_ff, *ff_pairs = plane_gather(
        unit_rows,
        assemble_in(share, shift(share, 1), shift(share, -1), shift(share, 2)),
        cotangent[0].astype(bf16),
        strip,
        doc_row,
        doc_col,
        gain_ff,
        *ff_pairs,
    )
    units = (near, far)
    w_out, qkv, attended, stats, *parts = plane_attention(
        *units, w_in, halves, doc_row, doc_col, place, table, strip
    )
    parts, lower, upper, cotangent_low = tie(
        parts,
        round_planes(ff_pairs[0], 1, near),
        round_planes(ff_pairs[0], -1, near),
        turn_in_plane(after(cotangent_low, near)),
    )
    parts, own = plane_scatter(*parts)
    parts, opposite_in = tie(parts, round_planes(ff_in[0], 2, own))
    middle, normed_rows = call(close_gain_kernel, units_shape, hidden, *parts, gain_ff[0])
    *normed, opposite_out = plane_gather(normed_rows, round_planes(ff_out[0], 2, normed_rows))
    pair, acts, slopes, parts = ff_forward(
        normed, ff_pairs[0], lower, upper, opposite_in, opposite_out
    )
    records = [
        (hidden, units, w_in, w_out, pair, qkv, attended, stats, middle, normed, acts, slopes)
    ]
    parts, lower, upper = tie(
        parts,
        round_planes(later_share, 1, normed[0]),
        round_planes(later_share, -1, normed[0]),
    )
    parts, own = plane_scatter(*parts)
    parts, opposite, upstream = tie(
        parts, round_planes(later_share, 2, own), turn_in_line(after(cotangent_low, own), line_turn)
    )
    shares = [later_share, lower, upper, opposite]
    hidden, unit_rows = call(close_kernel, units_shape, middle, *parts)

    near, far, lower, halves, w_in = plane_gather(
        unit_rows,
        round_planes(ff_pairs[1], 1, unit_rows),
        fetch_out(1, unit_rows),
        assemble_in(*after(shares, unit_rows)),
    )
    units = (near, far)
    w_out, qkv, attended, stats, *parts = plane_attention(
        *units, w_in, halves, doc_row, doc_col, place, table, strip
    )
    low = plane_gather(after(upstream, far))
    parts, near_low, upper = tie(parts, low[0], round_planes(ff_pairs[1], -1, far))
    low = (near_low, low[1])
    parts, own = plane_scatter(*parts)
    parts, opposite_in = tie(parts, round_planes(ff_in[1], 2, own))
    middle, normed_rows = call(close_gain_kernel, units_shape, hidden, *parts, gain_ff[1])
    *normed, opposite_out = plane_gather(normed_rows, round_planes(ff_out[1], 2, normed_rows))
    pair, acts, slopes, last_parts = ff_forward(
        normed, ff_pairs[1], lower, upper, opposite_in, opposite_out
    )
    records.append(
        (hidden, units, w_in, w_out, pair, qkv, attended, stats, middle, normed, acts, slopes)
    )

    def back_to_middle(parts, upstream, middle, gain):
        return call(
            middle_back_kernel, units_shape + [((1, model_width), f32)], upstream, *parts, middle, gain
        )

    def attention_grads(record, branch):
        _, _, w_in, w_out, _, qkv, attended, stats, *_ = record
        grad_qkv, grad_near, grad_far, near_part, far_part, *halves = plane_attention_back(
            qkv, doc_row, doc_col, attended, stats, *branch, w_in, w_out, place, table, strip
        )
        return grad_qkv, (grad_near, grad_far), (near_part, far_part), halves

    def table_grads(near_and_far):
        return bucket_grads(at_core.reshape(1) * heads_dev + 8, near_and_far, table.shape[0])

    record = records[1]
    hidden, units, _, _, pair, *_, middle, normed, acts, slopes = record
    pres, parts = ff_backward(low, slopes, pair)
    parts, own = plane_scatter(*parts)
    planes = ff_grads(after(pres, own), acts, normed, low)
    parts, ff_lower = tie(parts, shift(planes[1], -1))
    last_parts, _ = plane_scatter(*after(last_parts, parts))
    grad_middle, branch_rows, gain_1 = back_to_middle(parts, upstream, middle, gain_ff[1])
    *branch, ff_upper = plane_gather(branch_rows, round_planes(planes[2], 1, branch_rows))
    grad_qkv, strips_1, parts, halves_1 = attention_grads(record, branch)
    parts, last_parts, opposite_up = tie(
        parts, last_parts, round_planes(planes[3], 2, branch[1])
    )
    parts, own = plane_scatter(*parts)
    parts, opposite_down, output = tie(
        parts,
        round_planes(planes[4], 2, own),
        call(last_kernel, [(row_shape, bf16)], middle, *after(last_parts, own))[0],
    )
    grads_ff = [planes[0], ff_lower, ff_upper, opposite_up, opposite_down]
    upstream, low_rows = call(layer_back_kernel, units_shape, grad_middle, *parts, hidden)

    record = records[0]
    hidden, units, _, _, pair, *_, middle, normed, acts, slopes = record
    grad_in = in_grads(place, *records[1][1], after(grad_qkv, low_rows))
    *low, in_opposite, in_upper, table_1 = plane_gather(
        low_rows, shift(grad_in[3], 2), shift(grad_in[2], 1), table_grads(after(strips_1, low_rows))
    )
    pres, parts = ff_backward(low, slopes, pair)
    parts, in_lower = tie(parts, round_planes(grad_in[1], -1, low[0]))
    parts, own = plane_scatter(*parts)
    planes = ff_grads(after(pres, own), acts, normed, low)
    near_in, far_in = call(
        add_in_kernel,
        [((members // 2 * weight_rows, 3 * width), bf16)] * 2,
        *after([grad_in[0], in_lower, in_upper, in_opposite], own),
    )
    parts, ff_lower, first_half, arrived = tie(
        parts,
        shift(planes[1], -1),
        owners_halves(after(halves_1, own))[0],
        toggle(far_in, "core", 1),
    )
    grad_middle, branch_rows, gain_0 = back_to_middle(parts, upstream, middle, gain_ff[0])
    *branch, ff_upper, second_half, shares_1 = plane_gather(
        branch_rows,
        round_planes(planes[2], 1, branch_rows),
        owners_halves(after(halves_1, branch_rows))[1],
        pair_chips(near_in, after(arrived, branch_rows), 1),
    )
    halves_1 = [first_half, second_half]
    grad_qkv, strips_0, parts, halves_0 = attention_grads(record, branch)
    parts, shares_1, output, opposite_up = tie(
        parts,
        share_chips(after(shares_1, branch[1])), turn_in_line(after(output, branch[1]), line_back), round_planes(planes[3], 2, branch[1])
    )
    parts, own = plane_scatter(*parts)
    table_0 = table_grads(after(strips_0, own))
    grad_in = in_grads(
        place, *units, after(grad_qkv, own), gain_0, gain_1, table_0, table_1
    )
    parts, in_opposite, halves_0 = tie(
        parts, shift(grad_in[3], 2), owners_halves(after(halves_0, own))
    )
    upstream, low_rows = call(layer_back_kernel, units_shape, grad_middle, *parts, hidden)
    in_lower = round_planes(grad_in[1], -1, low_rows)
    in_upper = round_planes(grad_in[2], 1, low_rows)
    line = turn_in_line(low_rows, line_back)
    near_in, far_in = call(
        add_in_kernel,
        [((members // 2 * weight_rows, 3 * width + tile), bf16)] * 2,
        grad_in[0],
        in_lower,
        in_upper,
        in_opposite,
    )
    arrived = toggle(far_in, "core", 1)
    shares_0 = share_chips(pair_chips(near_in, arrived, 1))
    opposite_down = round_planes(planes[4], 2, near_in)
    grad_tokens = turn_in_plane(after(line, shares_0[1:]))
    output = turn_in_plane(after(output, shares_0[1:]))
    (output,) = call(widen_kernel, [(row_shape, f32)], output)
    (grad_tokens,) = call(widen_kernel, [(row_shape, f32)], grad_tokens)
    grads_ff = [planes[0], ff_lower, ff_upper, opposite_up, opposite_down] + grads_ff
    grad_up, grad_down = finish_ff(after(grads_ff, shares_0[1:]), ff_in.shape)
    own_out, other_out = call(
        add_out_kernel,
        [(attn_out.shape, f32), (attn_out.shape, bf16)],
        place,
        *after(halves_0 + halves_1, shares_0[1:]),
        smem=1,
    )
    (grad_attn_out,) = call(
        finish_out_kernel, [(attn_out.shape, f32)], own_out, toggle(other_out, "core", 1)
    )
    own_buckets = table.shape[0] // (z_n * core_n)
    grad_attn_in, grad_gains, ends = call(
        finish_in_kernel,
        [(attn_in.shape, f32), (gains.shape, f32), ((weight_rows, tile), f32)],
        place,
        *shares_0,
        *shares_1,
        attn_in,
        gain_attn,
        smem=1,
    )
    return (
        output[None],
        grad_tokens[None],
        grad_attn_in,
        grad_attn_out,
        grad_up,
        grad_down,
        grad_gains,
        ends[:own_buckets, 8 : 8 + heads_all // heads_n],
    )


def solution(mesh):
    sizes = dict(mesh.shape)
    cores = 2
    fine = Mesh(
        mesh.devices.reshape(sizes["head"], sizes["blk"] // cores, cores), everyone
    )
    blk = ("z", "core")
    in_specs = (
        P("head", blk, None),
        P(None, blk),
        P(),
        P(None, everyone, None),
        P(None, everyone, None),
        P(None, everyone, None),
        P(None, everyone, None),
        P(None, everyone, None),
        P("head", blk, None),
    )
    out_specs = (
        P("head", blk, None),
        P("head", blk, None),
        P(None, everyone, None),
        P(None, everyone, None),
        P(None, everyone, None),
        P(None, everyone, None),
        P(None, everyone, None),
        P(blk, "head"),
    )
    plane = sizes["head"] == 4 and sizes["blk"] == 8
    local = local_plane if plane else local_general
    return jax.shard_map(local, mesh=fine, in_specs=in_specs, out_specs=out_specs, check_vma=False)
```

```python
import functools

import jax
import jax.numpy as jnp
import numpy as np
from jax import lax
from jax.experimental import pallas as pl
from jax.experimental.pallas import tpu as pltpu
from jax.sharding import Mesh
from jax.sharding import PartitionSpec as P

bounds = (1, 2, 3, 4, 5, 6, 7, 8, 12, 16, 23, 32, 46, 64, 91)
epsilon = 1e-06
masked = -1e30
score_scale = 0.125
head_dim = 64
tile = 128
everyone = ("head", "z", "core")
bf16 = jnp.bfloat16
f32 = jnp.float32


def contract(lhs, rhs, lhs_dim, rhs_dim):
    return lax.dot_general(
        lhs, rhs, (((lhs_dim,), (rhs_dim,)), ((), ())), preferred_element_type=f32
    )


def near_buckets(shape):
    offsets = (
        lax.broadcasted_iota(jnp.int32, shape, 1) - tile - lax.broadcasted_iota(jnp.int32, shape, 0)
    )
    distance = jnp.abs(offsets)
    bucket = jnp.where(offsets > 0, 16, 0)
    for boundary in bounds:
        bucket = bucket + jnp.where(distance >= boundary, 1, 0)
    return bucket


def near_kernel(table, near):
    bucket = near_buckets(near.shape[1:])
    for head in range(near.shape[0]):
        values = jnp.zeros(near.shape[1:], f32)
        for bucket_id in range(table.shape[0]):
            values = jnp.where(bucket == bucket_id, table[bucket_id, head], values)
        near[head] = values


def bucket_kernel(first_lane, near, far, out):
    bucket = near_buckets(near.shape[1:])
    rows = lax.broadcasted_iota(jnp.int32, out.shape, 0)
    lanes = lax.broadcasted_iota(jnp.int32, out.shape, 1)
    total = jnp.zeros(out.shape, f32)
    for head in range(near.shape[0]):
        strip = near[head]
        for bucket_id in range(out.shape[0]):
            value = jnp.sum(jnp.where(bucket == bucket_id, strip, 0.0), axis=0, keepdims=True)
            value = jnp.sum(value, axis=1, keepdims=True)
            if bucket_id in (15, 31):
                value = value + far[head, bucket_id // 16, :1, :1]
            total = jnp.where((rows == bucket_id) & (lanes == head + first_lane[0]), value, total)
    out[...] = total


def fill_band(band, table, near, heads_dev, length):
    for head in range(heads_dev):
        band[head, :, : length - tile] = jnp.full((tile, length - tile), table[15, head], f32)
        band[head, :, length - tile : length + 2 * tile] = near[head]
        band[head, :, length + 2 * tile :] = jnp.full(
            (tile, length - 2 * tile), table[31, head], f32
        )


def band_starts(place, at, length, skip=0):
    return [
        pl.multiple_of(length + (place[skip + block] - place[skip + at]) * tile, tile)
        for block in range(length // tile)
    ]


def attention_kernel(
    heads_dev, length, first, place, table, near, qkv, doc_row, doc_col, out, local, stats, band
):
    step = pl.program_id(0)
    width = heads_dev * head_dim

    @pl.when(step == 0)
    def _():
        fill_band(band, table, near, heads_dev, length)

    row = pl.multiple_of((first[0] + step) * tile, tile)
    out_row = pl.multiple_of((place[first[0] + step] - first[0]) * tile, tile)
    starts = band_starts(place, first[0] + step, length)
    same_doc = doc_col[...] == doc_row[...]
    queries = qkv[pl.ds(row, tile), :width] * bf16(score_scale)
    lanes = lax.broadcasted_iota(jnp.int32, (tile, tile), 1)
    collected = jnp.zeros((tile, tile), f32)
    for head in range(heads_dev):
        own = slice(head * head_dim, (head + 1) * head_dim)
        keys = qkv[:, width + own.start : width + own.stop]
        values = qkv[:, 2 * width + own.start : 2 * width + own.stop]
        scores = contract(queries[:, own], keys, 1, 1)
        scores = scores + jnp.concatenate(
            [band[head, :, pl.ds(start, tile)] for start in starts], axis=1
        )
        scores = jnp.where(same_doc, scores, masked)
        peak = jnp.max(scores, axis=1, keepdims=True)
        weights = jnp.exp(scores - peak)
        total = jnp.sum(weights, axis=1, keepdims=True)
        mixed = contract(weights.astype(bf16), values, 1, 0) / total
        out[pl.ds(out_row, tile), own] = mixed.astype(bf16)
        local[:, own] = mixed.astype(bf16)
        collected = jnp.where(lanes == head, peak + jnp.log(total), collected)
    stats[...] = collected


def attention_back_kernel(
    heads_dev, length, split, first, place, table, near, qkv, doc_row, doc_col, attended, grad_out, stats,
    grad_qkv, grad_near, grad_far, band, grad_band, grad_keys, grad_values,
):
    step = pl.program_id(0)
    width = heads_dev * head_dim

    @pl.when(step == 0)
    def _():
        fill_band(band, table, near, heads_dev, length)
        grad_band[...] = jnp.zeros_like(grad_band)
        grad_keys[...] = jnp.zeros_like(grad_keys)
        grad_values[...] = jnp.zeros_like(grad_values)
        if split > 1:
            grad_qkv[...] = jnp.zeros_like(grad_qkv)

    row = pl.multiple_of((first[0] + step) * tile, tile)
    out_row = pl.multiple_of((place[first[0] + step] - first[0]) * tile, tile)
    starts = band_starts(place, first[0] + step, length)
    same_doc = doc_col[...] == doc_row[...]
    at_step = pl.multiple_of(step * tile, tile)
    queries = qkv[pl.ds(row, tile), :width] * bf16(score_scale)
    for head in range(heads_dev):
        own = slice(head * head_dim, (head + 1) * head_dim)
        keys = qkv[:, width + own.start : width + own.stop]
        values = qkv[:, 2 * width + own.start : 2 * width + own.stop]
        upstream = grad_out[pl.ds(out_row, tile), own]
        scores = contract(queries[:, own], keys, 1, 1) + jnp.concatenate(
            [band[head, :, pl.ds(start, tile)] for start in starts], axis=1
        )
        scores = jnp.where(same_doc, scores, masked)
        weights = jnp.exp(scores - stats[:, head : head + 1])
        delta = jnp.sum(
            upstream.astype(f32) * attended[pl.ds(at_step, tile), own].astype(f32),
            axis=1,
            keepdims=True,
        )
        grad_scores = weights * (contract(upstream, values, 1, 1) - delta)
        for block, start in enumerate(starts):
            grad_band[head, :, pl.ds(start, tile)] += grad_scores[
                :, block * tile : (block + 1) * tile
            ]
        grad_low = grad_scores.astype(bf16)
        grad_values[:, own] += contract(weights.astype(bf16), upstream, 0, 0)
        grad_keys[:, own] += contract(grad_low, queries[:, own], 0, 0)
        grad_qkv[pl.ds(row, tile), own] = (
            contract(grad_low, keys, 1, 0) * score_scale
        ).astype(bf16)

    @pl.when(step == pl.num_programs(0) - 1)
    def _():
        grad_qkv[:, width : 2 * width] = grad_keys[...].astype(bf16)
        grad_qkv[:, 2 * width :] = grad_values[...].astype(bf16)
        for head in range(heads_dev):
            grad_near[head] = grad_band[head, :, length - tile : length + 2 * tile]
            grad_far[head, 0] = jnp.full(
                (8, tile), jnp.sum(grad_band[head, :, : length - tile]), f32
            )
            grad_far[head, 1] = jnp.full(
                (8, tile), jnp.sum(grad_band[head, :, length + 2 * tile :]), f32
            )


def whole(shape):
    return pl.BlockSpec(shape, lambda step: (0,) * len(shape), pipeline_mode=pl.Buffered(1))


def attention(qkv, doc_row, doc_col, first, place, table, near, rows):
    length = qkv.shape[0]
    heads_dev = table.shape[1]
    width = heads_dev * head_dim
    return pl.pallas_call(
        functools.partial(attention_kernel, heads_dev, length),
        grid=(rows // tile,),
        in_specs=[
            pl.BlockSpec(memory_space=pltpu.SMEM),
            pl.BlockSpec(memory_space=pltpu.SMEM),
            pl.BlockSpec(memory_space=pltpu.SMEM),
            whole(near.shape),
            whole(qkv.shape),
            whole(doc_row.shape),
            pl.BlockSpec((tile, 1), lambda step: (step, 0)),
        ],
        out_specs=[
            whole((rows, width)),
            pl.BlockSpec((tile, width), lambda step: (step, 0)),
            pl.BlockSpec((tile, tile), lambda step: (step, 0)),
        ],
        out_shape=[
            jax.ShapeDtypeStruct((rows, width), bf16),
            jax.ShapeDtypeStruct((rows, width), bf16),
            jax.ShapeDtypeStruct((rows, tile), f32),
        ],
        scratch_shapes=[pltpu.VMEM((heads_dev, tile, 2 * length), f32)],
        compiler_params=pltpu.CompilerParams(vmem_limit_bytes=40 * 2**20),
        cost_estimate=pl.CostEstimate(
            flops=4 * rows * length * width,
            bytes_accessed=4 * length * width * 2,
            transcendentals=rows * length * heads_dev,
        ),
    )(first, place, table, near, qkv, doc_row, doc_col)


def attention_back(
    qkv, doc_row, doc_col, attended, grad_out, stats, first, place, table, near, split
):
    length = qkv.shape[0]
    rows = grad_out.shape[0]
    heads_dev = table.shape[1]
    width = heads_dev * head_dim
    return pl.pallas_call(
        functools.partial(attention_back_kernel, heads_dev, length, split),
        grid=(rows // tile,),
        in_specs=[
            pl.BlockSpec(memory_space=pltpu.SMEM),
            pl.BlockSpec(memory_space=pltpu.SMEM),
            pl.BlockSpec(memory_space=pltpu.SMEM),
            whole(near.shape),
            whole(qkv.shape),
            whole(doc_row.shape),
            pl.BlockSpec((tile, 1), lambda step: (step, 0)),
            whole((rows, width)),
            whole((rows, width)),
            pl.BlockSpec((tile, tile), lambda step: (step, 0)),
        ],
        out_specs=[
            whole((length, 3 * width)),
            whole((heads_dev, tile, 3 * tile)),
            whole((heads_dev, 2, 8, tile)),
        ],
        out_shape=[
            jax.ShapeDtypeStruct((length, 3 * width), bf16),
            jax.ShapeDtypeStruct((heads_dev, tile, 3 * tile), f32),
            jax.ShapeDtypeStruct((heads_dev, 2, 8, tile), f32),
        ],
        scratch_shapes=[
            pltpu.VMEM((heads_dev, tile, 2 * length), f32),
            pltpu.VMEM((heads_dev, tile, 2 * length), f32),
            pltpu.VMEM((length, width), f32),
            pltpu.VMEM((length, width), f32),
        ],
        compiler_params=pltpu.CompilerParams(vmem_limit_bytes=48 * 2**20),
        cost_estimate=pl.CostEstimate(
            flops=10 * rows * length * width,
            bytes_accessed=8 * length * width * 2,
            transcendentals=rows * length * heads_dev,
        ),
    )(first, place, table, near, qkv, doc_row, doc_col, attended, grad_out, stats)


def call(kernel, shapes, *operands, smem=0):
    return pl.pallas_call(
        kernel,
        in_specs=[pl.BlockSpec(memory_space=pltpu.SMEM)] * smem
        + [pl.BlockSpec(memory_space=pltpu.VMEM)] * (len(operands) - smem),
        out_specs=[pl.BlockSpec(memory_space=pltpu.VMEM)] * len(shapes),
        out_shape=[jax.ShapeDtypeStruct(shape, kind) for shape, kind in shapes],
        compiler_params=pltpu.CompilerParams(vmem_limit_bytes=10 * 2**20),
    )(*operands)


def share_in_kernel(place, attn_in, gains, near, far):
    layers, rows = attn_in.shape[:2]
    half = near.shape[0] // (layers * rows)
    width = near.shape[1] // 3
    for index in range(2 * half):
        member = place[index]
        for layer_id in range(layers):
            block = jnp.concatenate(
                [
                    attn_in[
                        layer_id,
                        :,
                        pl.ds(pl.multiple_of((part * 2 * half + member) * width, width), width),
                    ]
                    for part in range(3)
                ],
                axis=1,
            )
            at = (index % half * layers + layer_id) * rows
            out = near if index < half else far
            out[at : at + rows] = (block.astype(f32) * gains[layer_id]).astype(bf16)


def join_kernel(*refs):
    shares, outs = refs[:4], refs[4:]
    rows = outs[0].shape[0] // 8
    for chip, share in enumerate(shares):
        for core in range(2):
            for layer_id, out in enumerate(outs):
                source = (core * len(outs) + layer_id) * rows
                target = (chip * 2 + core) * rows
                out[target : target + rows] = share[source : source + rows]


def row_of(chip, plane, core, rows, planes=4):
    return pl.multiple_of(((chip * planes + plane) * 2 + core) * rows, rows)


def assemble_in_kernel(place, own, lower, upper, opposite, out):
    at_z, at_core, at_head = place[8], place[0] % 2, place[0] // 2
    rows = own.shape[0] // 8
    for part, offset in ((own, 0), (lower, 3), (upper, 1), (opposite, 2)):
        plane = (at_z + offset) % 4
        for index in range(8):
            row = row_of(at_head ^ (index // 2), plane, at_core ^ (index % 2), rows)
            out[pl.ds(row, rows)] = part[index * rows : (index + 1) * rows]


def plane_attention_kernel(
    length, place, table, strip, near, far, w_in, *refs
):
    halves, (doc_row, doc_col, w_out, qkv, attended, stats, near_part, far_part, band) = (
        refs[:2], refs[2:],
    )
    step = pl.program_id(0)
    half = length // 2
    heads_dev = table.shape[1]
    width = heads_dev * head_dim

    @pl.when(step == 0)
    def _():
        fill_band(band, table, strip, heads_dev, length)
        swapped = place[length // tile] % 2 == 1
        rows = width // 2
        w_out[:rows] = jnp.where(swapped, halves[1][...], halves[0][...])
        w_out[rows:] = jnp.where(swapped, halves[0][...], halves[1][...])
        qkv[:half] = contract(near[...], w_in[...], 1, 0).astype(bf16)
        qkv[half:] = contract(far[...], w_in[...], 1, 0).astype(bf16)

    row = pl.multiple_of(step * tile, tile)
    starts = band_starts(place, step, length, length // tile + 1)
    same_doc = doc_col[...] == doc_row[...]
    queries = qkv[pl.ds(row, tile), :width] * bf16(score_scale)
    lanes = lax.broadcasted_iota(jnp.int32, (tile, tile), 1)
    collected = jnp.zeros((tile, tile), f32)
    results = []
    for head in range(heads_dev):
        own = slice(head * head_dim, (head + 1) * head_dim)
        keys = qkv[:, width + own.start : width + own.stop]
        values = qkv[:, 2 * width + own.start : 2 * width + own.stop]
        scores = contract(queries[:, own], keys, 1, 1) + jnp.concatenate(
            [band[head, :, pl.ds(start, tile)] for start in starts], axis=1
        )
        scores = jnp.where(same_doc, scores, masked)
        peak = jnp.max(scores, axis=1, keepdims=True)
        weights = jnp.exp(scores - peak)
        total = jnp.sum(weights, axis=1, keepdims=True)
        results.append((contract(weights.astype(bf16), values, 1, 0) / total).astype(bf16))
        collected = jnp.where(lanes == head, peak + jnp.log(total), collected)
    stats[...] = collected
    merged = jnp.concatenate(results, axis=1)
    attended[...] = merged
    part = contract(merged, w_out[...], 1, 0)

    @pl.when(row < half)
    def _():
        near_part[...] = part

    @pl.when(row >= half)
    def _():
        far_part[...] = part.astype(bf16)


def near_block(steps, columns):
    return pl.BlockSpec((tile, columns), lambda step: (jnp.minimum(step, steps // 2 - 1), 0))


def far_block(steps, columns):
    return pl.BlockSpec((tile, columns), lambda step: (jnp.maximum(step - steps // 2, 0), 0))


def plane_attention(near, far, w_in, halves, doc_row, doc_col, place, table, strip):
    length, model_width = 2 * near.shape[0], near.shape[1]
    steps = length // tile
    heads_dev = table.shape[1]
    width = heads_dev * head_dim
    return pl.pallas_call(
        functools.partial(plane_attention_kernel, length),
        grid=(steps,),
        in_specs=[
            pl.BlockSpec(memory_space=pltpu.SMEM),
            pl.BlockSpec(memory_space=pltpu.SMEM),
            whole(strip.shape),
            whole(near.shape),
            whole(far.shape),
            whole(w_in.shape),
            *[whole(half.shape) for half in halves],
            whole(doc_row.shape),
            pl.BlockSpec((tile, 1), lambda step: (step, 0)),
        ],
        out_specs=[
            whole((width, model_width)),
            whole((length, 3 * width)),
            pl.BlockSpec((tile, width), lambda step: (step, 0)),
            pl.BlockSpec((tile, tile), lambda step: (step, 0)),
            near_block(steps, model_width),
            far_block(steps, model_width),
        ],
        out_shape=[
            jax.ShapeDtypeStruct((width, model_width), bf16),
            jax.ShapeDtypeStruct((length, 3 * width), bf16),
            jax.ShapeDtypeStruct((length, width), bf16),
            jax.ShapeDtypeStruct((length, tile), f32),
            jax.ShapeDtypeStruct((length // 2, model_width), f32),
            jax.ShapeDtypeStruct((length // 2, model_width), bf16),
        ],
        scratch_shapes=[pltpu.VMEM((heads_dev, tile, 2 * length), f32)],
        compiler_params=pltpu.CompilerParams(vmem_limit_bytes=14 * 2**20),
        cost_estimate=pl.CostEstimate(
            flops=4 * length * length * width + 8 * length * model_width * width,
            bytes_accessed=12 * 2**20,
            transcendentals=length * length * heads_dev,
        ),
    )(place, table, strip, near, far, w_in, *halves, doc_row, doc_col)


def plane_attention_back_kernel(
    length, place, table, strip, qkv, doc_row, doc_col, attended, stats, near, far, w_in, w_out,
    grad_qkv, grad_near, grad_far, near_part, far_part, *rest
):
    halves, (band, grad_band, grad_keys, grad_values, out_sum) = rest[:2], rest[2:]
    step = pl.program_id(0)
    half = length // 2
    heads_dev = table.shape[1]
    width = heads_dev * head_dim

    @pl.when(step == 0)
    def _():
        fill_band(band, table, strip, heads_dev, length)
        grad_band[...] = jnp.zeros_like(grad_band)
        grad_keys[...] = jnp.zeros_like(grad_keys)
        grad_values[...] = jnp.zeros_like(grad_values)
        out_sum[...] = jnp.zeros_like(out_sum)

    row = pl.multiple_of(step * half, half)
    branch = jnp.where(step == 0, near[...], far[...])
    merged = attended[...]
    grad_merged = contract(branch, w_out[...], 1, 1).astype(bf16)
    out_sum[...] += contract(merged, branch, 0, 0)
    products = grad_merged.astype(f32) * merged.astype(f32)
    queries = qkv[pl.ds(row, half), :width] * bf16(score_scale)
    blocks = half // tile
    for head in range(heads_dev):
        own = slice(head * head_dim, (head + 1) * head_dim)
        keys = qkv[:, width + own.start : width + own.stop]
        values = qkv[:, 2 * width + own.start : 2 * width + own.stop]
        upstream = grad_merged[:, own]
        raw_scores = contract(queries[:, own], keys, 1, 1)
        grad_weights = contract(upstream, values, 1, 1)
        delta = jnp.sum(products[:, own], axis=1, keepdims=True)
        weights_low, grads_low = [], []
        for block in range(blocks):
            lines = slice(block * tile, (block + 1) * tile)
            starts = band_starts(place, step * blocks + block, length, length // tile + 1)
            scores = raw_scores[lines] + jnp.concatenate(
                [band[head, :, pl.ds(start, tile)] for start in starts], axis=1
            )
            scores = jnp.where(doc_col[lines] == doc_row[...], scores, masked)
            weights = jnp.exp(scores - stats[lines, head : head + 1])
            grad_scores = weights * (grad_weights[lines] - delta[lines])
            for index, start in enumerate(starts):
                grad_band[head, :, pl.ds(start, tile)] += grad_scores[
                    :, index * tile : (index + 1) * tile
                ]
            weights_low.append(weights.astype(bf16))
            grads_low.append(grad_scores.astype(bf16))
        weights_low, grads_low = jnp.concatenate(weights_low), jnp.concatenate(grads_low)
        grad_values[:, own] += contract(weights_low, upstream, 0, 0)
        grad_keys[:, own] += contract(grads_low, queries[:, own], 0, 0)
        grad_qkv[pl.ds(row, half), own] = (
            contract(grads_low, keys, 1, 0) * score_scale
        ).astype(bf16)

    @pl.when(step == pl.num_programs(0) - 1)
    def _():
        grad_qkv[:, width : 2 * width] = grad_keys[...].astype(bf16)
        grad_qkv[:, 2 * width :] = grad_values[...].astype(bf16)
        far_part[...] = contract(grad_qkv[half:], w_in[...], 1, 1).astype(bf16)
        near_part[...] = contract(grad_qkv[:half], w_in[...], 1, 1)
        rows = width // 2
        for index, part in enumerate(halves):
            block = index ^ place[length // tile] % 2
            part[...] = out_sum[pl.ds(pl.multiple_of(block * rows, rows), rows)].astype(bf16)
        for head in range(heads_dev):
            grad_near[head] = grad_band[head, :, length - tile : length + 2 * tile]
            grad_far[head, 0] = jnp.full(
                (8, tile), jnp.sum(grad_band[head, :, : length - tile]), f32
            )
            grad_far[head, 1] = jnp.full(
                (8, tile), jnp.sum(grad_band[head, :, length + 2 * tile :]), f32
            )


def plane_attention_back(
    qkv, doc_row, doc_col, attended, stats, near, far, w_in, w_out, place, table, strip
):
    length, model_width = 2 * near.shape[0], near.shape[1]
    half = length // 2
    heads_dev = table.shape[1]
    width = heads_dev * head_dim
    shapes = [
        ((length, 3 * width), bf16),
        ((heads_dev, tile, 3 * tile), f32),
        ((heads_dev, 2, 8, tile), f32),
        ((length // 2, model_width), f32),
        ((length // 2, model_width), bf16),
    ] + [((width // 2, model_width), bf16)] * 2
    return pl.pallas_call(
        functools.partial(plane_attention_back_kernel, length),
        grid=(2,),
        in_specs=[
            pl.BlockSpec(memory_space=pltpu.SMEM),
            pl.BlockSpec(memory_space=pltpu.SMEM),
            whole(strip.shape),
            whole(qkv.shape),
            whole(doc_row.shape),
            pl.BlockSpec((half, 1), lambda step: (step, 0)),
            pl.BlockSpec((half, width), lambda step: (step, 0)),
            pl.BlockSpec((half, tile), lambda step: (step, 0)),
            whole((half, model_width)),
            whole((half, model_width)),
            whole(w_in.shape),
            whole(w_out.shape),
        ],
        out_specs=[whole(shape) for shape, _ in shapes],
        out_shape=[jax.ShapeDtypeStruct(shape, kind) for shape, kind in shapes],
        scratch_shapes=[
            pltpu.VMEM((heads_dev, tile, 2 * length), f32),
            pltpu.VMEM((heads_dev, tile, 2 * length), f32),
            pltpu.VMEM((length, width), f32),
            pltpu.VMEM((length, width), f32),
            pltpu.VMEM((width, model_width), f32),
        ],
        compiler_params=pltpu.CompilerParams(vmem_limit_bytes=32 * 2**20),
        cost_estimate=pl.CostEstimate(
            flops=10 * length * length * width + 10 * length * model_width * width,
            bytes_accessed=12 * 2**20,
            transcendentals=length * length * heads_dev,
        ),
    )(place, table, strip, qkv, doc_row, doc_col, attended, stats, near, far, w_in, w_out)


def gelu_and_slope(pre_act):
    size = jnp.abs(pre_act)
    gauss = jnp.exp(-0.5 * pre_act * pre_act)
    ratio = 1.0 / (1.0 + np.float32(0.3275911 * 0.5**0.5) * size)
    series = np.float32(1.061405429)
    for factor in (-1.453152027, 1.421413741, -0.284496736, 0.254829592):
        series = series * ratio + np.float32(factor)
    tail = 0.5 * series * ratio * gauss
    cumulative = jnp.where(pre_act < 0, tail, 1.0 - tail)
    slope = cumulative + pre_act * gauss * np.float32((2 * np.pi) ** -0.5)
    return pre_act * cumulative, slope


def ff_kernel(rows, pair, activated, slope, part):
    columns = rows.shape[1]
    value, gradient = gelu_and_slope(contract(rows[...], pair[:, :columns], 1, 1))
    activated[...] = value.astype(bf16)
    slope[...] = gradient.astype(bf16)
    part[...] = contract(activated[...], pair[:, columns:], 1, 0).astype(part.dtype)


def ff_first_kernel(rows, *refs):
    parts, (activated, slope, part, pair) = refs[:5], refs[5:]

    @pl.when(pl.program_id(0) == 0)
    def _():
        units, columns = parts[0].shape[0], rows.shape[1]
        for index, ref in enumerate(parts[:3]):
            pair[index * units : (index + 1) * units] = ref[...]
        pair[3 * units :, :columns] = parts[3][...]
        pair[3 * units :, columns:] = parts[4][...]

    ff_kernel(rows, pair, activated, slope, part)


def ff_back_kernel(rows, slope, pair, grad_pre, part):
    columns = rows.shape[1]
    grad_act = contract(rows[...], pair[:, columns:], 1, 1)
    grad_pre[...] = (grad_act * slope[...].astype(f32)).astype(bf16)
    part[...] = contract(grad_pre[...], pair[:, :columns], 1, 0).astype(part.dtype)


def by_rows(kernel, step_rows, row_operands, whole_operands, outs, whole_outs=()):
    rows = row_operands[0].shape[0]
    return pl.pallas_call(
        kernel,
        grid=(rows // step_rows,),
        in_specs=[
            pl.BlockSpec((step_rows, operand.shape[1]), lambda step: (step, 0))
            for operand in row_operands
        ]
        + [whole(operand.shape) for operand in whole_operands],
        out_specs=[pl.BlockSpec((step_rows, columns), lambda step: (step, 0)) for columns, _ in outs]
        + [whole(shape) for shape in whole_outs],
        out_shape=[jax.ShapeDtypeStruct((rows, columns), kind) for columns, kind in outs]
        + [jax.ShapeDtypeStruct(shape, bf16) for shape in whole_outs],
        compiler_params=pltpu.CompilerParams(vmem_limit_bytes=10 * 2**20),
        cost_estimate=pl.CostEstimate(
            flops=4 * rows * outs[0][0] * row_operands[0].shape[1],
            bytes_accessed=6 * 2**20,
            transcendentals=0,
        ),
    )(*row_operands, *whole_operands)


def ff_grads_kernel(
    pre_near, pre_far, act_near, act_far, normed_near, normed_far, low_near, low_far, *outs
):
    columns = normed_near.shape[1]
    units = outs[0].shape[0]
    up = (
        contract(pre_near[...], normed_near[...], 0, 0)
        + contract(pre_far[...], normed_far[...], 0, 0)
    ).astype(bf16)
    down = (
        contract(act_near[...], low_near[...], 0, 0) + contract(act_far[...], low_far[...], 0, 0)
    ).astype(bf16)

    @pl.when(pl.program_id(0) == 0)
    def _():
        for index in range(2):
            block = slice(index * units, (index + 1) * units)
            outs[index][:, :columns] = up[block]
            outs[index][:, columns:] = down[block]

    @pl.when(pl.program_id(0) == 1)
    def _():
        outs[2][:, :columns] = up[:units]
        outs[2][:, columns:] = down[:units]
        outs[3][...] = up[units:]
        outs[4][...] = down[units:]


def ff_grads(pre, act, normed, low):
    rows, hidden_units = pre[0].shape
    columns = normed[0].shape[1]
    shapes = [(hidden_units // 4, 2 * columns)] * 3 + [(hidden_units // 4, columns)] * 2
    return pl.pallas_call(
        ff_grads_kernel,
        grid=(2,),
        in_specs=[pl.BlockSpec((rows, hidden_units // 2), lambda step: (0, step))] * 4
        + [whole((rows, columns))] * 4,
        out_specs=[whole(shape) for shape in shapes],
        out_shape=[jax.ShapeDtypeStruct(shape, bf16) for shape in shapes],
        compiler_params=pltpu.CompilerParams(vmem_limit_bytes=14 * 2**20),
        cost_estimate=pl.CostEstimate(
            flops=8 * rows * hidden_units * columns, bytes_accessed=8 * 2**20, transcendentals=0
        ),
    )(*pre, *act, *normed, *low)


def in_grads_kernel(place, near, far, grad_qkv, *refs):
    ends, outs, (total, extra) = refs[:-6], refs[-6:-2], refs[-2:]
    half = near.shape[0]
    columns = grad_qkv.shape[1]
    total[:, :columns] = (
        contract(near[...], grad_qkv[:half], 0, 0) + contract(far[...], grad_qkv[half:], 0, 0)
    ).astype(bf16)
    rows = outs[0].shape[0] // 8
    if ends:
        gain_0, gain_1, table_0, table_1 = ends
        lines = lax.broadcasted_iota(jnp.int32, (tile, gain_0.shape[1]), 0)
        gains = jnp.where(lines == 0, gain_0[...], jnp.where(lines == 1, gain_1[...], 0.0))
        extra[...] = jnp.transpose(gains)
        table = table_0[...] + table_1[...]
        buckets = table.shape[0] // 8
        blank = jnp.zeros((8 - buckets, tile), f32)
        for block in range(8):
            row = pl.multiple_of((place[0] // 2 * 8 + block) * rows, rows)
            extra[pl.ds(row, 8)] += jnp.concatenate(
                [table[block * buckets : (block + 1) * buckets], blank]
            )
        total[:, columns:] = extra[...].astype(bf16)
    for out, offset in zip(outs, (0, 3, 1, 2)):
        plane = (place[8] + offset) % 4
        for index in range(8):
            owner = place[index]
            row = row_of(owner // 2, plane, owner % 2, rows)
            out[index * rows : (index + 1) * rows] = total[pl.ds(row, rows)]


def in_grads(place, near, far, grad_qkv, *ends):
    columns = grad_qkv.shape[1] + (tile if ends else 0)
    shape = (near.shape[1] // 4, columns)
    return pl.pallas_call(
        in_grads_kernel,
        in_specs=[pl.BlockSpec(memory_space=pltpu.SMEM)]
        + [pl.BlockSpec(memory_space=pltpu.VMEM)] * (3 + len(ends)),
        out_specs=[pl.BlockSpec(memory_space=pltpu.VMEM)] * 4,
        out_shape=[jax.ShapeDtypeStruct(shape, bf16)] * 4,
        scratch_shapes=[
            pltpu.VMEM((near.shape[1], columns), bf16),
            pltpu.VMEM((near.shape[1], tile), f32),
        ],
        compiler_params=pltpu.CompilerParams(vmem_limit_bytes=14 * 2**20),
        cost_estimate=pl.CostEstimate(
            flops=4 * near.shape[0] * near.shape[1] * columns,
            bytes_accessed=4 * 2**20,
            transcendentals=0,
        ),
    )(place, near, far, grad_qkv, *ends)


def add_in_kernel(own, lower, upper, opposite, near, far):
    total = sum_of_four([own, lower, upper, opposite]).astype(bf16)
    half = near.shape[0]
    near[...] = total[:half]
    far[...] = total[half:]


def combine_kernel(near_part, arrived, own, x_part, y_part, xy_part):
    rows = own.shape[0]
    own[...] = near_part[:rows] + arrived[:rows].astype(f32)
    for bits, out in ((1, x_part), (2, y_part), (3, xy_part)):
        block = slice(bits * rows, (bits + 1) * rows)
        out[...] = (near_part[block] + arrived[block].astype(f32)).astype(bf16)


def added(own, x_part, y_part, xy_part):
    return (own[...] + x_part[...].astype(f32)) + (
        y_part[...].astype(f32) + xy_part[...].astype(f32)
    )


def close_kernel(kept, own, x_part, y_part, xy_part, hidden, units):
    total = kept[...] + added(own, x_part, y_part, xy_part)
    hidden[...] = total
    units[...] = (total * inverse_rms(total)).astype(bf16)


def close_gain_kernel(kept, own, x_part, y_part, xy_part, gain, hidden, normed):
    total = kept[...] + added(own, x_part, y_part, xy_part)
    hidden[...] = total
    normed[...] = (total * inverse_rms(total) * gain[...]).astype(bf16)


def widen_kernel(low, out):
    out[...] = low[...].astype(f32)


def last_kernel(kept, own, x_part, y_part, xy_part, hidden):
    hidden[...] = (kept[...] + added(own, x_part, y_part, xy_part)).astype(bf16)


def middle_back_kernel(
    upstream, own, x_part, y_part, xy_part, middle, gain, grad_middle, branch, grad_gain
):
    grad_normed = added(own, x_part, y_part, xy_part)
    inverse = inverse_rms(middle[...])
    grad_gain[...] = jnp.sum(grad_normed * middle[...] * inverse, axis=0, keepdims=True)
    total = upstream[...].astype(f32) + unit_norm_back(
        middle[...], inverse, grad_normed * gain[...]
    )
    grad_middle[...] = total
    branch[...] = total.astype(bf16)


def layer_back_kernel(grad_middle, own, x_part, y_part, xy_part, hidden, upstream, low):
    total = grad_middle[...] + unit_norm_back(
        hidden[...], inverse_rms(hidden[...]), added(own, x_part, y_part, xy_part)
    )
    upstream[...] = total
    low[...] = total.astype(bf16)


def pair_kernel(axis, near, arrived, *outs):
    rows = near.shape[0] // len(outs)
    for index, out in enumerate(outs):
        block = slice(index * rows, (index + 1) * rows)
        if axis == 0:
            out[:rows] = near[block]
            out[rows:] = arrived[block]
        else:
            columns = near.shape[1]
            out[:, :columns] = near[block]
            out[:, columns:] = arrived[block]


def unit_kernel(tokens, hidden, units):
    total = tokens[...].astype(f32)
    hidden[...] = total
    units[...] = (total * inverse_rms(total)).astype(bf16)


def finish_in_kernel(place, *refs):
    chips, (attn_in, gains, grad_in, grad_gain, ends) = refs[:8], refs[8:]
    rows = attn_in.shape[1]
    width = tile
    members = attn_in.shape[2] // (3 * width)
    ends[...] = jnp.zeros_like(ends)
    for layer_id in range(2):
        row_dot = jnp.zeros((rows, 1), f32)
        for index in range(members):
            member = place[index]
            chip = chips[4 * layer_id + index % 4]
            half = chip.shape[1] // 2
            total = chip[:, index // 4 * half : (index // 4 + 1) * half].astype(f32)
            if layer_id == 0:
                ends[...] += total[:, 3 * width :]
            for part in range(3):
                block = total[:, part * width : (part + 1) * width]
                columns = pl.ds(pl.multiple_of((part * members + member) * width, width), width)
                grad_in[layer_id, :, columns] = block * gains[layer_id]
                row_dot = row_dot + jnp.sum(
                    block * attn_in[layer_id, :, columns].astype(f32), axis=1, keepdims=True
                )
        grad_gain[layer_id] = jnp.concatenate(
            [row_dot, ends[:, layer_id : layer_id + 1]], axis=1
        )


def sum_of_four(parts):
    return (parts[0][...].astype(f32) + parts[1][...].astype(f32)) + (
        parts[2][...].astype(f32) + parts[3][...].astype(f32)
    )


def finish_ff_kernel(*refs):
    count = (len(refs) - 3) // 2
    sources, grads, held, done = refs[:count], refs[count : count + 2], refs[count + 2 : -1], refs[-1]
    copies = [
        pltpu.make_async_copy(source, target, done.at[index])
        for index, (source, target) in enumerate(zip(sources, held))
    ]
    for copy in copies:
        copy.start()
    for copy in copies:
        copy.wait()
    refs = held
    columns = grads[0].shape[2]
    for layer_id in range(grads[0].shape[0]):
        parts = refs[5 * layer_id : 5 * layer_id + 5]
        for side, out in enumerate(grads):
            halves = [part.at[:, side * columns : (side + 1) * columns] for part in parts[:3]]
            out[layer_id] = sum_of_four(halves + [parts[3 + side]])


def finish_ff(grads, shape):
    return pl.pallas_call(
        finish_ff_kernel,
        in_specs=[pl.BlockSpec(memory_space=pl.ANY)] * len(grads),
        out_specs=[pl.BlockSpec(memory_space=pltpu.VMEM)] * 2,
        out_shape=[jax.ShapeDtypeStruct(shape, f32)] * 2,
        scratch_shapes=[pltpu.VMEM(grad.shape, bf16) for grad in grads]
        + [pltpu.SemaphoreType.DMA((len(grads),))],
        compiler_params=pltpu.CompilerParams(vmem_limit_bytes=14 * 2**20),
    )(*grads)


def add_out_kernel(place, *refs):
    parts, (own, other) = refs[:-2], refs[-2:]
    for layer_id in range(own.shape[0]):
        total = parts[2 * layer_id][...].astype(f32) + parts[2 * layer_id + 1][...].astype(f32)
        rows = total.shape[0] // 2
        second = place[0] % 2 == 1
        own[layer_id] = jnp.where(second, total[rows:], total[:rows])
        other[layer_id] = jnp.where(second, total[:rows], total[rows:]).astype(bf16)


def finish_out_kernel(own, arrived, out):
    out[...] = own[...] + arrived[...].astype(f32)


def inverse_rms(hidden):
    return lax.rsqrt(jnp.mean(hidden * hidden, axis=-1, keepdims=True) + epsilon)


def prepare(bias_table, first_head, heads_dev):
    table = lax.dynamic_slice_in_dim(bias_table, first_head, heads_dev, 1)
    (near,) = call(near_kernel, [((heads_dev, tile, 3 * tile), f32)], table, smem=1)
    return table, near


def bucket_grads(first_lane, grads, bucket_count):
    (total,) = call(bucket_kernel, [((bucket_count, tile), f32)], first_lane, *grads, smem=1)
    return total


def gelu_parts(pre_act):
    cumulative = 0.5 * (1.0 + lax.erf(pre_act * np.float32(0.5**0.5)))
    slope = cumulative + pre_act * jnp.exp(-0.5 * pre_act * pre_act) * np.float32(
        (2 * np.pi) ** -0.5
    )
    return (pre_act * cumulative).astype(bf16), slope


def unit_norm_back(hidden, inverse, grad_unit):
    unit = hidden * inverse
    return inverse * (grad_unit - unit * jnp.mean(grad_unit * unit, axis=-1, keepdims=True))


def gather_rows(block, axes):
    return lax.all_gather(block, axes, axis=0, tiled=True)


def toggle(array, axis, bits):
    return lax.ppermute(array, axis, [(i, i ^ bits) for i in range(lax.axis_size(axis))])


def shift(array, by):
    planes = lax.axis_size("z")
    return lax.ppermute(array, "z", [(i, (i + by) % planes) for i in range(planes)])


def plane_gather(block, *holds):
    near = jnp.concatenate([block] + [toggle(block, "head", bits) for bits in (1, 2, 3)])
    near, *holds = tie(near, *holds)
    return (near, toggle(near, "core", 1), *holds)


def plane_scatter(near_part, far_part):
    rows, columns = near_part.shape[0] // 4, near_part.shape[1]
    own, *others = call(
        combine_kernel,
        [((rows, columns), f32)] + [((rows, columns), bf16)] * 3,
        near_part,
        toggle(far_part, "core", 1),
    )
    shares = [own] + [toggle(other, "head", bits) for bits, other in zip((1, 2, 3), others)]
    return shares, own


def tie(*arrays):
    return lax.optimization_barrier(arrays)


def after(array, other):
    return lax.optimization_barrier((array, other))[0]


def scatter_sum(partial, axes, members):
    blocks = partial.astype(bf16).reshape(members, -1, partial.shape[1])
    return jnp.sum(lax.all_to_all(blocks, axes, 0, 0, tiled=True).astype(f32), axis=0)


def local_general(tokens, doc_start, bias_table, attn_in, attn_out, ff_in, ff_out, gains, cotangent):
    heads_n, z_n, core_n = (lax.axis_size(axis) for axis in everyone)
    devices = heads_n * z_n * core_n
    group, spare = ("z", "core"), "head"
    ff_group, ff_spare, ff_members = ("head", "core"), "z", heads_n * core_n
    blocks = z_n * core_n
    block_rows, model_width = tokens.shape[1:]
    layer_count, weight_rows = attn_in.shape[:2]
    length = block_rows * blocks
    heads_all = bias_table.shape[1]
    member = lax.axis_index("z") * core_n + lax.axis_index("core")
    heads_dev = max(1, heads_all // blocks)
    head_groups = heads_all // heads_dev
    split = blocks // head_groups
    head_group, query_part = member // split, member % split
    query_rows = length // split
    width = heads_dev * head_dim
    first = (query_part * (query_rows // tile)).astype(jnp.int32).reshape(1)
    place = jnp.arange(length // tile, dtype=jnp.int32)
    out_row = head_group * width

    def swap(array):
        return lax.all_to_all(array, everyone, 0, 0, tiled=True)

    starts = jnp.broadcast_to(
        doc_start.astype(f32)[:, None], (heads_n, blocks, block_rows)
    ).reshape(devices, block_rows)
    ff_gains = gains[:, :, 1].astype(f32).reshape(1, -1)
    small = swap(
        jnp.concatenate(
            [starts, jnp.broadcast_to(ff_gains, (devices, layer_count * weight_rows))], axis=1
        )
    )
    doc_row = small[:blocks, :block_rows].reshape(1, length)
    doc_col = lax.dynamic_slice_in_dim(
        doc_row.reshape(length, 1), query_part * query_rows, query_rows, 0
    )
    gain_ff = jnp.transpose(
        small[:, block_rows:].reshape(devices, layer_count, weight_rows), (1, 0, 2)
    ).reshape(layer_count, 1, model_width)
    table, near = prepare(bias_table, head_group * heads_dev, heads_dev)

    gain_attn = gains[:, :, 0].astype(f32)[:, :, None]
    own_in = attn_in.astype(f32)

    def fetch_in(layer_id):
        scaled = (own_in[layer_id] * gain_attn[layer_id]).astype(bf16)
        columns = jnp.transpose(
            scaled.reshape(weight_rows, 3, head_groups, width), (2, 0, 1, 3)
        ).reshape(head_groups, weight_rows, 3 * width)
        columns = jnp.repeat(columns, split, axis=0)
        columns = jnp.broadcast_to(columns[None], (heads_n, *columns.shape))
        return swap(columns.reshape(devices, weight_rows, 3 * width)).reshape(
            model_width, 3 * width
        )

    def fetch_ff(layer_id):
        pair = jnp.concatenate([ff_in[layer_id], ff_out[layer_id]], axis=1)
        pair = gather_rows(pair, ff_spare)
        return pair[:, :model_width], pair[:, model_width:]

    hidden, upstream = tokens[0].astype(f32), cotangent[0]
    weights_in = [fetch_in(layer_id) for layer_id in range(layer_count)]
    weights_out = lax.dynamic_slice_in_dim(
        lax.all_gather(attn_out, everyone, axis=1, tiled=True), out_row, width, 1
    )
    weights_ff = [fetch_ff(layer_id) for layer_id in range(layer_count)]

    records = []
    for layer_id in range(layer_count):
        w_in, w_out, (w_up, w_down) = (
            weights_in[layer_id], weights_out[layer_id], weights_ff[layer_id],
        )
        inverse = inverse_rms(hidden)
        units = gather_rows((hidden * inverse).astype(bf16), group)
        qkv = jnp.dot(units, w_in, preferred_element_type=f32).astype(bf16)
        attended, _, stats = attention(
            qkv, doc_row, doc_col, first, place, table, near, query_rows
        )
        mixed = jnp.dot(attended, w_out, preferred_element_type=f32)
        if split > 1:
            mixed = lax.dynamic_update_slice_in_dim(
                jnp.zeros((length, model_width), f32), mixed, query_part * query_rows, 0
            )
        middle = hidden + scatter_sum(mixed, group, blocks)
        inverse_ff = inverse_rms(middle)
        normed_ff = gather_rows((middle * inverse_ff * gain_ff[layer_id]).astype(bf16), ff_group)
        activated, slope = gelu_parts(contract(normed_ff, w_up, 1, 1))
        ff_result = jnp.dot(activated, w_down, preferred_element_type=f32)
        records.append(
            (hidden, inverse, units, qkv, attended, stats, middle, inverse_ff, normed_ff,
             activated, slope)
        )
        hidden = middle + scatter_sum(ff_result, ff_group, ff_members)
    output = hidden

    grads_ff, grads_in, grads_out, grads_gain_ff, grads_table = (
        [None] * layer_count for _ in range(5)
    )
    for layer_id in reversed(range(layer_count)):
        w_in, w_out, (w_up, w_down) = (
            weights_in[layer_id], weights_out[layer_id], weights_ff[layer_id],
        )
        (hidden, inverse, units, qkv, attended, stats, middle, inverse_ff, normed_ff,
         activated, slope) = records[layer_id]
        grad_low = gather_rows(upstream.astype(bf16), ff_group)
        grad_pre = (contract(grad_low, w_down, 1, 1) * slope).astype(bf16)
        grad_normed = scatter_sum(
            jnp.dot(grad_pre, w_up, preferred_element_type=f32), ff_group, ff_members
        )
        grad_pair = jnp.concatenate(
            [contract(grad_pre, normed_ff, 0, 0), contract(activated, grad_low, 0, 0)], axis=1
        ).astype(bf16)
        grads_ff[layer_id] = lax.psum_scatter(
            grad_pair, ff_spare, scatter_dimension=0, tiled=True
        ).astype(f32)
        grads_gain_ff[layer_id] = jnp.sum(grad_normed * middle * inverse_ff, axis=0)
        grad_middle = upstream + unit_norm_back(
            middle, inverse_ff, grad_normed * gain_ff[layer_id]
        )
        branch = gather_rows(grad_middle.astype(bf16), group)
        if split > 1:
            branch = lax.dynamic_slice_in_dim(branch, query_part * query_rows, query_rows, 0)
        grad_attended = contract(branch, w_out, 1, 1).astype(bf16)
        grad_qkv, grad_near, grad_far = attention_back(
            qkv, doc_row, doc_col, attended, grad_attended, stats, first, place, table, near, split
        )
        grads_table[layer_id] = (grad_near, grad_far)
        grad_units = scatter_sum(contract(grad_qkv, w_in, 1, 1), group, blocks)
        upstream = grad_middle + unit_norm_back(hidden, inverse, grad_units)
        grad_out = lax.dynamic_update_slice_in_dim(
            jnp.zeros((model_width, model_width), bf16),
            contract(attended, branch, 0, 0).astype(bf16),
            out_row,
            0,
        )
        grads_out[layer_id] = lax.psum_scatter(
            grad_out, everyone, scatter_dimension=0, tiled=True
        ).astype(f32)
        grads_in[layer_id] = contract(units, grad_qkv, 0, 0).astype(bf16)

    bucket_count = table.shape[0]
    grad_table = sum(
        bucket_grads(jnp.zeros((1,), jnp.int32), entry, bucket_count) for entry in grads_table
    )[:, :heads_dev]
    grad_table = lax.dynamic_update_slice_in_dim(
        jnp.zeros((bucket_count, heads_all), f32), grad_table, head_group * heads_dev, 1
    )
    grad_table = jnp.transpose(
        grad_table.reshape(blocks, bucket_count // blocks, heads_n, heads_all // heads_n),
        (2, 0, 1, 3),
    ).reshape(devices, -1)
    grad_gain_ff = jnp.transpose(
        jnp.stack(grads_gain_ff).reshape(layer_count, devices, weight_rows), (1, 0, 2)
    ).reshape(devices, -1)
    ends = jnp.sum(swap(jnp.concatenate([grad_gain_ff, grad_table], axis=1)), axis=0)
    grad_gain_ff = ends[: layer_count * weight_rows].reshape(layer_count, weight_rows)
    grad_bias_table = ends[layer_count * weight_rows :].reshape(
        bucket_count // blocks, heads_all // heads_n
    )
    grads_attn_in, grads_gains = [], []
    for layer_id in range(layer_count):
        parts = swap(grads_in[layer_id].reshape(devices, weight_rows, 3 * width)).astype(f32)
        parts = jnp.sum(parts.reshape(heads_n, blocks, weight_rows, 3 * width), axis=0)
        parts = jnp.sum(parts.reshape(head_groups, split, weight_rows, 3, width), axis=1)
        unit_grad = jnp.transpose(parts, (1, 2, 0, 3)).reshape(weight_rows, 3 * model_width)
        grads_attn_in.append(unit_grad * gain_attn[layer_id])
        grads_gains.append(
            jnp.stack(
                [jnp.sum(unit_grad * own_in[layer_id], axis=1), grad_gain_ff[layer_id]], axis=1
            )
        )
    return (
        output[None],
        upstream[None],
        jnp.stack(grads_attn_in),
        jnp.stack(grads_out),
        jnp.stack([entry[:, :model_width] for entry in grads_ff]),
        jnp.stack([entry[:, model_width:] for entry in grads_ff]),
        jnp.stack(grads_gains),
        grad_bias_table,
    )


def local_plane(tokens, doc_start, bias_table, attn_in, attn_out, ff_in, ff_out, gains, cotangent):
    heads_n, z_n, core_n = (lax.axis_size(axis) for axis in everyone)
    devices = heads_n * z_n * core_n
    at_head, at_z, at_core = (lax.axis_index(axis) for axis in everyone)
    members = heads_n * core_n
    block_rows, model_width = tokens.shape[1:]
    layer_count, weight_rows = attn_in.shape[:2]
    length = block_rows * members
    heads_all = bias_table.shape[1]
    heads_dev = heads_all // members
    width = heads_dev * head_dim
    member = at_head * core_n + at_core
    everywhere = [(h, z, c) for h in range(heads_n) for z in range(z_n) for c in range(core_n)]

    def swapped(bits):
        return bits % 2 * 2 + bits // 2

    def device(h, z, c):
        return (h * z_n + z) * core_n + c

    turn = [(device(h, z, c), device(h ^ swapped(z), h, c)) for h, z, c in everywhere]
    plane_turn = [(device(h, z, c), device(h ^ swapped(z), z, c)) for h, z, c in everywhere]
    line_turn = [(device(h, z, c), device(h, h ^ swapped(z), c)) for h, z, c in everywhere]
    line_back = [(target, source) for source, target in line_turn]
    place = jnp.stack(
        [
            (at_head ^ bits) * core_n + (at_core ^ other)
            for other in range(core_n)
            for bits in range(heads_n)
        ]
        + [at_z]
        + [
            swapped(at_head ^ bits ^ at_z) * core_n + (at_core ^ other)
            for other in range(core_n)
            for bits in range(heads_n)
        ]
    ).astype(jnp.int32)

    def relay(array):
        return lax.ppermute(array, everyone, turn)

    def turn_in_plane(array):
        return lax.ppermute(array, everyone, plane_turn)

    def turn_in_line(array, turns):
        return lax.ppermute(array, everyone, turns)

    def swap(array):
        return lax.all_to_all(array, everyone, 0, 0, tiled=True)

    row_shape = (block_rows, model_width)
    gain_attn = gains[:, :, 0].astype(f32)[:, :, None]
    near_share, far_share = call(
        share_in_kernel,
        [((members // 2 * layer_count * weight_rows, 3 * width), bf16)] * 2,
        place,
        attn_in,
        gain_attn,
        smem=1,
    )

    half_turns = [
        [
            (z * core_n + c, (2 * c + (a ^ z % 2)) * core_n + z // 2)
            for z in range(z_n)
            for c in range(core_n)
        ]
        for a in range(2)
    ]

    def fetch_out(layer_id, hold):
        own = attn_out[layer_id]
        other = toggle(own, "core", 1)
        head = jnp.where(
            at_core == 0, jnp.concatenate([own, other]), jnp.concatenate([other, own])
        )
        head = after(head, hold)
        return [
            lax.ppermute(head, ("z", "core"), [(holder, user) for user, holder in turns])
            for turns in half_turns
        ]

    def owners_halves(halves):
        return [
            lax.ppermute(half, ("z", "core"), turns) for half, turns in zip(halves, half_turns)
        ]

    def pair_chips(near, arrived, axis):
        rows, columns = near.shape[0] // 4, near.shape[1]
        shape = (2 * rows, columns) if axis == 0 else (rows, 2 * columns)
        return call(functools.partial(pair_kernel, axis), [(shape, bf16)] * 4, near, arrived)

    def share_chips(blocks):
        return [blocks[0]] + [toggle(blocks[bits], "head", bits) for bits in (1, 2, 3)]

    units_shape = [(row_shape, f32), (row_shape, bf16)]

    starts = jnp.broadcast_to(
        doc_start.astype(f32)[None, :, None], (heads_n, z_n, core_n, block_rows)
    )
    ff_gains = gains[:, :, 1].astype(f32).reshape(1, -1)
    small = jnp.concatenate(
        [
            starts.reshape(devices, block_rows),
            jnp.broadcast_to(ff_gains, (devices, layer_count * weight_rows)),
        ],
        axis=1,
    )
    table, strip = prepare(bias_table, member * heads_dev, heads_dev)
    hidden = relay(tokens[0])
    hidden, shares, halves, small = tie(
        hidden,
        share_chips(pair_chips(near_share, toggle(far_share, "core", 1), 0)),
        fetch_out(0, near_share),
        swap(after(small, near_share)),
    )
    hidden, unit_rows = call(unit_kernel, units_shape, hidden)
    doc_row = small[:members, :block_rows].reshape(2, 2, core_n, block_rows)
    at_block = swapped(at_head ^ at_z)
    for axis, bit in ((0, at_block // 2), (1, at_block % 2), (2, at_core)):
        doc_row = jnp.where(bit == 1, jnp.flip(doc_row, axis), doc_row)
    doc_row = jnp.transpose(doc_row, (2, 1, 0, 3)).reshape(1, length)
    doc_col = doc_row.reshape(length, 1)
    gain_ff = jnp.transpose(
        small[:, block_rows:].reshape(devices, layer_count, weight_rows), (1, 0, 2)
    ).reshape(layer_count, 1, model_width)

    def round_planes(array, by, hold):
        return shift(after(array, hold), by)

    ff_pairs = [
        jnp.concatenate([ff_in[layer_id], ff_out[layer_id]], axis=1) for layer_id in range(layer_count)
    ]

    def ff_both(kernel, row_operands, pair, columns):
        return zip(
            *(
                by_rows(
                    kernel,
                    256,
                    operands,
                    [pair],
                    [(pair.shape[0], bf16)] * columns + [(model_width, kind)],
                )
                for operands, kind in zip(zip(*row_operands), (f32, bf16))
            )
        )

    def ff_forward(normed, *parts):
        units = 4 * parts[0].shape[0]
        outs = [(units, bf16), (units, bf16)]
        *near, pair = by_rows(
            ff_first_kernel,
            256,
            [normed[0]],
            parts,
            outs + [(model_width, f32)],
            [(units, 2 * model_width)],
        )
        far = by_rows(ff_kernel, 256, [normed[1]], [pair], outs + [(model_width, bf16)])
        return pair, *zip(near, far)

    def ff_backward(low, slopes, pair):
        return ff_both(ff_back_kernel, [low, slopes], pair, 1)

    def assemble_in(share, lower, upper, opposite):
        return call(
            assemble_in_kernel,
            [((model_width, 3 * width), bf16)],
            place,
            share,
            lower,
            upper,
            opposite,
            smem=1,
        )[0]

    share, later_share = call(
        join_kernel, [((members * weight_rows, 3 * width), bf16)] * layer_count, *shares
    )
    near, far, lower, upper, opposite, cotangent_low, strip, doc_row, doc_col, gain_ff, *ff_pairs = plane_gather(
        unit_rows,
        shift(share, 1),
        shift(share, -1),
        shift(share, 2),
        cotangent[0].astype(bf16),
        strip,
        doc_row,
        doc_col,
        gain_ff,
        *ff_pairs,
    )
    w_in = assemble_in(share, lower, upper, opposite)
    units = (near, far)
    w_out, qkv, attended, stats, *parts = plane_attention(
        *units, w_in, halves, doc_row, doc_col, place, table, strip
    )
    parts, lower, upper, cotangent_low = tie(
        parts,
        round_planes(ff_pairs[0], 1, near),
        round_planes(ff_pairs[0], -1, near),
        turn_in_plane(after(cotangent_low, near)),
    )
    parts, own = plane_scatter(*parts)
    parts, opposite_in = tie(parts, round_planes(ff_in[0], 2, own))
    middle, normed_rows = call(close_gain_kernel, units_shape, hidden, *parts, gain_ff[0])
    *normed, opposite_out = plane_gather(normed_rows, round_planes(ff_out[0], 2, normed_rows))
    pair, acts, slopes, parts = ff_forward(
        normed, ff_pairs[0], lower, upper, opposite_in, opposite_out
    )
    records = [
        (hidden, units, w_in, w_out, pair, qkv, attended, stats, middle, normed, acts, slopes)
    ]
    parts, lower, upper = tie(
        parts,
        round_planes(later_share, 1, normed[0]),
        round_planes(later_share, -1, normed[0]),
    )
    parts, own = plane_scatter(*parts)
    parts, opposite, upstream = tie(
        parts, round_planes(later_share, 2, own), turn_in_line(after(cotangent_low, own), line_turn)
    )
    shares = [later_share, lower, upper, opposite]
    hidden, unit_rows = call(close_kernel, units_shape, middle, *parts)

    near, far, lower, halves, w_in = plane_gather(
        unit_rows,
        round_planes(ff_pairs[1], 1, unit_rows),
        fetch_out(1, unit_rows),
        assemble_in(*after(shares, unit_rows)),
    )
    units = (near, far)
    w_out, qkv, attended, stats, *parts = plane_attention(
        *units, w_in, halves, doc_row, doc_col, place, table, strip
    )
    low = plane_gather(after(upstream, far))
    parts, near_low, upper = tie(parts, low[0], round_planes(ff_pairs[1], -1, far))
    low = (near_low, low[1])
    parts, own = plane_scatter(*parts)
    parts, opposite_in = tie(parts, round_planes(ff_in[1], 2, own))
    middle, normed_rows = call(close_gain_kernel, units_shape, hidden, *parts, gain_ff[1])
    *normed, opposite_out = plane_gather(normed_rows, round_planes(ff_out[1], 2, normed_rows))
    pair, acts, slopes, last_parts = ff_forward(
        normed, ff_pairs[1], lower, upper, opposite_in, opposite_out
    )
    records.append(
        (hidden, units, w_in, w_out, pair, qkv, attended, stats, middle, normed, acts, slopes)
    )

    def back_to_middle(parts, upstream, middle, gain):
        return call(
            middle_back_kernel, units_shape + [((1, model_width), f32)], upstream, *parts, middle, gain
        )

    def attention_grads(record, branch):
        _, _, w_in, w_out, _, qkv, attended, stats, *_ = record
        grad_qkv, grad_near, grad_far, near_part, far_part, *halves = plane_attention_back(
            qkv, doc_row, doc_col, attended, stats, *branch, w_in, w_out, place, table, strip
        )
        return grad_qkv, (grad_near, grad_far), (near_part, far_part), halves

    def table_grads(near_and_far):
        return bucket_grads(at_core.reshape(1) * heads_dev + 8, near_and_far, table.shape[0])

    record = records[1]
    hidden, units, _, _, pair, *_, middle, normed, acts, slopes = record
    pres, parts = ff_backward(low, slopes, pair)
    parts, own = plane_scatter(*parts)
    planes = ff_grads(after(pres, own), acts, normed, low)
    parts, ff_lower = tie(parts, shift(planes[1], -1))
    last_parts, _ = plane_scatter(*after(last_parts, parts))
    grad_middle, branch_rows, gain_1 = back_to_middle(parts, upstream, middle, gain_ff[1])
    *branch, ff_upper = plane_gather(branch_rows, round_planes(planes[2], 1, branch_rows))
    grad_qkv, strips_1, parts, halves_1 = attention_grads(record, branch)
    parts, last_parts, opposite_up = tie(
        parts, last_parts, round_planes(planes[3], 2, branch[1])
    )
    parts, own = plane_scatter(*parts)
    parts, opposite_down, output = tie(
        parts,
        round_planes(planes[4], 2, own),
        call(last_kernel, [(row_shape, bf16)], middle, *after(last_parts, own))[0],
    )
    grads_ff = [planes[0], ff_lower, ff_upper, opposite_up, opposite_down]
    upstream, low_rows = call(layer_back_kernel, units_shape, grad_middle, *parts, hidden)

    record = records[0]
    hidden, units, _, _, pair, *_, middle, normed, acts, slopes = record
    grad_in = in_grads(place, *records[1][1], after(grad_qkv, low_rows))
    *low, in_opposite, in_upper, table_1 = plane_gather(
        low_rows, shift(grad_in[3], 2), shift(grad_in[2], 1), table_grads(after(strips_1, low_rows))
    )
    pres, parts = ff_backward(low, slopes, pair)
    parts, in_lower = tie(parts, round_planes(grad_in[1], -1, low[0]))
    parts, own = plane_scatter(*parts)
    planes = ff_grads(after(pres, own), acts, normed, low)
    near_in, far_in = call(
        add_in_kernel,
        [((members // 2 * weight_rows, 3 * width), bf16)] * 2,
        *after([grad_in[0], in_lower, in_upper, in_opposite], own),
    )
    parts, ff_lower, first_half, arrived = tie(
        parts,
        shift(planes[1], -1),
        owners_halves(after(halves_1, own))[0],
        toggle(far_in, "core", 1),
    )
    grad_middle, branch_rows, gain_0 = back_to_middle(parts, upstream, middle, gain_ff[0])
    *branch, ff_upper, second_half, shares_1 = plane_gather(
        branch_rows,
        round_planes(planes[2], 1, branch_rows),
        owners_halves(after(halves_1, branch_rows))[1],
        pair_chips(near_in, after(arrived, branch_rows), 1),
    )
    halves_1 = [first_half, second_half]
    grad_qkv, strips_0, parts, halves_0 = attention_grads(record, branch)
    parts, shares_1, output, opposite_up = tie(
        parts,
        share_chips(after(shares_1, branch[1])), turn_in_line(after(output, branch[1]), line_back), round_planes(planes[3], 2, branch[1])
    )
    parts, own = plane_scatter(*parts)
    table_0 = table_grads(after(strips_0, own))
    grad_in = in_grads(
        place, *units, after(grad_qkv, own), gain_0, gain_1, table_0, table_1
    )
    parts, in_opposite, halves_0 = tie(
        parts, shift(grad_in[3], 2), owners_halves(after(halves_0, own))
    )
    upstream, low_rows = call(layer_back_kernel, units_shape, grad_middle, *parts, hidden)
    in_lower = round_planes(grad_in[1], -1, low_rows)
    in_upper = round_planes(grad_in[2], 1, low_rows)
    line = turn_in_line(low_rows, line_back)
    near_in, far_in = call(
        add_in_kernel,
        [((members // 2 * weight_rows, 3 * width + tile), bf16)] * 2,
        grad_in[0],
        in_lower,
        in_upper,
        in_opposite,
    )
    arrived = toggle(far_in, "core", 1)
    shares_0 = share_chips(pair_chips(near_in, arrived, 1))
    opposite_down = round_planes(planes[4], 2, near_in)
    grad_tokens = turn_in_plane(after(line, shares_0[1:]))
    output = turn_in_plane(after(output, shares_0[1:]))
    (output,) = call(widen_kernel, [(row_shape, f32)], output)
    (grad_tokens,) = call(widen_kernel, [(row_shape, f32)], grad_tokens)
    grads_ff = [planes[0], ff_lower, ff_upper, opposite_up, opposite_down] + grads_ff
    grad_up, grad_down = finish_ff(after(grads_ff, shares_0[1:]), ff_in.shape)
    own_out, other_out = call(
        add_out_kernel,
        [(attn_out.shape, f32), (attn_out.shape, bf16)],
        place,
        *after(halves_0 + halves_1, shares_0[1:]),
        smem=1,
    )
    (grad_attn_out,) = call(
        finish_out_kernel, [(attn_out.shape, f32)], own_out, toggle(other_out, "core", 1)
    )
    own_buckets = table.shape[0] // (z_n * core_n)
    grad_attn_in, grad_gains, ends = call(
        finish_in_kernel,
        [(attn_in.shape, f32), (gains.shape, f32), ((weight_rows, tile), f32)],
        place,
        *shares_0,
        *shares_1,
        attn_in,
        gain_attn,
        smem=1,
    )
    return (
        output[None],
        grad_tokens[None],
        grad_attn_in,
        grad_attn_out,
        grad_up,
        grad_down,
        grad_gains,
        ends[:own_buckets, 8 : 8 + heads_all // heads_n],
    )


def solution(mesh):
    sizes = dict(mesh.shape)
    cores = 2
    fine = Mesh(
        mesh.devices.reshape(sizes["head"], sizes["blk"] // cores, cores), everyone
    )
    blk = ("z", "core")
    in_specs = (
        P("head", blk, None),
        P(None, blk),
        P(),
        P(None, everyone, None),
        P(None, everyone, None),
        P(None, everyone, None),
        P(None, everyone, None),
        P(None, everyone, None),
        P("head", blk, None),
    )
    out_specs = (
        P("head", blk, None),
        P("head", blk, None),
        P(None, everyone, None),
        P(None, everyone, None),
        P(None, everyone, None),
        P(None, everyone, None),
        P(None, everyone, None),
        P(blk, "head"),
    )
    plane = sizes["head"] == 4 and sizes["blk"] == 8
    local = local_plane if plane else local_general
    return jax.shard_map(local, mesh=fine, in_specs=in_specs, out_specs=out_specs, check_vma=False)
```
